32 devices in a mesh: dp: 16 (over z, x, core), tensor: 2 (over y).
Axes of the slice: x: 2, y: 2, z: 4, core: 2. Of those that a mesh axis runs over, the one named last changes fastest.
Arguments:
- layer_input: bfloat16 [4096, 2048], P(('dp', 'tensor')), may hold values from -17 to 17
- query_weight: bfloat16 [2048, 4096], P('dp', 'tensor'), may hold values from -0.125 to 0.125
- key_projection: bfloat16 [2048, 512], P('dp', 'tensor'), may hold values from -0.125 to 0.125
- value_projection: bfloat16 [2048, 512], P('dp', 'tensor'), may hold values from -0.125 to 0.125
- context_weight: bfloat16 [4096, 2048], P('tensor', 'dp'), may hold values from -0.75 to 0.75
- router_weight: bfloat16 [2048, 32], P('dp'), may hold values from -0.0625 to 0.0625
- expert_gate: bfloat16 [32, 2048, 768], P('dp', None, 'tensor'), may hold values from -0.125 to 0.125
- expert_up: bfloat16 [32, 2048, 768], P('dp', None, 'tensor'), may hold values from -0.125 to 0.125
- expert_down: bfloat16 [32, 768, 2048], P('dp', 'tensor'), may hold values from -0.875 to 0.875
- prenorm_gain: bfloat16 [2048], P('dp'), may hold values from 0.099609375 to 1.8984375
- midnorm_gain: bfloat16 [2048], P('dp'), may hold values from 0.099609375 to 1.8984375
- querynorm_gain: bfloat16 [128], P('dp'), may hold values from 0.099609375 to 1.8984375
- keynorm_gain: bfloat16 [128], P('dp'), may hold values from 0.099609375 to 1.8984375
- routes: int32 [4096, 8], P('dp'), may hold values from 0 to 31, all different within a row; in each aligned block of 256 rows (0 to 255, 256 to 511, ...) at most 80 rows name the same one
- lengths: int32 [16], replicated, may hold values from 1 to 256, 3072 in all
- sequence_order: int32 [16], replicated, may hold values from 0 to 15, each once
- output_cotangent: bfloat16 [4096, 2048], P(('dp', 'tensor')), may hold values from -6 to 6
Outputs:
- layer_output: bfloat16 [4096, 2048], P(('dp', 'tensor'))
- input_gradient: bfloat16 [4096, 2048], P(('dp', 'tensor'))
- query_gradient: float32 [2048, 4096], P('dp', 'tensor')
- key_gradient: float32 [2048, 512], P('dp', 'tensor')
- value_gradient: float32 [2048, 512], P('dp', 'tensor')
- context_gradient: float32 [4096, 2048], P('tensor', 'dp')
- router_gradient: float32 [2048, 32], P('dp')
- gate_gradient: float32 [32, 2048, 768], P('dp', None, 'tensor')
- up_gradient: float32 [32, 2048, 768], P('dp', None, 'tensor')
- down_gradient: float32 [32, 768, 2048], P('dp', 'tensor')
- prenorm_gradient: float32 [2048], P('dp')
- midnorm_gradient: float32 [2048], P('dp')
- querynorm_gradient: float32 [128], P('dp')
- keynorm_gradient: float32 [128], P('dp')
The draws below stay inside these ranges and needn't reach their ends.
Inputs may be any that keep to these rules, and one draw needn't show every extreme that they name: `routes`: each row names 8 different experts; in the rows of one index of dp (aligned blocks of 256 rows) no expert is named by more than 80 rows, and in every draw some expert is named by exactly 80 rows of a block. The lengths sum to 3072; the largest is exactly 256. `sequence_order`: each sequence appears once.
All inputs are finite; a program needn't handle non-finite values.
Results may differ from the reference program's by a relative error of at most 0.019.
Values may be sent and summed in bfloat16 or wider, within the bound.
A program may use at most 256 MiB of HBM per device.

```python
import math
import jax
import jax.numpy as jnp
import numpy as np
from jax import lax

MODEL_WIDTH = 2048
QUERY_HEADS = 32
KEY_VALUE_HEADS = 4
HEAD_SIZE = 128
EXP_FF = 768
TOP = 8
SLOT_TOKENS = 256
EXPERTS = 32
TOKENS = 4096
SEQS = 16
LIVE = 3072
CAP = 768
MOST = 80
N_DP = 16
N_TENSOR = 2


def draw_layer_input(key, part):
    first_key, second_key, third_key = jax.random.split(key, 3)
    row_scale = jnp.exp(jax.random.uniform(first_key, (TOKENS, 1), minval=math.log(0.2), maxval=math.log(2.0)))
    column_scale = jnp.exp(jax.random.uniform(second_key, (1, MODEL_WIDTH), minval=math.log(0.3), maxval=math.log(3.0)))
    base_values = jnp.clip(jax.random.normal(third_key, (TOKENS, MODEL_WIDTH)), -4.0, 4.0)
    return (base_values * row_scale * column_scale * 0.7).astype(jnp.bfloat16)


def spiked(drawn, own_key, source, target, blocks, factor):
    def block_of(position):
        return (jnp.arange(drawn.shape[position]) // (drawn.shape[position] // blocks)).reshape((-1,) + (1,) * (drawn.ndim - 1 - position))

    first = jax.random.permutation(own_key, blocks)[block_of(target)]
    second = (block_of(target) + blocks // 2) % blocks
    return jnp.where((block_of(source) == first) | (block_of(source) == second), factor * drawn, drawn)


def level_of(rng, extent, cuts, least, top_value):
    def one(position, shards_of):
        steps = jax.random.uniform(jax.random.fold_in(jax.random.fold_in(rng, 6), position), (shards_of,), jnp.float32, least / len(cuts), top_value / len(cuts))
        return jnp.repeat(jnp.exp(steps), extent[position] // shards_of).reshape((-1,) + (1,) * (len(extent) - position - 1))

    gain = one(*cuts[0])
    for cut in cuts[1:]:
        gain = gain * one(*cut)
    return gain


def profile(count, total, reach, slope):
    portions = [(1 << 20) // math.isqrt(grade ** slope) + 1 for grade in range(2, count + 1)]
    surplus, counts = total - reach - (count - 1), [1] * (count - 1)
    while surplus > 0:
        candidates = [i for i in range(count - 1) if counts[i] < reach]
        whole, left = sum([portions[i] for i in candidates]), surplus
        for i in candidates:
            more = min(reach - counts[i], max(1, left * portions[i] // whole), surplus)
            counts[i] = counts[i] + more
            surplus = surplus - more
    return np.array([reach] + counts)


def ragged_sizes(key, amount, total, limit, skew):
    if amount == 2:
        one = jax.random.randint(key, (), max(1, total - limit), min(limit, total - 1) + 1)
        return jnp.stack([one, total - one])
    sizes = jnp.asarray(profile(amount, total, limit, skew), jnp.int32)
    twos = (amount - 1) // 2
    giver, sink = sizes[1:1 + 2 * twos:2], sizes[2:2 + 2 * twos:2]
    slack = jnp.minimum(giver - 1, limit - sink)
    passed = jax.random.randint(jax.random.fold_in(key, 1), (twos,), 0, 1 << 20) % (slack + 1)
    sizes = sizes.at[1:1 + 2 * twos:2].set(giver - passed).at[2:2 + 2 * twos:2].set(sink + passed)
    return sizes[jax.random.permutation(jax.random.fold_in(key, 2), amount)]


def deal_out(rng, own, number, rows, number_of, top, bound, skew):
    sequence = jax.random.permutation(rng, number_of)
    heavy_load, common = load_shares(number_of, rows * top, bound, skew, True), load_shares(number_of, rows * top, bound, skew, False)
    places = jnp.arange(number_of)

    def named(sizes, rotation):
        used = int((sizes > 0).sum())
        fixed = max(1, used // 4)
        shifted = fixed + (places - fixed + rotation * (used - fixed)) % max(1, number_of - fixed)
        return jnp.zeros((number_of,), jnp.int32).at[sequence[jnp.where(places < fixed, places, shifted)]].set(jnp.asarray(sizes, jnp.int32))

    sizes = jnp.where(number % 4 == 0, named(heavy_load, number // 4), named(common, number - number // 4 - 1))
    mixed = jax.random.permutation(jax.random.fold_in(own, 3), number_of)
    source_of, receiver = mixed[0:number_of // 2 * 2:2], mixed[1:number_of // 2 * 2:2]
    margin = jnp.minimum(sizes[source_of] - 1, bound - sizes[receiver]) // 2
    margin = jnp.where((source_of == sequence[0]) | (receiver == sequence[0]) | (sizes[receiver] == 0), 0, jnp.maximum(margin, 0))
    shifted = jax.random.randint(jax.random.fold_in(own, 4), (number_of // 2,), 0, 1 << 20) % (margin + 1)
    sizes = sizes.at[source_of].add(-shifted).at[receiver].add(shifted)
    labels = jnp.searchsorted(jnp.cumsum(sizes), jnp.arange(rows * top), side="right").astype(jnp.int32)
    listing = labels.reshape(top, rows).T
    listing = listing[jax.random.permutation(jax.random.fold_in(own, 1), rows)]
    rotation = jax.random.randint(jax.random.fold_in(own, 2), (rows, 1), 0, top)
    return jnp.take_along_axis(listing, (jnp.arange(top)[None, :] + rotation) % top, axis=1)


def load_shares(amount, total, limit, slope, full):
    weights = [(1 << 20) // math.isqrt(rank ** slope) + 1 for rank in range(1, amount + 1)]
    largest = limit if full else min(limit, max(-(-total // amount), total * weights[0] // sum(weights)))
    least = 1 if total - largest >= amount - 1 else 0
    given, rest = [largest] + [least] * (amount - 1), total - largest - least * (amount - 1)
    while rest > 0:
        candidates = [i for i in range(1, amount) if given[i] < largest] or [i for i in range(1, amount) if given[i] < limit]
        mass, budget = sum([weights[i] for i in candidates]), rest
        for i in candidates:
            more = min(limit - given[i], max(1, budget * weights[i] // mass), rest)
            given[i] = given[i] + more
            rest = rest - more
    return np.array(given)


def gaussian(key, shape, spread, most, shards=(), kind=jnp.bfloat16):
    array = spread * jax.random.normal(key, shape, jnp.float32)
    if shards:
        array = array * level_of(key, shape, shards, -0.22, 0.18)
    return jnp.clip(array, -most, most).astype(kind)


def heavy_noise(stream_key, extent, deviation, most, cuts, heavy, held_as=jnp.bfloat16):
    values = deviation * jax.random.normal(stream_key, extent, jnp.float32)
    if cuts:
        values = values * level_of(stream_key, extent, cuts, -0.22, 0.18)
    return jnp.clip(spiked(values, jax.random.fold_in(stream_key, 3), *heavy), -most, most).astype(held_as)


def setup_inputs(seed: int = 0) -> dict:
    splits = jax.random.split(jax.random.key(seed), 18)
    layer_input = draw_layer_input(jax.random.fold_in(splits[17], 71), 0)
    query_weight = gaussian(splits[1], (MODEL_WIDTH, QUERY_HEADS * HEAD_SIZE), MODEL_WIDTH ** -0.5, 0.125, ((0, 16), (1, 2)))
    key_projection = gaussian(splits[2], (MODEL_WIDTH, KEY_VALUE_HEADS * HEAD_SIZE), MODEL_WIDTH ** -0.5, 0.125, ((0, 16), (1, 2)))
    value_projection = gaussian(splits[3], (MODEL_WIDTH, KEY_VALUE_HEADS * HEAD_SIZE), MODEL_WIDTH ** -0.5, 0.125, ((0, 16), (1, 2)))
    context_weight = gaussian(splits[4], (QUERY_HEADS * HEAD_SIZE, MODEL_WIDTH), (QUERY_HEADS * HEAD_SIZE // 64) ** -0.5, 0.75, ((0, 2), (1, 16)))
    router_weight = gaussian(splits[5], (MODEL_WIDTH, EXPERTS), (MODEL_WIDTH * 4) ** -0.5, 0.0625, ((0, 16),))
    expert_gate = gaussian(splits[6], (EXPERTS, MODEL_WIDTH, EXP_FF), MODEL_WIDTH ** -0.5, 0.125, ((0, 16), (2, 2)))
    expert_up = gaussian(splits[7], (EXPERTS, MODEL_WIDTH, EXP_FF), MODEL_WIDTH ** -0.5, 0.125, ((0, 16), (2, 2)))
    expert_down = gaussian(splits[8], (EXPERTS, EXP_FF, MODEL_WIDTH), (EXP_FF // 16) ** -0.5, 0.875, ((0, 16), (1, 2)))
    prenorm_gain = jnp.clip(1.0 + 0.18 * jax.random.normal(splits[9], (MODEL_WIDTH,), jnp.float32), 0.099609375, 1.8984375).astype(jnp.bfloat16)
    midnorm_gain = jnp.clip(1.0 + 0.18 * jax.random.normal(splits[10], (MODEL_WIDTH,), jnp.float32), 0.099609375, 1.8984375).astype(jnp.bfloat16)
    querynorm_gain = jnp.clip(1.0 + 0.18 * jax.random.normal(splits[11], (HEAD_SIZE,), jnp.float32), 0.099609375, 1.8984375).astype(jnp.bfloat16)
    keynorm_gain = jnp.clip(1.0 + 0.18 * jax.random.normal(splits[12], (HEAD_SIZE,), jnp.float32), 0.099609375, 1.8984375).astype(jnp.bfloat16)
    routes_keys = jax.random.split(jax.random.fold_in(splits[13], 1), TOKENS // SLOT_TOKENS)
    routes_turns = jax.random.permutation(jax.random.fold_in(splits[13], 3), TOKENS // SLOT_TOKENS)
    routes = jax.vmap(lambda own, number: deal_out(jax.random.fold_in(splits[13], 2), own, number, SLOT_TOKENS, EXPERTS, TOP, MOST, 2))(routes_keys, routes_turns).reshape((TOKENS, TOP))
    lengths = ragged_sizes(splits[14], SEQS, LIVE, SLOT_TOKENS, 2).astype(jnp.int32)
    sequence_order = jax.random.permutation(splits[15], SEQS).astype(jnp.int32)
    output_cotangent = heavy_noise(splits[16], (TOKENS, MODEL_WIDTH), 1.0, 6.0, ((0, 32),), (0, 1, 32, 2.75))
    return {"layer_input": layer_input, "query_weight": query_weight, "key_projection": key_projection, "value_projection": value_projection, "context_weight": context_weight, "router_weight": router_weight, "expert_gate": expert_gate, "expert_up": expert_up, "expert_down": expert_down, "prenorm_gain": prenorm_gain, "midnorm_gain": midnorm_gain, "querynorm_gain": querynorm_gain, "keynorm_gain": keynorm_gain, "routes": routes, "lengths": lengths, "sequence_order": sequence_order, "output_cotangent": output_cotangent}


@jax.custom_vjp
def reduced_precision(v):
    return lax.optimization_barrier(v.astype(jnp.bfloat16)).astype(jnp.float32)

@jax.custom_vjp
def reduced_precision_back(v):
    return v

def low_keep(v):
    return (reduced_precision(v), None)

def low_pass(kept, grad):
    return (grad,)

def back_keep(v):
    return (v, None)

def back_low(kept, grad):
    return (reduced_precision(grad),)
reduced_precision.defvjp(low_keep, low_pass)
reduced_precision_back.defvjp(back_keep, back_low)
epsilon = 1e-06
rope_base = 1000000.0
masked_score = -1e+30
highest = lax.Precision.HIGHEST

def matrix_product(former, latter):
    return jnp.dot(former, latter, precision=highest)

def rms_normalize(value_rows, factor):
    return value_rows * lax.rsqrt(lax.optimization_barrier(jnp.mean(value_rows * value_rows, axis=-1, keepdims=True)) + epsilon) * factor

def rotary_apply(value_rows, cosine_table, sine_values):
    middle = value_rows.shape[-1] // 2
    former = value_rows[..., :middle]
    latter = value_rows[..., middle:]
    return jnp.concatenate([former * cosine_table - latter * sine_values, latter * cosine_table + former * sine_values], axis=-1)

def reference(layer_input, query_weight, key_projection, value_projection, context_weight, router_weight, expert_gate, expert_up, expert_down, prenorm_gain, midnorm_gain, querynorm_gain, keynorm_gain, routes, lengths, sequence_order, output_cotangent):
    token_ids = jnp.arange(TOKENS, dtype=jnp.int32)
    block_of = token_ids // SLOT_TOKENS
    position_of = token_ids % SLOT_TOKENS
    seq_lengths = lengths[sequence_order]
    token_live = position_of < seq_lengths[block_of]
    pair_expert = routes.reshape(-1)
    pair_live = jnp.repeat(token_live, TOP)
    expert_ids = jnp.arange(EXPERTS, dtype=jnp.int32)
    pair_hot = ((pair_expert[:, None] == expert_ids[None, :]) & pair_live[:, None]).astype(jnp.int32)
    earlier = jnp.cumsum(pair_hot, axis=0) - pair_hot
    pair_slot = lax.optimization_barrier(jnp.sum(earlier * pair_hot, axis=1))
    pair_kept = pair_live & (pair_slot < CAP)
    target = jnp.where(pair_kept, pair_expert * CAP + pair_slot, EXPERTS * CAP)
    pair_ids = jnp.arange(TOKENS * TOP, dtype=jnp.int32)
    slot_pair = jnp.full((EXPERTS * CAP,), -1, dtype=jnp.int32).at[target].set(pair_ids, mode='drop')
    slot_used = slot_pair >= 0
    slot_safe = jnp.maximum(slot_pair, 0)
    slot_token = slot_safe // TOP
    positions = jnp.arange(SLOT_TOKENS, dtype=jnp.int32)
    frequency = jnp.exp(-math.log(rope_base) * jnp.arange(HEAD_SIZE // 2, dtype=jnp.float32) * (2.0 / HEAD_SIZE))
    angles = positions.astype(jnp.float32)[:, None] * frequency[None, :]
    cosine_table = jnp.cos(angles)[:, None, :]
    sine_values = jnp.sin(angles)[:, None, :]
    part_width = EXP_FF // N_TENSOR
    group_width = QUERY_HEADS // KEY_VALUE_HEADS

    def forward(stream, query_w, key_matrix, value_matrix, context_w, router_w, gate_w, up_w, down_w, gain_first, gain_second, query_gain, gain_key):

        def attend(block_pack):
            block_rows, block_length = block_pack
            first_layer_normed = reduced_precision(rms_normalize(block_rows, gain_first))
            query_unnormed = reduced_precision_back(matrix_product(first_layer_normed, query_w)).reshape(SLOT_TOKENS, QUERY_HEADS, HEAD_SIZE)
            key_unnormed = reduced_precision_back(matrix_product(first_layer_normed, key_matrix)).reshape(SLOT_TOKENS, KEY_VALUE_HEADS, HEAD_SIZE)
            value_rows = reduced_precision(reduced_precision_back(matrix_product(first_layer_normed, value_matrix))).reshape(SLOT_TOKENS, KEY_VALUE_HEADS, HEAD_SIZE)
            query_rows = reduced_precision(rotary_apply(rms_normalize(query_unnormed, query_gain), cosine_table, sine_values)).reshape(SLOT_TOKENS, KEY_VALUE_HEADS, group_width, HEAD_SIZE)
            keys_rot = reduced_precision(rotary_apply(rms_normalize(key_unnormed, gain_key), cosine_table, sine_values))
            scores = reduced_precision_back(jnp.einsum('ikrd,jkd->krij', query_rows, keys_rot, precision=highest) * HEAD_SIZE ** (-0.5))
            allowed = (positions[None, :] <= positions[:, None]) & (positions[None, :] < block_length)
            scores = jnp.where(allowed, scores, masked_score)
            soft_probs = reduced_precision(jax.nn.softmax(scores, axis=-1))
            context = jnp.einsum('krij,jkd->ikrd', soft_probs, value_rows, precision=highest).reshape(SLOT_TOKENS, QUERY_HEADS * HEAD_SIZE)
            context = reduced_precision(reduced_precision_back(context))
            return reduced_precision_back(matrix_product(context, context_w))
        attention = lax.map(jax.checkpoint(attend), (stream.reshape(N_DP, SLOT_TOKENS, MODEL_WIDTH), seq_lengths))
        residual = stream + attention.reshape(TOKENS, MODEL_WIDTH)
        normed_second = reduced_precision(rms_normalize(residual, gain_second))
        logits = reduced_precision_back(matrix_product(normed_second, router_w))
        gate_weights = jax.nn.softmax(jnp.take_along_axis(logits, routes, axis=1), axis=-1)

        def expert(operands):
            tokens_in, used_in, gate_e, up_e, down_e = operands
            rows_in = jnp.where(used_in[:, None], normed_second[tokens_in], 0.0)
            rounded = reduced_precision_back(rows_in)
            summed = jnp.zeros((CAP, MODEL_WIDTH), dtype=jnp.float32)
            for portion in range(N_TENSOR):
                first_col = portion * part_width
                last_col = first_col + part_width
                gate_pre = reduced_precision_back(matrix_product(rounded, gate_e[:, first_col:last_col]))
                up_pre = reduced_precision_back(matrix_product(rounded, up_e[:, first_col:last_col]))
                hidden = reduced_precision(jax.nn.silu(gate_pre) * up_pre)
                summed = summed + matrix_product(hidden, down_e[first_col:last_col, :])
            return reduced_precision(reduced_precision_back(summed))
        outputs = lax.map(jax.checkpoint(expert), (slot_token.reshape(EXPERTS, CAP), slot_used.reshape(EXPERTS, CAP), gate_w, up_w, down_w))
        slot_gates = jnp.where(slot_used, gate_weights.reshape(-1)[slot_safe], 0.0)
        combined = jnp.zeros((TOKENS, MODEL_WIDTH), dtype=jnp.float32).at[slot_token].add(outputs.reshape(EXPERTS * CAP, MODEL_WIDTH) * slot_gates[:, None])
        return residual + combined
    primals = tuple((operand.astype(jnp.float32) for operand in (layer_input, query_weight, key_projection, value_projection, context_weight, router_weight, expert_gate, expert_up, expert_down, prenorm_gain, midnorm_gain, querynorm_gain, keynorm_gain)))
    result, pullback = jax.vjp(forward, *primals)
    gradients = pullback(output_cotangent.astype(jnp.float32))
    return (result.astype(jnp.bfloat16), gradients[0].astype(jnp.bfloat16), gradients[1], gradients[2], gradients[3], gradients[4], gradients[5], gradients[6], gradients[7], gradients[8], gradients[9], gradients[10], gradients[11], gradients[12])
```

```python
import math

import jax
import jax.numpy as jnp
from jax import lax
from jax.sharding import PartitionSpec as P

HEAD_SIZE = 128
TOP = 8
EXP_DEV = 2


epsilon = 1e-06
rope_base = 1000000.0
masked_score = -1e30


def carried_in(value, axis, combine, identity):
    count, place = (lax.axis_size(axis), lax.axis_index(axis))
    everything = lax.all_gather(value, axis)
    start = jnp.broadcast_to(jnp.asarray(identity, value.dtype), value.shape)

    def hop(k, before):
        reached = k < place
        new = combine(before, everything[k])
        return jnp.where(reached, new, before)

    return lax.fori_loop(0, count, hop, start)


def rms_normalize(value_rows):
    scaling = lax.rsqrt(jnp.mean(value_rows * value_rows, axis=-1, keepdims=True) + epsilon)
    return (value_rows * scaling, scaling)


def norm_back(cotangent, unit_rows, scaling):
    return scaling * (
        cotangent - unit_rows * jnp.mean(cotangent * unit_rows, axis=-1, keepdims=True)
    )


def rotary_apply(value_rows, cosine_table, sine_values):
    middle = value_rows.shape[-1] // 2
    former = value_rows[..., :middle]
    latter = value_rows[..., middle:]
    return jnp.concatenate(
        [
            former * cosine_table - latter * sine_values,
            latter * cosine_table + former * sine_values,
        ],
        axis=-1,
    )


def matrix_product(former, latter):
    return jnp.dot(former, latter, preferred_element_type=jnp.float32)


def contract(former, latter):
    return lax.dot_general(
        former, latter, (((0,), (0,)), ((), ())), preferred_element_type=jnp.float32
    )


def transposed(former, latter):
    return lax.dot_general(
        former, latter, (((1,), (1,)), ((), ())), preferred_element_type=jnp.float32
    )


def to_owners(buffer):
    return lax.all_to_all(buffer, "dp", split_axis=1, concat_axis=1, tiled=True)


def owner_reduce(partial_rows):
    shares = lax.psum_scatter(
        partial_rows.astype(jnp.bfloat16), "tensor", scatter_dimension=2, tiled=True
    )
    return lax.all_gather(shares, "tensor", axis=2, tiled=True)


def body(
    layer_input,
    query_weight,
    key_projection,
    value_projection,
    context_weight,
    router_weight,
    expert_gate,
    expert_up,
    expert_down,
    prenorm_gain,
    midnorm_gain,
    querynorm_gain,
    keynorm_gain,
    routes,
    lengths,
    sequence_order,
    output_cotangent,
):
    tensor_count = lax.axis_size("tensor")
    tensor_index = lax.axis_index("tensor")
    dp_count = lax.axis_size("dp")
    own_rows = layer_input.shape[0]
    block_rows = own_rows * tensor_count
    features = layer_input.shape[1]
    expert_count = EXP_DEV * dp_count
    capacity = 3 * block_rows * TOP // (4 * EXP_DEV)
    most_rows = (5 * block_rows * TOP + 4 * expert_count - 1) // (4 * expert_count)
    slot_total = EXP_DEV * dp_count * most_rows
    (
        query_all,
        key_all,
        value_all,
        context_all,
        router_all,
        gain_first,
        gain_second,
        query_gain,
        gain_key,
    ) = (
        lax.all_gather(query_weight, "dp", axis=0, tiled=True),
        lax.all_gather(key_projection, "dp", axis=0, tiled=True),
        lax.all_gather(value_projection, "dp", axis=0, tiled=True),
        lax.all_gather(context_weight, "dp", axis=1, tiled=True),
        lax.all_gather(router_weight, "dp", axis=0, tiled=True),
        lax.all_gather(prenorm_gain, "dp", axis=0, tiled=True),
        lax.all_gather(midnorm_gain, "dp", axis=0, tiled=True),
        lax.all_gather(querynorm_gain, "dp", axis=0, tiled=True),
        lax.all_gather(keynorm_gain, "dp", axis=0, tiled=True),
    )
    input_rows, cot_rows = (
        lax.all_gather(layer_input, "tensor", axis=0, tiled=True),
        lax.all_gather(output_cotangent, "tensor", axis=0, tiled=True),
    )
    position = jnp.arange(block_rows, dtype=jnp.int32)
    seq_length = lengths[sequence_order[lax.axis_index("dp")]]
    token_live = position < seq_length
    frequency = jnp.exp(
        -math.log(rope_base) * jnp.arange(HEAD_SIZE // 2, dtype=jnp.float32) * (2.0 / HEAD_SIZE)
    )
    angles = position.astype(jnp.float32)[:, None] * frequency[None, :]
    cosine_table = jnp.cos(angles)[:, None, :]
    sine_values = jnp.sin(angles)[:, None, :]
    heads_query = query_all.shape[1] // HEAD_SIZE
    heads_key = key_all.shape[1] // HEAD_SIZE
    group_width = heads_query // heads_key
    gain_one = gain_first.astype(jnp.float32)
    gain_two = gain_second.astype(jnp.float32)
    query_factor = query_gain.astype(jnp.float32)
    key_factor = gain_key.astype(jnp.float32)
    stream = input_rows.astype(jnp.float32)
    unit_first, scale_first = rms_normalize(stream)
    first_layer_normed = (unit_first * gain_one).astype(jnp.bfloat16)
    query_unnormed = matrix_product(first_layer_normed, query_all).reshape(
        block_rows, heads_query, HEAD_SIZE
    )
    key_unnormed = matrix_product(first_layer_normed, key_all).reshape(
        block_rows, heads_key, HEAD_SIZE
    )
    value_rows = (
        matrix_product(first_layer_normed, value_all)
        .astype(jnp.bfloat16)
        .reshape(block_rows, heads_key, HEAD_SIZE)
    )
    query_unit, query_scale = rms_normalize(query_unnormed)
    key_unit, key_scale = rms_normalize(key_unnormed)
    query_rows = (
        rotary_apply(query_unit * query_factor, cosine_table, sine_values)
        .astype(jnp.bfloat16)
        .reshape(block_rows, heads_key, group_width, HEAD_SIZE)
    )
    keys_rot = rotary_apply(key_unit * key_factor, cosine_table, sine_values).astype(jnp.bfloat16)
    score_scale = HEAD_SIZE ** (-0.5)
    allowed = (position[None, :] <= position[:, None]) & token_live[None, :]

    def score_block():
        raw_scores = (
            jnp.einsum("ikrd,jkd->krij", query_rows, keys_rot, preferred_element_type=jnp.float32)
            * score_scale
        )
        return jnp.where(allowed, raw_scores, masked_score)

    scores = score_block()
    row_peak = jnp.max(scores, axis=-1, keepdims=True)
    log_total = row_peak + jnp.log(jnp.sum(jnp.exp(scores - row_peak), axis=-1, keepdims=True))
    soft_probs = jnp.exp(scores - log_total)
    context = jnp.einsum(
        "krij,jkd->ikrd",
        soft_probs.astype(jnp.bfloat16),
        value_rows,
        preferred_element_type=jnp.float32,
    )
    context = context.reshape(block_rows, heads_query * HEAD_SIZE).astype(jnp.bfloat16)
    attention = lax.psum(matrix_product(context, context_all), "tensor")
    residual = stream + attention
    unit_second, scale_second = rms_normalize(residual)
    normed_second = (unit_second * gain_two).astype(jnp.bfloat16)
    logits = matrix_product(normed_second, router_all)
    expert_ids = jnp.arange(expert_count, dtype=jnp.int32)
    route_hot = routes[:, :, None] == expert_ids[None, None, :]
    chosen = jnp.sum(jnp.where(route_hot, logits[:, None, :], 0.0), axis=-1)
    gate_weights = jax.nn.softmax(chosen, axis=-1)
    pair_expert = routes.reshape(-1)
    pair_live = jnp.repeat(token_live, TOP)
    pair_hot = ((pair_expert[:, None] == expert_ids[None, :]) & pair_live[:, None]).astype(
        jnp.int32
    )
    running = jnp.cumsum(pair_hot, axis=0)
    pair_rank = jnp.sum((running - pair_hot) * pair_hot, axis=1)
    counts = running[-1]
    earlier = carried_in(
        counts, "dp", lambda former, latter: former + latter, jnp.zeros_like(counts)
    )
    pair_slot = jnp.sum(earlier[None, :] * pair_hot, axis=1) + pair_rank
    pair_kept = pair_live & (pair_slot < capacity)
    local_expert = pair_expert % EXP_DEV
    owner_index = pair_expert // EXP_DEV
    buffer_index = (local_expert * dp_count + owner_index) * most_rows + pair_rank
    target = jnp.where(pair_kept, buffer_index, slot_total)
    pair_ids = jnp.arange(block_rows * TOP, dtype=jnp.int32)
    slot_pair = jnp.full((slot_total,), -1, dtype=jnp.int32).at[target].set(pair_ids, mode="drop")
    slot_used = slot_pair >= 0
    slot_safe = jnp.maximum(slot_pair, 0)
    slot_token = slot_safe // TOP
    bf_zero = jnp.zeros((), jnp.bfloat16)
    send_rows = jnp.where(slot_used[:, None], normed_second[slot_token], bf_zero)
    layout = (EXP_DEV, dp_count, most_rows, features)
    received = to_owners(send_rows.reshape(layout)).reshape(EXP_DEV, dp_count * most_rows, features)
    gate_pre = jnp.einsum("end,edf->enf", received, expert_gate, preferred_element_type=jnp.float32)
    up_pre = jnp.einsum("end,edf->enf", received, expert_up, preferred_element_type=jnp.float32)
    sigmoid_gate = jax.nn.sigmoid(gate_pre)
    gate_act = gate_pre * sigmoid_gate
    hidden = (gate_act * up_pre).astype(jnp.bfloat16)
    out_partial = jnp.einsum(
        "enf,efd->end", hidden, expert_down, preferred_element_type=jnp.float32
    )
    expert_out = owner_reduce(out_partial)
    width = expert_out.shape[2]
    returned = lax.all_to_all(
        expert_out.reshape(EXP_DEV, dp_count, most_rows, width),
        "dp",
        split_axis=1,
        concat_axis=1,
        tiled=True,
    ).reshape(slot_total, width)
    pair_place = jnp.where(pair_kept, buffer_index, 0)
    pair_out = jnp.where(pair_kept[:, None], returned[pair_place], bf_zero).reshape(
        block_rows, TOP, width
    )
    expert_part = jnp.sum(gate_weights[:, :, None] * pair_out, axis=1)
    cot_full = cot_rows.astype(jnp.float32)
    own_start = tensor_index * own_rows
    gate_part = jnp.sum(cot_full[:, None, :] * pair_out, axis=-1)
    expert_own = lax.dynamic_slice_in_dim(expert_part, own_start, own_rows, 0)
    residual_own = lax.dynamic_slice_in_dim(residual, own_start, own_rows, 0)
    layer_output = (residual_own + expert_own).astype(jnp.bfloat16)
    slot_gate = jnp.where(slot_used, gate_weights.reshape(-1)[slot_safe], 0.0)
    send_cot = (slot_gate[:, None] * cot_full[slot_token]).astype(jnp.bfloat16)
    expert_cot = to_owners(send_cot.reshape(layout)).reshape(
        EXP_DEV, dp_count * most_rows, features
    )
    hidden_cot = jnp.einsum(
        "end,efd->enf", expert_cot, expert_down, preferred_element_type=jnp.float32
    )
    gating_cot = (
        hidden_cot * up_pre * sigmoid_gate * (1.0 + gate_pre * (1.0 - sigmoid_gate))
    ).astype(jnp.bfloat16)
    upward_cot = (hidden_cot * gate_act).astype(jnp.bfloat16)
    down_gradient = jnp.einsum(
        "enf,end->efd", hidden, expert_cot, preferred_element_type=jnp.float32
    )
    gate_gradient = jnp.einsum(
        "end,enf->edf", received, gating_cot, preferred_element_type=jnp.float32
    )
    up_gradient = jnp.einsum(
        "end,enf->edf", received, upward_cot, preferred_element_type=jnp.float32
    )
    row_partial = jnp.einsum(
        "enf,edf->end", gating_cot, expert_gate, preferred_element_type=jnp.float32
    )
    row_partial = row_partial + jnp.einsum(
        "enf,edf->end", upward_cot, expert_up, preferred_element_type=jnp.float32
    )
    row_cot = owner_reduce(row_partial)
    row_back = lax.all_to_all(
        row_cot.reshape(EXP_DEV, dp_count, most_rows, width),
        "dp",
        split_axis=1,
        concat_axis=1,
        tiled=True,
    ).reshape(slot_total, width)
    pair_cot = jnp.where(pair_kept[:, None], row_back[pair_place], bf_zero).reshape(
        block_rows, TOP, width
    )
    normed_part = jnp.sum(pair_cot.astype(jnp.float32), axis=1)
    normed_cot = normed_part
    route_cot = gate_weights * (
        gate_part - jnp.sum(gate_weights * gate_part, axis=-1, keepdims=True)
    )
    logit_cot = jnp.sum(jnp.where(route_hot, route_cot[:, :, None], 0.0), axis=1).astype(
        jnp.bfloat16
    )
    router_gradient = contract(normed_second, logit_cot)
    normed_cot = normed_cot + transposed(logit_cot, router_all)
    midnorm_gradient = jnp.sum(normed_cot * unit_second, axis=0)
    residual_cot = cot_full + norm_back(normed_cot * gain_two, unit_second, scale_second)
    attention_cot = residual_cot.astype(jnp.bfloat16)
    context_gradient = contract(context, attention_cot)
    context_cot = (
        transposed(attention_cot, context_all)
        .astype(jnp.bfloat16)
        .reshape(block_rows, heads_key, group_width, HEAD_SIZE)
    )
    scores = score_block()
    soft_probs = jnp.exp(scores - log_total)
    prob_cot = jnp.einsum(
        "ikrd,jkd->krij", context_cot, value_rows, preferred_element_type=jnp.float32
    )
    score_cot = (
        soft_probs * (prob_cot - jnp.sum(soft_probs * prob_cot, axis=-1, keepdims=True))
    ).astype(jnp.bfloat16)
    value_cot = jnp.einsum(
        "krij,ikrd->jkd",
        soft_probs.astype(jnp.bfloat16),
        context_cot,
        preferred_element_type=jnp.float32,
    )
    value_cot = value_cot.astype(jnp.bfloat16).reshape(block_rows, heads_key * HEAD_SIZE)
    query_turned = (
        jnp.einsum(
            "krij,jkd->ikrd", score_cot, keys_rot, preferred_element_type=jnp.float32
        ).reshape(block_rows, heads_query, HEAD_SIZE)
        * score_scale
    )
    key_turned = (
        jnp.einsum("krij,ikrd->jkd", score_cot, query_rows, preferred_element_type=jnp.float32)
        * score_scale
    )
    query_back = rotary_apply(query_turned, cosine_table, -sine_values)
    key_back = rotary_apply(key_turned, cosine_table, -sine_values)
    querynorm_part = jnp.sum(query_back * query_unit, axis=(0, 1))
    keynorm_part = jnp.sum(key_back * key_unit, axis=(0, 1))
    query_raw_cot = (
        norm_back(query_back * query_factor, query_unit, query_scale)
        .astype(jnp.bfloat16)
        .reshape(block_rows, heads_query * HEAD_SIZE)
    )
    key_raw_cot = (
        norm_back(key_back * key_factor, key_unit, key_scale)
        .astype(jnp.bfloat16)
        .reshape(block_rows, heads_key * HEAD_SIZE)
    )
    query_gradient = contract(first_layer_normed, query_raw_cot)
    key_gradient = contract(first_layer_normed, key_raw_cot)
    value_gradient = contract(first_layer_normed, value_cot)
    first_part = (
        transposed(query_raw_cot, query_all)
        + transposed(key_raw_cot, key_all)
        + transposed(value_cot, value_all)
    )
    first_cot, querynorm_gradient, keynorm_gradient = (
        lax.psum(first_part.astype(jnp.bfloat16), "tensor").astype(jnp.float32),
        lax.psum(querynorm_part.astype(jnp.bfloat16), "tensor").astype(jnp.float32),
        lax.psum(keynorm_part.astype(jnp.bfloat16), "tensor").astype(jnp.float32),
    )
    prenorm_gradient = jnp.sum(first_cot * unit_first, axis=0)
    input_cot = residual_cot + norm_back(first_cot * gain_one, unit_first, scale_first)
    input_gradient = lax.dynamic_slice_in_dim(input_cot, own_start, own_rows, 0).astype(
        jnp.bfloat16
    )
    summed = (
        lax.psum_scatter(query_gradient, "dp", scatter_dimension=0, tiled=True),
        lax.psum_scatter(key_gradient, "dp", scatter_dimension=0, tiled=True),
        lax.psum_scatter(value_gradient, "dp", scatter_dimension=0, tiled=True),
        lax.psum_scatter(context_gradient, "dp", scatter_dimension=1, tiled=True),
        lax.psum_scatter(router_gradient, "dp", scatter_dimension=0, tiled=True),
        lax.psum_scatter(prenorm_gradient, "dp", scatter_dimension=0, tiled=True),
        lax.psum_scatter(midnorm_gradient, "dp", scatter_dimension=0, tiled=True),
        lax.psum_scatter(querynorm_gradient, "dp", scatter_dimension=0, tiled=True),
        lax.psum_scatter(keynorm_gradient, "dp", scatter_dimension=0, tiled=True),
    )
    return (
        layer_output,
        input_gradient,
        summed[0],
        summed[1],
        summed[2],
        summed[3],
        summed[4],
        gate_gradient,
        up_gradient,
        down_gradient,
        summed[5],
        summed[6],
        summed[7],
        summed[8],
    )


AUX = 128


def gather_dp(value):
    return lax.all_gather(value, "dp", axis=0, tiled=True)


def gather_all(value):
    return lax.all_gather(value, ("dp", "tensor"), axis=0, tiled=True)


def scatter_all(value):
    return lax.psum_scatter(value, ("dp", "tensor"), scatter_dimension=0, tiled=True)


def scatter_dp(value):
    return lax.psum_scatter(value, "dp", scatter_dimension=0, tiled=True)


def split_high_low(value):
    high = value.astype(jnp.bfloat16)
    return high, (value - high.astype(jnp.float32)).astype(jnp.bfloat16)


def gathered_body(
    layer_input,
    query_weight,
    key_projection,
    value_projection,
    context_weight,
    router_weight,
    expert_gate,
    expert_up,
    expert_down,
    prenorm_gain,
    midnorm_gain,
    querynorm_gain,
    keynorm_gain,
    routes,
    lengths,
    sequence_order,
    output_cotangent,
):
    bf16, f32 = jnp.bfloat16, jnp.float32
    tensor_count = lax.axis_size("tensor")
    tensor_index = lax.axis_index("tensor")
    dp_count = lax.axis_size("dp")
    dp_index = lax.axis_index("dp")
    own_rows, features = layer_input.shape
    block_rows = own_rows * tensor_count
    tokens = block_rows * dp_count
    expert_count = EXP_DEV * dp_count
    capacity = 3 * block_rows * TOP // (4 * EXP_DEV)
    most_rows = (5 * block_rows * TOP + 4 * expert_count - 1) // (4 * expert_count)
    shard = features // dp_count
    query_width = query_weight.shape[1]
    key_width = key_projection.shape[1]
    norm_part = HEAD_SIZE // dp_count

    gains = jnp.zeros((shard, AUX - expert_count), bf16)
    gains = gains.at[:, 0].set(prenorm_gain).at[:, 1].set(midnorm_gain)
    gains = gains.at[:norm_part, 2].set(querynorm_gain).at[:norm_part, 3].set(keynorm_gain)
    packed = jnp.concatenate(
        [query_weight, key_projection, value_projection, context_weight.T, router_weight, gains],
        axis=1,
    )
    packed = gather_dp(packed)
    edges = [0]
    for width in (query_width, key_width, key_width, query_width, expert_count, AUX - expert_count):
        edges.append(edges[-1] + width)
    qkv_all = packed[:, : edges[3]]
    context_all = packed[:, edges[3] : edges[4]]
    router_all = packed[:, edges[4] : edges[5]]
    gains_all = packed[:, edges[5] :].astype(f32)
    gain_one, gain_two = gains_all[:, 0], gains_all[:, 1]
    head_gains = gains_all.reshape(dp_count, shard, -1)[:, :norm_part, :]
    query_factor = head_gains[:, :, 2].reshape(-1)
    key_factor = head_gains[:, :, 3].reshape(-1)

    cot_all = gather_all(output_cotangent)
    routes_all = gather_dp(routes)
    input_rows = lax.all_gather(layer_input, "tensor", axis=0, tiled=True)
    position = jnp.arange(block_rows, dtype=jnp.int32)
    block_lengths = lengths[sequence_order]
    seq_length = block_lengths[dp_index]

    frequency = jnp.exp(
        -math.log(rope_base) * jnp.arange(HEAD_SIZE // 2, dtype=f32) * (2.0 / HEAD_SIZE)
    )
    angles = position.astype(f32)[:, None] * frequency[None, :]
    cosine_table = jnp.cos(angles)[:, None, :]
    sine_values = jnp.sin(angles)[:, None, :]
    heads_query = query_width // HEAD_SIZE
    heads_key = key_width // HEAD_SIZE
    group_width = heads_query // heads_key
    stream = input_rows.astype(f32)
    unit_first, scale_first = rms_normalize(stream)
    first_normed = (unit_first * gain_one).astype(bf16)
    raw = matrix_product(first_normed, qkv_all)
    query_unnormed = raw[:, : edges[1]].reshape(block_rows, heads_query, HEAD_SIZE)
    key_unnormed = raw[:, edges[1] : edges[2]].reshape(block_rows, heads_key, HEAD_SIZE)
    value_rows = raw[:, edges[2] :].astype(bf16).reshape(block_rows, heads_key, HEAD_SIZE)
    query_unit, query_scale = rms_normalize(query_unnormed)
    key_unit, key_scale = rms_normalize(key_unnormed)
    query_rows = (
        rotary_apply(query_unit * query_factor, cosine_table, sine_values)
        .astype(bf16)
        .reshape(block_rows, heads_key, group_width, HEAD_SIZE)
    )
    keys_rot = rotary_apply(key_unit * key_factor, cosine_table, sine_values).astype(bf16)
    score_scale = HEAD_SIZE ** (-0.5)
    allowed = (position[None, :] <= position[:, None]) & (position < seq_length)[None, :]
    scores = (
        jnp.einsum("ikrd,jkd->krij", query_rows, keys_rot, preferred_element_type=f32)
        * score_scale
    )
    scores = jnp.where(allowed, scores, masked_score)
    weights = jnp.exp(scores - jnp.max(scores, axis=-1, keepdims=True))
    soft_probs = weights / jnp.sum(weights, axis=-1, keepdims=True)
    probs_low = soft_probs.astype(bf16)
    context = jnp.einsum("krij,jkd->ikrd", probs_low, value_rows, preferred_element_type=f32)
    context = context.reshape(block_rows, query_width).astype(bf16)
    attention = lax.psum_scatter(
        transposed(context, context_all).astype(bf16),
        "tensor",
        scatter_dimension=0,
        tiled=True,
    )
    residual = layer_input.astype(f32) + attention.astype(f32)
    unit_second, scale_second = rms_normalize(residual)
    normed_second = (unit_second * gain_two).astype(bf16)

    normed_all = gather_all(normed_second)
    logits = matrix_product(normed_all, router_all)
    expert_ids = jnp.arange(expert_count, dtype=jnp.int32)
    chosen = jnp.zeros((tokens, expert_count), jnp.bool_)
    for j in range(TOP):
        chosen = chosen | (routes_all[:, j : j + 1] == expert_ids[None, :])
    peak = jnp.max(jnp.where(chosen, logits, masked_score), axis=-1, keepdims=True)
    spread = jnp.where(chosen, jnp.exp(jnp.minimum(logits - peak, 0.0)), 0.0)
    gates = spread / jnp.sum(spread, axis=-1, keepdims=True)
    live = position[None, :] < block_lengths[:, None]
    hot = chosen.reshape(dp_count, block_rows, expert_count) & live[:, :, None]
    hot_low = hot.astype(bf16)
    below = (position[None, :] < position[:, None]).astype(bf16)
    rank = jnp.einsum("ts,bse->bte", below, hot_low, preferred_element_type=f32)
    counts = jnp.sum(hot.astype(f32), axis=1)
    earlier = jnp.cumsum(counts, axis=0) - counts
    kept = hot & (earlier[:, None, :] + rank < capacity)

    first_expert = dp_index * EXP_DEV
    rank_own = lax.dynamic_slice_in_dim(rank, first_expert, EXP_DEV, 2)
    kept_own = lax.dynamic_slice_in_dim(kept, first_expert, EXP_DEV, 2)
    gates_own = lax.dynamic_slice_in_dim(
        gates.reshape(dp_count, block_rows, expert_count), first_expert, EXP_DEV, 2
    )
    slots = jnp.arange(most_rows, dtype=f32)
    place = kept_own.transpose(0, 2, 1)[:, :, None, :] & (
        rank_own.transpose(0, 2, 1)[:, :, None, :] == slots[None, None, :, None]
    )
    place_low = place.astype(bf16).reshape(dp_count, EXP_DEV * most_rows, block_rows)
    slot_gate = jnp.sum(
        jnp.where(place, gates_own.transpose(0, 2, 1)[:, :, None, :], 0.0), axis=-1
    )
    slot_gate = slot_gate.transpose(1, 0, 2).reshape(EXP_DEV, dp_count * most_rows, 1)

    def take(rows):
        taken = jnp.einsum(
            "bst,btd->bsd",
            place_low,
            rows.reshape(dp_count, block_rows, features),
            preferred_element_type=f32,
        ).astype(bf16)
        return (
            taken.reshape(dp_count, EXP_DEV, most_rows, features)
            .transpose(1, 0, 2, 3)
            .reshape(EXP_DEV, dp_count * most_rows, features)
        )

    def put(slot_rows):
        ordered = (
            slot_rows.astype(bf16)
            .reshape(EXP_DEV, dp_count, most_rows, features)
            .transpose(1, 0, 2, 3)
            .reshape(dp_count, EXP_DEV * most_rows, features)
        )
        return (
            jnp.einsum("bst,bsd->btd", place_low, ordered, preferred_element_type=f32)
            .astype(bf16)
            .reshape(tokens, features)
        )

    rows_in = take(normed_all)
    cot_in = take(cot_all)
    gate_pre = jnp.einsum("end,edf->enf", rows_in, expert_gate, preferred_element_type=f32)
    up_pre = jnp.einsum("end,edf->enf", rows_in, expert_up, preferred_element_type=f32)
    sigmoid_gate = jax.nn.sigmoid(gate_pre)
    gate_act = gate_pre * sigmoid_gate
    hidden = (gate_act * up_pre).astype(bf16)
    out_partial = jnp.einsum("enf,efd->end", hidden, expert_down, preferred_element_type=f32)
    expert_sum = scatter_all(put(out_partial * slot_gate))
    layer_output = (residual + expert_sum.astype(f32)).astype(bf16)

    down_cot = jnp.einsum("end,efd->enf", cot_in, expert_down, preferred_element_type=f32)
    slot_cot = jnp.sum(hidden.astype(f32) * down_cot, axis=-1)
    hidden_cot = down_cot * slot_gate
    gating_cot = (
        hidden_cot * up_pre * sigmoid_gate * (1.0 + gate_pre * (1.0 - sigmoid_gate))
    ).astype(bf16)
    upward_cot = (hidden_cot * gate_act).astype(bf16)
    hidden_gated = (hidden.astype(f32) * slot_gate).astype(bf16)
    down_gradient = jnp.einsum("enf,end->efd", hidden_gated, cot_in, preferred_element_type=f32)
    gate_gradient = jnp.einsum("end,enf->edf", rows_in, gating_cot, preferred_element_type=f32)
    up_gradient = jnp.einsum("end,enf->edf", rows_in, upward_cot, preferred_element_type=f32)
    row_partial = jnp.einsum("enf,edf->end", gating_cot, expert_gate, preferred_element_type=f32)
    row_partial = row_partial + jnp.einsum(
        "enf,edf->end", upward_cot, expert_up, preferred_element_type=f32
    )
    slot_cot = slot_cot.reshape(EXP_DEV, dp_count, most_rows).transpose(1, 0, 2)
    token_cot = jnp.sum(jnp.where(place, slot_cot[:, :, :, None], 0.0), axis=2)
    token_cot = token_cot.transpose(0, 2, 1).reshape(tokens, EXP_DEV)
    high, low = split_high_low(token_cot)
    quad = jnp.stack([high, low], axis=-1).reshape(tokens, 2 * EXP_DEV)
    aux = lax.dynamic_update_slice(
        jnp.zeros((tokens, 2 * tensor_count * expert_count), bf16),
        quad,
        (0, tensor_index * 2 * expert_count + dp_index * 2 * EXP_DEV),
    )
    returned = scatter_all(jnp.concatenate([put(row_partial), aux], axis=1)).astype(f32)
    gate_cot = jnp.sum(
        returned[:, features:].reshape(own_rows, tensor_count, expert_count, 2), axis=(1, 3)
    )
    own_start = (dp_index * tensor_count + tensor_index) * own_rows
    gates_mine = lax.dynamic_slice_in_dim(gates, own_start, own_rows, 0)
    logit_cot = (
        gates_mine * (gate_cot - jnp.sum(gates_mine * gate_cot, axis=-1, keepdims=True))
    ).astype(bf16)
    router_part = contract(normed_second, logit_cot)
    normed_cot = returned[:, :features] + transposed(logit_cot, router_all)
    midnorm_part = jnp.sum(normed_cot * unit_second, axis=0)
    residual_cot = output_cotangent.astype(f32) + norm_back(
        normed_cot * gain_two, unit_second, scale_second
    )
    attention_cot = lax.all_gather(residual_cot.astype(bf16), "tensor", axis=0, tiled=True)

    context_part = contract(attention_cot, context)
    context_cot = (
        matrix_product(attention_cot, context_all)
        .astype(bf16)
        .reshape(block_rows, heads_key, group_width, HEAD_SIZE)
    )
    prob_cot = jnp.einsum("ikrd,jkd->krij", context_cot, value_rows, preferred_element_type=f32)
    score_cot = (
        soft_probs * (prob_cot - jnp.sum(soft_probs * prob_cot, axis=-1, keepdims=True))
    ).astype(bf16)
    value_cot = jnp.einsum("krij,ikrd->jkd", probs_low, context_cot, preferred_element_type=f32)
    value_cot = value_cot.astype(bf16).reshape(block_rows, key_width)
    query_turned = (
        jnp.einsum("krij,jkd->ikrd", score_cot, keys_rot, preferred_element_type=f32).reshape(
            block_rows, heads_query, HEAD_SIZE
        )
        * score_scale
    )
    key_turned = (
        jnp.einsum("krij,ikrd->jkd", score_cot, query_rows, preferred_element_type=f32)
        * score_scale
    )
    query_back = rotary_apply(query_turned, cosine_table, -sine_values)
    key_back = rotary_apply(key_turned, cosine_table, -sine_values)
    querynorm_part = jnp.sum(query_back * query_unit, axis=(0, 1))
    keynorm_part = jnp.sum(key_back * key_unit, axis=(0, 1))
    query_raw_cot = norm_back(query_back * query_factor, query_unit, query_scale).astype(bf16)
    key_raw_cot = norm_back(key_back * key_factor, key_unit, key_scale).astype(bf16)
    raw_cot = jnp.concatenate(
        [
            query_raw_cot.reshape(block_rows, query_width),
            key_raw_cot.reshape(block_rows, key_width),
            value_cot,
        ],
        axis=1,
    )
    qkv_part = contract(first_normed, raw_cot)
    first_cot = lax.psum_scatter(
        transposed(raw_cot, qkv_all).astype(bf16), "tensor", scatter_dimension=0, tiled=True
    ).astype(f32)
    row_start = tensor_index * own_rows
    unit_own = lax.dynamic_slice_in_dim(unit_first, row_start, own_rows, 0)
    scale_own = lax.dynamic_slice_in_dim(scale_first, row_start, own_rows, 0)
    prenorm_part = jnp.sum(first_cot * unit_own, axis=0)
    input_gradient = (
        residual_cot + norm_back(first_cot * gain_one, unit_own, scale_own)
    ).astype(bf16)

    small = jnp.zeros((dp_count, shard, AUX), f32)
    small = small.at[:, :, :expert_count].set(router_part.reshape(dp_count, shard, expert_count))
    small = small.at[:, :, expert_count].set(prenorm_part.reshape(dp_count, shard))
    small = small.at[:, :, expert_count + 1].set(midnorm_part.reshape(dp_count, shard))
    small = small.at[:, :norm_part, expert_count + 2].set(querynorm_part.reshape(dp_count, -1))
    small = small.at[:, :norm_part, expert_count + 3].set(keynorm_part.reshape(dp_count, -1))
    small = scatter_dp(small.reshape(features, AUX))
    small = lax.psum(small, "tensor")
    summed = scatter_dp(jnp.concatenate([qkv_part.astype(bf16), context_part.astype(bf16)], axis=1))
    summed = summed.astype(f32)
    return (
        layer_output,
        input_gradient,
        summed[:, : edges[1]],
        summed[:, edges[1] : edges[2]],
        summed[:, edges[2] : edges[3]],
        summed[:, edges[3] :].T,
        small[:, :expert_count],
        gate_gradient,
        up_gradient,
        down_gradient,
        small[:, expert_count],
        small[:, expert_count + 1],
        small[:norm_part, expert_count + 2],
        small[:norm_part, expert_count + 3],
    )


def solution(mesh):
    return jax.shard_map(
        gathered_body if mesh.shape["dp"] <= 16 else body,
        mesh=mesh,
        in_specs=(
            P(("dp", "tensor"), None),
            P("dp", "tensor"),
            P("dp", "tensor"),
            P("dp", "tensor"),
            P("tensor", "dp"),
            P("dp", None),
            P("dp", None, "tensor"),
            P("dp", None, "tensor"),
            P("dp", "tensor", None),
            P("dp"),
            P("dp"),
            P("dp"),
            P("dp"),
            P("dp", None),
            P(),
            P(),
            P(("dp", "tensor"), None),
        ),
        out_specs=(
            P(("dp", "tensor"), None),
            P(("dp", "tensor"), None),
            P("dp", "tensor"),
            P("dp", "tensor"),
            P("dp", "tensor"),
            P("tensor", "dp"),
            P("dp", None),
            P("dp", None, "tensor"),
            P("dp", None, "tensor"),
            P("dp", "tensor", None),
            P("dp"),
            P("dp"),
            P("dp"),
            P("dp"),
        ),
        check_vma=False,
    )
```

```python
import math

import jax
import jax.numpy as jnp
from jax import lax
from jax.experimental import pallas as pl
from jax.experimental.pallas import tpu as pltpu
from jax.sharding import PartitionSpec as P

HEAD_SIZE = 128
TOP = 8
EXP_DEV = 2


epsilon = 1e-06
rope_base = 1000000.0
masked_score = -1e30


def carried_in(value, axis, combine, identity):
    count, place = (lax.axis_size(axis), lax.axis_index(axis))
    everything = lax.all_gather(value, axis)
    start = jnp.broadcast_to(jnp.asarray(identity, value.dtype), value.shape)

    def hop(k, before):
        reached = k < place
        new = combine(before, everything[k])
        return jnp.where(reached, new, before)

    return lax.fori_loop(0, count, hop, start)


def rms_normalize(value_rows):
    scaling = lax.rsqrt(jnp.mean(value_rows * value_rows, axis=-1, keepdims=True) + epsilon)
    return (value_rows * scaling, scaling)


def norm_back(cotangent, unit_rows, scaling):
    return scaling * (
        cotangent - unit_rows * jnp.mean(cotangent * unit_rows, axis=-1, keepdims=True)
    )


def rotary_apply(value_rows, cosine_table, sine_values):
    middle = value_rows.shape[-1] // 2
    former = value_rows[..., :middle]
    latter = value_rows[..., middle:]
    return jnp.concatenate(
        [
            former * cosine_table - latter * sine_values,
            latter * cosine_table + former * sine_values,
        ],
        axis=-1,
    )


def matrix_product(former, latter):
    return jnp.dot(former, latter, preferred_element_type=jnp.float32)


def contract(former, latter):
    return lax.dot_general(
        former, latter, (((0,), (0,)), ((), ())), preferred_element_type=jnp.float32
    )


def transposed(former, latter):
    return lax.dot_general(
        former, latter, (((1,), (1,)), ((), ())), preferred_element_type=jnp.float32
    )


def to_owners(buffer):
    return lax.all_to_all(buffer, "dp", split_axis=1, concat_axis=1, tiled=True)


def owner_reduce(partial_rows):
    shares = lax.psum_scatter(
        partial_rows.astype(jnp.bfloat16), "tensor", scatter_dimension=2, tiled=True
    )
    return lax.all_gather(shares, "tensor", axis=2, tiled=True)


def body(
    layer_input,
    query_weight,
    key_projection,
    value_projection,
    context_weight,
    router_weight,
    expert_gate,
    expert_up,
    expert_down,
    prenorm_gain,
    midnorm_gain,
    querynorm_gain,
    keynorm_gain,
    routes,
    lengths,
    sequence_order,
    output_cotangent,
):
    tensor_count = lax.axis_size("tensor")
    tensor_index = lax.axis_index("tensor")
    dp_count = lax.axis_size("dp")
    own_rows = layer_input.shape[0]
    block_rows = own_rows * tensor_count
    features = layer_input.shape[1]
    expert_count = EXP_DEV * dp_count
    capacity = 3 * block_rows * TOP // (4 * EXP_DEV)
    most_rows = (5 * block_rows * TOP + 4 * expert_count - 1) // (4 * expert_count)
    slot_total = EXP_DEV * dp_count * most_rows
    (
        query_all,
        key_all,
        value_all,
        context_all,
        router_all,
        gain_first,
        gain_second,
        query_gain,
        gain_key,
    ) = (
        lax.all_gather(query_weight, "dp", axis=0, tiled=True),
        lax.all_gather(key_projection, "dp", axis=0, tiled=True),
        lax.all_gather(value_projection, "dp", axis=0, tiled=True),
        lax.all_gather(context_weight, "dp", axis=1, tiled=True),
        lax.all_gather(router_weight, "dp", axis=0, tiled=True),
        lax.all_gather(prenorm_gain, "dp", axis=0, tiled=True),
        lax.all_gather(midnorm_gain, "dp", axis=0, tiled=True),
        lax.all_gather(querynorm_gain, "dp", axis=0, tiled=True),
        lax.all_gather(keynorm_gain, "dp", axis=0, tiled=True),
    )
    input_rows, cot_rows = (
        lax.all_gather(layer_input, "tensor", axis=0, tiled=True),
        lax.all_gather(output_cotangent, "tensor", axis=0, tiled=True),
    )
    position = jnp.arange(block_rows, dtype=jnp.int32)
    seq_length = lengths[sequence_order[lax.axis_index("dp")]]
    token_live = position < seq_length
    frequency = jnp.exp(
        -math.log(rope_base) * jnp.arange(HEAD_SIZE // 2, dtype=jnp.float32) * (2.0 / HEAD_SIZE)
    )
    angles = position.astype(jnp.float32)[:, None] * frequency[None, :]
    cosine_table = jnp.cos(angles)[:, None, :]
    sine_values = jnp.sin(angles)[:, None, :]
    heads_query = query_all.shape[1] // HEAD_SIZE
    heads_key = key_all.shape[1] // HEAD_SIZE
    group_width = heads_query // heads_key
    gain_one = gain_first.astype(jnp.float32)
    gain_two = gain_second.astype(jnp.float32)
    query_factor = query_gain.astype(jnp.float32)
    key_factor = gain_key.astype(jnp.float32)
    stream = input_rows.astype(jnp.float32)
    unit_first, scale_first = rms_normalize(stream)
    first_layer_normed = (unit_first * gain_one).astype(jnp.bfloat16)
    query_unnormed = matrix_product(first_layer_normed, query_all).reshape(
        block_rows, heads_query, HEAD_SIZE
    )
    key_unnormed = matrix_product(first_layer_normed, key_all).reshape(
        block_rows, heads_key, HEAD_SIZE
    )
    value_rows = (
        matrix_product(first_layer_normed, value_all)
        .astype(jnp.bfloat16)
        .reshape(block_rows, heads_key, HEAD_SIZE)
    )
    query_unit, query_scale = rms_normalize(query_unnormed)
    key_unit, key_scale = rms_normalize(key_unnormed)
    query_rows = (
        rotary_apply(query_unit * query_factor, cosine_table, sine_values)
        .astype(jnp.bfloat16)
        .reshape(block_rows, heads_key, group_width, HEAD_SIZE)
    )
    keys_rot = rotary_apply(key_unit * key_factor, cosine_table, sine_values).astype(jnp.bfloat16)
    score_scale = HEAD_SIZE ** (-0.5)
    allowed = (position[None, :] <= position[:, None]) & token_live[None, :]

    def score_block():
        raw_scores = (
            jnp.einsum("ikrd,jkd->krij", query_rows, keys_rot, preferred_element_type=jnp.float32)
            * score_scale
        )
        return jnp.where(allowed, raw_scores, masked_score)

    scores = score_block()
    row_peak = jnp.max(scores, axis=-1, keepdims=True)
    log_total = row_peak + jnp.log(jnp.sum(jnp.exp(scores - row_peak), axis=-1, keepdims=True))
    soft_probs = jnp.exp(scores - log_total)
    context = jnp.einsum(
        "krij,jkd->ikrd",
        soft_probs.astype(jnp.bfloat16),
        value_rows,
        preferred_element_type=jnp.float32,
    )
    context = context.reshape(block_rows, heads_query * HEAD_SIZE).astype(jnp.bfloat16)
    attention = lax.psum(matrix_product(context, context_all), "tensor")
    residual = stream + attention
    unit_second, scale_second = rms_normalize(residual)
    normed_second = (unit_second * gain_two).astype(jnp.bfloat16)
    logits = matrix_product(normed_second, router_all)
    expert_ids = jnp.arange(expert_count, dtype=jnp.int32)
    route_hot = routes[:, :, None] == expert_ids[None, None, :]
    chosen = jnp.sum(jnp.where(route_hot, logits[:, None, :], 0.0), axis=-1)
    gate_weights = jax.nn.softmax(chosen, axis=-1)
    pair_expert = routes.reshape(-1)
    pair_live = jnp.repeat(token_live, TOP)
    pair_hot = ((pair_expert[:, None] == expert_ids[None, :]) & pair_live[:, None]).astype(
        jnp.int32
    )
    running = jnp.cumsum(pair_hot, axis=0)
    pair_rank = jnp.sum((running - pair_hot) * pair_hot, axis=1)
    counts = running[-1]
    earlier = carried_in(
        counts, "dp", lambda former, latter: former + latter, jnp.zeros_like(counts)
    )
    pair_slot = jnp.sum(earlier[None, :] * pair_hot, axis=1) + pair_rank
    pair_kept = pair_live & (pair_slot < capacity)
    local_expert = pair_expert % EXP_DEV
    owner_index = pair_expert // EXP_DEV
    buffer_index = (local_expert * dp_count + owner_index) * most_rows + pair_rank
    target = jnp.where(pair_kept, buffer_index, slot_total)
    pair_ids = jnp.arange(block_rows * TOP, dtype=jnp.int32)
    slot_pair = jnp.full((slot_total,), -1, dtype=jnp.int32).at[target].set(pair_ids, mode="drop")
    slot_used = slot_pair >= 0
    slot_safe = jnp.maximum(slot_pair, 0)
    slot_token = slot_safe // TOP
    bf_zero = jnp.zeros((), jnp.bfloat16)
    send_rows = jnp.where(slot_used[:, None], normed_second[slot_token], bf_zero)
    layout = (EXP_DEV, dp_count, most_rows, features)
    received = to_owners(send_rows.reshape(layout)).reshape(EXP_DEV, dp_count * most_rows, features)
    gate_pre = jnp.einsum("end,edf->enf", received, expert_gate, preferred_element_type=jnp.float32)
    up_pre = jnp.einsum("end,edf->enf", received, expert_up, preferred_element_type=jnp.float32)
    sigmoid_gate = jax.nn.sigmoid(gate_pre)
    gate_act = gate_pre * sigmoid_gate
    hidden = (gate_act * up_pre).astype(jnp.bfloat16)
    out_partial = jnp.einsum(
        "enf,efd->end", hidden, expert_down, preferred_element_type=jnp.float32
    )
    expert_out = owner_reduce(out_partial)
    width = expert_out.shape[2]
    returned = lax.all_to_all(
        expert_out.reshape(EXP_DEV, dp_count, most_rows, width),
        "dp",
        split_axis=1,
        concat_axis=1,
        tiled=True,
    ).reshape(slot_total, width)
    pair_place = jnp.where(pair_kept, buffer_index, 0)
    pair_out = jnp.where(pair_kept[:, None], returned[pair_place], bf_zero).reshape(
        block_rows, TOP, width
    )
    expert_part = jnp.sum(gate_weights[:, :, None] * pair_out, axis=1)
    cot_full = cot_rows.astype(jnp.float32)
    own_start = tensor_index * own_rows
    gate_part = jnp.sum(cot_full[:, None, :] * pair_out, axis=-1)
    expert_own = lax.dynamic_slice_in_dim(expert_part, own_start, own_rows, 0)
    residual_own = lax.dynamic_slice_in_dim(residual, own_start, own_rows, 0)
    layer_output = (residual_own + expert_own).astype(jnp.bfloat16)
    slot_gate = jnp.where(slot_used, gate_weights.reshape(-1)[slot_safe], 0.0)
    send_cot = (slot_gate[:, None] * cot_full[slot_token]).astype(jnp.bfloat16)
    expert_cot = to_owners(send_cot.reshape(layout)).reshape(
        EXP_DEV, dp_count * most_rows, features
    )
    hidden_cot = jnp.einsum(
        "end,efd->enf", expert_cot, expert_down, preferred_element_type=jnp.float32
    )
    gating_cot = (
        hidden_cot * up_pre * sigmoid_gate * (1.0 + gate_pre * (1.0 - sigmoid_gate))
    ).astype(jnp.bfloat16)
    upward_cot = (hidden_cot * gate_act).astype(jnp.bfloat16)
    down_gradient = jnp.einsum(
        "enf,end->efd", hidden, expert_cot, preferred_element_type=jnp.float32
    )
    gate_gradient = jnp.einsum(
        "end,enf->edf", received, gating_cot, preferred_element_type=jnp.float32
    )
    up_gradient = jnp.einsum(
        "end,enf->edf", received, upward_cot, preferred_element_type=jnp.float32
    )
    row_partial = jnp.einsum(
        "enf,edf->end", gating_cot, expert_gate, preferred_element_type=jnp.float32
    )
    row_partial = row_partial + jnp.einsum(
        "enf,edf->end", upward_cot, expert_up, preferred_element_type=jnp.float32
    )
    row_cot = owner_reduce(row_partial)
    row_back = lax.all_to_all(
        row_cot.reshape(EXP_DEV, dp_count, most_rows, width),
        "dp",
        split_axis=1,
        concat_axis=1,
        tiled=True,
    ).reshape(slot_total, width)
    pair_cot = jnp.where(pair_kept[:, None], row_back[pair_place], bf_zero).reshape(
        block_rows, TOP, width
    )
    normed_part = jnp.sum(pair_cot.astype(jnp.float32), axis=1)
    normed_cot = normed_part
    route_cot = gate_weights * (
        gate_part - jnp.sum(gate_weights * gate_part, axis=-1, keepdims=True)
    )
    logit_cot = jnp.sum(jnp.where(route_hot, route_cot[:, :, None], 0.0), axis=1).astype(
        jnp.bfloat16
    )
    router_gradient = contract(normed_second, logit_cot)
    normed_cot = normed_cot + transposed(logit_cot, router_all)
    midnorm_gradient = jnp.sum(normed_cot * unit_second, axis=0)
    residual_cot = cot_full + norm_back(normed_cot * gain_two, unit_second, scale_second)
    attention_cot = residual_cot.astype(jnp.bfloat16)
    context_gradient = contract(context, attention_cot)
    context_cot = (
        transposed(attention_cot, context_all)
        .astype(jnp.bfloat16)
        .reshape(block_rows, heads_key, group_width, HEAD_SIZE)
    )
    scores = score_block()
    soft_probs = jnp.exp(scores - log_total)
    prob_cot = jnp.einsum(
        "ikrd,jkd->krij", context_cot, value_rows, preferred_element_type=jnp.float32
    )
    score_cot = (
        soft_probs * (prob_cot - jnp.sum(soft_probs * prob_cot, axis=-1, keepdims=True))
    ).astype(jnp.bfloat16)
    value_cot = jnp.einsum(
        "krij,ikrd->jkd",
        soft_probs.astype(jnp.bfloat16),
        context_cot,
        preferred_element_type=jnp.float32,
    )
    value_cot = value_cot.astype(jnp.bfloat16).reshape(block_rows, heads_key * HEAD_SIZE)
    query_turned = (
        jnp.einsum(
            "krij,jkd->ikrd", score_cot, keys_rot, preferred_element_type=jnp.float32
        ).reshape(block_rows, heads_query, HEAD_SIZE)
        * score_scale
    )
    key_turned = (
        jnp.einsum("krij,ikrd->jkd", score_cot, query_rows, preferred_element_type=jnp.float32)
        * score_scale
    )
    query_back = rotary_apply(query_turned, cosine_table, -sine_values)
    key_back = rotary_apply(key_turned, cosine_table, -sine_values)
    querynorm_part = jnp.sum(query_back * query_unit, axis=(0, 1))
    keynorm_part = jnp.sum(key_back * key_unit, axis=(0, 1))
    query_raw_cot = (
        norm_back(query_back * query_factor, query_unit, query_scale)
        .astype(jnp.bfloat16)
        .reshape(block_rows, heads_query * HEAD_SIZE)
    )
    key_raw_cot = (
        norm_back(key_back * key_factor, key_unit, key_scale)
        .astype(jnp.bfloat16)
        .reshape(block_rows, heads_key * HEAD_SIZE)
    )
    query_gradient = contract(first_layer_normed, query_raw_cot)
    key_gradient = contract(first_layer_normed, key_raw_cot)
    value_gradient = contract(first_layer_normed, value_cot)
    first_part = (
        transposed(query_raw_cot, query_all)
        + transposed(key_raw_cot, key_all)
        + transposed(value_cot, value_all)
    )
    first_cot, querynorm_gradient, keynorm_gradient = (
        lax.psum(first_part.astype(jnp.bfloat16), "tensor").astype(jnp.float32),
        lax.psum(querynorm_part.astype(jnp.bfloat16), "tensor").astype(jnp.float32),
        lax.psum(keynorm_part.astype(jnp.bfloat16), "tensor").astype(jnp.float32),
    )
    prenorm_gradient = jnp.sum(first_cot * unit_first, axis=0)
    input_cot = residual_cot + norm_back(first_cot * gain_one, unit_first, scale_first)
    input_gradient = lax.dynamic_slice_in_dim(input_cot, own_start, own_rows, 0).astype(
        jnp.bfloat16
    )
    summed = (
        lax.psum_scatter(query_gradient, "dp", scatter_dimension=0, tiled=True),
        lax.psum_scatter(key_gradient, "dp", scatter_dimension=0, tiled=True),
        lax.psum_scatter(value_gradient, "dp", scatter_dimension=0, tiled=True),
        lax.psum_scatter(context_gradient, "dp", scatter_dimension=1, tiled=True),
        lax.psum_scatter(router_gradient, "dp", scatter_dimension=0, tiled=True),
        lax.psum_scatter(prenorm_gradient, "dp", scatter_dimension=0, tiled=True),
        lax.psum_scatter(midnorm_gradient, "dp", scatter_dimension=0, tiled=True),
        lax.psum_scatter(querynorm_gradient, "dp", scatter_dimension=0, tiled=True),
        lax.psum_scatter(keynorm_gradient, "dp", scatter_dimension=0, tiled=True),
    )
    return (
        layer_output,
        input_gradient,
        summed[0],
        summed[1],
        summed[2],
        summed[3],
        summed[4],
        gate_gradient,
        up_gradient,
        down_gradient,
        summed[5],
        summed[6],
        summed[7],
        summed[8],
    )


AUX = 128


GRID_Z = 4
VMEM_LIMIT = 56 * 1024 * 1024


def remote(src, dst, send_sem, recv_sem, device):
    return pltpu.make_async_remote_copy(
        src_ref=src,
        dst_ref=dst,
        send_sem=send_sem,
        recv_sem=recv_sem,
        device_id=device,
        device_id_type=pl.DeviceIdType.MESH,
    )


class Place:
    def __init__(self):
        self.dp = lax.axis_index("dp")
        self.y = lax.axis_index("tensor")
        self.z = self.dp // 4
        self.x = (self.dp // 2) % 2
        self.core = self.dp % 2
        self.sibling = (self.dp + 1 - 2 * self.core, self.y)
        self.x_mate = (self.dp + 2 - 4 * self.x, self.y)
        self.y_mate = (self.dp, 1 - self.y)
        self.above = (self.dp + 4, self.y)
        self.below = (self.dp - 4, self.y)
        self.has_above = self.z < GRID_Z - 1
        self.has_below = self.z > 0

    def farthest(self, k):
        return (3 - 3 * (self.z // 2), (2 + 3 * self.z) % 5, 1 + self.z % 2, self.z)[k]

    def dp_at(self, z, flip_x, flip_core):
        x = self.x + flip_x * (1 - 2 * self.x)
        core = self.core + flip_core * (1 - 2 * self.core)
        return z * 4 + x * 2 + core

    def y_at(self, flip_y):
        return self.y + flip_y * (1 - 2 * self.y)

    def greet(self):
        barrier = pltpu.get_barrier_semaphore()
        for mate in (self.sibling, self.x_mate, self.y_mate):
            pl.semaphore_signal(barrier, 1, device_id=mate, device_id_type=pl.DeviceIdType.MESH)

        @pl.when(self.has_above)
        def _():
            pl.semaphore_signal(
                barrier, 1, device_id=self.above, device_id_type=pl.DeviceIdType.MESH
            )

        @pl.when(self.has_below)
        def _():
            pl.semaphore_signal(
                barrier, 1, device_id=self.below, device_id_type=pl.DeviceIdType.MESH
            )

        pl.semaphore_wait(barrier, 4 + self.z * (GRID_Z - 1 - self.z) // 2)


def add_rows(target, sources, rows, step=16):
    start, count = rows

    def one(i, carry):
        at = pl.ds(pl.multiple_of(start + i * step, step), step)
        total = target[at, :].astype(jnp.float32)
        for source, shift in sources:
            there = pl.ds(pl.multiple_of(start - shift + i * step, step), step)
            total = total + source[there, :].astype(jnp.float32)
        target[at, :] = total.astype(target.dtype)
        return carry

    lax.fori_loop(0, count // step, one, 0)


def scatter_kernel(
    part, out, own, core, diag_a, diag_b, from_x, from_y, from_z, result,
    load_s, core_s, diag_s, x_s, y_s, z_s, out_s,
):
    me = Place()
    rows = own.shape[3]
    half = rows // 2
    low, high = (0, half), (half, half)
    loads, sends = {}, []

    def chunk(k, flip_x, flip_y, flip_core):
        return part.at[me.dp_at(me.farthest(k), flip_x, flip_core) * 2 + me.y_at(flip_y)]

    order = ((1, 1), (1, 0), (0, 1), (0, 0))
    for k in range(GRID_Z):
        for fx, fy in order:
            copy = pltpu.make_async_copy(
                chunk(k, fx, fy, 0), own.at[k, fx, fy], load_s.at[k, fx, fy]
            )
            copy.start()
            loads[k, fx, fy] = copy
    me.greet()
    cores = {}
    for k in range(GRID_Z):
        for fx, fy in order:
            copy = remote(
                chunk(k, fx, fy, 1), core.at[k, fx, fy],
                core_s.at[0, k, fx, fy], core_s.at[1, k, fx, fy], me.sibling,
            )
            copy.start()
            cores[k, fx, fy] = copy
            sends.append(copy)

    da = [remote(own.at[k, 1, 1, pl.ds(0, half)], diag_a.at[k], diag_s.at[0, k], diag_s.at[1, k], me.y_mate) for k in range(4)]
    db = [remote(own.at[k, 1, 1, pl.ds(half, half)], diag_b.at[k], diag_s.at[2, k], diag_s.at[3, k], me.x_mate) for k in range(4)]
    xs = [[remote(own.at[k, 1, 0, pl.ds(h * half, half)], from_x.at[k, pl.ds(h * half, half)], x_s.at[0, k, h], x_s.at[1, k, h], me.x_mate) for h in range(2)] for k in range(4)]
    ys = [[remote(own.at[k, 0, 1, pl.ds(h * half, half)], from_y.at[k, pl.ds(h * half, half)], y_s.at[0, k, h], y_s.at[1, k, h], me.y_mate) for h in range(2)] for k in range(4)]

    def arrive(k, fx, fy):
        loads[k, fx, fy].wait()
        cores[k, fx, fy].wait_recv()

    def early(k):
        arrive(k, 1, 1)
        add_rows(own.at[k, 1, 1], [(core.at[k, 1, 1], 0)], low)
        da[k].start()
        add_rows(own.at[k, 1, 1], [(core.at[k, 1, 1], 0)], high)
        db[k].start()
        arrive(k, 1, 0)
        add_rows(own.at[k, 1, 0], [(core.at[k, 1, 0], 0)], high)
        xs[k][1].start()
        arrive(k, 0, 1)
        add_rows(own.at[k, 0, 1], [(core.at[k, 0, 1], 0)], low)
        ys[k][0].start()

    def late(k):
        da[k].wait_recv()
        add_rows(own.at[k, 1, 0], [(core.at[k, 1, 0], 0), (diag_a.at[k], 0)], low)
        xs[k][0].start()
        db[k].wait_recv()
        add_rows(own.at[k, 0, 1], [(core.at[k, 0, 1], 0), (diag_b.at[k], half)], high)
        ys[k][1].start()

    whole = (0, rows)

    def column(k):
        arrive(k, 0, 0)
        for h in range(2):
            xs[k][h].wait_recv()
            ys[k][h].wait_recv()
        mine = own.at[k, 0, 0]
        rest = [(core.at[k, 0, 0], 0), (from_x.at[k], 0), (from_y.at[k], 0)]
        if k < GRID_Z - 1:
            to = me.farthest(k)
            add_rows(mine, rest, whole)
            for side, ahead, mate, more in (
                (0, to > me.z, me.above, me.has_below),
                (1, to < me.z, me.below, me.has_above),
            ):
                copy = remote(
                    mine, from_z.at[side, to], z_s.at[0, side, to], z_s.at[1, side, to], mate
                )

                @pl.when(ahead)
                def _():
                    @pl.when(more)
                    def _():
                        copy.wait_recv()
                        add_rows(mine, [(from_z.at[side, to], 0)], whole)

                    copy.start()
        else:
            add_rows(mine, rest, whole)
            for side, more in ((0, me.has_below), (1, me.has_above)):
                copy = remote(
                    mine, from_z.at[side, me.z], z_s.at[0, side, me.z], z_s.at[1, side, me.z],
                    me.y_mate,
                )

                @pl.when(more)
                def _():
                    copy.wait_recv()
                    add_rows(mine, [(from_z.at[side, me.z], 0)], whole)

    early(0)
    early(1)
    late(0)
    early(2)
    late(1)
    column(0)
    early(3)
    late(2)
    column(1)
    late(3)
    column(2)
    column(3)
    copy = pltpu.make_async_copy(own.at[3, 0, 0], out, out_s)
    copy.start()
    for k in range(GRID_Z):
        da[k].wait_send()
        db[k].wait_send()
        for h in range(2):
            xs[k][h].wait_send()
            ys[k][h].wait_send()
        if k < GRID_Z - 1:
            to = me.farthest(k)
            for side, ahead, mate in ((0, to > me.z, me.above), (1, to < me.z, me.below)):
                @pl.when(ahead)
                def _():
                    remote(
                        own.at[k, 0, 0], from_z.at[side, to],
                        z_s.at[0, side, to], z_s.at[1, side, to], mate,
                    ).wait_send()
    for sent in sends:
        sent.wait_send()
    copy.wait()


def scatter_all(value, collective_id):
    devices = lax.axis_size("dp") * lax.axis_size("tensor")
    rows, width = value.shape[0] // devices, value.shape[1]
    half = rows // 2
    dma = pltpu.SemaphoreType.DMA
    low = value.dtype
    return pl.pallas_call(
        scatter_kernel,
        out_shape=jax.ShapeDtypeStruct((rows, width), low),
        in_specs=[pl.BlockSpec(memory_space=pl.ANY)],
        out_specs=pl.BlockSpec(memory_space=pl.ANY),
        scratch_shapes=[
            pltpu.VMEM((4, 2, 2, rows, width), low),
            pltpu.VMEM((4, 2, 2, rows, width), low),
            pltpu.VMEM((4, half, width), low),
            pltpu.VMEM((4, half, width), low),
            pltpu.VMEM((4, rows, width), low),
            pltpu.VMEM((4, rows, width), low),
            pltpu.VMEM((2, 4, rows, width), low),
            pltpu.VMEM((8, 128), low),
            dma((4, 2, 2)),
            dma((2, 4, 2, 2)),
            dma((4, 4)),
            dma((2, 4, 2)),
            dma((2, 4, 2)),
            dma((2, 2, 4)),
            dma(()),
        ],
        compiler_params=pltpu.CompilerParams(
            collective_id=collective_id, has_side_effects=True, vmem_limit_bytes=VMEM_LIMIT
        ),
    )(value.reshape(devices, rows, width))


def gather_kernel(src, out, own_s, z_s, x_s, y_s, dx_s, dy_s, core_s):
    me = Place()
    rows = src.shape[0]
    half = rows // 2
    low, high = pl.ds(0, half), pl.ds(half, half)

    def near(k):
        return me.farthest(GRID_Z - 1 - k)

    def at(k, fx, fy, fc):
        return out.at[me.dp_at(near(k), fx, fc) * 2 + me.y_at(fy)]

    mine = pltpu.make_async_copy(src, at(0, 0, 0, 0), own_s)
    mine.start()
    me.greet()

    def over(source, k, fx, fy, send, recv, mate):
        return remote(source, at(k, fx, fy, 0), send, recv, mate)

    def z_copy(k, source, side, mate):
        zn = near(k)
        return remote(source, at(k, 0, 0, 0), z_s.at[0, side, zn], z_s.at[1, side, zn], mate)

    xs, ys, dxs, dys, cores = {}, {}, {}, {}, {}
    for k in range(GRID_Z):
        source = src if k == 0 else at(k, 0, 0, 0)
        xs[k] = over(source, k, 0, 0, x_s.at[0, k], x_s.at[1, k], me.x_mate)
        ys[k] = over(source, k, 0, 0, y_s.at[0, k], y_s.at[1, k], me.y_mate)
        dys[k] = remote(at(k, 1, 0, 0).at[low], at(k, 1, 0, 0).at[low], dy_s.at[0, k], dy_s.at[1, k], me.y_mate)
        dxs[k] = remote(at(k, 0, 1, 0).at[high], at(k, 0, 1, 0).at[high], dx_s.at[0, k], dx_s.at[1, k], me.x_mate)
        for fx in range(2):
            for fy in range(2):
                block = source if (fx, fy) == (0, 0) else at(k, fx, fy, 0)
                if (fx, fy) == (1, 1):
                    for h, part in enumerate((low, high)):
                        cores[k, fx, fy, h] = remote(
                            block.at[part], block.at[part],
                            core_s.at[0, k, 3 + h], core_s.at[1, k, 3 + h], me.sibling,
                        )
                else:
                    cores[k, fx, fy] = remote(
                        block, at(k, fx, fy, 0), core_s.at[0, k, fx * 2 + fy],
                        core_s.at[1, k, fx * 2 + fy], me.sibling,
                    )

    def own(k):
        if k == 0:
            for side, more, mate in ((0, me.has_above, me.above), (1, me.has_below, me.below)):
                copy = z_copy(0, src, side, mate)

                @pl.when(more)
                def _():
                    copy.start()
        else:
            zn = near(k)
            for side, came, more, mate in (
                (0, zn < me.z, me.has_above, me.above),
                (1, zn > me.z, me.has_below, me.below),
            ):
                copy = z_copy(k, at(k, 0, 0, 0), side, mate)

                @pl.when(came)
                def _():
                    copy.wait_recv()

                    @pl.when(more)
                    def _():
                        copy.start()

        xs[k].start()
        ys[k].start()
        cores[k, 0, 0].start()

    def diag(k):
        xs[k].wait_recv()
        dys[k].start()
        cores[k, 1, 0].start()
        ys[k].wait_recv()
        dxs[k].start()
        cores[k, 0, 1].start()

    def corner(k):
        dys[k].wait_recv()
        cores[k, 1, 1, 0].start()
        dxs[k].wait_recv()
        cores[k, 1, 1, 1].start()

    own(0)
    own(1)
    diag(0)
    own(2)
    diag(1)
    corner(0)
    own(3)
    diag(2)
    corner(1)
    diag(3)
    corner(2)
    corner(3)
    mine.wait()
    for k in range(GRID_Z):
        zn = near(k)
        for side, came, more, mate in (
            (0, zn <= me.z, me.has_above, me.above),
            (1, zn >= me.z, me.has_below, me.below),
        ):
            copy = z_copy(k, src if k == 0 else at(k, 0, 0, 0), side, mate)

            @pl.when(came)
            def _():
                @pl.when(more)
                def _():
                    copy.wait_send()
        for copy in (xs[k], ys[k], dxs[k], dys[k]):
            copy.wait_send()
    for copy in cores.values():
        copy.wait()


def gather_all(value, collective_id):
    devices = lax.axis_size("dp") * lax.axis_size("tensor")
    rows, width = value.shape
    dma = pltpu.SemaphoreType.DMA
    return pl.pallas_call(
        gather_kernel,
        out_shape=jax.ShapeDtypeStruct((devices, rows, width), value.dtype),
        in_specs=[pl.BlockSpec(memory_space=pl.ANY)],
        out_specs=pl.BlockSpec(memory_space=pl.ANY),
        scratch_shapes=[
            dma(()),
            dma((2, 2, 4)),
            dma((2, 4)),
            dma((2, 4)),
            dma((2, 4)),
            dma((2, 4)),
            dma((2, 4, 5)),
        ],
        compiler_params=pltpu.CompilerParams(collective_id=collective_id, has_side_effects=True),
    )(value).reshape(devices * rows, width)


def plane_gather_kernel(src, out, own_s, z_s, x_s, core_s):
    me = Place()

    def near(k):
        return me.farthest(GRID_Z - 1 - k)

    def at(k, fx):
        return out.at[me.dp_at(near(k), fx, 0)]

    mine = pltpu.make_async_copy(src, at(0, 0), own_s)
    mine.start()
    me.greet()

    def z_copy(k, side, mate):
        zn = near(k)
        return remote(
            src if k == 0 else at(k, 0), at(k, 0), z_s.at[0, side, zn], z_s.at[1, side, zn], mate
        )

    xs, cores = {}, {}
    for k in range(GRID_Z):
        source = src if k == 0 else at(k, 0)
        xs[k] = remote(source, at(k, 0), x_s.at[0, k], x_s.at[1, k], me.x_mate)
        cores[k, 0] = remote(source, at(k, 0), core_s.at[0, k, 0], core_s.at[1, k, 0], me.sibling)
        cores[k, 1] = remote(at(k, 1), at(k, 1), core_s.at[0, k, 1], core_s.at[1, k, 1], me.sibling)

    def own(k):
        zn = near(k)
        for side, came, more, mate in (
            (0, zn < me.z, me.has_above, me.above),
            (1, zn > me.z, me.has_below, me.below),
        ):
            copy = z_copy(k, side, mate)
            if k == 0:

                @pl.when(more)
                def _():
                    copy.start()
            else:

                @pl.when(came)
                def _():
                    copy.wait_recv()

                    @pl.when(more)
                    def _():
                        copy.start()

        xs[k].start()
        cores[k, 0].start()

    def diag(k):
        xs[k].wait_recv()
        cores[k, 1].start()

    own(0)
    own(1)
    diag(0)
    own(2)
    diag(1)
    own(3)
    diag(2)
    diag(3)
    mine.wait()
    for k in range(GRID_Z):
        zn = near(k)
        for side, came, more, mate in (
            (0, zn <= me.z, me.has_above, me.above),
            (1, zn >= me.z, me.has_below, me.below),
        ):
            copy = z_copy(k, side, mate)

            @pl.when(came)
            def _():
                @pl.when(more)
                def _():
                    copy.wait_send()

        xs[k].wait_send()
    for copy in cores.values():
        copy.wait()


def gather_dp(value, collective_id):
    devices = lax.axis_size("dp")
    rows, width = value.shape
    dma = pltpu.SemaphoreType.DMA
    return pl.pallas_call(
        plane_gather_kernel,
        out_shape=jax.ShapeDtypeStruct((devices, rows, width), value.dtype),
        in_specs=[pl.BlockSpec(memory_space=pl.ANY)],
        out_specs=pl.BlockSpec(memory_space=pl.ANY),
        scratch_shapes=[dma(()), dma((2, 2, 4)), dma((2, 4)), dma((2, 4, 2))],
        compiler_params=pltpu.CompilerParams(collective_id=collective_id, has_side_effects=True),
    )(value).reshape(devices * rows, width)


def plane_scatter_kernel(
    part, out, own, core, from_x, from_z, load_s, core_s, x_s, z_s, out_s
):
    me = Place()
    rows = own.shape[2]
    whole = (0, rows)
    loads, cores = {}, {}

    def chunk(k, flip_x, flip_core):
        return part.at[me.dp_at(me.farthest(k), flip_x, flip_core)]

    for k in range(GRID_Z):
        for fx in (1, 0):
            loads[k, fx] = pltpu.make_async_copy(chunk(k, fx, 0), own.at[k, fx], load_s.at[k, fx])
            loads[k, fx].start()
    me.greet()
    for k in range(GRID_Z):
        for fx in (1, 0):
            cores[k, fx] = remote(
                chunk(k, fx, 1), core.at[k, fx],
                core_s.at[0, k, fx], core_s.at[1, k, fx], me.sibling,
            )
            cores[k, fx].start()
    half = rows // 2
    xs = [
        [
            remote(
                own.at[k, 1, pl.ds(h * half, half)], from_x.at[k, pl.ds(h * half, half)],
                x_s.at[0, k, h], x_s.at[1, k, h], me.x_mate,
            )
            for h in range(2)
        ]
        for k in range(GRID_Z)
    ]

    def z_copy(k, side, mate):
        to = me.farthest(k)
        return remote(
            own.at[k, 0], from_z.at[side, to], z_s.at[0, side, to], z_s.at[1, side, to], mate
        )

    def across(k):
        loads[k, 1].wait()
        cores[k, 1].wait_recv()
        for h in range(2):
            add_rows(own.at[k, 1], [(core.at[k, 1], 0)], (h * half, half))
            xs[k][h].start()

    def column(k):
        loads[k, 0].wait()
        cores[k, 0].wait_recv()
        for h in range(2):
            xs[k][h].wait_recv()
        mine = own.at[k, 0]
        add_rows(mine, [(core.at[k, 0], 0), (from_x.at[k], 0)], whole)
        to = me.farthest(k)
        for side, ahead, mate, more in (
            (0, to > me.z, me.above, me.has_below),
            (1, to < me.z, me.below, me.has_above),
        ):
            copy = z_copy(k, side, mate)
            if k < GRID_Z - 1:

                @pl.when(ahead)
                def _():
                    @pl.when(more)
                    def _():
                        copy.wait_recv()
                        add_rows(mine, [(from_z.at[side, to], 0)], whole)

                    copy.start()
            else:

                @pl.when(more)
                def _():
                    copy.wait_recv()
                    add_rows(mine, [(from_z.at[side, to], 0)], whole)

    for k in range(GRID_Z):
        across(k)
        if k:
            column(k - 1)
    column(GRID_Z - 1)
    copy = pltpu.make_async_copy(own.at[3, 0], out, out_s)
    copy.start()
    for k in range(GRID_Z):
        for h in range(2):
            xs[k][h].wait_send()
        if k < GRID_Z - 1:
            to = me.farthest(k)
            for side, ahead, mate in ((0, to > me.z, me.above), (1, to < me.z, me.below)):

                @pl.when(ahead)
                def _():
                    z_copy(k, side, mate).wait_send()
    for sent in cores.values():
        sent.wait_send()
    copy.wait()


def scatter_dp(value, collective_id):
    devices = lax.axis_size("dp")
    rows, width = value.shape[0] // devices, value.shape[1]
    dma = pltpu.SemaphoreType.DMA
    low = value.dtype
    return pl.pallas_call(
        plane_scatter_kernel,
        out_shape=jax.ShapeDtypeStruct((rows, width), low),
        in_specs=[pl.BlockSpec(memory_space=pl.ANY)],
        out_specs=pl.BlockSpec(memory_space=pl.ANY),
        scratch_shapes=[
            pltpu.VMEM((4, 2, rows, width), low),
            pltpu.VMEM((4, 2, rows, width), low),
            pltpu.VMEM((4, rows, width), low),
            pltpu.VMEM((2, 4, rows, width), low),
            dma((4, 2)),
            dma((2, 4, 2)),
            dma((2, 4, 2)),
            dma((2, 2, 4)),
            dma(()),
        ],
        compiler_params=pltpu.CompilerParams(
            collective_id=collective_id, has_side_effects=True, vmem_limit_bytes=VMEM_LIMIT
        ),
    )(value.reshape(devices, rows, width))


def split_high_low(value):
    high = value.astype(jnp.bfloat16)
    return high, (value - high.astype(jnp.float32)).astype(jnp.bfloat16)


def gathered_body(
    layer_input,
    query_weight,
    key_projection,
    value_projection,
    context_weight,
    router_weight,
    expert_gate,
    expert_up,
    expert_down,
    prenorm_gain,
    midnorm_gain,
    querynorm_gain,
    keynorm_gain,
    routes,
    lengths,
    sequence_order,
    output_cotangent,
):
    bf16, f32 = jnp.bfloat16, jnp.float32
    tensor_count = lax.axis_size("tensor")
    tensor_index = lax.axis_index("tensor")
    dp_count = lax.axis_size("dp")
    dp_index = lax.axis_index("dp")
    own_rows, features = layer_input.shape
    block_rows = own_rows * tensor_count
    tokens = block_rows * dp_count
    expert_count = EXP_DEV * dp_count
    capacity = 3 * block_rows * TOP // (4 * EXP_DEV)
    most_rows = (5 * block_rows * TOP + 4 * expert_count - 1) // (4 * expert_count)
    shard = features // dp_count
    query_width = query_weight.shape[1]
    key_width = key_projection.shape[1]
    norm_part = HEAD_SIZE // dp_count

    gains = jnp.zeros((shard, AUX - expert_count), bf16)
    gains = gains.at[:, 0].set(prenorm_gain).at[:, 1].set(midnorm_gain)
    gains = gains.at[:norm_part, 2].set(querynorm_gain).at[:norm_part, 3].set(keynorm_gain)
    packed = jnp.concatenate(
        [query_weight, key_projection, value_projection, context_weight.T, router_weight, gains],
        axis=1,
    )
    packed = gather_dp(packed, 0)
    edges = [0]
    for width in (query_width, key_width, key_width, query_width, expert_count, AUX - expert_count):
        edges.append(edges[-1] + width)
    qkv_all = packed[:, : edges[3]]
    context_all = packed[:, edges[3] : edges[4]]
    router_all = packed[:, edges[4] : edges[5]]
    gains_all = packed[:, edges[5] :].astype(f32)
    gain_one, gain_two = gains_all[:, 0], gains_all[:, 1]
    head_gains = gains_all.reshape(dp_count, shard, -1)[:, :norm_part, :]
    query_factor = head_gains[:, :, 2].reshape(-1)
    key_factor = head_gains[:, :, 3].reshape(-1)

    cot_all = lax.all_gather(output_cotangent, ("dp", "tensor"), axis=0, tiled=True)
    routes_all = lax.all_gather(routes, "dp", axis=0, tiled=True)
    input_rows = lax.all_gather(layer_input, "tensor", axis=0, tiled=True)
    position = jnp.arange(block_rows, dtype=jnp.int32)
    block_lengths = lengths[sequence_order]
    seq_length = block_lengths[dp_index]

    frequency = jnp.exp(
        -math.log(rope_base) * jnp.arange(HEAD_SIZE // 2, dtype=f32) * (2.0 / HEAD_SIZE)
    )
    angles = position.astype(f32)[:, None] * frequency[None, :]
    cosine_table = jnp.cos(angles)[:, None, :]
    sine_values = jnp.sin(angles)[:, None, :]
    heads_query = query_width // HEAD_SIZE
    heads_key = key_width // HEAD_SIZE
    group_width = heads_query // heads_key
    stream = input_rows.astype(f32)
    unit_first, scale_first = rms_normalize(stream)
    first_normed = (unit_first * gain_one).astype(bf16)
    raw = matrix_product(first_normed, qkv_all)
    query_unnormed = raw[:, : edges[1]].reshape(block_rows, heads_query, HEAD_SIZE)
    key_unnormed = raw[:, edges[1] : edges[2]].reshape(block_rows, heads_key, HEAD_SIZE)
    value_rows = raw[:, edges[2] :].astype(bf16).reshape(block_rows, heads_key, HEAD_SIZE)
    query_unit, query_scale = rms_normalize(query_unnormed)
    key_unit, key_scale = rms_normalize(key_unnormed)
    query_rows = (
        rotary_apply(query_unit * query_factor, cosine_table, sine_values)
        .astype(bf16)
        .reshape(block_rows, heads_key, group_width, HEAD_SIZE)
    )
    keys_rot = rotary_apply(key_unit * key_factor, cosine_table, sine_values).astype(bf16)
    score_scale = HEAD_SIZE ** (-0.5)
    allowed = (position[None, :] <= position[:, None]) & (position < seq_length)[None, :]
    scores = (
        jnp.einsum("ikrd,jkd->krij", query_rows, keys_rot, preferred_element_type=f32)
        * score_scale
    )
    scores = jnp.where(allowed, scores, masked_score)
    weights = jnp.exp(scores - jnp.max(scores, axis=-1, keepdims=True))
    soft_probs = weights / jnp.sum(weights, axis=-1, keepdims=True)
    probs_low = soft_probs.astype(bf16)
    context = jnp.einsum("krij,jkd->ikrd", probs_low, value_rows, preferred_element_type=f32)
    context = context.reshape(block_rows, query_width).astype(bf16)
    attention = lax.psum_scatter(
        transposed(context, context_all).astype(bf16),
        "tensor",
        scatter_dimension=0,
        tiled=True,
    )
    residual = layer_input.astype(f32) + attention.astype(f32)
    unit_second, scale_second = rms_normalize(residual)
    normed_second = (unit_second * gain_two).astype(bf16)

    normed_all = gather_all(normed_second, 1)
    logits = matrix_product(normed_all, router_all)
    expert_ids = jnp.arange(expert_count, dtype=jnp.int32)
    chosen = jnp.zeros((tokens, expert_count), jnp.bool_)
    for j in range(TOP):
        chosen = chosen | (routes_all[:, j : j + 1] == expert_ids[None, :])
    peak = jnp.max(jnp.where(chosen, logits, masked_score), axis=-1, keepdims=True)
    spread = jnp.where(chosen, jnp.exp(jnp.minimum(logits - peak, 0.0)), 0.0)
    gates = spread / jnp.sum(spread, axis=-1, keepdims=True)
    live = position[None, :] < block_lengths[:, None]
    hot = chosen.reshape(dp_count, block_rows, expert_count) & live[:, :, None]
    hot_low = hot.astype(bf16)
    below = (position[None, :] < position[:, None]).astype(bf16)
    rank = jnp.einsum("ts,bse->bte", below, hot_low, preferred_element_type=f32)
    counts = jnp.sum(hot.astype(f32), axis=1)
    earlier = jnp.cumsum(counts, axis=0) - counts
    kept = hot & (earlier[:, None, :] + rank < capacity)

    first_expert = dp_index * EXP_DEV
    rank_own = lax.dynamic_slice_in_dim(rank, first_expert, EXP_DEV, 2)
    kept_own = lax.dynamic_slice_in_dim(kept, first_expert, EXP_DEV, 2)
    gates_own = lax.dynamic_slice_in_dim(
        gates.reshape(dp_count, block_rows, expert_count), first_expert, EXP_DEV, 2
    )
    slots = jnp.arange(most_rows, dtype=f32)
    place = kept_own.transpose(0, 2, 1)[:, :, None, :] & (
        rank_own.transpose(0, 2, 1)[:, :, None, :] == slots[None, None, :, None]
    )
    place_low = place.astype(bf16).reshape(dp_count, EXP_DEV * most_rows, block_rows)
    slot_gate = jnp.sum(
        jnp.where(place, gates_own.transpose(0, 2, 1)[:, :, None, :], 0.0), axis=-1
    )
    slot_gate = slot_gate.transpose(1, 0, 2).reshape(EXP_DEV, dp_count * most_rows, 1)

    def take(rows):
        taken = jnp.einsum(
            "bst,btd->bsd",
            place_low,
            rows.reshape(dp_count, block_rows, features),
            preferred_element_type=f32,
        ).astype(bf16)
        return (
            taken.reshape(dp_count, EXP_DEV, most_rows, features)
            .transpose(1, 0, 2, 3)
            .reshape(EXP_DEV, dp_count * most_rows, features)
        )

    def put(slot_rows):
        ordered = (
            slot_rows.astype(bf16)
            .reshape(EXP_DEV, dp_count, most_rows, features)
            .transpose(1, 0, 2, 3)
            .reshape(dp_count, EXP_DEV * most_rows, features)
        )
        return (
            jnp.einsum("bst,bsd->btd", place_low, ordered, preferred_element_type=f32)
            .astype(bf16)
            .reshape(tokens, features)
        )

    rows_in = take(normed_all)
    cot_in = take(cot_all)
    gate_pre = jnp.einsum("end,edf->enf", rows_in, expert_gate, preferred_element_type=f32)
    up_pre = jnp.einsum("end,edf->enf", rows_in, expert_up, preferred_element_type=f32)
    sigmoid_gate = jax.nn.sigmoid(gate_pre)
    gate_act = gate_pre * sigmoid_gate
    hidden = (gate_act * up_pre).astype(bf16)
    out_partial = jnp.einsum("enf,efd->end", hidden, expert_down, preferred_element_type=f32)
    expert_sum = scatter_all(put(out_partial * slot_gate), 2)
    layer_output = (residual + expert_sum.astype(f32)).astype(bf16)

    down_cot = jnp.einsum("end,efd->enf", cot_in, expert_down, preferred_element_type=f32)
    slot_cot = jnp.sum(hidden.astype(f32) * down_cot, axis=-1)
    hidden_cot = down_cot * slot_gate
    gating_cot = (
        hidden_cot * up_pre * sigmoid_gate * (1.0 + gate_pre * (1.0 - sigmoid_gate))
    ).astype(bf16)
    upward_cot = (hidden_cot * gate_act).astype(bf16)
    hidden_gated = (hidden.astype(f32) * slot_gate).astype(bf16)
    down_gradient = jnp.einsum("enf,end->efd", hidden_gated, cot_in, preferred_element_type=f32)
    gate_gradient = jnp.einsum("end,enf->edf", rows_in, gating_cot, preferred_element_type=f32)
    up_gradient = jnp.einsum("end,enf->edf", rows_in, upward_cot, preferred_element_type=f32)
    row_partial = jnp.einsum("enf,edf->end", gating_cot, expert_gate, preferred_element_type=f32)
    row_partial = row_partial + jnp.einsum(
        "enf,edf->end", upward_cot, expert_up, preferred_element_type=f32
    )
    slot_cot = slot_cot.reshape(EXP_DEV, dp_count, most_rows).transpose(1, 0, 2)
    token_cot = jnp.sum(jnp.where(place, slot_cot[:, :, :, None], 0.0), axis=2)
    token_cot = token_cot.transpose(0, 2, 1).reshape(tokens, EXP_DEV)
    high, low = split_high_low(token_cot)
    quad = jnp.stack([high, low], axis=-1).reshape(tokens, 2 * EXP_DEV)
    aux = lax.dynamic_update_slice(
        jnp.zeros((tokens, 2 * tensor_count * expert_count), bf16),
        quad,
        (0, tensor_index * 2 * expert_count + dp_index * 2 * EXP_DEV),
    )
    returned = scatter_all(jnp.concatenate([put(row_partial), aux], axis=1), 3).astype(f32)
    gate_cot = jnp.sum(
        returned[:, features:].reshape(own_rows, tensor_count, expert_count, 2), axis=(1, 3)
    )
    own_start = (dp_index * tensor_count + tensor_index) * own_rows
    gates_mine = lax.dynamic_slice_in_dim(gates, own_start, own_rows, 0)
    logit_cot = (
        gates_mine * (gate_cot - jnp.sum(gates_mine * gate_cot, axis=-1, keepdims=True))
    ).astype(bf16)
    router_part = contract(normed_second, logit_cot)
    normed_cot = returned[:, :features] + transposed(logit_cot, router_all)
    midnorm_part = jnp.sum(normed_cot * unit_second, axis=0)
    residual_cot = output_cotangent.astype(f32) + norm_back(
        normed_cot * gain_two, unit_second, scale_second
    )
    attention_cot = lax.all_gather(residual_cot.astype(bf16), "tensor", axis=0, tiled=True)

    context_part = contract(attention_cot, context)
    context_cot = (
        matrix_product(attention_cot, context_all)
        .astype(bf16)
        .reshape(block_rows, heads_key, group_width, HEAD_SIZE)
    )
    prob_cot = jnp.einsum("ikrd,jkd->krij", context_cot, value_rows, preferred_element_type=f32)
    score_cot = (
        soft_probs * (prob_cot - jnp.sum(soft_probs * prob_cot, axis=-1, keepdims=True))
    ).astype(bf16)
    value_cot = jnp.einsum("krij,ikrd->jkd", probs_low, context_cot, preferred_element_type=f32)
    value_cot = value_cot.astype(bf16).reshape(block_rows, key_width)
    query_turned = (
        jnp.einsum("krij,jkd->ikrd", score_cot, keys_rot, preferred_element_type=f32).reshape(
            block_rows, heads_query, HEAD_SIZE
        )
        * score_scale
    )
    key_turned = (
        jnp.einsum("krij,ikrd->jkd", score_cot, query_rows, preferred_element_type=f32)
        * score_scale
    )
    query_back = rotary_apply(query_turned, cosine_table, -sine_values)
    key_back = rotary_apply(key_turned, cosine_table, -sine_values)
    querynorm_part = jnp.sum(query_back * query_unit, axis=(0, 1))
    keynorm_part = jnp.sum(key_back * key_unit, axis=(0, 1))
    query_raw_cot = norm_back(query_back * query_factor, query_unit, query_scale).astype(bf16)
    key_raw_cot = norm_back(key_back * key_factor, key_unit, key_scale).astype(bf16)
    raw_cot = jnp.concatenate(
        [
            query_raw_cot.reshape(block_rows, query_width),
            key_raw_cot.reshape(block_rows, key_width),
            value_cot,
        ],
        axis=1,
    )
    qkv_part = contract(first_normed, raw_cot)
    first_cot = lax.psum_scatter(
        transposed(raw_cot, qkv_all).astype(bf16), "tensor", scatter_dimension=0, tiled=True
    ).astype(f32)
    row_start = tensor_index * own_rows
    unit_own = lax.dynamic_slice_in_dim(unit_first, row_start, own_rows, 0)
    scale_own = lax.dynamic_slice_in_dim(scale_first, row_start, own_rows, 0)
    prenorm_part = jnp.sum(first_cot * unit_own, axis=0)
    input_gradient = (
        residual_cot + norm_back(first_cot * gain_one, unit_own, scale_own)
    ).astype(bf16)

    small = jnp.zeros((dp_count, shard, AUX), f32)
    small = small.at[:, :, :expert_count].set(router_part.reshape(dp_count, shard, expert_count))
    small = small.at[:, :, expert_count].set(prenorm_part.reshape(dp_count, shard))
    small = small.at[:, :, expert_count + 1].set(midnorm_part.reshape(dp_count, shard))
    small = small.at[:, :norm_part, expert_count + 2].set(querynorm_part.reshape(dp_count, -1))
    small = small.at[:, :norm_part, expert_count + 3].set(keynorm_part.reshape(dp_count, -1))
    small = lax.psum_scatter(small.reshape(features, AUX), "dp", scatter_dimension=0, tiled=True)
    small = lax.psum(small, "tensor")
    summed = scatter_dp(jnp.concatenate([qkv_part.astype(bf16), context_part.astype(bf16)], axis=1), 4)
    summed = summed.astype(f32)
    return (
        layer_output,
        input_gradient,
        summed[:, : edges[1]],
        summed[:, edges[1] : edges[2]],
        summed[:, edges[2] : edges[3]],
        summed[:, edges[3] :].T,
        small[:, :expert_count],
        gate_gradient,
        up_gradient,
        down_gradient,
        small[:, expert_count],
        small[:, expert_count + 1],
        small[:norm_part, expert_count + 2],
        small[:norm_part, expert_count + 3],
    )


def solution(mesh):
    return jax.shard_map(
        gathered_body if mesh.shape["dp"] <= 16 else body,
        mesh=mesh,
        in_specs=(
            P(("dp", "tensor"), None),
            P("dp", "tensor"),
            P("dp", "tensor"),
            P("dp", "tensor"),
            P("tensor", "dp"),
            P("dp", None),
            P("dp", None, "tensor"),
            P("dp", None, "tensor"),
            P("dp", "tensor", None),
            P("dp"),
            P("dp"),
            P("dp"),
            P("dp"),
            P("dp", None),
            P(),
            P(),
            P(("dp", "tensor"), None),
        ),
        out_specs=(
            P(("dp", "tensor"), None),
            P(("dp", "tensor"), None),
            P("dp", "tensor"),
            P("dp", "tensor"),
            P("dp", "tensor"),
            P("tensor", "dp"),
            P("dp", None),
            P("dp", None, "tensor"),
            P("dp", None, "tensor"),
            P("dp", "tensor", None),
            P("dp"),
            P("dp"),
            P("dp"),
            P("dp"),
        ),
        check_vma=False,
    )
```

```python
import math

import jax
import jax.numpy as jnp
from jax import lax
from jax.experimental import pallas as pl
from jax.experimental.pallas import tpu as pltpu
from jax.sharding import PartitionSpec as P

HEAD_SIZE = 128
TOP = 8
EXP_DEV = 2


epsilon = 1e-06
rope_base = 1000000.0
masked_score = -1e30


def carried_in(value, axis, combine, identity):
    count, place = (lax.axis_size(axis), lax.axis_index(axis))
    everything = lax.all_gather(value, axis)
    start = jnp.broadcast_to(jnp.asarray(identity, value.dtype), value.shape)

    def hop(k, before):
        reached = k < place
        new = combine(before, everything[k])
        return jnp.where(reached, new, before)

    return lax.fori_loop(0, count, hop, start)


def rms_normalize(value_rows):
    scaling = lax.rsqrt(jnp.mean(value_rows * value_rows, axis=-1, keepdims=True) + epsilon)
    return (value_rows * scaling, scaling)


def norm_back(cotangent, unit_rows, scaling):
    return scaling * (
        cotangent - unit_rows * jnp.mean(cotangent * unit_rows, axis=-1, keepdims=True)
    )


def rotary_apply(value_rows, cosine_table, sine_values):
    middle = value_rows.shape[-1] // 2
    former = value_rows[..., :middle]
    latter = value_rows[..., middle:]
    return jnp.concatenate(
        [
            former * cosine_table - latter * sine_values,
            latter * cosine_table + former * sine_values,
        ],
        axis=-1,
    )


def matrix_product(former, latter):
    return jnp.dot(former, latter, preferred_element_type=jnp.float32)


def contract(former, latter):
    return lax.dot_general(
        former, latter, (((0,), (0,)), ((), ())), preferred_element_type=jnp.float32
    )


def transposed(former, latter):
    return lax.dot_general(
        former, latter, (((1,), (1,)), ((), ())), preferred_element_type=jnp.float32
    )


def to_owners(buffer):
    return lax.all_to_all(buffer, "dp", split_axis=1, concat_axis=1, tiled=True)


def owner_reduce(partial_rows):
    shares = lax.psum_scatter(
        partial_rows.astype(jnp.bfloat16), "tensor", scatter_dimension=2, tiled=True
    )
    return lax.all_gather(shares, "tensor", axis=2, tiled=True)


def body(
    layer_input,
    query_weight,
    key_projection,
    value_projection,
    context_weight,
    router_weight,
    expert_gate,
    expert_up,
    expert_down,
    prenorm_gain,
    midnorm_gain,
    querynorm_gain,
    keynorm_gain,
    routes,
    lengths,
    sequence_order,
    output_cotangent,
):
    tensor_count = lax.axis_size("tensor")
    tensor_index = lax.axis_index("tensor")
    dp_count = lax.axis_size("dp")
    own_rows = layer_input.shape[0]
    block_rows = own_rows * tensor_count
    features = layer_input.shape[1]
    expert_count = EXP_DEV * dp_count
    capacity = 3 * block_rows * TOP // (4 * EXP_DEV)
    most_rows = (5 * block_rows * TOP + 4 * expert_count - 1) // (4 * expert_count)
    slot_total = EXP_DEV * dp_count * most_rows
    (
        query_all,
        key_all,
        value_all,
        context_all,
        router_all,
        gain_first,
        gain_second,
        query_gain,
        gain_key,
    ) = (
        lax.all_gather(query_weight, "dp", axis=0, tiled=True),
        lax.all_gather(key_projection, "dp", axis=0, tiled=True),
        lax.all_gather(value_projection, "dp", axis=0, tiled=True),
        lax.all_gather(context_weight, "dp", axis=1, tiled=True),
        lax.all_gather(router_weight, "dp", axis=0, tiled=True),
        lax.all_gather(prenorm_gain, "dp", axis=0, tiled=True),
        lax.all_gather(midnorm_gain, "dp", axis=0, tiled=True),
        lax.all_gather(querynorm_gain, "dp", axis=0, tiled=True),
        lax.all_gather(keynorm_gain, "dp", axis=0, tiled=True),
    )
    input_rows, cot_rows = (
        lax.all_gather(layer_input, "tensor", axis=0, tiled=True),
        lax.all_gather(output_cotangent, "tensor", axis=0, tiled=True),
    )
    position = jnp.arange(block_rows, dtype=jnp.int32)
    seq_length = lengths[sequence_order[lax.axis_index("dp")]]
    token_live = position < seq_length
    frequency = jnp.exp(
        -math.log(rope_base) * jnp.arange(HEAD_SIZE // 2, dtype=jnp.float32) * (2.0 / HEAD_SIZE)
    )
    angles = position.astype(jnp.float32)[:, None] * frequency[None, :]
    cosine_table = jnp.cos(angles)[:, None, :]
    sine_values = jnp.sin(angles)[:, None, :]
    heads_query = query_all.shape[1] // HEAD_SIZE
    heads_key = key_all.shape[1] // HEAD_SIZE
    group_width = heads_query // heads_key
    gain_one = gain_first.astype(jnp.float32)
    gain_two = gain_second.astype(jnp.float32)
    query_factor = query_gain.astype(jnp.float32)
    key_factor = gain_key.astype(jnp.float32)
    stream = input_rows.astype(jnp.float32)
    unit_first, scale_first = rms_normalize(stream)
    first_layer_normed = (unit_first * gain_one).astype(jnp.bfloat16)
    query_unnormed = matrix_product(first_layer_normed, query_all).reshape(
        block_rows, heads_query, HEAD_SIZE
    )
    key_unnormed = matrix_product(first_layer_normed, key_all).reshape(
        block_rows, heads_key, HEAD_SIZE
    )
    value_rows = (
        matrix_product(first_layer_normed, value_all)
        .astype(jnp.bfloat16)
        .reshape(block_rows, heads_key, HEAD_SIZE)
    )
    query_unit, query_scale = rms_normalize(query_unnormed)
    key_unit, key_scale = rms_normalize(key_unnormed)
    query_rows = (
        rotary_apply(query_unit * query_factor, cosine_table, sine_values)
        .astype(jnp.bfloat16)
        .reshape(block_rows, heads_key, group_width, HEAD_SIZE)
    )
    keys_rot = rotary_apply(key_unit * key_factor, cosine_table, sine_values).astype(jnp.bfloat16)
    score_scale = HEAD_SIZE ** (-0.5)
    allowed = (position[None, :] <= position[:, None]) & token_live[None, :]

    def score_block():
        raw_scores = (
            jnp.einsum("ikrd,jkd->krij", query_rows, keys_rot, preferred_element_type=jnp.float32)
            * score_scale
        )
        return jnp.where(allowed, raw_scores, masked_score)

    scores = score_block()
    row_peak = jnp.max(scores, axis=-1, keepdims=True)
    log_total = row_peak + jnp.log(jnp.sum(jnp.exp(scores - row_peak), axis=-1, keepdims=True))
    soft_probs = jnp.exp(scores - log_total)
    context = jnp.einsum(
        "krij,jkd->ikrd",
        soft_probs.astype(jnp.bfloat16),
        value_rows,
        preferred_element_type=jnp.float32,
    )
    context = context.reshape(block_rows, heads_query * HEAD_SIZE).astype(jnp.bfloat16)
    attention = lax.psum(matrix_product(context, context_all), "tensor")
    residual = stream + attention
    unit_second, scale_second = rms_normalize(residual)
    normed_second = (unit_second * gain_two).astype(jnp.bfloat16)
    logits = matrix_product(normed_second, router_all)
    expert_ids = jnp.arange(expert_count, dtype=jnp.int32)
    route_hot = routes[:, :, None] == expert_ids[None, None, :]
    chosen = jnp.sum(jnp.where(route_hot, logits[:, None, :], 0.0), axis=-1)
    gate_weights = jax.nn.softmax(chosen, axis=-1)
    pair_expert = routes.reshape(-1)
    pair_live = jnp.repeat(token_live, TOP)
    pair_hot = ((pair_expert[:, None] == expert_ids[None, :]) & pair_live[:, None]).astype(
        jnp.int32
    )
    running = jnp.cumsum(pair_hot, axis=0)
    pair_rank = jnp.sum((running - pair_hot) * pair_hot, axis=1)
    counts = running[-1]
    earlier = carried_in(
        counts, "dp", lambda former, latter: former + latter, jnp.zeros_like(counts)
    )
    pair_slot = jnp.sum(earlier[None, :] * pair_hot, axis=1) + pair_rank
    pair_kept = pair_live & (pair_slot < capacity)
    local_expert = pair_expert % EXP_DEV
    owner_index = pair_expert // EXP_DEV
    buffer_index = (local_expert * dp_count + owner_index) * most_rows + pair_rank
    target = jnp.where(pair_kept, buffer_index, slot_total)
    pair_ids = jnp.arange(block_rows * TOP, dtype=jnp.int32)
    slot_pair = jnp.full((slot_total,), -1, dtype=jnp.int32).at[target].set(pair_ids, mode="drop")
    slot_used = slot_pair >= 0
    slot_safe = jnp.maximum(slot_pair, 0)
    slot_token = slot_safe // TOP
    bf_zero = jnp.zeros((), jnp.bfloat16)
    send_rows = jnp.where(slot_used[:, None], normed_second[slot_token], bf_zero)
    layout = (EXP_DEV, dp_count, most_rows, features)
    received = to_owners(send_rows.reshape(layout)).reshape(EXP_DEV, dp_count * most_rows, features)
    gate_pre = jnp.einsum("end,edf->enf", received, expert_gate, preferred_element_type=jnp.float32)
    up_pre = jnp.einsum("end,edf->enf", received, expert_up, preferred_element_type=jnp.float32)
    sigmoid_gate = jax.nn.sigmoid(gate_pre)
    gate_act = gate_pre * sigmoid_gate
    hidden = (gate_act * up_pre).astype(jnp.bfloat16)
    out_partial = jnp.einsum(
        "enf,efd->end", hidden, expert_down, preferred_element_type=jnp.float32
    )
    expert_out = owner_reduce(out_partial)
    width = expert_out.shape[2]
    returned = lax.all_to_all(
        expert_out.reshape(EXP_DEV, dp_count, most_rows, width),
        "dp",
        split_axis=1,
        concat_axis=1,
        tiled=True,
    ).reshape(slot_total, width)
    pair_place = jnp.where(pair_kept, buffer_index, 0)
    pair_out = jnp.where(pair_kept[:, None], returned[pair_place], bf_zero).reshape(
        block_rows, TOP, width
    )
    expert_part = jnp.sum(gate_weights[:, :, None] * pair_out, axis=1)
    cot_full = cot_rows.astype(jnp.float32)
    own_start = tensor_index * own_rows
    gate_part = jnp.sum(cot_full[:, None, :] * pair_out, axis=-1)
    expert_own = lax.dynamic_slice_in_dim(expert_part, own_start, own_rows, 0)
    residual_own = lax.dynamic_slice_in_dim(residual, own_start, own_rows, 0)
    layer_output = (residual_own + expert_own).astype(jnp.bfloat16)
    slot_gate = jnp.where(slot_used, gate_weights.reshape(-1)[slot_safe], 0.0)
    send_cot = (slot_gate[:, None] * cot_full[slot_token]).astype(jnp.bfloat16)
    expert_cot = to_owners(send_cot.reshape(layout)).reshape(
        EXP_DEV, dp_count * most_rows, features
    )
    hidden_cot = jnp.einsum(
        "end,efd->enf", expert_cot, expert_down, preferred_element_type=jnp.float32
    )
    gating_cot = (
        hidden_cot * up_pre * sigmoid_gate * (1.0 + gate_pre * (1.0 - sigmoid_gate))
    ).astype(jnp.bfloat16)
    upward_cot = (hidden_cot * gate_act).astype(jnp.bfloat16)
    down_gradient = jnp.einsum(
        "enf,end->efd", hidden, expert_cot, preferred_element_type=jnp.float32
    )
    gate_gradient = jnp.einsum(
        "end,enf->edf", received, gating_cot, preferred_element_type=jnp.float32
    )
    up_gradient = jnp.einsum(
        "end,enf->edf", received, upward_cot, preferred_element_type=jnp.float32
    )
    row_partial = jnp.einsum(
        "enf,edf->end", gating_cot, expert_gate, preferred_element_type=jnp.float32
    )
    row_partial = row_partial + jnp.einsum(
        "enf,edf->end", upward_cot, expert_up, preferred_element_type=jnp.float32
    )
    row_cot = owner_reduce(row_partial)
    row_back = lax.all_to_all(
        row_cot.reshape(EXP_DEV, dp_count, most_rows, width),
        "dp",
        split_axis=1,
        concat_axis=1,
        tiled=True,
    ).reshape(slot_total, width)
    pair_cot = jnp.where(pair_kept[:, None], row_back[pair_place], bf_zero).reshape(
        block_rows, TOP, width
    )
    normed_part = jnp.sum(pair_cot.astype(jnp.float32), axis=1)
    normed_cot = normed_part
    route_cot = gate_weights * (
        gate_part - jnp.sum(gate_weights * gate_part, axis=-1, keepdims=True)
    )
    logit_cot = jnp.sum(jnp.where(route_hot, route_cot[:, :, None], 0.0), axis=1).astype(
        jnp.bfloat16
    )
    router_gradient = contract(normed_second, logit_cot)
    normed_cot = normed_cot + transposed(logit_cot, router_all)
    midnorm_gradient = jnp.sum(normed_cot * unit_second, axis=0)
    residual_cot = cot_full + norm_back(normed_cot * gain_two, unit_second, scale_second)
    attention_cot = residual_cot.astype(jnp.bfloat16)
    context_gradient = contract(context, attention_cot)
    context_cot = (
        transposed(attention_cot, context_all)
        .astype(jnp.bfloat16)
        .reshape(block_rows, heads_key, group_width, HEAD_SIZE)
    )
    scores = score_block()
    soft_probs = jnp.exp(scores - log_total)
    prob_cot = jnp.einsum(
        "ikrd,jkd->krij", context_cot, value_rows, preferred_element_type=jnp.float32
    )
    score_cot = (
        soft_probs * (prob_cot - jnp.sum(soft_probs * prob_cot, axis=-1, keepdims=True))
    ).astype(jnp.bfloat16)
    value_cot = jnp.einsum(
        "krij,ikrd->jkd",
        soft_probs.astype(jnp.bfloat16),
        context_cot,
        preferred_element_type=jnp.float32,
    )
    value_cot = value_cot.astype(jnp.bfloat16).reshape(block_rows, heads_key * HEAD_SIZE)
    query_turned = (
        jnp.einsum(
            "krij,jkd->ikrd", score_cot, keys_rot, preferred_element_type=jnp.float32
        ).reshape(block_rows, heads_query, HEAD_SIZE)
        * score_scale
    )
    key_turned = (
        jnp.einsum("krij,ikrd->jkd", score_cot, query_rows, preferred_element_type=jnp.float32)
        * score_scale
    )
    query_back = rotary_apply(query_turned, cosine_table, -sine_values)
    key_back = rotary_apply(key_turned, cosine_table, -sine_values)
    querynorm_part = jnp.sum(query_back * query_unit, axis=(0, 1))
    keynorm_part = jnp.sum(key_back * key_unit, axis=(0, 1))
    query_raw_cot = (
        norm_back(query_back * query_factor, query_unit, query_scale)
        .astype(jnp.bfloat16)
        .reshape(block_rows, heads_query * HEAD_SIZE)
    )
    key_raw_cot = (
        norm_back(key_back * key_factor, key_unit, key_scale)
        .astype(jnp.bfloat16)
        .reshape(block_rows, heads_key * HEAD_SIZE)
    )
    query_gradient = contract(first_layer_normed, query_raw_cot)
    key_gradient = contract(first_layer_normed, key_raw_cot)
    value_gradient = contract(first_layer_normed, value_cot)
    first_part = (
        transposed(query_raw_cot, query_all)
        + transposed(key_raw_cot, key_all)
        + transposed(value_cot, value_all)
    )
    first_cot, querynorm_gradient, keynorm_gradient = (
        lax.psum(first_part.astype(jnp.bfloat16), "tensor").astype(jnp.float32),
        lax.psum(querynorm_part.astype(jnp.bfloat16), "tensor").astype(jnp.float32),
        lax.psum(keynorm_part.astype(jnp.bfloat16), "tensor").astype(jnp.float32),
    )
    prenorm_gradient = jnp.sum(first_cot * unit_first, axis=0)
    input_cot = residual_cot + norm_back(first_cot * gain_one, unit_first, scale_first)
    input_gradient = lax.dynamic_slice_in_dim(input_cot, own_start, own_rows, 0).astype(
        jnp.bfloat16
    )
    summed = (
        lax.psum_scatter(query_gradient, "dp", scatter_dimension=0, tiled=True),
        lax.psum_scatter(key_gradient, "dp", scatter_dimension=0, tiled=True),
        lax.psum_scatter(value_gradient, "dp", scatter_dimension=0, tiled=True),
        lax.psum_scatter(context_gradient, "dp", scatter_dimension=1, tiled=True),
        lax.psum_scatter(router_gradient, "dp", scatter_dimension=0, tiled=True),
        lax.psum_scatter(prenorm_gradient, "dp", scatter_dimension=0, tiled=True),
        lax.psum_scatter(midnorm_gradient, "dp", scatter_dimension=0, tiled=True),
        lax.psum_scatter(querynorm_gradient, "dp", scatter_dimension=0, tiled=True),
        lax.psum_scatter(keynorm_gradient, "dp", scatter_dimension=0, tiled=True),
    )
    return (
        layer_output,
        input_gradient,
        summed[0],
        summed[1],
        summed[2],
        summed[3],
        summed[4],
        gate_gradient,
        up_gradient,
        down_gradient,
        summed[5],
        summed[6],
        summed[7],
        summed[8],
    )


AUX = 128


GRID_Z = 4
VMEM_LIMIT = 56 * 1024 * 1024


def remote(src, dst, send_sem, recv_sem, device):
    return pltpu.make_async_remote_copy(
        src_ref=src,
        dst_ref=dst,
        send_sem=send_sem,
        recv_sem=recv_sem,
        device_id=device,
        device_id_type=pl.DeviceIdType.MESH,
    )


class Place:
    def __init__(self):
        self.dp = lax.axis_index("dp")
        self.y = lax.axis_index("tensor")
        self.z = self.dp // 4
        self.x = (self.dp // 2) % 2
        self.core = self.dp % 2
        self.sibling = (self.dp + 1 - 2 * self.core, self.y)
        self.x_mate = (self.dp + 2 - 4 * self.x, self.y)
        self.y_mate = (self.dp, 1 - self.y)
        self.above = (self.dp + 4, self.y)
        self.below = (self.dp - 4, self.y)
        self.has_above = self.z < GRID_Z - 1
        self.has_below = self.z > 0

    def farthest(self, k):
        return (3 - 3 * (self.z // 2), (2 + 3 * self.z) % 5, 1 + self.z % 2, self.z)[k]

    def dp_at(self, z, flip_x, flip_core):
        x = self.x + flip_x * (1 - 2 * self.x)
        core = self.core + flip_core * (1 - 2 * self.core)
        return z * 4 + x * 2 + core

    def y_at(self, flip_y):
        return self.y + flip_y * (1 - 2 * self.y)

    def greet(self):
        barrier = pltpu.get_barrier_semaphore()
        for mate in (self.sibling, self.x_mate, self.y_mate):
            pl.semaphore_signal(barrier, 1, device_id=mate, device_id_type=pl.DeviceIdType.MESH)

        @pl.when(self.has_above)
        def _():
            pl.semaphore_signal(
                barrier, 1, device_id=self.above, device_id_type=pl.DeviceIdType.MESH
            )

        @pl.when(self.has_below)
        def _():
            pl.semaphore_signal(
                barrier, 1, device_id=self.below, device_id_type=pl.DeviceIdType.MESH
            )

        pl.semaphore_wait(barrier, 4 + self.z * (GRID_Z - 1 - self.z) // 2)


def add_rows(target, sources, rows, step=16):
    start, count = rows

    def one(i, carry):
        at = pl.ds(pl.multiple_of(start + i * step, step), step)
        total = target[at, :].astype(jnp.float32)
        for source, shift in sources:
            there = pl.ds(pl.multiple_of(start - shift + i * step, step), step)
            total = total + source[there, :].astype(jnp.float32)
        target[at, :] = total.astype(target.dtype)
        return carry

    lax.fori_loop(0, count // step, one, 0)


def scatter_kernel(
    part, out, own, core, diag_a, diag_b, from_x, from_y, from_z, result,
    load_s, core_s, diag_s, x_s, y_s, z_s, out_s,
):
    me = Place()
    rows = own.shape[3]
    half = rows // 2
    low, high = (0, half), (half, half)
    loads, sends = {}, []

    def chunk(k, flip_x, flip_y, flip_core):
        return part.at[me.dp_at(me.farthest(k), flip_x, flip_core) * 2 + me.y_at(flip_y)]

    order = ((1, 1), (1, 0), (0, 1), (0, 0))
    for k in range(GRID_Z):
        for fx, fy in order:
            copy = pltpu.make_async_copy(
                chunk(k, fx, fy, 0), own.at[k, fx, fy], load_s.at[k, fx, fy]
            )
            copy.start()
            loads[k, fx, fy] = copy
    me.greet()
    cores = {}
    for k in range(GRID_Z):
        for fx, fy in order:
            copy = remote(
                chunk(k, fx, fy, 1), core.at[k, fx, fy],
                core_s.at[0, k, fx, fy], core_s.at[1, k, fx, fy], me.sibling,
            )
            copy.start()
            cores[k, fx, fy] = copy
            sends.append(copy)

    da = [remote(own.at[k, 1, 1, pl.ds(0, half)], diag_a.at[k], diag_s.at[0, k], diag_s.at[1, k], me.y_mate) for k in range(4)]
    db = [remote(own.at[k, 1, 1, pl.ds(half, half)], diag_b.at[k], diag_s.at[2, k], diag_s.at[3, k], me.x_mate) for k in range(4)]
    xs = [[remote(own.at[k, 1, 0, pl.ds(h * half, half)], from_x.at[k, pl.ds(h * half, half)], x_s.at[0, k, h], x_s.at[1, k, h], me.x_mate) for h in range(2)] for k in range(4)]
    ys = [[remote(own.at[k, 0, 1, pl.ds(h * half, half)], from_y.at[k, pl.ds(h * half, half)], y_s.at[0, k, h], y_s.at[1, k, h], me.y_mate) for h in range(2)] for k in range(4)]

    def arrive(k, fx, fy):
        loads[k, fx, fy].wait()
        cores[k, fx, fy].wait_recv()

    def early(k):
        arrive(k, 1, 1)
        add_rows(own.at[k, 1, 1], [(core.at[k, 1, 1], 0)], low)
        da[k].start()
        add_rows(own.at[k, 1, 1], [(core.at[k, 1, 1], 0)], high)
        db[k].start()
        arrive(k, 1, 0)
        add_rows(own.at[k, 1, 0], [(core.at[k, 1, 0], 0)], high)
        xs[k][1].start()
        arrive(k, 0, 1)
        add_rows(own.at[k, 0, 1], [(core.at[k, 0, 1], 0)], low)
        ys[k][0].start()

    def late(k):
        da[k].wait_recv()
        add_rows(own.at[k, 1, 0], [(core.at[k, 1, 0], 0), (diag_a.at[k], 0)], low)
        xs[k][0].start()
        db[k].wait_recv()
        add_rows(own.at[k, 0, 1], [(core.at[k, 0, 1], 0), (diag_b.at[k], half)], high)
        ys[k][1].start()

    whole = (0, rows)

    def column(k):
        arrive(k, 0, 0)
        for h in range(2):
            xs[k][h].wait_recv()
            ys[k][h].wait_recv()
        mine = own.at[k, 0, 0]
        rest = [(core.at[k, 0, 0], 0), (from_x.at[k], 0), (from_y.at[k], 0)]
        if k < GRID_Z - 1:
            to = me.farthest(k)
            add_rows(mine, rest, whole)
            for side, ahead, mate, more in (
                (0, to > me.z, me.above, me.has_below),
                (1, to < me.z, me.below, me.has_above),
            ):
                copy = remote(
                    mine, from_z.at[side, to], z_s.at[0, side, to], z_s.at[1, side, to], mate
                )

                @pl.when(ahead)
                def _():
                    @pl.when(more)
                    def _():
                        copy.wait_recv()
                        add_rows(mine, [(from_z.at[side, to], 0)], whole)

                    copy.start()
        else:
            add_rows(mine, rest, whole)
            for side, more in ((0, me.has_below), (1, me.has_above)):
                copy = remote(
                    mine, from_z.at[side, me.z], z_s.at[0, side, me.z], z_s.at[1, side, me.z],
                    me.y_mate,
                )

                @pl.when(more)
                def _():
                    copy.wait_recv()
                    add_rows(mine, [(from_z.at[side, me.z], 0)], whole)

    early(0)
    early(1)
    late(0)
    early(2)
    late(1)
    column(0)
    early(3)
    late(2)
    column(1)
    late(3)
    column(2)
    column(3)
    copy = pltpu.make_async_copy(own.at[3, 0, 0], out, out_s)
    copy.start()
    for k in range(GRID_Z):
        da[k].wait_send()
        db[k].wait_send()
        for h in range(2):
            xs[k][h].wait_send()
            ys[k][h].wait_send()
        if k < GRID_Z - 1:
            to = me.farthest(k)
            for side, ahead, mate in ((0, to > me.z, me.above), (1, to < me.z, me.below)):
                @pl.when(ahead)
                def _():
                    remote(
                        own.at[k, 0, 0], from_z.at[side, to],
                        z_s.at[0, side, to], z_s.at[1, side, to], mate,
                    ).wait_send()
    for sent in sends:
        sent.wait_send()
    copy.wait()


def scatter_all(value, collective_id):
    devices = lax.axis_size("dp") * lax.axis_size("tensor")
    rows, width = value.shape[0] // devices, value.shape[1]
    half = rows // 2
    dma = pltpu.SemaphoreType.DMA
    low = value.dtype
    return pl.pallas_call(
        scatter_kernel,
        out_shape=jax.ShapeDtypeStruct((rows, width), low),
        in_specs=[pl.BlockSpec(memory_space=pl.ANY)],
        out_specs=pl.BlockSpec(memory_space=pl.ANY),
        scratch_shapes=[
            pltpu.VMEM((4, 2, 2, rows, width), low),
            pltpu.VMEM((4, 2, 2, rows, width), low),
            pltpu.VMEM((4, half, width), low),
            pltpu.VMEM((4, half, width), low),
            pltpu.VMEM((4, rows, width), low),
            pltpu.VMEM((4, rows, width), low),
            pltpu.VMEM((2, 4, rows, width), low),
            pltpu.VMEM((8, 128), low),
            dma((4, 2, 2)),
            dma((2, 4, 2, 2)),
            dma((4, 4)),
            dma((2, 4, 2)),
            dma((2, 4, 2)),
            dma((2, 2, 4)),
            dma(()),
        ],
        compiler_params=pltpu.CompilerParams(
            collective_id=collective_id, has_side_effects=True, vmem_limit_bytes=VMEM_LIMIT
        ),
    )(value.reshape(devices, rows, width))


def gather_kernel(src, out, own_s, z_s, x_s, y_s, dx_s, dy_s, core_s):
    me = Place()
    rows = src.shape[0]
    half = rows // 2
    low, high = pl.ds(0, half), pl.ds(half, half)

    def near(k):
        return me.farthest(GRID_Z - 1 - k)

    def at(k, fx, fy, fc):
        return out.at[me.dp_at(near(k), fx, fc) * 2 + me.y_at(fy)]

    mine = pltpu.make_async_copy(src, at(0, 0, 0, 0), own_s)
    mine.start()
    me.greet()

    def over(source, k, fx, fy, send, recv, mate):
        return remote(source, at(k, fx, fy, 0), send, recv, mate)

    def z_copy(k, source, side, mate):
        zn = near(k)
        return remote(source, at(k, 0, 0, 0), z_s.at[0, side, zn], z_s.at[1, side, zn], mate)

    xs, ys, dxs, dys, cores = {}, {}, {}, {}, {}
    for k in range(GRID_Z):
        source = src if k == 0 else at(k, 0, 0, 0)
        xs[k] = over(source, k, 0, 0, x_s.at[0, k], x_s.at[1, k], me.x_mate)
        ys[k] = over(source, k, 0, 0, y_s.at[0, k], y_s.at[1, k], me.y_mate)
        dys[k] = remote(at(k, 1, 0, 0).at[low], at(k, 1, 0, 0).at[low], dy_s.at[0, k], dy_s.at[1, k], me.y_mate)
        dxs[k] = remote(at(k, 0, 1, 0).at[high], at(k, 0, 1, 0).at[high], dx_s.at[0, k], dx_s.at[1, k], me.x_mate)
        for fx in range(2):
            for fy in range(2):
                block = source if (fx, fy) == (0, 0) else at(k, fx, fy, 0)
                if (fx, fy) == (1, 1):
                    for h, part in enumerate((low, high)):
                        cores[k, fx, fy, h] = remote(
                            block.at[part], block.at[part],
                            core_s.at[0, k, 3 + h], core_s.at[1, k, 3 + h], me.sibling,
                        )
                else:
                    cores[k, fx, fy] = remote(
                        block, at(k, fx, fy, 0), core_s.at[0, k, fx * 2 + fy],
                        core_s.at[1, k, fx * 2 + fy], me.sibling,
                    )

    def own(k):
        if k == 0:
            for side, more, mate in ((0, me.has_above, me.above), (1, me.has_below, me.below)):
                copy = z_copy(0, src, side, mate)

                @pl.when(more)
                def _():
                    copy.start()
        else:
            zn = near(k)
            for side, came, more, mate in (
                (0, zn < me.z, me.has_above, me.above),
                (1, zn > me.z, me.has_below, me.below),
            ):
                copy = z_copy(k, at(k, 0, 0, 0), side, mate)

                @pl.when(came)
                def _():
                    copy.wait_recv()

                    @pl.when(more)
                    def _():
                        copy.start()

        xs[k].start()
        ys[k].start()
        cores[k, 0, 0].start()

    def diag(k):
        xs[k].wait_recv()
        dys[k].start()
        cores[k, 1, 0].start()
        ys[k].wait_recv()
        dxs[k].start()
        cores[k, 0, 1].start()

    def corner(k):
        dys[k].wait_recv()
        cores[k, 1, 1, 0].start()
        dxs[k].wait_recv()
        cores[k, 1, 1, 1].start()

    own(0)
    own(1)
    diag(0)
    own(2)
    diag(1)
    corner(0)
    own(3)
    diag(2)
    corner(1)
    diag(3)
    corner(2)
    corner(3)
    mine.wait()
    for k in range(GRID_Z):
        zn = near(k)
        for side, came, more, mate in (
            (0, zn <= me.z, me.has_above, me.above),
            (1, zn >= me.z, me.has_below, me.below),
        ):
            copy = z_copy(k, src if k == 0 else at(k, 0, 0, 0), side, mate)

            @pl.when(came)
            def _():
                @pl.when(more)
                def _():
                    copy.wait_send()
        for copy in (xs[k], ys[k], dxs[k], dys[k]):
            copy.wait_send()
    for copy in cores.values():
        copy.wait()


def gather_all(value, collective_id):
    devices = lax.axis_size("dp") * lax.axis_size("tensor")
    rows, width = value.shape
    dma = pltpu.SemaphoreType.DMA
    return pl.pallas_call(
        gather_kernel,
        out_shape=jax.ShapeDtypeStruct((devices, rows, width), value.dtype),
        in_specs=[pl.BlockSpec(memory_space=pl.ANY)],
        out_specs=pl.BlockSpec(memory_space=pl.ANY),
        scratch_shapes=[
            dma(()),
            dma((2, 2, 4)),
            dma((2, 4)),
            dma((2, 4)),
            dma((2, 4)),
            dma((2, 4)),
            dma((2, 4, 5)),
        ],
        compiler_params=pltpu.CompilerParams(collective_id=collective_id, has_side_effects=True),
    )(value).reshape(devices * rows, width)


def plane_gather_kernel(src, out, own_s, z_s, x_s, core_s):
    me = Place()

    def near(k):
        return me.farthest(GRID_Z - 1 - k)

    def at(k, fx):
        return out.at[me.dp_at(near(k), fx, 0)]

    mine = pltpu.make_async_copy(src, at(0, 0), own_s)
    mine.start()
    me.greet()

    def z_copy(k, side, mate):
        zn = near(k)
        return remote(
            src if k == 0 else at(k, 0), at(k, 0), z_s.at[0, side, zn], z_s.at[1, side, zn], mate
        )

    xs, cores = {}, {}
    for k in range(GRID_Z):
        source = src if k == 0 else at(k, 0)
        xs[k] = remote(source, at(k, 0), x_s.at[0, k], x_s.at[1, k], me.x_mate)
        cores[k, 0] = remote(source, at(k, 0), core_s.at[0, k, 0], core_s.at[1, k, 0], me.sibling)
        cores[k, 1] = remote(at(k, 1), at(k, 1), core_s.at[0, k, 1], core_s.at[1, k, 1], me.sibling)

    def own(k):
        zn = near(k)
        for side, came, more, mate in (
            (0, zn < me.z, me.has_above, me.above),
            (1, zn > me.z, me.has_below, me.below),
        ):
            copy = z_copy(k, side, mate)
            if k == 0:

                @pl.when(more)
                def _():
                    copy.start()
            else:

                @pl.when(came)
                def _():
                    copy.wait_recv()

                    @pl.when(more)
                    def _():
                        copy.start()

        xs[k].start()
        cores[k, 0].start()

    def diag(k):
        xs[k].wait_recv()
        cores[k, 1].start()

    own(0)
    own(1)
    diag(0)
    own(2)
    diag(1)
    own(3)
    diag(2)
    diag(3)
    mine.wait()
    for k in range(GRID_Z):
        zn = near(k)
        for side, came, more, mate in (
            (0, zn <= me.z, me.has_above, me.above),
            (1, zn >= me.z, me.has_below, me.below),
        ):
            copy = z_copy(k, side, mate)

            @pl.when(came)
            def _():
                @pl.when(more)
                def _():
                    copy.wait_send()

        xs[k].wait_send()
    for copy in cores.values():
        copy.wait()


def gather_dp(value, collective_id):
    devices = lax.axis_size("dp")
    rows, width = value.shape
    dma = pltpu.SemaphoreType.DMA
    return pl.pallas_call(
        plane_gather_kernel,
        out_shape=jax.ShapeDtypeStruct((devices, rows, width), value.dtype),
        in_specs=[pl.BlockSpec(memory_space=pl.ANY)],
        out_specs=pl.BlockSpec(memory_space=pl.ANY),
        scratch_shapes=[dma(()), dma((2, 2, 4)), dma((2, 4)), dma((2, 4, 2))],
        compiler_params=pltpu.CompilerParams(collective_id=collective_id, has_side_effects=True),
    )(value).reshape(devices * rows, width)


def plane_scatter_kernel(
    part, out, own, core, from_x, from_z, load_s, core_s, x_s, z_s, out_s
):
    me = Place()
    rows = own.shape[2]
    whole = (0, rows)
    loads, cores = {}, {}

    def chunk(k, flip_x, flip_core):
        return part.at[me.dp_at(me.farthest(k), flip_x, flip_core)]

    for k in range(GRID_Z):
        for fx in (1, 0):
            loads[k, fx] = pltpu.make_async_copy(chunk(k, fx, 0), own.at[k, fx], load_s.at[k, fx])
            loads[k, fx].start()
    me.greet()
    for k in range(GRID_Z):
        for fx in (1, 0):
            cores[k, fx] = remote(
                chunk(k, fx, 1), core.at[k, fx],
                core_s.at[0, k, fx], core_s.at[1, k, fx], me.sibling,
            )
            cores[k, fx].start()
    half = rows // 2
    xs = [
        [
            remote(
                own.at[k, 1, pl.ds(h * half, half)], from_x.at[k, pl.ds(h * half, half)],
                x_s.at[0, k, h], x_s.at[1, k, h], me.x_mate,
            )
            for h in range(2)
        ]
        for k in range(GRID_Z)
    ]

    def z_copy(k, side, mate):
        to = me.farthest(k)
        return remote(
            own.at[k, 0], from_z.at[side, to], z_s.at[0, side, to], z_s.at[1, side, to], mate
        )

    def across(k):
        loads[k, 1].wait()
        cores[k, 1].wait_recv()
        for h in range(2):
            add_rows(own.at[k, 1], [(core.at[k, 1], 0)], (h * half, half))
            xs[k][h].start()

    def column(k):
        loads[k, 0].wait()
        cores[k, 0].wait_recv()
        for h in range(2):
            xs[k][h].wait_recv()
        mine = own.at[k, 0]
        add_rows(mine, [(core.at[k, 0], 0), (from_x.at[k], 0)], whole)
        to = me.farthest(k)
        for side, ahead, mate, more in (
            (0, to > me.z, me.above, me.has_below),
            (1, to < me.z, me.below, me.has_above),
        ):
            copy = z_copy(k, side, mate)
            if k < GRID_Z - 1:

                @pl.when(ahead)
                def _():
                    @pl.when(more)
                    def _():
                        copy.wait_recv()
                        add_rows(mine, [(from_z.at[side, to], 0)], whole)

                    copy.start()
            else:

                @pl.when(more)
                def _():
                    copy.wait_recv()
                    add_rows(mine, [(from_z.at[side, to], 0)], whole)

    for k in range(GRID_Z):
        across(k)
        if k:
            column(k - 1)
    column(GRID_Z - 1)
    copy = pltpu.make_async_copy(own.at[3, 0], out, out_s)
    copy.start()
    for k in range(GRID_Z):
        for h in range(2):
            xs[k][h].wait_send()
        if k < GRID_Z - 1:
            to = me.farthest(k)
            for side, ahead, mate in ((0, to > me.z, me.above), (1, to < me.z, me.below)):

                @pl.when(ahead)
                def _():
                    z_copy(k, side, mate).wait_send()
    for sent in cores.values():
        sent.wait_send()
    copy.wait()


def scatter_dp(value, collective_id):
    devices = lax.axis_size("dp")
    rows, width = value.shape[0] // devices, value.shape[1]
    dma = pltpu.SemaphoreType.DMA
    low = value.dtype
    return pl.pallas_call(
        plane_scatter_kernel,
        out_shape=jax.ShapeDtypeStruct((rows, width), low),
        in_specs=[pl.BlockSpec(memory_space=pl.ANY)],
        out_specs=pl.BlockSpec(memory_space=pl.ANY),
        scratch_shapes=[
            pltpu.VMEM((4, 2, rows, width), low),
            pltpu.VMEM((4, 2, rows, width), low),
            pltpu.VMEM((4, rows, width), low),
            pltpu.VMEM((2, 4, rows, width), low),
            dma((4, 2)),
            dma((2, 4, 2)),
            dma((2, 4, 2)),
            dma((2, 2, 4)),
            dma(()),
        ],
        compiler_params=pltpu.CompilerParams(
            collective_id=collective_id, has_side_effects=True, vmem_limit_bytes=VMEM_LIMIT
        ),
    )(value.reshape(devices, rows, width))


WINDOW_ALIGN = 16
EXPERT_VMEM = 60 * 1024 * 1024


def dot(left, right, dims=((1,), (0,))):
    return lax.dot_general(left, right, (dims, ((), ())), preferred_element_type=jnp.float32)


def expert_kernel(
    info, pos, rows_in, cots_in, gate_w, up_w, down_w,
    out, back, gate_g, up_g, down_g,
    x, dy, wgu, wd, slot_out, slot_row, gu, hg, rows_b, cots_b, g_stage, d_stage,
    load_s, w_s, out_s, g_s, d_s,
):
    bf16, f32 = jnp.bfloat16, jnp.float32
    blocks, block_rows, wide = rows_in.shape
    features = cots_in.shape[2]
    experts, padded = x.shape[0], x.shape[1]
    part = hg.shape[2]
    cap = hg.shape[1]
    window = padded - cap
    tile = 256
    chunk = 512

    def load(b):
        slot = b % 2
        return (
            pltpu.make_async_copy(rows_in.at[b], rows_b.at[slot], load_s.at[slot, 0]),
            pltpu.make_async_copy(cots_in.at[b], cots_b.at[slot], load_s.at[slot, 1]),
        )

    for copy in load(0):
        copy.start()
    weights = []
    for e in range(experts):
        weights.append(pltpu.make_async_copy(gate_w.at[e], wgu.at[e, :, pl.ds(0, part)], w_s.at[e, 0]))
        weights.append(pltpu.make_async_copy(up_w.at[e], wgu.at[e, :, pl.ds(part, part)], w_s.at[e, 1]))
        weights.append(pltpu.make_async_copy(down_w.at[e], wd.at[e], w_s.at[e, 2]))
    for copy in weights:
        copy.start()

    def clear(i, carry):
        at = pl.ds(pl.multiple_of(i * 16, 16), 16)
        for e in range(experts):
            x[e, at, :] = jnp.zeros((16, wide), bf16)
            dy[e, at, :] = jnp.zeros((16, features), bf16)
        return carry

    lax.fori_loop(0, padded // 16, clear, 0)
    for e in range(experts):
        slot_out[e, pl.ds(cap, window), :] = jnp.zeros((window, features), bf16)
        slot_row[e, pl.ds(cap, window), :] = jnp.zeros((window, wide), bf16)

    def starts(b):
        return [pl.multiple_of(info[1 + b * experts + e], WINDOW_ALIGN) for e in range(experts)]

    def picks(b, begin):
        slots = lax.broadcasted_iota(jnp.int32, (window, block_rows), 0)
        return jnp.concatenate(
            [(slots + begin[e] == pos[b, pl.ds(e, 1), :]).astype(f32) for e in range(experts)],
            axis=0,
        )

    def take(b, carry):
        slot = b % 2

        @pl.when(b + 1 < blocks)
        def _():
            for copy in load(b + 1):
                copy.start()

        begin = starts(b)
        picked = picks(b, begin).astype(bf16)
        for copy in load(b):
            copy.wait()
        for source, target, width in ((rows_b, x, wide), (cots_b, dy, features)):
            for first in range(0, width, chunk):
                cols = pl.ds(first, min(chunk, width - first))
                got = dot(picked, source[slot, :, cols]).astype(bf16)
                for e in range(experts):
                    at = pl.ds(begin[e], window)
                    target[e, at, cols] += got[e * window : (e + 1) * window]
        return carry

    lax.fori_loop(0, blocks, take, 0)
    for copy in weights:
        copy.wait()

    lanes = lax.broadcasted_iota(jnp.int32, (tile, AUX), 1)

    def mlp(step, carry):
        e = step // (cap // tile)
        at = pl.ds(pl.multiple_of((step % (cap // tile)) * tile, tile), tile)
        own = info[0] * experts + e
        total = blocks * experts
        aux = x[e, at, pl.ds(features, AUX)].astype(f32)
        gate = jnp.sum(
            jnp.where((lanes == own) | (lanes == own + total), aux, 0.0), axis=1, keepdims=True
        )
        pre = dot(x[e, at, pl.ds(0, features)], wgu[e])
        gate_pre, up_pre = pre[:, :part], pre[:, part:]
        sig = 1.0 / (1.0 + jnp.exp(-gate_pre))
        act = gate_pre * sig
        hidden = (act * up_pre).astype(bf16).astype(f32)
        gated = (hidden * gate).astype(bf16)
        hg[e, at, :] = gated
        down_cot = dot(dy[e, at, :], wd[e], ((1,), (1,)))
        slot_cot = jnp.sum(hidden * down_cot, axis=1, keepdims=True)
        hidden_cot = down_cot * gate
        gu[e, at, pl.ds(0, part)] = (
            hidden_cot * up_pre * sig * (1.0 + gate_pre * (1.0 - sig))
        ).astype(bf16)
        gu[e, at, pl.ds(part, part)] = (hidden_cot * act).astype(bf16)
        for first in range(0, features, chunk):
            cols = pl.ds(first, chunk)
            slot_out[e, at, cols] = dot(gated, wd[e, :, cols]).astype(bf16)
            slot_row[e, at, cols] = dot(
                gu[e, at, :], wgu[e, pl.ds(first, chunk), :], ((1,), (1,))
            ).astype(bf16)
        high = slot_cot.astype(bf16).astype(f32)
        place = info[1 + blocks * experts] * 2 * total + own * 2
        slot_row[e, at, pl.ds(features, AUX)] = jnp.where(
            lanes == place, high, jnp.where(lanes == place + 1, slot_cot - high, 0.0)
        ).astype(bf16)
        return carry

    lax.fori_loop(0, experts * (cap // tile), mlp, 0)

    def stored(b):
        slot = b % 2
        return (
            pltpu.make_async_copy(cots_b.at[slot], out.at[b], out_s.at[slot, 0]),
            pltpu.make_async_copy(rows_b.at[slot], back.at[b], out_s.at[slot, 1]),
        )

    def put(b, carry):
        slot = b % 2

        @pl.when(b >= 2)
        def _():
            for copy in stored(b - 2):
                copy.wait()

        begin = starts(b)
        spread = picks(b, begin).T.astype(bf16)
        for source, target, width in ((slot_out, cots_b, features), (slot_row, rows_b, wide)):
            for first in range(0, width, chunk):
                cols = pl.ds(first, min(chunk, width - first))
                held = jnp.concatenate(
                    [source[e, pl.ds(begin[e], window), cols] for e in range(experts)], axis=0
                )
                target[slot, :, cols] = dot(spread, held).astype(bf16)
        for copy in stored(b):
            copy.start()
        return carry

    lax.fori_loop(0, blocks, put, 0)

    tiles = features // tile

    def g_copies(step):
        slot = step % 2
        e, at = step // tiles, pl.ds(pl.multiple_of((step % tiles) * tile, tile), tile)
        return (
            pltpu.make_async_copy(g_stage.at[slot, :, pl.ds(0, part)], gate_g.at[e, at], g_s.at[slot, 0]),
            pltpu.make_async_copy(g_stage.at[slot, :, pl.ds(part, part)], up_g.at[e, at], g_s.at[slot, 1]),
        )

    def wide_grad(step, carry):
        slot = step % 2
        e, at = step // tiles, pl.ds(pl.multiple_of((step % tiles) * tile, tile), tile)

        @pl.when(step >= 2)
        def _():
            for copy in g_copies(step - 2):
                copy.wait()

        g_stage[slot] = dot(x[e, pl.ds(0, cap), at], gu[e], ((0,), (0,)))
        for copy in g_copies(step):
            copy.start()
        return carry

    lax.fori_loop(0, experts * tiles, wide_grad, 0)
    parts = features // chunk

    def d_copy(step):
        slot = step % 2
        e, at = step // parts, pl.ds(pl.multiple_of((step % parts) * chunk, chunk), chunk)
        return pltpu.make_async_copy(d_stage.at[slot], down_g.at[e, :, at], d_s.at[slot])

    def down_grad(step, carry):
        slot = step % 2
        e, at = step // parts, pl.ds(pl.multiple_of((step % parts) * chunk, chunk), chunk)

        @pl.when(step >= 2)
        def _():
            d_copy(step - 2).wait()

        d_stage[slot] = dot(hg[e], dy[e, pl.ds(0, cap), at], ((0,), (0,)))
        d_copy(step).start()
        return carry

    lax.fori_loop(0, experts * parts, down_grad, 0)
    for last in (2, 1):
        for copy in stored(blocks - last):
            copy.wait()
        for copy in g_copies(experts * tiles - last):
            copy.wait()
        d_copy(experts * parts - last).wait()


def expert_layer(info, pos, rows_in, cots_in, gate_w, up_w, down_w, capacity, most):
    bf16, f32 = jnp.bfloat16, jnp.float32
    blocks, block_rows, wide = rows_in.shape
    features = cots_in.shape[2]
    experts, part = gate_w.shape[0], gate_w.shape[2]
    padded = capacity + -(-most // WINDOW_ALIGN) * WINDOW_ALIGN + WINDOW_ALIGN
    dma = pltpu.SemaphoreType.DMA
    shape = jax.ShapeDtypeStruct
    anywhere = pl.BlockSpec(memory_space=pl.ANY)
    return pl.pallas_call(
        expert_kernel,
        out_shape=(
            shape((blocks, block_rows, features), bf16),
            shape((blocks, block_rows, wide), bf16),
            shape(gate_w.shape, f32),
            shape(up_w.shape, f32),
            shape(down_w.shape, f32),
        ),
        in_specs=[
            pl.BlockSpec(memory_space=pltpu.SMEM),
            pl.BlockSpec(memory_space=pltpu.VMEM),
        ]
        + [anywhere] * 5,
        out_specs=(anywhere,) * 5,
        scratch_shapes=[
            pltpu.VMEM((experts, padded, wide), bf16),
            pltpu.VMEM((experts, padded, features), bf16),
            pltpu.VMEM((experts, features, 2 * part), bf16),
            pltpu.VMEM((experts, part, features), bf16),
            pltpu.VMEM((experts, padded, features), bf16),
            pltpu.VMEM((experts, padded, wide), bf16),
            pltpu.VMEM((experts, capacity, 2 * part), bf16),
            pltpu.VMEM((experts, capacity, part), bf16),
            pltpu.VMEM((2, block_rows, wide), bf16),
            pltpu.VMEM((2, block_rows, features), bf16),
            pltpu.VMEM((2, 256, 2 * part), f32),
            pltpu.VMEM((2, part, 512), f32),
            dma((2, 2)),
            dma((experts, 3)),
            dma((2, 2)),
            dma((2, 2)),
            dma((2,)),
        ],
        compiler_params=pltpu.CompilerParams(vmem_limit_bytes=EXPERT_VMEM),
    )(info, pos, rows_in, cots_in, gate_w, up_w, down_w)


def split_high_low(value):
    high = value.astype(jnp.bfloat16)
    return high, (value - high.astype(jnp.float32)).astype(jnp.bfloat16)


def gathered_body(
    layer_input,
    query_weight,
    key_projection,
    value_projection,
    context_weight,
    router_weight,
    expert_gate,
    expert_up,
    expert_down,
    prenorm_gain,
    midnorm_gain,
    querynorm_gain,
    keynorm_gain,
    routes,
    lengths,
    sequence_order,
    output_cotangent,
):
    bf16, f32 = jnp.bfloat16, jnp.float32
    tensor_count = lax.axis_size("tensor")
    tensor_index = lax.axis_index("tensor")
    dp_count = lax.axis_size("dp")
    dp_index = lax.axis_index("dp")
    own_rows, features = layer_input.shape
    block_rows = own_rows * tensor_count
    tokens = block_rows * dp_count
    expert_count = EXP_DEV * dp_count
    capacity = 3 * block_rows * TOP // (4 * EXP_DEV)
    most_rows = (5 * block_rows * TOP + 4 * expert_count - 1) // (4 * expert_count)
    shard = features // dp_count
    query_width = query_weight.shape[1]
    key_width = key_projection.shape[1]
    norm_part = HEAD_SIZE // dp_count

    gains = jnp.zeros((shard, AUX - expert_count), bf16)
    gains = gains.at[:, 0].set(prenorm_gain).at[:, 1].set(midnorm_gain)
    gains = gains.at[:norm_part, 2].set(querynorm_gain).at[:norm_part, 3].set(keynorm_gain)
    packed = jnp.concatenate(
        [query_weight, key_projection, value_projection, context_weight.T, router_weight, gains],
        axis=1,
    )
    packed = gather_dp(packed, 0)
    edges = [0]
    for width in (query_width, key_width, key_width, query_width, expert_count, AUX - expert_count):
        edges.append(edges[-1] + width)
    qkv_all = packed[:, : edges[3]]
    context_all = packed[:, edges[3] : edges[4]]
    router_all = packed[:, edges[4] : edges[5]]
    gains_all = packed[:, edges[5] :].astype(f32)
    gain_one, gain_two = gains_all[:, 0], gains_all[:, 1]
    head_gains = gains_all.reshape(dp_count, shard, -1)[:, :norm_part, :]
    query_factor = head_gains[:, :, 2].reshape(-1)
    key_factor = head_gains[:, :, 3].reshape(-1)

    cot_all = lax.all_gather(output_cotangent, ("dp", "tensor"), axis=0, tiled=True)
    routes_all = lax.all_gather(routes.T, "dp")
    input_rows = lax.all_gather(layer_input, "tensor", axis=0, tiled=True)
    position = jnp.arange(block_rows, dtype=jnp.int32)
    block_lengths = lengths[sequence_order]
    seq_length = block_lengths[dp_index]

    frequency = jnp.exp(
        -math.log(rope_base) * jnp.arange(HEAD_SIZE // 2, dtype=f32) * (2.0 / HEAD_SIZE)
    )
    angles = position.astype(f32)[:, None] * frequency[None, :]
    cosine_table = jnp.cos(angles)[:, None, :]
    sine_values = jnp.sin(angles)[:, None, :]
    heads_query = query_width // HEAD_SIZE
    heads_key = key_width // HEAD_SIZE
    group_width = heads_query // heads_key
    stream = input_rows.astype(f32)
    unit_first, scale_first = rms_normalize(stream)
    first_normed = (unit_first * gain_one).astype(bf16)
    raw = matrix_product(first_normed, qkv_all)
    query_unnormed = raw[:, : edges[1]].reshape(block_rows, heads_query, HEAD_SIZE)
    key_unnormed = raw[:, edges[1] : edges[2]].reshape(block_rows, heads_key, HEAD_SIZE)
    value_rows = raw[:, edges[2] :].astype(bf16).reshape(block_rows, heads_key, HEAD_SIZE)
    query_unit, query_scale = rms_normalize(query_unnormed)
    key_unit, key_scale = rms_normalize(key_unnormed)
    query_rows = (
        rotary_apply(query_unit * query_factor, cosine_table, sine_values)
        .astype(bf16)
        .reshape(block_rows, heads_key, group_width, HEAD_SIZE)
    )
    keys_rot = rotary_apply(key_unit * key_factor, cosine_table, sine_values).astype(bf16)
    score_scale = HEAD_SIZE ** (-0.5)
    allowed = (position[None, :] <= position[:, None]) & (position < seq_length)[None, :]
    scores = (
        jnp.einsum("ikrd,jkd->krij", query_rows, keys_rot, preferred_element_type=f32)
        * score_scale
    )
    scores = jnp.where(allowed, scores, masked_score)
    weights = jnp.exp(scores - jnp.max(scores, axis=-1, keepdims=True))
    soft_probs = weights / jnp.sum(weights, axis=-1, keepdims=True)
    probs_low = soft_probs.astype(bf16)
    context = jnp.einsum("krij,jkd->ikrd", probs_low, value_rows, preferred_element_type=f32)
    context = context.reshape(block_rows, query_width).astype(bf16)
    attention = lax.psum_scatter(
        transposed(context, context_all).astype(bf16),
        "tensor",
        scatter_dimension=0,
        tiled=True,
    )
    residual = layer_input.astype(f32) + attention.astype(f32)
    unit_second, scale_second = rms_normalize(residual)
    normed_second = (unit_second * gain_two).astype(bf16)

    row_start = tensor_index * own_rows
    routes_own = lax.dynamic_slice_in_dim(routes, row_start, own_rows, 0)
    expert_ids = jnp.arange(expert_count, dtype=jnp.int32)
    chosen = jnp.any(routes_own[:, :, None] == expert_ids[None, None, :], axis=1)
    logits = jnp.where(chosen, matrix_product(normed_second, router_all), masked_score)
    spread = jnp.exp(logits - jnp.max(logits, axis=-1, keepdims=True))
    gates = spread / jnp.sum(spread, axis=-1, keepdims=True)
    high, low = split_high_low(gates)
    sent = jnp.concatenate(
        [normed_second, high, low, jnp.zeros((own_rows, AUX - 2 * expert_count), bf16)], axis=1
    )
    normed_all = gather_all(sent, 1).reshape(dp_count, block_rows, features + AUX)

    expert_own = dp_index * EXP_DEV + jnp.arange(EXP_DEV, dtype=jnp.int32)
    live = position[None, :] < block_lengths[:, None]
    hot = jnp.any(routes_all[:, None, :, :] == expert_own[None, :, None, None], axis=2)
    hot = hot & live[:, None, :]
    before = (position[:, None] < position[None, :]).astype(bf16)
    rank = jnp.einsum("bes,st->bet", hot.astype(bf16), before, preferred_element_type=f32)
    rank = rank.astype(jnp.int32)
    counts = rank[:, :, -1] + hot[:, :, -1]
    earlier = jnp.cumsum(counts, axis=0) - counts
    slot = earlier[:, :, None] + rank
    slot = jnp.where(hot & (slot < capacity), slot, -capacity)
    begin = jnp.minimum(earlier, capacity) // WINDOW_ALIGN * WINDOW_ALIGN
    info = jnp.concatenate([dp_index[None], begin.reshape(-1), tensor_index[None]])
    out_part, back_part, gate_gradient, up_gradient, down_gradient = expert_layer(
        info.astype(jnp.int32),
        slot,
        normed_all,
        cot_all.reshape(dp_count, block_rows, features),
        expert_gate,
        expert_up,
        expert_down,
        capacity,
        most_rows,
    )
    returned = scatter_all(back_part.reshape(tokens, features + AUX), 3).astype(f32)
    expert_sum = scatter_all(out_part.reshape(tokens, features), 2)
    layer_output = (residual + expert_sum.astype(f32)).astype(bf16)

    gate_cot = jnp.sum(
        returned[:, features:].reshape(own_rows, tensor_count, expert_count, 2), axis=(1, 3)
    )
    logit_cot = (
        gates * (gate_cot - jnp.sum(gates * gate_cot, axis=-1, keepdims=True))
    ).astype(bf16)
    router_part = contract(normed_second, logit_cot)
    normed_cot = returned[:, :features] + transposed(logit_cot, router_all)
    midnorm_part = jnp.sum(normed_cot * unit_second, axis=0)
    residual_cot = output_cotangent.astype(f32) + norm_back(
        normed_cot * gain_two, unit_second, scale_second
    )
    attention_cot = lax.all_gather(residual_cot.astype(bf16), "tensor", axis=0, tiled=True)

    context_part = contract(attention_cot, context)
    context_cot = (
        matrix_product(attention_cot, context_all)
        .astype(bf16)
        .reshape(block_rows, heads_key, group_width, HEAD_SIZE)
    )
    prob_cot = jnp.einsum("ikrd,jkd->krij", context_cot, value_rows, preferred_element_type=f32)
    score_cot = (
        soft_probs * (prob_cot - jnp.sum(soft_probs * prob_cot, axis=-1, keepdims=True))
    ).astype(bf16)
    value_cot = jnp.einsum("krij,ikrd->jkd", probs_low, context_cot, preferred_element_type=f32)
    value_cot = value_cot.astype(bf16).reshape(block_rows, key_width)
    query_turned = (
        jnp.einsum("krij,jkd->ikrd", score_cot, keys_rot, preferred_element_type=f32).reshape(
            block_rows, heads_query, HEAD_SIZE
        )
        * score_scale
    )
    key_turned = (
        jnp.einsum("krij,ikrd->jkd", score_cot, query_rows, preferred_element_type=f32)
        * score_scale
    )
    query_back = rotary_apply(query_turned, cosine_table, -sine_values)
    key_back = rotary_apply(key_turned, cosine_table, -sine_values)
    querynorm_part = jnp.sum(query_back * query_unit, axis=(0, 1))
    keynorm_part = jnp.sum(key_back * key_unit, axis=(0, 1))
    query_raw_cot = norm_back(query_back * query_factor, query_unit, query_scale).astype(bf16)
    key_raw_cot = norm_back(key_back * key_factor, key_unit, key_scale).astype(bf16)
    raw_cot = jnp.concatenate(
        [
            query_raw_cot.reshape(block_rows, query_width),
            key_raw_cot.reshape(block_rows, key_width),
            value_cot,
        ],
        axis=1,
    )
    qkv_part = contract(first_normed, raw_cot)
    first_cot = lax.psum_scatter(
        transposed(raw_cot, qkv_all).astype(bf16), "tensor", scatter_dimension=0, tiled=True
    ).astype(f32)
    unit_own = lax.dynamic_slice_in_dim(unit_first, row_start, own_rows, 0)
    scale_own = lax.dynamic_slice_in_dim(scale_first, row_start, own_rows, 0)
    prenorm_part = jnp.sum(first_cot * unit_own, axis=0)
    input_gradient = (
        residual_cot + norm_back(first_cot * gain_one, unit_own, scale_own)
    ).astype(bf16)

    small = jnp.zeros((dp_count, shard, AUX), f32)
    small = small.at[:, :, :expert_count].set(router_part.reshape(dp_count, shard, expert_count))
    small = small.at[:, :, expert_count].set(prenorm_part.reshape(dp_count, shard))
    small = small.at[:, :, expert_count + 1].set(midnorm_part.reshape(dp_count, shard))
    small = small.at[:, :norm_part, expert_count + 2].set(querynorm_part.reshape(dp_count, -1))
    small = small.at[:, :norm_part, expert_count + 3].set(keynorm_part.reshape(dp_count, -1))
    small = lax.psum_scatter(small.reshape(features, AUX), "dp", scatter_dimension=0, tiled=True)
    small = lax.psum(small, "tensor")
    summed = scatter_dp(jnp.concatenate([qkv_part.astype(bf16), context_part.astype(bf16)], axis=1), 4)
    summed = summed.astype(f32)
    return (
        layer_output,
        input_gradient,
        summed[:, : edges[1]],
        summed[:, edges[1] : edges[2]],
        summed[:, edges[2] : edges[3]],
        summed[:, edges[3] :].T,
        small[:, :expert_count],
        gate_gradient,
        up_gradient,
        down_gradient,
        small[:, expert_count],
        small[:, expert_count + 1],
        small[:norm_part, expert_count + 2],
        small[:norm_part, expert_count + 3],
    )


def solution(mesh):
    return jax.shard_map(
        gathered_body if mesh.shape["dp"] <= 16 else body,
        mesh=mesh,
        in_specs=(
            P(("dp", "tensor"), None),
            P("dp", "tensor"),
            P("dp", "tensor"),
            P("dp", "tensor"),
            P("tensor", "dp"),
            P("dp", None),
            P("dp", None, "tensor"),
            P("dp", None, "tensor"),
            P("dp", "tensor", None),
            P("dp"),
            P("dp"),
            P("dp"),
            P("dp"),
            P("dp", None),
            P(),
            P(),
            P(("dp", "tensor"), None),
        ),
        out_specs=(
            P(("dp", "tensor"), None),
            P(("dp", "tensor"), None),
            P("dp", "tensor"),
            P("dp", "tensor"),
            P("dp", "tensor"),
            P("tensor", "dp"),
            P("dp", None),
            P("dp", None, "tensor"),
            P("dp", None, "tensor"),
            P("dp", "tensor", None),
            P("dp"),
            P("dp"),
            P("dp"),
            P("dp"),
        ),
        check_vma=False,
    )
```

```python
import functools
import math

import jax
import jax.numpy as jnp
import numpy as np
from jax import lax
from jax.experimental import pallas as pl
from jax.experimental.pallas import tpu as pltpu
from jax.sharding import PartitionSpec as P

HEAD_SIZE = 128
TOP = 8
EXP_DEV = 2


epsilon = 1e-06
rope_base = 1000000.0
masked_score = -1e30


def carried_in(value, axis, combine, identity):
    count, place = (lax.axis_size(axis), lax.axis_index(axis))
    everything = lax.all_gather(value, axis)
    start = jnp.broadcast_to(jnp.asarray(identity, value.dtype), value.shape)

    def hop(k, before):
        reached = k < place
        new = combine(before, everything[k])
        return jnp.where(reached, new, before)

    return lax.fori_loop(0, count, hop, start)


def rms_normalize(value_rows):
    scaling = lax.rsqrt(jnp.mean(value_rows * value_rows, axis=-1, keepdims=True) + epsilon)
    return (value_rows * scaling, scaling)


def norm_back(cotangent, unit_rows, scaling):
    return scaling * (
        cotangent - unit_rows * jnp.mean(cotangent * unit_rows, axis=-1, keepdims=True)
    )


def rotary_apply(value_rows, cosine_table, sine_values):
    middle = value_rows.shape[-1] // 2
    former = value_rows[..., :middle]
    latter = value_rows[..., middle:]
    return jnp.concatenate(
        [
            former * cosine_table - latter * sine_values,
            latter * cosine_table + former * sine_values,
        ],
        axis=-1,
    )


def matrix_product(former, latter):
    return jnp.dot(former, latter, preferred_element_type=jnp.float32)


def contract(former, latter):
    return lax.dot_general(
        former, latter, (((0,), (0,)), ((), ())), preferred_element_type=jnp.float32
    )


def transposed(former, latter):
    return lax.dot_general(
        former, latter, (((1,), (1,)), ((), ())), preferred_element_type=jnp.float32
    )


def to_owners(buffer):
    return lax.all_to_all(buffer, "dp", split_axis=1, concat_axis=1, tiled=True)


def owner_reduce(partial_rows):
    shares = lax.psum_scatter(
        partial_rows.astype(jnp.bfloat16), "tensor", scatter_dimension=2, tiled=True
    )
    return lax.all_gather(shares, "tensor", axis=2, tiled=True)


def body(
    layer_input,
    query_weight,
    key_projection,
    value_projection,
    context_weight,
    router_weight,
    expert_gate,
    expert_up,
    expert_down,
    prenorm_gain,
    midnorm_gain,
    querynorm_gain,
    keynorm_gain,
    routes,
    lengths,
    sequence_order,
    output_cotangent,
):
    tensor_count = lax.axis_size("tensor")
    tensor_index = lax.axis_index("tensor")
    dp_count = lax.axis_size("dp")
    own_rows = layer_input.shape[0]
    block_rows = own_rows * tensor_count
    features = layer_input.shape[1]
    expert_count = EXP_DEV * dp_count
    capacity = 3 * block_rows * TOP // (4 * EXP_DEV)
    most_rows = (5 * block_rows * TOP + 4 * expert_count - 1) // (4 * expert_count)
    slot_total = EXP_DEV * dp_count * most_rows
    (
        query_all,
        key_all,
        value_all,
        context_all,
        router_all,
        gain_first,
        gain_second,
        query_gain,
        gain_key,
    ) = (
        lax.all_gather(query_weight, "dp", axis=0, tiled=True),
        lax.all_gather(key_projection, "dp", axis=0, tiled=True),
        lax.all_gather(value_projection, "dp", axis=0, tiled=True),
        lax.all_gather(context_weight, "dp", axis=1, tiled=True),
        lax.all_gather(router_weight, "dp", axis=0, tiled=True),
        lax.all_gather(prenorm_gain, "dp", axis=0, tiled=True),
        lax.all_gather(midnorm_gain, "dp", axis=0, tiled=True),
        lax.all_gather(querynorm_gain, "dp", axis=0, tiled=True),
        lax.all_gather(keynorm_gain, "dp", axis=0, tiled=True),
    )
    input_rows, cot_rows = (
        lax.all_gather(layer_input, "tensor", axis=0, tiled=True),
        lax.all_gather(output_cotangent, "tensor", axis=0, tiled=True),
    )
    position = jnp.arange(block_rows, dtype=jnp.int32)
    seq_length = lengths[sequence_order[lax.axis_index("dp")]]
    token_live = position < seq_length
    frequency = jnp.exp(
        -math.log(rope_base) * jnp.arange(HEAD_SIZE // 2, dtype=jnp.float32) * (2.0 / HEAD_SIZE)
    )
    angles = position.astype(jnp.float32)[:, None] * frequency[None, :]
    cosine_table = jnp.cos(angles)[:, None, :]
    sine_values = jnp.sin(angles)[:, None, :]
    heads_query = query_all.shape[1] // HEAD_SIZE
    heads_key = key_all.shape[1] // HEAD_SIZE
    group_width = heads_query // heads_key
    gain_one = gain_first.astype(jnp.float32)
    gain_two = gain_second.astype(jnp.float32)
    query_factor = query_gain.astype(jnp.float32)
    key_factor = gain_key.astype(jnp.float32)
    stream = input_rows.astype(jnp.float32)
    unit_first, scale_first = rms_normalize(stream)
    first_layer_normed = (unit_first * gain_one).astype(jnp.bfloat16)
    query_unnormed = matrix_product(first_layer_normed, query_all).reshape(
        block_rows, heads_query, HEAD_SIZE
    )
    key_unnormed = matrix_product(first_layer_normed, key_all).reshape(
        block_rows, heads_key, HEAD_SIZE
    )
    value_rows = (
        matrix_product(first_layer_normed, value_all)
        .astype(jnp.bfloat16)
        .reshape(block_rows, heads_key, HEAD_SIZE)
    )
    query_unit, query_scale = rms_normalize(query_unnormed)
    key_unit, key_scale = rms_normalize(key_unnormed)
    query_rows = (
        rotary_apply(query_unit * query_factor, cosine_table, sine_values)
        .astype(jnp.bfloat16)
        .reshape(block_rows, heads_key, group_width, HEAD_SIZE)
    )
    keys_rot = rotary_apply(key_unit * key_factor, cosine_table, sine_values).astype(jnp.bfloat16)
    score_scale = HEAD_SIZE ** (-0.5)
    allowed = (position[None, :] <= position[:, None]) & token_live[None, :]

    def score_block():
        raw_scores = (
            jnp.einsum("ikrd,jkd->krij", query_rows, keys_rot, preferred_element_type=jnp.float32)
            * score_scale
        )
        return jnp.where(allowed, raw_scores, masked_score)

    scores = score_block()
    row_peak = jnp.max(scores, axis=-1, keepdims=True)
    log_total = row_peak + jnp.log(jnp.sum(jnp.exp(scores - row_peak), axis=-1, keepdims=True))
    soft_probs = jnp.exp(scores - log_total)
    context = jnp.einsum(
        "krij,jkd->ikrd",
        soft_probs.astype(jnp.bfloat16),
        value_rows,
        preferred_element_type=jnp.float32,
    )
    context = context.reshape(block_rows, heads_query * HEAD_SIZE).astype(jnp.bfloat16)
    attention = lax.psum(matrix_product(context, context_all), "tensor")
    residual = stream + attention
    unit_second, scale_second = rms_normalize(residual)
    normed_second = (unit_second * gain_two).astype(jnp.bfloat16)
    logits = matrix_product(normed_second, router_all)
    expert_ids = jnp.arange(expert_count, dtype=jnp.int32)
    route_hot = routes[:, :, None] == expert_ids[None, None, :]
    chosen = jnp.sum(jnp.where(route_hot, logits[:, None, :], 0.0), axis=-1)
    gate_weights = jax.nn.softmax(chosen, axis=-1)
    pair_expert = routes.reshape(-1)
    pair_live = jnp.repeat(token_live, TOP)
    pair_hot = ((pair_expert[:, None] == expert_ids[None, :]) & pair_live[:, None]).astype(
        jnp.int32
    )
    running = jnp.cumsum(pair_hot, axis=0)
    pair_rank = jnp.sum((running - pair_hot) * pair_hot, axis=1)
    counts = running[-1]
    earlier = carried_in(
        counts, "dp", lambda former, latter: former + latter, jnp.zeros_like(counts)
    )
    pair_slot = jnp.sum(earlier[None, :] * pair_hot, axis=1) + pair_rank
    pair_kept = pair_live & (pair_slot < capacity)
    local_expert = pair_expert % EXP_DEV
    owner_index = pair_expert // EXP_DEV
    buffer_index = (local_expert * dp_count + owner_index) * most_rows + pair_rank
    target = jnp.where(pair_kept, buffer_index, slot_total)
    pair_ids = jnp.arange(block_rows * TOP, dtype=jnp.int32)
    slot_pair = jnp.full((slot_total,), -1, dtype=jnp.int32).at[target].set(pair_ids, mode="drop")
    slot_used = slot_pair >= 0
    slot_safe = jnp.maximum(slot_pair, 0)
    slot_token = slot_safe // TOP
    bf_zero = jnp.zeros((), jnp.bfloat16)
    send_rows = jnp.where(slot_used[:, None], normed_second[slot_token], bf_zero)
    layout = (EXP_DEV, dp_count, most_rows, features)
    received = to_owners(send_rows.reshape(layout)).reshape(EXP_DEV, dp_count * most_rows, features)
    gate_pre = jnp.einsum("end,edf->enf", received, expert_gate, preferred_element_type=jnp.float32)
    up_pre = jnp.einsum("end,edf->enf", received, expert_up, preferred_element_type=jnp.float32)
    sigmoid_gate = jax.nn.sigmoid(gate_pre)
    gate_act = gate_pre * sigmoid_gate
    hidden = (gate_act * up_pre).astype(jnp.bfloat16)
    out_partial = jnp.einsum(
        "enf,efd->end", hidden, expert_down, preferred_element_type=jnp.float32
    )
    expert_out = owner_reduce(out_partial)
    width = expert_out.shape[2]
    returned = lax.all_to_all(
        expert_out.reshape(EXP_DEV, dp_count, most_rows, width),
        "dp",
        split_axis=1,
        concat_axis=1,
        tiled=True,
    ).reshape(slot_total, width)
    pair_place = jnp.where(pair_kept, buffer_index, 0)
    pair_out = jnp.where(pair_kept[:, None], returned[pair_place], bf_zero).reshape(
        block_rows, TOP, width
    )
    expert_part = jnp.sum(gate_weights[:, :, None] * pair_out, axis=1)
    cot_full = cot_rows.astype(jnp.float32)
    own_start = tensor_index * own_rows
    gate_part = jnp.sum(cot_full[:, None, :] * pair_out, axis=-1)
    expert_own = lax.dynamic_slice_in_dim(expert_part, own_start, own_rows, 0)
    residual_own = lax.dynamic_slice_in_dim(residual, own_start, own_rows, 0)
    layer_output = (residual_own + expert_own).astype(jnp.bfloat16)
    slot_gate = jnp.where(slot_used, gate_weights.reshape(-1)[slot_safe], 0.0)
    send_cot = (slot_gate[:, None] * cot_full[slot_token]).astype(jnp.bfloat16)
    expert_cot = to_owners(send_cot.reshape(layout)).reshape(
        EXP_DEV, dp_count * most_rows, features
    )
    hidden_cot = jnp.einsum(
        "end,efd->enf", expert_cot, expert_down, preferred_element_type=jnp.float32
    )
    gating_cot = (
        hidden_cot * up_pre * sigmoid_gate * (1.0 + gate_pre * (1.0 - sigmoid_gate))
    ).astype(jnp.bfloat16)
    upward_cot = (hidden_cot * gate_act).astype(jnp.bfloat16)
    down_gradient = jnp.einsum(
        "enf,end->efd", hidden, expert_cot, preferred_element_type=jnp.float32
    )
    gate_gradient = jnp.einsum(
        "end,enf->edf", received, gating_cot, preferred_element_type=jnp.float32
    )
    up_gradient = jnp.einsum(
        "end,enf->edf", received, upward_cot, preferred_element_type=jnp.float32
    )
    row_partial = jnp.einsum(
        "enf,edf->end", gating_cot, expert_gate, preferred_element_type=jnp.float32
    )
    row_partial = row_partial + jnp.einsum(
        "enf,edf->end", upward_cot, expert_up, preferred_element_type=jnp.float32
    )
    row_cot = owner_reduce(row_partial)
    row_back = lax.all_to_all(
        row_cot.reshape(EXP_DEV, dp_count, most_rows, width),
        "dp",
        split_axis=1,
        concat_axis=1,
        tiled=True,
    ).reshape(slot_total, width)
    pair_cot = jnp.where(pair_kept[:, None], row_back[pair_place], bf_zero).reshape(
        block_rows, TOP, width
    )
    normed_part = jnp.sum(pair_cot.astype(jnp.float32), axis=1)
    normed_cot = normed_part
    route_cot = gate_weights * (
        gate_part - jnp.sum(gate_weights * gate_part, axis=-1, keepdims=True)
    )
    logit_cot = jnp.sum(jnp.where(route_hot, route_cot[:, :, None], 0.0), axis=1).astype(
        jnp.bfloat16
    )
    router_gradient = contract(normed_second, logit_cot)
    normed_cot = normed_cot + transposed(logit_cot, router_all)
    midnorm_gradient = jnp.sum(normed_cot * unit_second, axis=0)
    residual_cot = cot_full + norm_back(normed_cot * gain_two, unit_second, scale_second)
    attention_cot = residual_cot.astype(jnp.bfloat16)
    context_gradient = contract(context, attention_cot)
    context_cot = (
        transposed(attention_cot, context_all)
        .astype(jnp.bfloat16)
        .reshape(block_rows, heads_key, group_width, HEAD_SIZE)
    )
    scores = score_block()
    soft_probs = jnp.exp(scores - log_total)
    prob_cot = jnp.einsum(
        "ikrd,jkd->krij", context_cot, value_rows, preferred_element_type=jnp.float32
    )
    score_cot = (
        soft_probs * (prob_cot - jnp.sum(soft_probs * prob_cot, axis=-1, keepdims=True))
    ).astype(jnp.bfloat16)
    value_cot = jnp.einsum(
        "krij,ikrd->jkd",
        soft_probs.astype(jnp.bfloat16),
        context_cot,
        preferred_element_type=jnp.float32,
    )
    value_cot = value_cot.astype(jnp.bfloat16).reshape(block_rows, heads_key * HEAD_SIZE)
    query_turned = (
        jnp.einsum(
            "krij,jkd->ikrd", score_cot, keys_rot, preferred_element_type=jnp.float32
        ).reshape(block_rows, heads_query, HEAD_SIZE)
        * score_scale
    )
    key_turned = (
        jnp.einsum("krij,ikrd->jkd", score_cot, query_rows, preferred_element_type=jnp.float32)
        * score_scale
    )
    query_back = rotary_apply(query_turned, cosine_table, -sine_values)
    key_back = rotary_apply(key_turned, cosine_table, -sine_values)
    querynorm_part = jnp.sum(query_back * query_unit, axis=(0, 1))
    keynorm_part = jnp.sum(key_back * key_unit, axis=(0, 1))
    query_raw_cot = (
        norm_back(query_back * query_factor, query_unit, query_scale)
        .astype(jnp.bfloat16)
        .reshape(block_rows, heads_query * HEAD_SIZE)
    )
    key_raw_cot = (
        norm_back(key_back * key_factor, key_unit, key_scale)
        .astype(jnp.bfloat16)
        .reshape(block_rows, heads_key * HEAD_SIZE)
    )
    query_gradient = contract(first_layer_normed, query_raw_cot)
    key_gradient = contract(first_layer_normed, key_raw_cot)
    value_gradient = contract(first_layer_normed, value_cot)
    first_part = (
        transposed(query_raw_cot, query_all)
        + transposed(key_raw_cot, key_all)
        + transposed(value_cot, value_all)
    )
    first_cot, querynorm_gradient, keynorm_gradient = (
        lax.psum(first_part.astype(jnp.bfloat16), "tensor").astype(jnp.float32),
        lax.psum(querynorm_part.astype(jnp.bfloat16), "tensor").astype(jnp.float32),
        lax.psum(keynorm_part.astype(jnp.bfloat16), "tensor").astype(jnp.float32),
    )
    prenorm_gradient = jnp.sum(first_cot * unit_first, axis=0)
    input_cot = residual_cot + norm_back(first_cot * gain_one, unit_first, scale_first)
    input_gradient = lax.dynamic_slice_in_dim(input_cot, own_start, own_rows, 0).astype(
        jnp.bfloat16
    )
    summed = (
        lax.psum_scatter(query_gradient, "dp", scatter_dimension=0, tiled=True),
        lax.psum_scatter(key_gradient, "dp", scatter_dimension=0, tiled=True),
        lax.psum_scatter(value_gradient, "dp", scatter_dimension=0, tiled=True),
        lax.psum_scatter(context_gradient, "dp", scatter_dimension=1, tiled=True),
        lax.psum_scatter(router_gradient, "dp", scatter_dimension=0, tiled=True),
        lax.psum_scatter(prenorm_gradient, "dp", scatter_dimension=0, tiled=True),
        lax.psum_scatter(midnorm_gradient, "dp", scatter_dimension=0, tiled=True),
        lax.psum_scatter(querynorm_gradient, "dp", scatter_dimension=0, tiled=True),
        lax.psum_scatter(keynorm_gradient, "dp", scatter_dimension=0, tiled=True),
    )
    return (
        layer_output,
        input_gradient,
        summed[0],
        summed[1],
        summed[2],
        summed[3],
        summed[4],
        gate_gradient,
        up_gradient,
        down_gradient,
        summed[5],
        summed[6],
        summed[7],
        summed[8],
    )


AUX = 128


GRID_Z = 4
VMEM_LIMIT = 56 * 1024 * 1024


def remote(src, dst, send_sem, recv_sem, device):
    return pltpu.make_async_remote_copy(
        src_ref=src,
        dst_ref=dst,
        send_sem=send_sem,
        recv_sem=recv_sem,
        device_id=device,
        device_id_type=pl.DeviceIdType.MESH,
    )


class Place:
    def __init__(self):
        self.dp = lax.axis_index("dp")
        self.y = lax.axis_index("tensor")
        self.z = self.dp // 4
        self.x = (self.dp // 2) % 2
        self.core = self.dp % 2
        self.sibling = (self.dp + 1 - 2 * self.core, self.y)
        self.x_mate = (self.dp + 2 - 4 * self.x, self.y)
        self.y_mate = (self.dp, 1 - self.y)
        self.above = (self.dp + 4, self.y)
        self.below = (self.dp - 4, self.y)
        self.has_above = self.z < GRID_Z - 1
        self.has_below = self.z > 0

    def farthest(self, k):
        return (3 - 3 * (self.z // 2), (2 + 3 * self.z) % 5, 1 + self.z % 2, self.z)[k]

    def dp_at(self, z, flip_x, flip_core):
        x = self.x + flip_x * (1 - 2 * self.x)
        core = self.core + flip_core * (1 - 2 * self.core)
        return z * 4 + x * 2 + core

    def y_at(self, flip_y):
        return self.y + flip_y * (1 - 2 * self.y)

    def greet(self):
        barrier = pltpu.get_barrier_semaphore()
        for mate in (self.sibling, self.x_mate, self.y_mate):
            pl.semaphore_signal(barrier, 1, device_id=mate, device_id_type=pl.DeviceIdType.MESH)

        @pl.when(self.has_above)
        def _():
            pl.semaphore_signal(
                barrier, 1, device_id=self.above, device_id_type=pl.DeviceIdType.MESH
            )

        @pl.when(self.has_below)
        def _():
            pl.semaphore_signal(
                barrier, 1, device_id=self.below, device_id_type=pl.DeviceIdType.MESH
            )

        pl.semaphore_wait(barrier, 4 + self.z * (GRID_Z - 1 - self.z) // 2)


def add_rows(target, sources, rows, step=16):
    start, count = rows

    def one(i, carry):
        at = pl.ds(pl.multiple_of(start + i * step, step), step)
        total = target[at, :].astype(jnp.float32)
        for source, shift in sources:
            there = pl.ds(pl.multiple_of(start - shift + i * step, step), step)
            total = total + source[there, :].astype(jnp.float32)
        target[at, :] = total.astype(target.dtype)
        return carry

    lax.fori_loop(0, count // step, one, 0)


def scatter_kernel(
    part, out, own, core, diag_a, diag_b, from_x, from_y, from_z, result,
    load_s, core_s, diag_s, x_s, y_s, z_s, out_s,
):
    me = Place()
    rows = own.shape[3]
    half = rows // 2
    low, high = (0, half), (half, half)
    loads, sends = {}, []

    def chunk(k, flip_x, flip_y, flip_core):
        return part.at[me.dp_at(me.farthest(k), flip_x, flip_core) * 2 + me.y_at(flip_y)]

    order = ((1, 1), (1, 0), (0, 1), (0, 0))
    for k in range(GRID_Z):
        for fx, fy in order:
            copy = pltpu.make_async_copy(
                chunk(k, fx, fy, 0), own.at[k, fx, fy], load_s.at[k, fx, fy]
            )
            copy.start()
            loads[k, fx, fy] = copy
    me.greet()
    cores = {}
    for k in range(GRID_Z):
        for fx, fy in order:
            copy = remote(
                chunk(k, fx, fy, 1), core.at[k, fx, fy],
                core_s.at[0, k, fx, fy], core_s.at[1, k, fx, fy], me.sibling,
            )
            copy.start()
            cores[k, fx, fy] = copy
            sends.append(copy)

    da = [remote(own.at[k, 1, 1, pl.ds(0, half)], diag_a.at[k], diag_s.at[0, k], diag_s.at[1, k], me.y_mate) for k in range(4)]
    db = [remote(own.at[k, 1, 1, pl.ds(half, half)], diag_b.at[k], diag_s.at[2, k], diag_s.at[3, k], me.x_mate) for k in range(4)]
    xs = [[remote(own.at[k, 1, 0, pl.ds(h * half, half)], from_x.at[k, pl.ds(h * half, half)], x_s.at[0, k, h], x_s.at[1, k, h], me.x_mate) for h in range(2)] for k in range(4)]
    ys = [[remote(own.at[k, 0, 1, pl.ds(h * half, half)], from_y.at[k, pl.ds(h * half, half)], y_s.at[0, k, h], y_s.at[1, k, h], me.y_mate) for h in range(2)] for k in range(4)]

    def arrive(k, fx, fy):
        loads[k, fx, fy].wait()
        cores[k, fx, fy].wait_recv()

    def early(k):
        arrive(k, 1, 1)
        add_rows(own.at[k, 1, 1], [(core.at[k, 1, 1], 0)], low)
        da[k].start()
        add_rows(own.at[k, 1, 1], [(core.at[k, 1, 1], 0)], high)
        db[k].start()
        arrive(k, 1, 0)
        add_rows(own.at[k, 1, 0], [(core.at[k, 1, 0], 0)], high)
        xs[k][1].start()
        arrive(k, 0, 1)
        add_rows(own.at[k, 0, 1], [(core.at[k, 0, 1], 0)], low)
        ys[k][0].start()

    def late(k):
        da[k].wait_recv()
        add_rows(own.at[k, 1, 0], [(core.at[k, 1, 0], 0), (diag_a.at[k], 0)], low)
        xs[k][0].start()
        db[k].wait_recv()
        add_rows(own.at[k, 0, 1], [(core.at[k, 0, 1], 0), (diag_b.at[k], half)], high)
        ys[k][1].start()

    whole = (0, rows)

    def column(k):
        arrive(k, 0, 0)
        for h in range(2):
            xs[k][h].wait_recv()
            ys[k][h].wait_recv()
        mine = own.at[k, 0, 0]
        rest = [(core.at[k, 0, 0], 0), (from_x.at[k], 0), (from_y.at[k], 0)]
        if k < GRID_Z - 1:
            to = me.farthest(k)
            add_rows(mine, rest, whole)
            for side, ahead, mate, more in (
                (0, to > me.z, me.above, me.has_below),
                (1, to < me.z, me.below, me.has_above),
            ):
                copy = remote(
                    mine, from_z.at[side, to], z_s.at[0, side, to], z_s.at[1, side, to], mate
                )

                @pl.when(ahead)
                def _():
                    @pl.when(more)
                    def _():
                        copy.wait_recv()
                        add_rows(mine, [(from_z.at[side, to], 0)], whole)

                    copy.start()
        else:
            add_rows(mine, rest, whole)
            for side, more in ((0, me.has_below), (1, me.has_above)):
                copy = remote(
                    mine, from_z.at[side, me.z], z_s.at[0, side, me.z], z_s.at[1, side, me.z],
                    me.y_mate,
                )

                @pl.when(more)
                def _():
                    copy.wait_recv()
                    add_rows(mine, [(from_z.at[side, me.z], 0)], whole)

    early(0)
    early(1)
    late(0)
    early(2)
    late(1)
    column(0)
    early(3)
    late(2)
    column(1)
    late(3)
    column(2)
    column(3)
    copy = pltpu.make_async_copy(own.at[3, 0, 0], out, out_s)
    copy.start()
    for k in range(GRID_Z):
        da[k].wait_send()
        db[k].wait_send()
        for h in range(2):
            xs[k][h].wait_send()
            ys[k][h].wait_send()
        if k < GRID_Z - 1:
            to = me.farthest(k)
            for side, ahead, mate in ((0, to > me.z, me.above), (1, to < me.z, me.below)):
                @pl.when(ahead)
                def _():
                    remote(
                        own.at[k, 0, 0], from_z.at[side, to],
                        z_s.at[0, side, to], z_s.at[1, side, to], mate,
                    ).wait_send()
    for sent in sends:
        sent.wait_send()
    copy.wait()


def scatter_all(value, collective_id):
    devices = lax.axis_size("dp") * lax.axis_size("tensor")
    rows, width = value.shape[0] // devices, value.shape[1]
    half = rows // 2
    dma = pltpu.SemaphoreType.DMA
    low = value.dtype
    return pl.pallas_call(
        scatter_kernel,
        out_shape=jax.ShapeDtypeStruct((rows, width), low),
        in_specs=[pl.BlockSpec(memory_space=pl.ANY)],
        out_specs=pl.BlockSpec(memory_space=pl.ANY),
        scratch_shapes=[
            pltpu.VMEM((4, 2, 2, rows, width), low),
            pltpu.VMEM((4, 2, 2, rows, width), low),
            pltpu.VMEM((4, half, width), low),
            pltpu.VMEM((4, half, width), low),
            pltpu.VMEM((4, rows, width), low),
            pltpu.VMEM((4, rows, width), low),
            pltpu.VMEM((2, 4, rows, width), low),
            pltpu.VMEM((8, 128), low),
            dma((4, 2, 2)),
            dma((2, 4, 2, 2)),
            dma((4, 4)),
            dma((2, 4, 2)),
            dma((2, 4, 2)),
            dma((2, 2, 4)),
            dma(()),
        ],
        compiler_params=pltpu.CompilerParams(
            collective_id=collective_id, has_side_effects=True, vmem_limit_bytes=VMEM_LIMIT
        ),
    )(value.reshape(devices, rows, width))


def gather_kernel(src, out, own_s, z_s, x_s, y_s, dx_s, dy_s, core_s):
    me = Place()
    rows = src.shape[0]
    half = rows // 2
    low, high = pl.ds(0, half), pl.ds(half, half)

    def near(k):
        return me.farthest(GRID_Z - 1 - k)

    def at(k, fx, fy, fc):
        return out.at[me.dp_at(near(k), fx, fc) * 2 + me.y_at(fy)]

    mine = pltpu.make_async_copy(src, at(0, 0, 0, 0), own_s)
    mine.start()
    me.greet()

    def over(source, k, fx, fy, send, recv, mate):
        return remote(source, at(k, fx, fy, 0), send, recv, mate)

    def z_copy(k, source, side, mate):
        zn = near(k)
        return remote(source, at(k, 0, 0, 0), z_s.at[0, side, zn], z_s.at[1, side, zn], mate)

    xs, ys, dxs, dys, cores = {}, {}, {}, {}, {}
    for k in range(GRID_Z):
        source = src if k == 0 else at(k, 0, 0, 0)
        xs[k] = over(source, k, 0, 0, x_s.at[0, k], x_s.at[1, k], me.x_mate)
        ys[k] = over(source, k, 0, 0, y_s.at[0, k], y_s.at[1, k], me.y_mate)
        dys[k] = remote(at(k, 1, 0, 0).at[low], at(k, 1, 0, 0).at[low], dy_s.at[0, k], dy_s.at[1, k], me.y_mate)
        dxs[k] = remote(at(k, 0, 1, 0).at[high], at(k, 0, 1, 0).at[high], dx_s.at[0, k], dx_s.at[1, k], me.x_mate)
        for fx in range(2):
            for fy in range(2):
                block = source if (fx, fy) == (0, 0) else at(k, fx, fy, 0)
                if (fx, fy) == (1, 1):
                    for h, part in enumerate((low, high)):
                        cores[k, fx, fy, h] = remote(
                            block.at[part], block.at[part],
                            core_s.at[0, k, 3 + h], core_s.at[1, k, 3 + h], me.sibling,
                        )
                else:
                    cores[k, fx, fy] = remote(
                        block, at(k, fx, fy, 0), core_s.at[0, k, fx * 2 + fy],
                        core_s.at[1, k, fx * 2 + fy], me.sibling,
                    )

    def own(k):
        if k == 0:
            for side, more, mate in ((0, me.has_above, me.above), (1, me.has_below, me.below)):
                copy = z_copy(0, src, side, mate)

                @pl.when(more)
                def _():
                    copy.start()
        else:
            zn = near(k)
            for side, came, more, mate in (
                (0, zn < me.z, me.has_above, me.above),
                (1, zn > me.z, me.has_below, me.below),
            ):
                copy = z_copy(k, at(k, 0, 0, 0), side, mate)

                @pl.when(came)
                def _():
                    copy.wait_recv()

                    @pl.when(more)
                    def _():
                        copy.start()

        xs[k].start()
        ys[k].start()
        cores[k, 0, 0].start()

    def diag(k):
        xs[k].wait_recv()
        dys[k].start()
        cores[k, 1, 0].start()
        ys[k].wait_recv()
        dxs[k].start()
        cores[k, 0, 1].start()

    def corner(k):
        dys[k].wait_recv()
        cores[k, 1, 1, 0].start()
        dxs[k].wait_recv()
        cores[k, 1, 1, 1].start()

    own(0)
    own(1)
    diag(0)
    own(2)
    diag(1)
    corner(0)
    own(3)
    diag(2)
    corner(1)
    diag(3)
    corner(2)
    corner(3)
    mine.wait()
    for k in range(GRID_Z):
        zn = near(k)
        for side, came, more, mate in (
            (0, zn <= me.z, me.has_above, me.above),
            (1, zn >= me.z, me.has_below, me.below),
        ):
            copy = z_copy(k, src if k == 0 else at(k, 0, 0, 0), side, mate)

            @pl.when(came)
            def _():
                @pl.when(more)
                def _():
                    copy.wait_send()
        for copy in (xs[k], ys[k], dxs[k], dys[k]):
            copy.wait_send()
    for copy in cores.values():
        copy.wait()


def gather_all(value, collective_id):
    devices = lax.axis_size("dp") * lax.axis_size("tensor")
    rows, width = value.shape
    dma = pltpu.SemaphoreType.DMA
    return pl.pallas_call(
        gather_kernel,
        out_shape=jax.ShapeDtypeStruct((devices, rows, width), value.dtype),
        in_specs=[pl.BlockSpec(memory_space=pl.ANY)],
        out_specs=pl.BlockSpec(memory_space=pl.ANY),
        scratch_shapes=[
            dma(()),
            dma((2, 2, 4)),
            dma((2, 4)),
            dma((2, 4)),
            dma((2, 4)),
            dma((2, 4)),
            dma((2, 4, 5)),
        ],
        compiler_params=pltpu.CompilerParams(collective_id=collective_id, has_side_effects=True),
    )(value).reshape(devices * rows, width)


def plane_gather_kernel(src, out, own_s, z_s, x_s, core_s):
    me = Place()

    def near(k):
        return me.farthest(GRID_Z - 1 - k)

    def at(k, fx):
        return out.at[me.dp_at(near(k), fx, 0)]

    mine = pltpu.make_async_copy(src, at(0, 0), own_s)
    mine.start()
    me.greet()

    def z_copy(k, side, mate):
        zn = near(k)
        return remote(
            src if k == 0 else at(k, 0), at(k, 0), z_s.at[0, side, zn], z_s.at[1, side, zn], mate
        )

    xs, cores = {}, {}
    for k in range(GRID_Z):
        source = src if k == 0 else at(k, 0)
        xs[k] = remote(source, at(k, 0), x_s.at[0, k], x_s.at[1, k], me.x_mate)
        cores[k, 0] = remote(source, at(k, 0), core_s.at[0, k, 0], core_s.at[1, k, 0], me.sibling)
        cores[k, 1] = remote(at(k, 1), at(k, 1), core_s.at[0, k, 1], core_s.at[1, k, 1], me.sibling)

    def own(k):
        zn = near(k)
        for side, came, more, mate in (
            (0, zn < me.z, me.has_above, me.above),
            (1, zn > me.z, me.has_below, me.below),
        ):
            copy = z_copy(k, side, mate)
            if k == 0:

                @pl.when(more)
                def _():
                    copy.start()
            else:

                @pl.when(came)
                def _():
                    copy.wait_recv()

                    @pl.when(more)
                    def _():
                        copy.start()

        xs[k].start()
        cores[k, 0].start()

    def diag(k):
        xs[k].wait_recv()
        cores[k, 1].start()

    own(0)
    own(1)
    diag(0)
    own(2)
    diag(1)
    own(3)
    diag(2)
    diag(3)
    mine.wait()
    for k in range(GRID_Z):
        zn = near(k)
        for side, came, more, mate in (
            (0, zn <= me.z, me.has_above, me.above),
            (1, zn >= me.z, me.has_below, me.below),
        ):
            copy = z_copy(k, side, mate)

            @pl.when(came)
            def _():
                @pl.when(more)
                def _():
                    copy.wait_send()

        xs[k].wait_send()
    for copy in cores.values():
        copy.wait()


def gather_dp(value, collective_id):
    devices = lax.axis_size("dp")
    rows, width = value.shape
    dma = pltpu.SemaphoreType.DMA
    return pl.pallas_call(
        plane_gather_kernel,
        out_shape=jax.ShapeDtypeStruct((devices, rows, width), value.dtype),
        in_specs=[pl.BlockSpec(memory_space=pl.ANY)],
        out_specs=pl.BlockSpec(memory_space=pl.ANY),
        scratch_shapes=[dma(()), dma((2, 2, 4)), dma((2, 4)), dma((2, 4, 2))],
        compiler_params=pltpu.CompilerParams(collective_id=collective_id, has_side_effects=True),
    )(value).reshape(devices * rows, width)


def plane_scatter_kernel(
    part, out, own, core, from_x, from_z, load_s, core_s, x_s, z_s, out_s
):
    me = Place()
    rows = own.shape[2]
    whole = (0, rows)
    loads, cores = {}, {}

    def chunk(k, flip_x, flip_core):
        return part.at[me.dp_at(me.farthest(k), flip_x, flip_core)]

    for k in range(GRID_Z):
        for fx in (1, 0):
            loads[k, fx] = pltpu.make_async_copy(chunk(k, fx, 0), own.at[k, fx], load_s.at[k, fx])
            loads[k, fx].start()
    me.greet()
    for k in range(GRID_Z):
        for fx in (1, 0):
            cores[k, fx] = remote(
                chunk(k, fx, 1), core.at[k, fx],
                core_s.at[0, k, fx], core_s.at[1, k, fx], me.sibling,
            )
            cores[k, fx].start()
    half = rows // 2
    xs = [
        [
            remote(
                own.at[k, 1, pl.ds(h * half, half)], from_x.at[k, pl.ds(h * half, half)],
                x_s.at[0, k, h], x_s.at[1, k, h], me.x_mate,
            )
            for h in range(2)
        ]
        for k in range(GRID_Z)
    ]

    def z_copy(k, side, mate):
        to = me.farthest(k)
        return remote(
            own.at[k, 0], from_z.at[side, to], z_s.at[0, side, to], z_s.at[1, side, to], mate
        )

    def across(k):
        loads[k, 1].wait()
        cores[k, 1].wait_recv()
        for h in range(2):
            add_rows(own.at[k, 1], [(core.at[k, 1], 0)], (h * half, half))
            xs[k][h].start()

    def column(k):
        loads[k, 0].wait()
        cores[k, 0].wait_recv()
        for h in range(2):
            xs[k][h].wait_recv()
        mine = own.at[k, 0]
        add_rows(mine, [(core.at[k, 0], 0), (from_x.at[k], 0)], whole)
        to = me.farthest(k)
        for side, ahead, mate, more in (
            (0, to > me.z, me.above, me.has_below),
            (1, to < me.z, me.below, me.has_above),
        ):
            copy = z_copy(k, side, mate)
            if k < GRID_Z - 1:

                @pl.when(ahead)
                def _():
                    @pl.when(more)
                    def _():
                        copy.wait_recv()
                        add_rows(mine, [(from_z.at[side, to], 0)], whole)

                    copy.start()
            else:

                @pl.when(more)
                def _():
                    copy.wait_recv()
                    add_rows(mine, [(from_z.at[side, to], 0)], whole)

    for k in range(GRID_Z):
        across(k)
        if k:
            column(k - 1)
    column(GRID_Z - 1)
    copy = pltpu.make_async_copy(own.at[3, 0], out, out_s)
    copy.start()
    for k in range(GRID_Z):
        for h in range(2):
            xs[k][h].wait_send()
        if k < GRID_Z - 1:
            to = me.farthest(k)
            for side, ahead, mate in ((0, to > me.z, me.above), (1, to < me.z, me.below)):

                @pl.when(ahead)
                def _():
                    z_copy(k, side, mate).wait_send()
    for sent in cores.values():
        sent.wait_send()
    copy.wait()


def scatter_dp(value, collective_id):
    devices = lax.axis_size("dp")
    rows, width = value.shape[0] // devices, value.shape[1]
    dma = pltpu.SemaphoreType.DMA
    low = value.dtype
    return pl.pallas_call(
        plane_scatter_kernel,
        out_shape=jax.ShapeDtypeStruct((rows, width), low),
        in_specs=[pl.BlockSpec(memory_space=pl.ANY)],
        out_specs=pl.BlockSpec(memory_space=pl.ANY),
        scratch_shapes=[
            pltpu.VMEM((4, 2, rows, width), low),
            pltpu.VMEM((4, 2, rows, width), low),
            pltpu.VMEM((4, rows, width), low),
            pltpu.VMEM((2, 4, rows, width), low),
            dma((4, 2)),
            dma((2, 4, 2)),
            dma((2, 4, 2)),
            dma((2, 2, 4)),
            dma(()),
        ],
        compiler_params=pltpu.CompilerParams(
            collective_id=collective_id, has_side_effects=True, vmem_limit_bytes=VMEM_LIMIT
        ),
    )(value.reshape(devices, rows, width))


WINDOW_ALIGN = 16
EXPERT_VMEM = 60 * 1024 * 1024


def dot(left, right, dims=((1,), (0,))):
    return lax.dot_general(left, right, (dims, ((), ())), preferred_element_type=jnp.float32)


def expert_kernel(
    info, pos, rows_in, cots_in, gate_w, up_w, down_w,
    out, back, gate_g, up_g, down_g,
    x, dy, wgu, wd, slot_out, slot_row, gu, hg, rows_b, cots_b, g_stage, d_stage,
    load_s, w_s, out_s, g_s, d_s,
):
    bf16, f32 = jnp.bfloat16, jnp.float32
    blocks, block_rows, wide = rows_in.shape
    features = cots_in.shape[2]
    experts, padded = x.shape[0], x.shape[1]
    part = hg.shape[2]
    cap = hg.shape[1]
    window = padded - cap
    tile = 256
    chunk = 512

    def load(b):
        slot = b % 2
        return (
            pltpu.make_async_copy(rows_in.at[b], rows_b.at[slot], load_s.at[slot, 0]),
            pltpu.make_async_copy(cots_in.at[b], cots_b.at[slot], load_s.at[slot, 1]),
        )

    for copy in load(0):
        copy.start()
    weights = []
    for e in range(experts):
        weights.append(pltpu.make_async_copy(gate_w.at[e], wgu.at[e, :, pl.ds(0, part)], w_s.at[e, 0]))
        weights.append(pltpu.make_async_copy(up_w.at[e], wgu.at[e, :, pl.ds(part, part)], w_s.at[e, 1]))
        weights.append(pltpu.make_async_copy(down_w.at[e], wd.at[e], w_s.at[e, 2]))
    for copy in weights:
        copy.start()

    def clear(i, carry):
        at = pl.ds(pl.multiple_of(i * 16, 16), 16)
        for e in range(experts):
            x[e, at, :] = jnp.zeros((16, wide), bf16)
            dy[e, at, :] = jnp.zeros((16, features), bf16)
        return carry

    lax.fori_loop(0, padded // 16, clear, 0)
    for e in range(experts):
        slot_out[e, pl.ds(cap, window), :] = jnp.zeros((window, features), bf16)
        slot_row[e, pl.ds(cap, window), :] = jnp.zeros((window, wide), bf16)

    def starts(b):
        return [pl.multiple_of(info[1 + b * experts + e], WINDOW_ALIGN) for e in range(experts)]

    def picks(b, begin):
        slots = lax.broadcasted_iota(jnp.int32, (window, block_rows), 0)
        return jnp.concatenate(
            [(slots + begin[e] == pos[b, pl.ds(e, 1), :]).astype(f32) for e in range(experts)],
            axis=0,
        )

    def take(b, carry):
        slot = b % 2

        @pl.when(b + 1 < blocks)
        def _():
            for copy in load(b + 1):
                copy.start()

        begin = starts(b)
        picked = picks(b, begin).astype(bf16)
        for copy in load(b):
            copy.wait()
        for source, target, width in ((rows_b, x, wide), (cots_b, dy, features)):
            for first in range(0, width, chunk):
                cols = pl.ds(first, min(chunk, width - first))
                got = dot(picked, source[slot, :, cols]).astype(bf16)
                for e in range(experts):
                    at = pl.ds(begin[e], window)
                    target[e, at, cols] += got[e * window : (e + 1) * window]
        return carry

    lax.fori_loop(0, blocks, take, 0)
    for copy in weights:
        copy.wait()

    lanes = lax.broadcasted_iota(jnp.int32, (tile, AUX), 1)

    def mlp(step, carry):
        e = step // (cap // tile)
        at = pl.ds(pl.multiple_of((step % (cap // tile)) * tile, tile), tile)
        own = info[0] * experts + e
        total = blocks * experts
        aux = x[e, at, pl.ds(features, AUX)].astype(f32)
        gate = jnp.sum(
            jnp.where((lanes == own) | (lanes == own + total), aux, 0.0), axis=1, keepdims=True
        )
        pre = dot(x[e, at, pl.ds(0, features)], wgu[e])
        gate_pre, up_pre = pre[:, :part], pre[:, part:]
        sig = 1.0 / (1.0 + jnp.exp(-gate_pre))
        act = gate_pre * sig
        hidden = (act * up_pre).astype(bf16).astype(f32)
        gated = (hidden * gate).astype(bf16)
        hg[e, at, :] = gated
        down_cot = dot(dy[e, at, :], wd[e], ((1,), (1,)))
        slot_cot = jnp.sum(hidden * down_cot, axis=1, keepdims=True)
        hidden_cot = down_cot * gate
        gu[e, at, pl.ds(0, part)] = (
            hidden_cot * up_pre * sig * (1.0 + gate_pre * (1.0 - sig))
        ).astype(bf16)
        gu[e, at, pl.ds(part, part)] = (hidden_cot * act).astype(bf16)
        for first in range(0, features, chunk):
            cols = pl.ds(first, chunk)
            slot_out[e, at, cols] = dot(gated, wd[e, :, cols]).astype(bf16)
            slot_row[e, at, cols] = dot(
                gu[e, at, :], wgu[e, pl.ds(first, chunk), :], ((1,), (1,))
            ).astype(bf16)
        high = slot_cot.astype(bf16).astype(f32)
        place = info[1 + blocks * experts] * 2 * total + own * 2
        slot_row[e, at, pl.ds(features, AUX)] = jnp.where(
            lanes == place, high, jnp.where(lanes == place + 1, slot_cot - high, 0.0)
        ).astype(bf16)
        return carry

    lax.fori_loop(0, experts * (cap // tile), mlp, 0)

    def stored(b):
        slot = b % 2
        return (
            pltpu.make_async_copy(cots_b.at[slot], out.at[b], out_s.at[slot, 0]),
            pltpu.make_async_copy(rows_b.at[slot], back.at[b], out_s.at[slot, 1]),
        )

    def put(b, carry):
        slot = b % 2

        @pl.when(b >= 2)
        def _():
            for copy in stored(b - 2):
                copy.wait()

        begin = starts(b)
        spread = picks(b, begin).T.astype(bf16)
        for source, target, width in ((slot_out, cots_b, features), (slot_row, rows_b, wide)):
            for first in range(0, width, chunk):
                cols = pl.ds(first, min(chunk, width - first))
                held = jnp.concatenate(
                    [source[e, pl.ds(begin[e], window), cols] for e in range(experts)], axis=0
                )
                target[slot, :, cols] = dot(spread, held).astype(bf16)
        for copy in stored(b):
            copy.start()
        return carry

    lax.fori_loop(0, blocks, put, 0)

    tiles = features // tile

    def g_copies(step):
        slot = step % 2
        e, at = step // tiles, pl.ds(pl.multiple_of((step % tiles) * tile, tile), tile)
        return (
            pltpu.make_async_copy(g_stage.at[slot, :, pl.ds(0, part)], gate_g.at[e, at], g_s.at[slot, 0]),
            pltpu.make_async_copy(g_stage.at[slot, :, pl.ds(part, part)], up_g.at[e, at], g_s.at[slot, 1]),
        )

    def wide_grad(step, carry):
        slot = step % 2
        e, at = step // tiles, pl.ds(pl.multiple_of((step % tiles) * tile, tile), tile)

        @pl.when(step >= 2)
        def _():
            for copy in g_copies(step - 2):
                copy.wait()

        g_stage[slot] = dot(x[e, pl.ds(0, cap), at], gu[e], ((0,), (0,)))
        for copy in g_copies(step):
            copy.start()
        return carry

    lax.fori_loop(0, experts * tiles, wide_grad, 0)
    parts = features // chunk

    def d_copy(step):
        slot = step % 2
        e, at = step // parts, pl.ds(pl.multiple_of((step % parts) * chunk, chunk), chunk)
        return pltpu.make_async_copy(d_stage.at[slot], down_g.at[e, :, at], d_s.at[slot])

    def down_grad(step, carry):
        slot = step % 2
        e, at = step // parts, pl.ds(pl.multiple_of((step % parts) * chunk, chunk), chunk)

        @pl.when(step >= 2)
        def _():
            d_copy(step - 2).wait()

        d_stage[slot] = dot(hg[e], dy[e, pl.ds(0, cap), at], ((0,), (0,)))
        d_copy(step).start()
        return carry

    lax.fori_loop(0, experts * parts, down_grad, 0)
    for last in (2, 1):
        for copy in stored(blocks - last):
            copy.wait()
        for copy in g_copies(experts * tiles - last):
            copy.wait()
        d_copy(experts * parts - last).wait()


def expert_layer(info, pos, rows_in, cots_in, gate_w, up_w, down_w, capacity, most):
    bf16, f32 = jnp.bfloat16, jnp.float32
    blocks, block_rows, wide = rows_in.shape
    features = cots_in.shape[2]
    experts, part = gate_w.shape[0], gate_w.shape[2]
    padded = capacity + -(-most // WINDOW_ALIGN) * WINDOW_ALIGN + WINDOW_ALIGN
    dma = pltpu.SemaphoreType.DMA
    shape = jax.ShapeDtypeStruct
    anywhere = pl.BlockSpec(memory_space=pl.ANY)
    return pl.pallas_call(
        expert_kernel,
        out_shape=(
            shape((blocks, block_rows, features), bf16),
            shape((blocks, block_rows, wide), bf16),
            shape(gate_w.shape, f32),
            shape(up_w.shape, f32),
            shape(down_w.shape, f32),
        ),
        in_specs=[
            pl.BlockSpec(memory_space=pltpu.SMEM),
            pl.BlockSpec(memory_space=pltpu.VMEM),
        ]
        + [anywhere] * 5,
        out_specs=(anywhere,) * 5,
        scratch_shapes=[
            pltpu.VMEM((experts, padded, wide), bf16),
            pltpu.VMEM((experts, padded, features), bf16),
            pltpu.VMEM((experts, features, 2 * part), bf16),
            pltpu.VMEM((experts, part, features), bf16),
            pltpu.VMEM((experts, padded, features), bf16),
            pltpu.VMEM((experts, padded, wide), bf16),
            pltpu.VMEM((experts, capacity, 2 * part), bf16),
            pltpu.VMEM((experts, capacity, part), bf16),
            pltpu.VMEM((2, block_rows, wide), bf16),
            pltpu.VMEM((2, block_rows, features), bf16),
            pltpu.VMEM((2, 256, 2 * part), f32),
            pltpu.VMEM((2, part, 512), f32),
            dma((2, 2)),
            dma((experts, 3)),
            dma((2, 2)),
            dma((2, 2)),
            dma((2,)),
        ],
        compiler_params=pltpu.CompilerParams(vmem_limit_bytes=EXPERT_VMEM),
    )(info, pos, rows_in, cots_in, gate_w, up_w, down_w)


ATTENTION_VMEM = 60 * 1024 * 1024
SCORE_SCALE = HEAD_SIZE ** (-0.5)
def turn_tables(rows):
    frequency = np.exp(
        -math.log(rope_base) * np.arange(HEAD_SIZE // 2, dtype=np.float32) * (2.0 / HEAD_SIZE)
    ).astype(np.float32)
    angles = np.arange(rows, dtype=np.float32)[:, None] * frequency[None, :]
    cosine, sine = np.cos(angles), np.sin(angles)
    return (
        np.concatenate([cosine, cosine], axis=1).astype(np.float32),
        np.concatenate([-sine, sine], axis=1).astype(np.float32),
    )


def turn(value, cosine, sine):
    return value * cosine + pltpu.roll(value, HEAD_SIZE // 2, 1) * sine


def inverse_norm(value):
    return lax.rsqrt(jnp.mean(value * value, axis=-1, keepdims=True) + epsilon)


def meet_y(me):
    barrier = pltpu.get_barrier_semaphore()
    pl.semaphore_signal(barrier, 1, device_id=me.y_mate, device_id_type=pl.DeviceIdType.MESH)
    pl.semaphore_wait(barrier, 1)


def gain_rows(aux_t, experts, chunks):
    head = [aux_t[experts + 2 + i : experts + 3 + i, :] for i in range(2)]
    width = HEAD_SIZE
    heads = [sum(row[:, c * width : (c + 1) * width] for c in range(chunks)) for row in head]
    return aux_t[experts : experts + 1, :], aux_t[experts + 1 : experts + 2, :], *heads


def probabilities(query, key, allowed):
    scores = jnp.where(allowed, dot(query, key, ((1,), (1,))) * SCORE_SCALE, masked_score)
    spread = jnp.exp(scores - jnp.max(scores, axis=-1, keepdims=True))
    return spread / jnp.sum(spread, axis=-1, keepdims=True)


def allowed_pairs(live):
    rows = live.shape[1]
    later = lax.broadcasted_iota(jnp.int32, (rows, rows), 0)
    sooner = lax.broadcasted_iota(jnp.int32, (rows, rows), 1)
    return (sooner <= later) & (live[0:1, :] > 0.0)


def forward_kernel(
    experts, x_pair, packed, live, chosen, cosine, sine,
    sent_o, residual_o, normed_o, raw_o, query_o, key_o, value_o, context_o,
    x, w, ctx, aux_w, normed, raw, query, key, value, context, att, got, residual, sent,
    in_s, w_s, out_s, y_s,
):
    bf16, f32 = jnp.bfloat16, jnp.float32
    me = Place()
    rows, features = x.shape
    own_rows = rows // 2
    heads, key_heads = query.shape[0], key.shape[0]
    qkv = w.shape[1]
    chunk = 512
    mine = pl.ds(pl.multiple_of(me.y * own_rows, own_rows), own_rows)
    theirs = pl.ds(pl.multiple_of((1 - me.y) * own_rows, own_rows), own_rows)
    loads = [
        pltpu.make_async_copy(x_pair, x, in_s.at[0]),
        pltpu.make_async_copy(
            packed.at[:, pl.ds(qkv + ctx.shape[1], AUX)], aux_w, in_s.at[1]
        ),
        pltpu.make_async_copy(packed.at[:, pl.ds(qkv, ctx.shape[1])], ctx, in_s.at[2]),
    ]
    parts = [
        pltpu.make_async_copy(
            packed.at[:, pl.ds(c * chunk, chunk)], w.at[:, pl.ds(c * chunk, chunk)], w_s.at[c]
        )
        for c in range(qkv // chunk)
    ]
    loads[0].start()
    loads[1].start()
    for copy in parts:
        copy.start()
    loads[2].start()
    meet_y(me)
    loads[1].wait()
    aux_t = aux_w[...].astype(f32).T
    gain_one, gain_two, query_gain, key_gain = gain_rows(aux_t, experts, features // HEAD_SIZE)
    loads[0].wait()

    def first_norm(i, carry):
        at = pl.ds(pl.multiple_of(i * 32, 32), 32)
        stream = x[at, :].astype(f32)
        normed[at, :] = (stream * inverse_norm(stream) * gain_one).astype(bf16)
        return carry

    lax.fori_loop(0, rows // 32, first_norm, 0)
    for c, copy in enumerate(parts):
        copy.wait()
        got_raw = dot(normed[...], w[:, c * chunk : (c + 1) * chunk])
        for h in range(chunk // HEAD_SIZE):
            raw[c * (chunk // HEAD_SIZE) + h] = got_raw[:, h * HEAD_SIZE : (h + 1) * HEAD_SIZE]
    turn_c, turn_s = cosine[...], sine[...]
    for g in range(key_heads):
        unnormed = raw[heads + g]
        key[g] = turn(unnormed * inverse_norm(unnormed) * key_gain, turn_c, turn_s).astype(bf16)
        value[g] = raw[heads + key_heads + g].astype(bf16)
    allowed = allowed_pairs(live[...])

    def head(h, carry):
        g = h // (heads // key_heads)
        unnormed = raw[h]
        turned = turn(unnormed * inverse_norm(unnormed) * query_gain, turn_c, turn_s).astype(bf16)
        query[h] = turned
        probs = probabilities(turned, key[g], allowed).astype(bf16)
        at = pl.ds(pl.multiple_of(h * HEAD_SIZE, HEAD_SIZE), HEAD_SIZE)
        context[:, at] = dot(probs, value[g]).astype(bf16)
        return carry

    lax.fori_loop(0, heads, head, 0)
    outs = [
        pltpu.make_async_copy(source, target, out_s.at[i])
        for i, (source, target) in enumerate(
            ((normed, normed_o), (raw, raw_o), (query, query_o), (key, key_o), (value, value_o),
             (context, context_o))
        )
    ]
    for copy in outs:
        copy.start()
    loads[2].wait()
    copies = []
    for c in range(features // chunk):
        cols = pl.ds(c * chunk, chunk)
        att[theirs, cols] = dot(context[theirs, :], ctx[cols, :], ((1,), (1,))).astype(bf16)
        copy = remote(
            att.at[theirs, cols], got.at[:, cols], y_s.at[0, c], y_s.at[1, c], me.y_mate
        )
        copy.start()
        copies.append(copy)
    for c in range(features // chunk):
        cols = pl.ds(c * chunk, chunk)
        residual[:, cols] = dot(context[mine, :], ctx[cols, :], ((1,), (1,)))
    for copy in copies:
        copy.wait_recv()

    def second_norm(i, carry):
        at = pl.ds(pl.multiple_of(i * 16, 16), 16)
        there = pl.ds(pl.multiple_of(me.y * own_rows + i * 16, 16), 16)
        total = x[there, :].astype(f32) + (residual[at, :] + got[at, :].astype(f32))
        residual[at, :] = total
        sent[at, pl.ds(0, features)] = (total * inverse_norm(total) * gain_two).astype(bf16)
        return carry

    lax.fori_loop(0, own_rows // 16, second_norm, 0)
    logits = dot(sent[:, :features], aux_w[...])
    picked = chosen[...] > 0.0
    logits = jnp.where(picked, logits, masked_score)
    spread = jnp.where(picked, jnp.exp(logits - jnp.max(logits, axis=-1, keepdims=True)), 0.0)
    gates = spread / jnp.sum(spread, axis=-1, keepdims=True)
    high = gates.astype(bf16).astype(f32)
    sent[:, pl.ds(features, AUX)] = (high + pltpu.roll(gates - high, experts, 1)).astype(bf16)
    last = [
        pltpu.make_async_copy(sent, sent_o, out_s.at[6]),
        pltpu.make_async_copy(residual, residual_o, out_s.at[7]),
    ]
    for copy in last:
        copy.start()
    for copy in copies:
        copy.wait_send()
    for copy in outs + last:
        copy.wait()


def attention_forward(x_pair, packed, live, chosen, experts, heads, key_heads, collective_id):
    bf16, f32 = jnp.bfloat16, jnp.float32
    rows, features = x_pair.shape
    qkv = (heads + 2 * key_heads) * HEAD_SIZE
    cosine, sine = turn_tables(rows)
    dma = pltpu.SemaphoreType.DMA
    shapes = (
        ((rows // 2, features + AUX), bf16),
        ((rows // 2, features), f32),
        ((rows, features), bf16),
        ((heads + 2 * key_heads, rows, HEAD_SIZE), f32),
        ((heads, rows, HEAD_SIZE), bf16),
        ((key_heads, rows, HEAD_SIZE), bf16),
        ((key_heads, rows, HEAD_SIZE), bf16),
        ((rows, heads * HEAD_SIZE), bf16),
    )
    anywhere, vmem = pl.BlockSpec(memory_space=pl.ANY), pl.BlockSpec(memory_space=pltpu.VMEM)
    return pl.pallas_call(
        functools.partial(forward_kernel, experts),
        out_shape=tuple(jax.ShapeDtypeStruct(*shape) for shape in shapes),
        in_specs=[anywhere, anywhere, vmem, vmem, vmem, vmem],
        out_specs=(anywhere,) * len(shapes),
        scratch_shapes=[
            pltpu.VMEM((rows, features), bf16),
            pltpu.VMEM((features, qkv), bf16),
            pltpu.VMEM((features, heads * HEAD_SIZE), bf16),
            pltpu.VMEM((features, AUX), bf16),
            pltpu.VMEM((rows, features), bf16),
            pltpu.VMEM((heads + 2 * key_heads, rows, HEAD_SIZE), f32),
            pltpu.VMEM((heads, rows, HEAD_SIZE), bf16),
            pltpu.VMEM((key_heads, rows, HEAD_SIZE), bf16),
            pltpu.VMEM((key_heads, rows, HEAD_SIZE), bf16),
            pltpu.VMEM((rows, heads * HEAD_SIZE), bf16),
            pltpu.VMEM((rows, features), bf16),
            pltpu.VMEM((rows // 2, features), bf16),
            pltpu.VMEM((rows // 2, features), f32),
            pltpu.VMEM((rows // 2, features + AUX), bf16),
            dma((3,)),
            dma((qkv // 512,)),
            dma((8,)),
            dma((2, features // 512)),
        ],
        compiler_params=pltpu.CompilerParams(
            collective_id=collective_id, has_side_effects=True, vmem_limit_bytes=ATTENTION_VMEM
        ),
    )(x_pair, packed, live, chosen, cosine, sine)


def split_high_low(value):
    high = value.astype(jnp.bfloat16)
    return high, (value - high.astype(jnp.float32)).astype(jnp.bfloat16)


def gathered_body(
    layer_input,
    query_weight,
    key_projection,
    value_projection,
    context_weight,
    router_weight,
    expert_gate,
    expert_up,
    expert_down,
    prenorm_gain,
    midnorm_gain,
    querynorm_gain,
    keynorm_gain,
    routes,
    lengths,
    sequence_order,
    output_cotangent,
):
    bf16, f32 = jnp.bfloat16, jnp.float32
    tensor_count = lax.axis_size("tensor")
    tensor_index = lax.axis_index("tensor")
    dp_count = lax.axis_size("dp")
    dp_index = lax.axis_index("dp")
    own_rows, features = layer_input.shape
    block_rows = own_rows * tensor_count
    tokens = block_rows * dp_count
    expert_count = EXP_DEV * dp_count
    capacity = 3 * block_rows * TOP // (4 * EXP_DEV)
    most_rows = (5 * block_rows * TOP + 4 * expert_count - 1) // (4 * expert_count)
    shard = features // dp_count
    query_width = query_weight.shape[1]
    key_width = key_projection.shape[1]
    norm_part = HEAD_SIZE // dp_count

    place = dp_index * norm_part
    gains = jnp.concatenate(
        [
            prenorm_gain[:, None],
            midnorm_gain[:, None],
            lax.dynamic_update_slice(jnp.zeros((shard,), bf16), querynorm_gain, (place,))[:, None],
            lax.dynamic_update_slice(jnp.zeros((shard,), bf16), keynorm_gain, (place,))[:, None],
            jnp.zeros((shard, AUX - expert_count - 4), bf16),
        ],
        axis=1,
    )
    packed = jnp.concatenate(
        [query_weight, key_projection, value_projection, context_weight.T, router_weight, gains],
        axis=1,
    )
    packed = gather_dp(packed, 0)
    edges = [0]
    for width in (query_width, key_width, key_width, query_width, expert_count, AUX - expert_count):
        edges.append(edges[-1] + width)
    qkv_all = packed[:, : edges[3]]
    context_all = packed[:, edges[3] : edges[4]]
    router_all = packed[:, edges[4] : edges[5]]
    gains_all = packed[:, edges[5] :].astype(f32)
    gain_one, gain_two = gains_all[:, 0], gains_all[:, 1]
    query_factor = jnp.sum(gains_all[:, 2].reshape(dp_count, shard), axis=0)
    key_factor = jnp.sum(gains_all[:, 3].reshape(dp_count, shard), axis=0)

    cot_all = lax.all_gather(output_cotangent, ("dp", "tensor"), axis=0, tiled=True)
    routes_all = lax.all_gather(routes.T, "dp")
    input_rows = lax.all_gather(layer_input, "tensor", axis=0, tiled=True)
    position = jnp.arange(block_rows, dtype=jnp.int32)
    block_lengths = lengths[sequence_order]
    live = position[None, :] < block_lengths[:, None]
    live_own = lax.dynamic_slice_in_dim(live, dp_index, 1, 0)
    live_own = jnp.broadcast_to(live_own.astype(f32), (8, block_rows))
    heads_query = query_width // HEAD_SIZE
    heads_key = key_width // HEAD_SIZE
    group_width = heads_query // heads_key
    row_start = tensor_index * own_rows
    routes_own = lax.dynamic_slice_in_dim(routes, row_start, own_rows, 0)
    expert_ids = jnp.arange(AUX, dtype=jnp.int32)
    chosen = jnp.any(routes_own[:, :, None] == expert_ids[None, None, :], axis=1).astype(f32)
    (
        sent,
        residual,
        first_normed,
        raw,
        query_heads,
        key_heads,
        value_heads,
        context,
    ) = attention_forward(
        input_rows, packed, live_own, chosen, expert_count, heads_query, heads_key, 5
    )
    normed_all = gather_all(sent, 1).reshape(dp_count, block_rows, features + AUX)

    cosine_table, sine_values = turn_tables(block_rows)
    cosine_table = cosine_table[:, None, : HEAD_SIZE // 2]
    sine_values = sine_values[:, None, HEAD_SIZE // 2 :]
    unit_first, scale_first = rms_normalize(input_rows.astype(f32))
    rows_first = raw.transpose(1, 0, 2)
    query_unit, query_scale = rms_normalize(rows_first[:, :heads_query])
    key_unit, key_scale = rms_normalize(rows_first[:, heads_query : heads_query + heads_key])
    query_rows = query_heads.transpose(1, 0, 2).reshape(
        block_rows, heads_key, group_width, HEAD_SIZE
    )
    keys_rot = key_heads.transpose(1, 0, 2)
    value_rows = value_heads.transpose(1, 0, 2)
    score_scale = SCORE_SCALE
    allowed = (position[None, :] <= position[:, None]) & (live_own[0:1] > 0.0)
    scores = (
        jnp.einsum("ikrd,jkd->krij", query_rows, keys_rot, preferred_element_type=f32)
        * score_scale
    )
    scores = jnp.where(allowed, scores, masked_score)
    weights = jnp.exp(scores - jnp.max(scores, axis=-1, keepdims=True))
    soft_probs = weights / jnp.sum(weights, axis=-1, keepdims=True)
    probs_low = soft_probs.astype(bf16)
    unit_second, scale_second = rms_normalize(residual)
    normed_second = sent[:, :features]
    gates = (
        sent[:, features : features + expert_count].astype(f32)
        + sent[:, features + expert_count : features + 2 * expert_count].astype(f32)
    )

    expert_own = dp_index * EXP_DEV + jnp.arange(EXP_DEV, dtype=jnp.int32)
    hot = jnp.any(routes_all[:, None, :, :] == expert_own[None, :, None, None], axis=2)
    hot = hot & live[:, None, :]
    before = (position[:, None] < position[None, :]).astype(bf16)
    rank = jnp.einsum("bes,st->bet", hot.astype(bf16), before, preferred_element_type=f32)
    rank = rank.astype(jnp.int32)
    counts = rank[:, :, -1] + hot[:, :, -1]
    earlier = jnp.cumsum(counts, axis=0) - counts
    slot = earlier[:, :, None] + rank
    slot = jnp.where(hot & (slot < capacity), slot, -capacity)
    begin = jnp.minimum(earlier, capacity) // WINDOW_ALIGN * WINDOW_ALIGN
    info = jnp.concatenate([dp_index[None], begin.reshape(-1), tensor_index[None]])
    out_part, back_part, gate_gradient, up_gradient, down_gradient = expert_layer(
        info.astype(jnp.int32),
        slot,
        normed_all,
        cot_all.reshape(dp_count, block_rows, features),
        expert_gate,
        expert_up,
        expert_down,
        capacity,
        most_rows,
    )
    returned = scatter_all(back_part.reshape(tokens, features + AUX), 3).astype(f32)
    expert_sum = scatter_all(out_part.reshape(tokens, features), 2)
    layer_output = (residual + expert_sum.astype(f32)).astype(bf16)

    gate_cot = jnp.sum(
        returned[:, features:].reshape(own_rows, tensor_count, expert_count, 2), axis=(1, 3)
    )
    logit_cot = (
        gates * (gate_cot - jnp.sum(gates * gate_cot, axis=-1, keepdims=True))
    ).astype(bf16)
    router_part = contract(normed_second, logit_cot)
    normed_cot = returned[:, :features] + transposed(logit_cot, router_all)
    midnorm_part = jnp.sum(normed_cot * unit_second, axis=0)
    residual_cot = output_cotangent.astype(f32) + norm_back(
        normed_cot * gain_two, unit_second, scale_second
    )
    attention_cot = lax.all_gather(residual_cot.astype(bf16), "tensor", axis=0, tiled=True)

    context_part = contract(attention_cot, context)
    context_cot = (
        matrix_product(attention_cot, context_all)
        .astype(bf16)
        .reshape(block_rows, heads_key, group_width, HEAD_SIZE)
    )
    prob_cot = jnp.einsum("ikrd,jkd->krij", context_cot, value_rows, preferred_element_type=f32)
    score_cot = (
        soft_probs * (prob_cot - jnp.sum(soft_probs * prob_cot, axis=-1, keepdims=True))
    ).astype(bf16)
    value_cot = jnp.einsum("krij,ikrd->jkd", probs_low, context_cot, preferred_element_type=f32)
    value_cot = value_cot.astype(bf16).reshape(block_rows, key_width)
    query_turned = (
        jnp.einsum("krij,jkd->ikrd", score_cot, keys_rot, preferred_element_type=f32).reshape(
            block_rows, heads_query, HEAD_SIZE
        )
        * score_scale
    )
    key_turned = (
        jnp.einsum("krij,ikrd->jkd", score_cot, query_rows, preferred_element_type=f32)
        * score_scale
    )
    query_back = rotary_apply(query_turned, cosine_table, -sine_values)
    key_back = rotary_apply(key_turned, cosine_table, -sine_values)
    querynorm_part = jnp.sum(query_back * query_unit, axis=(0, 1))
    keynorm_part = jnp.sum(key_back * key_unit, axis=(0, 1))
    query_raw_cot = norm_back(query_back * query_factor, query_unit, query_scale).astype(bf16)
    key_raw_cot = norm_back(key_back * key_factor, key_unit, key_scale).astype(bf16)
    raw_cot = jnp.concatenate(
        [
            query_raw_cot.reshape(block_rows, query_width),
            key_raw_cot.reshape(block_rows, key_width),
            value_cot,
        ],
        axis=1,
    )
    qkv_part = contract(first_normed, raw_cot)
    first_cot = lax.psum_scatter(
        transposed(raw_cot, qkv_all).astype(bf16), "tensor", scatter_dimension=0, tiled=True
    ).astype(f32)
    unit_own = lax.dynamic_slice_in_dim(unit_first, row_start, own_rows, 0)
    scale_own = lax.dynamic_slice_in_dim(scale_first, row_start, own_rows, 0)
    prenorm_part = jnp.sum(first_cot * unit_own, axis=0)
    input_gradient = (
        residual_cot + norm_back(first_cot * gain_one, unit_own, scale_own)
    ).astype(bf16)

    small = jnp.zeros((dp_count, shard, AUX), f32)
    small = small.at[:, :, :expert_count].set(router_part.reshape(dp_count, shard, expert_count))
    small = small.at[:, :, expert_count].set(prenorm_part.reshape(dp_count, shard))
    small = small.at[:, :, expert_count + 1].set(midnorm_part.reshape(dp_count, shard))
    small = small.at[:, :norm_part, expert_count + 2].set(querynorm_part.reshape(dp_count, -1))
    small = small.at[:, :norm_part, expert_count + 3].set(keynorm_part.reshape(dp_count, -1))
    small = lax.psum_scatter(small.reshape(features, AUX), "dp", scatter_dimension=0, tiled=True)
    small = lax.psum(small, "tensor")
    summed = scatter_dp(jnp.concatenate([qkv_part.astype(bf16), context_part.astype(bf16)], axis=1), 4)
    summed = summed.astype(f32)
    return (
        layer_output,
        input_gradient,
        summed[:, : edges[1]],
        summed[:, edges[1] : edges[2]],
        summed[:, edges[2] : edges[3]],
        summed[:, edges[3] :].T,
        small[:, :expert_count],
        gate_gradient,
        up_gradient,
        down_gradient,
        small[:, expert_count],
        small[:, expert_count + 1],
        small[:norm_part, expert_count + 2],
        small[:norm_part, expert_count + 3],
    )


def solution(mesh):
    return jax.shard_map(
        gathered_body if mesh.shape["dp"] <= 16 else body,
        mesh=mesh,
        in_specs=(
            P(("dp", "tensor"), None),
            P("dp", "tensor"),
            P("dp", "tensor"),
            P("dp", "tensor"),
            P("tensor", "dp"),
            P("dp", None),
            P("dp", None, "tensor"),
            P("dp", None, "tensor"),
            P("dp", "tensor", None),
            P("dp"),
            P("dp"),
            P("dp"),
            P("dp"),
            P("dp", None),
            P(),
            P(),
            P(("dp", "tensor"), None),
        ),
        out_specs=(
            P(("dp", "tensor"), None),
            P(("dp", "tensor"), None),
            P("dp", "tensor"),
            P("dp", "tensor"),
            P("dp", "tensor"),
            P("tensor", "dp"),
            P("dp", None),
            P("dp", None, "tensor"),
            P("dp", None, "tensor"),
            P("dp", "tensor", None),
            P("dp"),
            P("dp"),
            P("dp"),
            P("dp"),
        ),
        check_vma=False,
    )
```

```python
import functools
import math

import jax
import jax.numpy as jnp
import numpy as np
from jax import lax
from jax.experimental import pallas as pl
from jax.experimental.pallas import tpu as pltpu
from jax.sharding import PartitionSpec as P

HEAD_SIZE = 128
TOP = 8
EXP_DEV = 2


epsilon = 1e-06
rope_base = 1000000.0
masked_score = -1e30


def carried_in(value, axis, combine, identity):
    count, place = (lax.axis_size(axis), lax.axis_index(axis))
    everything = lax.all_gather(value, axis)
    start = jnp.broadcast_to(jnp.asarray(identity, value.dtype), value.shape)

    def hop(k, before):
        reached = k < place
        new = combine(before, everything[k])
        return jnp.where(reached, new, before)

    return lax.fori_loop(0, count, hop, start)


def rms_normalize(value_rows):
    scaling = lax.rsqrt(jnp.mean(value_rows * value_rows, axis=-1, keepdims=True) + epsilon)
    return (value_rows * scaling, scaling)


def norm_back(cotangent, unit_rows, scaling):
    return scaling * (
        cotangent - unit_rows * jnp.mean(cotangent * unit_rows, axis=-1, keepdims=True)
    )


def rotary_apply(value_rows, cosine_table, sine_values):
    middle = value_rows.shape[-1] // 2
    former = value_rows[..., :middle]
    latter = value_rows[..., middle:]
    return jnp.concatenate(
        [
            former * cosine_table - latter * sine_values,
            latter * cosine_table + former * sine_values,
        ],
        axis=-1,
    )


def matrix_product(former, latter):
    return jnp.dot(former, latter, preferred_element_type=jnp.float32)


def contract(former, latter):
    return lax.dot_general(
        former, latter, (((0,), (0,)), ((), ())), preferred_element_type=jnp.float32
    )


def transposed(former, latter):
    return lax.dot_general(
        former, latter, (((1,), (1,)), ((), ())), preferred_element_type=jnp.float32
    )


def to_owners(buffer):
    return lax.all_to_all(buffer, "dp", split_axis=1, concat_axis=1, tiled=True)


def owner_reduce(partial_rows):
    shares = lax.psum_scatter(
        partial_rows.astype(jnp.bfloat16), "tensor", scatter_dimension=2, tiled=True
    )
    return lax.all_gather(shares, "tensor", axis=2, tiled=True)


def body(
    layer_input,
    query_weight,
    key_projection,
    value_projection,
    context_weight,
    router_weight,
    expert_gate,
    expert_up,
    expert_down,
    prenorm_gain,
    midnorm_gain,
    querynorm_gain,
    keynorm_gain,
    routes,
    lengths,
    sequence_order,
    output_cotangent,
):
    tensor_count = lax.axis_size("tensor")
    tensor_index = lax.axis_index("tensor")
    dp_count = lax.axis_size("dp")
    own_rows = layer_input.shape[0]
    block_rows = own_rows * tensor_count
    features = layer_input.shape[1]
    expert_count = EXP_DEV * dp_count
    capacity = 3 * block_rows * TOP // (4 * EXP_DEV)
    most_rows = (5 * block_rows * TOP + 4 * expert_count - 1) // (4 * expert_count)
    slot_total = EXP_DEV * dp_count * most_rows
    (
        query_all,
        key_all,
        value_all,
        context_all,
        router_all,
        gain_first,
        gain_second,
        query_gain,
        gain_key,
    ) = (
        lax.all_gather(query_weight, "dp", axis=0, tiled=True),
        lax.all_gather(key_projection, "dp", axis=0, tiled=True),
        lax.all_gather(value_projection, "dp", axis=0, tiled=True),
        lax.all_gather(context_weight, "dp", axis=1, tiled=True),
        lax.all_gather(router_weight, "dp", axis=0, tiled=True),
        lax.all_gather(prenorm_gain, "dp", axis=0, tiled=True),
        lax.all_gather(midnorm_gain, "dp", axis=0, tiled=True),
        lax.all_gather(querynorm_gain, "dp", axis=0, tiled=True),
        lax.all_gather(keynorm_gain, "dp", axis=0, tiled=True),
    )
    input_rows, cot_rows = (
        lax.all_gather(layer_input, "tensor", axis=0, tiled=True),
        lax.all_gather(output_cotangent, "tensor", axis=0, tiled=True),
    )
    position = jnp.arange(block_rows, dtype=jnp.int32)
    seq_length = lengths[sequence_order[lax.axis_index("dp")]]
    token_live = position < seq_length
    frequency = jnp.exp(
        -math.log(rope_base) * jnp.arange(HEAD_SIZE // 2, dtype=jnp.float32) * (2.0 / HEAD_SIZE)
    )
    angles = position.astype(jnp.float32)[:, None] * frequency[None, :]
    cosine_table = jnp.cos(angles)[:, None, :]
    sine_values = jnp.sin(angles)[:, None, :]
    heads_query = query_all.shape[1] // HEAD_SIZE
    heads_key = key_all.shape[1] // HEAD_SIZE
    group_width = heads_query // heads_key
    gain_one = gain_first.astype(jnp.float32)
    gain_two = gain_second.astype(jnp.float32)
    query_factor = query_gain.astype(jnp.float32)
    key_factor = gain_key.astype(jnp.float32)
    stream = input_rows.astype(jnp.float32)
    unit_first, scale_first = rms_normalize(stream)
    first_layer_normed = (unit_first * gain_one).astype(jnp.bfloat16)
    query_unnormed = matrix_product(first_layer_normed, query_all).reshape(
        block_rows, heads_query, HEAD_SIZE
    )
    key_unnormed = matrix_product(first_layer_normed, key_all).reshape(
        block_rows, heads_key, HEAD_SIZE
    )
    value_rows = (
        matrix_product(first_layer_normed, value_all)
        .astype(jnp.bfloat16)
        .reshape(block_rows, heads_key, HEAD_SIZE)
    )
    query_unit, query_scale = rms_normalize(query_unnormed)
    key_unit, key_scale = rms_normalize(key_unnormed)
    query_rows = (
        rotary_apply(query_unit * query_factor, cosine_table, sine_values)
        .astype(jnp.bfloat16)
        .reshape(block_rows, heads_key, group_width, HEAD_SIZE)
    )
    keys_rot = rotary_apply(key_unit * key_factor, cosine_table, sine_values).astype(jnp.bfloat16)
    score_scale = HEAD_SIZE ** (-0.5)
    allowed = (position[None, :] <= position[:, None]) & token_live[None, :]

    def score_block():
        raw_scores = (
            jnp.einsum("ikrd,jkd->krij", query_rows, keys_rot, preferred_element_type=jnp.float32)
            * score_scale
        )
        return jnp.where(allowed, raw_scores, masked_score)

    scores = score_block()
    row_peak = jnp.max(scores, axis=-1, keepdims=True)
    log_total = row_peak + jnp.log(jnp.sum(jnp.exp(scores - row_peak), axis=-1, keepdims=True))
    soft_probs = jnp.exp(scores - log_total)
    context = jnp.einsum(
        "krij,jkd->ikrd",
        soft_probs.astype(jnp.bfloat16),
        value_rows,
        preferred_element_type=jnp.float32,
    )
    context = context.reshape(block_rows, heads_query * HEAD_SIZE).astype(jnp.bfloat16)
    attention = lax.psum(matrix_product(context, context_all), "tensor")
    residual = stream + attention
    unit_second, scale_second = rms_normalize(residual)
    normed_second = (unit_second * gain_two).astype(jnp.bfloat16)
    logits = matrix_product(normed_second, router_all)
    expert_ids = jnp.arange(expert_count, dtype=jnp.int32)
    route_hot = routes[:, :, None] == expert_ids[None, None, :]
    chosen = jnp.sum(jnp.where(route_hot, logits[:, None, :], 0.0), axis=-1)
    gate_weights = jax.nn.softmax(chosen, axis=-1)
    pair_expert = routes.reshape(-1)
    pair_live = jnp.repeat(token_live, TOP)
    pair_hot = ((pair_expert[:, None] == expert_ids[None, :]) & pair_live[:, None]).astype(
        jnp.int32
    )
    running = jnp.cumsum(pair_hot, axis=0)
    pair_rank = jnp.sum((running - pair_hot) * pair_hot, axis=1)
    counts = running[-1]
    earlier = carried_in(
        counts, "dp", lambda former, latter: former + latter, jnp.zeros_like(counts)
    )
    pair_slot = jnp.sum(earlier[None, :] * pair_hot, axis=1) + pair_rank
    pair_kept = pair_live & (pair_slot < capacity)
    local_expert = pair_expert % EXP_DEV
    owner_index = pair_expert // EXP_DEV
    buffer_index = (local_expert * dp_count + owner_index) * most_rows + pair_rank
    target = jnp.where(pair_kept, buffer_index, slot_total)
    pair_ids = jnp.arange(block_rows * TOP, dtype=jnp.int32)
    slot_pair = jnp.full((slot_total,), -1, dtype=jnp.int32).at[target].set(pair_ids, mode="drop")
    slot_used = slot_pair >= 0
    slot_safe = jnp.maximum(slot_pair, 0)
    slot_token = slot_safe // TOP
    bf_zero = jnp.zeros((), jnp.bfloat16)
    send_rows = jnp.where(slot_used[:, None], normed_second[slot_token], bf_zero)
    layout = (EXP_DEV, dp_count, most_rows, features)
    received = to_owners(send_rows.reshape(layout)).reshape(EXP_DEV, dp_count * most_rows, features)
    gate_pre = jnp.einsum("end,edf->enf", received, expert_gate, preferred_element_type=jnp.float32)
    up_pre = jnp.einsum("end,edf->enf", received, expert_up, preferred_element_type=jnp.float32)
    sigmoid_gate = jax.nn.sigmoid(gate_pre)
    gate_act = gate_pre * sigmoid_gate
    hidden = (gate_act * up_pre).astype(jnp.bfloat16)
    out_partial = jnp.einsum(
        "enf,efd->end", hidden, expert_down, preferred_element_type=jnp.float32
    )
    expert_out = owner_reduce(out_partial)
    width = expert_out.shape[2]
    returned = lax.all_to_all(
        expert_out.reshape(EXP_DEV, dp_count, most_rows, width),
        "dp",
        split_axis=1,
        concat_axis=1,
        tiled=True,
    ).reshape(slot_total, width)
    pair_place = jnp.where(pair_kept, buffer_index, 0)
    pair_out = jnp.where(pair_kept[:, None], returned[pair_place], bf_zero).reshape(
        block_rows, TOP, width
    )
    expert_part = jnp.sum(gate_weights[:, :, None] * pair_out, axis=1)
    cot_full = cot_rows.astype(jnp.float32)
    own_start = tensor_index * own_rows
    gate_part = jnp.sum(cot_full[:, None, :] * pair_out, axis=-1)
    expert_own = lax.dynamic_slice_in_dim(expert_part, own_start, own_rows, 0)
    residual_own = lax.dynamic_slice_in_dim(residual, own_start, own_rows, 0)
    layer_output = (residual_own + expert_own).astype(jnp.bfloat16)
    slot_gate = jnp.where(slot_used, gate_weights.reshape(-1)[slot_safe], 0.0)
    send_cot = (slot_gate[:, None] * cot_full[slot_token]).astype(jnp.bfloat16)
    expert_cot = to_owners(send_cot.reshape(layout)).reshape(
        EXP_DEV, dp_count * most_rows, features
    )
    hidden_cot = jnp.einsum(
        "end,efd->enf", expert_cot, expert_down, preferred_element_type=jnp.float32
    )
    gating_cot = (
        hidden_cot * up_pre * sigmoid_gate * (1.0 + gate_pre * (1.0 - sigmoid_gate))
    ).astype(jnp.bfloat16)
    upward_cot = (hidden_cot * gate_act).astype(jnp.bfloat16)
    down_gradient = jnp.einsum(
        "enf,end->efd", hidden, expert_cot, preferred_element_type=jnp.float32
    )
    gate_gradient = jnp.einsum(
        "end,enf->edf", received, gating_cot, preferred_element_type=jnp.float32
    )
    up_gradient = jnp.einsum(
        "end,enf->edf", received, upward_cot, preferred_element_type=jnp.float32
    )
    row_partial = jnp.einsum(
        "enf,edf->end", gating_cot, expert_gate, preferred_element_type=jnp.float32
    )
    row_partial = row_partial + jnp.einsum(
        "enf,edf->end", upward_cot, expert_up, preferred_element_type=jnp.float32
    )
    row_cot = owner_reduce(row_partial)
    row_back = lax.all_to_all(
        row_cot.reshape(EXP_DEV, dp_count, most_rows, width),
        "dp",
        split_axis=1,
        concat_axis=1,
        tiled=True,
    ).reshape(slot_total, width)
    pair_cot = jnp.where(pair_kept[:, None], row_back[pair_place], bf_zero).reshape(
        block_rows, TOP, width
    )
    normed_part = jnp.sum(pair_cot.astype(jnp.float32), axis=1)
    normed_cot = normed_part
    route_cot = gate_weights * (
        gate_part - jnp.sum(gate_weights * gate_part, axis=-1, keepdims=True)
    )
    logit_cot = jnp.sum(jnp.where(route_hot, route_cot[:, :, None], 0.0), axis=1).astype(
        jnp.bfloat16
    )
    router_gradient = contract(normed_second, logit_cot)
    normed_cot = normed_cot + transposed(logit_cot, router_all)
    midnorm_gradient = jnp.sum(normed_cot * unit_second, axis=0)
    residual_cot = cot_full + norm_back(normed_cot * gain_two, unit_second, scale_second)
    attention_cot = residual_cot.astype(jnp.bfloat16)
    context_gradient = contract(context, attention_cot)
    context_cot = (
        transposed(attention_cot, context_all)
        .astype(jnp.bfloat16)
        .reshape(block_rows, heads_key, group_width, HEAD_SIZE)
    )
    scores = score_block()
    soft_probs = jnp.exp(scores - log_total)
    prob_cot = jnp.einsum(
        "ikrd,jkd->krij", context_cot, value_rows, preferred_element_type=jnp.float32
    )
    score_cot = (
        soft_probs * (prob_cot - jnp.sum(soft_probs * prob_cot, axis=-1, keepdims=True))
    ).astype(jnp.bfloat16)
    value_cot = jnp.einsum(
        "krij,ikrd->jkd",
        soft_probs.astype(jnp.bfloat16),
        context_cot,
        preferred_element_type=jnp.float32,
    )
    value_cot = value_cot.astype(jnp.bfloat16).reshape(block_rows, heads_key * HEAD_SIZE)
    query_turned = (
        jnp.einsum(
            "krij,jkd->ikrd", score_cot, keys_rot, preferred_element_type=jnp.float32
        ).reshape(block_rows, heads_query, HEAD_SIZE)
        * score_scale
    )
    key_turned = (
        jnp.einsum("krij,ikrd->jkd", score_cot, query_rows, preferred_element_type=jnp.float32)
        * score_scale
    )
    query_back = rotary_apply(query_turned, cosine_table, -sine_values)
    key_back = rotary_apply(key_turned, cosine_table, -sine_values)
    querynorm_part = jnp.sum(query_back * query_unit, axis=(0, 1))
    keynorm_part = jnp.sum(key_back * key_unit, axis=(0, 1))
    query_raw_cot = (
        norm_back(query_back * query_factor, query_unit, query_scale)
        .astype(jnp.bfloat16)
        .reshape(block_rows, heads_query * HEAD_SIZE)
    )
    key_raw_cot = (
        norm_back(key_back * key_factor, key_unit, key_scale)
        .astype(jnp.bfloat16)
        .reshape(block_rows, heads_key * HEAD_SIZE)
    )
    query_gradient = contract(first_layer_normed, query_raw_cot)
    key_gradient = contract(first_layer_normed, key_raw_cot)
    value_gradient = contract(first_layer_normed, value_cot)
    first_part = (
        transposed(query_raw_cot, query_all)
        + transposed(key_raw_cot, key_all)
        + transposed(value_cot, value_all)
    )
    first_cot, querynorm_gradient, keynorm_gradient = (
        lax.psum(first_part.astype(jnp.bfloat16), "tensor").astype(jnp.float32),
        lax.psum(querynorm_part.astype(jnp.bfloat16), "tensor").astype(jnp.float32),
        lax.psum(keynorm_part.astype(jnp.bfloat16), "tensor").astype(jnp.float32),
    )
    prenorm_gradient = jnp.sum(first_cot * unit_first, axis=0)
    input_cot = residual_cot + norm_back(first_cot * gain_one, unit_first, scale_first)
    input_gradient = lax.dynamic_slice_in_dim(input_cot, own_start, own_rows, 0).astype(
        jnp.bfloat16
    )
    summed = (
        lax.psum_scatter(query_gradient, "dp", scatter_dimension=0, tiled=True),
        lax.psum_scatter(key_gradient, "dp", scatter_dimension=0, tiled=True),
        lax.psum_scatter(value_gradient, "dp", scatter_dimension=0, tiled=True),
        lax.psum_scatter(context_gradient, "dp", scatter_dimension=1, tiled=True),
        lax.psum_scatter(router_gradient, "dp", scatter_dimension=0, tiled=True),
        lax.psum_scatter(prenorm_gradient, "dp", scatter_dimension=0, tiled=True),
        lax.psum_scatter(midnorm_gradient, "dp", scatter_dimension=0, tiled=True),
        lax.psum_scatter(querynorm_gradient, "dp", scatter_dimension=0, tiled=True),
        lax.psum_scatter(keynorm_gradient, "dp", scatter_dimension=0, tiled=True),
    )
    return (
        layer_output,
        input_gradient,
        summed[0],
        summed[1],
        summed[2],
        summed[3],
        summed[4],
        gate_gradient,
        up_gradient,
        down_gradient,
        summed[5],
        summed[6],
        summed[7],
        summed[8],
    )


AUX = 128


GRID_Z = 4
VMEM_LIMIT = 56 * 1024 * 1024


def remote(src, dst, send_sem, recv_sem, device):
    return pltpu.make_async_remote_copy(
        src_ref=src,
        dst_ref=dst,
        send_sem=send_sem,
        recv_sem=recv_sem,
        device_id=device,
        device_id_type=pl.DeviceIdType.MESH,
    )


class Place:
    def __init__(self):
        self.dp = lax.axis_index("dp")
        self.y = lax.axis_index("tensor")
        self.z = self.dp // 4
        self.x = (self.dp // 2) % 2
        self.core = self.dp % 2
        self.sibling = (self.dp + 1 - 2 * self.core, self.y)
        self.x_mate = (self.dp + 2 - 4 * self.x, self.y)
        self.y_mate = (self.dp, 1 - self.y)
        self.above = (self.dp + 4, self.y)
        self.below = (self.dp - 4, self.y)
        self.has_above = self.z < GRID_Z - 1
        self.has_below = self.z > 0

    def farthest(self, k):
        return (3 - 3 * (self.z // 2), (2 + 3 * self.z) % 5, 1 + self.z % 2, self.z)[k]

    def dp_at(self, z, flip_x, flip_core):
        x = self.x + flip_x * (1 - 2 * self.x)
        core = self.core + flip_core * (1 - 2 * self.core)
        return z * 4 + x * 2 + core

    def y_at(self, flip_y):
        return self.y + flip_y * (1 - 2 * self.y)

    def greet(self):
        barrier = pltpu.get_barrier_semaphore()
        for mate in (self.sibling, self.x_mate, self.y_mate):
            pl.semaphore_signal(barrier, 1, device_id=mate, device_id_type=pl.DeviceIdType.MESH)

        @pl.when(self.has_above)
        def _():
            pl.semaphore_signal(
                barrier, 1, device_id=self.above, device_id_type=pl.DeviceIdType.MESH
            )

        @pl.when(self.has_below)
        def _():
            pl.semaphore_signal(
                barrier, 1, device_id=self.below, device_id_type=pl.DeviceIdType.MESH
            )

        pl.semaphore_wait(barrier, 4 + self.z * (GRID_Z - 1 - self.z) // 2)


def add_rows(target, sources, rows, step=16):
    start, count = rows

    def one(i, carry):
        at = pl.ds(pl.multiple_of(start + i * step, step), step)
        total = target[at, :].astype(jnp.float32)
        for source, shift in sources:
            there = pl.ds(pl.multiple_of(start - shift + i * step, step), step)
            total = total + source[there, :].astype(jnp.float32)
        target[at, :] = total.astype(target.dtype)
        return carry

    lax.fori_loop(0, count // step, one, 0)


def scatter_kernel(
    part, out, own, core, diag_a, diag_b, from_x, from_y, from_z, result,
    load_s, core_s, diag_s, x_s, y_s, z_s, out_s,
):
    me = Place()
    rows = own.shape[3]
    half = rows // 2
    low, high = (0, half), (half, half)
    loads, sends = {}, []

    def chunk(k, flip_x, flip_y, flip_core):
        return part.at[me.dp_at(me.farthest(k), flip_x, flip_core) * 2 + me.y_at(flip_y)]

    order = ((1, 1), (1, 0), (0, 1), (0, 0))
    for k in range(GRID_Z):
        for fx, fy in order:
            copy = pltpu.make_async_copy(
                chunk(k, fx, fy, 0), own.at[k, fx, fy], load_s.at[k, fx, fy]
            )
            copy.start()
            loads[k, fx, fy] = copy
    me.greet()
    cores = {}
    for k in range(GRID_Z):
        for fx, fy in order:
            copy = remote(
                chunk(k, fx, fy, 1), core.at[k, fx, fy],
                core_s.at[0, k, fx, fy], core_s.at[1, k, fx, fy], me.sibling,
            )
            copy.start()
            cores[k, fx, fy] = copy
            sends.append(copy)

    da = [remote(own.at[k, 1, 1, pl.ds(0, half)], diag_a.at[k], diag_s.at[0, k], diag_s.at[1, k], me.y_mate) for k in range(4)]
    db = [remote(own.at[k, 1, 1, pl.ds(half, half)], diag_b.at[k], diag_s.at[2, k], diag_s.at[3, k], me.x_mate) for k in range(4)]
    xs = [[remote(own.at[k, 1, 0, pl.ds(h * half, half)], from_x.at[k, pl.ds(h * half, half)], x_s.at[0, k, h], x_s.at[1, k, h], me.x_mate) for h in range(2)] for k in range(4)]
    ys = [[remote(own.at[k, 0, 1, pl.ds(h * half, half)], from_y.at[k, pl.ds(h * half, half)], y_s.at[0, k, h], y_s.at[1, k, h], me.y_mate) for h in range(2)] for k in range(4)]

    def arrive(k, fx, fy):
        loads[k, fx, fy].wait()
        cores[k, fx, fy].wait_recv()

    def early(k):
        arrive(k, 1, 1)
        add_rows(own.at[k, 1, 1], [(core.at[k, 1, 1], 0)], low)
        da[k].start()
        add_rows(own.at[k, 1, 1], [(core.at[k, 1, 1], 0)], high)
        db[k].start()
        arrive(k, 1, 0)
        add_rows(own.at[k, 1, 0], [(core.at[k, 1, 0], 0)], high)
        xs[k][1].start()
        arrive(k, 0, 1)
        add_rows(own.at[k, 0, 1], [(core.at[k, 0, 1], 0)], low)
        ys[k][0].start()

    def late(k):
        da[k].wait_recv()
        add_rows(own.at[k, 1, 0], [(core.at[k, 1, 0], 0), (diag_a.at[k], 0)], low)
        xs[k][0].start()
        db[k].wait_recv()
        add_rows(own.at[k, 0, 1], [(core.at[k, 0, 1], 0), (diag_b.at[k], half)], high)
        ys[k][1].start()

    whole = (0, rows)

    def column(k):
        arrive(k, 0, 0)
        for h in range(2):
            xs[k][h].wait_recv()
            ys[k][h].wait_recv()
        mine = own.at[k, 0, 0]
        rest = [(core.at[k, 0, 0], 0), (from_x.at[k], 0), (from_y.at[k], 0)]
        if k < GRID_Z - 1:
            to = me.farthest(k)
            add_rows(mine, rest, whole)
            for side, ahead, mate, more in (
                (0, to > me.z, me.above, me.has_below),
                (1, to < me.z, me.below, me.has_above),
            ):
                copy = remote(
                    mine, from_z.at[side, to], z_s.at[0, side, to], z_s.at[1, side, to], mate
                )

                @pl.when(ahead)
                def _():
                    @pl.when(more)
                    def _():
                        copy.wait_recv()
                        add_rows(mine, [(from_z.at[side, to], 0)], whole)

                    copy.start()
        else:
            add_rows(mine, rest, whole)
            for side, more in ((0, me.has_below), (1, me.has_above)):
                copy = remote(
                    mine, from_z.at[side, me.z], z_s.at[0, side, me.z], z_s.at[1, side, me.z],
                    me.y_mate,
                )

                @pl.when(more)
                def _():
                    copy.wait_recv()
                    add_rows(mine, [(from_z.at[side, me.z], 0)], whole)

    early(0)
    early(1)
    late(0)
    early(2)
    late(1)
    column(0)
    early(3)
    late(2)
    column(1)
    late(3)
    column(2)
    column(3)
    copy = pltpu.make_async_copy(own.at[3, 0, 0], out, out_s)
    copy.start()
    for k in range(GRID_Z):
        da[k].wait_send()
        db[k].wait_send()
        for h in range(2):
            xs[k][h].wait_send()
            ys[k][h].wait_send()
        if k < GRID_Z - 1:
            to = me.farthest(k)
            for side, ahead, mate in ((0, to > me.z, me.above), (1, to < me.z, me.below)):
                @pl.when(ahead)
                def _():
                    remote(
                        own.at[k, 0, 0], from_z.at[side, to],
                        z_s.at[0, side, to], z_s.at[1, side, to], mate,
                    ).wait_send()
    for sent in sends:
        sent.wait_send()
    copy.wait()


def scatter_all(value, collective_id):
    devices = lax.axis_size("dp") * lax.axis_size("tensor")
    rows, width = value.shape[0] // devices, value.shape[1]
    half = rows // 2
    dma = pltpu.SemaphoreType.DMA
    low = value.dtype
    return pl.pallas_call(
        scatter_kernel,
        out_shape=jax.ShapeDtypeStruct((rows, width), low),
        in_specs=[pl.BlockSpec(memory_space=pl.ANY)],
        out_specs=pl.BlockSpec(memory_space=pl.ANY),
        scratch_shapes=[
            pltpu.VMEM((4, 2, 2, rows, width), low),
            pltpu.VMEM((4, 2, 2, rows, width), low),
            pltpu.VMEM((4, half, width), low),
            pltpu.VMEM((4, half, width), low),
            pltpu.VMEM((4, rows, width), low),
            pltpu.VMEM((4, rows, width), low),
            pltpu.VMEM((2, 4, rows, width), low),
            pltpu.VMEM((8, 128), low),
            dma((4, 2, 2)),
            dma((2, 4, 2, 2)),
            dma((4, 4)),
            dma((2, 4, 2)),
            dma((2, 4, 2)),
            dma((2, 2, 4)),
            dma(()),
        ],
        compiler_params=pltpu.CompilerParams(
            collective_id=collective_id, has_side_effects=True, vmem_limit_bytes=VMEM_LIMIT
        ),
    )(value.reshape(devices, rows, width))


def gather_kernel(src, out, own_s, z_s, x_s, y_s, dx_s, dy_s, core_s):
    me = Place()
    rows = src.shape[0]
    half = rows // 2
    low, high = pl.ds(0, half), pl.ds(half, half)

    def near(k):
        return me.farthest(GRID_Z - 1 - k)

    def at(k, fx, fy, fc):
        return out.at[me.dp_at(near(k), fx, fc) * 2 + me.y_at(fy)]

    mine = pltpu.make_async_copy(src, at(0, 0, 0, 0), own_s)
    mine.start()
    me.greet()

    def over(source, k, fx, fy, send, recv, mate):
        return remote(source, at(k, fx, fy, 0), send, recv, mate)

    def z_copy(k, source, side, mate):
        zn = near(k)
        return remote(source, at(k, 0, 0, 0), z_s.at[0, side, zn], z_s.at[1, side, zn], mate)

    xs, ys, dxs, dys, cores = {}, {}, {}, {}, {}
    for k in range(GRID_Z):
        source = src if k == 0 else at(k, 0, 0, 0)
        xs[k] = over(source, k, 0, 0, x_s.at[0, k], x_s.at[1, k], me.x_mate)
        ys[k] = over(source, k, 0, 0, y_s.at[0, k], y_s.at[1, k], me.y_mate)
        dys[k] = remote(at(k, 1, 0, 0).at[low], at(k, 1, 0, 0).at[low], dy_s.at[0, k], dy_s.at[1, k], me.y_mate)
        dxs[k] = remote(at(k, 0, 1, 0).at[high], at(k, 0, 1, 0).at[high], dx_s.at[0, k], dx_s.at[1, k], me.x_mate)
        for fx in range(2):
            for fy in range(2):
                block = source if (fx, fy) == (0, 0) else at(k, fx, fy, 0)
                if (fx, fy) == (1, 1):
                    for h, part in enumerate((low, high)):
                        cores[k, fx, fy, h] = remote(
                            block.at[part], block.at[part],
                            core_s.at[0, k, 3 + h], core_s.at[1, k, 3 + h], me.sibling,
                        )
                else:
                    cores[k, fx, fy] = remote(
                        block, at(k, fx, fy, 0), core_s.at[0, k, fx * 2 + fy],
                        core_s.at[1, k, fx * 2 + fy], me.sibling,
                    )

    def own(k):
        if k == 0:
            for side, more, mate in ((0, me.has_above, me.above), (1, me.has_below, me.below)):
                copy = z_copy(0, src, side, mate)

                @pl.when(more)
                def _():
                    copy.start()
        else:
            zn = near(k)
            for side, came, more, mate in (
                (0, zn < me.z, me.has_above, me.above),
                (1, zn > me.z, me.has_below, me.below),
            ):
                copy = z_copy(k, at(k, 0, 0, 0), side, mate)

                @pl.when(came)
                def _():
                    copy.wait_recv()

                    @pl.when(more)
                    def _():
                        copy.start()

        xs[k].start()
        ys[k].start()
        cores[k, 0, 0].start()

    def diag(k):
        xs[k].wait_recv()
        dys[k].start()
        cores[k, 1, 0].start()
        ys[k].wait_recv()
        dxs[k].start()
        cores[k, 0, 1].start()

    def corner(k):
        dys[k].wait_recv()
        cores[k, 1, 1, 0].start()
        dxs[k].wait_recv()
        cores[k, 1, 1, 1].start()

    own(0)
    own(1)
    diag(0)
    own(2)
    diag(1)
    corner(0)
    own(3)
    diag(2)
    corner(1)
    diag(3)
    corner(2)
    corner(3)
    mine.wait()
    for k in range(GRID_Z):
        zn = near(k)
        for side, came, more, mate in (
            (0, zn <= me.z, me.has_above, me.above),
            (1, zn >= me.z, me.has_below, me.below),
        ):
            copy = z_copy(k, src if k == 0 else at(k, 0, 0, 0), side, mate)

            @pl.when(came)
            def _():
                @pl.when(more)
                def _():
                    copy.wait_send()
        for copy in (xs[k], ys[k], dxs[k], dys[k]):
            copy.wait_send()
    for copy in cores.values():
        copy.wait()


def gather_all(value, collective_id):
    devices = lax.axis_size("dp") * lax.axis_size("tensor")
    rows, width = value.shape
    dma = pltpu.SemaphoreType.DMA
    return pl.pallas_call(
        gather_kernel,
        out_shape=jax.ShapeDtypeStruct((devices, rows, width), value.dtype),
        in_specs=[pl.BlockSpec(memory_space=pl.ANY)],
        out_specs=pl.BlockSpec(memory_space=pl.ANY),
        scratch_shapes=[
            dma(()),
            dma((2, 2, 4)),
            dma((2, 4)),
            dma((2, 4)),
            dma((2, 4)),
            dma((2, 4)),
            dma((2, 4, 5)),
        ],
        compiler_params=pltpu.CompilerParams(collective_id=collective_id, has_side_effects=True),
    )(value).reshape(devices * rows, width)


WINDOW_ALIGN = 16
EXPERT_VMEM = 60 * 1024 * 1024


def dot(left, right, dims=((1,), (0,))):
    return lax.dot_general(left, right, (dims, ((), ())), preferred_element_type=jnp.float32)


def expert_kernel(
    info, pos, rows_in, cots_in, gate_w, up_w, down_w,
    out, back, gate_g, up_g, down_g,
    x, dy, wgu, wd, slot_out, slot_row, gu, hg, rows_b, cots_b, g_stage, d_stage,
    load_s, w_s, out_s, g_s, d_s,
):
    bf16, f32 = jnp.bfloat16, jnp.float32
    blocks, block_rows, wide = rows_in.shape
    features = cots_in.shape[2]
    experts, padded = x.shape[0], x.shape[1]
    part = hg.shape[2]
    cap = hg.shape[1]
    window = padded - cap
    tile = 256
    chunk = 512

    def load(b):
        slot = b % 2
        return (
            pltpu.make_async_copy(rows_in.at[b], rows_b.at[slot], load_s.at[slot, 0]),
            pltpu.make_async_copy(cots_in.at[b], cots_b.at[slot], load_s.at[slot, 1]),
        )

    for copy in load(0):
        copy.start()
    weights = []
    for e in range(experts):
        weights.append(pltpu.make_async_copy(gate_w.at[e], wgu.at[e, :, pl.ds(0, part)], w_s.at[e, 0]))
        weights.append(pltpu.make_async_copy(up_w.at[e], wgu.at[e, :, pl.ds(part, part)], w_s.at[e, 1]))
        weights.append(pltpu.make_async_copy(down_w.at[e], wd.at[e], w_s.at[e, 2]))
    for copy in weights:
        copy.start()

    def clear(i, carry):
        at = pl.ds(pl.multiple_of(i * 16, 16), 16)
        for e in range(experts):
            x[e, at, :] = jnp.zeros((16, wide), bf16)
            dy[e, at, :] = jnp.zeros((16, features), bf16)
        return carry

    lax.fori_loop(0, padded // 16, clear, 0)
    for e in range(experts):
        slot_out[e, pl.ds(cap, window), :] = jnp.zeros((window, features), bf16)
        slot_row[e, pl.ds(cap, window), :] = jnp.zeros((window, wide), bf16)

    def starts(b):
        return [pl.multiple_of(info[1 + b * experts + e], WINDOW_ALIGN) for e in range(experts)]

    def picks(b, begin):
        slots = lax.broadcasted_iota(jnp.int32, (window, block_rows), 0)
        return jnp.concatenate(
            [(slots + begin[e] == pos[b, pl.ds(e, 1), :]).astype(f32) for e in range(experts)],
            axis=0,
        )

    def take(b, carry):
        slot = b % 2

        @pl.when(b + 1 < blocks)
        def _():
            for copy in load(b + 1):
                copy.start()

        begin = starts(b)
        picked = picks(b, begin).astype(bf16)
        for copy in load(b):
            copy.wait()
        for source, target, width in ((rows_b, x, wide), (cots_b, dy, features)):
            for first in range(0, width, chunk):
                cols = pl.ds(first, min(chunk, width - first))
                got = dot(picked, source[slot, :, cols]).astype(bf16)
                for e in range(experts):
                    at = pl.ds(begin[e], window)
                    target[e, at, cols] += got[e * window : (e + 1) * window]
        return carry

    lax.fori_loop(0, blocks, take, 0)
    for copy in weights:
        copy.wait()

    lanes = lax.broadcasted_iota(jnp.int32, (tile, AUX), 1)

    def mlp(step, carry):
        e = step // (cap // tile)
        at = pl.ds(pl.multiple_of((step % (cap // tile)) * tile, tile), tile)
        own = info[0] * experts + e
        total = blocks * experts
        aux = x[e, at, pl.ds(features, AUX)].astype(f32)
        gate = jnp.sum(
            jnp.where((lanes == own) | (lanes == own + total), aux, 0.0), axis=1, keepdims=True
        )
        pre = dot(x[e, at, pl.ds(0, features)], wgu[e])
        gate_pre, up_pre = pre[:, :part], pre[:, part:]
        sig = 1.0 / (1.0 + jnp.exp(-gate_pre))
        act = gate_pre * sig
        hidden = (act * up_pre).astype(bf16).astype(f32)
        gated = (hidden * gate).astype(bf16)
        hg[e, at, :] = gated
        down_cot = dot(dy[e, at, :], wd[e], ((1,), (1,)))
        slot_cot = jnp.sum(hidden * down_cot, axis=1, keepdims=True)
        hidden_cot = down_cot * gate
        gu[e, at, pl.ds(0, part)] = (
            hidden_cot * up_pre * sig * (1.0 + gate_pre * (1.0 - sig))
        ).astype(bf16)
        gu[e, at, pl.ds(part, part)] = (hidden_cot * act).astype(bf16)
        for first in range(0, features, chunk):
            cols = pl.ds(first, chunk)
            slot_out[e, at, cols] = dot(gated, wd[e, :, cols]).astype(bf16)
            slot_row[e, at, cols] = dot(
                gu[e, at, :], wgu[e, pl.ds(first, chunk), :], ((1,), (1,))
            ).astype(bf16)
        high = slot_cot.astype(bf16).astype(f32)
        place = info[1 + blocks * experts] * 2 * total + own * 2
        slot_row[e, at, pl.ds(features, AUX)] = jnp.where(
            lanes == place, high, jnp.where(lanes == place + 1, slot_cot - high, 0.0)
        ).astype(bf16)
        return carry

    lax.fori_loop(0, experts * (cap // tile), mlp, 0)

    def stored(b):
        slot = b % 2
        return (
            pltpu.make_async_copy(cots_b.at[slot], out.at[b], out_s.at[slot, 0]),
            pltpu.make_async_copy(rows_b.at[slot], back.at[b], out_s.at[slot, 1]),
        )

    def put(b, carry):
        slot = b % 2

        @pl.when(b >= 2)
        def _():
            for copy in stored(b - 2):
                copy.wait()

        begin = starts(b)
        spread = picks(b, begin).T.astype(bf16)
        for source, target, width in ((slot_out, cots_b, features), (slot_row, rows_b, wide)):
            for first in range(0, width, chunk):
                cols = pl.ds(first, min(chunk, width - first))
                held = jnp.concatenate(
                    [source[e, pl.ds(begin[e], window), cols] for e in range(experts)], axis=0
                )
                target[slot, :, cols] = dot(spread, held).astype(bf16)
        for copy in stored(b):
            copy.start()
        return carry

    lax.fori_loop(0, blocks, put, 0)

    tiles = features // tile

    def g_copies(step):
        slot = step % 2
        e, at = step // tiles, pl.ds(pl.multiple_of((step % tiles) * tile, tile), tile)
        return (
            pltpu.make_async_copy(g_stage.at[slot, :, pl.ds(0, part)], gate_g.at[e, at], g_s.at[slot, 0]),
            pltpu.make_async_copy(g_stage.at[slot, :, pl.ds(part, part)], up_g.at[e, at], g_s.at[slot, 1]),
        )

    def wide_grad(step, carry):
        slot = step % 2
        e, at = step // tiles, pl.ds(pl.multiple_of((step % tiles) * tile, tile), tile)

        @pl.when(step >= 2)
        def _():
            for copy in g_copies(step - 2):
                copy.wait()

        g_stage[slot] = dot(x[e, pl.ds(0, cap), at], gu[e], ((0,), (0,)))
        for copy in g_copies(step):
            copy.start()
        return carry

    lax.fori_loop(0, experts * tiles, wide_grad, 0)
    parts = features // chunk

    def d_copy(step):
        slot = step % 2
        e, at = step // parts, pl.ds(pl.multiple_of((step % parts) * chunk, chunk), chunk)
        return pltpu.make_async_copy(d_stage.at[slot], down_g.at[e, :, at], d_s.at[slot])

    def down_grad(step, carry):
        slot = step % 2
        e, at = step // parts, pl.ds(pl.multiple_of((step % parts) * chunk, chunk), chunk)

        @pl.when(step >= 2)
        def _():
            d_copy(step - 2).wait()

        d_stage[slot] = dot(hg[e], dy[e, pl.ds(0, cap), at], ((0,), (0,)))
        d_copy(step).start()
        return carry

    lax.fori_loop(0, experts * parts, down_grad, 0)
    for last in (2, 1):
        for copy in stored(blocks - last):
            copy.wait()
        for copy in g_copies(experts * tiles - last):
            copy.wait()
        d_copy(experts * parts - last).wait()


def expert_layer(info, pos, rows_in, cots_in, gate_w, up_w, down_w, capacity, most):
    bf16, f32 = jnp.bfloat16, jnp.float32
    blocks, block_rows, wide = rows_in.shape
    features = cots_in.shape[2]
    experts, part = gate_w.shape[0], gate_w.shape[2]
    padded = capacity + -(-most // WINDOW_ALIGN) * WINDOW_ALIGN + WINDOW_ALIGN
    dma = pltpu.SemaphoreType.DMA
    shape = jax.ShapeDtypeStruct
    anywhere = pl.BlockSpec(memory_space=pl.ANY)
    return pl.pallas_call(
        expert_kernel,
        out_shape=(
            shape((blocks, block_rows, features), bf16),
            shape((blocks, block_rows, wide), bf16),
            shape(gate_w.shape, f32),
            shape(up_w.shape, f32),
            shape(down_w.shape, f32),
        ),
        in_specs=[
            pl.BlockSpec(memory_space=pltpu.SMEM),
            pl.BlockSpec(memory_space=pltpu.VMEM),
        ]
        + [anywhere] * 5,
        out_specs=(anywhere,) * 5,
        scratch_shapes=[
            pltpu.VMEM((experts, padded, wide), bf16),
            pltpu.VMEM((experts, padded, features), bf16),
            pltpu.VMEM((experts, features, 2 * part), bf16),
            pltpu.VMEM((experts, part, features), bf16),
            pltpu.VMEM((experts, padded, features), bf16),
            pltpu.VMEM((experts, padded, wide), bf16),
            pltpu.VMEM((experts, capacity, 2 * part), bf16),
            pltpu.VMEM((experts, capacity, part), bf16),
            pltpu.VMEM((2, block_rows, wide), bf16),
            pltpu.VMEM((2, block_rows, features), bf16),
            pltpu.VMEM((2, 256, 2 * part), f32),
            pltpu.VMEM((2, part, 512), f32),
            dma((2, 2)),
            dma((experts, 3)),
            dma((2, 2)),
            dma((2, 2)),
            dma((2,)),
        ],
        compiler_params=pltpu.CompilerParams(vmem_limit_bytes=EXPERT_VMEM),
    )(info, pos, rows_in, cots_in, gate_w, up_w, down_w)


ATTENTION_VMEM = 60 * 1024 * 1024
SCORE_SCALE = HEAD_SIZE ** (-0.5)
def turn_tables(rows):
    frequency = np.exp(
        -math.log(rope_base) * np.arange(HEAD_SIZE // 2, dtype=np.float32) * (2.0 / HEAD_SIZE)
    ).astype(np.float32)
    angles = np.arange(rows, dtype=np.float32)[:, None] * frequency[None, :]
    cosine, sine = np.cos(angles), np.sin(angles)
    return (
        np.concatenate([cosine, cosine], axis=1).astype(np.float32),
        np.concatenate([-sine, sine], axis=1).astype(np.float32),
    )


def turn(value, cosine, sine):
    return value * cosine + pltpu.roll(value, HEAD_SIZE // 2, 1) * sine


def inverse_norm(value):
    return lax.rsqrt(jnp.mean(value * value, axis=-1, keepdims=True) + epsilon)


def meet_y(me):
    barrier = pltpu.get_barrier_semaphore()
    pl.semaphore_signal(barrier, 1, device_id=me.y_mate, device_id_type=pl.DeviceIdType.MESH)
    pl.semaphore_wait(barrier, 1)


def gain_rows(aux_t, experts, chunks):
    head = [aux_t[experts + 2 + i : experts + 3 + i, :] for i in range(2)]
    width = HEAD_SIZE
    heads = [sum(row[:, c * width : (c + 1) * width] for c in range(chunks)) for row in head]
    return aux_t[experts : experts + 1, :], aux_t[experts + 1 : experts + 2, :], *heads


def probabilities(query, key, allowed):
    scores = jnp.where(allowed, dot(query, key, ((1,), (1,))) * SCORE_SCALE, masked_score)
    spread = jnp.exp(scores - jnp.max(scores, axis=-1, keepdims=True))
    return spread / jnp.sum(spread, axis=-1, keepdims=True)


def allowed_pairs(live):
    rows = live.shape[1]
    later = lax.broadcasted_iota(jnp.int32, (rows, rows), 0)
    sooner = lax.broadcasted_iota(jnp.int32, (rows, rows), 1)
    return (sooner <= later) & (live[0:1, :] > 0.0)


def forward_kernel(
    experts, x_pair, packed, live, chosen, cosine, sine,
    sent_o, residual_o, normed_o, raw_o, query_o, key_o, value_o, context_o,
    x, w, ctx, aux_w, normed, raw, query, key, value, context, att, got, residual, sent,
    in_s, w_s, out_s, y_s,
):
    bf16, f32 = jnp.bfloat16, jnp.float32
    me = Place()
    rows, features = x.shape
    own_rows = rows // 2
    heads, key_heads = query.shape[0], key.shape[0]
    qkv = w.shape[1]
    chunk = 512
    mine = pl.ds(pl.multiple_of(me.y * own_rows, own_rows), own_rows)
    theirs = pl.ds(pl.multiple_of((1 - me.y) * own_rows, own_rows), own_rows)
    loads = [
        pltpu.make_async_copy(x_pair, x, in_s.at[0]),
        pltpu.make_async_copy(
            packed.at[:, pl.ds(qkv + ctx.shape[1], AUX)], aux_w, in_s.at[1]
        ),
        pltpu.make_async_copy(packed.at[:, pl.ds(qkv, ctx.shape[1])], ctx, in_s.at[2]),
    ]
    parts = [
        pltpu.make_async_copy(
            packed.at[:, pl.ds(c * chunk, chunk)], w.at[:, pl.ds(c * chunk, chunk)], w_s.at[c]
        )
        for c in range(qkv // chunk)
    ]
    loads[0].start()
    loads[1].start()
    for copy in parts:
        copy.start()
    loads[2].start()
    meet_y(me)
    loads[1].wait()
    aux_t = aux_w[...].astype(f32).T
    gain_one, gain_two, query_gain, key_gain = gain_rows(aux_t, experts, features // HEAD_SIZE)
    loads[0].wait()

    def first_norm(i, carry):
        at = pl.ds(pl.multiple_of(i * 32, 32), 32)
        stream = x[at, :].astype(f32)
        normed[at, :] = (stream * inverse_norm(stream) * gain_one).astype(bf16)
        return carry

    lax.fori_loop(0, rows // 32, first_norm, 0)
    for c, copy in enumerate(parts):
        copy.wait()
        got_raw = dot(normed[...], w[:, c * chunk : (c + 1) * chunk])
        for h in range(chunk // HEAD_SIZE):
            raw[c * (chunk // HEAD_SIZE) + h] = got_raw[:, h * HEAD_SIZE : (h + 1) * HEAD_SIZE]
    turn_c, turn_s = cosine[...], sine[...]
    for g in range(key_heads):
        unnormed = raw[heads + g]
        key[g] = turn(unnormed * inverse_norm(unnormed) * key_gain, turn_c, turn_s).astype(bf16)
        value[g] = raw[heads + key_heads + g].astype(bf16)
    allowed = allowed_pairs(live[...])

    def head(h, carry):
        g = h // (heads // key_heads)
        unnormed = raw[h]
        turned = turn(unnormed * inverse_norm(unnormed) * query_gain, turn_c, turn_s).astype(bf16)
        query[h] = turned
        probs = probabilities(turned, key[g], allowed).astype(bf16)
        at = pl.ds(pl.multiple_of(h * HEAD_SIZE, HEAD_SIZE), HEAD_SIZE)
        context[:, at] = dot(probs, value[g]).astype(bf16)
        return carry

    lax.fori_loop(0, heads, head, 0)
    outs = [
        pltpu.make_async_copy(source, target, out_s.at[i])
        for i, (source, target) in enumerate(
            ((normed, normed_o), (raw, raw_o), (query, query_o), (key, key_o), (value, value_o),
             (context, context_o))
        )
    ]
    for copy in outs:
        copy.start()
    loads[2].wait()
    copies = []
    for c in range(features // chunk):
        cols = pl.ds(c * chunk, chunk)
        att[theirs, cols] = dot(context[theirs, :], ctx[cols, :], ((1,), (1,))).astype(bf16)
        copy = remote(
            att.at[theirs, cols], got.at[:, cols], y_s.at[0, c], y_s.at[1, c], me.y_mate
        )
        copy.start()
        copies.append(copy)
    for c in range(features // chunk):
        cols = pl.ds(c * chunk, chunk)
        residual[:, cols] = dot(context[mine, :], ctx[cols, :], ((1,), (1,)))
    for copy in copies:
        copy.wait_recv()

    def second_norm(i, carry):
        at = pl.ds(pl.multiple_of(i * 16, 16), 16)
        there = pl.ds(pl.multiple_of(me.y * own_rows + i * 16, 16), 16)
        total = x[there, :].astype(f32) + (residual[at, :] + got[at, :].astype(f32))
        residual[at, :] = total
        sent[at, pl.ds(0, features)] = (total * inverse_norm(total) * gain_two).astype(bf16)
        return carry

    lax.fori_loop(0, own_rows // 16, second_norm, 0)
    logits = dot(sent[:, :features], aux_w[...])
    picked = chosen[...] > 0.0
    logits = jnp.where(picked, logits, masked_score)
    spread = jnp.where(picked, jnp.exp(logits - jnp.max(logits, axis=-1, keepdims=True)), 0.0)
    gates = spread / jnp.sum(spread, axis=-1, keepdims=True)
    high = gates.astype(bf16).astype(f32)
    sent[:, pl.ds(features, AUX)] = (high + pltpu.roll(gates - high, experts, 1)).astype(bf16)
    last = [
        pltpu.make_async_copy(sent, sent_o, out_s.at[6]),
        pltpu.make_async_copy(residual, residual_o, out_s.at[7]),
    ]
    for copy in last:
        copy.start()
    for copy in copies:
        copy.wait_send()
    for copy in outs + last:
        copy.wait()


def attention_forward(x_pair, packed, live, chosen, experts, heads, key_heads, collective_id):
    bf16, f32 = jnp.bfloat16, jnp.float32
    rows, features = x_pair.shape
    qkv = (heads + 2 * key_heads) * HEAD_SIZE
    cosine, sine = turn_tables(rows)
    dma = pltpu.SemaphoreType.DMA
    shapes = (
        ((rows // 2, features + AUX), bf16),
        ((rows // 2, features), f32),
        ((rows, features), bf16),
        ((heads + 2 * key_heads, rows, HEAD_SIZE), f32),
        ((heads, rows, HEAD_SIZE), bf16),
        ((key_heads, rows, HEAD_SIZE), bf16),
        ((key_heads, rows, HEAD_SIZE), bf16),
        ((rows, heads * HEAD_SIZE), bf16),
    )
    anywhere, vmem = pl.BlockSpec(memory_space=pl.ANY), pl.BlockSpec(memory_space=pltpu.VMEM)
    return pl.pallas_call(
        functools.partial(forward_kernel, experts),
        out_shape=tuple(jax.ShapeDtypeStruct(*shape) for shape in shapes),
        in_specs=[anywhere, anywhere, vmem, vmem, vmem, vmem],
        out_specs=(anywhere,) * len(shapes),
        scratch_shapes=[
            pltpu.VMEM((rows, features), bf16),
            pltpu.VMEM((features, qkv), bf16),
            pltpu.VMEM((features, heads * HEAD_SIZE), bf16),
            pltpu.VMEM((features, AUX), bf16),
            pltpu.VMEM((rows, features), bf16),
            pltpu.VMEM((heads + 2 * key_heads, rows, HEAD_SIZE), f32),
            pltpu.VMEM((heads, rows, HEAD_SIZE), bf16),
            pltpu.VMEM((key_heads, rows, HEAD_SIZE), bf16),
            pltpu.VMEM((key_heads, rows, HEAD_SIZE), bf16),
            pltpu.VMEM((rows, heads * HEAD_SIZE), bf16),
            pltpu.VMEM((rows, features), bf16),
            pltpu.VMEM((rows // 2, features), bf16),
            pltpu.VMEM((rows // 2, features), f32),
            pltpu.VMEM((rows // 2, features + AUX), bf16),
            dma((3,)),
            dma((qkv // 512,)),
            dma((8,)),
            dma((2, features // 512)),
        ],
        compiler_params=pltpu.CompilerParams(
            collective_id=collective_id, has_side_effects=True, vmem_limit_bytes=ATTENTION_VMEM
        ),
    )(x_pair, packed, live, chosen, cosine, sine)


def first_gather_kernel(
    w_src, d_src, x_src, w_out, d_out, x_out,
    local_s, pair_s, wz_s, wx_s, wc_s, az_s, ax_s, ay_s, bz_s, bx_s, by_s, dc_s,
):
    me = Place()
    w_half, half = w_src.shape[0] // 2, d_src.shape[0] // 2
    low, high = pl.ds(0, half), pl.ds(half, half)
    waits, sent = [], []

    def near(k):
        return me.farthest(GRID_Z - 1 - k)

    def w_at(k, fx, p):
        return w_out.at[me.dp_at(near(k), fx, 0), pl.ds(p * w_half, w_half)]

    def d_at(k, fx, fy, rows):
        return d_out.at[me.dp_at(near(k), fx, 0) * 2 + me.y_at(fy), rows]

    for i, (source, target) in enumerate(
        (
            (w_src, w_out.at[me.dp]),
            (d_src, d_out.at[me.dp * 2 + me.y]),
            (x_src, x_out.at[me.y]),
        )
    ):
        copy = pltpu.make_async_copy(source, target, local_s.at[i])
        copy.start()
        waits.append(copy)
    me.greet()

    def line(k, source, target, sem, start_only):
        zn = near(k)
        for side, came, more, mate in (
            (0, zn < me.z, me.has_above, me.above),
            (1, zn > me.z, me.has_below, me.below),
        ):
            copy = remote(source, target, sem.at[0, side, zn], sem.at[1, side, zn], mate)
            if start_only:

                @pl.when(more)
                def _():
                    copy.start()
            else:

                @pl.when(came)
                def _():
                    copy.wait_recv()

                    @pl.when(more)
                    def _():
                        copy.start()

    def line_done(k, source, target, sem):
        zn = near(k)
        for side, came, more, mate in (
            (0, zn <= me.z, me.has_above, me.above),
            (1, zn >= me.z, me.has_below, me.below),
        ):
            copy = remote(source, target, sem.at[0, side, zn], sem.at[1, side, zn], mate)

            @pl.when(came)
            def _():
                @pl.when(more)
                def _():
                    copy.wait_send()

    def w_source(k, p):
        return w_src.at[pl.ds(p * w_half, w_half)] if k == 0 else w_at(k, 0, p)

    def d_source(k, rows):
        return d_src.at[rows] if k == 0 else d_at(k, 0, 0, rows)

    def go(source, target, sem, index, mate):
        copy = remote(source, target, sem.at[(0, *index)], sem.at[(1, *index)], mate)
        copy.start()
        sent.append(copy)
        return copy

    def to_core(source, target, sem, index):
        go(source, target, sem, index, me.sibling)

    wx, ax, ay, by = {}, {}, {}, {}

    def w_own(k, p):
        line(k, w_source(k, p), w_at(k, 0, p), wz_s.at[p], k == 0)
        wx[k, p] = go(w_source(k, p), w_at(k, 0, p), wx_s, (k, p), me.x_mate)
        to_core(w_source(k, p), w_at(k, 0, p), wc_s, (k, 0, p))

    def w_across(k):
        for p in range(2):
            wx[k, p].wait_recv()
            to_core(w_at(k, 1, p), w_at(k, 1, p), wc_s, (k, 1, p))

    def a_own(k):
        line(k, d_source(k, low), d_at(k, 0, 0, low), az_s, k == 0)
        ax[k] = go(d_source(k, low), d_at(k, 0, 0, low), ax_s, (k,), me.x_mate)
        ay[k, 0] = go(d_source(k, low), d_at(k, 0, 0, low), ay_s, (k, 0), me.y_mate)
        to_core(d_source(k, low), d_at(k, 0, 0, low), dc_s, (k, 0, 0, 0))

    def a_across(k):
        ax[k].wait_recv()
        block = d_at(k, 1, 0, low)
        ay[k, 1] = go(block, block, ay_s, (k, 1), me.y_mate)
        to_core(block, block, dc_s, (k, 1, 0, 0))

    def b_own(k, fx):
        source = d_source(k, high) if fx == 0 else d_at(k, 1, 0, high)
        block = d_at(k, fx, 0, high)
        line(k, source, block, bz_s.at[fx], k == 0)
        by[k, fx] = go(source, block, by_s, (k, fx), me.y_mate)
        to_core(source, block, dc_s, (k, fx, 0, 1))

    def y_done(k):
        for fx in range(2):
            for h, (copies, rows) in enumerate(((ay, low), (by, high))):
                copies[k, fx].wait_recv()
                block = d_at(k, fx, 1, rows)
                to_core(block, block, dc_s, (k, fx, 1, h))

    pair = go(x_src, x_out.at[me.y], pair_s, (0,), me.y_mate)
    for p in range(2):
        w_own(0, p)
    bx = go(d_src.at[high], d_at(0, 0, 0, high), bx_s, (0,), me.x_mate)
    a_own(0)
    b_own(0, 0)
    bx.wait_recv()
    b_own(0, 1)
    for k in range(1, GRID_Z):
        for p in range(2):
            w_own(k, p)
        a_own(k)
        for fx in range(2):
            b_own(k, fx)
        w_across(k - 1)
        a_across(k - 1)
        if k > 1:
            y_done(k - 2)
    y_done(GRID_Z - 2)
    w_across(GRID_Z - 1)
    a_across(GRID_Z - 1)
    y_done(GRID_Z - 1)
    for k in range(GRID_Z):
        for p in range(2):
            line_done(k, w_source(k, p), w_at(k, 0, p), wz_s.at[p])
        line_done(k, d_source(k, low), d_at(k, 0, 0, low), az_s)
        line_done(k, d_source(k, high), d_at(k, 0, 0, high), bz_s.at[0])
        line_done(k, d_at(k, 1, 0, high), d_at(k, 1, 0, high), bz_s.at[1])
    for copy in sent:
        copy.wait_send()
    pair.wait_recv()
    for k in range(GRID_Z):
        for fx in range(2):
            for p in range(2):
                block = w_at(k, fx, p)
                remote(block, block, wc_s.at[0, k, fx, p], wc_s.at[1, k, fx, p], me.sibling).wait_recv()
            for fy in range(2):
                for h, rows in enumerate((low, high)):
                    block = d_at(k, fx, fy, rows)
                    remote(
                        block, block, dc_s.at[0, k, fx, fy, h], dc_s.at[1, k, fx, fy, h], me.sibling
                    ).wait_recv()
    for copy in waits:
        copy.wait()


def first_gather(weights, cotangents, inputs, collective_id):
    chips = lax.axis_size("dp")
    pair = lax.axis_size("tensor")
    dma = pltpu.SemaphoreType.DMA
    low = weights.dtype
    anywhere = pl.BlockSpec(memory_space=pl.ANY)
    w, d, x = pl.pallas_call(
        first_gather_kernel,
        out_shape=(
            jax.ShapeDtypeStruct((chips, *weights.shape), low),
            jax.ShapeDtypeStruct((chips * pair, *cotangents.shape), low),
            jax.ShapeDtypeStruct((pair, *inputs.shape), low),
        ),
        in_specs=[anywhere] * 3,
        out_specs=(anywhere,) * 3,
        scratch_shapes=[
            dma((3,)),
            dma((2, 1)),
            dma((2, 2, 2, 4)),
            dma((2, 4, 2)),
            dma((2, 4, 2, 2)),
            dma((2, 2, 4)),
            dma((2, 4)),
            dma((2, 4, 2)),
            dma((2, 2, 2, 4)),
            dma((2, 1)),
            dma((2, 4, 2)),
            dma((2, 4, 2, 2, 2)),
        ],
        compiler_params=pltpu.CompilerParams(collective_id=collective_id, has_side_effects=True),
    )(weights, cotangents, inputs)
    return (
        w.reshape(-1, w.shape[2]),
        d.reshape(chips, -1, d.shape[2]),
        x.reshape(-1, x.shape[2]),
    )


def unturn(value, cosine, sine):
    return value * cosine - pltpu.roll(value, HEAD_SIZE // 2, 1) * sine


def backward_kernel(
    experts, back_in, residual_in, sent_in, dy_in, x_in, packed, live, cosine, sine, normed_in,
    raw_in, query_in, key_in, value_in, context_in,
    grads, input_gradient,
    back, residual, sent, dy, x, w, ctx, aux_w, normed, raw, query, key, value, context,
    cot, context_cot, raw_cot, key_sum, value_sum, small, first, first_got, stage, result,
    in_s, out_s, y_s, g_s,
):
    bf16, f32 = jnp.bfloat16, jnp.float32
    me = Place()
    own_rows, features = residual.shape
    rows = 2 * own_rows
    heads, key_heads = query.shape[0], key.shape[0]
    group = heads // key_heads
    qkv, wide = w.shape[1], heads * HEAD_SIZE
    chunk = 512
    mine = pl.ds(pl.multiple_of(me.y * own_rows, own_rows), own_rows)
    theirs = pl.ds(pl.multiple_of((1 - me.y) * own_rows, own_rows), own_rows)
    loads = [
        pltpu.make_async_copy(source, target, in_s.at[i])
        for i, (source, target) in enumerate(
            (
                (packed.at[:, pl.ds(qkv + wide, AUX)], aux_w),
                (back_in, back),
                (sent_in, sent),
                (residual_in, residual),
                (dy_in, dy),
                (packed.at[:, pl.ds(qkv, wide)], ctx),
                (context_in, context),
                (value_in, value),
                (key_in, key),
                (query_in, query),
                (raw_in, raw),
                (packed.at[:, pl.ds(0, qkv)], w),
                (normed_in, normed),
                (x_in, x),
            )
        )
    ]
    for copy in loads:
        copy.start()
    meet_y(me)
    for copy in loads[:5]:
        copy.wait()
    aux_t = aux_w[...].astype(f32).T
    gain_one, gain_two, query_gain, key_gain = gain_rows(aux_t, experts, features // HEAD_SIZE)

    lane = lax.broadcasted_iota(jnp.int32, (own_rows, AUX), 1)
    coded = sent[:, features:].astype(f32)
    gates = coded + pltpu.roll(coded, AUX - experts, 1)
    gates = jnp.where(lane < experts, gates, 0.0)
    column = lax.broadcasted_iota(jnp.int32, (AUX, AUX), 0)
    target = lax.broadcasted_iota(jnp.int32, (AUX, AUX), 1)
    fold = ((column % (2 * experts)) // 2 == target).astype(bf16)
    gate_cot = dot(back[:, features:], fold)
    logit_cot = gates * (gate_cot - jnp.sum(gates * gate_cot, axis=-1, keepdims=True))
    logit_cot = logit_cot.astype(bf16)
    small[...] = dot(sent[:, :features], logit_cot, ((0,), (0,)))
    midnorm = jnp.zeros((1, features), f32)
    step = 32
    for i in range(own_rows // step):
        at = slice(i * step, (i + 1) * step)
        total = residual[at, :]
        scale = inverse_norm(total)
        unit = total * scale
        normed_cot = back[at, :features].astype(f32) + dot(
            logit_cot[at, :], aux_w[...], ((1,), (1,))
        )
        midnorm = midnorm + jnp.sum(normed_cot * unit, axis=0, keepdims=True)
        gained = normed_cot * gain_two
        total_cot = dy[at, :].astype(f32) + scale * (
            gained - unit * jnp.mean(gained * unit, axis=-1, keepdims=True)
        )
        residual[at, :] = total_cot
        cot[pl.ds(pl.multiple_of(me.y * own_rows + i * step, step), step), :] = total_cot.astype(bf16)
    swap = remote(cot.at[mine], cot.at[mine], y_s.at[0, 0], y_s.at[1, 0], me.y_mate)
    swap.start()
    for copy in loads[5:10]:
        copy.wait()

    def spread_context(part):
        for c in range(wide // chunk):
            cols = pl.ds(c * chunk, chunk)
            context_cot[part, cols] = dot(cot[part, :], ctx[:, cols]).astype(bf16)

    spread_context(mine)
    swap.wait_recv()
    spread_context(theirs)
    for copy in loads[10:]:
        copy.wait()

    turn_c, turn_s = cosine[...], sine[...]
    allowed = allowed_pairs(live[...])
    key_sum[...] = jnp.zeros_like(key_sum)
    value_sum[...] = jnp.zeros_like(value_sum)

    def raw_back(back_rows, unnormed, gain):
        scale = inverse_norm(unnormed)
        unit = unnormed * scale
        part = jnp.sum(back_rows * unit, axis=0, keepdims=True)
        gained = back_rows * gain
        raw_rows = scale * (gained - unit * jnp.mean(gained * unit, axis=-1, keepdims=True))
        return raw_rows.astype(bf16), part

    def head(h, query_part):
        g = h // group
        at = pl.ds(pl.multiple_of(h * HEAD_SIZE, HEAD_SIZE), HEAD_SIZE)
        probs = probabilities(query[h], key[g], allowed)
        cots = context_cot[:, at]
        prob_cot = dot(cots, value[g], ((1,), (1,)))
        score_cot = probs * (prob_cot - jnp.sum(probs * prob_cot, axis=-1, keepdims=True))
        score_cot = score_cot.astype(bf16)
        value_sum[g] += dot(probs.astype(bf16), cots, ((0,), (0,)))
        key_sum[g] += dot(score_cot, query[h], ((0,), (0,)))
        turned = dot(score_cot, key[g]) * SCORE_SCALE
        raw_cot[:, at], part = raw_back(unturn(turned, turn_c, turn_s), raw[h], query_gain)
        return query_part + part

    query_part = lax.fori_loop(0, heads, head, jnp.zeros((1, HEAD_SIZE), f32))
    key_part = jnp.zeros((1, HEAD_SIZE), f32)
    for g in range(key_heads):
        turned = key_sum[g] * SCORE_SCALE
        at = wide + g * HEAD_SIZE
        raw_cot[:, at : at + HEAD_SIZE], part = raw_back(
            unturn(turned, turn_c, turn_s), raw[heads + g], key_gain
        )
        key_part = key_part + part
        at = at + key_heads * HEAD_SIZE
        raw_cot[:, at : at + HEAD_SIZE] = value_sum[g].astype(bf16)

    copies = []
    for c in range(features // chunk):
        cols = pl.ds(c * chunk, chunk)
        first[:, cols] = dot(raw_cot[theirs, :], w[cols, :], ((1,), (1,))).astype(bf16)
        copy = remote(
            first.at[:, cols], first_got.at[:, cols], y_s.at[0, 1 + c], y_s.at[1, 1 + c], me.y_mate
        )
        copy.start()
        copies.append(copy)
    block = 256

    def store(i):
        slot = i % 2
        return pltpu.make_async_copy(
            stage.at[slot],
            grads.at[pl.ds(pl.multiple_of(i * block, block), block), pl.ds(0, qkv + wide)],
            g_s.at[slot],
        )

    def weight_grads(i, carry):
        slot = i % 2
        at = pl.ds(pl.multiple_of(i * block, block), block)

        @pl.when(i >= 2)
        def _():
            store(i - 2).wait()

        for c in range(qkv // chunk):
            cols = pl.ds(c * chunk, chunk)
            stage[slot, :, cols] = dot(normed[:, at], raw_cot[:, cols], ((0,), (0,))).astype(bf16)
        for c in range(wide // chunk):
            cols = pl.ds(c * chunk, chunk)
            stage[slot, :, pl.ds(qkv + c * chunk, chunk)] = dot(
                cot[:, at], context[:, cols], ((0,), (0,))
            ).astype(bf16)
        store(i).start()
        return carry

    lax.fori_loop(0, features // block, weight_grads, 0)
    prenorm = jnp.zeros((1, features), f32)
    for copy in copies:
        copy.wait_recv()
    for c in range(features // chunk):
        cols = pl.ds(c * chunk, chunk)
        back_cols = dot(raw_cot[mine, :], w[cols, :], ((1,), (1,)))
        result_part = back_cols + first_got[:, cols].astype(f32)
        back[:, cols] = result_part.astype(bf16)
    step = 32
    for i in range(own_rows // step):
        at = slice(i * step, (i + 1) * step)
        stream = x[pl.ds(pl.multiple_of(me.y * own_rows + i * step, step), step), :].astype(f32)
        scale = inverse_norm(stream)
        unit = stream * scale
        first_cot = back[at, :features].astype(f32)
        prenorm = prenorm + jnp.sum(first_cot * unit, axis=0, keepdims=True)
        gained = first_cot * gain_one
        result[at, :] = (
            residual[at, :]
            + scale * (gained - unit * jnp.mean(gained * unit, axis=-1, keepdims=True))
        ).astype(bf16)
    done = pltpu.make_async_copy(result, input_gradient, out_s.at[0])
    done.start()
    chunks = features // HEAD_SIZE
    extra = jnp.concatenate(
        [
            jnp.zeros((experts, features), f32),
            prenorm,
            midnorm,
            jnp.concatenate([query_part] * chunks, axis=1),
            jnp.concatenate([key_part] * chunks, axis=1),
            jnp.zeros((AUX - experts - 4, features), f32),
        ],
        axis=0,
    )
    aux_w[...] = (small[...] + extra.T).astype(bf16)
    last = pltpu.make_async_copy(aux_w, grads.at[:, pl.ds(qkv + wide, AUX)], out_s.at[1])
    last.start()
    swap.wait_send()
    for copy in copies:
        copy.wait_send()
    for i in (2, 1):
        store(features // block - i).wait()
    done.wait()
    last.wait()


def attention_backward(
    back, residual, sent, dy, x_pair, packed, live, saved, experts, collective_id
):
    bf16, f32 = jnp.bfloat16, jnp.float32
    normed, raw, query, key, value, context = saved
    own_rows, features = residual.shape
    rows = 2 * own_rows
    heads, key_heads = query.shape[0], key.shape[0]
    wide = heads * HEAD_SIZE
    qkv = wide + 2 * key_heads * HEAD_SIZE
    cosine, sine = turn_tables(rows)
    dma = pltpu.SemaphoreType.DMA
    anywhere, vmem = pl.BlockSpec(memory_space=pl.ANY), pl.BlockSpec(memory_space=pltpu.VMEM)
    return pl.pallas_call(
        functools.partial(backward_kernel, experts),
        out_shape=(
            jax.ShapeDtypeStruct((features, qkv + wide + AUX), bf16),
            jax.ShapeDtypeStruct((own_rows, features), bf16),
        ),
        in_specs=[anywhere] * 6 + [vmem] * 3 + [anywhere] * 6,
        out_specs=(anywhere,) * 2,
        scratch_shapes=[
            pltpu.VMEM((own_rows, features + AUX), bf16),
            pltpu.VMEM((own_rows, features), f32),
            pltpu.VMEM((own_rows, features + AUX), bf16),
            pltpu.VMEM((own_rows, features), bf16),
            pltpu.VMEM((rows, features), bf16),
            pltpu.VMEM((features, qkv), bf16),
            pltpu.VMEM((features, wide), bf16),
            pltpu.VMEM((features, AUX), bf16),
            pltpu.VMEM((rows, features), bf16),
            pltpu.VMEM((heads + 2 * key_heads, rows, HEAD_SIZE), f32),
            pltpu.VMEM((heads, rows, HEAD_SIZE), bf16),
            pltpu.VMEM((key_heads, rows, HEAD_SIZE), bf16),
            pltpu.VMEM((key_heads, rows, HEAD_SIZE), bf16),
            pltpu.VMEM((rows, wide), bf16),
            pltpu.VMEM((rows, features), bf16),
            pltpu.VMEM((rows, wide), bf16),
            pltpu.VMEM((rows, qkv), bf16),
            pltpu.VMEM((key_heads, rows, HEAD_SIZE), f32),
            pltpu.VMEM((key_heads, rows, HEAD_SIZE), f32),
            pltpu.VMEM((features, AUX), f32),
            pltpu.VMEM((own_rows, features), bf16),
            pltpu.VMEM((own_rows, features), bf16),
            pltpu.VMEM((2, 256, qkv + wide), bf16),
            pltpu.VMEM((own_rows, features), bf16),
            dma((14,)),
            dma((2,)),
            dma((2, 1 + features // 512)),
            dma((2,)),
        ],
        compiler_params=pltpu.CompilerParams(
            collective_id=collective_id, has_side_effects=True, vmem_limit_bytes=ATTENTION_VMEM
        ),
    )(
        back, residual, sent, dy, x_pair, packed, live, cosine, sine,
        normed, raw, query, key, value, context,
    )


def last_scatter_kernel(
    g_part, d_part, g_out, d_out,
    g_own, g_core, g_x, g_z, d_own, d_core, d_y, a_x, b_x, a_z, b_z, small_got,
    gl_s, gc_s, gx_s, gz_s, dl_s, dc_s, dy_s, ax_s, bx_s, az_s, bz_s, small_s, out_s,
):
    me = Place()
    g_rows, d_rows = g_own.shape[2], d_own.shape[3]
    half, g_half = d_rows // 2, g_rows // 2
    g_all, low, high = (0, g_rows), (0, half), (half, half)
    low_at, high_at = pl.ds(0, half), pl.ds(half, half)
    last = GRID_Z - 1
    loads, cores, sends = {}, {}, []

    def g_chunk(k, fx, fc):
        return g_part.at[me.dp_at(me.farthest(k), fx, fc)]

    def d_chunk(k, fx, fy, fc):
        return d_part.at[me.dp_at(me.farthest(k), fx, fc) * 2 + me.y_at(fy)]

    pairs = ((1, 1), (0, 1), (1, 0), (0, 0))
    for k in range(GRID_Z):
        for fx in (1, 0):
            loads[k, fx] = pltpu.make_async_copy(g_chunk(k, fx, 0), g_own.at[k, fx], gl_s.at[k, fx])
            loads[k, fx].start()
        for fx, fy in pairs:
            loads[k, fx, fy] = pltpu.make_async_copy(
                d_chunk(k, fx, fy, 0), d_own.at[k, fx, fy], dl_s.at[k, fx, fy]
            )
            loads[k, fx, fy].start()
    me.greet()
    for k in range(GRID_Z):
        for fx in (1, 0):
            cores[k, fx] = remote(
                g_chunk(k, fx, 1), g_core.at[k, fx],
                gc_s.at[0, k, fx], gc_s.at[1, k, fx], me.sibling,
            )
        for fx, fy in pairs:
            cores[k, fx, fy] = remote(
                d_chunk(k, fx, fy, 1), d_core.at[k, fx, fy],
                dc_s.at[0, k, fx, fy], dc_s.at[1, k, fx, fy], me.sibling,
            )
        for index in ((1,), (1, 1), (0, 1), (0,), (1, 0), (0, 0)):
            cores[(k, *index)].start()

    gx = [
        [
            remote(
                g_own.at[k, 1, pl.ds(h * g_half, g_half)], g_x.at[k, pl.ds(h * g_half, g_half)],
                gx_s.at[0, k, h], gx_s.at[1, k, h], me.x_mate,
            )
            for h in range(2)
        ]
        for k in range(GRID_Z)
    ]
    dy = {
        (k, fx): remote(
            d_own.at[k, fx, 1], d_y.at[k, fx], dy_s.at[0, k, fx], dy_s.at[1, k, fx], me.y_mate
        )
        for k in range(GRID_Z)
        for fx in range(2)
    }
    ax = [
        remote(d_own.at[k, 1, 0, low_at], a_x.at[k], ax_s.at[0, k], ax_s.at[1, k], me.x_mate)
        for k in range(GRID_Z)
    ]
    bx = remote(d_own.at[last, 1, 0, high_at], b_x, bx_s.at[0], bx_s.at[1], me.x_mate)

    def arrive(*index):
        loads[index].wait()
        cores[index].wait_recv()

    def onward(source, buffer, sem, to, side, mate):
        ends = 1 - (me.z - 1 - to + GRID_Z - 1) // GRID_Z
        slot = to if side == 0 else to + (GRID_Z - to) * ends
        return remote(source, buffer.at[slot], sem.at[0, to], sem.at[1, slot], mate)

    def line(k, block, source, rows, buffer, sem, shift):
        to = me.farthest(k)
        for side, ahead, mate, more in (
            (0, to > me.z, me.above, me.has_below),
            (1, to < me.z, me.below, me.has_above),
        ):
            slot = to if k < last or side == 0 else GRID_Z
            came = remote(source, buffer.at[slot], sem.at[0, slot], sem.at[1, slot], mate)

            def gather(came=came, slot=slot):
                came.wait_recv()
                add_rows(block, [(buffer.at[slot], shift)], rows)

            if k < last:

                @pl.when(ahead)
                def _():
                    pl.when(more)(gather)
                    onward(source, buffer, sem, to, side, mate).start()
            else:
                pl.when(more)(gather)

    def line_done(k, source, buffer, sem):
        to = me.farthest(k)
        for side, ahead, mate in ((0, to > me.z, me.above), (1, to < me.z, me.below)):

            @pl.when(ahead)
            def _():
                onward(source, buffer, sem, to, side, mate).wait_send()

    def across(k):
        arrive(k, 1)
        for h in range(2):
            add_rows(g_own.at[k, 1], [(g_core.at[k, 1], 0)], (h * g_half, g_half))
            gx[k][h].start()

    def over_y(k):
        for fx in (1, 0):
            arrive(k, fx, 1)
            add_rows(d_own.at[k, fx, 1], [(d_core.at[k, fx, 1], 0)], (0, d_rows))
            dy[k, fx].start()

    def column(k):
        arrive(k, 0)
        for h in range(2):
            gx[k][h].wait_recv()
        add_rows(g_own.at[k, 0], [(g_core.at[k, 0], 0), (g_x.at[k], 0)], g_all)
        line(k, g_own.at[k, 0], g_own.at[k, 0], g_all, g_z, gz_s, 0)

    def merge(k):
        for fx in (1, 0):
            arrive(k, fx, 0)
            dy[k, fx].wait_recv()
            block = d_own.at[k, fx, 0]
            if fx:
                add_rows(block, [(d_core.at[k, fx, 0], 0), (d_y.at[k, fx], 0)], low)
                ax[k].start()
                add_rows(block, [(d_core.at[k, fx, 0], 0), (d_y.at[k, fx], 0)], high)
            else:
                add_rows(block, [(d_core.at[k, fx, 0], 0), (d_y.at[k, fx], 0)], (0, d_rows))
            line(k, block, block.at[high_at], high, b_z.at[fx], bz_s.at[fx], half)
            if fx and k == last:
                bx.start()

    def settle(k):
        ax[k].wait_recv()
        block = d_own.at[k, 0, 0]
        add_rows(block, [(a_x.at[k], 0)], low)
        line(k, block, block.at[low_at], low, a_z, az_s, 0)

    for k in range(GRID_Z):
        across(k)
        over_y(k)
        if k >= 1:
            column(k - 1)
            merge(k - 1)
        if k >= 2:
            settle(k - 2)
    merge(last)
    column(last)
    settle(last - 1)
    width = g_own.shape[3]
    small = remote(
        g_own.at[last, 0, :, pl.ds(width - AUX, AUX)], small_got,
        small_s.at[0], small_s.at[1], me.y_mate,
    )
    small.start()
    settle(last)
    bx.wait_recv()
    add_rows(d_own.at[last, 0, 0], [(b_x, half)], high)
    outs = [pltpu.make_async_copy(d_own.at[last, 0, 0], d_out, out_s.at[0])]
    outs[0].start()
    small.wait()
    block = g_own.at[last, 0, :, pl.ds(width - AUX, AUX)]
    block[...] = (block[...].astype(jnp.float32) + small_got[...].astype(jnp.float32)).astype(
        block.dtype
    )
    outs.append(pltpu.make_async_copy(g_own.at[last, 0], g_out, out_s.at[1]))
    outs[1].start()
    for k in range(GRID_Z):
        for h in range(2):
            gx[k][h].wait_send()
        for fx in range(2):
            dy[k, fx].wait_send()
        ax[k].wait_send()
        if k < last:
            line_done(k, g_own.at[k, 0], g_z, gz_s)
            for fx in range(2):
                line_done(k, d_own.at[k, fx, 0, high_at], b_z.at[fx], bz_s.at[fx])
            line_done(k, d_own.at[k, 0, 0, low_at], a_z, az_s)
    bx.wait_send()
    for sent in cores.values():
        sent.wait_send()
    for copy in outs:
        copy.wait()


def last_scatter(grads, sums, collective_id):
    chips, pair = lax.axis_size("dp"), lax.axis_size("tensor")
    g_rows, g_wide = grads.shape[0] // chips, grads.shape[1]
    d_rows, d_wide = sums.shape[0] // (chips * pair), sums.shape[1]
    half = d_rows // 2
    dma = pltpu.SemaphoreType.DMA
    low = grads.dtype
    anywhere = pl.BlockSpec(memory_space=pl.ANY)
    return pl.pallas_call(
        last_scatter_kernel,
        out_shape=(
            jax.ShapeDtypeStruct((g_rows, g_wide), low),
            jax.ShapeDtypeStruct((d_rows, d_wide), low),
        ),
        in_specs=[anywhere] * 2,
        out_specs=(anywhere,) * 2,
        scratch_shapes=[
            pltpu.VMEM((4, 2, g_rows, g_wide), low),
            pltpu.VMEM((4, 2, g_rows, g_wide), low),
            pltpu.VMEM((4, g_rows, g_wide), low),
            pltpu.VMEM((5, g_rows, g_wide), low),
            pltpu.VMEM((4, 2, 2, d_rows, d_wide), low),
            pltpu.VMEM((4, 2, 2, d_rows, d_wide), low),
            pltpu.VMEM((4, 2, d_rows, d_wide), low),
            pltpu.VMEM((4, half, d_wide), low),
            pltpu.VMEM((half, d_wide), low),
            pltpu.VMEM((5, half, d_wide), low),
            pltpu.VMEM((2, 5, half, d_wide), low),
            pltpu.VMEM((g_rows, AUX), low),
            dma((4, 2)),
            dma((2, 4, 2)),
            dma((2, 4, 2)),
            dma((2, 5)),
            dma((4, 2, 2)),
            dma((2, 4, 2, 2)),
            dma((2, 4, 2)),
            dma((2, 4)),
            dma((2,)),
            dma((2, 5)),
            dma((2, 2, 5)),
            dma((2,)),
            dma((2,)),
        ],
        compiler_params=pltpu.CompilerParams(
            collective_id=collective_id, has_side_effects=True, vmem_limit_bytes=60 * 1024 * 1024
        ),
    )(grads.reshape(chips, g_rows, g_wide), sums.reshape(chips * pair, d_rows, d_wide))


def gathered_body(
    layer_input,
    query_weight,
    key_projection,
    value_projection,
    context_weight,
    router_weight,
    expert_gate,
    expert_up,
    expert_down,
    prenorm_gain,
    midnorm_gain,
    querynorm_gain,
    keynorm_gain,
    routes,
    lengths,
    sequence_order,
    output_cotangent,
):
    bf16, f32 = jnp.bfloat16, jnp.float32
    tensor_count = lax.axis_size("tensor")
    tensor_index = lax.axis_index("tensor")
    dp_count = lax.axis_size("dp")
    dp_index = lax.axis_index("dp")
    own_rows, features = layer_input.shape
    block_rows = own_rows * tensor_count
    tokens = block_rows * dp_count
    expert_count = EXP_DEV * dp_count
    capacity = 3 * block_rows * TOP // (4 * EXP_DEV)
    most_rows = (5 * block_rows * TOP + 4 * expert_count - 1) // (4 * expert_count)
    shard = features // dp_count
    query_width = query_weight.shape[1]
    key_width = key_projection.shape[1]
    norm_part = HEAD_SIZE // dp_count

    place = dp_index * norm_part
    route_wide = block_rows * TOP // shard
    gains = jnp.concatenate(
        [
            prenorm_gain[:, None],
            midnorm_gain[:, None],
            lax.dynamic_update_slice(jnp.zeros((shard,), bf16), querynorm_gain, (place,))[:, None],
            lax.dynamic_update_slice(jnp.zeros((shard,), bf16), keynorm_gain, (place,))[:, None],
            routes.T.reshape(shard, -1).astype(bf16),
            jnp.zeros((shard, AUX - expert_count - 4 - route_wide), bf16),
        ],
        axis=1,
    )
    packed = jnp.concatenate(
        [query_weight, key_projection, value_projection, context_weight.T, router_weight, gains],
        axis=1,
    )
    packed, cot_all, input_rows = first_gather(packed, output_cotangent, layer_input, 0)
    route_from = packed.shape[1] - AUX + expert_count + 4
    routes_all = packed[:, route_from : route_from + route_wide].astype(jnp.int32)
    routes_all = routes_all.reshape(dp_count, TOP, block_rows)
    position = jnp.arange(block_rows, dtype=jnp.int32)
    block_lengths = lengths[sequence_order]
    live = position[None, :] < block_lengths[:, None]
    live_own = lax.dynamic_slice_in_dim(live, dp_index, 1, 0)
    live_own = jnp.broadcast_to(live_own.astype(f32), (8, block_rows))
    heads_query = query_width // HEAD_SIZE
    heads_key = key_width // HEAD_SIZE
    row_start = tensor_index * own_rows
    routes_own = lax.dynamic_slice_in_dim(routes, row_start, own_rows, 0)
    expert_ids = jnp.arange(AUX, dtype=jnp.int32)
    chosen = jnp.any(routes_own[:, :, None] == expert_ids[None, None, :], axis=1).astype(f32)
    sent, residual, *saved = attention_forward(
        input_rows, packed, live_own, chosen, expert_count, heads_query, heads_key, 5
    )
    normed_all = gather_all(sent, 1).reshape(dp_count, block_rows, features + AUX)

    expert_own = dp_index * EXP_DEV + jnp.arange(EXP_DEV, dtype=jnp.int32)
    hot = jnp.any(routes_all[:, None, :, :] == expert_own[None, :, None, None], axis=2)
    hot = hot & live[:, None, :]
    before = (position[:, None] < position[None, :]).astype(bf16)
    rank = jnp.einsum("bes,st->bet", hot.astype(bf16), before, preferred_element_type=f32)
    rank = rank.astype(jnp.int32)
    counts = rank[:, :, -1] + hot[:, :, -1]
    earlier = jnp.cumsum(counts, axis=0) - counts
    slot = earlier[:, :, None] + rank
    slot = jnp.where(hot & (slot < capacity), slot, -capacity)
    begin = jnp.minimum(earlier, capacity) // WINDOW_ALIGN * WINDOW_ALIGN
    info = jnp.concatenate([dp_index[None], begin.reshape(-1), tensor_index[None]])
    out_part, back_part, gate_gradient, up_gradient, down_gradient = expert_layer(
        info.astype(jnp.int32),
        slot,
        normed_all,
        cot_all,
        expert_gate,
        expert_up,
        expert_down,
        capacity,
        most_rows,
    )
    returned = scatter_all(back_part.reshape(tokens, features + AUX), 3)
    grads, input_gradient = attention_backward(
        returned,
        residual,
        sent,
        output_cotangent,
        input_rows,
        packed,
        live_own,
        saved,
        expert_count,
        6,
    )
    summed, expert_sum = last_scatter(grads, out_part.reshape(tokens, features), 4)
    summed = summed.astype(f32)
    layer_output = (residual + expert_sum.astype(f32)).astype(bf16)
    ends = [0]
    for width in (query_width, key_width, key_width, query_width, AUX):
        ends.append(ends[-1] + width)
    small = summed[:, ends[4] :]
    head_small = lax.dynamic_slice_in_dim(small, place, norm_part, 0)
    return (
        layer_output,
        input_gradient,
        summed[:, : ends[1]],
        summed[:, ends[1] : ends[2]],
        summed[:, ends[2] : ends[3]],
        summed[:, ends[3] : ends[4]].T,
        small[:, :expert_count],
        gate_gradient,
        up_gradient,
        down_gradient,
        small[:, expert_count],
        small[:, expert_count + 1],
        head_small[:, expert_count + 2],
        head_small[:, expert_count + 3],
    )


def solution(mesh):
    return jax.shard_map(
        gathered_body if mesh.shape["dp"] <= 16 else body,
        mesh=mesh,
        in_specs=(
            P(("dp", "tensor"), None),
            P("dp", "tensor"),
            P("dp", "tensor"),
            P("dp", "tensor"),
            P("tensor", "dp"),
            P("dp", None),
            P("dp", None, "tensor"),
            P("dp", None, "tensor"),
            P("dp", "tensor", None),
            P("dp"),
            P("dp"),
            P("dp"),
            P("dp"),
            P("dp", None),
            P(),
            P(),
            P(("dp", "tensor"), None),
        ),
        out_specs=(
            P(("dp", "tensor"), None),
            P(("dp", "tensor"), None),
            P("dp", "tensor"),
            P("dp", "tensor"),
            P("dp", "tensor"),
            P("tensor", "dp"),
            P("dp", None),
            P("dp", None, "tensor"),
            P("dp", None, "tensor"),
            P("dp", "tensor", None),
            P("dp"),
            P("dp"),
            P("dp"),
            P("dp"),
        ),
        check_vma=False,
    )
```

```python
import functools
import math

import jax
import jax.numpy as jnp
import numpy as np
from jax import lax
from jax.experimental import pallas as pl
from jax.experimental.pallas import tpu as pltpu
from jax.sharding import PartitionSpec as P

HEAD_SIZE = 128
TOP = 8
EXP_DEV = 2


epsilon = 1e-06
rope_base = 1000000.0
masked_score = -1e30


def carried_in(value, axis, combine, identity):
    count, place = (lax.axis_size(axis), lax.axis_index(axis))
    everything = lax.all_gather(value, axis)
    start = jnp.broadcast_to(jnp.asarray(identity, value.dtype), value.shape)

    def hop(k, before):
        reached = k < place
        new = combine(before, everything[k])
        return jnp.where(reached, new, before)

    return lax.fori_loop(0, count, hop, start)


def rms_normalize(value_rows):
    scaling = lax.rsqrt(jnp.mean(value_rows * value_rows, axis=-1, keepdims=True) + epsilon)
    return (value_rows * scaling, scaling)


def norm_back(cotangent, unit_rows, scaling):
    return scaling * (
        cotangent - unit_rows * jnp.mean(cotangent * unit_rows, axis=-1, keepdims=True)
    )


def rotary_apply(value_rows, cosine_table, sine_values):
    middle = value_rows.shape[-1] // 2
    former = value_rows[..., :middle]
    latter = value_rows[..., middle:]
    return jnp.concatenate(
        [
            former * cosine_table - latter * sine_values,
            latter * cosine_table + former * sine_values,
        ],
        axis=-1,
    )


def matrix_product(former, latter):
    return jnp.dot(former, latter, preferred_element_type=jnp.float32)


def contract(former, latter):
    return lax.dot_general(
        former, latter, (((0,), (0,)), ((), ())), preferred_element_type=jnp.float32
    )


def transposed(former, latter):
    return lax.dot_general(
        former, latter, (((1,), (1,)), ((), ())), preferred_element_type=jnp.float32
    )


def to_owners(buffer):
    return lax.all_to_all(buffer, "dp", split_axis=1, concat_axis=1, tiled=True)


def owner_reduce(partial_rows):
    shares = lax.psum_scatter(
        partial_rows.astype(jnp.bfloat16), "tensor", scatter_dimension=2, tiled=True
    )
    return lax.all_gather(shares, "tensor", axis=2, tiled=True)


def body(
    layer_input,
    query_weight,
    key_projection,
    value_projection,
    context_weight,
    router_weight,
    expert_gate,
    expert_up,
    expert_down,
    prenorm_gain,
    midnorm_gain,
    querynorm_gain,
    keynorm_gain,
    routes,
    lengths,
    sequence_order,
    output_cotangent,
):
    tensor_count = lax.axis_size("tensor")
    tensor_index = lax.axis_index("tensor")
    dp_count = lax.axis_size("dp")
    own_rows = layer_input.shape[0]
    block_rows = own_rows * tensor_count
    features = layer_input.shape[1]
    expert_count = EXP_DEV * dp_count
    capacity = 3 * block_rows * TOP // (4 * EXP_DEV)
    most_rows = (5 * block_rows * TOP + 4 * expert_count - 1) // (4 * expert_count)
    slot_total = EXP_DEV * dp_count * most_rows
    (
        query_all,
        key_all,
        value_all,
        context_all,
        router_all,
        gain_first,
        gain_second,
        query_gain,
        gain_key,
    ) = (
        lax.all_gather(query_weight, "dp", axis=0, tiled=True),
        lax.all_gather(key_projection, "dp", axis=0, tiled=True),
        lax.all_gather(value_projection, "dp", axis=0, tiled=True),
        lax.all_gather(context_weight, "dp", axis=1, tiled=True),
        lax.all_gather(router_weight, "dp", axis=0, tiled=True),
        lax.all_gather(prenorm_gain, "dp", axis=0, tiled=True),
        lax.all_gather(midnorm_gain, "dp", axis=0, tiled=True),
        lax.all_gather(querynorm_gain, "dp", axis=0, tiled=True),
        lax.all_gather(keynorm_gain, "dp", axis=0, tiled=True),
    )
    input_rows, cot_rows = (
        lax.all_gather(layer_input, "tensor", axis=0, tiled=True),
        lax.all_gather(output_cotangent, "tensor", axis=0, tiled=True),
    )
    position = jnp.arange(block_rows, dtype=jnp.int32)
    seq_length = lengths[sequence_order[lax.axis_index("dp")]]
    token_live = position < seq_length
    frequency = jnp.exp(
        -math.log(rope_base) * jnp.arange(HEAD_SIZE // 2, dtype=jnp.float32) * (2.0 / HEAD_SIZE)
    )
    angles = position.astype(jnp.float32)[:, None] * frequency[None, :]
    cosine_table = jnp.cos(angles)[:, None, :]
    sine_values = jnp.sin(angles)[:, None, :]
    heads_query = query_all.shape[1] // HEAD_SIZE
    heads_key = key_all.shape[1] // HEAD_SIZE
    group_width = heads_query // heads_key
    gain_one = gain_first.astype(jnp.float32)
    gain_two = gain_second.astype(jnp.float32)
    query_factor = query_gain.astype(jnp.float32)
    key_factor = gain_key.astype(jnp.float32)
    stream = input_rows.astype(jnp.float32)
    unit_first, scale_first = rms_normalize(stream)
    first_layer_normed = (unit_first * gain_one).astype(jnp.bfloat16)
    query_unnormed = matrix_product(first_layer_normed, query_all).reshape(
        block_rows, heads_query, HEAD_SIZE
    )
    key_unnormed = matrix_product(first_layer_normed, key_all).reshape(
        block_rows, heads_key, HEAD_SIZE
    )
    value_rows = (
        matrix_product(first_layer_normed, value_all)
        .astype(jnp.bfloat16)
        .reshape(block_rows, heads_key, HEAD_SIZE)
    )
    query_unit, query_scale = rms_normalize(query_unnormed)
    key_unit, key_scale = rms_normalize(key_unnormed)
    query_rows = (
        rotary_apply(query_unit * query_factor, cosine_table, sine_values)
        .astype(jnp.bfloat16)
        .reshape(block_rows, heads_key, group_width, HEAD_SIZE)
    )
    keys_rot = rotary_apply(key_unit * key_factor, cosine_table, sine_values).astype(jnp.bfloat16)
    score_scale = HEAD_SIZE ** (-0.5)
    allowed = (position[None, :] <= position[:, None]) & token_live[None, :]

    def score_block():
        raw_scores = (
            jnp.einsum("ikrd,jkd->krij", query_rows, keys_rot, preferred_element_type=jnp.float32)
            * score_scale
        )
        return jnp.where(allowed, raw_scores, masked_score)

    scores = score_block()
    row_peak = jnp.max(scores, axis=-1, keepdims=True)
    log_total = row_peak + jnp.log(jnp.sum(jnp.exp(scores - row_peak), axis=-1, keepdims=True))
    soft_probs = jnp.exp(scores - log_total)
    context = jnp.einsum(
        "krij,jkd->ikrd",
        soft_probs.astype(jnp.bfloat16),
        value_rows,
        preferred_element_type=jnp.float32,
    )
    context = context.reshape(block_rows, heads_query * HEAD_SIZE).astype(jnp.bfloat16)
    attention = lax.psum(matrix_product(context, context_all), "tensor")
    residual = stream + attention
    unit_second, scale_second = rms_normalize(residual)
    normed_second = (unit_second * gain_two).astype(jnp.bfloat16)
    logits = matrix_product(normed_second, router_all)
    expert_ids = jnp.arange(expert_count, dtype=jnp.int32)
    route_hot = routes[:, :, None] == expert_ids[None, None, :]
    chosen = jnp.sum(jnp.where(route_hot, logits[:, None, :], 0.0), axis=-1)
    gate_weights = jax.nn.softmax(chosen, axis=-1)
    pair_expert = routes.reshape(-1)
    pair_live = jnp.repeat(token_live, TOP)
    pair_hot = ((pair_expert[:, None] == expert_ids[None, :]) & pair_live[:, None]).astype(
        jnp.int32
    )
    running = jnp.cumsum(pair_hot, axis=0)
    pair_rank = jnp.sum((running - pair_hot) * pair_hot, axis=1)
    counts = running[-1]
    earlier = carried_in(
        counts, "dp", lambda former, latter: former + latter, jnp.zeros_like(counts)
    )
    pair_slot = jnp.sum(earlier[None, :] * pair_hot, axis=1) + pair_rank
    pair_kept = pair_live & (pair_slot < capacity)
    local_expert = pair_expert % EXP_DEV
    owner_index = pair_expert // EXP_DEV
    buffer_index = (local_expert * dp_count + owner_index) * most_rows + pair_rank
    target = jnp.where(pair_kept, buffer_index, slot_total)
    pair_ids = jnp.arange(block_rows * TOP, dtype=jnp.int32)
    slot_pair = jnp.full((slot_total,), -1, dtype=jnp.int32).at[target].set(pair_ids, mode="drop")
    slot_used = slot_pair >= 0
    slot_safe = jnp.maximum(slot_pair, 0)
    slot_token = slot_safe // TOP
    bf_zero = jnp.zeros((), jnp.bfloat16)
    send_rows = jnp.where(slot_used[:, None], normed_second[slot_token], bf_zero)
    layout = (EXP_DEV, dp_count, most_rows, features)
    received = to_owners(send_rows.reshape(layout)).reshape(EXP_DEV, dp_count * most_rows, features)
    gate_pre = jnp.einsum("end,edf->enf", received, expert_gate, preferred_element_type=jnp.float32)
    up_pre = jnp.einsum("end,edf->enf", received, expert_up, preferred_element_type=jnp.float32)
    sigmoid_gate = jax.nn.sigmoid(gate_pre)
    gate_act = gate_pre * sigmoid_gate
    hidden = (gate_act * up_pre).astype(jnp.bfloat16)
    out_partial = jnp.einsum(
        "enf,efd->end", hidden, expert_down, preferred_element_type=jnp.float32
    )
    expert_out = owner_reduce(out_partial)
    width = expert_out.shape[2]
    returned = lax.all_to_all(
        expert_out.reshape(EXP_DEV, dp_count, most_rows, width),
        "dp",
        split_axis=1,
        concat_axis=1,
        tiled=True,
    ).reshape(slot_total, width)
    pair_place = jnp.where(pair_kept, buffer_index, 0)
    pair_out = jnp.where(pair_kept[:, None], returned[pair_place], bf_zero).reshape(
        block_rows, TOP, width
    )
    expert_part = jnp.sum(gate_weights[:, :, None] * pair_out, axis=1)
    cot_full = cot_rows.astype(jnp.float32)
    own_start = tensor_index * own_rows
    gate_part = jnp.sum(cot_full[:, None, :] * pair_out, axis=-1)
    expert_own = lax.dynamic_slice_in_dim(expert_part, own_start, own_rows, 0)
    residual_own = lax.dynamic_slice_in_dim(residual, own_start, own_rows, 0)
    layer_output = (residual_own + expert_own).astype(jnp.bfloat16)
    slot_gate = jnp.where(slot_used, gate_weights.reshape(-1)[slot_safe], 0.0)
    send_cot = (slot_gate[:, None] * cot_full[slot_token]).astype(jnp.bfloat16)
    expert_cot = to_owners(send_cot.reshape(layout)).reshape(
        EXP_DEV, dp_count * most_rows, features
    )
    hidden_cot = jnp.einsum(
        "end,efd->enf", expert_cot, expert_down, preferred_element_type=jnp.float32
    )
    gating_cot = (
        hidden_cot * up_pre * sigmoid_gate * (1.0 + gate_pre * (1.0 - sigmoid_gate))
    ).astype(jnp.bfloat16)
    upward_cot = (hidden_cot * gate_act).astype(jnp.bfloat16)
    down_gradient = jnp.einsum(
        "enf,end->efd", hidden, expert_cot, preferred_element_type=jnp.float32
    )
    gate_gradient = jnp.einsum(
        "end,enf->edf", received, gating_cot, preferred_element_type=jnp.float32
    )
    up_gradient = jnp.einsum(
        "end,enf->edf", received, upward_cot, preferred_element_type=jnp.float32
    )
    row_partial = jnp.einsum(
        "enf,edf->end", gating_cot, expert_gate, preferred_element_type=jnp.float32
    )
    row_partial = row_partial + jnp.einsum(
        "enf,edf->end", upward_cot, expert_up, preferred_element_type=jnp.float32
    )
    row_cot = owner_reduce(row_partial)
    row_back = lax.all_to_all(
        row_cot.reshape(EXP_DEV, dp_count, most_rows, width),
        "dp",
        split_axis=1,
        concat_axis=1,
        tiled=True,
    ).reshape(slot_total, width)
    pair_cot = jnp.where(pair_kept[:, None], row_back[pair_place], bf_zero).reshape(
        block_rows, TOP, width
    )
    normed_part = jnp.sum(pair_cot.astype(jnp.float32), axis=1)
    normed_cot = normed_part
    route_cot = gate_weights * (
        gate_part - jnp.sum(gate_weights * gate_part, axis=-1, keepdims=True)
    )
    logit_cot = jnp.sum(jnp.where(route_hot, route_cot[:, :, None], 0.0), axis=1).astype(
        jnp.bfloat16
    )
    router_gradient = contract(normed_second, logit_cot)
    normed_cot = normed_cot + transposed(logit_cot, router_all)
    midnorm_gradient = jnp.sum(normed_cot * unit_second, axis=0)
    residual_cot = cot_full + norm_back(normed_cot * gain_two, unit_second, scale_second)
    attention_cot = residual_cot.astype(jnp.bfloat16)
    context_gradient = contract(context, attention_cot)
    context_cot = (
        transposed(attention_cot, context_all)
        .astype(jnp.bfloat16)
        .reshape(block_rows, heads_key, group_width, HEAD_SIZE)
    )
    scores = score_block()
    soft_probs = jnp.exp(scores - log_total)
    prob_cot = jnp.einsum(
        "ikrd,jkd->krij", context_cot, value_rows, preferred_element_type=jnp.float32
    )
    score_cot = (
        soft_probs * (prob_cot - jnp.sum(soft_probs * prob_cot, axis=-1, keepdims=True))
    ).astype(jnp.bfloat16)
    value_cot = jnp.einsum(
        "krij,ikrd->jkd",
        soft_probs.astype(jnp.bfloat16),
        context_cot,
        preferred_element_type=jnp.float32,
    )
    value_cot = value_cot.astype(jnp.bfloat16).reshape(block_rows, heads_key * HEAD_SIZE)
    query_turned = (
        jnp.einsum(
            "krij,jkd->ikrd", score_cot, keys_rot, preferred_element_type=jnp.float32
        ).reshape(block_rows, heads_query, HEAD_SIZE)
        * score_scale
    )
    key_turned = (
        jnp.einsum("krij,ikrd->jkd", score_cot, query_rows, preferred_element_type=jnp.float32)
        * score_scale
    )
    query_back = rotary_apply(query_turned, cosine_table, -sine_values)
    key_back = rotary_apply(key_turned, cosine_table, -sine_values)
    querynorm_part = jnp.sum(query_back * query_unit, axis=(0, 1))
    keynorm_part = jnp.sum(key_back * key_unit, axis=(0, 1))
    query_raw_cot = (
        norm_back(query_back * query_factor, query_unit, query_scale)
        .astype(jnp.bfloat16)
        .reshape(block_rows, heads_query * HEAD_SIZE)
    )
    key_raw_cot = (
        norm_back(key_back * key_factor, key_unit, key_scale)
        .astype(jnp.bfloat16)
        .reshape(block_rows, heads_key * HEAD_SIZE)
    )
    query_gradient = contract(first_layer_normed, query_raw_cot)
    key_gradient = contract(first_layer_normed, key_raw_cot)
    value_gradient = contract(first_layer_normed, value_cot)
    first_part = (
        transposed(query_raw_cot, query_all)
        + transposed(key_raw_cot, key_all)
        + transposed(value_cot, value_all)
    )
    first_cot, querynorm_gradient, keynorm_gradient = (
        lax.psum(first_part.astype(jnp.bfloat16), "tensor").astype(jnp.float32),
        lax.psum(querynorm_part.astype(jnp.bfloat16), "tensor").astype(jnp.float32),
        lax.psum(keynorm_part.astype(jnp.bfloat16), "tensor").astype(jnp.float32),
    )
    prenorm_gradient = jnp.sum(first_cot * unit_first, axis=0)
    input_cot = residual_cot + norm_back(first_cot * gain_one, unit_first, scale_first)
    input_gradient = lax.dynamic_slice_in_dim(input_cot, own_start, own_rows, 0).astype(
        jnp.bfloat16
    )
    summed = (
        lax.psum_scatter(query_gradient, "dp", scatter_dimension=0, tiled=True),
        lax.psum_scatter(key_gradient, "dp", scatter_dimension=0, tiled=True),
        lax.psum_scatter(value_gradient, "dp", scatter_dimension=0, tiled=True),
        lax.psum_scatter(context_gradient, "dp", scatter_dimension=1, tiled=True),
        lax.psum_scatter(router_gradient, "dp", scatter_dimension=0, tiled=True),
        lax.psum_scatter(prenorm_gradient, "dp", scatter_dimension=0, tiled=True),
        lax.psum_scatter(midnorm_gradient, "dp", scatter_dimension=0, tiled=True),
        lax.psum_scatter(querynorm_gradient, "dp", scatter_dimension=0, tiled=True),
        lax.psum_scatter(keynorm_gradient, "dp", scatter_dimension=0, tiled=True),
    )
    return (
        layer_output,
        input_gradient,
        summed[0],
        summed[1],
        summed[2],
        summed[3],
        summed[4],
        gate_gradient,
        up_gradient,
        down_gradient,
        summed[5],
        summed[6],
        summed[7],
        summed[8],
    )


AUX = 128


GRID_Z = 4
VMEM_LIMIT = 56 * 1024 * 1024


def remote(src, dst, send_sem, recv_sem, device):
    return pltpu.make_async_remote_copy(
        src_ref=src,
        dst_ref=dst,
        send_sem=send_sem,
        recv_sem=recv_sem,
        device_id=device,
        device_id_type=pl.DeviceIdType.MESH,
    )


class Place:
    def __init__(self):
        self.dp = lax.axis_index("dp")
        self.y = lax.axis_index("tensor")
        self.z = self.dp // 4
        self.x = (self.dp // 2) % 2
        self.core = self.dp % 2
        self.sibling = (self.dp + 1 - 2 * self.core, self.y)
        self.x_mate = (self.dp + 2 - 4 * self.x, self.y)
        self.y_mate = (self.dp, 1 - self.y)
        self.above = (self.dp + 4, self.y)
        self.below = (self.dp - 4, self.y)
        self.has_above = self.z < GRID_Z - 1
        self.has_below = self.z > 0

    def farthest(self, k):
        return (3 - 3 * (self.z // 2), (2 + 3 * self.z) % 5, 1 + self.z % 2, self.z)[k]

    def dp_at(self, z, flip_x, flip_core):
        x = self.x + flip_x * (1 - 2 * self.x)
        core = self.core + flip_core * (1 - 2 * self.core)
        return z * 4 + x * 2 + core

    def y_at(self, flip_y):
        return self.y + flip_y * (1 - 2 * self.y)

    def greet(self):
        barrier = pltpu.get_barrier_semaphore()
        for mate in (self.sibling, self.x_mate, self.y_mate):
            pl.semaphore_signal(barrier, 1, device_id=mate, device_id_type=pl.DeviceIdType.MESH)

        @pl.when(self.has_above)
        def _():
            pl.semaphore_signal(
                barrier, 1, device_id=self.above, device_id_type=pl.DeviceIdType.MESH
            )

        @pl.when(self.has_below)
        def _():
            pl.semaphore_signal(
                barrier, 1, device_id=self.below, device_id_type=pl.DeviceIdType.MESH
            )

        pl.semaphore_wait(barrier, 4 + self.z * (GRID_Z - 1 - self.z) // 2)


def add_rows(target, sources, rows, step=16):
    start, count = rows

    def one(i, carry):
        at = pl.ds(pl.multiple_of(start + i * step, step), step)
        total = target[at, :].astype(jnp.float32)
        for source, shift in sources:
            there = pl.ds(pl.multiple_of(start - shift + i * step, step), step)
            total = total + source[there, :].astype(jnp.float32)
        target[at, :] = total.astype(target.dtype)
        return carry

    lax.fori_loop(0, count // step, one, 0)


def scatter_kernel(
    part, out, own, core, diag_a, diag_b, from_x, from_y, from_z, result,
    load_s, core_s, diag_s, x_s, y_s, z_s, out_s,
):
    me = Place()
    rows = own.shape[3]
    half = rows // 2
    low, high = (0, half), (half, half)
    loads, sends = {}, []

    def chunk(k, flip_x, flip_y, flip_core):
        return part.at[me.dp_at(me.farthest(k), flip_x, flip_core) * 2 + me.y_at(flip_y)]

    order = ((1, 1), (1, 0), (0, 1), (0, 0))
    for k in range(GRID_Z):
        for fx, fy in order:
            copy = pltpu.make_async_copy(
                chunk(k, fx, fy, 0), own.at[k, fx, fy], load_s.at[k, fx, fy]
            )
            copy.start()
            loads[k, fx, fy] = copy
    me.greet()
    cores = {}
    for k in range(GRID_Z):
        for fx, fy in order:
            copy = remote(
                chunk(k, fx, fy, 1), core.at[k, fx, fy],
                core_s.at[0, k, fx, fy], core_s.at[1, k, fx, fy], me.sibling,
            )
            copy.start()
            cores[k, fx, fy] = copy
            sends.append(copy)

    da = [remote(own.at[k, 1, 1, pl.ds(0, half)], diag_a.at[k], diag_s.at[0, k], diag_s.at[1, k], me.y_mate) for k in range(4)]
    db = [remote(own.at[k, 1, 1, pl.ds(half, half)], diag_b.at[k], diag_s.at[2, k], diag_s.at[3, k], me.x_mate) for k in range(4)]
    xs = [[remote(own.at[k, 1, 0, pl.ds(h * half, half)], from_x.at[k, pl.ds(h * half, half)], x_s.at[0, k, h], x_s.at[1, k, h], me.x_mate) for h in range(2)] for k in range(4)]
    ys = [[remote(own.at[k, 0, 1, pl.ds(h * half, half)], from_y.at[k, pl.ds(h * half, half)], y_s.at[0, k, h], y_s.at[1, k, h], me.y_mate) for h in range(2)] for k in range(4)]

    def arrive(k, fx, fy):
        loads[k, fx, fy].wait()
        cores[k, fx, fy].wait_recv()

    def early(k):
        arrive(k, 1, 1)
        add_rows(own.at[k, 1, 1], [(core.at[k, 1, 1], 0)], low)
        da[k].start()
        add_rows(own.at[k, 1, 1], [(core.at[k, 1, 1], 0)], high)
        db[k].start()
        arrive(k, 1, 0)
        add_rows(own.at[k, 1, 0], [(core.at[k, 1, 0], 0)], high)
        xs[k][1].start()
        arrive(k, 0, 1)
        add_rows(own.at[k, 0, 1], [(core.at[k, 0, 1], 0)], low)
        ys[k][0].start()

    def late(k):
        da[k].wait_recv()
        add_rows(own.at[k, 1, 0], [(core.at[k, 1, 0], 0), (diag_a.at[k], 0)], low)
        xs[k][0].start()
        db[k].wait_recv()
        add_rows(own.at[k, 0, 1], [(core.at[k, 0, 1], 0), (diag_b.at[k], half)], high)
        ys[k][1].start()

    whole = (0, rows)

    def column(k):
        arrive(k, 0, 0)
        for h in range(2):
            xs[k][h].wait_recv()
            ys[k][h].wait_recv()
        mine = own.at[k, 0, 0]
        rest = [(core.at[k, 0, 0], 0), (from_x.at[k], 0), (from_y.at[k], 0)]
        if k < GRID_Z - 1:
            to = me.farthest(k)
            add_rows(mine, rest, whole)
            for side, ahead, mate, more in (
                (0, to > me.z, me.above, me.has_below),
                (1, to < me.z, me.below, me.has_above),
            ):
                copy = remote(
                    mine, from_z.at[side, to], z_s.at[0, side, to], z_s.at[1, side, to], mate
                )

                @pl.when(ahead)
                def _():
                    @pl.when(more)
                    def _():
                        copy.wait_recv()
                        add_rows(mine, [(from_z.at[side, to], 0)], whole)

                    copy.start()
        else:
            add_rows(mine, rest, whole)
            for side, more in ((0, me.has_below), (1, me.has_above)):
                copy = remote(
                    mine, from_z.at[side, me.z], z_s.at[0, side, me.z], z_s.at[1, side, me.z],
                    me.y_mate,
                )

                @pl.when(more)
                def _():
                    copy.wait_recv()
                    add_rows(mine, [(from_z.at[side, me.z], 0)], whole)

    early(0)
    early(1)
    late(0)
    early(2)
    late(1)
    column(0)
    early(3)
    late(2)
    column(1)
    late(3)
    column(2)
    column(3)
    copy = pltpu.make_async_copy(own.at[3, 0, 0], out, out_s)
    copy.start()
    for k in range(GRID_Z):
        da[k].wait_send()
        db[k].wait_send()
        for h in range(2):
            xs[k][h].wait_send()
            ys[k][h].wait_send()
        if k < GRID_Z - 1:
            to = me.farthest(k)
            for side, ahead, mate in ((0, to > me.z, me.above), (1, to < me.z, me.below)):
                @pl.when(ahead)
                def _():
                    remote(
                        own.at[k, 0, 0], from_z.at[side, to],
                        z_s.at[0, side, to], z_s.at[1, side, to], mate,
                    ).wait_send()
    for sent in sends:
        sent.wait_send()
    copy.wait()


def scatter_all(value, collective_id):
    devices = lax.axis_size("dp") * lax.axis_size("tensor")
    rows, width = value.shape[0] // devices, value.shape[1]
    half = rows // 2
    dma = pltpu.SemaphoreType.DMA
    low = value.dtype
    return pl.pallas_call(
        scatter_kernel,
        out_shape=jax.ShapeDtypeStruct((rows, width), low),
        in_specs=[pl.BlockSpec(memory_space=pl.ANY)],
        out_specs=pl.BlockSpec(memory_space=pl.ANY),
        scratch_shapes=[
            pltpu.VMEM((4, 2, 2, rows, width), low),
            pltpu.VMEM((4, 2, 2, rows, width), low),
            pltpu.VMEM((4, half, width), low),
            pltpu.VMEM((4, half, width), low),
            pltpu.VMEM((4, rows, width), low),
            pltpu.VMEM((4, rows, width), low),
            pltpu.VMEM((2, 4, rows, width), low),
            pltpu.VMEM((8, 128), low),
            dma((4, 2, 2)),
            dma((2, 4, 2, 2)),
            dma((4, 4)),
            dma((2, 4, 2)),
            dma((2, 4, 2)),
            dma((2, 2, 4)),
            dma(()),
        ],
        compiler_params=pltpu.CompilerParams(
            collective_id=collective_id, has_side_effects=True, vmem_limit_bytes=VMEM_LIMIT
        ),
    )(value.reshape(devices, rows, width))


def gather_kernel(src, out, own_s, z_s, x_s, y_s, dx_s, dy_s, core_s):
    me = Place()
    rows = src.shape[0]
    half = rows // 2
    low, high = pl.ds(0, half), pl.ds(half, half)

    def near(k):
        return me.farthest(GRID_Z - 1 - k)

    def at(k, fx, fy, fc):
        return out.at[me.dp_at(near(k), fx, fc) * 2 + me.y_at(fy)]

    mine = pltpu.make_async_copy(src, at(0, 0, 0, 0), own_s)
    mine.start()
    me.greet()

    def over(source, k, fx, fy, send, recv, mate):
        return remote(source, at(k, fx, fy, 0), send, recv, mate)

    def z_copy(k, source, side, mate):
        zn = near(k)
        return remote(source, at(k, 0, 0, 0), z_s.at[0, side, zn], z_s.at[1, side, zn], mate)

    xs, ys, dxs, dys, cores = {}, {}, {}, {}, {}
    for k in range(GRID_Z):
        source = src if k == 0 else at(k, 0, 0, 0)
        xs[k] = over(source, k, 0, 0, x_s.at[0, k], x_s.at[1, k], me.x_mate)
        ys[k] = over(source, k, 0, 0, y_s.at[0, k], y_s.at[1, k], me.y_mate)
        dys[k] = remote(at(k, 1, 0, 0).at[low], at(k, 1, 0, 0).at[low], dy_s.at[0, k], dy_s.at[1, k], me.y_mate)
        dxs[k] = remote(at(k, 0, 1, 0).at[high], at(k, 0, 1, 0).at[high], dx_s.at[0, k], dx_s.at[1, k], me.x_mate)
        for fx in range(2):
            for fy in range(2):
                block = source if (fx, fy) == (0, 0) else at(k, fx, fy, 0)
                if (fx, fy) == (1, 1):
                    for h, part in enumerate((low, high)):
                        cores[k, fx, fy, h] = remote(
                            block.at[part], block.at[part],
                            core_s.at[0, k, 3 + h], core_s.at[1, k, 3 + h], me.sibling,
                        )
                else:
                    cores[k, fx, fy] = remote(
                        block, at(k, fx, fy, 0), core_s.at[0, k, fx * 2 + fy],
                        core_s.at[1, k, fx * 2 + fy], me.sibling,
                    )

    def own(k):
        if k == 0:
            for side, more, mate in ((0, me.has_above, me.above), (1, me.has_below, me.below)):
                copy = z_copy(0, src, side, mate)

                @pl.when(more)
                def _():
                    copy.start()
        else:
            zn = near(k)
            for side, came, more, mate in (
                (0, zn < me.z, me.has_above, me.above),
                (1, zn > me.z, me.has_below, me.below),
            ):
                copy = z_copy(k, at(k, 0, 0, 0), side, mate)

                @pl.when(came)
                def _():
                    copy.wait_recv()

                    @pl.when(more)
                    def _():
                        copy.start()

        xs[k].start()
        ys[k].start()
        cores[k, 0, 0].start()

    def diag(k):
        xs[k].wait_recv()
        dys[k].start()
        cores[k, 1, 0].start()
        ys[k].wait_recv()
        dxs[k].start()
        cores[k, 0, 1].start()

    def corner(k):
        dys[k].wait_recv()
        cores[k, 1, 1, 0].start()
        dxs[k].wait_recv()
        cores[k, 1, 1, 1].start()

    own(0)
    own(1)
    diag(0)
    own(2)
    diag(1)
    corner(0)
    own(3)
    diag(2)
    corner(1)
    diag(3)
    corner(2)
    corner(3)
    mine.wait()
    for k in range(GRID_Z):
        zn = near(k)
        for side, came, more, mate in (
            (0, zn <= me.z, me.has_above, me.above),
            (1, zn >= me.z, me.has_below, me.below),
        ):
            copy = z_copy(k, src if k == 0 else at(k, 0, 0, 0), side, mate)

            @pl.when(came)
            def _():
                @pl.when(more)
                def _():
                    copy.wait_send()
        for copy in (xs[k], ys[k], dxs[k], dys[k]):
            copy.wait_send()
    for copy in cores.values():
        copy.wait()


def gather_all(value, collective_id):
    devices = lax.axis_size("dp") * lax.axis_size("tensor")
    rows, width = value.shape
    dma = pltpu.SemaphoreType.DMA
    return pl.pallas_call(
        gather_kernel,
        out_shape=jax.ShapeDtypeStruct((devices, rows, width), value.dtype),
        in_specs=[pl.BlockSpec(memory_space=pl.ANY)],
        out_specs=pl.BlockSpec(memory_space=pl.ANY),
        scratch_shapes=[
            dma(()),
            dma((2, 2, 4)),
            dma((2, 4)),
            dma((2, 4)),
            dma((2, 4)),
            dma((2, 4)),
            dma((2, 4, 5)),
        ],
        compiler_params=pltpu.CompilerParams(collective_id=collective_id, has_side_effects=True),
    )(value).reshape(devices * rows, width)


WINDOW_ALIGN = 16
EXPERT_VMEM = 60 * 1024 * 1024


def dot(left, right, dims=((1,), (0,))):
    return lax.dot_general(left, right, (dims, ((), ())), preferred_element_type=jnp.float32)


def expert_kernel(
    info, pos, rows_in, cots_in, gate_w, up_w, down_w,
    out, back, gate_g, up_g, down_g,
    x, dy, wgu, wd, slot_out, slot_row, gu, hg, rows_b, cots_b, g_stage, d_stage,
    load_s, w_s, out_s, g_s, d_s,
):
    bf16, f32 = jnp.bfloat16, jnp.float32
    blocks, block_rows, wide = rows_in.shape
    features = cots_in.shape[2]
    experts, padded = x.shape[0], x.shape[1]
    part = hg.shape[2]
    cap = hg.shape[1]
    window = padded - cap
    tile = 256
    chunk = 512

    def load(b):
        slot = b % 2
        return (
            pltpu.make_async_copy(rows_in.at[b], rows_b.at[slot], load_s.at[slot, 0]),
            pltpu.make_async_copy(cots_in.at[b], cots_b.at[slot], load_s.at[slot, 1]),
        )

    for copy in load(0):
        copy.start()
    weights = []
    for e in range(experts):
        weights.append(pltpu.make_async_copy(gate_w.at[e], wgu.at[e, :, pl.ds(0, part)], w_s.at[e, 0]))
        weights.append(pltpu.make_async_copy(up_w.at[e], wgu.at[e, :, pl.ds(part, part)], w_s.at[e, 1]))
        weights.append(pltpu.make_async_copy(down_w.at[e], wd.at[e], w_s.at[e, 2]))
    for copy in weights:
        copy.start()

    def clear(i, carry):
        at = pl.ds(pl.multiple_of(i * 16, 16), 16)
        for e in range(experts):
            x[e, at, :] = jnp.zeros((16, wide), bf16)
            dy[e, at, :] = jnp.zeros((16, features), bf16)
        return carry

    lax.fori_loop(0, padded // 16, clear, 0)
    for e in range(experts):
        slot_out[e, pl.ds(cap, window), :] = jnp.zeros((window, features), bf16)
        slot_row[e, pl.ds(cap, window), :] = jnp.zeros((window, wide), bf16)

    def starts(b):
        return [pl.multiple_of(info[1 + b * experts + e], WINDOW_ALIGN) for e in range(experts)]

    def picks(b, begin):
        slots = lax.broadcasted_iota(jnp.int32, (window, block_rows), 0)
        return jnp.concatenate(
            [(slots + begin[e] == pos[b, pl.ds(e, 1), :]).astype(f32) for e in range(experts)],
            axis=0,
        )

    def take(b, carry):
        slot = b % 2

        @pl.when(b + 1 < blocks)
        def _():
            for copy in load(b + 1):
                copy.start()

        begin = starts(b)
        picked = picks(b, begin).astype(bf16)
        for copy in load(b):
            copy.wait()
        for source, target, width in ((rows_b, x, wide), (cots_b, dy, features)):
            for first in range(0, width, chunk):
                cols = pl.ds(first, min(chunk, width - first))
                got = dot(picked, source[slot, :, cols]).astype(bf16)
                for e in range(experts):
                    at = pl.ds(begin[e], window)
                    target[e, at, cols] += got[e * window : (e + 1) * window]
        return carry

    lax.fori_loop(0, blocks, take, 0)
    for copy in weights:
        copy.wait()

    lanes = lax.broadcasted_iota(jnp.int32, (tile, AUX), 1)

    def mlp(step, carry):
        e = step // (cap // tile)
        at = pl.ds(pl.multiple_of((step % (cap // tile)) * tile, tile), tile)
        own = info[0] * experts + e
        total = blocks * experts
        aux = x[e, at, pl.ds(features, AUX)].astype(f32)
        gate = jnp.sum(
            jnp.where((lanes == own) | (lanes == own + total), aux, 0.0), axis=1, keepdims=True
        )
        pre = dot(x[e, at, pl.ds(0, features)], wgu[e])
        gate_pre, up_pre = pre[:, :part], pre[:, part:]
        sig = 1.0 / (1.0 + jnp.exp(-gate_pre))
        act = gate_pre * sig
        hidden = (act * up_pre).astype(bf16).astype(f32)
        gated = (hidden * gate).astype(bf16)
        hg[e, at, :] = gated
        down_cot = dot(dy[e, at, :], wd[e], ((1,), (1,)))
        slot_cot = jnp.sum(hidden * down_cot, axis=1, keepdims=True)
        hidden_cot = down_cot * gate
        gu[e, at, pl.ds(0, part)] = (
            hidden_cot * up_pre * sig * (1.0 + gate_pre * (1.0 - sig))
        ).astype(bf16)
        gu[e, at, pl.ds(part, part)] = (hidden_cot * act).astype(bf16)
        for first in range(0, features, chunk):
            cols = pl.ds(first, chunk)
            slot_out[e, at, cols] = dot(gated, wd[e, :, cols]).astype(bf16)
            slot_row[e, at, cols] = dot(
                gu[e, at, :], wgu[e, pl.ds(first, chunk), :], ((1,), (1,))
            ).astype(bf16)
        high = slot_cot.astype(bf16).astype(f32)
        place = info[1 + blocks * experts] * 2 * total + own * 2
        slot_row[e, at, pl.ds(features, AUX)] = jnp.where(
            lanes == place, high, jnp.where(lanes == place + 1, slot_cot - high, 0.0)
        ).astype(bf16)
        return carry

    lax.fori_loop(0, experts * (cap // tile), mlp, 0)

    def stored(b):
        slot = b % 2
        return (
            pltpu.make_async_copy(cots_b.at[slot], out.at[b], out_s.at[slot, 0]),
            pltpu.make_async_copy(rows_b.at[slot], back.at[b], out_s.at[slot, 1]),
        )

    def put(b, carry):
        slot = b % 2

        @pl.when(b >= 2)
        def _():
            for copy in stored(b - 2):
                copy.wait()

        begin = starts(b)
        spread = picks(b, begin).T.astype(bf16)
        for source, target, width in ((slot_out, cots_b, features), (slot_row, rows_b, wide)):
            for first in range(0, width, chunk):
                cols = pl.ds(first, min(chunk, width - first))
                held = jnp.concatenate(
                    [source[e, pl.ds(begin[e], window), cols] for e in range(experts)], axis=0
                )
                target[slot, :, cols] = dot(spread, held).astype(bf16)
        for copy in stored(b):
            copy.start()
        return carry

    lax.fori_loop(0, blocks, put, 0)

    tiles = features // tile

    def g_copies(step):
        slot = step % 2
        e, at = step // tiles, pl.ds(pl.multiple_of((step % tiles) * tile, tile), tile)
        return (
            pltpu.make_async_copy(g_stage.at[slot, :, pl.ds(0, part)], gate_g.at[e, at], g_s.at[slot, 0]),
            pltpu.make_async_copy(g_stage.at[slot, :, pl.ds(part, part)], up_g.at[e, at], g_s.at[slot, 1]),
        )

    def wide_grad(step, carry):
        slot = step % 2
        e, at = step // tiles, pl.ds(pl.multiple_of((step % tiles) * tile, tile), tile)

        @pl.when(step >= 2)
        def _():
            for copy in g_copies(step - 2):
                copy.wait()

        g_stage[slot] = dot(x[e, pl.ds(0, cap), at], gu[e], ((0,), (0,)))
        for copy in g_copies(step):
            copy.start()
        return carry

    lax.fori_loop(0, experts * tiles, wide_grad, 0)
    parts = features // chunk

    def d_copy(step):
        slot = step % 2
        e, at = step // parts, pl.ds(pl.multiple_of((step % parts) * chunk, chunk), chunk)
        return pltpu.make_async_copy(d_stage.at[slot], down_g.at[e, :, at], d_s.at[slot])

    def down_grad(step, carry):
        slot = step % 2
        e, at = step // parts, pl.ds(pl.multiple_of((step % parts) * chunk, chunk), chunk)

        @pl.when(step >= 2)
        def _():
            d_copy(step - 2).wait()

        d_stage[slot] = dot(hg[e], dy[e, pl.ds(0, cap), at], ((0,), (0,)))
        d_copy(step).start()
        return carry

    lax.fori_loop(0, experts * parts, down_grad, 0)
    for last in (2, 1):
        for copy in stored(blocks - last):
            copy.wait()
        for copy in g_copies(experts * tiles - last):
            copy.wait()
        d_copy(experts * parts - last).wait()


def expert_layer(info, pos, rows_in, cots_in, gate_w, up_w, down_w, capacity, most):
    bf16, f32 = jnp.bfloat16, jnp.float32
    blocks, block_rows, wide = rows_in.shape
    features = cots_in.shape[2]
    experts, part = gate_w.shape[0], gate_w.shape[2]
    padded = capacity + -(-most // WINDOW_ALIGN) * WINDOW_ALIGN + WINDOW_ALIGN
    dma = pltpu.SemaphoreType.DMA
    shape = jax.ShapeDtypeStruct
    anywhere = pl.BlockSpec(memory_space=pl.ANY)
    return pl.pallas_call(
        expert_kernel,
        out_shape=(
            shape((blocks, block_rows, features), bf16),
            shape((blocks, block_rows, wide), bf16),
            shape(gate_w.shape, f32),
            shape(up_w.shape, f32),
            shape(down_w.shape, f32),
        ),
        in_specs=[
            pl.BlockSpec(memory_space=pltpu.SMEM),
            pl.BlockSpec(memory_space=pltpu.VMEM),
        ]
        + [anywhere] * 5,
        out_specs=(anywhere,) * 5,
        scratch_shapes=[
            pltpu.VMEM((experts, padded, wide), bf16),
            pltpu.VMEM((experts, padded, features), bf16),
            pltpu.VMEM((experts, features, 2 * part), bf16),
            pltpu.VMEM((experts, part, features), bf16),
            pltpu.VMEM((experts, padded, features), bf16),
            pltpu.VMEM((experts, padded, wide), bf16),
            pltpu.VMEM((experts, capacity, 2 * part), bf16),
            pltpu.VMEM((experts, capacity, part), bf16),
            pltpu.VMEM((2, block_rows, wide), bf16),
            pltpu.VMEM((2, block_rows, features), bf16),
            pltpu.VMEM((2, 256, 2 * part), f32),
            pltpu.VMEM((2, part, 512), f32),
            dma((2, 2)),
            dma((experts, 3)),
            dma((2, 2)),
            dma((2, 2)),
            dma((2,)),
        ],
        compiler_params=pltpu.CompilerParams(vmem_limit_bytes=EXPERT_VMEM),
    )(info, pos, rows_in, cots_in, gate_w, up_w, down_w)


ATTENTION_VMEM = 60 * 1024 * 1024
SCORE_SCALE = HEAD_SIZE ** (-0.5)
def turn_tables(rows):
    frequency = np.exp(
        -math.log(rope_base) * np.arange(HEAD_SIZE // 2, dtype=np.float32) * (2.0 / HEAD_SIZE)
    ).astype(np.float32)
    angles = np.arange(rows, dtype=np.float32)[:, None] * frequency[None, :]
    cosine, sine = np.cos(angles), np.sin(angles)
    return (
        np.concatenate([cosine, cosine], axis=1).astype(np.float32),
        np.concatenate([-sine, sine], axis=1).astype(np.float32),
    )


def turn(value, cosine, sine):
    return value * cosine + pltpu.roll(value, HEAD_SIZE // 2, 1) * sine


def inverse_norm(value):
    return lax.rsqrt(jnp.mean(value * value, axis=-1, keepdims=True) + epsilon)


def meet_y(me):
    barrier = pltpu.get_barrier_semaphore()
    pl.semaphore_signal(barrier, 1, device_id=me.y_mate, device_id_type=pl.DeviceIdType.MESH)
    pl.semaphore_wait(barrier, 1)


def gain_rows(aux_t, experts, chunks):
    head = [aux_t[experts + 2 + i : experts + 3 + i, :] for i in range(2)]
    width = HEAD_SIZE
    heads = [sum(row[:, c * width : (c + 1) * width] for c in range(chunks)) for row in head]
    return aux_t[experts : experts + 1, :], aux_t[experts + 1 : experts + 2, :], *heads


def probabilities(query, key, allowed):
    scores = jnp.where(allowed, dot(query, key, ((1,), (1,))) * SCORE_SCALE, masked_score)
    spread = jnp.exp(scores - jnp.max(scores, axis=-1, keepdims=True))
    return spread / jnp.sum(spread, axis=-1, keepdims=True)


def allowed_pairs(live):
    rows = live.shape[1]
    later = lax.broadcasted_iota(jnp.int32, (rows, rows), 0)
    sooner = lax.broadcasted_iota(jnp.int32, (rows, rows), 1)
    return (sooner <= later) & (live[0:1, :] > 0.0)


OPENING_PLAN = (
    ("bx",), ("w", 0, 0), ("w", 1, 0), ("ay0",), ("a", 0), ("w", 2, 0), ("pair",), ("a", 1),
    ("b", 0, 0), ("wx", 1, 0), ("a", 2), ("ax", 0), ("w", 3, 0), ("wx", 0, 0), ("b", 1, 0),
    ("w", 0, 1), ("ax", 1), ("a", 3), ("wx", 2, 0), ("w", 1, 1), ("wx", 3, 0), ("ax", 2),
    ("prep",), ("w", 2, 1), ("b", 0, 1), ("b", 2, 0), ("wx", 0, 1), ("qkv",), ("h", 0),
    ("ax", 3), ("w", 3, 1), ("y", 0), ("b", 1, 1), ("h", 1), ("b", 2, 1), ("h", 2), ("b", 3, 0),
    ("wx", 1, 1), ("wx", 2, 1), ("h", 3), ("b", 3, 1), ("wx", 3, 1), ("y", 1), ("ctx",),
    ("ctx2",), ("y", 2), ("y", 3), ("fin",),
)


def opening_kernel(
    experts, qkv,
    w_src, d_src, x_src, live, chosen, cosine, sine,
    w_out, d_out, x_out,
    sent_o, residual_o, normed_o, raw_o, query_o, key_o, value_o, context_o,
    x, w, ctx, aux_w, normed, raw, query, key, value, context, att, got, residual, sent,
    local_s, pair_s, wz_s, wx_s, wc_s, az_s, ax_s, ay_s, bz_s, bx_s, by_s, dc_s,
    in_s, w_s, out_s, y_s,
):
    bf16, f32 = jnp.bfloat16, jnp.float32
    me = Place()
    half = d_src.shape[0] // 2
    low, high = pl.ds(0, half), pl.ds(half, half)
    width = w_src.shape[1]
    first_cols = qkv + AUX
    columns = (pl.ds(0, first_cols), pl.ds(first_cols, width - first_cols))
    waits, sent_on = [], []

    def near(k):
        return me.farthest(GRID_Z - 1 - k)

    def w_at(k, fx, p):
        return w_out.at[me.dp_at(near(k), fx, 0), :, columns[p]]

    def d_at(k, fx, fy, rows):
        return d_out.at[me.dp_at(near(k), fx, 0) * 2 + me.y_at(fy), rows]

    for i, (source, target) in enumerate(
        (
            (w_src, w_out.at[me.dp]),
            (d_src, d_out.at[me.dp * 2 + me.y]),
            (x_src, x_out.at[me.y]),
        )
    ):
        copy = pltpu.make_async_copy(source, target, local_s.at[i])
        copy.start()
        waits.append(copy)
    me.greet()

    def line(k, source, target, sem, start_only):
        zn = near(k)
        for side, came, more, mate in (
            (0, zn < me.z, me.has_above, me.above),
            (1, zn > me.z, me.has_below, me.below),
        ):
            copy = remote(source, target, sem.at[0, side, zn], sem.at[1, side, zn], mate)
            if start_only:

                @pl.when(more)
                def _():
                    copy.start()
            else:

                @pl.when(came)
                def _():
                    copy.wait_recv()

                    @pl.when(more)
                    def _():
                        copy.start()

    def line_done(k, source, target, sem):
        zn = near(k)
        for side, came, more, mate in (
            (0, zn <= me.z, me.has_above, me.above),
            (1, zn >= me.z, me.has_below, me.below),
        ):
            copy = remote(source, target, sem.at[0, side, zn], sem.at[1, side, zn], mate)

            @pl.when(came)
            def _():
                @pl.when(more)
                def _():
                    copy.wait_send()

    def w_source(k, p):
        return w_src.at[:, columns[p]] if k == 0 else w_at(k, 0, p)

    def d_source(k, rows):
        return d_src.at[rows] if k == 0 else d_at(k, 0, 0, rows)

    def go(source, target, sem, index, mate):
        copy = remote(source, target, sem.at[(0, *index)], sem.at[(1, *index)], mate)
        copy.start()
        sent_on.append(copy)
        return copy

    def to_core(source, target, sem, index):
        go(source, target, sem, index, me.sibling)

    wx, ax, ay, by = {}, {}, {}, {}

    def w_own(k, p):
        line(k, w_source(k, p), w_at(k, 0, p), wz_s.at[p], k == 0)
        wx[k, p] = go(w_source(k, p), w_at(k, 0, p), wx_s, (k, p), me.x_mate)
        to_core(w_source(k, p), w_at(k, 0, p), wc_s, (k, 0, p))

    def w_across(k, p):
        wx[k, p].wait_recv()
        to_core(w_at(k, 1, p), w_at(k, 1, p), wc_s, (k, 1, p))

    def w_from_core(k, p):
        for fx in range(2):
            block = w_at(k, fx, p)
            remote(block, block, wc_s.at[0, k, fx, p], wc_s.at[1, k, fx, p], me.sibling).wait_recv()

    def a_over_y(k):
        ay[k, 0] = go(d_source(k, low), d_at(k, 0, 0, low), ay_s, (k, 0), me.y_mate)

    def a_own(k):
        line(k, d_source(k, low), d_at(k, 0, 0, low), az_s, k == 0)
        if k:
            a_over_y(k)
        ax[k] = go(d_source(k, low), d_at(k, 0, 0, low), ax_s, (k,), me.x_mate)
        to_core(d_source(k, low), d_at(k, 0, 0, low), dc_s, (k, 0, 0, 0))

    def a_across(k):
        ax[k].wait_recv()
        block = d_at(k, 1, 0, low)
        ay[k, 1] = go(block, block, ay_s, (k, 1), me.y_mate)
        to_core(block, block, dc_s, (k, 1, 0, 0))

    def b_own(k, fx):
        source = d_source(k, high) if fx == 0 else d_at(k, 1, 0, high)
        block = d_at(k, fx, 0, high)
        line(k, source, block, bz_s.at[fx], k == 0)
        by[k, fx] = go(source, block, by_s, (k, fx), me.y_mate)
        to_core(source, block, dc_s, (k, fx, 0, 1))

    def y_done(k):
        for fx in range(2):
            for h, (copies, rows) in enumerate(((ay, low), (by, high))):
                copies[k, fx].wait_recv()
                block = d_at(k, fx, 1, rows)
                to_core(block, block, dc_s, (k, fx, 1, h))

    rows, features = x.shape[0] * x.shape[1], x.shape[2]
    own_rows = rows // 2
    heads, key_heads = query.shape[0], key.shape[0]
    chunk = 512
    mine = pl.ds(pl.multiple_of(me.y * own_rows, own_rows), own_rows)
    theirs = pl.ds(pl.multiple_of((1 - me.y) * own_rows, own_rows), own_rows)
    turn_c, turn_s = cosine[...], sine[...]
    held, outs, copies = {}, [], []

    def pair_rows():
        held["pair"] = go(x_src, x_out.at[me.y], pair_s, (0,), me.y_mate)

    def b_over_x():
        held["bx"] = go(d_src.at[high], d_at(0, 0, 0, high), bx_s, (0,), me.x_mate)

    def b_step(k, fx):
        if (k, fx) == (0, 1):
            held["bx"].wait_recv()
        b_own(k, fx)

    def prepare():
        held["pair"].wait_recv()
        waits[2].wait()
        for k in range(GRID_Z):
            w_from_core(k, 0)
        waits[0].wait()
        loads = [
            pltpu.make_async_copy(w_out.at[:, :, pl.ds(qkv, AUX)], aux_w, in_s.at[1]),
            pltpu.make_async_copy(x_out, x, in_s.at[0]),
        ]
        held["parts"] = [
            pltpu.make_async_copy(
                w_out.at[:, :, pl.ds(c * chunk, chunk)],
                w.at[:, :, pl.ds(c * chunk, chunk)],
                w_s.at[c],
            )
            for c in range(qkv // chunk)
        ]
        for copy in loads + held["parts"]:
            copy.start()
        loads[0].wait()
        aux_t = aux_w[...].reshape(features, AUX).astype(f32).T
        held["gains"] = gain_rows(aux_t, experts, features // HEAD_SIZE)
        gain_one = held["gains"][0]
        loads[1].wait()

        def one(i, carry):
            at = pl.ds(pl.multiple_of(i * 32, 32), 32)
            for part in range(2):
                stream = x[part, at, :].astype(f32)
                there = pl.ds(pl.multiple_of(part * own_rows + i * 32, 32), 32)
                normed[there, :] = (stream * inverse_norm(stream) * gain_one).astype(bf16)
            return carry

        lax.fori_loop(0, own_rows // 32, one, 0)

    def project():
        for c, copy in enumerate(held["parts"]):
            copy.wait()
            cols = slice(c * chunk, (c + 1) * chunk)
            got_raw = dot(normed[...], w[:, :, cols].reshape(features, chunk))
            for h in range(chunk // HEAD_SIZE):
                raw[c * (chunk // HEAD_SIZE) + h] = got_raw[:, h * HEAD_SIZE : (h + 1) * HEAD_SIZE]
        for g in range(key_heads):
            unnormed = raw[heads + g]
            gained = unnormed * inverse_norm(unnormed) * held["gains"][3]
            key[g] = turn(gained, turn_c, turn_s).astype(bf16)
            value[g] = raw[heads + key_heads + g].astype(bf16)

    def attend(part):
        allowed = allowed_pairs(live[...])
        query_gain = held["gains"][2]

        def head(h, carry):
            g = h // (heads // key_heads)
            unnormed = raw[h]
            gained = unnormed * inverse_norm(unnormed) * query_gain
            turned = turn(gained, turn_c, turn_s).astype(bf16)
            query[h] = turned
            probs = probabilities(turned, key[g], allowed).astype(bf16)
            at = pl.ds(pl.multiple_of(h * HEAD_SIZE, HEAD_SIZE), HEAD_SIZE)
            context[:, at] = dot(probs, value[g]).astype(bf16)
            return carry

        share = heads // 4
        lax.fori_loop(part * share, (part + 1) * share, head, 0)

    def save(pairs):
        for source, target in pairs:
            copy = pltpu.make_async_copy(source, target, out_s.at[len(outs)])
            copy.start()
            outs.append(copy)

    def ctx_part(c):
        span = chunk // ctx.shape[1]
        return ctx[c * span : (c + 1) * span].reshape(chunk, ctx.shape[2])

    def output_over_y():
        save(
            (
                (normed, normed_o), (raw, raw_o), (query, query_o), (key, key_o),
                (value, value_o), (context, context_o),
            )
        )
        for k in range(GRID_Z):
            w_from_core(k, 1)
        load = pltpu.make_async_copy(w_out.at[:, :, columns[1]], ctx, in_s.at[2])
        load.start()
        load.wait()
        for c in range(features // chunk):
            cols = pl.ds(c * chunk, chunk)
            att[:, cols] = dot(context[theirs, :], ctx_part(c), ((1,), (1,))).astype(bf16)
            copy = remote(att.at[:, cols], got.at[:, cols], y_s.at[0, c], y_s.at[1, c], me.y_mate)
            copy.start()
            copies.append(copy)

    def output_own():
        for c in range(features // chunk):
            residual[:, pl.ds(c * chunk, chunk)] = dot(context[mine, :], ctx_part(c), ((1,), (1,)))

    def finish():
        for copy in copies:
            copy.wait_recv()
        gain_two = held["gains"][1]

        def second_norm(i, carry):
            at = pl.ds(pl.multiple_of(i * 16, 16), 16)
            total = x[me.y, at, :].astype(f32) + (residual[at, :] + got[at, :].astype(f32))
            residual[at, :] = total
            sent[at, pl.ds(0, features)] = (total * inverse_norm(total) * gain_two).astype(bf16)
            return carry

        lax.fori_loop(0, own_rows // 16, second_norm, 0)
        logits = dot(sent[:, :features], aux_w[...].reshape(features, AUX))
        picked = chosen[...] > 0.0
        logits = jnp.where(picked, logits, masked_score)
        spread = jnp.where(picked, jnp.exp(logits - jnp.max(logits, axis=-1, keepdims=True)), 0.0)
        gates = spread / jnp.sum(spread, axis=-1, keepdims=True)
        coarse = gates.astype(bf16).astype(f32)
        sent[:, pl.ds(features, AUX)] = (coarse + pltpu.roll(gates - coarse, experts, 1)).astype(bf16)
        save(((sent, sent_o), (residual, residual_o)))

    actions = {
        "pair": pair_rows, "bx": b_over_x, "ay0": lambda: a_over_y(0), "w": w_own, "wx": w_across,
        "a": a_own, "ax": a_across, "b": b_step, "y": y_done, "prep": prepare, "qkv": project,
        "h": attend, "ctx": output_over_y, "ctx2": output_own, "fin": finish,
    }
    for name, *which in OPENING_PLAN:
        actions[name](*which)
    for k in range(GRID_Z):
        for p in range(2):
            line_done(k, w_source(k, p), w_at(k, 0, p), wz_s.at[p])
        line_done(k, d_source(k, low), d_at(k, 0, 0, low), az_s)
        line_done(k, d_source(k, high), d_at(k, 0, 0, high), bz_s.at[0])
        line_done(k, d_at(k, 1, 0, high), d_at(k, 1, 0, high), bz_s.at[1])
    for copy in sent_on + copies:
        copy.wait_send()
    for k in range(GRID_Z):
        for fx in range(2):
            for fy in range(2):
                for h, at in enumerate((low, high)):
                    block = d_at(k, fx, fy, at)
                    remote(
                        block, block, dc_s.at[0, k, fx, fy, h], dc_s.at[1, k, fx, fy, h], me.sibling
                    ).wait_recv()
    waits[1].wait()
    for copy in outs:
        copy.wait()


def opening(
    weights, cotangents, inputs, live, chosen, experts, heads, key_heads, collective_id
):
    bf16, f32 = jnp.bfloat16, jnp.float32
    chips, pair = lax.axis_size("dp"), lax.axis_size("tensor")
    own_rows, features = inputs.shape
    rows = pair * own_rows
    shard = weights.shape[0]
    wide = heads * HEAD_SIZE
    qkv = (heads + 2 * key_heads) * HEAD_SIZE
    cosine, sine = turn_tables(rows)
    dma = pltpu.SemaphoreType.DMA
    shapes = (
        ((chips, *weights.shape), bf16),
        ((chips * pair, *cotangents.shape), bf16),
        ((pair, *inputs.shape), bf16),
        ((own_rows, features + AUX), bf16),
        ((own_rows, features), f32),
        ((rows, features), bf16),
        ((heads + 2 * key_heads, rows, HEAD_SIZE), f32),
        ((heads, rows, HEAD_SIZE), bf16),
        ((key_heads, rows, HEAD_SIZE), bf16),
        ((key_heads, rows, HEAD_SIZE), bf16),
        ((rows, wide), bf16),
    )
    anywhere, vmem = pl.BlockSpec(memory_space=pl.ANY), pl.BlockSpec(memory_space=pltpu.VMEM)
    w, d, x, *rest = pl.pallas_call(
        functools.partial(opening_kernel, experts, qkv),
        out_shape=tuple(jax.ShapeDtypeStruct(*shape) for shape in shapes),
        in_specs=[anywhere] * 3 + [vmem] * 4,
        out_specs=(anywhere,) * len(shapes),
        scratch_shapes=[
            pltpu.VMEM((pair, own_rows, features), bf16),
            pltpu.VMEM((chips, shard, qkv), bf16),
            pltpu.VMEM((chips, shard, wide), bf16),
            pltpu.VMEM((chips, shard, AUX), bf16),
            pltpu.VMEM((rows, features), bf16),
            pltpu.VMEM((heads + 2 * key_heads, rows, HEAD_SIZE), f32),
            pltpu.VMEM((heads, rows, HEAD_SIZE), bf16),
            pltpu.VMEM((key_heads, rows, HEAD_SIZE), bf16),
            pltpu.VMEM((key_heads, rows, HEAD_SIZE), bf16),
            pltpu.VMEM((rows, wide), bf16),
            pltpu.VMEM((own_rows, features), bf16),
            pltpu.VMEM((own_rows, features), bf16),
            pltpu.VMEM((own_rows, features), f32),
            pltpu.VMEM((own_rows, features + AUX), bf16),
            dma((3,)),
            dma((2, 1)),
            dma((2, 2, 2, 4)),
            dma((2, 4, 2)),
            dma((2, 4, 2, 2)),
            dma((2, 2, 4)),
            dma((2, 4)),
            dma((2, 4, 2)),
            dma((2, 2, 2, 4)),
            dma((2, 1)),
            dma((2, 4, 2)),
            dma((2, 4, 2, 2, 2)),
            dma((3,)),
            dma((qkv // 512,)),
            dma((8,)),
            dma((2, features // 512)),
        ],
        compiler_params=pltpu.CompilerParams(
            collective_id=collective_id, has_side_effects=True, vmem_limit_bytes=ATTENTION_VMEM
        ),
    )(weights, cotangents, inputs, live, chosen, cosine, sine)
    return (
        w.reshape(-1, w.shape[2]),
        d.reshape(chips, -1, d.shape[2]),
        x.reshape(-1, x.shape[2]),
        *rest,
    )


def unturn(value, cosine, sine):
    return value * cosine - pltpu.roll(value, HEAD_SIZE // 2, 1) * sine


def backward_kernel(
    experts, back_in, residual_in, sent_in, dy_in, x_in, packed, live, cosine, sine, normed_in,
    raw_in, query_in, key_in, value_in, context_in,
    grads, input_gradient,
    back, residual, sent, dy, x, w, ctx, aux_w, normed, raw, query, key, value, context,
    cot, context_cot, raw_cot, key_sum, value_sum, small, first, first_got, stage, result,
    in_s, out_s, y_s, g_s,
):
    bf16, f32 = jnp.bfloat16, jnp.float32
    me = Place()
    own_rows, features = residual.shape
    rows = 2 * own_rows
    heads, key_heads = query.shape[0], key.shape[0]
    group = heads // key_heads
    qkv, wide = w.shape[1], heads * HEAD_SIZE
    chunk = 512
    mine = pl.ds(pl.multiple_of(me.y * own_rows, own_rows), own_rows)
    theirs = pl.ds(pl.multiple_of((1 - me.y) * own_rows, own_rows), own_rows)
    loads = [
        pltpu.make_async_copy(source, target, in_s.at[i])
        for i, (source, target) in enumerate(
            (
                (packed.at[:, pl.ds(qkv, AUX)], aux_w),
                (back_in, back),
                (sent_in, sent),
                (residual_in, residual),
                (dy_in, dy),
                (packed.at[:, pl.ds(qkv + AUX, wide)], ctx),
                (context_in, context),
                (value_in, value),
                (key_in, key),
                (query_in, query),
                (raw_in, raw),
                (packed.at[:, pl.ds(0, qkv)], w),
                (normed_in, normed),
                (x_in, x),
            )
        )
    ]
    for copy in loads:
        copy.start()
    meet_y(me)
    for copy in loads[:5]:
        copy.wait()
    aux_t = aux_w[...].astype(f32).T
    gain_one, gain_two, query_gain, key_gain = gain_rows(aux_t, experts, features // HEAD_SIZE)

    lane = lax.broadcasted_iota(jnp.int32, (own_rows, AUX), 1)
    coded = sent[:, features:].astype(f32)
    gates = coded + pltpu.roll(coded, AUX - experts, 1)
    gates = jnp.where(lane < experts, gates, 0.0)
    column = lax.broadcasted_iota(jnp.int32, (AUX, AUX), 0)
    target = lax.broadcasted_iota(jnp.int32, (AUX, AUX), 1)
    fold = ((column % (2 * experts)) // 2 == target).astype(bf16)
    gate_cot = dot(back[:, features:], fold)
    logit_cot = gates * (gate_cot - jnp.sum(gates * gate_cot, axis=-1, keepdims=True))
    logit_cot = logit_cot.astype(bf16)
    small[...] = dot(sent[:, :features], logit_cot, ((0,), (0,)))
    midnorm = jnp.zeros((1, features), f32)
    step = 32
    for i in range(own_rows // step):
        at = slice(i * step, (i + 1) * step)
        total = residual[at, :]
        scale = inverse_norm(total)
        unit = total * scale
        normed_cot = back[at, :features].astype(f32) + dot(
            logit_cot[at, :], aux_w[...], ((1,), (1,))
        )
        midnorm = midnorm + jnp.sum(normed_cot * unit, axis=0, keepdims=True)
        gained = normed_cot * gain_two
        total_cot = dy[at, :].astype(f32) + scale * (
            gained - unit * jnp.mean(gained * unit, axis=-1, keepdims=True)
        )
        residual[at, :] = total_cot
        cot[pl.ds(pl.multiple_of(me.y * own_rows + i * step, step), step), :] = total_cot.astype(bf16)
    swap = remote(cot.at[mine], cot.at[mine], y_s.at[0, 0], y_s.at[1, 0], me.y_mate)
    swap.start()
    for copy in loads[5:10]:
        copy.wait()

    def spread_context(part):
        for c in range(wide // chunk):
            cols = pl.ds(c * chunk, chunk)
            context_cot[part, cols] = dot(cot[part, :], ctx[:, cols]).astype(bf16)

    spread_context(mine)
    swap.wait_recv()
    spread_context(theirs)
    for copy in loads[10:]:
        copy.wait()

    turn_c, turn_s = cosine[...], sine[...]
    allowed = allowed_pairs(live[...])
    key_sum[...] = jnp.zeros_like(key_sum)
    value_sum[...] = jnp.zeros_like(value_sum)

    def raw_back(back_rows, unnormed, gain):
        scale = inverse_norm(unnormed)
        unit = unnormed * scale
        part = jnp.sum(back_rows * unit, axis=0, keepdims=True)
        gained = back_rows * gain
        raw_rows = scale * (gained - unit * jnp.mean(gained * unit, axis=-1, keepdims=True))
        return raw_rows.astype(bf16), part

    def head(h, query_part):
        g = h // group
        at = pl.ds(pl.multiple_of(h * HEAD_SIZE, HEAD_SIZE), HEAD_SIZE)
        probs = probabilities(query[h], key[g], allowed)
        cots = context_cot[:, at]
        prob_cot = dot(cots, value[g], ((1,), (1,)))
        score_cot = probs * (prob_cot - jnp.sum(probs * prob_cot, axis=-1, keepdims=True))
        score_cot = score_cot.astype(bf16)
        value_sum[g] += dot(probs.astype(bf16), cots, ((0,), (0,)))
        key_sum[g] += dot(score_cot, query[h], ((0,), (0,)))
        turned = dot(score_cot, key[g]) * SCORE_SCALE
        raw_cot[:, at], part = raw_back(unturn(turned, turn_c, turn_s), raw[h], query_gain)
        return query_part + part

    query_part = lax.fori_loop(0, heads, head, jnp.zeros((1, HEAD_SIZE), f32))
    key_part = jnp.zeros((1, HEAD_SIZE), f32)
    for g in range(key_heads):
        turned = key_sum[g] * SCORE_SCALE
        at = wide + g * HEAD_SIZE
        raw_cot[:, at : at + HEAD_SIZE], part = raw_back(
            unturn(turned, turn_c, turn_s), raw[heads + g], key_gain
        )
        key_part = key_part + part
        at = at + key_heads * HEAD_SIZE
        raw_cot[:, at : at + HEAD_SIZE] = value_sum[g].astype(bf16)

    copies = []
    for c in range(features // chunk):
        cols = pl.ds(c * chunk, chunk)
        first[:, cols] = dot(raw_cot[theirs, :], w[cols, :], ((1,), (1,))).astype(bf16)
        copy = remote(
            first.at[:, cols], first_got.at[:, cols], y_s.at[0, 1 + c], y_s.at[1, 1 + c], me.y_mate
        )
        copy.start()
        copies.append(copy)
    block = 256

    def store(i):
        slot = i % 2
        return pltpu.make_async_copy(
            stage.at[slot],
            grads.at[pl.ds(pl.multiple_of(i * block, block), block), pl.ds(0, qkv + wide)],
            g_s.at[slot],
        )

    def weight_grads(i, carry):
        slot = i % 2
        at = pl.ds(pl.multiple_of(i * block, block), block)

        @pl.when(i >= 2)
        def _():
            store(i - 2).wait()

        for c in range(qkv // chunk):
            cols = pl.ds(c * chunk, chunk)
            stage[slot, :, cols] = dot(normed[:, at], raw_cot[:, cols], ((0,), (0,))).astype(bf16)
        for c in range(wide // chunk):
            cols = pl.ds(c * chunk, chunk)
            stage[slot, :, pl.ds(qkv + c * chunk, chunk)] = dot(
                cot[:, at], context[:, cols], ((0,), (0,))
            ).astype(bf16)
        store(i).start()
        return carry

    lax.fori_loop(0, features // block, weight_grads, 0)
    prenorm = jnp.zeros((1, features), f32)
    for copy in copies:
        copy.wait_recv()
    for c in range(features // chunk):
        cols = pl.ds(c * chunk, chunk)
        back_cols = dot(raw_cot[mine, :], w[cols, :], ((1,), (1,)))
        result_part = back_cols + first_got[:, cols].astype(f32)
        back[:, cols] = result_part.astype(bf16)
    step = 32
    for i in range(own_rows // step):
        at = slice(i * step, (i + 1) * step)
        stream = x[pl.ds(pl.multiple_of(me.y * own_rows + i * step, step), step), :].astype(f32)
        scale = inverse_norm(stream)
        unit = stream * scale
        first_cot = back[at, :features].astype(f32)
        prenorm = prenorm + jnp.sum(first_cot * unit, axis=0, keepdims=True)
        gained = first_cot * gain_one
        result[at, :] = (
            residual[at, :]
            + scale * (gained - unit * jnp.mean(gained * unit, axis=-1, keepdims=True))
        ).astype(bf16)
    done = pltpu.make_async_copy(result, input_gradient, out_s.at[0])
    done.start()
    chunks = features // HEAD_SIZE
    extra = jnp.concatenate(
        [
            jnp.zeros((experts, features), f32),
            prenorm,
            midnorm,
            jnp.concatenate([query_part] * chunks, axis=1),
            jnp.concatenate([key_part] * chunks, axis=1),
            jnp.zeros((AUX - experts - 4, features), f32),
        ],
        axis=0,
    )
    aux_w[...] = (small[...] + extra.T).astype(bf16)
    last = pltpu.make_async_copy(aux_w, grads.at[:, pl.ds(qkv + wide, AUX)], out_s.at[1])
    last.start()
    swap.wait_send()
    for copy in copies:
        copy.wait_send()
    for i in (2, 1):
        store(features // block - i).wait()
    done.wait()
    last.wait()


def attention_backward(
    back, residual, sent, dy, x_pair, packed, live, saved, experts, collective_id
):
    bf16, f32 = jnp.bfloat16, jnp.float32
    normed, raw, query, key, value, context = saved
    own_rows, features = residual.shape
    rows = 2 * own_rows
    heads, key_heads = query.shape[0], key.shape[0]
    wide = heads * HEAD_SIZE
    qkv = wide + 2 * key_heads * HEAD_SIZE
    cosine, sine = turn_tables(rows)
    dma = pltpu.SemaphoreType.DMA
    anywhere, vmem = pl.BlockSpec(memory_space=pl.ANY), pl.BlockSpec(memory_space=pltpu.VMEM)
    return pl.pallas_call(
        functools.partial(backward_kernel, experts),
        out_shape=(
            jax.ShapeDtypeStruct((features, qkv + wide + AUX), bf16),
            jax.ShapeDtypeStruct((own_rows, features), bf16),
        ),
        in_specs=[anywhere] * 6 + [vmem] * 3 + [anywhere] * 6,
        out_specs=(anywhere,) * 2,
        scratch_shapes=[
            pltpu.VMEM((own_rows, features + AUX), bf16),
            pltpu.VMEM((own_rows, features), f32),
            pltpu.VMEM((own_rows, features + AUX), bf16),
            pltpu.VMEM((own_rows, features), bf16),
            pltpu.VMEM((rows, features), bf16),
            pltpu.VMEM((features, qkv), bf16),
            pltpu.VMEM((features, wide), bf16),
            pltpu.VMEM((features, AUX), bf16),
            pltpu.VMEM((rows, features), bf16),
            pltpu.VMEM((heads + 2 * key_heads, rows, HEAD_SIZE), f32),
            pltpu.VMEM((heads, rows, HEAD_SIZE), bf16),
            pltpu.VMEM((key_heads, rows, HEAD_SIZE), bf16),
            pltpu.VMEM((key_heads, rows, HEAD_SIZE), bf16),
            pltpu.VMEM((rows, wide), bf16),
            pltpu.VMEM((rows, features), bf16),
            pltpu.VMEM((rows, wide), bf16),
            pltpu.VMEM((rows, qkv), bf16),
            pltpu.VMEM((key_heads, rows, HEAD_SIZE), f32),
            pltpu.VMEM((key_heads, rows, HEAD_SIZE), f32),
            pltpu.VMEM((features, AUX), f32),
            pltpu.VMEM((own_rows, features), bf16),
            pltpu.VMEM((own_rows, features), bf16),
            pltpu.VMEM((2, 256, qkv + wide), bf16),
            pltpu.VMEM((own_rows, features), bf16),
            dma((14,)),
            dma((2,)),
            dma((2, 1 + features // 512)),
            dma((2,)),
        ],
        compiler_params=pltpu.CompilerParams(
            collective_id=collective_id, has_side_effects=True, vmem_limit_bytes=ATTENTION_VMEM
        ),
    )(
        back, residual, sent, dy, x_pair, packed, live, cosine, sine,
        normed, raw, query, key, value, context,
    )


LAST_CUT = 5
LAST_PLAN = (
    ("gx", 0, 0), ("dy", 0, 1, 1), ("gx", 0, 1), ("dy", 0, 0, 1), ("dy", 1, 1, 1), ("db", 0, 1),
    ("gx", 1, 1), ("db", 0, 0), ("dy", 2, 1, 1), ("dy", 1, 1, 0), ("gx", 1, 0), ("db", 1, 1),
    ("dy", 2, 1, 0), ("gx", 2, 0), ("db", 2, 1), ("dy", 0, 1, 0), ("dy", 2, 0, 1),
    ("dy", 0, 0, 0), ("dy", 3, 1, 1), ("gc", 0), ("dy", 1, 0, 0), ("dy", 1, 0, 1),
    ("dy", 3, 1, 0), ("dy", 2, 0, 0), ("gx", 2, 1), ("dax", 2), ("dax", 0), ("dax", 1),
    ("gc", 1), ("gc", 2), ("gx", 3, 0), ("dy", 3, 0, 1), ("gx", 3, 1), ("da", 0), ("dax", 3),
    ("dy", 3, 0, 0), ("db", 1, 0), ("da", 1), ("db", 2, 0), ("da", 2), ("gc", 3), ("sm",),
    ("db", 3, 1), ("db", 3, 0), ("sm2",), ("da", 3), ("bx",),
)


def last_scatter_kernel(
    g_part, d_part, g_out, d_out,
    g_own, g_core, g_x, g_z, d_own, d_core, d_y, a_x, b_x, a_z, b_z, small_got,
    gl_s, gc_s, gx_s, gz_s, dl_s, dc_s, dy_s, ax_s, bx_s, az_s, bz_s, small_s, out_s,
):
    me = Place()
    g_rows, d_rows = g_own.shape[2], d_own.shape[3]
    cut, g_half = a_x.shape[1], g_rows // 2
    g_all, low, high = (0, g_rows), (0, cut), (cut, d_rows - cut)
    low_at, high_at = pl.ds(0, cut), pl.ds(cut, d_rows - cut)
    last = GRID_Z - 1
    loads, cores, sends = {}, {}, []

    def g_chunk(k, fx, fc):
        return g_part.at[me.dp_at(me.farthest(k), fx, fc)]

    def d_chunk(k, fx, fy, fc):
        return d_part.at[me.dp_at(me.farthest(k), fx, fc) * 2 + me.y_at(fy)]

    pairs = ((1, 1), (0, 1), (1, 0), (0, 0))
    for k in range(GRID_Z):
        for fx in (1, 0):
            loads[k, fx] = pltpu.make_async_copy(g_chunk(k, fx, 0), g_own.at[k, fx], gl_s.at[k, fx])
            loads[k, fx].start()
        for fx, fy in pairs:
            loads[k, fx, fy] = pltpu.make_async_copy(
                d_chunk(k, fx, fy, 0), d_own.at[k, fx, fy], dl_s.at[k, fx, fy]
            )
            loads[k, fx, fy].start()
    me.greet()
    for k in range(GRID_Z):
        for fx in (1, 0):
            cores[k, fx] = remote(
                g_chunk(k, fx, 1), g_core.at[k, fx],
                gc_s.at[0, k, fx], gc_s.at[1, k, fx], me.sibling,
            )
        for fx, fy in pairs:
            cores[k, fx, fy] = remote(
                d_chunk(k, fx, fy, 1), d_core.at[k, fx, fy],
                dc_s.at[0, k, fx, fy], dc_s.at[1, k, fx, fy], me.sibling,
            )
        for index in ((1,), (1, 1), (0, 1), (0,), (1, 0), (0, 0)):
            cores[(k, *index)].start()

    gx = [
        [
            remote(
                g_own.at[k, 1, pl.ds(h * g_half, g_half)], g_x.at[k, pl.ds(h * g_half, g_half)],
                gx_s.at[0, k, h], gx_s.at[1, k, h], me.x_mate,
            )
            for h in range(2)
        ]
        for k in range(GRID_Z)
    ]
    dy = {
        (k, fx, h): remote(
            d_own.at[k, fx, 1, at], d_y.at[k, fx, at],
            dy_s.at[0, k, fx, h], dy_s.at[1, k, fx, h], me.y_mate,
        )
        for k in range(GRID_Z)
        for fx in range(2)
        for h, at in enumerate((low_at, high_at))
    }
    ax = [
        remote(d_own.at[k, 1, 0, low_at], a_x.at[k], ax_s.at[0, k], ax_s.at[1, k], me.x_mate)
        for k in range(GRID_Z)
    ]
    bx = remote(d_own.at[last, 1, 0, high_at], b_x, bx_s.at[0], bx_s.at[1], me.x_mate)

    here = set()

    def arrive(*index):
        if index not in here:
            here.add(index)
            loads[index].wait()
            cores[index].wait_recv()

    def onward(source, buffer, sem, to, side, mate):
        ends = 1 - (me.z - 1 - to + GRID_Z - 1) // GRID_Z
        slot = to if side == 0 else to + (GRID_Z - to) * ends
        return remote(source, buffer.at[slot], sem.at[0, to], sem.at[1, slot], mate)

    def line(k, block, source, rows, buffer, sem, shift):
        to = me.farthest(k)
        for side, ahead, mate, more in (
            (0, to > me.z, me.above, me.has_below),
            (1, to < me.z, me.below, me.has_above),
        ):
            slot = to if k < last or side == 0 else GRID_Z
            came = remote(source, buffer.at[slot], sem.at[0, slot], sem.at[1, slot], mate)

            def gather(came=came, slot=slot):
                came.wait_recv()
                add_rows(block, [(buffer.at[slot], shift)], rows)

            if k < last:

                @pl.when(ahead)
                def _():
                    pl.when(more)(gather)
                    onward(source, buffer, sem, to, side, mate).start()
            else:
                pl.when(more)(gather)

    def line_done(k, source, buffer, sem):
        to = me.farthest(k)
        for side, ahead, mate in ((0, to > me.z, me.above), (1, to < me.z, me.below)):

            @pl.when(ahead)
            def _():
                onward(source, buffer, sem, to, side, mate).wait_send()

    width = g_own.shape[3]
    small_block = g_own.at[last, 0, :, pl.ds(width - AUX, AUX)]
    small = remote(small_block, small_got, small_s.at[0], small_s.at[1], me.y_mate)

    def g_across(k, h):
        arrive(k, 1)
        add_rows(g_own.at[k, 1], [(g_core.at[k, 1], 0)], (h * g_half, g_half))
        gx[k][h].start()

    def g_column(k):
        arrive(k, 0)
        for h in range(2):
            gx[k][h].wait_recv()
        add_rows(g_own.at[k, 0], [(g_core.at[k, 0], 0), (g_x.at[k], 0)], g_all)
        line(k, g_own.at[k, 0], g_own.at[k, 0], g_all, g_z, gz_s, 0)

    def over_y(k, fx, h):
        arrive(k, fx, 1)
        add_rows(d_own.at[k, fx, 1], [(d_core.at[k, fx, 1], 0)], (low, high)[h])
        dy[k, fx, h].start()

    def from_y(k, fx, h, *more):
        arrive(k, fx, 0)
        dy[k, fx, h].wait_recv()
        rest = [(d_core.at[k, fx, 0], 0), (d_y.at[k, fx], 0), *more]
        add_rows(d_own.at[k, fx, 0], rest, (low, high)[h])

    def b_line(k, fx):
        from_y(k, fx, 1)
        block = d_own.at[k, fx, 0]
        line(k, block, block.at[high_at], high, b_z.at[fx], bz_s.at[fx], cut)
        if fx and k == last:
            bx.start()

    def a_over_x(k):
        from_y(k, 1, 0)
        ax[k].start()

    def a_line(k):
        ax[k].wait_recv()
        from_y(k, 0, 0, (a_x.at[k], 0))
        block = d_own.at[k, 0, 0]
        line(k, block, block.at[low_at], low, a_z, az_s, 0)

    def b_from_x():
        bx.wait_recv()
        add_rows(d_own.at[last, 0, 0], [(b_x, cut)], high)

    def small_sum():
        small.wait()
        total = small_block[...].astype(jnp.float32) + small_got[...].astype(jnp.float32)
        small_block[...] = total.astype(small_got.dtype)

    actions = {
        "gx": g_across, "gc": g_column, "dy": over_y, "db": b_line, "dax": a_over_x, "da": a_line,
        "bx": b_from_x, "sm": small.start, "sm2": small_sum,
    }
    for name, *which in LAST_PLAN:
        actions[name](*which)
    outs = [
        pltpu.make_async_copy(d_own.at[last, 0, 0], d_out, out_s.at[0]),
        pltpu.make_async_copy(g_own.at[last, 0], g_out, out_s.at[1]),
    ]
    for copy in outs:
        copy.start()
    for k in range(GRID_Z):
        for h in range(2):
            gx[k][h].wait_send()
        for fx in range(2):
            for h in range(2):
                dy[k, fx, h].wait_send()
        ax[k].wait_send()
        if k < last:
            line_done(k, g_own.at[k, 0], g_z, gz_s)
            for fx in range(2):
                line_done(k, d_own.at[k, fx, 0, high_at], b_z.at[fx], bz_s.at[fx])
            line_done(k, d_own.at[k, 0, 0, low_at], a_z, az_s)
    bx.wait_send()
    for sent in cores.values():
        sent.wait_send()
    for copy in outs:
        copy.wait()


def last_scatter(grads, sums, collective_id):
    chips, pair = lax.axis_size("dp"), lax.axis_size("tensor")
    g_rows, g_wide = grads.shape[0] // chips, grads.shape[1]
    d_rows, d_wide = sums.shape[0] // (chips * pair), sums.shape[1]
    cut = d_rows * LAST_CUT // 8
    dma = pltpu.SemaphoreType.DMA
    low = grads.dtype
    anywhere = pl.BlockSpec(memory_space=pl.ANY)
    return pl.pallas_call(
        last_scatter_kernel,
        out_shape=(
            jax.ShapeDtypeStruct((g_rows, g_wide), low),
            jax.ShapeDtypeStruct((d_rows, d_wide), low),
        ),
        in_specs=[anywhere] * 2,
        out_specs=(anywhere,) * 2,
        scratch_shapes=[
            pltpu.VMEM((4, 2, g_rows, g_wide), low),
            pltpu.VMEM((4, 2, g_rows, g_wide), low),
            pltpu.VMEM((4, g_rows, g_wide), low),
            pltpu.VMEM((5, g_rows, g_wide), low),
            pltpu.VMEM((4, 2, 2, d_rows, d_wide), low),
            pltpu.VMEM((4, 2, 2, d_rows, d_wide), low),
            pltpu.VMEM((4, 2, d_rows, d_wide), low),
            pltpu.VMEM((4, cut, d_wide), low),
            pltpu.VMEM((d_rows - cut, d_wide), low),
            pltpu.VMEM((5, cut, d_wide), low),
            pltpu.VMEM((2, 5, d_rows - cut, d_wide), low),
            pltpu.VMEM((g_rows, AUX), low),
            dma((4, 2)),
            dma((2, 4, 2)),
            dma((2, 4, 2)),
            dma((2, 5)),
            dma((4, 2, 2)),
            dma((2, 4, 2, 2)),
            dma((2, 4, 2, 2)),
            dma((2, 4)),
            dma((2,)),
            dma((2, 5)),
            dma((2, 2, 5)),
            dma((2,)),
            dma((2,)),
        ],
        compiler_params=pltpu.CompilerParams(
            collective_id=collective_id, has_side_effects=True, vmem_limit_bytes=60 * 1024 * 1024
        ),
    )(grads.reshape(chips, g_rows, g_wide), sums.reshape(chips * pair, d_rows, d_wide))


def gathered_body(
    layer_input,
    query_weight,
    key_projection,
    value_projection,
    context_weight,
    router_weight,
    expert_gate,
    expert_up,
    expert_down,
    prenorm_gain,
    midnorm_gain,
    querynorm_gain,
    keynorm_gain,
    routes,
    lengths,
    sequence_order,
    output_cotangent,
):
    bf16, f32 = jnp.bfloat16, jnp.float32
    tensor_count = lax.axis_size("tensor")
    tensor_index = lax.axis_index("tensor")
    dp_count = lax.axis_size("dp")
    dp_index = lax.axis_index("dp")
    own_rows, features = layer_input.shape
    block_rows = own_rows * tensor_count
    tokens = block_rows * dp_count
    expert_count = EXP_DEV * dp_count
    capacity = 3 * block_rows * TOP // (4 * EXP_DEV)
    most_rows = (5 * block_rows * TOP + 4 * expert_count - 1) // (4 * expert_count)
    shard = features // dp_count
    query_width = query_weight.shape[1]
    key_width = key_projection.shape[1]
    norm_part = HEAD_SIZE // dp_count

    place = dp_index * norm_part
    route_wide = block_rows * TOP // shard
    gains = jnp.concatenate(
        [
            prenorm_gain[:, None],
            midnorm_gain[:, None],
            lax.dynamic_update_slice(jnp.zeros((shard,), bf16), querynorm_gain, (place,))[:, None],
            lax.dynamic_update_slice(jnp.zeros((shard,), bf16), keynorm_gain, (place,))[:, None],
            routes.T.reshape(shard, -1).astype(bf16),
            jnp.zeros((shard, AUX - expert_count - 4 - route_wide), bf16),
        ],
        axis=1,
    )
    packed = jnp.concatenate(
        [query_weight, key_projection, value_projection, router_weight, gains, context_weight.T],
        axis=1,
    )
    position = jnp.arange(block_rows, dtype=jnp.int32)
    block_lengths = lengths[sequence_order]
    live = position[None, :] < block_lengths[:, None]
    live_own = lax.dynamic_slice_in_dim(live, dp_index, 1, 0)
    live_own = jnp.broadcast_to(live_own.astype(f32), (8, block_rows))
    heads_query = query_width // HEAD_SIZE
    heads_key = key_width // HEAD_SIZE
    row_start = tensor_index * own_rows
    routes_own = lax.dynamic_slice_in_dim(routes, row_start, own_rows, 0)
    expert_ids = jnp.arange(AUX, dtype=jnp.int32)
    chosen = jnp.any(routes_own[:, :, None] == expert_ids[None, None, :], axis=1).astype(f32)
    packed, cot_all, input_rows, sent, residual, *saved = opening(
        packed,
        output_cotangent,
        layer_input,
        live_own,
        chosen,
        expert_count,
        heads_query,
        heads_key,
        0,
    )
    route_from = query_width + 2 * key_width + expert_count + 4
    routes_all = packed[:, route_from : route_from + route_wide].astype(jnp.int32)
    routes_all = routes_all.reshape(dp_count, TOP, block_rows)
    normed_all = gather_all(sent, 1).reshape(dp_count, block_rows, features + AUX)

    expert_own = dp_index * EXP_DEV + jnp.arange(EXP_DEV, dtype=jnp.int32)
    hot = jnp.any(routes_all[:, None, :, :] == expert_own[None, :, None, None], axis=2)
    hot = hot & live[:, None, :]
    before = (position[:, None] < position[None, :]).astype(bf16)
    rank = jnp.einsum("bes,st->bet", hot.astype(bf16), before, preferred_element_type=f32)
    rank = rank.astype(jnp.int32)
    counts = rank[:, :, -1] + hot[:, :, -1]
    earlier = jnp.cumsum(counts, axis=0) - counts
    slot = earlier[:, :, None] + rank
    slot = jnp.where(hot & (slot < capacity), slot, -capacity)
    begin = jnp.minimum(earlier, capacity) // WINDOW_ALIGN * WINDOW_ALIGN
    info = jnp.concatenate([dp_index[None], begin.reshape(-1), tensor_index[None]])
    out_part, back_part, gate_gradient, up_gradient, down_gradient = expert_layer(
        info.astype(jnp.int32),
        slot,
        normed_all,
        cot_all,
        expert_gate,
        expert_up,
        expert_down,
        capacity,
        most_rows,
    )
    returned = scatter_all(back_part.reshape(tokens, features + AUX), 3)
    grads, input_gradient = attention_backward(
        returned,
        residual,
        sent,
        output_cotangent,
        input_rows,
        packed,
        live_own,
        saved,
        expert_count,
        6,
    )
    summed, expert_sum = last_scatter(grads, out_part.reshape(tokens, features), 4)
    summed = summed.astype(f32)
    layer_output = (residual + expert_sum.astype(f32)).astype(bf16)
    ends = [0]
    for width in (query_width, key_width, key_width, query_width, AUX):
        ends.append(ends[-1] + width)
    small = summed[:, ends[4] :]
    head_small = lax.dynamic_slice_in_dim(small, place, norm_part, 0)
    return (
        layer_output,
        input_gradient,
        summed[:, : ends[1]],
        summed[:, ends[1] : ends[2]],
        summed[:, ends[2] : ends[3]],
        summed[:, ends[3] : ends[4]].T,
        small[:, :expert_count],
        gate_gradient,
        up_gradient,
        down_gradient,
        small[:, expert_count],
        small[:, expert_count + 1],
        head_small[:, expert_count + 2],
        head_small[:, expert_count + 3],
    )


def solution(mesh):
    return jax.shard_map(
        gathered_body if mesh.shape["dp"] <= 16 else body,
        mesh=mesh,
        in_specs=(
            P(("dp", "tensor"), None),
            P("dp", "tensor"),
            P("dp", "tensor"),
            P("dp", "tensor"),
            P("tensor", "dp"),
            P("dp", None),
            P("dp", None, "tensor"),
            P("dp", None, "tensor"),
            P("dp", "tensor", None),
            P("dp"),
            P("dp"),
            P("dp"),
            P("dp"),
            P("dp", None),
            P(),
            P(),
            P(("dp", "tensor"), None),
        ),
        out_specs=(
            P(("dp", "tensor"), None),
            P(("dp", "tensor"), None),
            P("dp", "tensor"),
            P("dp", "tensor"),
            P("dp", "tensor"),
            P("tensor", "dp"),
            P("dp", None),
            P("dp", None, "tensor"),
            P("dp", None, "tensor"),
            P("dp", "tensor", None),
            P("dp"),
            P("dp"),
            P("dp"),
            P("dp"),
        ),
        check_vma=False,
    )
```

```python
import functools
import math

import jax
import jax.numpy as jnp
import numpy as np
from jax import lax
from jax.experimental import pallas as pl
from jax.experimental.pallas import tpu as pltpu
from jax.sharding import PartitionSpec as P

HEAD_SIZE = 128
TOP = 8
EXP_DEV = 2


epsilon = 1e-06
rope_base = 1000000.0
masked_score = -1e30


def carried_in(value, axis, combine, identity):
    count, place = (lax.axis_size(axis), lax.axis_index(axis))
    everything = lax.all_gather(value, axis)
    start = jnp.broadcast_to(jnp.asarray(identity, value.dtype), value.shape)

    def hop(k, before):
        reached = k < place
        new = combine(before, everything[k])
        return jnp.where(reached, new, before)

    return lax.fori_loop(0, count, hop, start)


def rms_normalize(value_rows):
    scaling = lax.rsqrt(jnp.mean(value_rows * value_rows, axis=-1, keepdims=True) + epsilon)
    return (value_rows * scaling, scaling)


def norm_back(cotangent, unit_rows, scaling):
    return scaling * (
        cotangent - unit_rows * jnp.mean(cotangent * unit_rows, axis=-1, keepdims=True)
    )


def rotary_apply(value_rows, cosine_table, sine_values):
    middle = value_rows.shape[-1] // 2
    former = value_rows[..., :middle]
    latter = value_rows[..., middle:]
    return jnp.concatenate(
        [
            former * cosine_table - latter * sine_values,
            latter * cosine_table + former * sine_values,
        ],
        axis=-1,
    )


def matrix_product(former, latter):
    return jnp.dot(former, latter, preferred_element_type=jnp.float32)


def contract(former, latter):
    return lax.dot_general(
        former, latter, (((0,), (0,)), ((), ())), preferred_element_type=jnp.float32
    )


def transposed(former, latter):
    return lax.dot_general(
        former, latter, (((1,), (1,)), ((), ())), preferred_element_type=jnp.float32
    )


def to_owners(buffer):
    return lax.all_to_all(buffer, "dp", split_axis=1, concat_axis=1, tiled=True)


def owner_reduce(partial_rows):
    shares = lax.psum_scatter(
        partial_rows.astype(jnp.bfloat16), "tensor", scatter_dimension=2, tiled=True
    )
    return lax.all_gather(shares, "tensor", axis=2, tiled=True)


def body(
    layer_input,
    query_weight,
    key_projection,
    value_projection,
    context_weight,
    router_weight,
    expert_gate,
    expert_up,
    expert_down,
    prenorm_gain,
    midnorm_gain,
    querynorm_gain,
    keynorm_gain,
    routes,
    lengths,
    sequence_order,
    output_cotangent,
):
    tensor_count = lax.axis_size("tensor")
    tensor_index = lax.axis_index("tensor")
    dp_count = lax.axis_size("dp")
    own_rows = layer_input.shape[0]
    block_rows = own_rows * tensor_count
    features = layer_input.shape[1]
    expert_count = EXP_DEV * dp_count
    capacity = 3 * block_rows * TOP // (4 * EXP_DEV)
    most_rows = (5 * block_rows * TOP + 4 * expert_count - 1) // (4 * expert_count)
    slot_total = EXP_DEV * dp_count * most_rows
    (
        query_all,
        key_all,
        value_all,
        context_all,
        router_all,
        gain_first,
        gain_second,
        query_gain,
        gain_key,
    ) = (
        lax.all_gather(query_weight, "dp", axis=0, tiled=True),
        lax.all_gather(key_projection, "dp", axis=0, tiled=True),
        lax.all_gather(value_projection, "dp", axis=0, tiled=True),
        lax.all_gather(context_weight, "dp", axis=1, tiled=True),
        lax.all_gather(router_weight, "dp", axis=0, tiled=True),
        lax.all_gather(prenorm_gain, "dp", axis=0, tiled=True),
        lax.all_gather(midnorm_gain, "dp", axis=0, tiled=True),
        lax.all_gather(querynorm_gain, "dp", axis=0, tiled=True),
        lax.all_gather(keynorm_gain, "dp", axis=0, tiled=True),
    )
    input_rows, cot_rows = (
        lax.all_gather(layer_input, "tensor", axis=0, tiled=True),
        lax.all_gather(output_cotangent, "tensor", axis=0, tiled=True),
    )
    position = jnp.arange(block_rows, dtype=jnp.int32)
    seq_length = lengths[sequence_order[lax.axis_index("dp")]]
    token_live = position < seq_length
    frequency = jnp.exp(
        -math.log(rope_base) * jnp.arange(HEAD_SIZE // 2, dtype=jnp.float32) * (2.0 / HEAD_SIZE)
    )
    angles = position.astype(jnp.float32)[:, None] * frequency[None, :]
    cosine_table = jnp.cos(angles)[:, None, :]
    sine_values = jnp.sin(angles)[:, None, :]
    heads_query = query_all.shape[1] // HEAD_SIZE
    heads_key = key_all.shape[1] // HEAD_SIZE
    group_width = heads_query // heads_key
    gain_one = gain_first.astype(jnp.float32)
    gain_two = gain_second.astype(jnp.float32)
    query_factor = query_gain.astype(jnp.float32)
    key_factor = gain_key.astype(jnp.float32)
    stream = input_rows.astype(jnp.float32)
    unit_first, scale_first = rms_normalize(stream)
    first_layer_normed = (unit_first * gain_one).astype(jnp.bfloat16)
    query_unnormed = matrix_product(first_layer_normed, query_all).reshape(
        block_rows, heads_query, HEAD_SIZE
    )
    key_unnormed = matrix_product(first_layer_normed, key_all).reshape(
        block_rows, heads_key, HEAD_SIZE
    )
    value_rows = (
        matrix_product(first_layer_normed, value_all)
        .astype(jnp.bfloat16)
        .reshape(block_rows, heads_key, HEAD_SIZE)
    )
    query_unit, query_scale = rms_normalize(query_unnormed)
    key_unit, key_scale = rms_normalize(key_unnormed)
    query_rows = (
        rotary_apply(query_unit * query_factor, cosine_table, sine_values)
        .astype(jnp.bfloat16)
        .reshape(block_rows, heads_key, group_width, HEAD_SIZE)
    )
    keys_rot = rotary_apply(key_unit * key_factor, cosine_table, sine_values).astype(jnp.bfloat16)
    score_scale = HEAD_SIZE ** (-0.5)
    allowed = (position[None, :] <= position[:, None]) & token_live[None, :]

    def score_block():
        raw_scores = (
            jnp.einsum("ikrd,jkd->krij", query_rows, keys_rot, preferred_element_type=jnp.float32)
            * score_scale
        )
        return jnp.where(allowed, raw_scores, masked_score)

    scores = score_block()
    row_peak = jnp.max(scores, axis=-1, keepdims=True)
    log_total = row_peak + jnp.log(jnp.sum(jnp.exp(scores - row_peak), axis=-1, keepdims=True))
    soft_probs = jnp.exp(scores - log_total)
    context = jnp.einsum(
        "krij,jkd->ikrd",
        soft_probs.astype(jnp.bfloat16),
        value_rows,
        preferred_element_type=jnp.float32,
    )
    context = context.reshape(block_rows, heads_query * HEAD_SIZE).astype(jnp.bfloat16)
    attention = lax.psum(matrix_product(context, context_all), "tensor")
    residual = stream + attention
    unit_second, scale_second = rms_normalize(residual)
    normed_second = (unit_second * gain_two).astype(jnp.bfloat16)
    logits = matrix_product(normed_second, router_all)
    expert_ids = jnp.arange(expert_count, dtype=jnp.int32)
    route_hot = routes[:, :, None] == expert_ids[None, None, :]
    chosen = jnp.sum(jnp.where(route_hot, logits[:, None, :], 0.0), axis=-1)
    gate_weights = jax.nn.softmax(chosen, axis=-1)
    pair_expert = routes.reshape(-1)
    pair_live = jnp.repeat(token_live, TOP)
    pair_hot = ((pair_expert[:, None] == expert_ids[None, :]) & pair_live[:, None]).astype(
        jnp.int32
    )
    running = jnp.cumsum(pair_hot, axis=0)
    pair_rank = jnp.sum((running - pair_hot) * pair_hot, axis=1)
    counts = running[-1]
    earlier = carried_in(
        counts, "dp", lambda former, latter: former + latter, jnp.zeros_like(counts)
    )
    pair_slot = jnp.sum(earlier[None, :] * pair_hot, axis=1) + pair_rank
    pair_kept = pair_live & (pair_slot < capacity)
    local_expert = pair_expert % EXP_DEV
    owner_index = pair_expert // EXP_DEV
    buffer_index = (local_expert * dp_count + owner_index) * most_rows + pair_rank
    target = jnp.where(pair_kept, buffer_index, slot_total)
    pair_ids = jnp.arange(block_rows * TOP, dtype=jnp.int32)
    slot_pair = jnp.full((slot_total,), -1, dtype=jnp.int32).at[target].set(pair_ids, mode="drop")
    slot_used = slot_pair >= 0
    slot_safe = jnp.maximum(slot_pair, 0)
    slot_token = slot_safe // TOP
    bf_zero = jnp.zeros((), jnp.bfloat16)
    send_rows = jnp.where(slot_used[:, None], normed_second[slot_token], bf_zero)
    layout = (EXP_DEV, dp_count, most_rows, features)
    received = to_owners(send_rows.reshape(layout)).reshape(EXP_DEV, dp_count * most_rows, features)
    gate_pre = jnp.einsum("end,edf->enf", received, expert_gate, preferred_element_type=jnp.float32)
    up_pre = jnp.einsum("end,edf->enf", received, expert_up, preferred_element_type=jnp.float32)
    sigmoid_gate = jax.nn.sigmoid(gate_pre)
    gate_act = gate_pre * sigmoid_gate
    hidden = (gate_act * up_pre).astype(jnp.bfloat16)
    out_partial = jnp.einsum(
        "enf,efd->end", hidden, expert_down, preferred_element_type=jnp.float32
    )
    expert_out = owner_reduce(out_partial)
    width = expert_out.shape[2]
    returned = lax.all_to_all(
        expert_out.reshape(EXP_DEV, dp_count, most_rows, width),
        "dp",
        split_axis=1,
        concat_axis=1,
        tiled=True,
    ).reshape(slot_total, width)
    pair_place = jnp.where(pair_kept, buffer_index, 0)
    pair_out = jnp.where(pair_kept[:, None], returned[pair_place], bf_zero).reshape(
        block_rows, TOP, width
    )
    expert_part = jnp.sum(gate_weights[:, :, None] * pair_out, axis=1)
    cot_full = cot_rows.astype(jnp.float32)
    own_start = tensor_index * own_rows
    gate_part = jnp.sum(cot_full[:, None, :] * pair_out, axis=-1)
    expert_own = lax.dynamic_slice_in_dim(expert_part, own_start, own_rows, 0)
    residual_own = lax.dynamic_slice_in_dim(residual, own_start, own_rows, 0)
    layer_output = (residual_own + expert_own).astype(jnp.bfloat16)
    slot_gate = jnp.where(slot_used, gate_weights.reshape(-1)[slot_safe], 0.0)
    send_cot = (slot_gate[:, None] * cot_full[slot_token]).astype(jnp.bfloat16)
    expert_cot = to_owners(send_cot.reshape(layout)).reshape(
        EXP_DEV, dp_count * most_rows, features
    )
    hidden_cot = jnp.einsum(
        "end,efd->enf", expert_cot, expert_down, preferred_element_type=jnp.float32
    )
    gating_cot = (
        hidden_cot * up_pre * sigmoid_gate * (1.0 + gate_pre * (1.0 - sigmoid_gate))
    ).astype(jnp.bfloat16)
    upward_cot = (hidden_cot * gate_act).astype(jnp.bfloat16)
    down_gradient = jnp.einsum(
        "enf,end->efd", hidden, expert_cot, preferred_element_type=jnp.float32
    )
    gate_gradient = jnp.einsum(
        "end,enf->edf", received, gating_cot, preferred_element_type=jnp.float32
    )
    up_gradient = jnp.einsum(
        "end,enf->edf", received, upward_cot, preferred_element_type=jnp.float32
    )
    row_partial = jnp.einsum(
        "enf,edf->end", gating_cot, expert_gate, preferred_element_type=jnp.float32
    )
    row_partial = row_partial + jnp.einsum(
        "enf,edf->end", upward_cot, expert_up, preferred_element_type=jnp.float32
    )
    row_cot = owner_reduce(row_partial)
    row_back = lax.all_to_all(
        row_cot.reshape(EXP_DEV, dp_count, most_rows, width),
        "dp",
        split_axis=1,
        concat_axis=1,
        tiled=True,
    ).reshape(slot_total, width)
    pair_cot = jnp.where(pair_kept[:, None], row_back[pair_place], bf_zero).reshape(
        block_rows, TOP, width
    )
    normed_part = jnp.sum(pair_cot.astype(jnp.float32), axis=1)
    normed_cot = normed_part
    route_cot = gate_weights * (
        gate_part - jnp.sum(gate_weights * gate_part, axis=-1, keepdims=True)
    )
    logit_cot = jnp.sum(jnp.where(route_hot, route_cot[:, :, None], 0.0), axis=1).astype(
        jnp.bfloat16
    )
    router_gradient = contract(normed_second, logit_cot)
    normed_cot = normed_cot + transposed(logit_cot, router_all)
    midnorm_gradient = jnp.sum(normed_cot * unit_second, axis=0)
    residual_cot = cot_full + norm_back(normed_cot * gain_two, unit_second, scale_second)
    attention_cot = residual_cot.astype(jnp.bfloat16)
    context_gradient = contract(context, attention_cot)
    context_cot = (
        transposed(attention_cot, context_all)
        .astype(jnp.bfloat16)
        .reshape(block_rows, heads_key, group_width, HEAD_SIZE)
    )
    scores = score_block()
    soft_probs = jnp.exp(scores - log_total)
    prob_cot = jnp.einsum(
        "ikrd,jkd->krij", context_cot, value_rows, preferred_element_type=jnp.float32
    )
    score_cot = (
        soft_probs * (prob_cot - jnp.sum(soft_probs * prob_cot, axis=-1, keepdims=True))
    ).astype(jnp.bfloat16)
    value_cot = jnp.einsum(
        "krij,ikrd->jkd",
        soft_probs.astype(jnp.bfloat16),
        context_cot,
        preferred_element_type=jnp.float32,
    )
    value_cot = value_cot.astype(jnp.bfloat16).reshape(block_rows, heads_key * HEAD_SIZE)
    query_turned = (
        jnp.einsum(
            "krij,jkd->ikrd", score_cot, keys_rot, preferred_element_type=jnp.float32
        ).reshape(block_rows, heads_query, HEAD_SIZE)
        * score_scale
    )
    key_turned = (
        jnp.einsum("krij,ikrd->jkd", score_cot, query_rows, preferred_element_type=jnp.float32)
        * score_scale
    )
    query_back = rotary_apply(query_turned, cosine_table, -sine_values)
    key_back = rotary_apply(key_turned, cosine_table, -sine_values)
    querynorm_part = jnp.sum(query_back * query_unit, axis=(0, 1))
    keynorm_part = jnp.sum(key_back * key_unit, axis=(0, 1))
    query_raw_cot = (
        norm_back(query_back * query_factor, query_unit, query_scale)
        .astype(jnp.bfloat16)
        .reshape(block_rows, heads_query * HEAD_SIZE)
    )
    key_raw_cot = (
        norm_back(key_back * key_factor, key_unit, key_scale)
        .astype(jnp.bfloat16)
        .reshape(block_rows, heads_key * HEAD_SIZE)
    )
    query_gradient = contract(first_layer_normed, query_raw_cot)
    key_gradient = contract(first_layer_normed, key_raw_cot)
    value_gradient = contract(first_layer_normed, value_cot)
    first_part = (
        transposed(query_raw_cot, query_all)
        + transposed(key_raw_cot, key_all)
        + transposed(value_cot, value_all)
    )
    first_cot, querynorm_gradient, keynorm_gradient = (
        lax.psum(first_part.astype(jnp.bfloat16), "tensor").astype(jnp.float32),
        lax.psum(querynorm_part.astype(jnp.bfloat16), "tensor").astype(jnp.float32),
        lax.psum(keynorm_part.astype(jnp.bfloat16), "tensor").astype(jnp.float32),
    )
    prenorm_gradient = jnp.sum(first_cot * unit_first, axis=0)
    input_cot = residual_cot + norm_back(first_cot * gain_one, unit_first, scale_first)
    input_gradient = lax.dynamic_slice_in_dim(input_cot, own_start, own_rows, 0).astype(
        jnp.bfloat16
    )
    summed = (
        lax.psum_scatter(query_gradient, "dp", scatter_dimension=0, tiled=True),
        lax.psum_scatter(key_gradient, "dp", scatter_dimension=0, tiled=True),
        lax.psum_scatter(value_gradient, "dp", scatter_dimension=0, tiled=True),
        lax.psum_scatter(context_gradient, "dp", scatter_dimension=1, tiled=True),
        lax.psum_scatter(router_gradient, "dp", scatter_dimension=0, tiled=True),
        lax.psum_scatter(prenorm_gradient, "dp", scatter_dimension=0, tiled=True),
        lax.psum_scatter(midnorm_gradient, "dp", scatter_dimension=0, tiled=True),
        lax.psum_scatter(querynorm_gradient, "dp", scatter_dimension=0, tiled=True),
        lax.psum_scatter(keynorm_gradient, "dp", scatter_dimension=0, tiled=True),
    )
    return (
        layer_output,
        input_gradient,
        summed[0],
        summed[1],
        summed[2],
        summed[3],
        summed[4],
        gate_gradient,
        up_gradient,
        down_gradient,
        summed[5],
        summed[6],
        summed[7],
        summed[8],
    )


AUX = 128


GRID_Z = 4
VMEM_LIMIT = 56 * 1024 * 1024


def remote(src, dst, send_sem, recv_sem, device):
    return pltpu.make_async_remote_copy(
        src_ref=src,
        dst_ref=dst,
        send_sem=send_sem,
        recv_sem=recv_sem,
        device_id=device,
        device_id_type=pl.DeviceIdType.MESH,
    )


class Place:
    def __init__(self):
        self.dp = lax.axis_index("dp")
        self.y = lax.axis_index("tensor")
        self.z = self.dp // 4
        self.x = (self.dp // 2) % 2
        self.core = self.dp % 2
        self.sibling = (self.dp + 1 - 2 * self.core, self.y)
        self.x_mate = (self.dp + 2 - 4 * self.x, self.y)
        self.y_mate = (self.dp, 1 - self.y)
        self.above = (self.dp + 4, self.y)
        self.below = (self.dp - 4, self.y)
        self.has_above = self.z < GRID_Z - 1
        self.has_below = self.z > 0

    def farthest(self, k):
        return (3 - 3 * (self.z // 2), (2 + 3 * self.z) % 5, 1 + self.z % 2, self.z)[k]

    def dp_at(self, z, flip_x, flip_core):
        x = self.x + flip_x * (1 - 2 * self.x)
        core = self.core + flip_core * (1 - 2 * self.core)
        return z * 4 + x * 2 + core

    def y_at(self, flip_y):
        return self.y + flip_y * (1 - 2 * self.y)

    def greet(self):
        barrier = pltpu.get_barrier_semaphore()
        for mate in (self.sibling, self.x_mate, self.y_mate):
            pl.semaphore_signal(barrier, 1, device_id=mate, device_id_type=pl.DeviceIdType.MESH)

        @pl.when(self.has_above)
        def _():
            pl.semaphore_signal(
                barrier, 1, device_id=self.above, device_id_type=pl.DeviceIdType.MESH
            )

        @pl.when(self.has_below)
        def _():
            pl.semaphore_signal(
                barrier, 1, device_id=self.below, device_id_type=pl.DeviceIdType.MESH
            )

        pl.semaphore_wait(barrier, 4 + self.z * (GRID_Z - 1 - self.z) // 2)


def add_rows(target, sources, rows, step=16):
    start, count = rows

    def one(i, carry):
        at = pl.ds(pl.multiple_of(start + i * step, step), step)
        total = target[at, :].astype(jnp.float32)
        for source, shift in sources:
            there = pl.ds(pl.multiple_of(start - shift + i * step, step), step)
            total = total + source[there, :].astype(jnp.float32)
        target[at, :] = total.astype(target.dtype)
        return carry

    lax.fori_loop(0, count // step, one, 0)


def scatter_kernel(
    part, out, own, core, diag_a, diag_b, from_x, from_y, from_z, result,
    load_s, core_s, diag_s, x_s, y_s, z_s, out_s,
):
    me = Place()
    rows = own.shape[3]
    half = rows // 2
    low, high = (0, half), (half, half)
    loads, sends = {}, []

    def chunk(k, flip_x, flip_y, flip_core):
        return part.at[me.dp_at(me.farthest(k), flip_x, flip_core) * 2 + me.y_at(flip_y)]

    order = ((1, 1), (1, 0), (0, 1), (0, 0))
    for k in range(GRID_Z):
        for fx, fy in order:
            copy = pltpu.make_async_copy(
                chunk(k, fx, fy, 0), own.at[k, fx, fy], load_s.at[k, fx, fy]
            )
            copy.start()
            loads[k, fx, fy] = copy
    me.greet()
    cores = {}
    for k in range(GRID_Z):
        for fx, fy in order:
            copy = remote(
                chunk(k, fx, fy, 1), core.at[k, fx, fy],
                core_s.at[0, k, fx, fy], core_s.at[1, k, fx, fy], me.sibling,
            )
            copy.start()
            cores[k, fx, fy] = copy
            sends.append(copy)

    da = [remote(own.at[k, 1, 1, pl.ds(0, half)], diag_a.at[k], diag_s.at[0, k], diag_s.at[1, k], me.y_mate) for k in range(4)]
    db = [remote(own.at[k, 1, 1, pl.ds(half, half)], diag_b.at[k], diag_s.at[2, k], diag_s.at[3, k], me.x_mate) for k in range(4)]
    xs = [[remote(own.at[k, 1, 0, pl.ds(h * half, half)], from_x.at[k, pl.ds(h * half, half)], x_s.at[0, k, h], x_s.at[1, k, h], me.x_mate) for h in range(2)] for k in range(4)]
    ys = [[remote(own.at[k, 0, 1, pl.ds(h * half, half)], from_y.at[k, pl.ds(h * half, half)], y_s.at[0, k, h], y_s.at[1, k, h], me.y_mate) for h in range(2)] for k in range(4)]

    def arrive(k, fx, fy):
        loads[k, fx, fy].wait()
        cores[k, fx, fy].wait_recv()

    def early(k):
        arrive(k, 1, 1)
        add_rows(own.at[k, 1, 1], [(core.at[k, 1, 1], 0)], low)
        da[k].start()
        add_rows(own.at[k, 1, 1], [(core.at[k, 1, 1], 0)], high)
        db[k].start()
        arrive(k, 1, 0)
        add_rows(own.at[k, 1, 0], [(core.at[k, 1, 0], 0)], high)
        xs[k][1].start()
        arrive(k, 0, 1)
        add_rows(own.at[k, 0, 1], [(core.at[k, 0, 1], 0)], low)
        ys[k][0].start()

    def late(k):
        da[k].wait_recv()
        add_rows(own.at[k, 1, 0], [(core.at[k, 1, 0], 0), (diag_a.at[k], 0)], low)
        xs[k][0].start()
        db[k].wait_recv()
        add_rows(own.at[k, 0, 1], [(core.at[k, 0, 1], 0), (diag_b.at[k], half)], high)
        ys[k][1].start()

    whole = (0, rows)

    def column(k):
        arrive(k, 0, 0)
        for h in range(2):
            xs[k][h].wait_recv()
            ys[k][h].wait_recv()
        mine = own.at[k, 0, 0]
        rest = [(core.at[k, 0, 0], 0), (from_x.at[k], 0), (from_y.at[k], 0)]
        if k < GRID_Z - 1:
            to = me.farthest(k)
            add_rows(mine, rest, whole)
            for side, ahead, mate, more in (
                (0, to > me.z, me.above, me.has_below),
                (1, to < me.z, me.below, me.has_above),
            ):
                copy = remote(
                    mine, from_z.at[side, to], z_s.at[0, side, to], z_s.at[1, side, to], mate
                )

                @pl.when(ahead)
                def _():
                    @pl.when(more)
                    def _():
                        copy.wait_recv()
                        add_rows(mine, [(from_z.at[side, to], 0)], whole)

                    copy.start()
        else:
            add_rows(mine, rest, whole)
            for side, more in ((0, me.has_below), (1, me.has_above)):
                copy = remote(
                    mine, from_z.at[side, me.z], z_s.at[0, side, me.z], z_s.at[1, side, me.z],
                    me.y_mate,
                )

                @pl.when(more)
                def _():
                    copy.wait_recv()
                    add_rows(mine, [(from_z.at[side, me.z], 0)], whole)

    early(0)
    early(1)
    late(0)
    early(2)
    late(1)
    column(0)
    early(3)
    late(2)
    column(1)
    late(3)
    column(2)
    column(3)
    copy = pltpu.make_async_copy(own.at[3, 0, 0], out, out_s)
    copy.start()
    for k in range(GRID_Z):
        da[k].wait_send()
        db[k].wait_send()
        for h in range(2):
            xs[k][h].wait_send()
            ys[k][h].wait_send()
        if k < GRID_Z - 1:
            to = me.farthest(k)
            for side, ahead, mate in ((0, to > me.z, me.above), (1, to < me.z, me.below)):
                @pl.when(ahead)
                def _():
                    remote(
                        own.at[k, 0, 0], from_z.at[side, to],
                        z_s.at[0, side, to], z_s.at[1, side, to], mate,
                    ).wait_send()
    for sent in sends:
        sent.wait_send()
    copy.wait()


def scatter_all(value, collective_id):
    devices = lax.axis_size("dp") * lax.axis_size("tensor")
    rows, width = value.shape[0] // devices, value.shape[1]
    half = rows // 2
    dma = pltpu.SemaphoreType.DMA
    low = value.dtype
    return pl.pallas_call(
        scatter_kernel,
        out_shape=jax.ShapeDtypeStruct((rows, width), low),
        in_specs=[pl.BlockSpec(memory_space=pl.ANY)],
        out_specs=pl.BlockSpec(memory_space=pl.ANY),
        scratch_shapes=[
            pltpu.VMEM((4, 2, 2, rows, width), low),
            pltpu.VMEM((4, 2, 2, rows, width), low),
            pltpu.VMEM((4, half, width), low),
            pltpu.VMEM((4, half, width), low),
            pltpu.VMEM((4, rows, width), low),
            pltpu.VMEM((4, rows, width), low),
            pltpu.VMEM((2, 4, rows, width), low),
            pltpu.VMEM((8, 128), low),
            dma((4, 2, 2)),
            dma((2, 4, 2, 2)),
            dma((4, 4)),
            dma((2, 4, 2)),
            dma((2, 4, 2)),
            dma((2, 2, 4)),
            dma(()),
        ],
        compiler_params=pltpu.CompilerParams(
            collective_id=collective_id, has_side_effects=True, vmem_limit_bytes=VMEM_LIMIT
        ),
    )(value.reshape(devices, rows, width))


WINDOW_ALIGN = 16
EXPERT_VMEM = 60 * 1024 * 1024


def dot(left, right, dims=((1,), (0,))):
    return lax.dot_general(left, right, (dims, ((), ())), preferred_element_type=jnp.float32)


def expert_kernel(
    info, pos, rows_in, cots_in, gate_w, up_w, down_w,
    out, back, gate_g, up_g, down_g,
    x, dy, wgu, wd, slot_out, slot_row, gu, hg, rows_b, cots_b, g_stage, d_stage,
    load_s, w_s, out_s, g_s, d_s,
):
    bf16, f32 = jnp.bfloat16, jnp.float32
    blocks, block_rows, wide = rows_in.shape
    features = cots_in.shape[2]
    experts, padded = x.shape[0], x.shape[1]
    part = hg.shape[2]
    cap = hg.shape[1]
    window = padded - cap
    tile = 256
    chunk = 512

    def load(b):
        slot = b % 2
        return (
            pltpu.make_async_copy(rows_in.at[b], rows_b.at[slot], load_s.at[slot, 0]),
            pltpu.make_async_copy(cots_in.at[b], cots_b.at[slot], load_s.at[slot, 1]),
        )

    for copy in load(0):
        copy.start()
    weights = []
    for e in range(experts):
        weights.append(pltpu.make_async_copy(gate_w.at[e], wgu.at[e, :, pl.ds(0, part)], w_s.at[e, 0]))
        weights.append(pltpu.make_async_copy(up_w.at[e], wgu.at[e, :, pl.ds(part, part)], w_s.at[e, 1]))
        weights.append(pltpu.make_async_copy(down_w.at[e], wd.at[e], w_s.at[e, 2]))
    for copy in weights:
        copy.start()

    def clear(i, carry):
        at = pl.ds(pl.multiple_of(i * 16, 16), 16)
        for e in range(experts):
            x[e, at, :] = jnp.zeros((16, wide), bf16)
            dy[e, at, :] = jnp.zeros((16, features), bf16)
        return carry

    lax.fori_loop(0, padded // 16, clear, 0)
    for e in range(experts):
        slot_out[e, pl.ds(cap, window), :] = jnp.zeros((window, features), bf16)
        slot_row[e, pl.ds(cap, window), :] = jnp.zeros((window, wide), bf16)

    def starts(b):
        return [pl.multiple_of(info[1 + b * experts + e], WINDOW_ALIGN) for e in range(experts)]

    def picks(b, begin):
        slots = lax.broadcasted_iota(jnp.int32, (window, block_rows), 0)
        return jnp.concatenate(
            [(slots + begin[e] == pos[b, pl.ds(e, 1), :]).astype(f32) for e in range(experts)],
            axis=0,
        )

    def take(b, carry):
        slot = b % 2

        @pl.when(b + 1 < blocks)
        def _():
            for copy in load(b + 1):
                copy.start()

        begin = starts(b)
        picked = picks(b, begin).astype(bf16)
        for copy in load(b):
            copy.wait()
        for source, target, width in ((rows_b, x, wide), (cots_b, dy, features)):
            for first in range(0, width, chunk):
                cols = pl.ds(first, min(chunk, width - first))
                got = dot(picked, source[slot, :, cols]).astype(bf16)
                for e in range(experts):
                    at = pl.ds(begin[e], window)
                    target[e, at, cols] += got[e * window : (e + 1) * window]
        return carry

    lax.fori_loop(0, blocks, take, 0)
    for copy in weights:
        copy.wait()

    lanes = lax.broadcasted_iota(jnp.int32, (tile, AUX), 1)

    def mlp(step, carry):
        e = step // (cap // tile)
        at = pl.ds(pl.multiple_of((step % (cap // tile)) * tile, tile), tile)
        own = info[0] * experts + e
        total = blocks * experts
        aux = x[e, at, pl.ds(features, AUX)].astype(f32)
        gate = jnp.sum(
            jnp.where((lanes == own) | (lanes == own + total), aux, 0.0), axis=1, keepdims=True
        )
        pre = dot(x[e, at, pl.ds(0, features)], wgu[e])
        gate_pre, up_pre = pre[:, :part], pre[:, part:]
        sig = 1.0 / (1.0 + jnp.exp(-gate_pre))
        act = gate_pre * sig
        hidden = (act * up_pre).astype(bf16).astype(f32)
        gated = (hidden * gate).astype(bf16)
        hg[e, at, :] = gated
        down_cot = dot(dy[e, at, :], wd[e], ((1,), (1,)))
        slot_cot = jnp.sum(hidden * down_cot, axis=1, keepdims=True)
        hidden_cot = down_cot * gate
        gu[e, at, pl.ds(0, part)] = (
            hidden_cot * up_pre * sig * (1.0 + gate_pre * (1.0 - sig))
        ).astype(bf16)
        gu[e, at, pl.ds(part, part)] = (hidden_cot * act).astype(bf16)
        for first in range(0, features, chunk):
            cols = pl.ds(first, chunk)
            slot_out[e, at, cols] = dot(gated, wd[e, :, cols]).astype(bf16)
            slot_row[e, at, cols] = dot(
                gu[e, at, :], wgu[e, pl.ds(first, chunk), :], ((1,), (1,))
            ).astype(bf16)
        high = slot_cot.astype(bf16).astype(f32)
        place = info[1 + blocks * experts] * 2 * total + own * 2
        slot_row[e, at, pl.ds(features, AUX)] = jnp.where(
            lanes == place, high, jnp.where(lanes == place + 1, slot_cot - high, 0.0)
        ).astype(bf16)
        return carry

    lax.fori_loop(0, experts * (cap // tile), mlp, 0)

    def stored(b):
        slot = b % 2
        return (
            pltpu.make_async_copy(cots_b.at[slot], out.at[b], out_s.at[slot, 0]),
            pltpu.make_async_copy(rows_b.at[slot], back.at[b], out_s.at[slot, 1]),
        )

    def put(b, carry):
        slot = b % 2

        @pl.when(b >= 2)
        def _():
            for copy in stored(b - 2):
                copy.wait()

        begin = starts(b)
        spread = picks(b, begin).T.astype(bf16)
        for source, target, width in ((slot_out, cots_b, features), (slot_row, rows_b, wide)):
            for first in range(0, width, chunk):
                cols = pl.ds(first, min(chunk, width - first))
                held = jnp.concatenate(
                    [source[e, pl.ds(begin[e], window), cols] for e in range(experts)], axis=0
                )
                target[slot, :, cols] = dot(spread, held).astype(bf16)
        for copy in stored(b):
            copy.start()
        return carry

    lax.fori_loop(0, blocks, put, 0)

    tiles = features // tile

    def g_copies(step):
        slot = step % 2
        e, at = step // tiles, pl.ds(pl.multiple_of((step % tiles) * tile, tile), tile)
        return (
            pltpu.make_async_copy(g_stage.at[slot, :, pl.ds(0, part)], gate_g.at[e, at], g_s.at[slot, 0]),
            pltpu.make_async_copy(g_stage.at[slot, :, pl.ds(part, part)], up_g.at[e, at], g_s.at[slot, 1]),
        )

    def wide_grad(step, carry):
        slot = step % 2
        e, at = step // tiles, pl.ds(pl.multiple_of((step % tiles) * tile, tile), tile)

        @pl.when(step >= 2)
        def _():
            for copy in g_copies(step - 2):
                copy.wait()

        g_stage[slot] = dot(x[e, pl.ds(0, cap), at], gu[e], ((0,), (0,)))
        for copy in g_copies(step):
            copy.start()
        return carry

    lax.fori_loop(0, experts * tiles, wide_grad, 0)
    parts = features // chunk

    def d_copy(step):
        slot = step % 2
        e, at = step // parts, pl.ds(pl.multiple_of((step % parts) * chunk, chunk), chunk)
        return pltpu.make_async_copy(d_stage.at[slot], down_g.at[e, :, at], d_s.at[slot])

    def down_grad(step, carry):
        slot = step % 2
        e, at = step // parts, pl.ds(pl.multiple_of((step % parts) * chunk, chunk), chunk)

        @pl.when(step >= 2)
        def _():
            d_copy(step - 2).wait()

        d_stage[slot] = dot(hg[e], dy[e, pl.ds(0, cap), at], ((0,), (0,)))
        d_copy(step).start()
        return carry

    lax.fori_loop(0, experts * parts, down_grad, 0)
    for last in (2, 1):
        for copy in stored(blocks - last):
            copy.wait()
        for copy in g_copies(experts * tiles - last):
            copy.wait()
        d_copy(experts * parts - last).wait()


def expert_layer(info, pos, rows_in, cots_in, gate_w, up_w, down_w, capacity, most):
    bf16, f32 = jnp.bfloat16, jnp.float32
    blocks, block_rows, wide = rows_in.shape
    features = cots_in.shape[2]
    experts, part = gate_w.shape[0], gate_w.shape[2]
    padded = capacity + -(-most // WINDOW_ALIGN) * WINDOW_ALIGN + WINDOW_ALIGN
    dma = pltpu.SemaphoreType.DMA
    shape = jax.ShapeDtypeStruct
    anywhere = pl.BlockSpec(memory_space=pl.ANY)
    return pl.pallas_call(
        expert_kernel,
        out_shape=(
            shape((blocks, block_rows, features), bf16),
            shape((blocks, block_rows, wide), bf16),
            shape(gate_w.shape, f32),
            shape(up_w.shape, f32),
            shape(down_w.shape, f32),
        ),
        in_specs=[
            pl.BlockSpec(memory_space=pltpu.SMEM),
            pl.BlockSpec(memory_space=pltpu.VMEM),
        ]
        + [anywhere] * 5,
        out_specs=(anywhere,) * 5,
        scratch_shapes=[
            pltpu.VMEM((experts, padded, wide), bf16),
            pltpu.VMEM((experts, padded, features), bf16),
            pltpu.VMEM((experts, features, 2 * part), bf16),
            pltpu.VMEM((experts, part, features), bf16),
            pltpu.VMEM((experts, padded, features), bf16),
            pltpu.VMEM((experts, padded, wide), bf16),
            pltpu.VMEM((experts, capacity, 2 * part), bf16),
            pltpu.VMEM((experts, capacity, part), bf16),
            pltpu.VMEM((2, block_rows, wide), bf16),
            pltpu.VMEM((2, block_rows, features), bf16),
            pltpu.VMEM((2, 256, 2 * part), f32),
            pltpu.VMEM((2, part, 512), f32),
            dma((2, 2)),
            dma((experts, 3)),
            dma((2, 2)),
            dma((2, 2)),
            dma((2,)),
        ],
        compiler_params=pltpu.CompilerParams(vmem_limit_bytes=EXPERT_VMEM),
    )(info, pos, rows_in, cots_in, gate_w, up_w, down_w)


ATTENTION_VMEM = 60 * 1024 * 1024
SCORE_SCALE = HEAD_SIZE ** (-0.5)
def turn_tables(rows):
    frequency = np.exp(
        -math.log(rope_base) * np.arange(HEAD_SIZE // 2, dtype=np.float32) * (2.0 / HEAD_SIZE)
    ).astype(np.float32)
    angles = np.arange(rows, dtype=np.float32)[:, None] * frequency[None, :]
    cosine, sine = np.cos(angles), np.sin(angles)
    return (
        np.concatenate([cosine, cosine], axis=1).astype(np.float32),
        np.concatenate([-sine, sine], axis=1).astype(np.float32),
    )


def turn(value, cosine, sine):
    return value * cosine + pltpu.roll(value, HEAD_SIZE // 2, 1) * sine


def inverse_norm(value):
    return lax.rsqrt(jnp.mean(value * value, axis=-1, keepdims=True) + epsilon)


def meet_y(me):
    barrier = pltpu.get_barrier_semaphore()
    pl.semaphore_signal(barrier, 1, device_id=me.y_mate, device_id_type=pl.DeviceIdType.MESH)
    pl.semaphore_wait(barrier, 1)


def gain_rows(aux_t, experts, chunks):
    head = [aux_t[experts + 2 + i : experts + 3 + i, :] for i in range(2)]
    width = HEAD_SIZE
    heads = [sum(row[:, c * width : (c + 1) * width] for c in range(chunks)) for row in head]
    return aux_t[experts : experts + 1, :], aux_t[experts + 1 : experts + 2, :], *heads


def probabilities(query, key, allowed):
    scores = jnp.where(allowed, dot(query, key, ((1,), (1,))) * SCORE_SCALE, masked_score)
    spread = jnp.exp(scores - jnp.max(scores, axis=-1, keepdims=True))
    return spread / jnp.sum(spread, axis=-1, keepdims=True)


def allowed_pairs(length, rows):
    later = lax.broadcasted_iota(jnp.int32, (rows, rows), 0)
    sooner = lax.broadcasted_iota(jnp.int32, (rows, rows), 1)
    return (sooner <= later) & (sooner < length)


def placed(count, offset):
    row = lax.broadcasted_iota(jnp.int32, (count, AUX), 0)
    return (row + offset == lax.broadcasted_iota(jnp.int32, (count, AUX), 1)).astype(jnp.bfloat16)


OPENING_PLAN = (
    ("w", 0, 0), ("a", 0), ("w", 1, 0), ("pair",), ("a", 1), ("b", 0, 0), ("w", 2, 0), ("a", 2),
    ("ax", 0), ("bx",), ("w", 3, 0), ("w", 0, 1), ("y1", 1, 0, 0), ("ax", 2), ("b", 0, 1),
    ("ax", 1), ("wx", 1, 0), ("b", 1, 1), ("ay0",), ("w", 1, 1), ("wx", 0, 0), ("b", 1, 0),
    ("wx", 2, 0), ("b", 2, 1), ("w", 2, 1), ("wx", 3, 0), ("y1", 1, 1, 0), ("prep",), ("qkv",),
    ("h", 0), ("y1", 1, 0, 1), ("b", 2, 0), ("w", 3, 1), ("y1", 0, 0, 1), ("h", 1), ("b", 3, 0),
    ("wx", 1, 1), ("h", 2), ("wx", 2, 1), ("a", 3), ("h", 3), ("wx", 0, 1), ("b", 3, 1),
    ("wx", 3, 1), ("ctx",), ("ax", 3), ("ctx2",), ("fin",), ("n", 0), ("y1", 0, 1, 0),
    ("y1", 1, 1, 1), ("c0",), ("n", 1), ("n", 2), ("c1",), ("n", 3), ("nx", 1), ("c2", 0),
    ("cz", 1, 1, 0), ("nx", 0), ("c2", 1), ("cz", 1, 1, 1), ("ny", 1), ("ny", 2),
    ("cz", 2, 1, 0), ("cz", 1, 0, 0), ("y1", 2, 0, 1), ("ny", 3), ("y1", 0, 1, 1),
    ("y1", 3, 1, 0), ("y1", 2, 1, 0), ("ny", 0), ("nx", 3), ("cz", 2, 1, 1), ("y1", 3, 0, 1),
    ("nx", 2), ("y1", 0, 0, 0), ("cz", 3, 1, 0), ("y1", 2, 0, 0), ("cz", 3, 1, 1),
    ("y1", 3, 0, 0), ("y1", 3, 1, 1), ("y1", 2, 1, 1), ("cz", 2, 0, 0), ("cz", 1, 0, 1),
    ("nca", 1), ("cz", 2, 0, 1), ("cz", 3, 0, 1), ("nca", 0), ("ncb", 2), ("ncb", 0),
    ("nca", 3), ("ncb", 1), ("ncb", 3), ("cz", 3, 0, 0), ("nca", 2),
)


def opening_kernel(
    experts, qkv,
    lengths, sequence_order, query_w, key_w, value_w, context_w, router_t, prenorm, midnorm,
    querynorm, keynorm, routes_t, d_src, x_src, cosine_in, sine_in,
    w_out, d_out, x_out,
    rows_o, sent_o, residual_o, normed_o, raw_o, query_o, key_o, value_o, context_o,
    x, w, ctx, aux_w, normed, raw, query, key, value, context, att, got, residual, sent,
    local_s, pair_s, wz_s, wx_s, wc_s, az_s, ax_s, ay_s, bz_s, bx_s, by_s, dc_s,
    in_s, w_s, out_s, y_s,
    w_src, flat_ctx, flat_router, flat_gains, head_gains, flat_routes, cosine, sine, load_s,
    nl_s, nz_s, nx_s, ny_s, ndx_s, ndy_s, nc_s, cx_s, cy_s, cz_s, cc_s,
):
    bf16, f32 = jnp.bfloat16, jnp.float32
    me = Place()
    half = d_src.shape[0] // 2
    low, high = pl.ds(0, half), pl.ds(half, half)
    width = w_src.shape[1]
    first_cols = qkv + AUX
    columns = (pl.ds(0, first_cols), pl.ds(first_cols, width - first_cols))
    waits, sent_on = [], []

    def near(k):
        return me.farthest(GRID_Z - 1 - k)

    def w_at(k, fx, p):
        return w_out.at[me.dp_at(near(k), fx, 0), :, columns[p]]

    def d_at(k, fx, fy, rows):
        return d_out.at[me.dp_at(near(k), fx, 0) * 2 + me.y_at(fy), rows]

    wide, narrow = query_w.shape[1], key_w.shape[1]
    loads = [
        pltpu.make_async_copy(source, target, load_s.at[i])
        for i, (source, target) in enumerate(
            (
                (context_w, flat_ctx),
                (router_t, flat_router),
                (prenorm, flat_gains.at[0]),
                (midnorm, flat_gains.at[1]),
                (querynorm, head_gains.at[0]),
                (keynorm, head_gains.at[1]),
                (routes_t, flat_routes),
                (query_w, w_src.at[:, pl.ds(0, wide)]),
                (key_w, w_src.at[:, pl.ds(wide, narrow)]),
                (value_w, w_src.at[:, pl.ds(wide + narrow, narrow)]),
                (cosine_in, cosine),
                (sine_in, sine),
            )
        )
    ]
    for copy in loads:
        copy.start()
    for copy in loads[:7]:
        copy.wait()
    count = head_gains.shape[2]
    top, block_rows = flat_routes.shape
    w_src[:, pl.ds(first_cols, width - first_cols)] = flat_ctx[...].astype(f32).T.astype(bf16)
    gains = jnp.concatenate(
        [
            flat_gains[0].astype(f32),
            flat_gains[1].astype(f32),
            dot(head_gains[0], placed(count, me.dp * count)),
            dot(head_gains[1], placed(count, me.dp * count)),
            jnp.zeros((4, AUX), f32),
        ],
        axis=0,
    ).T.astype(bf16)
    aux = dot(flat_router[...].astype(f32).T.astype(bf16), placed(experts, 0))
    aux = aux + dot(gains, placed(8, experts))
    for part in range(block_rows // AUX):
        some = flat_routes[:, part * AUX : (part + 1) * AUX].astype(f32).T.astype(bf16)
        aux = aux + dot(some, placed(top, experts + 4 + part * top))
    w_src[:, pl.ds(qkv, AUX)] = aux.astype(bf16)
    for copy in loads[7:]:
        copy.wait()
    for i, (source, target) in enumerate(
        (
            (w_src, w_out.at[me.dp]),
            (d_src, d_out.at[me.dp * 2 + me.y]),
            (x_src, x_out.at[me.y]),
        )
    ):
        copy = pltpu.make_async_copy(source, target, local_s.at[i])
        copy.start()
        waits.append(copy)
    me.greet()

    def line(k, source, target, sem, start_only):
        zn = near(k)
        for side, came, more, mate in (
            (0, zn < me.z, me.has_above, me.above),
            (1, zn > me.z, me.has_below, me.below),
        ):
            copy = remote(source, target, sem.at[0, side, zn], sem.at[1, side, zn], mate)
            if start_only:

                @pl.when(more)
                def _():
                    copy.start()
            else:

                @pl.when(came)
                def _():
                    copy.wait_recv()

                    @pl.when(more)
                    def _():
                        copy.start()

    def line_done(k, source, target, sem):
        zn = near(k)
        for side, came, more, mate in (
            (0, zn <= me.z, me.has_above, me.above),
            (1, zn >= me.z, me.has_below, me.below),
        ):
            copy = remote(source, target, sem.at[0, side, zn], sem.at[1, side, zn], mate)

            @pl.when(came)
            def _():
                @pl.when(more)
                def _():
                    copy.wait_send()

    def w_source(k, p):
        return w_src.at[:, columns[p]] if k == 0 else w_at(k, 0, p)

    def d_source(k, rows):
        return d_src.at[rows] if k == 0 else d_at(k, 0, 0, rows)

    def go(source, target, sem, index, mate):
        copy = remote(source, target, sem.at[(0, *index)], sem.at[(1, *index)], mate)
        copy.start()
        sent_on.append(copy)
        return copy

    def to_core(source, target, sem, index):
        go(source, target, sem, index, me.sibling)

    wx, ax, ay, by = {}, {}, {}, {}

    def w_own(k, p):
        line(k, w_source(k, p), w_at(k, 0, p), wz_s.at[p], k == 0)
        wx[k, p] = go(w_source(k, p), w_at(k, 0, p), wx_s, (k, p), me.x_mate)
        to_core(w_source(k, p), w_at(k, 0, p), wc_s, (k, 0, p))

    def w_across(k, p):
        wx[k, p].wait_recv()
        to_core(w_at(k, 1, p), w_at(k, 1, p), wc_s, (k, 1, p))

    def w_from_core(k, p):
        for fx in range(2):
            block = w_at(k, fx, p)
            remote(block, block, wc_s.at[0, k, fx, p], wc_s.at[1, k, fx, p], me.sibling).wait_recv()

    def a_over_y(k):
        ay[k, 0] = go(d_source(k, low), d_at(k, 0, 0, low), ay_s, (k, 0), me.y_mate)

    def a_own(k):
        line(k, d_source(k, low), d_at(k, 0, 0, low), az_s, k == 0)
        if k:
            a_over_y(k)
        ax[k] = go(d_source(k, low), d_at(k, 0, 0, low), ax_s, (k,), me.x_mate)
        to_core(d_source(k, low), d_at(k, 0, 0, low), dc_s, (k, 0, 0, 0))

    def a_across(k):
        ax[k].wait_recv()
        block = d_at(k, 1, 0, low)
        ay[k, 1] = go(block, block, ay_s, (k, 1), me.y_mate)
        to_core(block, block, dc_s, (k, 1, 0, 0))

    def b_own(k, fx):
        source = d_source(k, high) if fx == 0 else d_at(k, 1, 0, high)
        block = d_at(k, fx, 0, high)
        line(k, source, block, bz_s.at[fx], k == 0)
        by[k, fx] = go(source, block, by_s, (k, fx), me.y_mate)
        to_core(source, block, dc_s, (k, fx, 0, 1))

    def y_done(k, fx, h):
        (ay, by)[h][k, fx].wait_recv()
        block = d_at(k, fx, 1, (low, high)[h])
        to_core(block, block, dc_s, (k, fx, 1, h))

    rows, features = x.shape[0] * x.shape[1], x.shape[2]
    own_rows = rows // 2
    heads, key_heads = query.shape[0], key.shape[0]
    chunk = 512
    mine = pl.ds(pl.multiple_of(me.y * own_rows, own_rows), own_rows)
    theirs = pl.ds(pl.multiple_of((1 - me.y) * own_rows, own_rows), own_rows)
    turn_c, turn_s = cosine[...], sine[...]
    held, outs, copies = {}, [], []

    def pair_rows():
        held["pair"] = go(x_src, x_out.at[me.y], pair_s, (0,), me.y_mate)

    def b_over_x():
        held["bx"] = go(d_src.at[high], d_at(0, 0, 0, high), bx_s, (0,), me.x_mate)

    def b_step(k, fx):
        if (k, fx) == (0, 1):
            held["bx"].wait_recv()
        b_own(k, fx)

    def prepare():
        held["pair"].wait_recv()
        waits[2].wait()
        for k in range(GRID_Z):
            w_from_core(k, 0)
        waits[0].wait()
        loads = [
            pltpu.make_async_copy(w_out.at[:, :, pl.ds(qkv, AUX)], aux_w, in_s.at[1]),
            pltpu.make_async_copy(x_out, x, in_s.at[0]),
        ]
        held["parts"] = [
            pltpu.make_async_copy(
                w_out.at[:, :, pl.ds(c * chunk, chunk)],
                w.at[:, :, pl.ds(c * chunk, chunk)],
                w_s.at[c],
            )
            for c in range(qkv // chunk)
        ]
        for copy in loads + held["parts"]:
            copy.start()
        loads[0].wait()
        aux_t = aux_w[...].reshape(features, AUX).astype(f32).T
        held["gains"] = gain_rows(aux_t, experts, features // HEAD_SIZE)
        gain_one = held["gains"][0]
        loads[1].wait()

        def one(i, carry):
            at = pl.ds(pl.multiple_of(i * 32, 32), 32)
            for part in range(2):
                stream = x[part, at, :].astype(f32)
                there = pl.ds(pl.multiple_of(part * own_rows + i * 32, 32), 32)
                normed[there, :] = (stream * inverse_norm(stream) * gain_one).astype(bf16)
            return carry

        lax.fori_loop(0, own_rows // 32, one, 0)

    def project():
        for c, copy in enumerate(held["parts"]):
            copy.wait()
            cols = slice(c * chunk, (c + 1) * chunk)
            got_raw = dot(normed[...], w[:, :, cols].reshape(features, chunk))
            for h in range(chunk // HEAD_SIZE):
                raw[c * (chunk // HEAD_SIZE) + h] = got_raw[:, h * HEAD_SIZE : (h + 1) * HEAD_SIZE]
        for g in range(key_heads):
            unnormed = raw[heads + g]
            gained = unnormed * inverse_norm(unnormed) * held["gains"][3]
            key[g] = turn(gained, turn_c, turn_s).astype(bf16)
            value[g] = raw[heads + key_heads + g].astype(bf16)

    def attend(part):
        allowed = allowed_pairs(lengths[sequence_order[me.dp]], rows)
        query_gain = held["gains"][2]

        def head(h, carry):
            g = h // (heads // key_heads)
            unnormed = raw[h]
            gained = unnormed * inverse_norm(unnormed) * query_gain
            turned = turn(gained, turn_c, turn_s).astype(bf16)
            query[h] = turned
            probs = probabilities(turned, key[g], allowed).astype(bf16)
            at = pl.ds(pl.multiple_of(h * HEAD_SIZE, HEAD_SIZE), HEAD_SIZE)
            context[:, at] = dot(probs, value[g]).astype(bf16)
            return carry

        share = heads // 4
        lax.fori_loop(part * share, (part + 1) * share, head, 0)

    def save(pairs):
        for source, target in pairs:
            copy = pltpu.make_async_copy(source, target, out_s.at[len(outs)])
            copy.start()
            outs.append(copy)

    def ctx_part(c):
        span = chunk // ctx.shape[1]
        return ctx[c * span : (c + 1) * span].reshape(chunk, ctx.shape[2])

    def output_over_y():
        save(
            (
                (normed, normed_o), (raw, raw_o), (query, query_o), (key, key_o),
                (value, value_o), (context, context_o),
            )
        )
        for k in range(GRID_Z):
            w_from_core(k, 1)
        load = pltpu.make_async_copy(w_out.at[:, :, columns[1]], ctx, in_s.at[2])
        load.start()
        load.wait()
        for c in range(features // chunk):
            cols = pl.ds(c * chunk, chunk)
            att[:, cols] = dot(context[theirs, :], ctx_part(c), ((1,), (1,))).astype(bf16)
            copy = remote(att.at[:, cols], got.at[:, cols], y_s.at[0, c], y_s.at[1, c], me.y_mate)
            copy.start()
            copies.append(copy)

    def output_own():
        for c in range(features // chunk):
            residual[:, pl.ds(c * chunk, chunk)] = dot(context[mine, :], ctx_part(c), ((1,), (1,)))

    def finish():
        for copy in copies:
            copy.wait_recv()
        gain_two = held["gains"][1]

        def second_norm(i, carry):
            at = pl.ds(pl.multiple_of(i * 16, 16), 16)
            total = x[me.y, at, :].astype(f32) + (residual[at, :] + got[at, :].astype(f32))
            residual[at, :] = total
            sent[at, pl.ds(0, features)] = (total * inverse_norm(total) * gain_two).astype(bf16)
            return carry

        lax.fori_loop(0, own_rows // 16, second_norm, 0)
        logits = dot(sent[:, :features], aux_w[...].reshape(features, AUX))
        own = flat_routes[:, pl.ds(pl.multiple_of(me.y * own_rows, own_rows), own_rows)]
        own = own.astype(f32).T
        lane = lax.broadcasted_iota(jnp.int32, (own_rows, AUX), 1).astype(f32)
        hits = [lane == own[:, j : j + 1] for j in range(top)]
        picked = functools.reduce(jnp.logical_or, hits)
        logits = jnp.where(picked, logits, masked_score)
        spread = jnp.where(picked, jnp.exp(logits - jnp.max(logits, axis=-1, keepdims=True)), 0.0)
        gates = spread / jnp.sum(spread, axis=-1, keepdims=True)
        coarse = gates.astype(bf16).astype(f32)
        sent[:, pl.ds(features, AUX)] = (coarse + pltpu.roll(gates - coarse, experts, 1)).astype(bf16)
        save(((sent, sent_o), (residual, residual_o)))

    third = 3 * own_rows // 8
    n_low, n_high = pl.ds(0, third), pl.ds(third, third)
    n_most, n_rest = pl.ds(0, 2 * third), pl.ds(2 * third, own_rows - 2 * third)
    nx, ny, ndx, ndy, cy = {}, {}, {}, {}, {}

    def n_at(k, fx, fy, rows):
        return rows_o.at[me.dp_at(near(k), fx, 0) * 2 + me.y_at(fy), rows]

    def n_source(k, rows):
        return sent.at[rows] if k == 0 else n_at(k, 0, 0, rows)

    def n_own(k):
        source, block = n_source(k, n_most), n_at(k, 0, 0, n_most)
        line(k, source, block, nz_s, k == 0)
        nx[k] = go(source, block, nx_s, (k,), me.x_mate)
        ny[k] = go(source, block, ny_s, (k,), me.y_mate)
        to_core(source, block, nc_s, (k, 0))
        if k == 0:
            copy = pltpu.make_async_copy(sent, rows_o.at[me.dp * 2 + me.y], nl_s.at[0])
            copy.start()
            outs.append(copy)

    def n_over_y(k):
        nx[k].wait_recv()
        block = n_at(k, 1, 0, n_low)
        ndy[k] = go(block, block, ndy_s, (k,), me.y_mate)
        block = n_at(k, 1, 0, n_most)
        to_core(block, block, nc_s, (k, 1))

    def n_over_x(k):
        ny[k].wait_recv()
        block = n_at(k, 0, 1, n_high)
        ndx[k] = go(block, block, ndx_s, (k,), me.x_mate)
        block = n_at(k, 0, 1, n_most)
        to_core(block, block, nc_s, (k, 2))

    def n_corner(k, copies, rows, index):
        copies[k].wait_recv()
        block = n_at(k, 1, 1, rows)
        to_core(block, block, nc_s, (k, index))

    def c_line(k, fx, fy, source=None):
        block = n_at(k, fx, fy, n_rest)
        source = block if source is None else source
        line(k, source, block, cz_s.at[fx, fy], k == 0)
        to_core(source, block, cc_s, (k, fx, fy))

    def c_own():
        source, block = sent.at[n_rest], n_at(0, 0, 0, n_rest)
        held["cx"] = go(source, block, cx_s, (0,), me.x_mate)
        cy[0] = go(source, block, cy_s, (0,), me.y_mate)
        c_line(0, 0, 0, source)

    def c_from_x():
        held["cx"].wait_recv()
        block = n_at(0, 1, 0, n_rest)
        cy[1] = go(block, block, cy_s, (1,), me.y_mate)
        c_line(0, 1, 0)

    def c_from_y(fx):
        cy[fx].wait_recv()
        c_line(0, fx, 1)

    actions = {
        "n": n_own, "nx": n_over_y, "ny": n_over_x,
        "nca": lambda k: n_corner(k, ndy, n_low, 3), "ncb": lambda k: n_corner(k, ndx, n_high, 4),
        "c0": c_own, "c1": c_from_x, "c2": c_from_y, "cz": c_line,
        "pair": pair_rows, "bx": b_over_x, "ay0": lambda: a_over_y(0), "w": w_own, "wx": w_across,
        "a": a_own, "ax": a_across, "b": b_step, "y1": y_done, "prep": prepare, "qkv": project,
        "h": attend, "ctx": output_over_y, "ctx2": output_own, "fin": finish,
    }
    for name, *which in OPENING_PLAN:
        actions[name](*which)
    for k in range(GRID_Z):
        for p in range(2):
            line_done(k, w_source(k, p), w_at(k, 0, p), wz_s.at[p])
        line_done(k, d_source(k, low), d_at(k, 0, 0, low), az_s)
        line_done(k, d_source(k, high), d_at(k, 0, 0, high), bz_s.at[0])
        line_done(k, d_at(k, 1, 0, high), d_at(k, 1, 0, high), bz_s.at[1])
        line_done(k, n_source(k, n_most), n_at(k, 0, 0, n_most), nz_s)
        for fx in range(2):
            for fy in range(2):
                source = n_source(k, n_rest) if (fx, fy) == (0, 0) else n_at(k, fx, fy, n_rest)
                line_done(k, source, n_at(k, fx, fy, n_rest), cz_s.at[fx, fy])
    for copy in sent_on + copies:
        copy.wait_send()
    for k in range(GRID_Z):
        for fx in range(2):
            for fy in range(2):
                for h, at in enumerate((low, high)):
                    block = d_at(k, fx, fy, at)
                    remote(
                        block, block, dc_s.at[0, k, fx, fy, h], dc_s.at[1, k, fx, fy, h], me.sibling
                    ).wait_recv()
            for fy in range(2):
                block = n_at(k, fx, fy, n_rest)
                remote(
                    block, block, cc_s.at[0, k, fx, fy], cc_s.at[1, k, fx, fy], me.sibling
                ).wait_recv()
        for i, (fx, fy, at) in enumerate(
            ((0, 0, n_most), (1, 0, n_most), (0, 1, n_most), (1, 1, n_low), (1, 1, n_high))
        ):
            block = n_at(k, fx, fy, at)
            remote(block, block, nc_s.at[0, k, i], nc_s.at[1, k, i], me.sibling).wait_recv()
    waits[1].wait()
    for copy in outs:
        copy.wait()


def opening(
    lengths, sequence_order, weights, gains, routes, cotangents, inputs, experts, collective_id
):
    bf16, f32 = jnp.bfloat16, jnp.float32
    chips, pair = lax.axis_size("dp"), lax.axis_size("tensor")
    own_rows, features = inputs.shape
    rows = pair * own_rows
    query, key, value, context, router = weights
    shard, wide = query.shape
    heads, key_heads = wide // HEAD_SIZE, key.shape[1] // HEAD_SIZE
    width = 2 * wide + 2 * key.shape[1] + AUX
    count, top = gains[2].shape[0], routes.shape[1]
    qkv = (heads + 2 * key_heads) * HEAD_SIZE
    cosine, sine = turn_tables(rows)
    dma = pltpu.SemaphoreType.DMA
    shapes = (
        ((chips, shard, width), bf16),
        ((chips * pair, *cotangents.shape), bf16),
        ((pair, *inputs.shape), bf16),
        ((chips * pair, own_rows, features + AUX), bf16),
        ((own_rows, features + AUX), bf16),
        ((own_rows, features), f32),
        ((rows, features), bf16),
        ((heads + 2 * key_heads, rows, HEAD_SIZE), f32),
        ((heads, rows, HEAD_SIZE), bf16),
        ((key_heads, rows, HEAD_SIZE), bf16),
        ((key_heads, rows, HEAD_SIZE), bf16),
        ((rows, wide), bf16),
    )
    anywhere, smem = pl.BlockSpec(memory_space=pl.ANY), pl.BlockSpec(memory_space=pltpu.SMEM)
    w, d, x, gathered, *rest = pl.pallas_call(
        functools.partial(opening_kernel, experts, qkv),
        out_shape=tuple(jax.ShapeDtypeStruct(*shape) for shape in shapes),
        in_specs=[smem] * 2 + [anywhere] * 14,
        out_specs=(anywhere,) * len(shapes),
        scratch_shapes=[
            pltpu.VMEM((pair, own_rows, features), bf16),
            pltpu.VMEM((chips, shard, qkv), bf16),
            pltpu.VMEM((chips, shard, wide), bf16),
            pltpu.VMEM((chips, shard, AUX), bf16),
            pltpu.VMEM((rows, features), bf16),
            pltpu.VMEM((heads + 2 * key_heads, rows, HEAD_SIZE), f32),
            pltpu.VMEM((heads, rows, HEAD_SIZE), bf16),
            pltpu.VMEM((key_heads, rows, HEAD_SIZE), bf16),
            pltpu.VMEM((key_heads, rows, HEAD_SIZE), bf16),
            pltpu.VMEM((rows, wide), bf16),
            pltpu.VMEM((own_rows, features), bf16),
            pltpu.VMEM((own_rows, features), bf16),
            pltpu.VMEM((own_rows, features), f32),
            pltpu.VMEM((own_rows, features + AUX), bf16),
            dma((3,)),
            dma((2, 1)),
            dma((2, 2, 2, 4)),
            dma((2, 4, 2)),
            dma((2, 4, 2, 2)),
            dma((2, 2, 4)),
            dma((2, 4)),
            dma((2, 4, 2)),
            dma((2, 2, 2, 4)),
            dma((2, 1)),
            dma((2, 4, 2)),
            dma((2, 4, 2, 2, 2)),
            dma((3,)),
            dma((qkv // 512,)),
            dma((8,)),
            dma((2, features // 512)),
            pltpu.VMEM((shard, width), bf16),
            pltpu.VMEM(context.shape, bf16),
            pltpu.VMEM((experts, shard), bf16),
            pltpu.VMEM((2, 1, shard), bf16),
            pltpu.VMEM((2, 1, count), bf16),
            pltpu.VMEM((top, rows), jnp.int32),
            pltpu.VMEM((rows, HEAD_SIZE), f32),
            pltpu.VMEM((rows, HEAD_SIZE), f32),
            dma((12,)),
            dma((1,)),
            dma((2, 2, 4)),
            dma((2, 4)),
            dma((2, 4)),
            dma((2, 4)),
            dma((2, 4)),
            dma((2, 4, 5)),
            dma((2, 1)),
            dma((2, 2)),
            dma((2, 2, 2, 2, 4)),
            dma((2, 4, 2, 2)),
        ],
        compiler_params=pltpu.CompilerParams(
            collective_id=collective_id, has_side_effects=True, vmem_limit_bytes=ATTENTION_VMEM
        ),
    )(
        lengths, sequence_order, query, key, value, context, router.T,
        *(gain[None] for gain in gains), routes.T, cotangents, inputs, cosine, sine,
    )
    return (
        w.reshape(-1, w.shape[2]),
        d.reshape(chips, -1, d.shape[2]),
        x.reshape(-1, x.shape[2]),
        gathered.reshape(chips, -1, gathered.shape[2]),
        *rest,
    )


def unturn(value, cosine, sine):
    return value * cosine - pltpu.roll(value, HEAD_SIZE // 2, 1) * sine


def backward_kernel(
    experts, lengths, sequence_order, back_in, residual_in, sent_in, dy_in, x_in, packed,
    cosine_in, sine_in, normed_in,
    raw_in, query_in, key_in, value_in, context_in,
    grads, input_gradient,
    back, residual, sent, dy, x, w, ctx, aux_w, normed, raw, query, key, value, context,
    cot, context_cot, raw_cot, key_sum, value_sum, small, first, first_got, stage, result,
    cosine, sine, in_s, out_s, y_s, g_s,
):
    bf16, f32 = jnp.bfloat16, jnp.float32
    me = Place()
    own_rows, features = residual.shape
    rows = 2 * own_rows
    heads, key_heads = query.shape[0], key.shape[0]
    group = heads // key_heads
    qkv, wide = w.shape[1], heads * HEAD_SIZE
    chunk = 512
    mine = pl.ds(pl.multiple_of(me.y * own_rows, own_rows), own_rows)
    theirs = pl.ds(pl.multiple_of((1 - me.y) * own_rows, own_rows), own_rows)
    loads = [
        pltpu.make_async_copy(source, target, in_s.at[i])
        for i, (source, target) in enumerate(
            (
                (packed.at[:, pl.ds(qkv, AUX)], aux_w),
                (back_in, back),
                (sent_in, sent),
                (residual_in, residual),
                (dy_in, dy),
                (packed.at[:, pl.ds(qkv + AUX, wide)], ctx),
                (context_in, context),
                (value_in, value),
                (key_in, key),
                (query_in, query),
                (raw_in, raw),
                (packed.at[:, pl.ds(0, qkv)], w),
                (normed_in, normed),
                (x_in, x),
                (cosine_in, cosine),
                (sine_in, sine),
            )
        )
    ]
    for copy in loads:
        copy.start()
    meet_y(me)
    for copy in loads[:5]:
        copy.wait()
    aux_t = aux_w[...].astype(f32).T
    gain_one, gain_two, query_gain, key_gain = gain_rows(aux_t, experts, features // HEAD_SIZE)

    lane = lax.broadcasted_iota(jnp.int32, (own_rows, AUX), 1)
    coded = sent[:, features:].astype(f32)
    gates = coded + pltpu.roll(coded, AUX - experts, 1)
    gates = jnp.where(lane < experts, gates, 0.0)
    column = lax.broadcasted_iota(jnp.int32, (AUX, AUX), 0)
    target = lax.broadcasted_iota(jnp.int32, (AUX, AUX), 1)
    fold = ((column % (2 * experts)) // 2 == target).astype(bf16)
    gate_cot = dot(back[:, features:], fold)
    logit_cot = gates * (gate_cot - jnp.sum(gates * gate_cot, axis=-1, keepdims=True))
    logit_cot = logit_cot.astype(bf16)
    small[...] = dot(sent[:, :features], logit_cot, ((0,), (0,)))
    midnorm = jnp.zeros((1, features), f32)
    step = 32
    for i in range(own_rows // step):
        at = slice(i * step, (i + 1) * step)
        total = residual[at, :]
        scale = inverse_norm(total)
        unit = total * scale
        normed_cot = back[at, :features].astype(f32) + dot(
            logit_cot[at, :], aux_w[...], ((1,), (1,))
        )
        midnorm = midnorm + jnp.sum(normed_cot * unit, axis=0, keepdims=True)
        gained = normed_cot * gain_two
        total_cot = dy[at, :].astype(f32) + scale * (
            gained - unit * jnp.mean(gained * unit, axis=-1, keepdims=True)
        )
        residual[at, :] = total_cot
        cot[pl.ds(pl.multiple_of(me.y * own_rows + i * step, step), step), :] = total_cot.astype(bf16)
    swap = remote(cot.at[mine], cot.at[mine], y_s.at[0, 0], y_s.at[1, 0], me.y_mate)
    swap.start()
    for copy in loads[5:10]:
        copy.wait()

    def spread_context(part):
        for c in range(wide // chunk):
            cols = pl.ds(c * chunk, chunk)
            context_cot[part, cols] = dot(cot[part, :], ctx[:, cols]).astype(bf16)

    spread_context(mine)
    swap.wait_recv()
    spread_context(theirs)
    for copy in loads[10:]:
        copy.wait()

    turn_c, turn_s = cosine[...], sine[...]
    allowed = allowed_pairs(lengths[sequence_order[me.dp]], rows)
    key_sum[...] = jnp.zeros_like(key_sum)
    value_sum[...] = jnp.zeros_like(value_sum)

    def raw_back(back_rows, unnormed, gain):
        scale = inverse_norm(unnormed)
        unit = unnormed * scale
        part = jnp.sum(back_rows * unit, axis=0, keepdims=True)
        gained = back_rows * gain
        raw_rows = scale * (gained - unit * jnp.mean(gained * unit, axis=-1, keepdims=True))
        return raw_rows.astype(bf16), part

    def head(h, query_part):
        g = h // group
        at = pl.ds(pl.multiple_of(h * HEAD_SIZE, HEAD_SIZE), HEAD_SIZE)
        probs = probabilities(query[h], key[g], allowed)
        cots = context_cot[:, at]
        prob_cot = dot(cots, value[g], ((1,), (1,)))
        score_cot = probs * (prob_cot - jnp.sum(probs * prob_cot, axis=-1, keepdims=True))
        score_cot = score_cot.astype(bf16)
        value_sum[g] += dot(probs.astype(bf16), cots, ((0,), (0,)))
        key_sum[g] += dot(score_cot, query[h], ((0,), (0,)))
        turned = dot(score_cot, key[g]) * SCORE_SCALE
        raw_cot[:, at], part = raw_back(unturn(turned, turn_c, turn_s), raw[h], query_gain)
        return query_part + part

    query_part = lax.fori_loop(0, heads, head, jnp.zeros((1, HEAD_SIZE), f32))
    key_part = jnp.zeros((1, HEAD_SIZE), f32)
    for g in range(key_heads):
        turned = key_sum[g] * SCORE_SCALE
        at = wide + g * HEAD_SIZE
        raw_cot[:, at : at + HEAD_SIZE], part = raw_back(
            unturn(turned, turn_c, turn_s), raw[heads + g], key_gain
        )
        key_part = key_part + part
        at = at + key_heads * HEAD_SIZE
        raw_cot[:, at : at + HEAD_SIZE] = value_sum[g].astype(bf16)

    copies = []
    for c in range(features // chunk):
        cols = pl.ds(c * chunk, chunk)
        first[:, cols] = dot(raw_cot[theirs, :], w[cols, :], ((1,), (1,))).astype(bf16)
        copy = remote(
            first.at[:, cols], first_got.at[:, cols], y_s.at[0, 1 + c], y_s.at[1, 1 + c], me.y_mate
        )
        copy.start()
        copies.append(copy)
    block = 256

    def store(i):
        slot = i % 2
        return pltpu.make_async_copy(
            stage.at[slot],
            grads.at[pl.ds(pl.multiple_of(i * block, block), block), pl.ds(0, qkv + wide)],
            g_s.at[slot],
        )

    def weight_grads(i, carry):
        slot = i % 2
        at = pl.ds(pl.multiple_of(i * block, block), block)

        @pl.when(i >= 2)
        def _():
            store(i - 2).wait()

        for c in range(qkv // chunk):
            cols = pl.ds(c * chunk, chunk)
            stage[slot, :, cols] = dot(normed[:, at], raw_cot[:, cols], ((0,), (0,))).astype(bf16)
        for c in range(wide // chunk):
            cols = pl.ds(c * chunk, chunk)
            stage[slot, :, pl.ds(qkv + c * chunk, chunk)] = dot(
                cot[:, at], context[:, cols], ((0,), (0,))
            ).astype(bf16)
        store(i).start()
        return carry

    lax.fori_loop(0, features // block, weight_grads, 0)
    prenorm = jnp.zeros((1, features), f32)
    for copy in copies:
        copy.wait_recv()
    for c in range(features // chunk):
        cols = pl.ds(c * chunk, chunk)
        back_cols = dot(raw_cot[mine, :], w[cols, :], ((1,), (1,)))
        result_part = back_cols + first_got[:, cols].astype(f32)
        back[:, cols] = result_part.astype(bf16)
    step = 32
    for i in range(own_rows // step):
        at = slice(i * step, (i + 1) * step)
        stream = x[pl.ds(pl.multiple_of(me.y * own_rows + i * step, step), step), :].astype(f32)
        scale = inverse_norm(stream)
        unit = stream * scale
        first_cot = back[at, :features].astype(f32)
        prenorm = prenorm + jnp.sum(first_cot * unit, axis=0, keepdims=True)
        gained = first_cot * gain_one
        result[at, :] = (
            residual[at, :]
            + scale * (gained - unit * jnp.mean(gained * unit, axis=-1, keepdims=True))
        ).astype(bf16)
    done = pltpu.make_async_copy(result, input_gradient, out_s.at[0])
    done.start()
    chunks = features // HEAD_SIZE
    extra = jnp.concatenate(
        [
            jnp.zeros((experts, features), f32),
            prenorm,
            midnorm,
            jnp.concatenate([query_part] * chunks, axis=1),
            jnp.concatenate([key_part] * chunks, axis=1),
            jnp.zeros((AUX - experts - 4, features), f32),
        ],
        axis=0,
    )
    aux_w[...] = (small[...] + extra.T).astype(bf16)
    last = pltpu.make_async_copy(aux_w, grads.at[:, pl.ds(qkv + wide, AUX)], out_s.at[1])
    last.start()
    swap.wait_send()
    for copy in copies:
        copy.wait_send()
    for i in (2, 1):
        store(features // block - i).wait()
    done.wait()
    last.wait()


def attention_backward(
    lengths, sequence_order, back, residual, sent, dy, x_pair, packed, saved, experts, collective_id
):
    bf16, f32 = jnp.bfloat16, jnp.float32
    normed, raw, query, key, value, context = saved
    own_rows, features = residual.shape
    rows = 2 * own_rows
    heads, key_heads = query.shape[0], key.shape[0]
    wide = heads * HEAD_SIZE
    qkv = wide + 2 * key_heads * HEAD_SIZE
    cosine, sine = turn_tables(rows)
    dma = pltpu.SemaphoreType.DMA
    anywhere, smem = pl.BlockSpec(memory_space=pl.ANY), pl.BlockSpec(memory_space=pltpu.SMEM)
    return pl.pallas_call(
        functools.partial(backward_kernel, experts),
        out_shape=(
            jax.ShapeDtypeStruct((features, qkv + wide + AUX), bf16),
            jax.ShapeDtypeStruct((own_rows, features), bf16),
        ),
        in_specs=[smem] * 2 + [anywhere] * 14,
        out_specs=(anywhere,) * 2,
        scratch_shapes=[
            pltpu.VMEM((own_rows, features + AUX), bf16),
            pltpu.VMEM((own_rows, features), f32),
            pltpu.VMEM((own_rows, features + AUX), bf16),
            pltpu.VMEM((own_rows, features), bf16),
            pltpu.VMEM((rows, features), bf16),
            pltpu.VMEM((features, qkv), bf16),
            pltpu.VMEM((features, wide), bf16),
            pltpu.VMEM((features, AUX), bf16),
            pltpu.VMEM((rows, features), bf16),
            pltpu.VMEM((heads + 2 * key_heads, rows, HEAD_SIZE), f32),
            pltpu.VMEM((heads, rows, HEAD_SIZE), bf16),
            pltpu.VMEM((key_heads, rows, HEAD_SIZE), bf16),
            pltpu.VMEM((key_heads, rows, HEAD_SIZE), bf16),
            pltpu.VMEM((rows, wide), bf16),
            pltpu.VMEM((rows, features), bf16),
            pltpu.VMEM((rows, wide), bf16),
            pltpu.VMEM((rows, qkv), bf16),
            pltpu.VMEM((key_heads, rows, HEAD_SIZE), f32),
            pltpu.VMEM((key_heads, rows, HEAD_SIZE), f32),
            pltpu.VMEM((features, AUX), f32),
            pltpu.VMEM((own_rows, features), bf16),
            pltpu.VMEM((own_rows, features), bf16),
            pltpu.VMEM((2, 256, qkv + wide), bf16),
            pltpu.VMEM((own_rows, features), bf16),
            pltpu.VMEM((rows, HEAD_SIZE), f32),
            pltpu.VMEM((rows, HEAD_SIZE), f32),
            dma((16,)),
            dma((2,)),
            dma((2, 1 + features // 512)),
            dma((2,)),
        ],
        compiler_params=pltpu.CompilerParams(
            collective_id=collective_id, has_side_effects=True, vmem_limit_bytes=ATTENTION_VMEM
        ),
    )(
        lengths, sequence_order, back, residual, sent, dy, x_pair, packed, cosine, sine,
        normed, raw, query, key, value, context,
    )


LAST_CUT = 5
LAST_PLAN = (
    ("gx", 0, 0), ("dy", 0, 1, 1), ("gx", 0, 1), ("dy", 0, 0, 1), ("dy", 1, 1, 1), ("db", 0, 1),
    ("gx", 1, 1), ("db", 0, 0), ("dy", 2, 1, 1), ("dy", 1, 1, 0), ("gx", 1, 0), ("db", 1, 1),
    ("dy", 2, 1, 0), ("gx", 2, 0), ("db", 2, 1), ("dy", 0, 1, 0), ("dy", 2, 0, 1),
    ("dy", 0, 0, 0), ("dy", 3, 1, 1), ("gc", 0), ("dy", 1, 0, 0), ("dy", 1, 0, 1),
    ("dy", 3, 1, 0), ("dy", 2, 0, 0), ("gx", 2, 1), ("dax", 2), ("dax", 0), ("dax", 1),
    ("gc", 1), ("gc", 2), ("gx", 3, 0), ("dy", 3, 0, 1), ("gx", 3, 1), ("da", 0), ("dax", 3),
    ("dy", 3, 0, 0), ("db", 1, 0), ("da", 1), ("db", 2, 0), ("da", 2), ("gc", 3), ("sm",),
    ("db", 3, 1), ("db", 3, 0), ("sm2",), ("da", 3), ("bx",),
)


def last_scatter_kernel(
    g_part, d_part, g_out, d_out,
    g_own, g_core, g_x, g_z, d_own, d_core, d_y, a_x, b_x, a_z, b_z, small_got,
    gl_s, gc_s, gx_s, gz_s, dl_s, dc_s, dy_s, ax_s, bx_s, az_s, bz_s, small_s, out_s,
):
    me = Place()
    g_rows, d_rows = g_own.shape[2], d_own.shape[3]
    cut, g_half = a_x.shape[1], g_rows // 2
    g_all, low, high = (0, g_rows), (0, cut), (cut, d_rows - cut)
    low_at, high_at = pl.ds(0, cut), pl.ds(cut, d_rows - cut)
    last = GRID_Z - 1
    loads, cores, sends = {}, {}, []

    def g_chunk(k, fx, fc):
        return g_part.at[me.dp_at(me.farthest(k), fx, fc)]

    def d_chunk(k, fx, fy, fc):
        return d_part.at[me.dp_at(me.farthest(k), fx, fc) * 2 + me.y_at(fy)]

    pairs = ((1, 1), (0, 1), (1, 0), (0, 0))
    for k in range(GRID_Z):
        for fx in (1, 0):
            loads[k, fx] = pltpu.make_async_copy(g_chunk(k, fx, 0), g_own.at[k, fx], gl_s.at[k, fx])
            loads[k, fx].start()
        for fx, fy in pairs:
            loads[k, fx, fy] = pltpu.make_async_copy(
                d_chunk(k, fx, fy, 0), d_own.at[k, fx, fy], dl_s.at[k, fx, fy]
            )
            loads[k, fx, fy].start()
    me.greet()
    for k in range(GRID_Z):
        for fx in (1, 0):
            cores[k, fx] = remote(
                g_chunk(k, fx, 1), g_core.at[k, fx],
                gc_s.at[0, k, fx], gc_s.at[1, k, fx], me.sibling,
            )
        for fx, fy in pairs:
            cores[k, fx, fy] = remote(
                d_chunk(k, fx, fy, 1), d_core.at[k, fx, fy],
                dc_s.at[0, k, fx, fy], dc_s.at[1, k, fx, fy], me.sibling,
            )
        for index in ((1,), (1, 1), (0, 1), (0,), (1, 0), (0, 0)):
            cores[(k, *index)].start()

    gx = [
        [
            remote(
                g_own.at[k, 1, pl.ds(h * g_half, g_half)], g_x.at[k, pl.ds(h * g_half, g_half)],
                gx_s.at[0, k, h], gx_s.at[1, k, h], me.x_mate,
            )
            for h in range(2)
        ]
        for k in range(GRID_Z)
    ]
    dy = {
        (k, fx, h): remote(
            d_own.at[k, fx, 1, at], d_y.at[k, fx, at],
            dy_s.at[0, k, fx, h], dy_s.at[1, k, fx, h], me.y_mate,
        )
        for k in range(GRID_Z)
        for fx in range(2)
        for h, at in enumerate((low_at, high_at))
    }
    ax = [
        remote(d_own.at[k, 1, 0, low_at], a_x.at[k], ax_s.at[0, k], ax_s.at[1, k], me.x_mate)
        for k in range(GRID_Z)
    ]
    bx = remote(d_own.at[last, 1, 0, high_at], b_x, bx_s.at[0], bx_s.at[1], me.x_mate)

    here = set()

    def arrive(*index):
        if index not in here:
            here.add(index)
            loads[index].wait()
            cores[index].wait_recv()

    def onward(source, buffer, sem, to, side, mate):
        ends = 1 - (me.z - 1 - to + GRID_Z - 1) // GRID_Z
        slot = to if side == 0 else to + (GRID_Z - to) * ends
        return remote(source, buffer.at[slot], sem.at[0, to], sem.at[1, slot], mate)

    def line(k, block, source, rows, buffer, sem, shift):
        to = me.farthest(k)
        for side, ahead, mate, more in (
            (0, to > me.z, me.above, me.has_below),
            (1, to < me.z, me.below, me.has_above),
        ):
            slot = to if k < last or side == 0 else GRID_Z
            came = remote(source, buffer.at[slot], sem.at[0, slot], sem.at[1, slot], mate)

            def gather(came=came, slot=slot):
                came.wait_recv()
                add_rows(block, [(buffer.at[slot], shift)], rows)

            if k < last:

                @pl.when(ahead)
                def _():
                    pl.when(more)(gather)
                    onward(source, buffer, sem, to, side, mate).start()
            else:
                pl.when(more)(gather)

    def line_done(k, source, buffer, sem):
        to = me.farthest(k)
        for side, ahead, mate in ((0, to > me.z, me.above), (1, to < me.z, me.below)):

            @pl.when(ahead)
            def _():
                onward(source, buffer, sem, to, side, mate).wait_send()

    width = g_own.shape[3]
    small_block = g_own.at[last, 0, :, pl.ds(width - AUX, AUX)]
    small = remote(small_block, small_got, small_s.at[0], small_s.at[1], me.y_mate)

    def g_across(k, h):
        arrive(k, 1)
        add_rows(g_own.at[k, 1], [(g_core.at[k, 1], 0)], (h * g_half, g_half))
        gx[k][h].start()

    def g_column(k):
        arrive(k, 0)
        for h in range(2):
            gx[k][h].wait_recv()
        add_rows(g_own.at[k, 0], [(g_core.at[k, 0], 0), (g_x.at[k], 0)], g_all)
        line(k, g_own.at[k, 0], g_own.at[k, 0], g_all, g_z, gz_s, 0)

    def over_y(k, fx, h):
        arrive(k, fx, 1)
        add_rows(d_own.at[k, fx, 1], [(d_core.at[k, fx, 1], 0)], (low, high)[h])
        dy[k, fx, h].start()

    def from_y(k, fx, h, *more):
        arrive(k, fx, 0)
        dy[k, fx, h].wait_recv()
        rest = [(d_core.at[k, fx, 0], 0), (d_y.at[k, fx], 0), *more]
        add_rows(d_own.at[k, fx, 0], rest, (low, high)[h])

    def b_line(k, fx):
        from_y(k, fx, 1)
        block = d_own.at[k, fx, 0]
        line(k, block, block.at[high_at], high, b_z.at[fx], bz_s.at[fx], cut)
        if fx and k == last:
            bx.start()

    def a_over_x(k):
        from_y(k, 1, 0)
        ax[k].start()

    def a_line(k):
        ax[k].wait_recv()
        from_y(k, 0, 0, (a_x.at[k], 0))
        block = d_own.at[k, 0, 0]
        line(k, block, block.at[low_at], low, a_z, az_s, 0)

    def b_from_x():
        bx.wait_recv()
        add_rows(d_own.at[last, 0, 0], [(b_x, cut)], high)

    def small_sum():
        small.wait()
        total = small_block[...].astype(jnp.float32) + small_got[...].astype(jnp.float32)
        small_block[...] = total.astype(small_got.dtype)

    actions = {
        "gx": g_across, "gc": g_column, "dy": over_y, "db": b_line, "dax": a_over_x, "da": a_line,
        "bx": b_from_x, "sm": small.start, "sm2": small_sum,
    }
    for name, *which in LAST_PLAN:
        actions[name](*which)
    outs = [
        pltpu.make_async_copy(d_own.at[last, 0, 0], d_out, out_s.at[0]),
        pltpu.make_async_copy(g_own.at[last, 0], g_out, out_s.at[1]),
    ]
    for copy in outs:
        copy.start()
    for k in range(GRID_Z):
        for h in range(2):
            gx[k][h].wait_send()
        for fx in range(2):
            for h in range(2):
                dy[k, fx, h].wait_send()
        ax[k].wait_send()
        if k < last:
            line_done(k, g_own.at[k, 0], g_z, gz_s)
            for fx in range(2):
                line_done(k, d_own.at[k, fx, 0, high_at], b_z.at[fx], bz_s.at[fx])
            line_done(k, d_own.at[k, 0, 0, low_at], a_z, az_s)
    bx.wait_send()
    for sent in cores.values():
        sent.wait_send()
    for copy in outs:
        copy.wait()


def last_scatter(grads, sums, collective_id):
    chips, pair = lax.axis_size("dp"), lax.axis_size("tensor")
    g_rows, g_wide = grads.shape[0] // chips, grads.shape[1]
    d_rows, d_wide = sums.shape[0] // (chips * pair), sums.shape[1]
    cut = d_rows * LAST_CUT // 8
    dma = pltpu.SemaphoreType.DMA
    low = grads.dtype
    anywhere = pl.BlockSpec(memory_space=pl.ANY)
    return pl.pallas_call(
        last_scatter_kernel,
        out_shape=(
            jax.ShapeDtypeStruct((g_rows, g_wide), low),
            jax.ShapeDtypeStruct((d_rows, d_wide), low),
        ),
        in_specs=[anywhere] * 2,
        out_specs=(anywhere,) * 2,
        scratch_shapes=[
            pltpu.VMEM((4, 2, g_rows, g_wide), low),
            pltpu.VMEM((4, 2, g_rows, g_wide), low),
            pltpu.VMEM((4, g_rows, g_wide), low),
            pltpu.VMEM((5, g_rows, g_wide), low),
            pltpu.VMEM((4, 2, 2, d_rows, d_wide), low),
            pltpu.VMEM((4, 2, 2, d_rows, d_wide), low),
            pltpu.VMEM((4, 2, d_rows, d_wide), low),
            pltpu.VMEM((4, cut, d_wide), low),
            pltpu.VMEM((d_rows - cut, d_wide), low),
            pltpu.VMEM((5, cut, d_wide), low),
            pltpu.VMEM((2, 5, d_rows - cut, d_wide), low),
            pltpu.VMEM((g_rows, AUX), low),
            dma((4, 2)),
            dma((2, 4, 2)),
            dma((2, 4, 2)),
            dma((2, 5)),
            dma((4, 2, 2)),
            dma((2, 4, 2, 2)),
            dma((2, 4, 2, 2)),
            dma((2, 4)),
            dma((2,)),
            dma((2, 5)),
            dma((2, 2, 5)),
            dma((2,)),
            dma((2,)),
        ],
        compiler_params=pltpu.CompilerParams(
            collective_id=collective_id, has_side_effects=True, vmem_limit_bytes=60 * 1024 * 1024
        ),
    )(grads.reshape(chips, g_rows, g_wide), sums.reshape(chips * pair, d_rows, d_wide))


def unpack_kernel(
    experts, summed, added, residual,
    layer_output, query, key, value, context, router, prenorm, midnorm, querynorm, keynorm,
):
    f32 = jnp.float32
    wide, narrow = query.shape[1], key.shape[1]
    layer_output[...] = (residual[...] + added[...].astype(f32)).astype(layer_output.dtype)
    query[...] = summed[:, pl.ds(0, wide)].astype(f32)
    key[...] = summed[:, pl.ds(wide, narrow)].astype(f32)
    value[...] = summed[:, pl.ds(wide + narrow, narrow)].astype(f32)
    start = wide + 2 * narrow
    context[...] = summed[:, pl.ds(start, wide)].astype(f32).T
    small = summed[:, pl.ds(start + wide, AUX)].astype(f32)
    router[...] = small[:, :experts]
    rows = small.T
    prenorm[...] = rows[experts : experts + 1, :]
    midnorm[...] = rows[experts + 1 : experts + 2, :]
    count = querynorm.shape[1]
    lane = lax.broadcasted_iota(jnp.int32, (count, AUX), 1)
    row = lax.broadcasted_iota(jnp.int32, (count, AUX), 0)
    pick = row + lax.axis_index("dp") * count == lane
    for target, at in ((querynorm, experts + 2), (keynorm, experts + 3)):
        part = jnp.where(pick, rows[at : at + 1, :], 0.0)
        target[...] = jnp.sum(part, axis=1, keepdims=True).T


def unpack(summed, added, residual, query_width, key_width, experts, norm_part):
    bf16, f32 = jnp.bfloat16, jnp.float32
    shard = summed.shape[0]
    own_rows, features = residual.shape
    shapes = (
        ((own_rows, features), bf16),
        ((shard, query_width), f32),
        ((shard, key_width), f32),
        ((shard, key_width), f32),
        ((query_width, shard), f32),
        ((shard, experts), f32),
        ((1, shard), f32),
        ((1, shard), f32),
        ((1, norm_part), f32),
        ((1, norm_part), f32),
    )
    vmem = pl.BlockSpec(memory_space=pltpu.VMEM)
    *large, first, second, third, fourth = pl.pallas_call(
        functools.partial(unpack_kernel, experts),
        out_shape=tuple(jax.ShapeDtypeStruct(*shape) for shape in shapes),
        in_specs=[vmem] * 3,
        out_specs=(vmem,) * len(shapes),
        compiler_params=pltpu.CompilerParams(vmem_limit_bytes=32 * 1024 * 1024),
    )(summed, added, residual)
    return (*large, first[0], second[0], third[0], fourth[0])


def gathered_body(
    layer_input,
    query_weight,
    key_projection,
    value_projection,
    context_weight,
    router_weight,
    expert_gate,
    expert_up,
    expert_down,
    prenorm_gain,
    midnorm_gain,
    querynorm_gain,
    keynorm_gain,
    routes,
    lengths,
    sequence_order,
    output_cotangent,
):
    bf16, f32 = jnp.bfloat16, jnp.float32
    tensor_count = lax.axis_size("tensor")
    tensor_index = lax.axis_index("tensor")
    dp_count = lax.axis_size("dp")
    dp_index = lax.axis_index("dp")
    own_rows, features = layer_input.shape
    block_rows = own_rows * tensor_count
    tokens = block_rows * dp_count
    expert_count = EXP_DEV * dp_count
    capacity = 3 * block_rows * TOP // (4 * EXP_DEV)
    most_rows = (5 * block_rows * TOP + 4 * expert_count - 1) // (4 * expert_count)
    shard = features // dp_count
    query_width = query_weight.shape[1]
    key_width = key_projection.shape[1]
    norm_part = HEAD_SIZE // dp_count

    packed, cot_all, input_rows, normed_all, sent, residual, *saved = opening(
        lengths,
        sequence_order,
        (query_weight, key_projection, value_projection, context_weight, router_weight),
        (prenorm_gain, midnorm_gain, querynorm_gain, keynorm_gain),
        routes,
        output_cotangent,
        layer_input,
        expert_count,
        0,
    )
    route_from = query_width + 2 * key_width + expert_count + 4
    routes_all = packed[:, route_from : route_from + 2 * TOP].astype(jnp.int32)
    routes_all = routes_all.reshape(dp_count, shard, 2, TOP).transpose(0, 3, 2, 1)
    routes_all = routes_all.reshape(dp_count, TOP, block_rows)
    position = jnp.arange(block_rows, dtype=jnp.int32)
    live = position[None, :] < lengths[sequence_order][:, None]

    expert_own = dp_index * EXP_DEV + jnp.arange(EXP_DEV, dtype=jnp.int32)
    hot = jnp.any(routes_all[:, None, :, :] == expert_own[None, :, None, None], axis=2)
    hot = hot & live[:, None, :]
    before = (position[:, None] < position[None, :]).astype(bf16)
    rank = jnp.einsum("bes,st->bet", hot.astype(bf16), before, preferred_element_type=f32)
    rank = rank.astype(jnp.int32)
    counts = rank[:, :, -1] + hot[:, :, -1]
    earlier = jnp.cumsum(counts, axis=0) - counts
    slot = earlier[:, :, None] + rank
    slot = jnp.where(hot & (slot < capacity), slot, -capacity)
    begin = jnp.minimum(earlier, capacity) // WINDOW_ALIGN * WINDOW_ALIGN
    info = jnp.concatenate([dp_index[None], begin.reshape(-1), tensor_index[None]])
    out_part, back_part, gate_gradient, up_gradient, down_gradient = expert_layer(
        info.astype(jnp.int32),
        slot,
        normed_all,
        cot_all,
        expert_gate,
        expert_up,
        expert_down,
        capacity,
        most_rows,
    )
    returned = scatter_all(back_part.reshape(tokens, features + AUX), 3)
    grads, input_gradient = attention_backward(
        lengths,
        sequence_order,
        returned,
        residual,
        sent,
        output_cotangent,
        input_rows,
        packed,
        saved,
        expert_count,
        6,
    )
    summed, expert_sum = last_scatter(grads, out_part.reshape(tokens, features), 4)
    (
        layer_output,
        query_gradient,
        key_gradient,
        value_gradient,
        context_gradient,
        router_gradient,
        prenorm_gradient,
        midnorm_gradient,
        querynorm_gradient,
        keynorm_gradient,
    ) = unpack(summed, expert_sum, residual, query_width, key_width, expert_count, norm_part)
    return (
        layer_output,
        input_gradient,
        query_gradient,
        key_gradient,
        value_gradient,
        context_gradient,
        router_gradient,
        gate_gradient,
        up_gradient,
        down_gradient,
        prenorm_gradient,
        midnorm_gradient,
        querynorm_gradient,
        keynorm_gradient,
    )


def solution(mesh):
    return jax.shard_map(
        gathered_body if mesh.shape["dp"] <= 16 else body,
        mesh=mesh,
        in_specs=(
            P(("dp", "tensor"), None),
            P("dp", "tensor"),
            P("dp", "tensor"),
            P("dp", "tensor"),
            P("tensor", "dp"),
            P("dp", None),
            P("dp", None, "tensor"),
            P("dp", None, "tensor"),
            P("dp", "tensor", None),
            P("dp"),
            P("dp"),
            P("dp"),
            P("dp"),
            P("dp", None),
            P(),
            P(),
            P(("dp", "tensor"), None),
        ),
        out_specs=(
            P(("dp", "tensor"), None),
            P(("dp", "tensor"), None),
            P("dp", "tensor"),
            P("dp", "tensor"),
            P("dp", "tensor"),
            P("tensor", "dp"),
            P("dp", None),
            P("dp", None, "tensor"),
            P("dp", None, "tensor"),
            P("dp", "tensor", None),
            P("dp"),
            P("dp"),
            P("dp"),
            P("dp"),
        ),
        check_vma=False,
    )
```

```python
import functools
import math

import jax
import jax.numpy as jnp
import numpy as np
from jax import lax
from jax.experimental import pallas as pl
from jax.experimental.pallas import tpu as pltpu
from jax.sharding import PartitionSpec as P

HEAD_SIZE = 128
TOP = 8
EXP_DEV = 2


epsilon = 1e-06
rope_base = 1000000.0
masked_score = -1e30


def carried_in(value, axis, combine, identity):
    count, place = (lax.axis_size(axis), lax.axis_index(axis))
    everything = lax.all_gather(value, axis)
    start = jnp.broadcast_to(jnp.asarray(identity, value.dtype), value.shape)

    def hop(k, before):
        reached = k < place
        new = combine(before, everything[k])
        return jnp.where(reached, new, before)

    return lax.fori_loop(0, count, hop, start)


def rms_normalize(value_rows):
    scaling = lax.rsqrt(jnp.mean(value_rows * value_rows, axis=-1, keepdims=True) + epsilon)
    return (value_rows * scaling, scaling)


def norm_back(cotangent, unit_rows, scaling):
    return scaling * (
        cotangent - unit_rows * jnp.mean(cotangent * unit_rows, axis=-1, keepdims=True)
    )


def rotary_apply(value_rows, cosine_table, sine_values):
    middle = value_rows.shape[-1] // 2
    former = value_rows[..., :middle]
    latter = value_rows[..., middle:]
    return jnp.concatenate(
        [
            former * cosine_table - latter * sine_values,
            latter * cosine_table + former * sine_values,
        ],
        axis=-1,
    )


def matrix_product(former, latter):
    return jnp.dot(former, latter, preferred_element_type=jnp.float32)


def contract(former, latter):
    return lax.dot_general(
        former, latter, (((0,), (0,)), ((), ())), preferred_element_type=jnp.float32
    )


def transposed(former, latter):
    return lax.dot_general(
        former, latter, (((1,), (1,)), ((), ())), preferred_element_type=jnp.float32
    )


def to_owners(buffer):
    return lax.all_to_all(buffer, "dp", split_axis=1, concat_axis=1, tiled=True)


def owner_reduce(partial_rows):
    shares = lax.psum_scatter(
        partial_rows.astype(jnp.bfloat16), "tensor", scatter_dimension=2, tiled=True
    )
    return lax.all_gather(shares, "tensor", axis=2, tiled=True)


def body(
    layer_input,
    query_weight,
    key_projection,
    value_projection,
    context_weight,
    router_weight,
    expert_gate,
    expert_up,
    expert_down,
    prenorm_gain,
    midnorm_gain,
    querynorm_gain,
    keynorm_gain,
    routes,
    lengths,
    sequence_order,
    output_cotangent,
):
    tensor_count = lax.axis_size("tensor")
    tensor_index = lax.axis_index("tensor")
    dp_count = lax.axis_size("dp")
    own_rows = layer_input.shape[0]
    block_rows = own_rows * tensor_count
    features = layer_input.shape[1]
    expert_count = EXP_DEV * dp_count
    capacity = 3 * block_rows * TOP // (4 * EXP_DEV)
    most_rows = (5 * block_rows * TOP + 4 * expert_count - 1) // (4 * expert_count)
    slot_total = EXP_DEV * dp_count * most_rows
    (
        query_all,
        key_all,
        value_all,
        context_all,
        router_all,
        gain_first,
        gain_second,
        query_gain,
        gain_key,
    ) = (
        lax.all_gather(query_weight, "dp", axis=0, tiled=True),
        lax.all_gather(key_projection, "dp", axis=0, tiled=True),
        lax.all_gather(value_projection, "dp", axis=0, tiled=True),
        lax.all_gather(context_weight, "dp", axis=1, tiled=True),
        lax.all_gather(router_weight, "dp", axis=0, tiled=True),
        lax.all_gather(prenorm_gain, "dp", axis=0, tiled=True),
        lax.all_gather(midnorm_gain, "dp", axis=0, tiled=True),
        lax.all_gather(querynorm_gain, "dp", axis=0, tiled=True),
        lax.all_gather(keynorm_gain, "dp", axis=0, tiled=True),
    )
    input_rows, cot_rows = (
        lax.all_gather(layer_input, "tensor", axis=0, tiled=True),
        lax.all_gather(output_cotangent, "tensor", axis=0, tiled=True),
    )
    position = jnp.arange(block_rows, dtype=jnp.int32)
    seq_length = lengths[sequence_order[lax.axis_index("dp")]]
    token_live = position < seq_length
    frequency = jnp.exp(
        -math.log(rope_base) * jnp.arange(HEAD_SIZE // 2, dtype=jnp.float32) * (2.0 / HEAD_SIZE)
    )
    angles = position.astype(jnp.float32)[:, None] * frequency[None, :]
    cosine_table = jnp.cos(angles)[:, None, :]
    sine_values = jnp.sin(angles)[:, None, :]
    heads_query = query_all.shape[1] // HEAD_SIZE
    heads_key = key_all.shape[1] // HEAD_SIZE
    group_width = heads_query // heads_key
    gain_one = gain_first.astype(jnp.float32)
    gain_two = gain_second.astype(jnp.float32)
    query_factor = query_gain.astype(jnp.float32)
    key_factor = gain_key.astype(jnp.float32)
    stream = input_rows.astype(jnp.float32)
    unit_first, scale_first = rms_normalize(stream)
    first_layer_normed = (unit_first * gain_one).astype(jnp.bfloat16)
    query_unnormed = matrix_product(first_layer_normed, query_all).reshape(
        block_rows, heads_query, HEAD_SIZE
    )
    key_unnormed = matrix_product(first_layer_normed, key_all).reshape(
        block_rows, heads_key, HEAD_SIZE
    )
    value_rows = (
        matrix_product(first_layer_normed, value_all)
        .astype(jnp.bfloat16)
        .reshape(block_rows, heads_key, HEAD_SIZE)
    )
    query_unit, query_scale = rms_normalize(query_unnormed)
    key_unit, key_scale = rms_normalize(key_unnormed)
    query_rows = (
        rotary_apply(query_unit * query_factor, cosine_table, sine_values)
        .astype(jnp.bfloat16)
        .reshape(block_rows, heads_key, group_width, HEAD_SIZE)
    )
    keys_rot = rotary_apply(key_unit * key_factor, cosine_table, sine_values).astype(jnp.bfloat16)
    score_scale = HEAD_SIZE ** (-0.5)
    allowed = (position[None, :] <= position[:, None]) & token_live[None, :]

    def score_block():
        raw_scores = (
            jnp.einsum("ikrd,jkd->krij", query_rows, keys_rot, preferred_element_type=jnp.float32)
            * score_scale
        )
        return jnp.where(allowed, raw_scores, masked_score)

    scores = score_block()
    row_peak = jnp.max(scores, axis=-1, keepdims=True)
    log_total = row_peak + jnp.log(jnp.sum(jnp.exp(scores - row_peak), axis=-1, keepdims=True))
    soft_probs = jnp.exp(scores - log_total)
    context = jnp.einsum(
        "krij,jkd->ikrd",
        soft_probs.astype(jnp.bfloat16),
        value_rows,
        preferred_element_type=jnp.float32,
    )
    context = context.reshape(block_rows, heads_query * HEAD_SIZE).astype(jnp.bfloat16)
    attention = lax.psum(matrix_product(context, context_all), "tensor")
    residual = stream + attention
    unit_second, scale_second = rms_normalize(residual)
    normed_second = (unit_second * gain_two).astype(jnp.bfloat16)
    logits = matrix_product(normed_second, router_all)
    expert_ids = jnp.arange(expert_count, dtype=jnp.int32)
    route_hot = routes[:, :, None] == expert_ids[None, None, :]
    chosen = jnp.sum(jnp.where(route_hot, logits[:, None, :], 0.0), axis=-1)
    gate_weights = jax.nn.softmax(chosen, axis=-1)
    pair_expert = routes.reshape(-1)
    pair_live = jnp.repeat(token_live, TOP)
    pair_hot = ((pair_expert[:, None] == expert_ids[None, :]) & pair_live[:, None]).astype(
        jnp.int32
    )
    running = jnp.cumsum(pair_hot, axis=0)
    pair_rank = jnp.sum((running - pair_hot) * pair_hot, axis=1)
    counts = running[-1]
    earlier = carried_in(
        counts, "dp", lambda former, latter: former + latter, jnp.zeros_like(counts)
    )
    pair_slot = jnp.sum(earlier[None, :] * pair_hot, axis=1) + pair_rank
    pair_kept = pair_live & (pair_slot < capacity)
    local_expert = pair_expert % EXP_DEV
    owner_index = pair_expert // EXP_DEV
    buffer_index = (local_expert * dp_count + owner_index) * most_rows + pair_rank
    target = jnp.where(pair_kept, buffer_index, slot_total)
    pair_ids = jnp.arange(block_rows * TOP, dtype=jnp.int32)
    slot_pair = jnp.full((slot_total,), -1, dtype=jnp.int32).at[target].set(pair_ids, mode="drop")
    slot_used = slot_pair >= 0
    slot_safe = jnp.maximum(slot_pair, 0)
    slot_token = slot_safe // TOP
    bf_zero = jnp.zeros((), jnp.bfloat16)
    send_rows = jnp.where(slot_used[:, None], normed_second[slot_token], bf_zero)
    layout = (EXP_DEV, dp_count, most_rows, features)
    received = to_owners(send_rows.reshape(layout)).reshape(EXP_DEV, dp_count * most_rows, features)
    gate_pre = jnp.einsum("end,edf->enf", received, expert_gate, preferred_element_type=jnp.float32)
    up_pre = jnp.einsum("end,edf->enf", received, expert_up, preferred_element_type=jnp.float32)
    sigmoid_gate = jax.nn.sigmoid(gate_pre)
    gate_act = gate_pre * sigmoid_gate
    hidden = (gate_act * up_pre).astype(jnp.bfloat16)
    out_partial = jnp.einsum(
        "enf,efd->end", hidden, expert_down, preferred_element_type=jnp.float32
    )
    expert_out = owner_reduce(out_partial)
    width = expert_out.shape[2]
    returned = lax.all_to_all(
        expert_out.reshape(EXP_DEV, dp_count, most_rows, width),
        "dp",
        split_axis=1,
        concat_axis=1,
        tiled=True,
    ).reshape(slot_total, width)
    pair_place = jnp.where(pair_kept, buffer_index, 0)
    pair_out = jnp.where(pair_kept[:, None], returned[pair_place], bf_zero).reshape(
        block_rows, TOP, width
    )
    expert_part = jnp.sum(gate_weights[:, :, None] * pair_out, axis=1)
    cot_full = cot_rows.astype(jnp.float32)
    own_start = tensor_index * own_rows
    gate_part = jnp.sum(cot_full[:, None, :] * pair_out, axis=-1)
    expert_own = lax.dynamic_slice_in_dim(expert_part, own_start, own_rows, 0)
    residual_own = lax.dynamic_slice_in_dim(residual, own_start, own_rows, 0)
    layer_output = (residual_own + expert_own).astype(jnp.bfloat16)
    slot_gate = jnp.where(slot_used, gate_weights.reshape(-1)[slot_safe], 0.0)
    send_cot = (slot_gate[:, None] * cot_full[slot_token]).astype(jnp.bfloat16)
    expert_cot = to_owners(send_cot.reshape(layout)).reshape(
        EXP_DEV, dp_count * most_rows, features
    )
    hidden_cot = jnp.einsum(
        "end,efd->enf", expert_cot, expert_down, preferred_element_type=jnp.float32
    )
    gating_cot = (
        hidden_cot * up_pre * sigmoid_gate * (1.0 + gate_pre * (1.0 - sigmoid_gate))
    ).astype(jnp.bfloat16)
    upward_cot = (hidden_cot * gate_act).astype(jnp.bfloat16)
    down_gradient = jnp.einsum(
        "enf,end->efd", hidden, expert_cot, preferred_element_type=jnp.float32
    )
    gate_gradient = jnp.einsum(
        "end,enf->edf", received, gating_cot, preferred_element_type=jnp.float32
    )
    up_gradient = jnp.einsum(
        "end,enf->edf", received, upward_cot, preferred_element_type=jnp.float32
    )
    row_partial = jnp.einsum(
        "enf,edf->end", gating_cot, expert_gate, preferred_element_type=jnp.float32
    )
    row_partial = row_partial + jnp.einsum(
        "enf,edf->end", upward_cot, expert_up, preferred_element_type=jnp.float32
    )
    row_cot = owner_reduce(row_partial)
    row_back = lax.all_to_all(
        row_cot.reshape(EXP_DEV, dp_count, most_rows, width),
        "dp",
        split_axis=1,
        concat_axis=1,
        tiled=True,
    ).reshape(slot_total, width)
    pair_cot = jnp.where(pair_kept[:, None], row_back[pair_place], bf_zero).reshape(
        block_rows, TOP, width
    )
    normed_part = jnp.sum(pair_cot.astype(jnp.float32), axis=1)
    normed_cot = normed_part
    route_cot = gate_weights * (
        gate_part - jnp.sum(gate_weights * gate_part, axis=-1, keepdims=True)
    )
    logit_cot = jnp.sum(jnp.where(route_hot, route_cot[:, :, None], 0.0), axis=1).astype(
        jnp.bfloat16
    )
    router_gradient = contract(normed_second, logit_cot)
    normed_cot = normed_cot + transposed(logit_cot, router_all)
    midnorm_gradient = jnp.sum(normed_cot * unit_second, axis=0)
    residual_cot = cot_full + norm_back(normed_cot * gain_two, unit_second, scale_second)
    attention_cot = residual_cot.astype(jnp.bfloat16)
    context_gradient = contract(context, attention_cot)
    context_cot = (
        transposed(attention_cot, context_all)
        .astype(jnp.bfloat16)
        .reshape(block_rows, heads_key, group_width, HEAD_SIZE)
    )
    scores = score_block()
    soft_probs = jnp.exp(scores - log_total)
    prob_cot = jnp.einsum(
        "ikrd,jkd->krij", context_cot, value_rows, preferred_element_type=jnp.float32
    )
    score_cot = (
        soft_probs * (prob_cot - jnp.sum(soft_probs * prob_cot, axis=-1, keepdims=True))
    ).astype(jnp.bfloat16)
    value_cot = jnp.einsum(
        "krij,ikrd->jkd",
        soft_probs.astype(jnp.bfloat16),
        context_cot,
        preferred_element_type=jnp.float32,
    )
    value_cot = value_cot.astype(jnp.bfloat16).reshape(block_rows, heads_key * HEAD_SIZE)
    query_turned = (
        jnp.einsum(
            "krij,jkd->ikrd", score_cot, keys_rot, preferred_element_type=jnp.float32
        ).reshape(block_rows, heads_query, HEAD_SIZE)
        * score_scale
    )
    key_turned = (
        jnp.einsum("krij,ikrd->jkd", score_cot, query_rows, preferred_element_type=jnp.float32)
        * score_scale
    )
    query_back = rotary_apply(query_turned, cosine_table, -sine_values)
    key_back = rotary_apply(key_turned, cosine_table, -sine_values)
    querynorm_part = jnp.sum(query_back * query_unit, axis=(0, 1))
    keynorm_part = jnp.sum(key_back * key_unit, axis=(0, 1))
    query_raw_cot = (
        norm_back(query_back * query_factor, query_unit, query_scale)
        .astype(jnp.bfloat16)
        .reshape(block_rows, heads_query * HEAD_SIZE)
    )
    key_raw_cot = (
        norm_back(key_back * key_factor, key_unit, key_scale)
        .astype(jnp.bfloat16)
        .reshape(block_rows, heads_key * HEAD_SIZE)
    )
    query_gradient = contract(first_layer_normed, query_raw_cot)
    key_gradient = contract(first_layer_normed, key_raw_cot)
    value_gradient = contract(first_layer_normed, value_cot)
    first_part = (
        transposed(query_raw_cot, query_all)
        + transposed(key_raw_cot, key_all)
        + transposed(value_cot, value_all)
    )
    first_cot, querynorm_gradient, keynorm_gradient = (
        lax.psum(first_part.astype(jnp.bfloat16), "tensor").astype(jnp.float32),
        lax.psum(querynorm_part.astype(jnp.bfloat16), "tensor").astype(jnp.float32),
        lax.psum(keynorm_part.astype(jnp.bfloat16), "tensor").astype(jnp.float32),
    )
    prenorm_gradient = jnp.sum(first_cot * unit_first, axis=0)
    input_cot = residual_cot + norm_back(first_cot * gain_one, unit_first, scale_first)
    input_gradient = lax.dynamic_slice_in_dim(input_cot, own_start, own_rows, 0).astype(
        jnp.bfloat16
    )
    summed = (
        lax.psum_scatter(query_gradient, "dp", scatter_dimension=0, tiled=True),
        lax.psum_scatter(key_gradient, "dp", scatter_dimension=0, tiled=True),
        lax.psum_scatter(value_gradient, "dp", scatter_dimension=0, tiled=True),
        lax.psum_scatter(context_gradient, "dp", scatter_dimension=1, tiled=True),
        lax.psum_scatter(router_gradient, "dp", scatter_dimension=0, tiled=True),
        lax.psum_scatter(prenorm_gradient, "dp", scatter_dimension=0, tiled=True),
        lax.psum_scatter(midnorm_gradient, "dp", scatter_dimension=0, tiled=True),
        lax.psum_scatter(querynorm_gradient, "dp", scatter_dimension=0, tiled=True),
        lax.psum_scatter(keynorm_gradient, "dp", scatter_dimension=0, tiled=True),
    )
    return (
        layer_output,
        input_gradient,
        summed[0],
        summed[1],
        summed[2],
        summed[3],
        summed[4],
        gate_gradient,
        up_gradient,
        down_gradient,
        summed[5],
        summed[6],
        summed[7],
        summed[8],
    )


AUX = 128


GRID_Z = 4
VMEM_LIMIT = 56 * 1024 * 1024


def remote(src, dst, send_sem, recv_sem, device):
    return pltpu.make_async_remote_copy(
        src_ref=src,
        dst_ref=dst,
        send_sem=send_sem,
        recv_sem=recv_sem,
        device_id=device,
        device_id_type=pl.DeviceIdType.MESH,
    )


class Place:
    def __init__(self):
        self.dp = lax.axis_index("dp")
        self.y = lax.axis_index("tensor")
        self.z = self.dp // 4
        self.x = (self.dp // 2) % 2
        self.core = self.dp % 2
        self.sibling = (self.dp + 1 - 2 * self.core, self.y)
        self.x_mate = (self.dp + 2 - 4 * self.x, self.y)
        self.y_mate = (self.dp, 1 - self.y)
        self.above = (self.dp + 4, self.y)
        self.below = (self.dp - 4, self.y)
        self.has_above = self.z < GRID_Z - 1
        self.has_below = self.z > 0

    def farthest(self, k):
        return (3 - 3 * (self.z // 2), (2 + 3 * self.z) % 5, 1 + self.z % 2, self.z)[k]

    def dp_at(self, z, flip_x, flip_core):
        x = self.x + flip_x * (1 - 2 * self.x)
        core = self.core + flip_core * (1 - 2 * self.core)
        return z * 4 + x * 2 + core

    def y_at(self, flip_y):
        return self.y + flip_y * (1 - 2 * self.y)

    def greet(self):
        barrier = pltpu.get_barrier_semaphore()
        for mate in (self.sibling, self.x_mate, self.y_mate):
            pl.semaphore_signal(barrier, 1, device_id=mate, device_id_type=pl.DeviceIdType.MESH)

        @pl.when(self.has_above)
        def _():
            pl.semaphore_signal(
                barrier, 1, device_id=self.above, device_id_type=pl.DeviceIdType.MESH
            )

        @pl.when(self.has_below)
        def _():
            pl.semaphore_signal(
                barrier, 1, device_id=self.below, device_id_type=pl.DeviceIdType.MESH
            )

        pl.semaphore_wait(barrier, 4 + self.z * (GRID_Z - 1 - self.z) // 2)


def add_rows(target, sources, rows, step=16):
    start, count = rows

    def one(i, carry):
        at = pl.ds(pl.multiple_of(start + i * step, step), step)
        total = target[at, :].astype(jnp.float32)
        for source, shift in sources:
            there = pl.ds(pl.multiple_of(start - shift + i * step, step), step)
            total = total + source[there, :].astype(jnp.float32)
        target[at, :] = total.astype(target.dtype)
        return carry

    lax.fori_loop(0, count // step, one, 0)


def line_onward(me, source, buffer, sem, to, side, mate):
    ends = 1 - (me.z - 1 - to + GRID_Z - 1) // GRID_Z
    slot = to if side == 0 else to + (GRID_Z - to) * ends
    return remote(source, buffer.at[slot], sem.at[0, to], sem.at[1, slot], mate)


def line_sum(me, k, block, source, rows, buffer, sem, shift):
    to = me.farthest(k)
    for side, ahead, mate, more in (
        (0, to > me.z, me.above, me.has_below),
        (1, to < me.z, me.below, me.has_above),
    ):
        slot = to if k < GRID_Z - 1 or side == 0 else GRID_Z
        came = remote(source, buffer.at[slot], sem.at[0, slot], sem.at[1, slot], mate)

        def gather(came=came, slot=slot):
            came.wait_recv()
            add_rows(block, [(buffer.at[slot], shift)], rows)

        if k < GRID_Z - 1:

            @pl.when(ahead)
            def _():
                pl.when(more)(gather)
                line_onward(me, source, buffer, sem, to, side, mate).start()
        else:
            pl.when(more)(gather)


def line_sent(me, k, source, buffer, sem):
    to = me.farthest(k)
    for side, ahead, mate in ((0, to > me.z, me.above), (1, to < me.z, me.below)):

        @pl.when(ahead)
        def _():
            line_onward(me, source, buffer, sem, to, side, mate).wait_send()


ROW_PLAN = (
    ("eda", 0), ("cz", 0, 1, 1), ("edb", 0), ("ey", 0), ("cz", 0, 0, 1), ("ex", 0), ("eda", 1),
    ("cz", 0, 0, 0), ("cz", 1, 0, 1), ("edb", 1), ("lx", 0), ("cz", 1, 1, 1), ("eda", 2),
    ("cz", 2, 1, 1), ("ly", 0), ("ly", 1), ("cz", 2, 0, 1), ("lx", 2), ("ex", 1), ("eda", 3),
    ("cz", 0, 1, 0), ("cz", 1, 1, 0), ("edb", 2), ("lx", 1), ("ey", 1), ("ey", 2), ("col", 0),
    ("edb", 3), ("cz", 2, 1, 0), ("cz", 1, 0, 0), ("cz", 3, 0, 1), ("cy", 0), ("cz", 3, 1, 1),
    ("ly", 2), ("ex", 2), ("col", 1), ("ly", 3), ("cz", 2, 0, 0), ("lx", 3), ("ex", 3),
    ("col", 2), ("cy", 1), ("ey", 3), ("cz", 3, 0, 0), ("cz", 3, 1, 0), ("cx",), ("cend",),
    ("col", 3),
)


def row_scatter_kernel(
    part, out, own, core, diag_a, diag_b, from_x, from_y, from_z, c_z, c_y, c_x,
    load_s, core_s, diag_s, x_s, y_s, z_s, cz_s, cy_s, cx_s, out_s,
):
    me = Place()
    rows, third = own.shape[3], diag_a.shape[1]
    last = GRID_Z - 1
    spans = ((0, third), (third, third), (2 * third, rows - 2 * third))
    a_at, b_at, c_at = (pl.ds(*span) for span in spans)
    most, most_at = (0, 2 * third), pl.ds(0, 2 * third)
    loads, cores, here = {}, {}, set()

    def chunk(k, flip_x, flip_y, flip_core):
        return part.at[me.dp_at(me.farthest(k), flip_x, flip_core) * 2 + me.y_at(flip_y)]

    order = ((1, 1), (1, 0), (0, 1), (0, 0))
    for k in range(GRID_Z):
        for fx, fy in order:
            copy = pltpu.make_async_copy(
                chunk(k, fx, fy, 0), own.at[k, fx, fy], load_s.at[k, fx, fy]
            )
            copy.start()
            loads[k, fx, fy] = copy
    me.greet()
    for k in range(GRID_Z):
        for fx, fy in order:
            copy = remote(
                chunk(k, fx, fy, 1), core.at[k, fx, fy],
                core_s.at[0, k, fx, fy], core_s.at[1, k, fx, fy], me.sibling,
            )
            copy.start()
            cores[k, fx, fy] = copy

    def pieces(make):
        return [make(k) for k in range(GRID_Z)]

    da = pieces(lambda k: remote(own.at[k, 1, 1, a_at], diag_a.at[k], diag_s.at[0, k], diag_s.at[1, k], me.y_mate))
    db = pieces(lambda k: remote(own.at[k, 1, 1, b_at], diag_b.at[k], diag_s.at[2, k], diag_s.at[3, k], me.x_mate))
    xs = pieces(
        lambda k: [
            remote(own.at[k, 1, 0, at], from_x.at[k, at], x_s.at[0, k, h], x_s.at[1, k, h], me.x_mate)
            for h, at in enumerate((a_at, b_at))
        ]
    )
    ys = pieces(
        lambda k: [
            remote(own.at[k, 0, 1, at], from_y.at[k, at], y_s.at[0, k, h], y_s.at[1, k, h], me.y_mate)
            for h, at in enumerate((a_at, b_at))
        ]
    )
    cy = [
        remote(own.at[last, fx, 1, c_at], c_y.at[fx], cy_s.at[0, fx], cy_s.at[1, fx], me.y_mate)
        for fx in range(2)
    ]
    cx = remote(own.at[last, 1, 0, c_at], c_x, cx_s.at[0], cx_s.at[1], me.x_mate)

    def add(k, fx, fy, h, *more):
        if (k, fx, fy) not in here:
            here.add((k, fx, fy))
            loads[k, fx, fy].wait()
            cores[k, fx, fy].wait_recv()
        span = most if h is None else spans[h]
        add_rows(own.at[k, fx, fy], [(core.at[k, fx, fy], 0), *more], span)

    def diagonal_a(k):
        add(k, 1, 1, 0)
        da[k].start()

    def diagonal_b(k):
        add(k, 1, 1, 1)
        db[k].start()

    def early_x(k):
        add(k, 1, 0, 1)
        xs[k][1].start()

    def early_y(k):
        add(k, 0, 1, 0)
        ys[k][0].start()

    def late_x(k):
        da[k].wait_recv()
        add(k, 1, 0, 0, (diag_a.at[k], 0))
        xs[k][0].start()

    def late_y(k):
        db[k].wait_recv()
        add(k, 0, 1, 1, (diag_b.at[k], third))
        ys[k][1].start()

    def column(k):
        for h in range(2):
            xs[k][h].wait_recv()
            ys[k][h].wait_recv()
        add(k, 0, 0, None, (from_x.at[k], 0), (from_y.at[k], 0))
        block = own.at[k, 0, 0]
        line_sum(me, k, block, block.at[most_at], most, from_z, z_s, 0)

    def c_line(k, fx, fy):
        add(k, fx, fy, 2)
        block = own.at[k, fx, fy]
        line_sum(
            me, k, block, block.at[c_at], spans[2], c_z.at[fx, fy], cz_s.at[fx, fy], 2 * third
        )

    def c_over_x():
        cy[1].wait_recv()
        add_rows(own.at[last, 1, 0], [(c_y.at[1], 2 * third)], spans[2])
        cx.start()

    def c_end():
        cy[0].wait_recv()
        cx.wait_recv()
        add_rows(own.at[last, 0, 0], [(c_y.at[0], 2 * third), (c_x, 2 * third)], spans[2])

    actions = {
        "eda": diagonal_a, "edb": diagonal_b, "ex": early_x, "ey": early_y, "lx": late_x,
        "ly": late_y, "col": column, "cz": c_line, "cy": lambda fx: cy[fx].start(),
        "cx": c_over_x, "cend": c_end,
    }
    for name, *which in ROW_PLAN:
        actions[name](*which)
    copy = pltpu.make_async_copy(own.at[last, 0, 0], out, out_s)
    copy.start()
    for k in range(GRID_Z):
        da[k].wait_send()
        db[k].wait_send()
        for h in range(2):
            xs[k][h].wait_send()
            ys[k][h].wait_send()
        if k < last:
            line_sent(me, k, own.at[k, 0, 0, most_at], from_z, z_s)
            for fx, fy in order:
                line_sent(me, k, own.at[k, fx, fy, c_at], c_z.at[fx, fy], cz_s.at[fx, fy])
    for sent in (*cores.values(), *cy, cx):
        sent.wait_send()
    copy.wait()


def scatter_all(value, collective_id):
    devices = lax.axis_size("dp") * lax.axis_size("tensor")
    rows, width = value.shape[0] // devices, value.shape[1]
    third = 3 * rows // 8
    dma = pltpu.SemaphoreType.DMA
    low = value.dtype
    shapes = (
        (4, 2, 2, rows), (4, 2, 2, rows), (4, third), (4, third), (4, 2 * third), (4, 2 * third),
        (5, 2 * third), (2, 2, 5, rows - 2 * third), (2, rows - 2 * third), (rows - 2 * third,),
    )
    return pl.pallas_call(
        row_scatter_kernel,
        out_shape=jax.ShapeDtypeStruct((rows, width), low),
        in_specs=[pl.BlockSpec(memory_space=pl.ANY)],
        out_specs=pl.BlockSpec(memory_space=pl.ANY),
        scratch_shapes=[
            *(pltpu.VMEM((*shape, width), low) for shape in shapes),
            dma((4, 2, 2)),
            dma((2, 4, 2, 2)),
            dma((4, 4)),
            dma((2, 4, 2)),
            dma((2, 4, 2)),
            dma((2, 5)),
            dma((2, 2, 2, 5)),
            dma((2, 2)),
            dma((2,)),
            dma(()),
        ],
        compiler_params=pltpu.CompilerParams(
            collective_id=collective_id, has_side_effects=True, vmem_limit_bytes=VMEM_LIMIT
        ),
    )(value.reshape(devices, rows, width))


WINDOW_ALIGN = 16
EXPERT_VMEM = 60 * 1024 * 1024


def dot(left, right, dims=((1,), (0,))):
    return lax.dot_general(left, right, (dims, ((), ())), preferred_element_type=jnp.float32)


def expert_kernel(
    info, pos, rows_in, cots_in, gate_w, up_w, down_w,
    out, back, gate_g, up_g, down_g,
    x, dy, wgu, wd, slot_out, slot_row, gu, hg, rows_b, cots_b, g_stage, d_stage,
    load_s, w_s, out_s, g_s, d_s,
):
    bf16, f32 = jnp.bfloat16, jnp.float32
    blocks, block_rows, wide = rows_in.shape
    features = cots_in.shape[2]
    experts, padded = x.shape[0], x.shape[1]
    part = hg.shape[2]
    cap = hg.shape[1]
    window = padded - cap
    tile = 256
    chunk = 512

    def load(b):
        slot = b % 2
        return (
            pltpu.make_async_copy(rows_in.at[b], rows_b.at[slot], load_s.at[slot, 0]),
            pltpu.make_async_copy(cots_in.at[b], cots_b.at[slot], load_s.at[slot, 1]),
        )

    for copy in load(0):
        copy.start()
    weights = []
    for e in range(experts):
        weights.append(pltpu.make_async_copy(gate_w.at[e], wgu.at[e, :, pl.ds(0, part)], w_s.at[e, 0]))
        weights.append(pltpu.make_async_copy(up_w.at[e], wgu.at[e, :, pl.ds(part, part)], w_s.at[e, 1]))
        weights.append(pltpu.make_async_copy(down_w.at[e], wd.at[e], w_s.at[e, 2]))
    for copy in weights:
        copy.start()

    def clear(i, carry):
        at = pl.ds(pl.multiple_of(i * 16, 16), 16)
        for e in range(experts):
            x[e, at, :] = jnp.zeros((16, wide), bf16)
            dy[e, at, :] = jnp.zeros((16, features), bf16)
        return carry

    lax.fori_loop(0, padded // 16, clear, 0)
    for e in range(experts):
        slot_out[e, pl.ds(cap, window), :] = jnp.zeros((window, features), bf16)
        slot_row[e, pl.ds(cap, window), :] = jnp.zeros((window, wide), bf16)

    def starts(b):
        return [pl.multiple_of(info[1 + b * experts + e], WINDOW_ALIGN) for e in range(experts)]

    def picks(b, begin):
        slots = lax.broadcasted_iota(jnp.int32, (window, block_rows), 0)
        return jnp.concatenate(
            [(slots + begin[e] == pos[b, pl.ds(e, 1), :]).astype(f32) for e in range(experts)],
            axis=0,
        )

    def take(b, carry):
        slot = b % 2

        @pl.when(b + 1 < blocks)
        def _():
            for copy in load(b + 1):
                copy.start()

        begin = starts(b)
        picked = picks(b, begin).astype(bf16)
        for copy in load(b):
            copy.wait()
        for source, target, width in ((rows_b, x, wide), (cots_b, dy, features)):
            for first in range(0, width, chunk):
                cols = pl.ds(first, min(chunk, width - first))
                got = dot(picked, source[slot, :, cols]).astype(bf16)
                for e in range(experts):
                    first_at = pl.ds(begin[e], WINDOW_ALIGN)
                    rest_at = pl.ds(begin[e] + WINDOW_ALIGN, window - WINDOW_ALIGN)
                    split = e * window + WINDOW_ALIGN
                    target[e, first_at, cols] += got[e * window : split]
                    target[e, rest_at, cols] = got[split : (e + 1) * window]
        return carry

    lax.fori_loop(0, blocks, take, 0)
    for copy in weights:
        copy.wait()

    lanes = lax.broadcasted_iota(jnp.int32, (tile, AUX), 1)

    def mlp(step, carry):
        e = step // (cap // tile)
        at = pl.ds(pl.multiple_of((step % (cap // tile)) * tile, tile), tile)
        own = info[0] * experts + e
        total = blocks * experts
        aux = x[e, at, pl.ds(features, AUX)].astype(f32)
        gate = jnp.sum(
            jnp.where((lanes == own) | (lanes == own + total), aux, 0.0), axis=1, keepdims=True
        )
        pre = dot(x[e, at, pl.ds(0, features)], wgu[e])
        gate_pre, up_pre = pre[:, :part], pre[:, part:]
        sig = 1.0 / (1.0 + jnp.exp(-gate_pre))
        act = gate_pre * sig
        hidden = (act * up_pre).astype(bf16).astype(f32)
        gated = (hidden * gate).astype(bf16)
        hg[e, at, :] = gated
        down_cot = dot(dy[e, at, :], wd[e], ((1,), (1,)))
        slot_cot = jnp.sum(hidden * down_cot, axis=1, keepdims=True)
        hidden_cot = down_cot * gate
        gu[e, at, pl.ds(0, part)] = (
            hidden_cot * up_pre * sig * (1.0 + gate_pre * (1.0 - sig))
        ).astype(bf16)
        gu[e, at, pl.ds(part, part)] = (hidden_cot * act).astype(bf16)
        for first in range(0, features, chunk):
            cols = pl.ds(first, chunk)
            slot_out[e, at, cols] = dot(gated, wd[e, :, cols]).astype(bf16)
            slot_row[e, at, cols] = dot(
                gu[e, at, :], wgu[e, pl.ds(first, chunk), :], ((1,), (1,))
            ).astype(bf16)
        high = slot_cot.astype(bf16).astype(f32)
        place = info[1 + blocks * experts] * 2 * total + own * 2
        slot_row[e, at, pl.ds(features, AUX)] = jnp.where(
            lanes == place, high, jnp.where(lanes == place + 1, slot_cot - high, 0.0)
        ).astype(bf16)
        return carry

    lax.fori_loop(0, experts * (cap // tile), mlp, 0)

    def stored(b):
        slot = b % 2
        return (
            pltpu.make_async_copy(cots_b.at[slot], out.at[b], out_s.at[slot, 0]),
            pltpu.make_async_copy(rows_b.at[slot], back.at[b], out_s.at[slot, 1]),
        )

    def put(b, carry):
        slot = b % 2

        @pl.when(b >= 2)
        def _():
            for copy in stored(b - 2):
                copy.wait()

        begin = starts(b)
        spread = picks(b, begin).T.astype(bf16)
        for source, target, width in ((slot_out, cots_b, features), (slot_row, rows_b, wide)):
            for first in range(0, width, chunk):
                cols = pl.ds(first, min(chunk, width - first))
                held = jnp.concatenate(
                    [source[e, pl.ds(begin[e], window), cols] for e in range(experts)], axis=0
                )
                target[slot, :, cols] = dot(spread, held).astype(bf16)
        for copy in stored(b):
            copy.start()
        return carry

    lax.fori_loop(0, blocks, put, 0)

    tiles = features // tile

    def g_copies(step):
        slot = step % 2
        e, at = step // tiles, pl.ds(pl.multiple_of((step % tiles) * tile, tile), tile)
        return (
            pltpu.make_async_copy(g_stage.at[slot, :, pl.ds(0, part)], gate_g.at[e, at], g_s.at[slot, 0]),
            pltpu.make_async_copy(g_stage.at[slot, :, pl.ds(part, part)], up_g.at[e, at], g_s.at[slot, 1]),
        )

    def wide_grad(step, carry):
        slot = step % 2
        e, at = step // tiles, pl.ds(pl.multiple_of((step % tiles) * tile, tile), tile)

        @pl.when(step >= 2)
        def _():
            for copy in g_copies(step - 2):
                copy.wait()

        g_stage[slot] = dot(x[e, pl.ds(0, cap), at], gu[e], ((0,), (0,)))
        for copy in g_copies(step):
            copy.start()
        return carry

    lax.fori_loop(0, experts * tiles, wide_grad, 0)
    parts = features // chunk

    def d_copy(step):
        slot = step % 2
        e, at = step // parts, pl.ds(pl.multiple_of((step % parts) * chunk, chunk), chunk)
        return pltpu.make_async_copy(d_stage.at[slot], down_g.at[e, :, at], d_s.at[slot])

    def down_grad(step, carry):
        slot = step % 2
        e, at = step // parts, pl.ds(pl.multiple_of((step % parts) * chunk, chunk), chunk)

        @pl.when(step >= 2)
        def _():
            d_copy(step - 2).wait()

        d_stage[slot] = dot(hg[e], dy[e, pl.ds(0, cap), at], ((0,), (0,)))
        d_copy(step).start()
        return carry

    lax.fori_loop(0, experts * parts, down_grad, 0)
    for last in (2, 1):
        for copy in stored(blocks - last):
            copy.wait()
        for copy in g_copies(experts * tiles - last):
            copy.wait()
        d_copy(experts * parts - last).wait()


def expert_layer(info, pos, rows_in, cots_in, gate_w, up_w, down_w, capacity, most):
    bf16, f32 = jnp.bfloat16, jnp.float32
    blocks, block_rows, wide = rows_in.shape
    features = cots_in.shape[2]
    experts, part = gate_w.shape[0], gate_w.shape[2]
    padded = capacity + -(-most // WINDOW_ALIGN) * WINDOW_ALIGN + WINDOW_ALIGN
    dma = pltpu.SemaphoreType.DMA
    shape = jax.ShapeDtypeStruct
    anywhere = pl.BlockSpec(memory_space=pl.ANY)
    return pl.pallas_call(
        expert_kernel,
        out_shape=(
            shape((blocks, block_rows, features), bf16),
            shape((blocks, block_rows, wide), bf16),
            shape(gate_w.shape, f32),
            shape(up_w.shape, f32),
            shape(down_w.shape, f32),
        ),
        in_specs=[
            pl.BlockSpec(memory_space=pltpu.SMEM),
            pl.BlockSpec(memory_space=pltpu.VMEM),
        ]
        + [anywhere] * 5,
        out_specs=(anywhere,) * 5,
        scratch_shapes=[
            pltpu.VMEM((experts, padded, wide), bf16),
            pltpu.VMEM((experts, padded, features), bf16),
            pltpu.VMEM((experts, features, 2 * part), bf16),
            pltpu.VMEM((experts, part, features), bf16),
            pltpu.VMEM((experts, padded, features), bf16),
            pltpu.VMEM((experts, padded, wide), bf16),
            pltpu.VMEM((experts, capacity, 2 * part), bf16),
            pltpu.VMEM((experts, capacity, part), bf16),
            pltpu.VMEM((2, block_rows, wide), bf16),
            pltpu.VMEM((2, block_rows, features), bf16),
            pltpu.VMEM((2, 256, 2 * part), f32),
            pltpu.VMEM((2, part, 512), f32),
            dma((2, 2)),
            dma((experts, 3)),
            dma((2, 2)),
            dma((2, 2)),
            dma((2,)),
        ],
        compiler_params=pltpu.CompilerParams(vmem_limit_bytes=EXPERT_VMEM),
    )(info, pos, rows_in, cots_in, gate_w, up_w, down_w)


ATTENTION_VMEM = 60 * 1024 * 1024
SCORE_SCALE = HEAD_SIZE ** (-0.5)
def turn_tables(rows):
    frequency = np.exp(
        -math.log(rope_base) * np.arange(HEAD_SIZE // 2, dtype=np.float32) * (2.0 / HEAD_SIZE)
    ).astype(np.float32)
    angles = np.arange(rows, dtype=np.float32)[:, None] * frequency[None, :]
    cosine, sine = np.cos(angles), np.sin(angles)
    return (
        np.concatenate([cosine, cosine], axis=1).astype(np.float32),
        np.concatenate([-sine, sine], axis=1).astype(np.float32),
    )


def turn(value, cosine, sine):
    return value * cosine + pltpu.roll(value, HEAD_SIZE // 2, 1) * sine


def inverse_norm(value):
    return lax.rsqrt(jnp.mean(value * value, axis=-1, keepdims=True) + epsilon)


def meet_y(me):
    barrier = pltpu.get_barrier_semaphore()
    pl.semaphore_signal(barrier, 1, device_id=me.y_mate, device_id_type=pl.DeviceIdType.MESH)
    pl.semaphore_wait(barrier, 1)


def gain_rows(aux_t, experts, chunks):
    head = [aux_t[experts + 2 + i : experts + 3 + i, :] for i in range(2)]
    width = HEAD_SIZE
    heads = [sum(row[:, c * width : (c + 1) * width] for c in range(chunks)) for row in head]
    return aux_t[experts : experts + 1, :], aux_t[experts + 1 : experts + 2, :], *heads


def probabilities(query, key, allowed):
    scores = jnp.where(allowed, dot(query, key, ((1,), (1,))) * SCORE_SCALE, masked_score)
    spread = jnp.exp(scores - jnp.max(scores, axis=-1, keepdims=True))
    return spread / jnp.sum(spread, axis=-1, keepdims=True)


def allowed_pairs(length, rows):
    later = lax.broadcasted_iota(jnp.int32, (rows, rows), 0)
    sooner = lax.broadcasted_iota(jnp.int32, (rows, rows), 1)
    return (sooner <= later) & (sooner < length)


def placed(count, offset):
    row = lax.broadcasted_iota(jnp.int32, (count, AUX), 0)
    return (row + offset == lax.broadcasted_iota(jnp.int32, (count, AUX), 1)).astype(jnp.bfloat16)


OPENING_PLAN = (
    ("w", 0, 0), ("a", 0), ("w", 1, 0), ("pair",), ("a", 1), ("b", 0, 0), ("w", 2, 0), ("a", 2),
    ("ax", 0), ("bx",), ("w", 3, 0), ("w", 0, 1), ("y1", 1, 0, 0), ("ax", 2), ("b", 0, 1),
    ("ax", 1), ("wx", 1, 0), ("b", 1, 1), ("ay0",), ("w", 1, 1), ("wx", 0, 0), ("b", 1, 0),
    ("wx", 2, 0), ("b", 2, 1), ("w", 2, 1), ("wx", 3, 0), ("y1", 1, 1, 0), ("prep",), ("qkv",),
    ("h", 0), ("y1", 1, 0, 1), ("b", 2, 0), ("w", 3, 1), ("y1", 0, 0, 1), ("h", 1), ("b", 3, 0),
    ("wx", 1, 1), ("h", 2), ("wx", 2, 1), ("a", 3), ("h", 3), ("wx", 0, 1), ("b", 3, 1),
    ("wx", 3, 1), ("ctx",), ("ax", 3), ("ctx2",), ("fin",), ("n", 0), ("y1", 0, 1, 0),
    ("y1", 1, 1, 1), ("c0",), ("n", 1), ("n", 2), ("c1",), ("n", 3), ("nx", 1), ("c2", 0),
    ("cz", 1, 1, 0), ("nx", 0), ("c2", 1), ("cz", 1, 1, 1), ("ny", 1), ("ny", 2),
    ("cz", 2, 1, 0), ("cz", 1, 0, 0), ("y1", 2, 0, 1), ("ny", 3), ("y1", 0, 1, 1),
    ("y1", 3, 1, 0), ("y1", 2, 1, 0), ("ny", 0), ("nx", 3), ("cz", 2, 1, 1), ("y1", 3, 0, 1),
    ("nx", 2), ("y1", 0, 0, 0), ("cz", 3, 1, 0), ("y1", 2, 0, 0), ("cz", 3, 1, 1),
    ("y1", 3, 0, 0), ("y1", 3, 1, 1), ("y1", 2, 1, 1), ("cz", 2, 0, 0), ("cz", 1, 0, 1),
    ("nca", 1), ("cz", 2, 0, 1), ("cz", 3, 0, 1), ("nca", 0), ("ncb", 2), ("ncb", 0),
    ("nca", 3), ("ncb", 1), ("ncb", 3), ("cz", 3, 0, 0), ("nca", 2),
)


def opening_kernel(
    experts, qkv,
    lengths, sequence_order, query_w, key_w, value_w, context_w, router_t, prenorm, midnorm,
    querynorm, keynorm, routes_t, d_src, x_src, cosine_in, sine_in,
    w_out, d_out, x_out,
    rows_o, sent_o, residual_o, normed_o, raw_o, query_o, key_o, value_o, context_o,
    x, w, ctx, aux_w, normed, raw, query, key, value, context, att, got, residual, sent,
    local_s, pair_s, wz_s, wx_s, wc_s, az_s, ax_s, ay_s, bz_s, bx_s, by_s, dc_s,
    in_s, w_s, out_s, y_s,
    w_src, flat_ctx, flat_router, flat_gains, head_gains, flat_routes, cosine, sine, load_s,
    nl_s, nz_s, nx_s, ny_s, ndx_s, ndy_s, nc_s, cx_s, cy_s, cz_s, cc_s,
):
    bf16, f32 = jnp.bfloat16, jnp.float32
    me = Place()
    half = d_src.shape[0] // 2
    low, high = pl.ds(0, half), pl.ds(half, half)
    width = w_src.shape[1]
    first_cols = qkv + AUX
    columns = (pl.ds(0, first_cols), pl.ds(first_cols, width - first_cols))
    waits, sent_on = [], []

    def near(k):
        return me.farthest(GRID_Z - 1 - k)

    def w_at(k, fx, p):
        return w_out.at[me.dp_at(near(k), fx, 0), :, columns[p]]

    def d_at(k, fx, fy, rows):
        return d_out.at[me.dp_at(near(k), fx, 0) * 2 + me.y_at(fy), rows]

    wide, narrow = query_w.shape[1], key_w.shape[1]
    loads = [
        pltpu.make_async_copy(source, target, load_s.at[i])
        for i, (source, target) in enumerate(
            (
                (context_w, flat_ctx),
                (router_t, flat_router),
                (prenorm, flat_gains.at[0]),
                (midnorm, flat_gains.at[1]),
                (querynorm, head_gains.at[0]),
                (keynorm, head_gains.at[1]),
                (routes_t, flat_routes),
                (query_w, w_src.at[:, pl.ds(0, wide)]),
                (key_w, w_src.at[:, pl.ds(wide, narrow)]),
                (value_w, w_src.at[:, pl.ds(wide + narrow, narrow)]),
                (cosine_in, cosine),
                (sine_in, sine),
            )
        )
    ]
    for copy in loads:
        copy.start()
    for copy in loads[:7]:
        copy.wait()
    count = head_gains.shape[2]
    top, block_rows = flat_routes.shape
    w_src[:, pl.ds(first_cols, width - first_cols)] = flat_ctx[...].astype(f32).T.astype(bf16)
    gains = jnp.concatenate(
        [
            flat_gains[0].astype(f32),
            flat_gains[1].astype(f32),
            dot(head_gains[0], placed(count, me.dp * count)),
            dot(head_gains[1], placed(count, me.dp * count)),
            jnp.zeros((4, AUX), f32),
        ],
        axis=0,
    ).T.astype(bf16)
    aux = dot(flat_router[...].astype(f32).T.astype(bf16), placed(experts, 0))
    aux = aux + dot(gains, placed(8, experts))
    for part in range(block_rows // AUX):
        some = flat_routes[:, part * AUX : (part + 1) * AUX].astype(f32).T.astype(bf16)
        aux = aux + dot(some, placed(top, experts + 4 + part * top))
    w_src[:, pl.ds(qkv, AUX)] = aux.astype(bf16)
    for copy in loads[7:]:
        copy.wait()
    for i, (source, target) in enumerate(
        (
            (w_src, w_out.at[me.dp]),
            (d_src, d_out.at[me.dp * 2 + me.y]),
            (x_src, x_out.at[me.y]),
        )
    ):
        copy = pltpu.make_async_copy(source, target, local_s.at[i])
        copy.start()
        waits.append(copy)
    me.greet()

    def line(k, source, target, sem, start_only):
        zn = near(k)
        for side, came, more, mate in (
            (0, zn < me.z, me.has_above, me.above),
            (1, zn > me.z, me.has_below, me.below),
        ):
            copy = remote(source, target, sem.at[0, side, zn], sem.at[1, side, zn], mate)
            if start_only:

                @pl.when(more)
                def _():
                    copy.start()
            else:

                @pl.when(came)
                def _():
                    copy.wait_recv()

                    @pl.when(more)
                    def _():
                        copy.start()

    def line_done(k, source, target, sem):
        zn = near(k)
        for side, came, more, mate in (
            (0, zn <= me.z, me.has_above, me.above),
            (1, zn >= me.z, me.has_below, me.below),
        ):
            copy = remote(source, target, sem.at[0, side, zn], sem.at[1, side, zn], mate)

            @pl.when(came)
            def _():
                @pl.when(more)
                def _():
                    copy.wait_send()

    def w_source(k, p):
        return w_src.at[:, columns[p]] if k == 0 else w_at(k, 0, p)

    def d_source(k, rows):
        return d_src.at[rows] if k == 0 else d_at(k, 0, 0, rows)

    def go(source, target, sem, index, mate):
        copy = remote(source, target, sem.at[(0, *index)], sem.at[(1, *index)], mate)
        copy.start()
        sent_on.append(copy)
        return copy

    def to_core(source, target, sem, index):
        go(source, target, sem, index, me.sibling)

    wx, ax, ay, by = {}, {}, {}, {}

    def w_own(k, p):
        line(k, w_source(k, p), w_at(k, 0, p), wz_s.at[p], k == 0)
        wx[k, p] = go(w_source(k, p), w_at(k, 0, p), wx_s, (k, p), me.x_mate)
        to_core(w_source(k, p), w_at(k, 0, p), wc_s, (k, 0, p))

    def w_across(k, p):
        wx[k, p].wait_recv()
        to_core(w_at(k, 1, p), w_at(k, 1, p), wc_s, (k, 1, p))

    def w_from_core(k, p):
        for fx in range(2):
            block = w_at(k, fx, p)
            remote(block, block, wc_s.at[0, k, fx, p], wc_s.at[1, k, fx, p], me.sibling).wait_recv()

    def a_over_y(k):
        ay[k, 0] = go(d_source(k, low), d_at(k, 0, 0, low), ay_s, (k, 0), me.y_mate)

    def a_own(k):
        line(k, d_source(k, low), d_at(k, 0, 0, low), az_s, k == 0)
        if k:
            a_over_y(k)
        ax[k] = go(d_source(k, low), d_at(k, 0, 0, low), ax_s, (k,), me.x_mate)
        to_core(d_source(k, low), d_at(k, 0, 0, low), dc_s, (k, 0, 0, 0))

    def a_across(k):
        ax[k].wait_recv()
        block = d_at(k, 1, 0, low)
        ay[k, 1] = go(block, block, ay_s, (k, 1), me.y_mate)
        to_core(block, block, dc_s, (k, 1, 0, 0))

    def b_own(k, fx):
        source = d_source(k, high) if fx == 0 else d_at(k, 1, 0, high)
        block = d_at(k, fx, 0, high)
        line(k, source, block, bz_s.at[fx], k == 0)
        by[k, fx] = go(source, block, by_s, (k, fx), me.y_mate)
        to_core(source, block, dc_s, (k, fx, 0, 1))

    def y_done(k, fx, h):
        (ay, by)[h][k, fx].wait_recv()
        block = d_at(k, fx, 1, (low, high)[h])
        to_core(block, block, dc_s, (k, fx, 1, h))

    rows, features = x.shape[0] * x.shape[1], x.shape[2]
    own_rows = rows // 2
    heads, key_heads = query.shape[0], key.shape[0]
    chunk = 512
    mine = pl.ds(pl.multiple_of(me.y * own_rows, own_rows), own_rows)
    theirs = pl.ds(pl.multiple_of((1 - me.y) * own_rows, own_rows), own_rows)
    turn_c, turn_s = cosine[...], sine[...]
    held, outs, copies = {}, [], []

    def pair_rows():
        held["pair"] = go(x_src, x_out.at[me.y], pair_s, (0,), me.y_mate)

    def b_over_x():
        held["bx"] = go(d_src.at[high], d_at(0, 0, 0, high), bx_s, (0,), me.x_mate)

    def b_step(k, fx):
        if (k, fx) == (0, 1):
            held["bx"].wait_recv()
        b_own(k, fx)

    def prepare():
        held["pair"].wait_recv()
        waits[2].wait()
        for k in range(GRID_Z):
            w_from_core(k, 0)
        waits[0].wait()
        loads = [
            pltpu.make_async_copy(w_out.at[:, :, pl.ds(qkv, AUX)], aux_w, in_s.at[1]),
            pltpu.make_async_copy(x_out, x, in_s.at[0]),
        ]
        held["parts"] = [
            pltpu.make_async_copy(
                w_out.at[:, :, pl.ds(c * chunk, chunk)],
                w.at[:, :, pl.ds(c * chunk, chunk)],
                w_s.at[c],
            )
            for c in range(qkv // chunk)
        ]
        for copy in loads + held["parts"]:
            copy.start()
        loads[0].wait()
        aux_t = aux_w[...].reshape(features, AUX).astype(f32).T
        held["gains"] = gain_rows(aux_t, experts, features // HEAD_SIZE)
        gain_one = held["gains"][0]
        loads[1].wait()

        def one(i, carry):
            at = pl.ds(pl.multiple_of(i * 32, 32), 32)
            for part in range(2):
                stream = x[part, at, :].astype(f32)
                there = pl.ds(pl.multiple_of(part * own_rows + i * 32, 32), 32)
                normed[there, :] = (stream * inverse_norm(stream) * gain_one).astype(bf16)
            return carry

        lax.fori_loop(0, own_rows // 32, one, 0)

    def project():
        for c, copy in enumerate(held["parts"]):
            copy.wait()
            cols = slice(c * chunk, (c + 1) * chunk)
            got_raw = dot(normed[...], w[:, :, cols].reshape(features, chunk))
            for h in range(chunk // HEAD_SIZE):
                raw[c * (chunk // HEAD_SIZE) + h] = got_raw[:, h * HEAD_SIZE : (h + 1) * HEAD_SIZE]
        for g in range(key_heads):
            unnormed = raw[heads + g]
            gained = unnormed * inverse_norm(unnormed) * held["gains"][3]
            key[g] = turn(gained, turn_c, turn_s).astype(bf16)
            value[g] = raw[heads + key_heads + g].astype(bf16)

    def attend(part):
        allowed = allowed_pairs(lengths[sequence_order[me.dp]], rows)
        query_gain = held["gains"][2]

        def head(h, carry):
            g = h // (heads // key_heads)
            unnormed = raw[h]
            gained = unnormed * inverse_norm(unnormed) * query_gain
            turned = turn(gained, turn_c, turn_s).astype(bf16)
            query[h] = turned
            probs = probabilities(turned, key[g], allowed).astype(bf16)
            at = pl.ds(pl.multiple_of(h * HEAD_SIZE, HEAD_SIZE), HEAD_SIZE)
            context[:, at] = dot(probs, value[g]).astype(bf16)
            return carry

        share = heads // 4
        lax.fori_loop(part * share, (part + 1) * share, head, 0)

    def save(pairs):
        for source, target in pairs:
            copy = pltpu.make_async_copy(source, target, out_s.at[len(outs)])
            copy.start()
            outs.append(copy)

    def ctx_part(c):
        span = chunk // ctx.shape[1]
        return ctx[c * span : (c + 1) * span].reshape(chunk, ctx.shape[2])

    def output_over_y():
        save(
            (
                (normed, normed_o), (raw, raw_o), (query, query_o), (key, key_o),
                (value, value_o), (context, context_o),
            )
        )
        for k in range(GRID_Z):
            w_from_core(k, 1)
        load = pltpu.make_async_copy(w_out.at[:, :, columns[1]], ctx, in_s.at[2])
        load.start()
        load.wait()
        for c in range(features // chunk):
            cols = pl.ds(c * chunk, chunk)
            att[:, cols] = dot(context[theirs, :], ctx_part(c), ((1,), (1,))).astype(bf16)
            copy = remote(att.at[:, cols], got.at[:, cols], y_s.at[0, c], y_s.at[1, c], me.y_mate)
            copy.start()
            copies.append(copy)

    def output_own():
        for c in range(features // chunk):
            residual[:, pl.ds(c * chunk, chunk)] = dot(context[mine, :], ctx_part(c), ((1,), (1,)))

    def finish():
        for copy in copies:
            copy.wait_recv()
        gain_two = held["gains"][1]

        def second_norm(i, carry):
            at = pl.ds(pl.multiple_of(i * 16, 16), 16)
            total = x[me.y, at, :].astype(f32) + (residual[at, :] + got[at, :].astype(f32))
            residual[at, :] = total
            sent[at, pl.ds(0, features)] = (total * inverse_norm(total) * gain_two).astype(bf16)
            return carry

        lax.fori_loop(0, own_rows // 16, second_norm, 0)
        logits = dot(sent[:, :features], aux_w[...].reshape(features, AUX))
        own = flat_routes[:, pl.ds(pl.multiple_of(me.y * own_rows, own_rows), own_rows)]
        own = own.astype(f32).T
        lane = lax.broadcasted_iota(jnp.int32, (own_rows, AUX), 1).astype(f32)
        hits = [lane == own[:, j : j + 1] for j in range(top)]
        picked = functools.reduce(jnp.logical_or, hits)
        logits = jnp.where(picked, logits, masked_score)
        spread = jnp.where(picked, jnp.exp(logits - jnp.max(logits, axis=-1, keepdims=True)), 0.0)
        gates = spread / jnp.sum(spread, axis=-1, keepdims=True)
        coarse = gates.astype(bf16).astype(f32)
        sent[:, pl.ds(features, AUX)] = (coarse + pltpu.roll(gates - coarse, experts, 1)).astype(bf16)
        save(((sent, sent_o), (residual, residual_o)))

    third = 3 * own_rows // 8
    n_low, n_high = pl.ds(0, third), pl.ds(third, third)
    n_most, n_rest = pl.ds(0, 2 * third), pl.ds(2 * third, own_rows - 2 * third)
    nx, ny, ndx, ndy, cy = {}, {}, {}, {}, {}

    def n_at(k, fx, fy, rows):
        return rows_o.at[me.dp_at(near(k), fx, 0) * 2 + me.y_at(fy), rows]

    def n_source(k, rows):
        return sent.at[rows] if k == 0 else n_at(k, 0, 0, rows)

    def n_own(k):
        source, block = n_source(k, n_most), n_at(k, 0, 0, n_most)
        line(k, source, block, nz_s, k == 0)
        nx[k] = go(source, block, nx_s, (k,), me.x_mate)
        ny[k] = go(source, block, ny_s, (k,), me.y_mate)
        to_core(source, block, nc_s, (k, 0))
        if k == 0:
            copy = pltpu.make_async_copy(sent, rows_o.at[me.dp * 2 + me.y], nl_s.at[0])
            copy.start()
            outs.append(copy)

    def n_over_y(k):
        nx[k].wait_recv()
        block = n_at(k, 1, 0, n_low)
        ndy[k] = go(block, block, ndy_s, (k,), me.y_mate)
        block = n_at(k, 1, 0, n_most)
        to_core(block, block, nc_s, (k, 1))

    def n_over_x(k):
        ny[k].wait_recv()
        block = n_at(k, 0, 1, n_high)
        ndx[k] = go(block, block, ndx_s, (k,), me.x_mate)
        block = n_at(k, 0, 1, n_most)
        to_core(block, block, nc_s, (k, 2))

    def n_corner(k, copies, rows, index):
        copies[k].wait_recv()
        block = n_at(k, 1, 1, rows)
        to_core(block, block, nc_s, (k, index))

    def c_line(k, fx, fy, source=None):
        block = n_at(k, fx, fy, n_rest)
        source = block if source is None else source
        line(k, source, block, cz_s.at[fx, fy], k == 0)
        to_core(source, block, cc_s, (k, fx, fy))

    def c_own():
        source, block = sent.at[n_rest], n_at(0, 0, 0, n_rest)
        held["cx"] = go(source, block, cx_s, (0,), me.x_mate)
        cy[0] = go(source, block, cy_s, (0,), me.y_mate)
        c_line(0, 0, 0, source)

    def c_from_x():
        held["cx"].wait_recv()
        block = n_at(0, 1, 0, n_rest)
        cy[1] = go(block, block, cy_s, (1,), me.y_mate)
        c_line(0, 1, 0)

    def c_from_y(fx):
        cy[fx].wait_recv()
        c_line(0, fx, 1)

    actions = {
        "n": n_own, "nx": n_over_y, "ny": n_over_x,
        "nca": lambda k: n_corner(k, ndy, n_low, 3), "ncb": lambda k: n_corner(k, ndx, n_high, 4),
        "c0": c_own, "c1": c_from_x, "c2": c_from_y, "cz": c_line,
        "pair": pair_rows, "bx": b_over_x, "ay0": lambda: a_over_y(0), "w": w_own, "wx": w_across,
        "a": a_own, "ax": a_across, "b": b_step, "y1": y_done, "prep": prepare, "qkv": project,
        "h": attend, "ctx": output_over_y, "ctx2": output_own, "fin": finish,
    }
    for name, *which in OPENING_PLAN:
        actions[name](*which)
    for k in range(GRID_Z):
        for p in range(2):
            line_done(k, w_source(k, p), w_at(k, 0, p), wz_s.at[p])
        line_done(k, d_source(k, low), d_at(k, 0, 0, low), az_s)
        line_done(k, d_source(k, high), d_at(k, 0, 0, high), bz_s.at[0])
        line_done(k, d_at(k, 1, 0, high), d_at(k, 1, 0, high), bz_s.at[1])
        line_done(k, n_source(k, n_most), n_at(k, 0, 0, n_most), nz_s)
        for fx in range(2):
            for fy in range(2):
                source = n_source(k, n_rest) if (fx, fy) == (0, 0) else n_at(k, fx, fy, n_rest)
                line_done(k, source, n_at(k, fx, fy, n_rest), cz_s.at[fx, fy])
    for copy in sent_on + copies:
        copy.wait_send()
    for k in range(GRID_Z):
        for fx in range(2):
            for fy in range(2):
                for h, at in enumerate((low, high)):
                    block = d_at(k, fx, fy, at)
                    remote(
                        block, block, dc_s.at[0, k, fx, fy, h], dc_s.at[1, k, fx, fy, h], me.sibling
                    ).wait_recv()
            for fy in range(2):
                block = n_at(k, fx, fy, n_rest)
                remote(
                    block, block, cc_s.at[0, k, fx, fy], cc_s.at[1, k, fx, fy], me.sibling
                ).wait_recv()
        for i, (fx, fy, at) in enumerate(
            ((0, 0, n_most), (1, 0, n_most), (0, 1, n_most), (1, 1, n_low), (1, 1, n_high))
        ):
            block = n_at(k, fx, fy, at)
            remote(block, block, nc_s.at[0, k, i], nc_s.at[1, k, i], me.sibling).wait_recv()
    waits[1].wait()
    for copy in outs:
        copy.wait()


def opening(
    lengths, sequence_order, weights, gains, routes, cotangents, inputs, experts, collective_id
):
    bf16, f32 = jnp.bfloat16, jnp.float32
    chips, pair = lax.axis_size("dp"), lax.axis_size("tensor")
    own_rows, features = inputs.shape
    rows = pair * own_rows
    query, key, value, context, router = weights
    shard, wide = query.shape
    heads, key_heads = wide // HEAD_SIZE, key.shape[1] // HEAD_SIZE
    width = 2 * wide + 2 * key.shape[1] + AUX
    count, top = gains[2].shape[0], routes.shape[1]
    qkv = (heads + 2 * key_heads) * HEAD_SIZE
    cosine, sine = turn_tables(rows)
    dma = pltpu.SemaphoreType.DMA
    shapes = (
        ((chips, shard, width), bf16),
        ((chips * pair, *cotangents.shape), bf16),
        ((pair, *inputs.shape), bf16),
        ((chips * pair, own_rows, features + AUX), bf16),
        ((own_rows, features + AUX), bf16),
        ((own_rows, features), f32),
        ((rows, features), bf16),
        ((heads + 2 * key_heads, rows, HEAD_SIZE), f32),
        ((heads, rows, HEAD_SIZE), bf16),
        ((key_heads, rows, HEAD_SIZE), bf16),
        ((key_heads, rows, HEAD_SIZE), bf16),
        ((rows, wide), bf16),
    )
    anywhere, smem = pl.BlockSpec(memory_space=pl.ANY), pl.BlockSpec(memory_space=pltpu.SMEM)
    w, d, x, gathered, *rest = pl.pallas_call(
        functools.partial(opening_kernel, experts, qkv),
        out_shape=tuple(jax.ShapeDtypeStruct(*shape) for shape in shapes),
        in_specs=[smem] * 2 + [anywhere] * 14,
        out_specs=(anywhere,) * len(shapes),
        scratch_shapes=[
            pltpu.VMEM((pair, own_rows, features), bf16),
            pltpu.VMEM((chips, shard, qkv), bf16),
            pltpu.VMEM((chips, shard, wide), bf16),
            pltpu.VMEM((chips, shard, AUX), bf16),
            pltpu.VMEM((rows, features), bf16),
            pltpu.VMEM((heads + 2 * key_heads, rows, HEAD_SIZE), f32),
            pltpu.VMEM((heads, rows, HEAD_SIZE), bf16),
            pltpu.VMEM((key_heads, rows, HEAD_SIZE), bf16),
            pltpu.VMEM((key_heads, rows, HEAD_SIZE), bf16),
            pltpu.VMEM((rows, wide), bf16),
            pltpu.VMEM((own_rows, features), bf16),
            pltpu.VMEM((own_rows, features), bf16),
            pltpu.VMEM((own_rows, features), f32),
            pltpu.VMEM((own_rows, features + AUX), bf16),
            dma((3,)),
            dma((2, 1)),
            dma((2, 2, 2, 4)),
            dma((2, 4, 2)),
            dma((2, 4, 2, 2)),
            dma((2, 2, 4)),
            dma((2, 4)),
            dma((2, 4, 2)),
            dma((2, 2, 2, 4)),
            dma((2, 1)),
            dma((2, 4, 2)),
            dma((2, 4, 2, 2, 2)),
            dma((3,)),
            dma((qkv // 512,)),
            dma((8,)),
            dma((2, features // 512)),
            pltpu.VMEM((shard, width), bf16),
            pltpu.VMEM(context.shape, bf16),
            pltpu.VMEM((experts, shard), bf16),
            pltpu.VMEM((2, 1, shard), bf16),
            pltpu.VMEM((2, 1, count), bf16),
            pltpu.VMEM((top, rows), jnp.int32),
            pltpu.VMEM((rows, HEAD_SIZE), f32),
            pltpu.VMEM((rows, HEAD_SIZE), f32),
            dma((12,)),
            dma((1,)),
            dma((2, 2, 4)),
            dma((2, 4)),
            dma((2, 4)),
            dma((2, 4)),
            dma((2, 4)),
            dma((2, 4, 5)),
            dma((2, 1)),
            dma((2, 2)),
            dma((2, 2, 2, 2, 4)),
            dma((2, 4, 2, 2)),
        ],
        compiler_params=pltpu.CompilerParams(
            collective_id=collective_id, has_side_effects=True, vmem_limit_bytes=ATTENTION_VMEM
        ),
    )(
        lengths, sequence_order, query, key, value, context, router.T,
        *(gain[None] for gain in gains), routes.T, cotangents, inputs, cosine, sine,
    )
    return (
        w.reshape(-1, w.shape[2]),
        d.reshape(chips, -1, d.shape[2]),
        x.reshape(-1, x.shape[2]),
        gathered.reshape(chips, -1, gathered.shape[2]),
        *rest,
    )


def unturn(value, cosine, sine):
    return value * cosine - pltpu.roll(value, HEAD_SIZE // 2, 1) * sine


def backward_kernel(
    experts, lengths, sequence_order, back_in, residual_in, sent_in, dy_in, x_in, packed,
    cosine_in, sine_in, normed_in,
    raw_in, query_in, key_in, value_in, context_in,
    grads, input_gradient,
    back, residual, sent, dy, x, w, ctx, aux_w, normed, raw, query, key, value, context,
    cot, context_cot, raw_cot, key_sum, value_sum, small, first, first_got, stage, result,
    cosine, sine, probs, in_s, out_s, y_s, g_s,
):
    bf16, f32 = jnp.bfloat16, jnp.float32
    me = Place()
    own_rows, features = residual.shape
    rows = 2 * own_rows
    heads, key_heads = query.shape[0], key.shape[0]
    group = heads // key_heads
    qkv, wide = w.shape[1], heads * HEAD_SIZE
    chunk = 512
    mine = pl.ds(pl.multiple_of(me.y * own_rows, own_rows), own_rows)
    theirs = pl.ds(pl.multiple_of((1 - me.y) * own_rows, own_rows), own_rows)
    loads = [
        pltpu.make_async_copy(source, target, in_s.at[i])
        for i, (source, target) in enumerate(
            (
                (packed.at[:, pl.ds(qkv, AUX)], aux_w),
                (back_in, back),
                (sent_in, sent),
                (residual_in, residual),
                (dy_in, dy),
                (packed.at[:, pl.ds(qkv + AUX, wide)], ctx),
                (context_in, context),
                (value_in, value),
                (key_in, key),
                (query_in, query),
                (raw_in, raw),
                (packed.at[:, pl.ds(0, qkv)], w),
                (normed_in, normed),
                (x_in, x),
                (cosine_in, cosine),
                (sine_in, sine),
            )
        )
    ]
    for copy in loads:
        copy.start()
    meet_y(me)
    for copy in loads[:5]:
        copy.wait()
    aux_t = aux_w[...].astype(f32).T
    gain_one, gain_two, query_gain, key_gain = gain_rows(aux_t, experts, features // HEAD_SIZE)

    lane = lax.broadcasted_iota(jnp.int32, (own_rows, AUX), 1)
    coded = sent[:, features:].astype(f32)
    gates = coded + pltpu.roll(coded, AUX - experts, 1)
    gates = jnp.where(lane < experts, gates, 0.0)
    column = lax.broadcasted_iota(jnp.int32, (AUX, AUX), 0)
    target = lax.broadcasted_iota(jnp.int32, (AUX, AUX), 1)
    fold = ((column % (2 * experts)) // 2 == target).astype(bf16)
    gate_cot = dot(back[:, features:], fold)
    logit_cot = gates * (gate_cot - jnp.sum(gates * gate_cot, axis=-1, keepdims=True))
    logit_cot = logit_cot.astype(bf16)
    small[...] = dot(sent[:, :features], logit_cot, ((0,), (0,)))
    midnorm = jnp.zeros((1, features), f32)
    step, swaps = 32, []
    for i in range(own_rows // step):
        at = slice(i * step, (i + 1) * step)
        total = residual[at, :]
        scale = inverse_norm(total)
        unit = total * scale
        normed_cot = back[at, :features].astype(f32) + dot(
            logit_cot[at, :], aux_w[...], ((1,), (1,))
        )
        midnorm = midnorm + jnp.sum(normed_cot * unit, axis=0, keepdims=True)
        gained = normed_cot * gain_two
        total_cot = dy[at, :].astype(f32) + scale * (
            gained - unit * jnp.mean(gained * unit, axis=-1, keepdims=True)
        )
        residual[at, :] = total_cot
        there = pl.ds(pl.multiple_of(me.y * own_rows + i * step, step), step)
        cot[there, :] = total_cot.astype(bf16)
        swap = remote(cot.at[there], cot.at[there], y_s.at[0, i], y_s.at[1, i], me.y_mate)
        swap.start()
        swaps.append(swap)
    for copy in loads[5:10]:
        copy.wait()

    def spread_context(part):
        for c in range(wide // chunk):
            cols = pl.ds(c * chunk, chunk)
            context_cot[part, cols] = dot(cot[part, :], ctx[:, cols]).astype(bf16)

    allowed = allowed_pairs(lengths[sequence_order[me.dp]], rows)

    def recall(h, carry):
        probs[h] = probabilities(query[h], key[h // group], allowed)
        return carry

    spread_context(mine)
    lax.fori_loop(0, heads, recall, 0)
    for swap in swaps:
        swap.wait_recv()
    spread_context(theirs)
    for copy in loads[10:]:
        copy.wait()

    turn_c, turn_s = cosine[...], sine[...]
    key_sum[...] = jnp.zeros_like(key_sum)
    value_sum[...] = jnp.zeros_like(value_sum)

    def raw_back(back_rows, unnormed, gain):
        scale = inverse_norm(unnormed)
        unit = unnormed * scale
        part = jnp.sum(back_rows * unit, axis=0, keepdims=True)
        gained = back_rows * gain
        raw_rows = scale * (gained - unit * jnp.mean(gained * unit, axis=-1, keepdims=True))
        return raw_rows.astype(bf16), part

    def head(h, query_part):
        g = h // group
        at = pl.ds(pl.multiple_of(h * HEAD_SIZE, HEAD_SIZE), HEAD_SIZE)
        soft = probs[h]
        cots = context_cot[:, at]
        prob_cot = dot(cots, value[g], ((1,), (1,)))
        score_cot = soft * (prob_cot - jnp.sum(soft * prob_cot, axis=-1, keepdims=True))
        score_cot = score_cot.astype(bf16)
        value_sum[g] += dot(soft.astype(bf16), cots, ((0,), (0,)))
        key_sum[g] += dot(score_cot, query[h], ((0,), (0,)))
        turned = dot(score_cot, key[g]) * SCORE_SCALE
        raw_cot[:, at], part = raw_back(unturn(turned, turn_c, turn_s), raw[h], query_gain)
        return query_part + part

    query_part = lax.fori_loop(0, heads, head, jnp.zeros((1, HEAD_SIZE), f32))
    key_part = jnp.zeros((1, HEAD_SIZE), f32)
    for g in range(key_heads):
        turned = key_sum[g] * SCORE_SCALE
        at = wide + g * HEAD_SIZE
        raw_cot[:, at : at + HEAD_SIZE], part = raw_back(
            unturn(turned, turn_c, turn_s), raw[heads + g], key_gain
        )
        key_part = key_part + part
        at = at + key_heads * HEAD_SIZE
        raw_cot[:, at : at + HEAD_SIZE] = value_sum[g].astype(bf16)

    copies = []
    for c in range(features // chunk):
        cols = pl.ds(c * chunk, chunk)
        first[:, cols] = dot(raw_cot[theirs, :], w[cols, :], ((1,), (1,))).astype(bf16)
        copy = remote(
            first.at[:, cols], first_got.at[:, cols], y_s.at[0, len(swaps) + c], y_s.at[1, len(swaps) + c], me.y_mate
        )
        copy.start()
        copies.append(copy)
    block = 256

    def store(i):
        slot = i % 2
        return pltpu.make_async_copy(
            stage.at[slot],
            grads.at[pl.ds(pl.multiple_of(i * block, block), block), pl.ds(0, qkv + wide)],
            g_s.at[slot],
        )

    def weight_grads(i, carry):
        slot = i % 2
        at = pl.ds(pl.multiple_of(i * block, block), block)

        @pl.when(i >= 2)
        def _():
            store(i - 2).wait()

        for c in range(qkv // chunk):
            cols = pl.ds(c * chunk, chunk)
            stage[slot, :, cols] = dot(normed[:, at], raw_cot[:, cols], ((0,), (0,))).astype(bf16)
        for c in range(wide // chunk):
            cols = pl.ds(c * chunk, chunk)
            stage[slot, :, pl.ds(qkv + c * chunk, chunk)] = dot(
                cot[:, at], context[:, cols], ((0,), (0,))
            ).astype(bf16)
        store(i).start()
        return carry

    lax.fori_loop(0, features // block, weight_grads, 0)
    prenorm = jnp.zeros((1, features), f32)
    for copy in copies:
        copy.wait_recv()
    for c in range(features // chunk):
        cols = pl.ds(c * chunk, chunk)
        back_cols = dot(raw_cot[mine, :], w[cols, :], ((1,), (1,)))
        result_part = back_cols + first_got[:, cols].astype(f32)
        back[:, cols] = result_part.astype(bf16)
    step = 32
    for i in range(own_rows // step):
        at = slice(i * step, (i + 1) * step)
        stream = x[pl.ds(pl.multiple_of(me.y * own_rows + i * step, step), step), :].astype(f32)
        scale = inverse_norm(stream)
        unit = stream * scale
        first_cot = back[at, :features].astype(f32)
        prenorm = prenorm + jnp.sum(first_cot * unit, axis=0, keepdims=True)
        gained = first_cot * gain_one
        result[at, :] = (
            residual[at, :]
            + scale * (gained - unit * jnp.mean(gained * unit, axis=-1, keepdims=True))
        ).astype(bf16)
    done = pltpu.make_async_copy(result, input_gradient, out_s.at[0])
    done.start()
    chunks = features // HEAD_SIZE
    extra = jnp.concatenate(
        [
            jnp.zeros((experts, features), f32),
            prenorm,
            midnorm,
            jnp.concatenate([query_part] * chunks, axis=1),
            jnp.concatenate([key_part] * chunks, axis=1),
            jnp.zeros((AUX - experts - 4, features), f32),
        ],
        axis=0,
    )
    aux_w[...] = (small[...] + extra.T).astype(bf16)
    last = pltpu.make_async_copy(aux_w, grads.at[:, pl.ds(qkv + wide, AUX)], out_s.at[1])
    last.start()
    for swap in swaps:
        swap.wait_send()
    for copy in copies:
        copy.wait_send()
    for i in (2, 1):
        store(features // block - i).wait()
    done.wait()
    last.wait()


def attention_backward(
    lengths, sequence_order, back, residual, sent, dy, x_pair, packed, saved, experts, collective_id
):
    bf16, f32 = jnp.bfloat16, jnp.float32
    normed, raw, query, key, value, context = saved
    own_rows, features = residual.shape
    rows = 2 * own_rows
    heads, key_heads = query.shape[0], key.shape[0]
    wide = heads * HEAD_SIZE
    qkv = wide + 2 * key_heads * HEAD_SIZE
    cosine, sine = turn_tables(rows)
    dma = pltpu.SemaphoreType.DMA
    anywhere, smem = pl.BlockSpec(memory_space=pl.ANY), pl.BlockSpec(memory_space=pltpu.SMEM)
    return pl.pallas_call(
        functools.partial(backward_kernel, experts),
        out_shape=(
            jax.ShapeDtypeStruct((features, qkv + wide + AUX), bf16),
            jax.ShapeDtypeStruct((own_rows, features), bf16),
        ),
        in_specs=[smem] * 2 + [anywhere] * 14,
        out_specs=(anywhere,) * 2,
        scratch_shapes=[
            pltpu.VMEM((own_rows, features + AUX), bf16),
            pltpu.VMEM((own_rows, features), f32),
            pltpu.VMEM((own_rows, features + AUX), bf16),
            pltpu.VMEM((own_rows, features), bf16),
            pltpu.VMEM((rows, features), bf16),
            pltpu.VMEM((features, qkv), bf16),
            pltpu.VMEM((features, wide), bf16),
            pltpu.VMEM((features, AUX), bf16),
            pltpu.VMEM((rows, features), bf16),
            pltpu.VMEM((heads + 2 * key_heads, rows, HEAD_SIZE), f32),
            pltpu.VMEM((heads, rows, HEAD_SIZE), bf16),
            pltpu.VMEM((key_heads, rows, HEAD_SIZE), bf16),
            pltpu.VMEM((key_heads, rows, HEAD_SIZE), bf16),
            pltpu.VMEM((rows, wide), bf16),
            pltpu.VMEM((rows, features), bf16),
            pltpu.VMEM((rows, wide), bf16),
            pltpu.VMEM((rows, qkv), bf16),
            pltpu.VMEM((key_heads, rows, HEAD_SIZE), f32),
            pltpu.VMEM((key_heads, rows, HEAD_SIZE), f32),
            pltpu.VMEM((features, AUX), f32),
            pltpu.VMEM((own_rows, features), bf16),
            pltpu.VMEM((own_rows, features), bf16),
            pltpu.VMEM((2, 256, qkv + wide), bf16),
            pltpu.VMEM((own_rows, features), bf16),
            pltpu.VMEM((rows, HEAD_SIZE), f32),
            pltpu.VMEM((rows, HEAD_SIZE), f32),
            pltpu.VMEM((heads, rows, rows), f32),
            dma((16,)),
            dma((2,)),
            dma((2, own_rows // 32 + features // 512)),
            dma((2,)),
        ],
        compiler_params=pltpu.CompilerParams(
            collective_id=collective_id, has_side_effects=True, vmem_limit_bytes=ATTENTION_VMEM
        ),
    )(
        lengths, sequence_order, back, residual, sent, dy, x_pair, packed, cosine, sine,
        normed, raw, query, key, value, context,
    )


LAST_CUT = 5
LAST_PLAN = (
    ("gx", 0, 0), ("dy", 0, 1, 1), ("gx", 0, 1), ("dy", 0, 0, 1), ("dy", 1, 1, 1), ("db", 0, 1),
    ("gx", 1, 1), ("db", 0, 0), ("dy", 2, 1, 1), ("dy", 1, 1, 0), ("gx", 1, 0), ("db", 1, 1),
    ("dy", 2, 1, 0), ("gx", 2, 0), ("db", 2, 1), ("dy", 0, 1, 0), ("dy", 2, 0, 1),
    ("dy", 0, 0, 0), ("dy", 3, 1, 1), ("gc", 0), ("dy", 1, 0, 0), ("dy", 1, 0, 1),
    ("dy", 3, 1, 0), ("dy", 2, 0, 0), ("gx", 2, 1), ("dax", 2), ("dax", 0), ("dax", 1),
    ("gc", 1), ("gc", 2), ("gx", 3, 0), ("dy", 3, 0, 1), ("gx", 3, 1), ("da", 0), ("dax", 3),
    ("dy", 3, 0, 0), ("db", 1, 0), ("da", 1), ("db", 2, 0), ("da", 2), ("gc", 3), ("sm",),
    ("db", 3, 1), ("db", 3, 0), ("sm2",), ("da", 3), ("bx",),
)


def last_scatter_kernel(
    g_part, d_part, g_out, d_out,
    g_own, g_core, g_x, g_z, d_own, d_core, d_y, a_x, b_x, a_z, b_z, small_got,
    gl_s, gc_s, gx_s, gz_s, dl_s, dc_s, dy_s, ax_s, bx_s, az_s, bz_s, small_s, out_s,
):
    me = Place()
    g_rows, d_rows = g_own.shape[2], d_own.shape[3]
    cut, g_half = a_x.shape[1], g_rows // 2
    g_all, low, high = (0, g_rows), (0, cut), (cut, d_rows - cut)
    low_at, high_at = pl.ds(0, cut), pl.ds(cut, d_rows - cut)
    last = GRID_Z - 1
    loads, cores, sends = {}, {}, []

    def g_chunk(k, fx, fc):
        return g_part.at[me.dp_at(me.farthest(k), fx, fc)]

    def d_chunk(k, fx, fy, fc):
        return d_part.at[me.dp_at(me.farthest(k), fx, fc) * 2 + me.y_at(fy)]

    pairs = ((1, 1), (0, 1), (1, 0), (0, 0))
    for k in range(GRID_Z):
        for fx in (1, 0):
            loads[k, fx] = pltpu.make_async_copy(g_chunk(k, fx, 0), g_own.at[k, fx], gl_s.at[k, fx])
            loads[k, fx].start()
        for fx, fy in pairs:
            loads[k, fx, fy] = pltpu.make_async_copy(
                d_chunk(k, fx, fy, 0), d_own.at[k, fx, fy], dl_s.at[k, fx, fy]
            )
            loads[k, fx, fy].start()
    me.greet()
    for k in range(GRID_Z):
        for fx in (1, 0):
            cores[k, fx] = remote(
                g_chunk(k, fx, 1), g_core.at[k, fx],
                gc_s.at[0, k, fx], gc_s.at[1, k, fx], me.sibling,
            )
        for fx, fy in pairs:
            cores[k, fx, fy] = remote(
                d_chunk(k, fx, fy, 1), d_core.at[k, fx, fy],
                dc_s.at[0, k, fx, fy], dc_s.at[1, k, fx, fy], me.sibling,
            )
        for index in ((1,), (1, 1), (0, 1), (0,), (1, 0), (0, 0)):
            cores[(k, *index)].start()

    gx = [
        [
            remote(
                g_own.at[k, 1, pl.ds(h * g_half, g_half)], g_x.at[k, pl.ds(h * g_half, g_half)],
                gx_s.at[0, k, h], gx_s.at[1, k, h], me.x_mate,
            )
            for h in range(2)
        ]
        for k in range(GRID_Z)
    ]
    dy = {
        (k, fx, h): remote(
            d_own.at[k, fx, 1, at], d_y.at[k, fx, at],
            dy_s.at[0, k, fx, h], dy_s.at[1, k, fx, h], me.y_mate,
        )
        for k in range(GRID_Z)
        for fx in range(2)
        for h, at in enumerate((low_at, high_at))
    }
    ax = [
        remote(d_own.at[k, 1, 0, low_at], a_x.at[k], ax_s.at[0, k], ax_s.at[1, k], me.x_mate)
        for k in range(GRID_Z)
    ]
    bx = remote(d_own.at[last, 1, 0, high_at], b_x, bx_s.at[0], bx_s.at[1], me.x_mate)

    here = set()

    def arrive(*index):
        if index not in here:
            here.add(index)
            loads[index].wait()
            cores[index].wait_recv()

    def onward(source, buffer, sem, to, side, mate):
        ends = 1 - (me.z - 1 - to + GRID_Z - 1) // GRID_Z
        slot = to if side == 0 else to + (GRID_Z - to) * ends
        return remote(source, buffer.at[slot], sem.at[0, to], sem.at[1, slot], mate)

    def line(k, block, source, rows, buffer, sem, shift):
        to = me.farthest(k)
        for side, ahead, mate, more in (
            (0, to > me.z, me.above, me.has_below),
            (1, to < me.z, me.below, me.has_above),
        ):
            slot = to if k < last or side == 0 else GRID_Z
            came = remote(source, buffer.at[slot], sem.at[0, slot], sem.at[1, slot], mate)

            def gather(came=came, slot=slot):
                came.wait_recv()
                add_rows(block, [(buffer.at[slot], shift)], rows)

            if k < last:

                @pl.when(ahead)
                def _():
                    pl.when(more)(gather)
                    onward(source, buffer, sem, to, side, mate).start()
            else:
                pl.when(more)(gather)

    def line_done(k, source, buffer, sem):
        to = me.farthest(k)
        for side, ahead, mate in ((0, to > me.z, me.above), (1, to < me.z, me.below)):

            @pl.when(ahead)
            def _():
                onward(source, buffer, sem, to, side, mate).wait_send()

    width = g_own.shape[3]
    small_block = g_own.at[last, 0, :, pl.ds(width - AUX, AUX)]
    small = remote(small_block, small_got, small_s.at[0], small_s.at[1], me.y_mate)

    def g_across(k, h):
        arrive(k, 1)
        add_rows(g_own.at[k, 1], [(g_core.at[k, 1], 0)], (h * g_half, g_half))
        gx[k][h].start()

    def g_column(k):
        arrive(k, 0)
        for h in range(2):
            gx[k][h].wait_recv()
        add_rows(g_own.at[k, 0], [(g_core.at[k, 0], 0), (g_x.at[k], 0)], g_all)
        line(k, g_own.at[k, 0], g_own.at[k, 0], g_all, g_z, gz_s, 0)

    def over_y(k, fx, h):
        arrive(k, fx, 1)
        add_rows(d_own.at[k, fx, 1], [(d_core.at[k, fx, 1], 0)], (low, high)[h])
        dy[k, fx, h].start()

    def from_y(k, fx, h, *more):
        arrive(k, fx, 0)
        dy[k, fx, h].wait_recv()
        rest = [(d_core.at[k, fx, 0], 0), (d_y.at[k, fx], 0), *more]
        add_rows(d_own.at[k, fx, 0], rest, (low, high)[h])

    def b_line(k, fx):
        from_y(k, fx, 1)
        block = d_own.at[k, fx, 0]
        line(k, block, block.at[high_at], high, b_z.at[fx], bz_s.at[fx], cut)
        if fx and k == last:
            bx.start()

    def a_over_x(k):
        from_y(k, 1, 0)
        ax[k].start()

    def a_line(k):
        ax[k].wait_recv()
        from_y(k, 0, 0, (a_x.at[k], 0))
        block = d_own.at[k, 0, 0]
        line(k, block, block.at[low_at], low, a_z, az_s, 0)

    def b_from_x():
        bx.wait_recv()
        add_rows(d_own.at[last, 0, 0], [(b_x, cut)], high)

    def small_sum():
        small.wait()
        total = small_block[...].astype(jnp.float32) + small_got[...].astype(jnp.float32)
        small_block[...] = total.astype(small_got.dtype)

    actions = {
        "gx": g_across, "gc": g_column, "dy": over_y, "db": b_line, "dax": a_over_x, "da": a_line,
        "bx": b_from_x, "sm": small.start, "sm2": small_sum,
    }
    for name, *which in LAST_PLAN:
        actions[name](*which)
    outs = [
        pltpu.make_async_copy(d_own.at[last, 0, 0], d_out, out_s.at[0]),
        pltpu.make_async_copy(g_own.at[last, 0], g_out, out_s.at[1]),
    ]
    for copy in outs:
        copy.start()
    for k in range(GRID_Z):
        for h in range(2):
            gx[k][h].wait_send()
        for fx in range(2):
            for h in range(2):
                dy[k, fx, h].wait_send()
        ax[k].wait_send()
        if k < last:
            line_done(k, g_own.at[k, 0], g_z, gz_s)
            for fx in range(2):
                line_done(k, d_own.at[k, fx, 0, high_at], b_z.at[fx], bz_s.at[fx])
            line_done(k, d_own.at[k, 0, 0, low_at], a_z, az_s)
    bx.wait_send()
    for sent in cores.values():
        sent.wait_send()
    for copy in outs:
        copy.wait()


def last_scatter(grads, sums, collective_id):
    chips, pair = lax.axis_size("dp"), lax.axis_size("tensor")
    g_rows, g_wide = grads.shape[0] // chips, grads.shape[1]
    d_rows, d_wide = sums.shape[0] // (chips * pair), sums.shape[1]
    cut = d_rows * LAST_CUT // 8
    dma = pltpu.SemaphoreType.DMA
    low = grads.dtype
    anywhere = pl.BlockSpec(memory_space=pl.ANY)
    return pl.pallas_call(
        last_scatter_kernel,
        out_shape=(
            jax.ShapeDtypeStruct((g_rows, g_wide), low),
            jax.ShapeDtypeStruct((d_rows, d_wide), low),
        ),
        in_specs=[anywhere] * 2,
        out_specs=(anywhere,) * 2,
        scratch_shapes=[
            pltpu.VMEM((4, 2, g_rows, g_wide), low),
            pltpu.VMEM((4, 2, g_rows, g_wide), low),
            pltpu.VMEM((4, g_rows, g_wide), low),
            pltpu.VMEM((5, g_rows, g_wide), low),
            pltpu.VMEM((4, 2, 2, d_rows, d_wide), low),
            pltpu.VMEM((4, 2, 2, d_rows, d_wide), low),
            pltpu.VMEM((4, 2, d_rows, d_wide), low),
            pltpu.VMEM((4, cut, d_wide), low),
            pltpu.VMEM((d_rows - cut, d_wide), low),
            pltpu.VMEM((5, cut, d_wide), low),
            pltpu.VMEM((2, 5, d_rows - cut, d_wide), low),
            pltpu.VMEM((g_rows, AUX), low),
            dma((4, 2)),
            dma((2, 4, 2)),
            dma((2, 4, 2)),
            dma((2, 5)),
            dma((4, 2, 2)),
            dma((2, 4, 2, 2)),
            dma((2, 4, 2, 2)),
            dma((2, 4)),
            dma((2,)),
            dma((2, 5)),
            dma((2, 2, 5)),
            dma((2,)),
            dma((2,)),
        ],
        compiler_params=pltpu.CompilerParams(
            collective_id=collective_id, has_side_effects=True, vmem_limit_bytes=60 * 1024 * 1024
        ),
    )(grads.reshape(chips, g_rows, g_wide), sums.reshape(chips * pair, d_rows, d_wide))


def unpack_kernel(
    experts, summed, added, residual,
    layer_output, query, key, value, context, router, prenorm, midnorm, querynorm, keynorm,
):
    f32 = jnp.float32
    wide, narrow = query.shape[1], key.shape[1]
    layer_output[...] = (residual[...] + added[...].astype(f32)).astype(layer_output.dtype)
    query[...] = summed[:, pl.ds(0, wide)].astype(f32)
    key[...] = summed[:, pl.ds(wide, narrow)].astype(f32)
    value[...] = summed[:, pl.ds(wide + narrow, narrow)].astype(f32)
    start = wide + 2 * narrow
    context[...] = summed[:, pl.ds(start, wide)].astype(f32).T
    small = summed[:, pl.ds(start + wide, AUX)].astype(f32)
    router[...] = small[:, :experts]
    rows = small.T
    prenorm[...] = rows[experts : experts + 1, :]
    midnorm[...] = rows[experts + 1 : experts + 2, :]
    count = querynorm.shape[1]
    lane = lax.broadcasted_iota(jnp.int32, (count, AUX), 1)
    row = lax.broadcasted_iota(jnp.int32, (count, AUX), 0)
    pick = row + lax.axis_index("dp") * count == lane
    for target, at in ((querynorm, experts + 2), (keynorm, experts + 3)):
        part = jnp.where(pick, rows[at : at + 1, :], 0.0)
        target[...] = jnp.sum(part, axis=1, keepdims=True).T


def unpack(summed, added, residual, query_width, key_width, experts, norm_part):
    bf16, f32 = jnp.bfloat16, jnp.float32
    shard = summed.shape[0]
    own_rows, features = residual.shape
    shapes = (
        ((own_rows, features), bf16),
        ((shard, query_width), f32),
        ((shard, key_width), f32),
        ((shard, key_width), f32),
        ((query_width, shard), f32),
        ((shard, experts), f32),
        ((1, shard), f32),
        ((1, shard), f32),
        ((1, norm_part), f32),
        ((1, norm_part), f32),
    )
    vmem = pl.BlockSpec(memory_space=pltpu.VMEM)
    *large, first, second, third, fourth = pl.pallas_call(
        functools.partial(unpack_kernel, experts),
        out_shape=tuple(jax.ShapeDtypeStruct(*shape) for shape in shapes),
        in_specs=[vmem] * 3,
        out_specs=(vmem,) * len(shapes),
        compiler_params=pltpu.CompilerParams(vmem_limit_bytes=32 * 1024 * 1024),
    )(summed, added, residual)
    return (*large, first[0], second[0], third[0], fourth[0])


def gathered_body(
    layer_input,
    query_weight,
    key_projection,
    value_projection,
    context_weight,
    router_weight,
    expert_gate,
    expert_up,
    expert_down,
    prenorm_gain,
    midnorm_gain,
    querynorm_gain,
    keynorm_gain,
    routes,
    lengths,
    sequence_order,
    output_cotangent,
):
    bf16, f32 = jnp.bfloat16, jnp.float32
    tensor_count = lax.axis_size("tensor")
    tensor_index = lax.axis_index("tensor")
    dp_count = lax.axis_size("dp")
    dp_index = lax.axis_index("dp")
    own_rows, features = layer_input.shape
    block_rows = own_rows * tensor_count
    tokens = block_rows * dp_count
    expert_count = EXP_DEV * dp_count
    capacity = 3 * block_rows * TOP // (4 * EXP_DEV)
    most_rows = (5 * block_rows * TOP + 4 * expert_count - 1) // (4 * expert_count)
    shard = features // dp_count
    query_width = query_weight.shape[1]
    key_width = key_projection.shape[1]
    norm_part = HEAD_SIZE // dp_count

    packed, cot_all, input_rows, normed_all, sent, residual, *saved = opening(
        lengths,
        sequence_order,
        (query_weight, key_projection, value_projection, context_weight, router_weight),
        (prenorm_gain, midnorm_gain, querynorm_gain, keynorm_gain),
        routes,
        output_cotangent,
        layer_input,
        expert_count,
        0,
    )
    route_from = query_width + 2 * key_width + expert_count + 4
    routes_all = packed[:, route_from : route_from + 2 * TOP].astype(jnp.int32)
    routes_all = routes_all.reshape(dp_count, shard, 2, TOP).transpose(0, 3, 2, 1)
    routes_all = routes_all.reshape(dp_count, TOP, block_rows)
    position = jnp.arange(block_rows, dtype=jnp.int32)
    live = position[None, :] < lengths[sequence_order][:, None]

    expert_own = dp_index * EXP_DEV + jnp.arange(EXP_DEV, dtype=jnp.int32)
    hot = jnp.any(routes_all[:, None, :, :] == expert_own[None, :, None, None], axis=2)
    hot = hot & live[:, None, :]
    before = (position[:, None] < position[None, :]).astype(bf16)
    rank = jnp.einsum("bes,st->bet", hot.astype(bf16), before, preferred_element_type=f32)
    rank = rank.astype(jnp.int32)
    counts = rank[:, :, -1] + hot[:, :, -1]
    earlier = jnp.cumsum(counts, axis=0) - counts
    slot = earlier[:, :, None] + rank
    slot = jnp.where(hot & (slot < capacity), slot, -capacity)
    begin = jnp.minimum(earlier, capacity) // WINDOW_ALIGN * WINDOW_ALIGN
    info = jnp.concatenate([dp_index[None], begin.reshape(-1), tensor_index[None]])
    out_part, back_part, gate_gradient, up_gradient, down_gradient = expert_layer(
        info.astype(jnp.int32),
        slot,
        normed_all,
        cot_all,
        expert_gate,
        expert_up,
        expert_down,
        capacity,
        most_rows,
    )
    returned = scatter_all(back_part.reshape(tokens, features + AUX), 3)
    grads, input_gradient = attention_backward(
        lengths,
        sequence_order,
        returned,
        residual,
        sent,
        output_cotangent,
        input_rows,
        packed,
        saved,
        expert_count,
        6,
    )
    summed, expert_sum = last_scatter(grads, out_part.reshape(tokens, features), 4)
    (
        layer_output,
        query_gradient,
        key_gradient,
        value_gradient,
        context_gradient,
        router_gradient,
        prenorm_gradient,
        midnorm_gradient,
        querynorm_gradient,
        keynorm_gradient,
    ) = unpack(summed, expert_sum, residual, query_width, key_width, expert_count, norm_part)
    return (
        layer_output,
        input_gradient,
        query_gradient,
        key_gradient,
        value_gradient,
        context_gradient,
        router_gradient,
        gate_gradient,
        up_gradient,
        down_gradient,
        prenorm_gradient,
        midnorm_gradient,
        querynorm_gradient,
        keynorm_gradient,
    )


def solution(mesh):
    return jax.shard_map(
        gathered_body if mesh.shape["dp"] <= 16 else body,
        mesh=mesh,
        in_specs=(
            P(("dp", "tensor"), None),
            P("dp", "tensor"),
            P("dp", "tensor"),
            P("dp", "tensor"),
            P("tensor", "dp"),
            P("dp", None),
            P("dp", None, "tensor"),
            P("dp", None, "tensor"),
            P("dp", "tensor", None),
            P("dp"),
            P("dp"),
            P("dp"),
            P("dp"),
            P("dp", None),
            P(),
            P(),
            P(("dp", "tensor"), None),
        ),
        out_specs=(
            P(("dp", "tensor"), None),
            P(("dp", "tensor"), None),
            P("dp", "tensor"),
            P("dp", "tensor"),
            P("dp", "tensor"),
            P("tensor", "dp"),
            P("dp", None),
            P("dp", None, "tensor"),
            P("dp", None, "tensor"),
            P("dp", "tensor", None),
            P("dp"),
            P("dp"),
            P("dp"),
            P("dp"),
        ),
        check_vma=False,
    )
```

```python
import functools
import math

import jax
import jax.numpy as jnp
import numpy as np
from jax import lax
from jax.experimental import pallas as pl
from jax.experimental.pallas import tpu as pltpu
from jax.sharding import PartitionSpec as P

HEAD_SIZE = 128
TOP = 8
EXP_DEV = 2


epsilon = 1e-06
rope_base = 1000000.0
masked_score = -1e30


def carried_in(value, axis, combine, identity):
    count, place = (lax.axis_size(axis), lax.axis_index(axis))
    everything = lax.all_gather(value, axis)
    start = jnp.broadcast_to(jnp.asarray(identity, value.dtype), value.shape)

    def hop(k, before):
        reached = k < place
        new = combine(before, everything[k])
        return jnp.where(reached, new, before)

    return lax.fori_loop(0, count, hop, start)


def rms_normalize(value_rows):
    scaling = lax.rsqrt(jnp.mean(value_rows * value_rows, axis=-1, keepdims=True) + epsilon)
    return (value_rows * scaling, scaling)


def norm_back(cotangent, unit_rows, scaling):
    return scaling * (
        cotangent - unit_rows * jnp.mean(cotangent * unit_rows, axis=-1, keepdims=True)
    )


def rotary_apply(value_rows, cosine_table, sine_values):
    middle = value_rows.shape[-1] // 2
    former = value_rows[..., :middle]
    latter = value_rows[..., middle:]
    return jnp.concatenate(
        [
            former * cosine_table - latter * sine_values,
            latter * cosine_table + former * sine_values,
        ],
        axis=-1,
    )


def matrix_product(former, latter):
    return jnp.dot(former, latter, preferred_element_type=jnp.float32)


def contract(former, latter):
    return lax.dot_general(
        former, latter, (((0,), (0,)), ((), ())), preferred_element_type=jnp.float32
    )


def transposed(former, latter):
    return lax.dot_general(
        former, latter, (((1,), (1,)), ((), ())), preferred_element_type=jnp.float32
    )


def to_owners(buffer):
    return lax.all_to_all(buffer, "dp", split_axis=1, concat_axis=1, tiled=True)


def owner_reduce(partial_rows):
    shares = lax.psum_scatter(
        partial_rows.astype(jnp.bfloat16), "tensor", scatter_dimension=2, tiled=True
    )
    return lax.all_gather(shares, "tensor", axis=2, tiled=True)


def body(
    layer_input,
    query_weight,
    key_projection,
    value_projection,
    context_weight,
    router_weight,
    expert_gate,
    expert_up,
    expert_down,
    prenorm_gain,
    midnorm_gain,
    querynorm_gain,
    keynorm_gain,
    routes,
    lengths,
    sequence_order,
    output_cotangent,
):
    tensor_count = lax.axis_size("tensor")
    tensor_index = lax.axis_index("tensor")
    dp_count = lax.axis_size("dp")
    own_rows = layer_input.shape[0]
    block_rows = own_rows * tensor_count
    features = layer_input.shape[1]
    expert_count = EXP_DEV * dp_count
    capacity = 3 * block_rows * TOP // (4 * EXP_DEV)
    most_rows = (5 * block_rows * TOP + 4 * expert_count - 1) // (4 * expert_count)
    slot_total = EXP_DEV * dp_count * most_rows
    (
        query_all,
        key_all,
        value_all,
        context_all,
        router_all,
        gain_first,
        gain_second,
        query_gain,
        gain_key,
    ) = (
        lax.all_gather(query_weight, "dp", axis=0, tiled=True),
        lax.all_gather(key_projection, "dp", axis=0, tiled=True),
        lax.all_gather(value_projection, "dp", axis=0, tiled=True),
        lax.all_gather(context_weight, "dp", axis=1, tiled=True),
        lax.all_gather(router_weight, "dp", axis=0, tiled=True),
        lax.all_gather(prenorm_gain, "dp", axis=0, tiled=True),
        lax.all_gather(midnorm_gain, "dp", axis=0, tiled=True),
        lax.all_gather(querynorm_gain, "dp", axis=0, tiled=True),
        lax.all_gather(keynorm_gain, "dp", axis=0, tiled=True),
    )
    input_rows, cot_rows = (
        lax.all_gather(layer_input, "tensor", axis=0, tiled=True),
        lax.all_gather(output_cotangent, "tensor", axis=0, tiled=True),
    )
    position = jnp.arange(block_rows, dtype=jnp.int32)
    seq_length = lengths[sequence_order[lax.axis_index("dp")]]
    token_live = position < seq_length
    frequency = jnp.exp(
        -math.log(rope_base) * jnp.arange(HEAD_SIZE // 2, dtype=jnp.float32) * (2.0 / HEAD_SIZE)
    )
    angles = position.astype(jnp.float32)[:, None] * frequency[None, :]
    cosine_table = jnp.cos(angles)[:, None, :]
    sine_values = jnp.sin(angles)[:, None, :]
    heads_query = query_all.shape[1] // HEAD_SIZE
    heads_key = key_all.shape[1] // HEAD_SIZE
    group_width = heads_query // heads_key
    gain_one = gain_first.astype(jnp.float32)
    gain_two = gain_second.astype(jnp.float32)
    query_factor = query_gain.astype(jnp.float32)
    key_factor = gain_key.astype(jnp.float32)
    stream = input_rows.astype(jnp.float32)
    unit_first, scale_first = rms_normalize(stream)
    first_layer_normed = (unit_first * gain_one).astype(jnp.bfloat16)
    query_unnormed = matrix_product(first_layer_normed, query_all).reshape(
        block_rows, heads_query, HEAD_SIZE
    )
    key_unnormed = matrix_product(first_layer_normed, key_all).reshape(
        block_rows, heads_key, HEAD_SIZE
    )
    value_rows = (
        matrix_product(first_layer_normed, value_all)
        .astype(jnp.bfloat16)
        .reshape(block_rows, heads_key, HEAD_SIZE)
    )
    query_unit, query_scale = rms_normalize(query_unnormed)
    key_unit, key_scale = rms_normalize(key_unnormed)
    query_rows = (
        rotary_apply(query_unit * query_factor, cosine_table, sine_values)
        .astype(jnp.bfloat16)
        .reshape(block_rows, heads_key, group_width, HEAD_SIZE)
    )
    keys_rot = rotary_apply(key_unit * key_factor, cosine_table, sine_values).astype(jnp.bfloat16)
    score_scale = HEAD_SIZE ** (-0.5)
    allowed = (position[None, :] <= position[:, None]) & token_live[None, :]

    def score_block():
        raw_scores = (
            jnp.einsum("ikrd,jkd->krij", query_rows, keys_rot, preferred_element_type=jnp.float32)
            * score_scale
        )
        return jnp.where(allowed, raw_scores, masked_score)

    scores = score_block()
    row_peak = jnp.max(scores, axis=-1, keepdims=True)
    log_total = row_peak + jnp.log(jnp.sum(jnp.exp(scores - row_peak), axis=-1, keepdims=True))
    soft_probs = jnp.exp(scores - log_total)
    context = jnp.einsum(
        "krij,jkd->ikrd",
        soft_probs.astype(jnp.bfloat16),
        value_rows,
        preferred_element_type=jnp.float32,
    )
    context = context.reshape(block_rows, heads_query * HEAD_SIZE).astype(jnp.bfloat16)
    attention = lax.psum(matrix_product(context, context_all), "tensor")
    residual = stream + attention
    unit_second, scale_second = rms_normalize(residual)
    normed_second = (unit_second * gain_two).astype(jnp.bfloat16)
    logits = matrix_product(normed_second, router_all)
    expert_ids = jnp.arange(expert_count, dtype=jnp.int32)
    route_hot = routes[:, :, None] == expert_ids[None, None, :]
    chosen = jnp.sum(jnp.where(route_hot, logits[:, None, :], 0.0), axis=-1)
    gate_weights = jax.nn.softmax(chosen, axis=-1)
    pair_expert = routes.reshape(-1)
    pair_live = jnp.repeat(token_live, TOP)
    pair_hot = ((pair_expert[:, None] == expert_ids[None, :]) & pair_live[:, None]).astype(
        jnp.int32
    )
    running = jnp.cumsum(pair_hot, axis=0)
    pair_rank = jnp.sum((running - pair_hot) * pair_hot, axis=1)
    counts = running[-1]
    earlier = carried_in(
        counts, "dp", lambda former, latter: former + latter, jnp.zeros_like(counts)
    )
    pair_slot = jnp.sum(earlier[None, :] * pair_hot, axis=1) + pair_rank
    pair_kept = pair_live & (pair_slot < capacity)
    local_expert = pair_expert % EXP_DEV
    owner_index = pair_expert // EXP_DEV
    buffer_index = (local_expert * dp_count + owner_index) * most_rows + pair_rank
    target = jnp.where(pair_kept, buffer_index, slot_total)
    pair_ids = jnp.arange(block_rows * TOP, dtype=jnp.int32)
    slot_pair = jnp.full((slot_total,), -1, dtype=jnp.int32).at[target].set(pair_ids, mode="drop")
    slot_used = slot_pair >= 0
    slot_safe = jnp.maximum(slot_pair, 0)
    slot_token = slot_safe // TOP
    bf_zero = jnp.zeros((), jnp.bfloat16)
    send_rows = jnp.where(slot_used[:, None], normed_second[slot_token], bf_zero)
    layout = (EXP_DEV, dp_count, most_rows, features)
    received = to_owners(send_rows.reshape(layout)).reshape(EXP_DEV, dp_count * most_rows, features)
    gate_pre = jnp.einsum("end,edf->enf", received, expert_gate, preferred_element_type=jnp.float32)
    up_pre = jnp.einsum("end,edf->enf", received, expert_up, preferred_element_type=jnp.float32)
    sigmoid_gate = jax.nn.sigmoid(gate_pre)
    gate_act = gate_pre * sigmoid_gate
    hidden = (gate_act * up_pre).astype(jnp.bfloat16)
    out_partial = jnp.einsum(
        "enf,efd->end", hidden, expert_down, preferred_element_type=jnp.float32
    )
    expert_out = owner_reduce(out_partial)
    width = expert_out.shape[2]
    returned = lax.all_to_all(
        expert_out.reshape(EXP_DEV, dp_count, most_rows, width),
        "dp",
        split_axis=1,
        concat_axis=1,
        tiled=True,
    ).reshape(slot_total, width)
    pair_place = jnp.where(pair_kept, buffer_index, 0)
    pair_out = jnp.where(pair_kept[:, None], returned[pair_place], bf_zero).reshape(
        block_rows, TOP, width
    )
    expert_part = jnp.sum(gate_weights[:, :, None] * pair_out, axis=1)
    cot_full = cot_rows.astype(jnp.float32)
    own_start = tensor_index * own_rows
    gate_part = jnp.sum(cot_full[:, None, :] * pair_out, axis=-1)
    expert_own = lax.dynamic_slice_in_dim(expert_part, own_start, own_rows, 0)
    residual_own = lax.dynamic_slice_in_dim(residual, own_start, own_rows, 0)
    layer_output = (residual_own + expert_own).astype(jnp.bfloat16)
    slot_gate = jnp.where(slot_used, gate_weights.reshape(-1)[slot_safe], 0.0)
    send_cot = (slot_gate[:, None] * cot_full[slot_token]).astype(jnp.bfloat16)
    expert_cot = to_owners(send_cot.reshape(layout)).reshape(
        EXP_DEV, dp_count * most_rows, features
    )
    hidden_cot = jnp.einsum(
        "end,efd->enf", expert_cot, expert_down, preferred_element_type=jnp.float32
    )
    gating_cot = (
        hidden_cot * up_pre * sigmoid_gate * (1.0 + gate_pre * (1.0 - sigmoid_gate))
    ).astype(jnp.bfloat16)
    upward_cot = (hidden_cot * gate_act).astype(jnp.bfloat16)
    down_gradient = jnp.einsum(
        "enf,end->efd", hidden, expert_cot, preferred_element_type=jnp.float32
    )
    gate_gradient = jnp.einsum(
        "end,enf->edf", received, gating_cot, preferred_element_type=jnp.float32
    )
    up_gradient = jnp.einsum(
        "end,enf->edf", received, upward_cot, preferred_element_type=jnp.float32
    )
    row_partial = jnp.einsum(
        "enf,edf->end", gating_cot, expert_gate, preferred_element_type=jnp.float32
    )
    row_partial = row_partial + jnp.einsum(
        "enf,edf->end", upward_cot, expert_up, preferred_element_type=jnp.float32
    )
    row_cot = owner_reduce(row_partial)
    row_back = lax.all_to_all(
        row_cot.reshape(EXP_DEV, dp_count, most_rows, width),
        "dp",
        split_axis=1,
        concat_axis=1,
        tiled=True,
    ).reshape(slot_total, width)
    pair_cot = jnp.where(pair_kept[:, None], row_back[pair_place], bf_zero).reshape(
        block_rows, TOP, width
    )
    normed_part = jnp.sum(pair_cot.astype(jnp.float32), axis=1)
    normed_cot = normed_part
    route_cot = gate_weights * (
        gate_part - jnp.sum(gate_weights * gate_part, axis=-1, keepdims=True)
    )
    logit_cot = jnp.sum(jnp.where(route_hot, route_cot[:, :, None], 0.0), axis=1).astype(
        jnp.bfloat16
    )
    router_gradient = contract(normed_second, logit_cot)
    normed_cot = normed_cot + transposed(logit_cot, router_all)
    midnorm_gradient = jnp.sum(normed_cot * unit_second, axis=0)
    residual_cot = cot_full + norm_back(normed_cot * gain_two, unit_second, scale_second)
    attention_cot = residual_cot.astype(jnp.bfloat16)
    context_gradient = contract(context, attention_cot)
    context_cot = (
        transposed(attention_cot, context_all)
        .astype(jnp.bfloat16)
        .reshape(block_rows, heads_key, group_width, HEAD_SIZE)
    )
    scores = score_block()
    soft_probs = jnp.exp(scores - log_total)
    prob_cot = jnp.einsum(
        "ikrd,jkd->krij", context_cot, value_rows, preferred_element_type=jnp.float32
    )
    score_cot = (
        soft_probs * (prob_cot - jnp.sum(soft_probs * prob_cot, axis=-1, keepdims=True))
    ).astype(jnp.bfloat16)
    value_cot = jnp.einsum(
        "krij,ikrd->jkd",
        soft_probs.astype(jnp.bfloat16),
        context_cot,
        preferred_element_type=jnp.float32,
    )
    value_cot = value_cot.astype(jnp.bfloat16).reshape(block_rows, heads_key * HEAD_SIZE)
    query_turned = (
        jnp.einsum(
            "krij,jkd->ikrd", score_cot, keys_rot, preferred_element_type=jnp.float32
        ).reshape(block_rows, heads_query, HEAD_SIZE)
        * score_scale
    )
    key_turned = (
        jnp.einsum("krij,ikrd->jkd", score_cot, query_rows, preferred_element_type=jnp.float32)
        * score_scale
    )
    query_back = rotary_apply(query_turned, cosine_table, -sine_values)
    key_back = rotary_apply(key_turned, cosine_table, -sine_values)
    querynorm_part = jnp.sum(query_back * query_unit, axis=(0, 1))
    keynorm_part = jnp.sum(key_back * key_unit, axis=(0, 1))
    query_raw_cot = (
        norm_back(query_back * query_factor, query_unit, query_scale)
        .astype(jnp.bfloat16)
        .reshape(block_rows, heads_query * HEAD_SIZE)
    )
    key_raw_cot = (
        norm_back(key_back * key_factor, key_unit, key_scale)
        .astype(jnp.bfloat16)
        .reshape(block_rows, heads_key * HEAD_SIZE)
    )
    query_gradient = contract(first_layer_normed, query_raw_cot)
    key_gradient = contract(first_layer_normed, key_raw_cot)
    value_gradient = contract(first_layer_normed, value_cot)
    first_part = (
        transposed(query_raw_cot, query_all)
        + transposed(key_raw_cot, key_all)
        + transposed(value_cot, value_all)
    )
    first_cot, querynorm_gradient, keynorm_gradient = (
        lax.psum(first_part.astype(jnp.bfloat16), "tensor").astype(jnp.float32),
        lax.psum(querynorm_part.astype(jnp.bfloat16), "tensor").astype(jnp.float32),
        lax.psum(keynorm_part.astype(jnp.bfloat16), "tensor").astype(jnp.float32),
    )
    prenorm_gradient = jnp.sum(first_cot * unit_first, axis=0)
    input_cot = residual_cot + norm_back(first_cot * gain_one, unit_first, scale_first)
    input_gradient = lax.dynamic_slice_in_dim(input_cot, own_start, own_rows, 0).astype(
        jnp.bfloat16
    )
    summed = (
        lax.psum_scatter(query_gradient, "dp", scatter_dimension=0, tiled=True),
        lax.psum_scatter(key_gradient, "dp", scatter_dimension=0, tiled=True),
        lax.psum_scatter(value_gradient, "dp", scatter_dimension=0, tiled=True),
        lax.psum_scatter(context_gradient, "dp", scatter_dimension=1, tiled=True),
        lax.psum_scatter(router_gradient, "dp", scatter_dimension=0, tiled=True),
        lax.psum_scatter(prenorm_gradient, "dp", scatter_dimension=0, tiled=True),
        lax.psum_scatter(midnorm_gradient, "dp", scatter_dimension=0, tiled=True),
        lax.psum_scatter(querynorm_gradient, "dp", scatter_dimension=0, tiled=True),
        lax.psum_scatter(keynorm_gradient, "dp", scatter_dimension=0, tiled=True),
    )
    return (
        layer_output,
        input_gradient,
        summed[0],
        summed[1],
        summed[2],
        summed[3],
        summed[4],
        gate_gradient,
        up_gradient,
        down_gradient,
        summed[5],
        summed[6],
        summed[7],
        summed[8],
    )


AUX = 128


GRID_Z = 4
VMEM_LIMIT = 56 * 1024 * 1024


def remote(src, dst, send_sem, recv_sem, device):
    return pltpu.make_async_remote_copy(
        src_ref=src,
        dst_ref=dst,
        send_sem=send_sem,
        recv_sem=recv_sem,
        device_id=device,
        device_id_type=pl.DeviceIdType.MESH,
    )


class Place:
    def __init__(self):
        self.dp = lax.axis_index("dp")
        self.y = lax.axis_index("tensor")
        self.z = self.dp // 4
        self.x = (self.dp // 2) % 2
        self.core = self.dp % 2
        self.sibling = (self.dp + 1 - 2 * self.core, self.y)
        self.x_mate = (self.dp + 2 - 4 * self.x, self.y)
        self.y_mate = (self.dp, 1 - self.y)
        self.above = (self.dp + 4, self.y)
        self.below = (self.dp - 4, self.y)
        self.has_above = self.z < GRID_Z - 1
        self.has_below = self.z > 0

    def farthest(self, k):
        return (3 - 3 * (self.z // 2), (2 + 3 * self.z) % 5, 1 + self.z % 2, self.z)[k]

    def dp_at(self, z, flip_x, flip_core):
        x = self.x + flip_x * (1 - 2 * self.x)
        core = self.core + flip_core * (1 - 2 * self.core)
        return z * 4 + x * 2 + core

    def y_at(self, flip_y):
        return self.y + flip_y * (1 - 2 * self.y)

    def greet(self):
        barrier = pltpu.get_barrier_semaphore()
        for mate in (self.sibling, self.x_mate, self.y_mate):
            pl.semaphore_signal(barrier, 1, device_id=mate, device_id_type=pl.DeviceIdType.MESH)

        @pl.when(self.has_above)
        def _():
            pl.semaphore_signal(
                barrier, 1, device_id=self.above, device_id_type=pl.DeviceIdType.MESH
            )

        @pl.when(self.has_below)
        def _():
            pl.semaphore_signal(
                barrier, 1, device_id=self.below, device_id_type=pl.DeviceIdType.MESH
            )

        pl.semaphore_wait(barrier, 4 + self.z * (GRID_Z - 1 - self.z) // 2)


def add_rows(target, sources, rows, step=16):
    start, count = rows

    def one(i, carry):
        at = pl.ds(pl.multiple_of(start + i * step, step), step)
        total = target[at, :].astype(jnp.float32)
        for source, shift in sources:
            there = pl.ds(pl.multiple_of(start - shift + i * step, step), step)
            total = total + source[there, :].astype(jnp.float32)
        target[at, :] = total.astype(target.dtype)
        return carry

    lax.fori_loop(0, count // step, one, 0)


def line_onward(me, source, buffer, sem, to, side, mate):
    ends = 1 - (me.z - 1 - to + GRID_Z - 1) // GRID_Z
    slot = to if side == 0 else to + (GRID_Z - to) * ends
    return remote(source, buffer.at[slot], sem.at[0, to], sem.at[1, slot], mate)


def line_sum(me, k, block, source, rows, buffer, sem, shift):
    to = me.farthest(k)
    for side, ahead, mate, more in (
        (0, to > me.z, me.above, me.has_below),
        (1, to < me.z, me.below, me.has_above),
    ):
        slot = to if k < GRID_Z - 1 or side == 0 else GRID_Z
        came = remote(source, buffer.at[slot], sem.at[0, slot], sem.at[1, slot], mate)

        def gather(came=came, slot=slot):
            came.wait_recv()
            add_rows(block, [(buffer.at[slot], shift)], rows)

        if k < GRID_Z - 1:

            @pl.when(ahead)
            def _():
                pl.when(more)(gather)
                line_onward(me, source, buffer, sem, to, side, mate).start()
        else:
            pl.when(more)(gather)


def line_sent(me, k, source, buffer, sem):
    to = me.farthest(k)
    for side, ahead, mate in ((0, to > me.z, me.above), (1, to < me.z, me.below)):

        @pl.when(ahead)
        def _():
            line_onward(me, source, buffer, sem, to, side, mate).wait_send()


ROW_PLAN = (
    ("eda", 0), ("cz", 0, 1, 1), ("edb", 0), ("ey", 0), ("cz", 0, 0, 1), ("ex", 0), ("eda", 1),
    ("cz", 0, 0, 0), ("cz", 1, 0, 1), ("edb", 1), ("lx", 0), ("cz", 1, 1, 1), ("eda", 2),
    ("cz", 2, 1, 1), ("ly", 0), ("ly", 1), ("cz", 2, 0, 1), ("lx", 2), ("ex", 1), ("eda", 3),
    ("cz", 0, 1, 0), ("cz", 1, 1, 0), ("edb", 2), ("lx", 1), ("ey", 1), ("ey", 2), ("col", 0),
    ("edb", 3), ("cz", 2, 1, 0), ("cz", 1, 0, 0), ("cz", 3, 0, 1), ("cy", 0), ("cz", 3, 1, 1),
    ("ly", 2), ("ex", 2), ("col", 1), ("ly", 3), ("cz", 2, 0, 0), ("lx", 3), ("ex", 3),
    ("col", 2), ("cy", 1), ("ey", 3), ("cz", 3, 0, 0), ("cz", 3, 1, 0), ("cx",), ("cend",),
    ("col", 3),
)


def row_scatter_kernel(
    part, out, own, core, diag_a, diag_b, from_x, from_y, from_z, c_z, c_y, c_x,
    load_s, core_s, diag_s, x_s, y_s, z_s, cz_s, cy_s, cx_s, out_s,
):
    me = Place()
    rows, third = own.shape[3], diag_a.shape[1]
    last = GRID_Z - 1
    spans = ((0, third), (third, third), (2 * third, rows - 2 * third))
    a_at, b_at, c_at = (pl.ds(*span) for span in spans)
    most, most_at = (0, 2 * third), pl.ds(0, 2 * third)
    loads, cores, here = {}, {}, set()

    def chunk(k, flip_x, flip_y, flip_core):
        return part.at[me.dp_at(me.farthest(k), flip_x, flip_core) * 2 + me.y_at(flip_y)]

    order = ((1, 1), (1, 0), (0, 1), (0, 0))
    for k in range(GRID_Z):
        for fx, fy in order:
            copy = pltpu.make_async_copy(
                chunk(k, fx, fy, 0), own.at[k, fx, fy], load_s.at[k, fx, fy]
            )
            copy.start()
            loads[k, fx, fy] = copy
    me.greet()
    for k in range(GRID_Z):
        for fx, fy in order:
            copy = remote(
                chunk(k, fx, fy, 1), core.at[k, fx, fy],
                core_s.at[0, k, fx, fy], core_s.at[1, k, fx, fy], me.sibling,
            )
            copy.start()
            cores[k, fx, fy] = copy

    def pieces(make):
        return [make(k) for k in range(GRID_Z)]

    da = pieces(lambda k: remote(own.at[k, 1, 1, a_at], diag_a.at[k], diag_s.at[0, k], diag_s.at[1, k], me.y_mate))
    db = pieces(lambda k: remote(own.at[k, 1, 1, b_at], diag_b.at[k], diag_s.at[2, k], diag_s.at[3, k], me.x_mate))
    xs = pieces(
        lambda k: [
            remote(own.at[k, 1, 0, at], from_x.at[k, at], x_s.at[0, k, h], x_s.at[1, k, h], me.x_mate)
            for h, at in enumerate((a_at, b_at))
        ]
    )
    ys = pieces(
        lambda k: [
            remote(own.at[k, 0, 1, at], from_y.at[k, at], y_s.at[0, k, h], y_s.at[1, k, h], me.y_mate)
            for h, at in enumerate((a_at, b_at))
        ]
    )
    cy = [
        remote(own.at[last, fx, 1, c_at], c_y.at[fx], cy_s.at[0, fx], cy_s.at[1, fx], me.y_mate)
        for fx in range(2)
    ]
    cx = remote(own.at[last, 1, 0, c_at], c_x, cx_s.at[0], cx_s.at[1], me.x_mate)

    def add(k, fx, fy, h, *more):
        if (k, fx, fy) not in here:
            here.add((k, fx, fy))
            loads[k, fx, fy].wait()
            cores[k, fx, fy].wait_recv()
        span = most if h is None else spans[h]
        add_rows(own.at[k, fx, fy], [(core.at[k, fx, fy], 0), *more], span)

    def diagonal_a(k):
        add(k, 1, 1, 0)
        da[k].start()

    def diagonal_b(k):
        add(k, 1, 1, 1)
        db[k].start()

    def early_x(k):
        add(k, 1, 0, 1)
        xs[k][1].start()

    def early_y(k):
        add(k, 0, 1, 0)
        ys[k][0].start()

    def late_x(k):
        da[k].wait_recv()
        add(k, 1, 0, 0, (diag_a.at[k], 0))
        xs[k][0].start()

    def late_y(k):
        db[k].wait_recv()
        add(k, 0, 1, 1, (diag_b.at[k], third))
        ys[k][1].start()

    def column(k):
        for h in range(2):
            xs[k][h].wait_recv()
            ys[k][h].wait_recv()
        add(k, 0, 0, None, (from_x.at[k], 0), (from_y.at[k], 0))
        block = own.at[k, 0, 0]
        line_sum(me, k, block, block.at[most_at], most, from_z, z_s, 0)

    def c_line(k, fx, fy):
        add(k, fx, fy, 2)
        block = own.at[k, fx, fy]
        line_sum(
            me, k, block, block.at[c_at], spans[2], c_z.at[fx, fy], cz_s.at[fx, fy], 2 * third
        )

    def c_over_x():
        cy[1].wait_recv()
        add_rows(own.at[last, 1, 0], [(c_y.at[1], 2 * third)], spans[2])
        cx.start()

    def c_end():
        cy[0].wait_recv()
        cx.wait_recv()
        add_rows(own.at[last, 0, 0], [(c_y.at[0], 2 * third), (c_x, 2 * third)], spans[2])

    actions = {
        "eda": diagonal_a, "edb": diagonal_b, "ex": early_x, "ey": early_y, "lx": late_x,
        "ly": late_y, "col": column, "cz": c_line, "cy": lambda fx: cy[fx].start(),
        "cx": c_over_x, "cend": c_end,
    }
    for name, *which in ROW_PLAN:
        actions[name](*which)
    copy = pltpu.make_async_copy(own.at[last, 0, 0], out, out_s)
    copy.start()
    for k in range(GRID_Z):
        da[k].wait_send()
        db[k].wait_send()
        for h in range(2):
            xs[k][h].wait_send()
            ys[k][h].wait_send()
        if k < last:
            line_sent(me, k, own.at[k, 0, 0, most_at], from_z, z_s)
            for fx, fy in order:
                line_sent(me, k, own.at[k, fx, fy, c_at], c_z.at[fx, fy], cz_s.at[fx, fy])
    for sent in (*cores.values(), *cy, cx):
        sent.wait_send()
    copy.wait()


def scatter_all(value, collective_id):
    devices = lax.axis_size("dp") * lax.axis_size("tensor")
    rows, width = value.shape[0] // devices, value.shape[1]
    third = 3 * rows // 8
    dma = pltpu.SemaphoreType.DMA
    low = value.dtype
    shapes = (
        (4, 2, 2, rows), (4, 2, 2, rows), (4, third), (4, third), (4, 2 * third), (4, 2 * third),
        (5, 2 * third), (2, 2, 5, rows - 2 * third), (2, rows - 2 * third), (rows - 2 * third,),
    )
    return pl.pallas_call(
        row_scatter_kernel,
        out_shape=jax.ShapeDtypeStruct((rows, width), low),
        in_specs=[pl.BlockSpec(memory_space=pl.ANY)],
        out_specs=pl.BlockSpec(memory_space=pl.ANY),
        scratch_shapes=[
            *(pltpu.VMEM((*shape, width), low) for shape in shapes),
            dma((4, 2, 2)),
            dma((2, 4, 2, 2)),
            dma((4, 4)),
            dma((2, 4, 2)),
            dma((2, 4, 2)),
            dma((2, 5)),
            dma((2, 2, 2, 5)),
            dma((2, 2)),
            dma((2,)),
            dma(()),
        ],
        compiler_params=pltpu.CompilerParams(
            collective_id=collective_id, has_side_effects=True, vmem_limit_bytes=VMEM_LIMIT
        ),
    )(value.reshape(devices, rows, width))


WINDOW_ALIGN = 16
EXPERT_VMEM = 60 * 1024 * 1024


def dot(left, right, dims=((1,), (0,))):
    return lax.dot_general(left, right, (dims, ((), ())), preferred_element_type=jnp.float32)


def expert_kernel(
    info, pos, rows_in, cots_in, gate_w, up_w, down_w,
    out, back, gate_g, up_g, down_g,
    x, dy, wgu, wd, slot_out, slot_row, gu, hg, rows_b, cots_b, g_stage, d_stage,
    load_s, w_s, out_s, g_s, d_s,
):
    bf16, f32 = jnp.bfloat16, jnp.float32
    blocks, block_rows, wide = rows_in.shape
    features = cots_in.shape[2]
    experts, padded = x.shape[0], x.shape[1]
    part = hg.shape[2]
    cap = hg.shape[1]
    window = padded - cap
    tile = cap // 2
    chunk = d_stage.shape[2]

    def load(b):
        slot = b % 2
        return (
            pltpu.make_async_copy(rows_in.at[b], rows_b.at[slot], load_s.at[slot, 0]),
            pltpu.make_async_copy(cots_in.at[b], cots_b.at[slot], load_s.at[slot, 1]),
        )

    for copy in load(0):
        copy.start()
    weights = []
    for e in range(experts):
        weights.append(pltpu.make_async_copy(gate_w.at[e], wgu.at[e, :, pl.ds(0, part)], w_s.at[e, 0]))
        weights.append(pltpu.make_async_copy(up_w.at[e], wgu.at[e, :, pl.ds(part, part)], w_s.at[e, 1]))
        weights.append(pltpu.make_async_copy(down_w.at[e], wd.at[e], w_s.at[e, 2]))
    for copy in weights:
        copy.start()

    def clear(i, carry):
        at = pl.ds(pl.multiple_of(i * 16, 16), 16)
        for e in range(experts):
            x[e, at, :] = jnp.zeros((16, wide), bf16)
            dy[e, at, :] = jnp.zeros((16, features), bf16)
        return carry

    lax.fori_loop(0, padded // 16, clear, 0)
    for e in range(experts):
        slot_out[e, pl.ds(cap, window), :] = jnp.zeros((window, features), bf16)
        slot_row[e, pl.ds(cap, window), :] = jnp.zeros((window, wide), bf16)

    def starts(b):
        return [pl.multiple_of(info[1 + b * experts + e], WINDOW_ALIGN) for e in range(experts)]

    def picks(b, begin):
        slots = lax.broadcasted_iota(jnp.int32, (window, block_rows), 0)
        return jnp.concatenate(
            [(slots + begin[e] == pos[b, pl.ds(e, 1), :]).astype(f32) for e in range(experts)],
            axis=0,
        )

    def take(b, carry):
        slot = b % 2

        @pl.when(b + 1 < blocks)
        def _():
            for copy in load(b + 1):
                copy.start()

        begin = starts(b)
        picked = picks(b, begin).astype(bf16)
        for copy in load(b):
            copy.wait()
        for source, target, width in ((rows_b, x, wide), (cots_b, dy, features)):
            for first in range(0, width, chunk):
                cols = pl.ds(first, min(chunk, width - first))
                got = dot(picked, source[slot, :, cols]).astype(bf16)
                for e in range(experts):
                    first_at = pl.ds(begin[e], WINDOW_ALIGN)
                    rest_at = pl.ds(begin[e] + WINDOW_ALIGN, window - WINDOW_ALIGN)
                    split = e * window + WINDOW_ALIGN
                    target[e, first_at, cols] += got[e * window : split]
                    target[e, rest_at, cols] = got[split : (e + 1) * window]
        return carry

    lax.fori_loop(0, blocks, take, 0)
    for copy in weights:
        copy.wait()

    lanes = lax.broadcasted_iota(jnp.int32, (tile, AUX), 1)

    def mlp(step, carry):
        e = step // (cap // tile)
        at = pl.ds(pl.multiple_of((step % (cap // tile)) * tile, tile), tile)
        own = info[0] * experts + e
        total = blocks * experts
        aux = x[e, at, pl.ds(features, AUX)].astype(f32)
        gate = jnp.sum(
            jnp.where((lanes == own) | (lanes == own + total), aux, 0.0), axis=1, keepdims=True
        )
        pre = dot(x[e, at, pl.ds(0, features)], wgu[e])
        gate_pre, up_pre = pre[:, :part], pre[:, part:]
        sig = 1.0 / (1.0 + jnp.exp(-gate_pre))
        act = gate_pre * sig
        hidden = (act * up_pre).astype(bf16).astype(f32)
        gated = (hidden * gate).astype(bf16)
        hg[e, at, :] = gated
        down_cot = dot(dy[e, at, :], wd[e], ((1,), (1,)))
        slot_cot = jnp.sum(hidden * down_cot, axis=1, keepdims=True)
        hidden_cot = down_cot * gate
        gu[e, at, pl.ds(0, part)] = (
            hidden_cot * up_pre * sig * (1.0 + gate_pre * (1.0 - sig))
        ).astype(bf16)
        gu[e, at, pl.ds(part, part)] = (hidden_cot * act).astype(bf16)
        for first in range(0, features, chunk):
            cols = pl.ds(first, chunk)
            slot_out[e, at, cols] = dot(gated, wd[e, :, cols]).astype(bf16)
            slot_row[e, at, cols] = dot(
                gu[e, at, :], wgu[e, pl.ds(first, chunk), :], ((1,), (1,))
            ).astype(bf16)
        high = slot_cot.astype(bf16).astype(f32)
        place = info[1 + blocks * experts] * 2 * total + own * 2
        slot_row[e, at, pl.ds(features, AUX)] = jnp.where(
            lanes == place, high, jnp.where(lanes == place + 1, slot_cot - high, 0.0)
        ).astype(bf16)
        return carry

    lax.fori_loop(0, experts * (cap // tile), mlp, 0)

    def stored(b):
        slot = b % 2
        return (
            pltpu.make_async_copy(cots_b.at[slot], out.at[b], out_s.at[slot, 0]),
            pltpu.make_async_copy(rows_b.at[slot], back.at[b], out_s.at[slot, 1]),
        )

    def put(b, carry):
        slot = b % 2

        @pl.when(b >= 2)
        def _():
            for copy in stored(b - 2):
                copy.wait()

        begin = starts(b)
        spread = picks(b, begin).T.astype(bf16)
        for source, target, width in ((slot_out, cots_b, features), (slot_row, rows_b, wide)):
            for first in range(0, width, chunk):
                cols = pl.ds(first, min(chunk, width - first))
                held = jnp.concatenate(
                    [source[e, pl.ds(begin[e], window), cols] for e in range(experts)], axis=0
                )
                target[slot, :, cols] = dot(spread, held).astype(bf16)
        for copy in stored(b):
            copy.start()
        return carry

    lax.fori_loop(0, blocks, put, 0)

    tile = g_stage.shape[1]
    tiles = features // tile

    def g_copies(step):
        slot = step % 2
        e, at = step // tiles, pl.ds(pl.multiple_of((step % tiles) * tile, tile), tile)
        return (
            pltpu.make_async_copy(g_stage.at[slot, :, pl.ds(0, part)], gate_g.at[e, at], g_s.at[slot, 0]),
            pltpu.make_async_copy(g_stage.at[slot, :, pl.ds(part, part)], up_g.at[e, at], g_s.at[slot, 1]),
        )

    def wide_grad(step, carry):
        slot = step % 2
        e, at = step // tiles, pl.ds(pl.multiple_of((step % tiles) * tile, tile), tile)

        @pl.when(step >= 2)
        def _():
            for copy in g_copies(step - 2):
                copy.wait()

        g_stage[slot] = dot(x[e, pl.ds(0, cap), at], gu[e], ((0,), (0,)))
        for copy in g_copies(step):
            copy.start()
        return carry

    lax.fori_loop(0, experts * tiles, wide_grad, 0)
    parts = features // chunk

    def d_copy(step):
        slot = step % 2
        e, at = step // parts, pl.ds(pl.multiple_of((step % parts) * chunk, chunk), chunk)
        return pltpu.make_async_copy(d_stage.at[slot], down_g.at[e, :, at], d_s.at[slot])

    def down_grad(step, carry):
        slot = step % 2
        e, at = step // parts, pl.ds(pl.multiple_of((step % parts) * chunk, chunk), chunk)

        @pl.when(step >= 2)
        def _():
            d_copy(step - 2).wait()

        d_stage[slot] = dot(hg[e], dy[e, pl.ds(0, cap), at], ((0,), (0,)))
        d_copy(step).start()
        return carry

    lax.fori_loop(0, experts * parts, down_grad, 0)
    for last in (2, 1):
        for copy in stored(blocks - last):
            copy.wait()
        for copy in g_copies(experts * tiles - last):
            copy.wait()
        d_copy(experts * parts - last).wait()


def expert_layer(info, pos, rows_in, cots_in, gate_w, up_w, down_w, capacity, most):
    bf16, f32 = jnp.bfloat16, jnp.float32
    blocks, block_rows, wide = rows_in.shape
    features = cots_in.shape[2]
    experts, part = gate_w.shape[0], gate_w.shape[2]
    padded = capacity + -(-most // WINDOW_ALIGN) * WINDOW_ALIGN + WINDOW_ALIGN
    dma = pltpu.SemaphoreType.DMA
    shape = jax.ShapeDtypeStruct
    anywhere = pl.BlockSpec(memory_space=pl.ANY)
    return pl.pallas_call(
        expert_kernel,
        out_shape=(
            shape((blocks, block_rows, features), bf16),
            shape((blocks, block_rows, wide), bf16),
            shape(gate_w.shape, f32),
            shape(up_w.shape, f32),
            shape(down_w.shape, f32),
        ),
        in_specs=[
            pl.BlockSpec(memory_space=pltpu.SMEM),
            pl.BlockSpec(memory_space=pltpu.VMEM),
        ]
        + [anywhere] * 5,
        out_specs=(anywhere,) * 5,
        scratch_shapes=[
            pltpu.VMEM((experts, padded, wide), bf16),
            pltpu.VMEM((experts, padded, features), bf16),
            pltpu.VMEM((experts, features, 2 * part), bf16),
            pltpu.VMEM((experts, part, features), bf16),
            pltpu.VMEM((experts, padded, features), bf16),
            pltpu.VMEM((experts, padded, wide), bf16),
            pltpu.VMEM((experts, capacity, 2 * part), bf16),
            pltpu.VMEM((experts, capacity, part), bf16),
            pltpu.VMEM((2, block_rows, wide), bf16),
            pltpu.VMEM((2, block_rows, features), bf16),
            pltpu.VMEM((2, features // 2, 2 * part), f32),
            pltpu.VMEM((2, part, features // 2), f32),
            dma((2, 2)),
            dma((experts, 3)),
            dma((2, 2)),
            dma((2, 2)),
            dma((2,)),
        ],
        compiler_params=pltpu.CompilerParams(vmem_limit_bytes=EXPERT_VMEM),
    )(info, pos, rows_in, cots_in, gate_w, up_w, down_w)


ATTENTION_VMEM = 60 * 1024 * 1024
SCORE_SCALE = HEAD_SIZE ** (-0.5)
def turn_tables(rows):
    frequency = np.exp(
        -math.log(rope_base) * np.arange(HEAD_SIZE // 2, dtype=np.float32) * (2.0 / HEAD_SIZE)
    ).astype(np.float32)
    angles = np.arange(rows, dtype=np.float32)[:, None] * frequency[None, :]
    cosine, sine = np.cos(angles), np.sin(angles)
    return (
        np.concatenate([cosine, cosine], axis=1).astype(np.float32),
        np.concatenate([-sine, sine], axis=1).astype(np.float32),
    )


def turn(value, cosine, sine):
    return value * cosine + pltpu.roll(value, HEAD_SIZE // 2, 1) * sine


def inverse_norm(value):
    return lax.rsqrt(jnp.mean(value * value, axis=-1, keepdims=True) + epsilon)


def split_pair(me, both):
    half = both.shape[0] // 2
    first = me.y == 0
    lower, upper = both[:half], both[half:]
    return jnp.where(first, upper, lower), jnp.where(first, lower, upper)


def meet_y(me):
    barrier = pltpu.get_barrier_semaphore()
    pl.semaphore_signal(barrier, 1, device_id=me.y_mate, device_id_type=pl.DeviceIdType.MESH)
    pl.semaphore_wait(barrier, 1)


def gain_rows(aux_t, experts, chunks):
    head = [aux_t[experts + 2 + i : experts + 3 + i, :] for i in range(2)]
    width = HEAD_SIZE
    heads = [sum(row[:, c * width : (c + 1) * width] for c in range(chunks)) for row in head]
    return aux_t[experts : experts + 1, :], aux_t[experts + 1 : experts + 2, :], *heads


def probabilities(query, key, allowed):
    scores = jnp.where(allowed, dot(query, key, ((1,), (1,))) * SCORE_SCALE, masked_score)
    spread = jnp.exp(scores - jnp.max(scores, axis=-1, keepdims=True))
    return spread / jnp.sum(spread, axis=-1, keepdims=True)


def allowed_pairs(length, rows):
    later = lax.broadcasted_iota(jnp.int32, (rows, rows), 0)
    sooner = lax.broadcasted_iota(jnp.int32, (rows, rows), 1)
    return (sooner <= later) & (sooner < length)


def placed(count, offset):
    row = lax.broadcasted_iota(jnp.int32, (count, AUX), 0)
    return (row + offset == lax.broadcasted_iota(jnp.int32, (count, AUX), 1)).astype(jnp.bfloat16)


OPENING_PLAN = (
    ("w", 0, 0), ("a", 0), ("w", 1, 0), ("pair",), ("a", 1), ("b", 0, 0), ("w", 2, 0), ("a", 2),
    ("ax", 0), ("bx",), ("w", 3, 0), ("w", 0, 1), ("y1", 1, 0, 0), ("ax", 2), ("b", 0, 1),
    ("ax", 1), ("wx", 1, 0), ("b", 1, 1), ("ay0",), ("w", 1, 1), ("wx", 0, 0), ("b", 1, 0),
    ("wx", 2, 0), ("b", 2, 1), ("w", 2, 1), ("wx", 3, 0), ("y1", 1, 1, 0), ("prep",), ("qkv",),
    ("h", 0), ("y1", 1, 0, 1), ("b", 2, 0), ("w", 3, 1), ("y1", 0, 0, 1), ("h", 1), ("b", 3, 0),
    ("wx", 1, 1), ("h", 2), ("wx", 2, 1), ("a", 3), ("h", 3), ("wx", 0, 1), ("b", 3, 1),
    ("wx", 3, 1), ("ctx",), ("ax", 3), ("fin",), ("n", 0), ("y1", 0, 1, 0),
    ("y1", 1, 1, 1), ("c0",), ("n", 1), ("n", 2), ("c1",), ("n", 3), ("nx", 1), ("c2", 0),
    ("cz", 1, 1, 0), ("nx", 0), ("c2", 1), ("cz", 1, 1, 1), ("ny", 1), ("ny", 2),
    ("cz", 2, 1, 0), ("cz", 1, 0, 0), ("y1", 2, 0, 1), ("ny", 3), ("y1", 0, 1, 1),
    ("y1", 3, 1, 0), ("y1", 2, 1, 0), ("ny", 0), ("nx", 3), ("cz", 2, 1, 1), ("y1", 3, 0, 1),
    ("nx", 2), ("y1", 0, 0, 0), ("cz", 3, 1, 0), ("y1", 2, 0, 0), ("cz", 3, 1, 1),
    ("y1", 3, 0, 0), ("y1", 3, 1, 1), ("y1", 2, 1, 1), ("cz", 2, 0, 0), ("cz", 1, 0, 1),
    ("nca", 1), ("cz", 2, 0, 1), ("cz", 3, 0, 1), ("nca", 0), ("ncb", 2), ("ncb", 0),
    ("nca", 3), ("ncb", 1), ("ncb", 3), ("cz", 3, 0, 0), ("nca", 2),
)


def opening_kernel(
    experts, qkv,
    lengths, sequence_order, query_w, key_w, value_w, context_w, router_t, prenorm, midnorm,
    querynorm, keynorm, routes_t, d_src, x_src, cosine_in, sine_in,
    w_out, d_out, x_out,
    rows_o, sent_o, residual_o, normed_o, raw_o, query_o, key_o, value_o, context_o,
    x, w, ctx, aux_w, normed, raw, query, key, value, context, att, got, residual, sent,
    local_s, pair_s, wz_s, wx_s, wc_s, az_s, ax_s, ay_s, bz_s, bx_s, by_s, dc_s,
    in_s, w_s, out_s, y_s,
    w_src, flat_ctx, flat_router, flat_gains, head_gains, flat_routes, cosine, sine, load_s,
    nl_s, nz_s, nx_s, ny_s, ndx_s, ndy_s, nc_s, cx_s, cy_s, cz_s, cc_s,
):
    bf16, f32 = jnp.bfloat16, jnp.float32
    me = Place()
    half = d_src.shape[0] // 2
    low, high = pl.ds(0, half), pl.ds(half, half)
    width = w_src.shape[1]
    first_cols = qkv + AUX
    columns = (pl.ds(0, first_cols), pl.ds(first_cols, width - first_cols))
    waits, sent_on = [], []

    def near(k):
        return me.farthest(GRID_Z - 1 - k)

    def w_at(k, fx, p):
        return w_out.at[me.dp_at(near(k), fx, 0), :, columns[p]]

    def d_at(k, fx, fy, rows):
        return d_out.at[me.dp_at(near(k), fx, 0) * 2 + me.y_at(fy), rows]

    wide, narrow = query_w.shape[1], key_w.shape[1]
    loads = [
        pltpu.make_async_copy(source, target, load_s.at[i])
        for i, (source, target) in enumerate(
            (
                (context_w, flat_ctx),
                (router_t, flat_router),
                (prenorm, flat_gains.at[0]),
                (midnorm, flat_gains.at[1]),
                (querynorm, head_gains.at[0]),
                (keynorm, head_gains.at[1]),
                (routes_t, flat_routes),
                (query_w, w_src.at[:, pl.ds(0, wide)]),
                (key_w, w_src.at[:, pl.ds(wide, narrow)]),
                (value_w, w_src.at[:, pl.ds(wide + narrow, narrow)]),
                (cosine_in, cosine),
                (sine_in, sine),
            )
        )
    ]
    for copy in loads:
        copy.start()
    for copy in loads[:7]:
        copy.wait()
    count = head_gains.shape[2]
    top, block_rows = flat_routes.shape
    w_src[:, pl.ds(first_cols, width - first_cols)] = flat_ctx[...].astype(f32).T.astype(bf16)
    gains = jnp.concatenate(
        [
            flat_gains[0].astype(f32),
            flat_gains[1].astype(f32),
            dot(head_gains[0], placed(count, me.dp * count)),
            dot(head_gains[1], placed(count, me.dp * count)),
            jnp.zeros((4, AUX), f32),
        ],
        axis=0,
    ).T.astype(bf16)
    aux = dot(flat_router[...].astype(f32).T.astype(bf16), placed(experts, 0))
    aux = aux + dot(gains, placed(8, experts))
    for part in range(block_rows // AUX):
        some = flat_routes[:, part * AUX : (part + 1) * AUX].astype(f32).T.astype(bf16)
        aux = aux + dot(some, placed(top, experts + 4 + part * top))
    w_src[:, pl.ds(qkv, AUX)] = aux.astype(bf16)
    for copy in loads[7:]:
        copy.wait()
    for i, (source, target) in enumerate(
        (
            (w_src, w_out.at[me.dp]),
            (d_src, d_out.at[me.dp * 2 + me.y]),
            (x_src, x_out.at[me.y]),
        )
    ):
        copy = pltpu.make_async_copy(source, target, local_s.at[i])
        copy.start()
        waits.append(copy)
    me.greet()

    def line(k, source, target, sem, start_only):
        zn = near(k)
        for side, came, more, mate in (
            (0, zn < me.z, me.has_above, me.above),
            (1, zn > me.z, me.has_below, me.below),
        ):
            copy = remote(source, target, sem.at[0, side, zn], sem.at[1, side, zn], mate)
            if start_only:

                @pl.when(more)
                def _():
                    copy.start()
            else:

                @pl.when(came)
                def _():
                    copy.wait_recv()

                    @pl.when(more)
                    def _():
                        copy.start()

    def line_done(k, source, target, sem):
        zn = near(k)
        for side, came, more, mate in (
            (0, zn <= me.z, me.has_above, me.above),
            (1, zn >= me.z, me.has_below, me.below),
        ):
            copy = remote(source, target, sem.at[0, side, zn], sem.at[1, side, zn], mate)

            @pl.when(came)
            def _():
                @pl.when(more)
                def _():
                    copy.wait_send()

    def w_source(k, p):
        return w_src.at[:, columns[p]] if k == 0 else w_at(k, 0, p)

    def d_source(k, rows):
        return d_src.at[rows] if k == 0 else d_at(k, 0, 0, rows)

    def go(source, target, sem, index, mate):
        copy = remote(source, target, sem.at[(0, *index)], sem.at[(1, *index)], mate)
        copy.start()
        sent_on.append(copy)
        return copy

    def to_core(source, target, sem, index):
        go(source, target, sem, index, me.sibling)

    wx, ax, ay, by = {}, {}, {}, {}

    def w_own(k, p):
        line(k, w_source(k, p), w_at(k, 0, p), wz_s.at[p], k == 0)
        wx[k, p] = go(w_source(k, p), w_at(k, 0, p), wx_s, (k, p), me.x_mate)
        to_core(w_source(k, p), w_at(k, 0, p), wc_s, (k, 0, p))

    def w_across(k, p):
        wx[k, p].wait_recv()
        to_core(w_at(k, 1, p), w_at(k, 1, p), wc_s, (k, 1, p))

    def w_from_core(k, p):
        for fx in range(2):
            block = w_at(k, fx, p)
            remote(block, block, wc_s.at[0, k, fx, p], wc_s.at[1, k, fx, p], me.sibling).wait_recv()

    def a_over_y(k):
        ay[k, 0] = go(d_source(k, low), d_at(k, 0, 0, low), ay_s, (k, 0), me.y_mate)

    def a_own(k):
        line(k, d_source(k, low), d_at(k, 0, 0, low), az_s, k == 0)
        if k:
            a_over_y(k)
        ax[k] = go(d_source(k, low), d_at(k, 0, 0, low), ax_s, (k,), me.x_mate)
        to_core(d_source(k, low), d_at(k, 0, 0, low), dc_s, (k, 0, 0, 0))

    def a_across(k):
        ax[k].wait_recv()
        block = d_at(k, 1, 0, low)
        ay[k, 1] = go(block, block, ay_s, (k, 1), me.y_mate)
        to_core(block, block, dc_s, (k, 1, 0, 0))

    def b_own(k, fx):
        source = d_source(k, high) if fx == 0 else d_at(k, 1, 0, high)
        block = d_at(k, fx, 0, high)
        line(k, source, block, bz_s.at[fx], k == 0)
        by[k, fx] = go(source, block, by_s, (k, fx), me.y_mate)
        to_core(source, block, dc_s, (k, fx, 0, 1))

    def y_done(k, fx, h):
        (ay, by)[h][k, fx].wait_recv()
        block = d_at(k, fx, 1, (low, high)[h])
        to_core(block, block, dc_s, (k, fx, 1, h))

    rows, features = x.shape[0] * x.shape[1], x.shape[2]
    own_rows = rows // 2
    heads, key_heads = query.shape[0], key.shape[0]
    chunk = 512
    turn_c, turn_s = cosine[...], sine[...]
    held, outs, copies = {}, [], []

    def pair_rows():
        held["pair"] = go(x_src, x_out.at[me.y], pair_s, (0,), me.y_mate)

    def b_over_x():
        held["bx"] = go(d_src.at[high], d_at(0, 0, 0, high), bx_s, (0,), me.x_mate)

    def b_step(k, fx):
        if (k, fx) == (0, 1):
            held["bx"].wait_recv()
        b_own(k, fx)

    def prepare():
        held["pair"].wait_recv()
        waits[2].wait()
        for k in range(GRID_Z):
            w_from_core(k, 0)
        waits[0].wait()
        loads = [
            pltpu.make_async_copy(w_out.at[:, :, pl.ds(qkv, AUX)], aux_w, in_s.at[1]),
            pltpu.make_async_copy(x_out, x, in_s.at[0]),
        ]
        held["parts"] = [
            pltpu.make_async_copy(
                w_out.at[:, :, pl.ds(c * chunk, chunk)],
                w.at[:, :, pl.ds(c * chunk, chunk)],
                w_s.at[c],
            )
            for c in range(qkv // chunk)
        ]
        for copy in loads + held["parts"]:
            copy.start()
        loads[0].wait()
        aux_t = aux_w[...].reshape(features, AUX).astype(f32).T
        held["gains"] = gain_rows(aux_t, experts, features // HEAD_SIZE)
        gain_one = held["gains"][0]
        loads[1].wait()

        def one(i, carry):
            at = pl.ds(pl.multiple_of(i * 32, 32), 32)
            for part in range(2):
                stream = x[part, at, :].astype(f32)
                there = pl.ds(pl.multiple_of(part * own_rows + i * 32, 32), 32)
                normed[there, :] = (stream * inverse_norm(stream) * gain_one).astype(bf16)
            return carry

        lax.fori_loop(0, own_rows // 32, one, 0)

    def project():
        for c, copy in enumerate(held["parts"]):
            copy.wait()
            cols = slice(c * chunk, (c + 1) * chunk)
            got_raw = dot(normed[...], w[:, :, cols].reshape(features, chunk))
            for h in range(chunk // HEAD_SIZE):
                raw[c * (chunk // HEAD_SIZE) + h] = got_raw[:, h * HEAD_SIZE : (h + 1) * HEAD_SIZE]
        for g in range(key_heads):
            unnormed = raw[heads + g]
            gained = unnormed * inverse_norm(unnormed) * held["gains"][3]
            key[g] = turn(gained, turn_c, turn_s).astype(bf16)
            value[g] = raw[heads + key_heads + g].astype(bf16)

    def attend(part):
        allowed = allowed_pairs(lengths[sequence_order[me.dp]], rows)
        query_gain = held["gains"][2]

        def head(h, carry):
            g = h // (heads // key_heads)
            unnormed = raw[h]
            gained = unnormed * inverse_norm(unnormed) * query_gain
            turned = turn(gained, turn_c, turn_s).astype(bf16)
            query[h] = turned
            probs = probabilities(turned, key[g], allowed).astype(bf16)
            at = pl.ds(pl.multiple_of(h * HEAD_SIZE, HEAD_SIZE), HEAD_SIZE)
            context[:, at] = dot(probs, value[g]).astype(bf16)
            return carry

        share = heads // 4
        lax.fori_loop(part * share, (part + 1) * share, head, 0)

    def save(pairs):
        for source, target in pairs:
            copy = pltpu.make_async_copy(source, target, out_s.at[len(outs)])
            copy.start()
            outs.append(copy)

    def ctx_part(c):
        span = chunk // ctx.shape[1]
        return ctx[c * span : (c + 1) * span].reshape(chunk, ctx.shape[2])

    def output_over_y():
        save(
            (
                (normed, normed_o), (raw, raw_o), (query, query_o), (key, key_o),
                (value, value_o), (context, context_o),
            )
        )
        for k in range(GRID_Z):
            w_from_core(k, 1)
        load = pltpu.make_async_copy(w_out.at[:, :, columns[1]], ctx, in_s.at[2])
        load.start()
        load.wait()
        for c in range(features // chunk):
            cols = pl.ds(c * chunk, chunk)
            their_part, residual[:, cols] = split_pair(
                me, dot(context[...], ctx_part(c), ((1,), (1,)))
            )
            att[:, cols] = their_part.astype(bf16)
            copy = remote(att.at[:, cols], got.at[:, cols], y_s.at[0, c], y_s.at[1, c], me.y_mate)
            copy.start()
            copies.append(copy)

    def finish():
        for copy in copies:
            copy.wait_recv()
        gain_two = held["gains"][1]

        def second_norm(i, carry):
            at = pl.ds(pl.multiple_of(i * 16, 16), 16)
            total = x[me.y, at, :].astype(f32) + (residual[at, :] + got[at, :].astype(f32))
            residual[at, :] = total
            sent[at, pl.ds(0, features)] = (total * inverse_norm(total) * gain_two).astype(bf16)
            return carry

        lax.fori_loop(0, own_rows // 16, second_norm, 0)
        logits = dot(sent[:, :features], aux_w[...].reshape(features, AUX))
        own = flat_routes[:, pl.ds(pl.multiple_of(me.y * own_rows, own_rows), own_rows)]
        own = own.astype(f32).T
        lane = lax.broadcasted_iota(jnp.int32, (own_rows, AUX), 1).astype(f32)
        hits = [lane == own[:, j : j + 1] for j in range(top)]
        picked = functools.reduce(jnp.logical_or, hits)
        logits = jnp.where(picked, logits, masked_score)
        spread = jnp.where(picked, jnp.exp(logits - jnp.max(logits, axis=-1, keepdims=True)), 0.0)
        gates = spread / jnp.sum(spread, axis=-1, keepdims=True)
        coarse = gates.astype(bf16).astype(f32)
        sent[:, pl.ds(features, AUX)] = (coarse + pltpu.roll(gates - coarse, experts, 1)).astype(bf16)
        save(((sent, sent_o), (residual, residual_o)))

    third = 3 * own_rows // 8
    n_low, n_high = pl.ds(0, third), pl.ds(third, third)
    n_most, n_rest = pl.ds(0, 2 * third), pl.ds(2 * third, own_rows - 2 * third)
    nx, ny, ndx, ndy, cy = {}, {}, {}, {}, {}

    def n_at(k, fx, fy, rows):
        return rows_o.at[me.dp_at(near(k), fx, 0) * 2 + me.y_at(fy), rows]

    def n_source(k, rows):
        return sent.at[rows] if k == 0 else n_at(k, 0, 0, rows)

    def n_own(k):
        source, block = n_source(k, n_most), n_at(k, 0, 0, n_most)
        line(k, source, block, nz_s, k == 0)
        nx[k] = go(source, block, nx_s, (k,), me.x_mate)
        ny[k] = go(source, block, ny_s, (k,), me.y_mate)
        to_core(source, block, nc_s, (k, 0))
        if k == 0:
            copy = pltpu.make_async_copy(sent, rows_o.at[me.dp * 2 + me.y], nl_s.at[0])
            copy.start()
            outs.append(copy)

    def n_over_y(k):
        nx[k].wait_recv()
        block = n_at(k, 1, 0, n_low)
        ndy[k] = go(block, block, ndy_s, (k,), me.y_mate)
        block = n_at(k, 1, 0, n_most)
        to_core(block, block, nc_s, (k, 1))

    def n_over_x(k):
        ny[k].wait_recv()
        block = n_at(k, 0, 1, n_high)
        ndx[k] = go(block, block, ndx_s, (k,), me.x_mate)
        block = n_at(k, 0, 1, n_most)
        to_core(block, block, nc_s, (k, 2))

    def n_corner(k, copies, rows, index):
        copies[k].wait_recv()
        block = n_at(k, 1, 1, rows)
        to_core(block, block, nc_s, (k, index))

    def c_line(k, fx, fy, source=None):
        block = n_at(k, fx, fy, n_rest)
        source = block if source is None else source
        line(k, source, block, cz_s.at[fx, fy], k == 0)
        to_core(source, block, cc_s, (k, fx, fy))

    def c_own():
        source, block = sent.at[n_rest], n_at(0, 0, 0, n_rest)
        held["cx"] = go(source, block, cx_s, (0,), me.x_mate)
        cy[0] = go(source, block, cy_s, (0,), me.y_mate)
        c_line(0, 0, 0, source)

    def c_from_x():
        held["cx"].wait_recv()
        block = n_at(0, 1, 0, n_rest)
        cy[1] = go(block, block, cy_s, (1,), me.y_mate)
        c_line(0, 1, 0)

    def c_from_y(fx):
        cy[fx].wait_recv()
        c_line(0, fx, 1)

    actions = {
        "n": n_own, "nx": n_over_y, "ny": n_over_x,
        "nca": lambda k: n_corner(k, ndy, n_low, 3), "ncb": lambda k: n_corner(k, ndx, n_high, 4),
        "c0": c_own, "c1": c_from_x, "c2": c_from_y, "cz": c_line,
        "pair": pair_rows, "bx": b_over_x, "ay0": lambda: a_over_y(0), "w": w_own, "wx": w_across,
        "a": a_own, "ax": a_across, "b": b_step, "y1": y_done, "prep": prepare, "qkv": project,
        "h": attend, "ctx": output_over_y, "fin": finish,
    }
    for name, *which in OPENING_PLAN:
        actions[name](*which)
    for k in range(GRID_Z):
        for p in range(2):
            line_done(k, w_source(k, p), w_at(k, 0, p), wz_s.at[p])
        line_done(k, d_source(k, low), d_at(k, 0, 0, low), az_s)
        line_done(k, d_source(k, high), d_at(k, 0, 0, high), bz_s.at[0])
        line_done(k, d_at(k, 1, 0, high), d_at(k, 1, 0, high), bz_s.at[1])
        line_done(k, n_source(k, n_most), n_at(k, 0, 0, n_most), nz_s)
        for fx in range(2):
            for fy in range(2):
                source = n_source(k, n_rest) if (fx, fy) == (0, 0) else n_at(k, fx, fy, n_rest)
                line_done(k, source, n_at(k, fx, fy, n_rest), cz_s.at[fx, fy])
    for copy in sent_on + copies:
        copy.wait_send()
    for k in range(GRID_Z):
        for fx in range(2):
            for fy in range(2):
                for h, at in enumerate((low, high)):
                    block = d_at(k, fx, fy, at)
                    remote(
                        block, block, dc_s.at[0, k, fx, fy, h], dc_s.at[1, k, fx, fy, h], me.sibling
                    ).wait_recv()
            for fy in range(2):
                block = n_at(k, fx, fy, n_rest)
                remote(
                    block, block, cc_s.at[0, k, fx, fy], cc_s.at[1, k, fx, fy], me.sibling
                ).wait_recv()
        for i, (fx, fy, at) in enumerate(
            ((0, 0, n_most), (1, 0, n_most), (0, 1, n_most), (1, 1, n_low), (1, 1, n_high))
        ):
            block = n_at(k, fx, fy, at)
            remote(block, block, nc_s.at[0, k, i], nc_s.at[1, k, i], me.sibling).wait_recv()
    waits[1].wait()
    for copy in outs:
        copy.wait()


def opening(
    lengths, sequence_order, weights, gains, routes, cotangents, inputs, experts, collective_id
):
    bf16, f32 = jnp.bfloat16, jnp.float32
    chips, pair = lax.axis_size("dp"), lax.axis_size("tensor")
    own_rows, features = inputs.shape
    rows = pair * own_rows
    query, key, value, context, router = weights
    shard, wide = query.shape
    heads, key_heads = wide // HEAD_SIZE, key.shape[1] // HEAD_SIZE
    width = 2 * wide + 2 * key.shape[1] + AUX
    count, top = gains[2].shape[0], routes.shape[1]
    qkv = (heads + 2 * key_heads) * HEAD_SIZE
    cosine, sine = turn_tables(rows)
    dma = pltpu.SemaphoreType.DMA
    shapes = (
        ((chips, shard, width), bf16),
        ((chips * pair, *cotangents.shape), bf16),
        ((pair, *inputs.shape), bf16),
        ((chips * pair, own_rows, features + AUX), bf16),
        ((own_rows, features + AUX), bf16),
        ((own_rows, features), f32),
        ((rows, features), bf16),
        ((heads + 2 * key_heads, rows, HEAD_SIZE), f32),
        ((heads, rows, HEAD_SIZE), bf16),
        ((key_heads, rows, HEAD_SIZE), bf16),
        ((key_heads, rows, HEAD_SIZE), bf16),
        ((rows, wide), bf16),
    )
    anywhere, smem = pl.BlockSpec(memory_space=pl.ANY), pl.BlockSpec(memory_space=pltpu.SMEM)
    w, d, x, gathered, *rest = pl.pallas_call(
        functools.partial(opening_kernel, experts, qkv),
        out_shape=tuple(jax.ShapeDtypeStruct(*shape) for shape in shapes),
        in_specs=[smem] * 2 + [anywhere] * 14,
        out_specs=(anywhere,) * len(shapes),
        scratch_shapes=[
            pltpu.VMEM((pair, own_rows, features), bf16),
            pltpu.VMEM((chips, shard, qkv), bf16),
            pltpu.VMEM((chips, shard, wide), bf16),
            pltpu.VMEM((chips, shard, AUX), bf16),
            pltpu.VMEM((rows, features), bf16),
            pltpu.VMEM((heads + 2 * key_heads, rows, HEAD_SIZE), f32),
            pltpu.VMEM((heads, rows, HEAD_SIZE), bf16),
            pltpu.VMEM((key_heads, rows, HEAD_SIZE), bf16),
            pltpu.VMEM((key_heads, rows, HEAD_SIZE), bf16),
            pltpu.VMEM((rows, wide), bf16),
            pltpu.VMEM((own_rows, features), bf16),
            pltpu.VMEM((own_rows, features), bf16),
            pltpu.VMEM((own_rows, features), f32),
            pltpu.VMEM((own_rows, features + AUX), bf16),
            dma((3,)),
            dma((2, 1)),
            dma((2, 2, 2, 4)),
            dma((2, 4, 2)),
            dma((2, 4, 2, 2)),
            dma((2, 2, 4)),
            dma((2, 4)),
            dma((2, 4, 2)),
            dma((2, 2, 2, 4)),
            dma((2, 1)),
            dma((2, 4, 2)),
            dma((2, 4, 2, 2, 2)),
            dma((3,)),
            dma((qkv // 512,)),
            dma((8,)),
            dma((2, features // 512)),
            pltpu.VMEM((shard, width), bf16),
            pltpu.VMEM(context.shape, bf16),
            pltpu.VMEM((experts, shard), bf16),
            pltpu.VMEM((2, 1, shard), bf16),
            pltpu.VMEM((2, 1, count), bf16),
            pltpu.VMEM((top, rows), jnp.int32),
            pltpu.VMEM((rows, HEAD_SIZE), f32),
            pltpu.VMEM((rows, HEAD_SIZE), f32),
            dma((12,)),
            dma((1,)),
            dma((2, 2, 4)),
            dma((2, 4)),
            dma((2, 4)),
            dma((2, 4)),
            dma((2, 4)),
            dma((2, 4, 5)),
            dma((2, 1)),
            dma((2, 2)),
            dma((2, 2, 2, 2, 4)),
            dma((2, 4, 2, 2)),
        ],
        compiler_params=pltpu.CompilerParams(
            collective_id=collective_id, has_side_effects=True, vmem_limit_bytes=ATTENTION_VMEM
        ),
    )(
        lengths, sequence_order, query, key, value, context, router.T,
        *(gain[None] for gain in gains), routes.T, cotangents, inputs, cosine, sine,
    )
    return (
        w.reshape(-1, w.shape[2]),
        d.reshape(chips, -1, d.shape[2]),
        x.reshape(-1, x.shape[2]),
        gathered.reshape(chips, -1, gathered.shape[2]),
        *rest,
    )


def unturn(value, cosine, sine):
    return value * cosine - pltpu.roll(value, HEAD_SIZE // 2, 1) * sine


def backward_kernel(
    experts, lengths, sequence_order, back_in, residual_in, sent_in, dy_in, x_in, packed,
    cosine_in, sine_in, normed_in,
    raw_in, query_in, key_in, value_in, context_in,
    grads, input_gradient,
    back, residual, sent, dy, x, w, ctx, aux_w, normed, raw, query, key, value, context,
    cot, context_cot, raw_cot, key_sum, value_sum, small, first, first_got, stage, result,
    cosine, sine, probs, own_first, in_s, out_s, y_s, g_s,
):
    bf16, f32 = jnp.bfloat16, jnp.float32
    me = Place()
    own_rows, features = residual.shape
    rows = 2 * own_rows
    heads, key_heads = query.shape[0], key.shape[0]
    group = heads // key_heads
    qkv, wide = w.shape[1], heads * HEAD_SIZE
    chunk = 512
    loads = [
        pltpu.make_async_copy(source, target, in_s.at[i])
        for i, (source, target) in enumerate(
            (
                (packed.at[:, pl.ds(qkv, AUX)], aux_w),
                (back_in, back),
                (sent_in, sent),
                (residual_in, residual),
                (dy_in, dy),
                (packed.at[:, pl.ds(qkv + AUX, wide)], ctx),
                (context_in, context),
                (value_in, value),
                (key_in, key),
                (query_in, query),
                (raw_in, raw),
                (packed.at[:, pl.ds(0, qkv)], w),
                (normed_in, normed),
                (x_in, x),
                (cosine_in, cosine),
                (sine_in, sine),
            )
        )
    ]
    for copy in loads:
        copy.start()
    meet_y(me)
    for copy in loads[:5]:
        copy.wait()
    aux_t = aux_w[...].astype(f32).T
    gain_one, gain_two, query_gain, key_gain = gain_rows(aux_t, experts, features // HEAD_SIZE)

    lane = lax.broadcasted_iota(jnp.int32, (own_rows, AUX), 1)
    coded = sent[:, features:].astype(f32)
    gates = coded + pltpu.roll(coded, AUX - experts, 1)
    gates = jnp.where(lane < experts, gates, 0.0)
    column = lax.broadcasted_iota(jnp.int32, (AUX, AUX), 0)
    target = lax.broadcasted_iota(jnp.int32, (AUX, AUX), 1)
    fold = ((column % (2 * experts)) // 2 == target).astype(bf16)
    gate_cot = dot(back[:, features:], fold)
    logit_cot = gates * (gate_cot - jnp.sum(gates * gate_cot, axis=-1, keepdims=True))
    logit_cot = logit_cot.astype(bf16)
    small[...] = dot(sent[:, :features], logit_cot, ((0,), (0,)))
    midnorm = jnp.zeros((1, features), f32)
    step, swaps = 32, []
    for i in range(own_rows // step):
        at = slice(i * step, (i + 1) * step)
        total = residual[at, :]
        scale = inverse_norm(total)
        unit = total * scale
        normed_cot = back[at, :features].astype(f32) + dot(
            logit_cot[at, :], aux_w[...], ((1,), (1,))
        )
        midnorm = midnorm + jnp.sum(normed_cot * unit, axis=0, keepdims=True)
        gained = normed_cot * gain_two
        total_cot = dy[at, :].astype(f32) + scale * (
            gained - unit * jnp.mean(gained * unit, axis=-1, keepdims=True)
        )
        residual[at, :] = total_cot
        there = pl.ds(pl.multiple_of(me.y * own_rows + i * step, step), step)
        cot[there, :] = total_cot.astype(bf16)
        swap = remote(cot.at[there], cot.at[there], y_s.at[0, i], y_s.at[1, i], me.y_mate)
        swap.start()
        swaps.append(swap)
    for copy in loads[5:10]:
        copy.wait()

    allowed = allowed_pairs(lengths[sequence_order[me.dp]], rows)

    def recall(h, carry):
        probs[h] = probabilities(query[h], key[h // group], allowed)
        return carry

    lax.fori_loop(0, heads, recall, 0, unroll=2)
    for swap in swaps:
        swap.wait_recv()
    for c in range(wide // chunk):
        cols = pl.ds(c * chunk, chunk)
        context_cot[:, cols] = dot(cot[...], ctx[:, cols]).astype(bf16)
    for copy in loads[10:]:
        copy.wait()

    turn_c, turn_s = cosine[...], sine[...]
    key_sum[...] = jnp.zeros_like(key_sum)
    value_sum[...] = jnp.zeros_like(value_sum)

    def raw_back(back_rows, unnormed, gain):
        scale = inverse_norm(unnormed)
        unit = unnormed * scale
        part = jnp.sum(back_rows * unit, axis=0, keepdims=True)
        gained = back_rows * gain
        raw_rows = scale * (gained - unit * jnp.mean(gained * unit, axis=-1, keepdims=True))
        return raw_rows.astype(bf16), part

    def head(h, query_part):
        g = h // group
        at = pl.ds(pl.multiple_of(h * HEAD_SIZE, HEAD_SIZE), HEAD_SIZE)
        soft = probs[h]
        cots = context_cot[:, at]
        prob_cot = dot(cots, value[g], ((1,), (1,)))
        score_cot = soft * (prob_cot - jnp.sum(soft * prob_cot, axis=-1, keepdims=True))
        score_cot = score_cot.astype(bf16)
        value_sum[g] += dot(soft.astype(bf16), cots, ((0,), (0,)))
        key_sum[g] += dot(score_cot, query[h], ((0,), (0,)))
        turned = dot(score_cot, key[g]) * SCORE_SCALE
        raw_cot[:, at], part = raw_back(unturn(turned, turn_c, turn_s), raw[h], query_gain)
        return query_part + part

    query_part = lax.fori_loop(0, heads, head, jnp.zeros((1, HEAD_SIZE), f32), unroll=2)
    key_part = jnp.zeros((1, HEAD_SIZE), f32)
    for g in range(key_heads):
        turned = key_sum[g] * SCORE_SCALE
        at = wide + g * HEAD_SIZE
        raw_cot[:, at : at + HEAD_SIZE], part = raw_back(
            unturn(turned, turn_c, turn_s), raw[heads + g], key_gain
        )
        key_part = key_part + part
        at = at + key_heads * HEAD_SIZE
        raw_cot[:, at : at + HEAD_SIZE] = value_sum[g].astype(bf16)

    copies = []
    for c in range(features // chunk):
        cols = pl.ds(c * chunk, chunk)
        their_part, own_first[:, cols] = split_pair(
            me, dot(raw_cot[...], w[cols, :], ((1,), (1,)))
        )
        first[:, cols] = their_part.astype(bf16)
        copy = remote(
            first.at[:, cols], first_got.at[:, cols], y_s.at[0, len(swaps) + c], y_s.at[1, len(swaps) + c], me.y_mate
        )
        copy.start()
        copies.append(copy)
    block = stage.shape[1]

    def store(i):
        slot = i % 2
        return pltpu.make_async_copy(
            stage.at[slot],
            grads.at[pl.ds(pl.multiple_of(i * block, block), block), pl.ds(0, qkv + wide)],
            g_s.at[slot],
        )

    def weight_grads(i, carry):
        slot = i % 2
        at = pl.ds(pl.multiple_of(i * block, block), block)

        @pl.when(i >= 2)
        def _():
            store(i - 2).wait()

        normed_t = normed[:, at].astype(f32).T.astype(bf16)
        cot_t = cot[:, at].astype(f32).T.astype(bf16)
        for c in range(qkv // chunk):
            cols = pl.ds(c * chunk, chunk)
            stage[slot, :, cols] = dot(normed_t, raw_cot[:, cols]).astype(bf16)
        for c in range(wide // chunk):
            cols = pl.ds(c * chunk, chunk)
            stage[slot, :, pl.ds(qkv + c * chunk, chunk)] = dot(cot_t, context[:, cols]).astype(bf16)
        store(i).start()
        return carry

    lax.fori_loop(0, features // block, weight_grads, 0)
    prenorm = jnp.zeros((1, features), f32)
    for copy in copies:
        copy.wait_recv()
    for c in range(features // chunk):
        cols = pl.ds(c * chunk, chunk)
        result_part = own_first[:, cols] + first_got[:, cols].astype(f32)
        back[:, cols] = result_part.astype(bf16)
    step = 32
    for i in range(own_rows // step):
        at = slice(i * step, (i + 1) * step)
        stream = x[pl.ds(pl.multiple_of(me.y * own_rows + i * step, step), step), :].astype(f32)
        scale = inverse_norm(stream)
        unit = stream * scale
        first_cot = back[at, :features].astype(f32)
        prenorm = prenorm + jnp.sum(first_cot * unit, axis=0, keepdims=True)
        gained = first_cot * gain_one
        result[at, :] = (
            residual[at, :]
            + scale * (gained - unit * jnp.mean(gained * unit, axis=-1, keepdims=True))
        ).astype(bf16)
    done = pltpu.make_async_copy(result, input_gradient, out_s.at[0])
    done.start()
    chunks = features // HEAD_SIZE
    extra = jnp.concatenate(
        [
            jnp.zeros((experts, features), f32),
            prenorm,
            midnorm,
            jnp.concatenate([query_part] * chunks, axis=1),
            jnp.concatenate([key_part] * chunks, axis=1),
            jnp.zeros((AUX - experts - 4, features), f32),
        ],
        axis=0,
    )
    aux_w[...] = (small[...] + extra.T).astype(bf16)
    last = pltpu.make_async_copy(aux_w, grads.at[:, pl.ds(qkv + wide, AUX)], out_s.at[1])
    last.start()
    for swap in swaps:
        swap.wait_send()
    for copy in copies:
        copy.wait_send()
    for i in (2, 1):
        store(features // block - i).wait()
    done.wait()
    last.wait()


def attention_backward(
    lengths, sequence_order, back, residual, sent, dy, x_pair, packed, saved, experts, collective_id
):
    bf16, f32 = jnp.bfloat16, jnp.float32
    normed, raw, query, key, value, context = saved
    own_rows, features = residual.shape
    rows = 2 * own_rows
    heads, key_heads = query.shape[0], key.shape[0]
    wide = heads * HEAD_SIZE
    qkv = wide + 2 * key_heads * HEAD_SIZE
    cosine, sine = turn_tables(rows)
    dma = pltpu.SemaphoreType.DMA
    anywhere, smem = pl.BlockSpec(memory_space=pl.ANY), pl.BlockSpec(memory_space=pltpu.SMEM)
    return pl.pallas_call(
        functools.partial(backward_kernel, experts),
        out_shape=(
            jax.ShapeDtypeStruct((features, qkv + wide + AUX), bf16),
            jax.ShapeDtypeStruct((own_rows, features), bf16),
        ),
        in_specs=[smem] * 2 + [anywhere] * 14,
        out_specs=(anywhere,) * 2,
        scratch_shapes=[
            pltpu.VMEM((own_rows, features + AUX), bf16),
            pltpu.VMEM((own_rows, features), f32),
            pltpu.VMEM((own_rows, features + AUX), bf16),
            pltpu.VMEM((own_rows, features), bf16),
            pltpu.VMEM((rows, features), bf16),
            pltpu.VMEM((features, qkv), bf16),
            pltpu.VMEM((features, wide), bf16),
            pltpu.VMEM((features, AUX), bf16),
            pltpu.VMEM((rows, features), bf16),
            pltpu.VMEM((heads + 2 * key_heads, rows, HEAD_SIZE), f32),
            pltpu.VMEM((heads, rows, HEAD_SIZE), bf16),
            pltpu.VMEM((key_heads, rows, HEAD_SIZE), bf16),
            pltpu.VMEM((key_heads, rows, HEAD_SIZE), bf16),
            pltpu.VMEM((rows, wide), bf16),
            pltpu.VMEM((rows, features), bf16),
            pltpu.VMEM((rows, wide), bf16),
            pltpu.VMEM((rows, qkv), bf16),
            pltpu.VMEM((key_heads, rows, HEAD_SIZE), f32),
            pltpu.VMEM((key_heads, rows, HEAD_SIZE), f32),
            pltpu.VMEM((features, AUX), f32),
            pltpu.VMEM((own_rows, features), bf16),
            pltpu.VMEM((own_rows, features), bf16),
            pltpu.VMEM((2, 512, qkv + wide), bf16),
            pltpu.VMEM((own_rows, features), bf16),
            pltpu.VMEM((rows, HEAD_SIZE), f32),
            pltpu.VMEM((rows, HEAD_SIZE), f32),
            pltpu.VMEM((heads, rows, rows), f32),
            pltpu.VMEM((own_rows, features), f32),
            dma((16,)),
            dma((2,)),
            dma((2, own_rows // 32 + features // 512)),
            dma((2,)),
        ],
        compiler_params=pltpu.CompilerParams(
            collective_id=collective_id, has_side_effects=True, vmem_limit_bytes=ATTENTION_VMEM
        ),
    )(
        lengths, sequence_order, back, residual, sent, dy, x_pair, packed, cosine, sine,
        normed, raw, query, key, value, context,
    )


LAST_CUT = 5
LAST_PLAN = (
    ("gx", 0, 0), ("dy", 0, 1, 1), ("gx", 0, 1), ("dy", 0, 0, 1), ("dy", 1, 1, 1), ("db", 0, 1),
    ("gx", 1, 1), ("db", 0, 0), ("dy", 2, 1, 1), ("dy", 1, 1, 0), ("gx", 1, 0), ("db", 1, 1),
    ("dy", 2, 1, 0), ("gx", 2, 0), ("db", 2, 1), ("dy", 0, 1, 0), ("dy", 2, 0, 1),
    ("dy", 0, 0, 0), ("dy", 3, 1, 1), ("gc", 0), ("dy", 1, 0, 0), ("dy", 1, 0, 1),
    ("dy", 3, 1, 0), ("dy", 2, 0, 0), ("gx", 2, 1), ("dax", 2), ("dax", 0), ("dax", 1),
    ("gc", 1), ("gc", 2), ("gx", 3, 0), ("dy", 3, 0, 1), ("gx", 3, 1), ("da", 0), ("dax", 3),
    ("dy", 3, 0, 0), ("db", 1, 0), ("da", 1), ("db", 2, 0), ("da", 2), ("gc", 3), ("sm",),
    ("db", 3, 1), ("db", 3, 0), ("sm2",), ("da", 3), ("bx",),
)


def last_scatter_kernel(
    g_part, d_part, g_out, d_out,
    g_own, g_core, g_x, g_z, d_own, d_core, d_y, a_x, b_x, a_z, b_z, small_got,
    gl_s, gc_s, gx_s, gz_s, dl_s, dc_s, dy_s, ax_s, bx_s, az_s, bz_s, small_s, out_s,
):
    me = Place()
    g_rows, d_rows = g_own.shape[2], d_own.shape[3]
    cut, g_half = a_x.shape[1], g_rows // 2
    g_all, low, high = (0, g_rows), (0, cut), (cut, d_rows - cut)
    low_at, high_at = pl.ds(0, cut), pl.ds(cut, d_rows - cut)
    last = GRID_Z - 1
    loads, cores, sends = {}, {}, []

    def g_chunk(k, fx, fc):
        return g_part.at[me.dp_at(me.farthest(k), fx, fc)]

    def d_chunk(k, fx, fy, fc):
        return d_part.at[me.dp_at(me.farthest(k), fx, fc) * 2 + me.y_at(fy)]

    pairs = ((1, 1), (0, 1), (1, 0), (0, 0))
    for k in range(GRID_Z):
        for fx in (1, 0):
            loads[k, fx] = pltpu.make_async_copy(g_chunk(k, fx, 0), g_own.at[k, fx], gl_s.at[k, fx])
            loads[k, fx].start()
        for fx, fy in pairs:
            loads[k, fx, fy] = pltpu.make_async_copy(
                d_chunk(k, fx, fy, 0), d_own.at[k, fx, fy], dl_s.at[k, fx, fy]
            )
            loads[k, fx, fy].start()
    me.greet()
    for k in range(GRID_Z):
        for fx in (1, 0):
            cores[k, fx] = remote(
                g_chunk(k, fx, 1), g_core.at[k, fx],
                gc_s.at[0, k, fx], gc_s.at[1, k, fx], me.sibling,
            )
        for fx, fy in pairs:
            cores[k, fx, fy] = remote(
                d_chunk(k, fx, fy, 1), d_core.at[k, fx, fy],
                dc_s.at[0, k, fx, fy], dc_s.at[1, k, fx, fy], me.sibling,
            )
        for index in ((1,), (1, 1), (0, 1), (0,), (1, 0), (0, 0)):
            cores[(k, *index)].start()

    gx = [
        [
            remote(
                g_own.at[k, 1, pl.ds(h * g_half, g_half)], g_x.at[k, pl.ds(h * g_half, g_half)],
                gx_s.at[0, k, h], gx_s.at[1, k, h], me.x_mate,
            )
            for h in range(2)
        ]
        for k in range(GRID_Z)
    ]
    dy = {
        (k, fx, h): remote(
            d_own.at[k, fx, 1, at], d_y.at[k, fx, at],
            dy_s.at[0, k, fx, h], dy_s.at[1, k, fx, h], me.y_mate,
        )
        for k in range(GRID_Z)
        for fx in range(2)
        for h, at in enumerate((low_at, high_at))
    }
    ax = [
        remote(d_own.at[k, 1, 0, low_at], a_x.at[k], ax_s.at[0, k], ax_s.at[1, k], me.x_mate)
        for k in range(GRID_Z)
    ]
    bx = remote(d_own.at[last, 1, 0, high_at], b_x, bx_s.at[0], bx_s.at[1], me.x_mate)

    here = set()

    def arrive(*index):
        if index not in here:
            here.add(index)
            loads[index].wait()
            cores[index].wait_recv()

    def onward(source, buffer, sem, to, side, mate):
        ends = 1 - (me.z - 1 - to + GRID_Z - 1) // GRID_Z
        slot = to if side == 0 else to + (GRID_Z - to) * ends
        return remote(source, buffer.at[slot], sem.at[0, to], sem.at[1, slot], mate)

    def line(k, block, source, rows, buffer, sem, shift):
        to = me.farthest(k)
        for side, ahead, mate, more in (
            (0, to > me.z, me.above, me.has_below),
            (1, to < me.z, me.below, me.has_above),
        ):
            slot = to if k < last or side == 0 else GRID_Z
            came = remote(source, buffer.at[slot], sem.at[0, slot], sem.at[1, slot], mate)

            def gather(came=came, slot=slot):
                came.wait_recv()
                add_rows(block, [(buffer.at[slot], shift)], rows)

            if k < last:

                @pl.when(ahead)
                def _():
                    pl.when(more)(gather)
                    onward(source, buffer, sem, to, side, mate).start()
            else:
                pl.when(more)(gather)

    def line_done(k, source, buffer, sem):
        to = me.farthest(k)
        for side, ahead, mate in ((0, to > me.z, me.above), (1, to < me.z, me.below)):

            @pl.when(ahead)
            def _():
                onward(source, buffer, sem, to, side, mate).wait_send()

    width = g_own.shape[3]
    small_block = g_own.at[last, 0, :, pl.ds(width - AUX, AUX)]
    small = remote(small_block, small_got, small_s.at[0], small_s.at[1], me.y_mate)

    def g_across(k, h):
        arrive(k, 1)
        add_rows(g_own.at[k, 1], [(g_core.at[k, 1], 0)], (h * g_half, g_half))
        gx[k][h].start()

    def g_column(k):
        arrive(k, 0)
        for h in range(2):
            gx[k][h].wait_recv()
        add_rows(g_own.at[k, 0], [(g_core.at[k, 0], 0), (g_x.at[k], 0)], g_all)
        line(k, g_own.at[k, 0], g_own.at[k, 0], g_all, g_z, gz_s, 0)

    def over_y(k, fx, h):
        arrive(k, fx, 1)
        add_rows(d_own.at[k, fx, 1], [(d_core.at[k, fx, 1], 0)], (low, high)[h])
        dy[k, fx, h].start()

    def from_y(k, fx, h, *more):
        arrive(k, fx, 0)
        dy[k, fx, h].wait_recv()
        rest = [(d_core.at[k, fx, 0], 0), (d_y.at[k, fx], 0), *more]
        add_rows(d_own.at[k, fx, 0], rest, (low, high)[h])

    def b_line(k, fx):
        from_y(k, fx, 1)
        block = d_own.at[k, fx, 0]
        line(k, block, block.at[high_at], high, b_z.at[fx], bz_s.at[fx], cut)
        if fx and k == last:
            bx.start()

    def a_over_x(k):
        from_y(k, 1, 0)
        ax[k].start()

    def a_line(k):
        ax[k].wait_recv()
        from_y(k, 0, 0, (a_x.at[k], 0))
        block = d_own.at[k, 0, 0]
        line(k, block, block.at[low_at], low, a_z, az_s, 0)

    def b_from_x():
        bx.wait_recv()
        add_rows(d_own.at[last, 0, 0], [(b_x, cut)], high)

    def small_sum():
        small.wait()
        total = small_block[...].astype(jnp.float32) + small_got[...].astype(jnp.float32)
        small_block[...] = total.astype(small_got.dtype)

    actions = {
        "gx": g_across, "gc": g_column, "dy": over_y, "db": b_line, "dax": a_over_x, "da": a_line,
        "bx": b_from_x, "sm": small.start, "sm2": small_sum,
    }
    for name, *which in LAST_PLAN:
        actions[name](*which)
    outs = [
        pltpu.make_async_copy(d_own.at[last, 0, 0], d_out, out_s.at[0]),
        pltpu.make_async_copy(g_own.at[last, 0], g_out, out_s.at[1]),
    ]
    for copy in outs:
        copy.start()
    for k in range(GRID_Z):
        for h in range(2):
            gx[k][h].wait_send()
        for fx in range(2):
            for h in range(2):
                dy[k, fx, h].wait_send()
        ax[k].wait_send()
        if k < last:
            line_done(k, g_own.at[k, 0], g_z, gz_s)
            for fx in range(2):
                line_done(k, d_own.at[k, fx, 0, high_at], b_z.at[fx], bz_s.at[fx])
            line_done(k, d_own.at[k, 0, 0, low_at], a_z, az_s)
    bx.wait_send()
    for sent in cores.values():
        sent.wait_send()
    for copy in outs:
        copy.wait()


def last_scatter(grads, sums, collective_id):
    chips, pair = lax.axis_size("dp"), lax.axis_size("tensor")
    g_rows, g_wide = grads.shape[0] // chips, grads.shape[1]
    d_rows, d_wide = sums.shape[0] // (chips * pair), sums.shape[1]
    cut = d_rows * LAST_CUT // 8
    dma = pltpu.SemaphoreType.DMA
    low = grads.dtype
    anywhere = pl.BlockSpec(memory_space=pl.ANY)
    return pl.pallas_call(
        last_scatter_kernel,
        out_shape=(
            jax.ShapeDtypeStruct((g_rows, g_wide), low),
            jax.ShapeDtypeStruct((d_rows, d_wide), low),
        ),
        in_specs=[anywhere] * 2,
        out_specs=(anywhere,) * 2,
        scratch_shapes=[
            pltpu.VMEM((4, 2, g_rows, g_wide), low),
            pltpu.VMEM((4, 2, g_rows, g_wide), low),
            pltpu.VMEM((4, g_rows, g_wide), low),
            pltpu.VMEM((5, g_rows, g_wide), low),
            pltpu.VMEM((4, 2, 2, d_rows, d_wide), low),
            pltpu.VMEM((4, 2, 2, d_rows, d_wide), low),
            pltpu.VMEM((4, 2, d_rows, d_wide), low),
            pltpu.VMEM((4, cut, d_wide), low),
            pltpu.VMEM((d_rows - cut, d_wide), low),
            pltpu.VMEM((5, cut, d_wide), low),
            pltpu.VMEM((2, 5, d_rows - cut, d_wide), low),
            pltpu.VMEM((g_rows, AUX), low),
            dma((4, 2)),
            dma((2, 4, 2)),
            dma((2, 4, 2)),
            dma((2, 5)),
            dma((4, 2, 2)),
            dma((2, 4, 2, 2)),
            dma((2, 4, 2, 2)),
            dma((2, 4)),
            dma((2,)),
            dma((2, 5)),
            dma((2, 2, 5)),
            dma((2,)),
            dma((2,)),
        ],
        compiler_params=pltpu.CompilerParams(
            collective_id=collective_id, has_side_effects=True, vmem_limit_bytes=60 * 1024 * 1024
        ),
    )(grads.reshape(chips, g_rows, g_wide), sums.reshape(chips * pair, d_rows, d_wide))


def unpack_kernel(
    experts, summed, added, residual,
    layer_output, query, key, value, context, router, prenorm, midnorm, querynorm, keynorm,
):
    f32 = jnp.float32
    wide, narrow = query.shape[1], key.shape[1]
    layer_output[...] = (residual[...] + added[...].astype(f32)).astype(layer_output.dtype)
    query[...] = summed[:, pl.ds(0, wide)].astype(f32)
    key[...] = summed[:, pl.ds(wide, narrow)].astype(f32)
    value[...] = summed[:, pl.ds(wide + narrow, narrow)].astype(f32)
    start = wide + 2 * narrow
    context[...] = summed[:, pl.ds(start, wide)].astype(f32).T
    small = summed[:, pl.ds(start + wide, AUX)].astype(f32)
    router[...] = small[:, :experts]
    rows = small.T
    prenorm[...] = rows[experts : experts + 1, :]
    midnorm[...] = rows[experts + 1 : experts + 2, :]
    count = querynorm.shape[1]
    lane = lax.broadcasted_iota(jnp.int32, (count, AUX), 1)
    row = lax.broadcasted_iota(jnp.int32, (count, AUX), 0)
    pick = row + lax.axis_index("dp") * count == lane
    for target, at in ((querynorm, experts + 2), (keynorm, experts + 3)):
        part = jnp.where(pick, rows[at : at + 1, :], 0.0)
        target[...] = jnp.sum(part, axis=1, keepdims=True).T


def unpack(summed, added, residual, query_width, key_width, experts, norm_part):
    bf16, f32 = jnp.bfloat16, jnp.float32
    shard = summed.shape[0]
    own_rows, features = residual.shape
    shapes = (
        ((own_rows, features), bf16),
        ((shard, query_width), f32),
        ((shard, key_width), f32),
        ((shard, key_width), f32),
        ((query_width, shard), f32),
        ((shard, experts), f32),
        ((1, shard), f32),
        ((1, shard), f32),
        ((1, norm_part), f32),
        ((1, norm_part), f32),
    )
    vmem = pl.BlockSpec(memory_space=pltpu.VMEM)
    *large, first, second, third, fourth = pl.pallas_call(
        functools.partial(unpack_kernel, experts),
        out_shape=tuple(jax.ShapeDtypeStruct(*shape) for shape in shapes),
        in_specs=[vmem] * 3,
        out_specs=(vmem,) * len(shapes),
        compiler_params=pltpu.CompilerParams(vmem_limit_bytes=32 * 1024 * 1024),
    )(summed, added, residual)
    return (*large, first[0], second[0], third[0], fourth[0])


def gathered_body(
    layer_input,
    query_weight,
    key_projection,
    value_projection,
    context_weight,
    router_weight,
    expert_gate,
    expert_up,
    expert_down,
    prenorm_gain,
    midnorm_gain,
    querynorm_gain,
    keynorm_gain,
    routes,
    lengths,
    sequence_order,
    output_cotangent,
):
    bf16, f32 = jnp.bfloat16, jnp.float32
    tensor_count = lax.axis_size("tensor")
    tensor_index = lax.axis_index("tensor")
    dp_count = lax.axis_size("dp")
    dp_index = lax.axis_index("dp")
    own_rows, features = layer_input.shape
    block_rows = own_rows * tensor_count
    tokens = block_rows * dp_count
    expert_count = EXP_DEV * dp_count
    capacity = 3 * block_rows * TOP // (4 * EXP_DEV)
    most_rows = (5 * block_rows * TOP + 4 * expert_count - 1) // (4 * expert_count)
    shard = features // dp_count
    query_width = query_weight.shape[1]
    key_width = key_projection.shape[1]
    norm_part = HEAD_SIZE // dp_count

    packed, cot_all, input_rows, normed_all, sent, residual, *saved = opening(
        lengths,
        sequence_order,
        (query_weight, key_projection, value_projection, context_weight, router_weight),
        (prenorm_gain, midnorm_gain, querynorm_gain, keynorm_gain),
        routes,
        output_cotangent,
        layer_input,
        expert_count,
        0,
    )
    route_from = query_width + 2 * key_width + expert_count + 4
    routes_all = packed[:, route_from : route_from + 2 * TOP].astype(jnp.int32)
    routes_all = routes_all.reshape(dp_count, shard, 2, TOP).transpose(0, 3, 2, 1)
    routes_all = routes_all.reshape(dp_count, TOP, block_rows)
    position = jnp.arange(block_rows, dtype=jnp.int32)
    live = position[None, :] < lengths[sequence_order][:, None]

    expert_own = dp_index * EXP_DEV + jnp.arange(EXP_DEV, dtype=jnp.int32)
    hot = jnp.any(routes_all[:, None, :, :] == expert_own[None, :, None, None], axis=2)
    hot = hot & live[:, None, :]
    before = (position[:, None] < position[None, :]).astype(bf16)
    rank = jnp.einsum("bes,st->bet", hot.astype(bf16), before, preferred_element_type=f32)
    rank = rank.astype(jnp.int32)
    counts = rank[:, :, -1] + hot[:, :, -1]
    earlier = jnp.cumsum(counts, axis=0) - counts
    slot = earlier[:, :, None] + rank
    slot = jnp.where(hot & (slot < capacity), slot, -capacity)
    begin = jnp.minimum(earlier, capacity) // WINDOW_ALIGN * WINDOW_ALIGN
    info = jnp.concatenate([dp_index[None], begin.reshape(-1), tensor_index[None]])
    out_part, back_part, gate_gradient, up_gradient, down_gradient = expert_layer(
        info.astype(jnp.int32),
        slot,
        normed_all,
        cot_all,
        expert_gate,
        expert_up,
        expert_down,
        capacity,
        most_rows,
    )
    returned = scatter_all(back_part.reshape(tokens, features + AUX), 3)
    grads, input_gradient = attention_backward(
        lengths,
        sequence_order,
        returned,
        residual,
        sent,
        output_cotangent,
        input_rows,
        packed,
        saved,
        expert_count,
        6,
    )
    summed, expert_sum = last_scatter(grads, out_part.reshape(tokens, features), 4)
    (
        layer_output,
        query_gradient,
        key_gradient,
        value_gradient,
        context_gradient,
        router_gradient,
        prenorm_gradient,
        midnorm_gradient,
        querynorm_gradient,
        keynorm_gradient,
    ) = unpack(summed, expert_sum, residual, query_width, key_width, expert_count, norm_part)
    return (
        layer_output,
        input_gradient,
        query_gradient,
        key_gradient,
        value_gradient,
        context_gradient,
        router_gradient,
        gate_gradient,
        up_gradient,
        down_gradient,
        prenorm_gradient,
        midnorm_gradient,
        querynorm_gradient,
        keynorm_gradient,
    )


def solution(mesh):
    return jax.shard_map(
        gathered_body if mesh.shape["dp"] <= 16 else body,
        mesh=mesh,
        in_specs=(
            P(("dp", "tensor"), None),
            P("dp", "tensor"),
            P("dp", "tensor"),
            P("dp", "tensor"),
            P("tensor", "dp"),
            P("dp", None),
            P("dp", None, "tensor"),
            P("dp", None, "tensor"),
            P("dp", "tensor", None),
            P("dp"),
            P("dp"),
            P("dp"),
            P("dp"),
            P("dp", None),
            P(),
            P(),
            P(("dp", "tensor"), None),
        ),
        out_specs=(
            P(("dp", "tensor"), None),
            P(("dp", "tensor"), None),
            P("dp", "tensor"),
            P("dp", "tensor"),
            P("dp", "tensor"),
            P("tensor", "dp"),
            P("dp", None),
            P("dp", None, "tensor"),
            P("dp", None, "tensor"),
            P("dp", "tensor", None),
            P("dp"),
            P("dp"),
            P("dp"),
            P("dp"),
        ),
        check_vma=False,
    )
```

```python
import functools
import math

import jax
import jax.numpy as jnp
import numpy as np
from jax import lax
from jax.experimental import pallas as pl
from jax.experimental.pallas import tpu as pltpu
from jax.sharding import PartitionSpec as P

HEAD_SIZE = 128
TOP = 8
EXP_DEV = 2


epsilon = 1e-06
rope_base = 1000000.0
masked_score = -1e30


def carried_in(value, axis, combine, identity):
    count, place = (lax.axis_size(axis), lax.axis_index(axis))
    everything = lax.all_gather(value, axis)
    start = jnp.broadcast_to(jnp.asarray(identity, value.dtype), value.shape)

    def hop(k, before):
        reached = k < place
        new = combine(before, everything[k])
        return jnp.where(reached, new, before)

    return lax.fori_loop(0, count, hop, start)


def rms_normalize(value_rows):
    scaling = lax.rsqrt(jnp.mean(value_rows * value_rows, axis=-1, keepdims=True) + epsilon)
    return (value_rows * scaling, scaling)


def norm_back(cotangent, unit_rows, scaling):
    return scaling * (
        cotangent - unit_rows * jnp.mean(cotangent * unit_rows, axis=-1, keepdims=True)
    )


def rotary_apply(value_rows, cosine_table, sine_values):
    middle = value_rows.shape[-1] // 2
    former = value_rows[..., :middle]
    latter = value_rows[..., middle:]
    return jnp.concatenate(
        [
            former * cosine_table - latter * sine_values,
            latter * cosine_table + former * sine_values,
        ],
        axis=-1,
    )


def matrix_product(former, latter):
    return jnp.dot(former, latter, preferred_element_type=jnp.float32)


def contract(former, latter):
    return lax.dot_general(
        former, latter, (((0,), (0,)), ((), ())), preferred_element_type=jnp.float32
    )


def transposed(former, latter):
    return lax.dot_general(
        former, latter, (((1,), (1,)), ((), ())), preferred_element_type=jnp.float32
    )


def to_owners(buffer):
    return lax.all_to_all(buffer, "dp", split_axis=1, concat_axis=1, tiled=True)


def owner_reduce(partial_rows):
    shares = lax.psum_scatter(
        partial_rows.astype(jnp.bfloat16), "tensor", scatter_dimension=2, tiled=True
    )
    return lax.all_gather(shares, "tensor", axis=2, tiled=True)


def body(
    layer_input,
    query_weight,
    key_projection,
    value_projection,
    context_weight,
    router_weight,
    expert_gate,
    expert_up,
    expert_down,
    prenorm_gain,
    midnorm_gain,
    querynorm_gain,
    keynorm_gain,
    routes,
    lengths,
    sequence_order,
    output_cotangent,
):
    tensor_count = lax.axis_size("tensor")
    tensor_index = lax.axis_index("tensor")
    dp_count = lax.axis_size("dp")
    own_rows = layer_input.shape[0]
    block_rows = own_rows * tensor_count
    features = layer_input.shape[1]
    expert_count = EXP_DEV * dp_count
    capacity = 3 * block_rows * TOP // (4 * EXP_DEV)
    most_rows = (5 * block_rows * TOP + 4 * expert_count - 1) // (4 * expert_count)
    slot_total = EXP_DEV * dp_count * most_rows
    (
        query_all,
        key_all,
        value_all,
        context_all,
        router_all,
        gain_first,
        gain_second,
        query_gain,
        gain_key,
    ) = (
        lax.all_gather(query_weight, "dp", axis=0, tiled=True),
        lax.all_gather(key_projection, "dp", axis=0, tiled=True),
        lax.all_gather(value_projection, "dp", axis=0, tiled=True),
        lax.all_gather(context_weight, "dp", axis=1, tiled=True),
        lax.all_gather(router_weight, "dp", axis=0, tiled=True),
        lax.all_gather(prenorm_gain, "dp", axis=0, tiled=True),
        lax.all_gather(midnorm_gain, "dp", axis=0, tiled=True),
        lax.all_gather(querynorm_gain, "dp", axis=0, tiled=True),
        lax.all_gather(keynorm_gain, "dp", axis=0, tiled=True),
    )
    input_rows, cot_rows = (
        lax.all_gather(layer_input, "tensor", axis=0, tiled=True),
        lax.all_gather(output_cotangent, "tensor", axis=0, tiled=True),
    )
    position = jnp.arange(block_rows, dtype=jnp.int32)
    seq_length = lengths[sequence_order[lax.axis_index("dp")]]
    token_live = position < seq_length
    frequency = jnp.exp(
        -math.log(rope_base) * jnp.arange(HEAD_SIZE // 2, dtype=jnp.float32) * (2.0 / HEAD_SIZE)
    )
    angles = position.astype(jnp.float32)[:, None] * frequency[None, :]
    cosine_table = jnp.cos(angles)[:, None, :]
    sine_values = jnp.sin(angles)[:, None, :]
    heads_query = query_all.shape[1] // HEAD_SIZE
    heads_key = key_all.shape[1] // HEAD_SIZE
    group_width = heads_query // heads_key
    gain_one = gain_first.astype(jnp.float32)
    gain_two = gain_second.astype(jnp.float32)
    query_factor = query_gain.astype(jnp.float32)
    key_factor = gain_key.astype(jnp.float32)
    stream = input_rows.astype(jnp.float32)
    unit_first, scale_first = rms_normalize(stream)
    first_layer_normed = (unit_first * gain_one).astype(jnp.bfloat16)
    query_unnormed = matrix_product(first_layer_normed, query_all).reshape(
        block_rows, heads_query, HEAD_SIZE
    )
    key_unnormed = matrix_product(first_layer_normed, key_all).reshape(
        block_rows, heads_key, HEAD_SIZE
    )
    value_rows = (
        matrix_product(first_layer_normed, value_all)
        .astype(jnp.bfloat16)
        .reshape(block_rows, heads_key, HEAD_SIZE)
    )
    query_unit, query_scale = rms_normalize(query_unnormed)
    key_unit, key_scale = rms_normalize(key_unnormed)
    query_rows = (
        rotary_apply(query_unit * query_factor, cosine_table, sine_values)
        .astype(jnp.bfloat16)
        .reshape(block_rows, heads_key, group_width, HEAD_SIZE)
    )
    keys_rot = rotary_apply(key_unit * key_factor, cosine_table, sine_values).astype(jnp.bfloat16)
    score_scale = HEAD_SIZE ** (-0.5)
    allowed = (position[None, :] <= position[:, None]) & token_live[None, :]

    def score_block():
        raw_scores = (
            jnp.einsum("ikrd,jkd->krij", query_rows, keys_rot, preferred_element_type=jnp.float32)
            * score_scale
        )
        return jnp.where(allowed, raw_scores, masked_score)

    scores = score_block()
    row_peak = jnp.max(scores, axis=-1, keepdims=True)
    log_total = row_peak + jnp.log(jnp.sum(jnp.exp(scores - row_peak), axis=-1, keepdims=True))
    soft_probs = jnp.exp(scores - log_total)
    context = jnp.einsum(
        "krij,jkd->ikrd",
        soft_probs.astype(jnp.bfloat16),
        value_rows,
        preferred_element_type=jnp.float32,
    )
    context = context.reshape(block_rows, heads_query * HEAD_SIZE).astype(jnp.bfloat16)
    attention = lax.psum(matrix_product(context, context_all), "tensor")
    residual = stream + attention
    unit_second, scale_second = rms_normalize(residual)
    normed_second = (unit_second * gain_two).astype(jnp.bfloat16)
    logits = matrix_product(normed_second, router_all)
    expert_ids = jnp.arange(expert_count, dtype=jnp.int32)
    route_hot = routes[:, :, None] == expert_ids[None, None, :]
    chosen = jnp.sum(jnp.where(route_hot, logits[:, None, :], 0.0), axis=-1)
    gate_weights = jax.nn.softmax(chosen, axis=-1)
    pair_expert = routes.reshape(-1)
    pair_live = jnp.repeat(token_live, TOP)
    pair_hot = ((pair_expert[:, None] == expert_ids[None, :]) & pair_live[:, None]).astype(
        jnp.int32
    )
    running = jnp.cumsum(pair_hot, axis=0)
    pair_rank = jnp.sum((running - pair_hot) * pair_hot, axis=1)
    counts = running[-1]
    earlier = carried_in(
        counts, "dp", lambda former, latter: former + latter, jnp.zeros_like(counts)
    )
    pair_slot = jnp.sum(earlier[None, :] * pair_hot, axis=1) + pair_rank
    pair_kept = pair_live & (pair_slot < capacity)
    local_expert = pair_expert % EXP_DEV
    owner_index = pair_expert // EXP_DEV
    buffer_index = (local_expert * dp_count + owner_index) * most_rows + pair_rank
    target = jnp.where(pair_kept, buffer_index, slot_total)
    pair_ids = jnp.arange(block_rows * TOP, dtype=jnp.int32)
    slot_pair = jnp.full((slot_total,), -1, dtype=jnp.int32).at[target].set(pair_ids, mode="drop")
    slot_used = slot_pair >= 0
    slot_safe = jnp.maximum(slot_pair, 0)
    slot_token = slot_safe // TOP
    bf_zero = jnp.zeros((), jnp.bfloat16)
    send_rows = jnp.where(slot_used[:, None], normed_second[slot_token], bf_zero)
    layout = (EXP_DEV, dp_count, most_rows, features)
    received = to_owners(send_rows.reshape(layout)).reshape(EXP_DEV, dp_count * most_rows, features)
    gate_pre = jnp.einsum("end,edf->enf", received, expert_gate, preferred_element_type=jnp.float32)
    up_pre = jnp.einsum("end,edf->enf", received, expert_up, preferred_element_type=jnp.float32)
    sigmoid_gate = jax.nn.sigmoid(gate_pre)
    gate_act = gate_pre * sigmoid_gate
    hidden = (gate_act * up_pre).astype(jnp.bfloat16)
    out_partial = jnp.einsum(
        "enf,efd->end", hidden, expert_down, preferred_element_type=jnp.float32
    )
    expert_out = owner_reduce(out_partial)
    width = expert_out.shape[2]
    returned = lax.all_to_all(
        expert_out.reshape(EXP_DEV, dp_count, most_rows, width),
        "dp",
        split_axis=1,
        concat_axis=1,
        tiled=True,
    ).reshape(slot_total, width)
    pair_place = jnp.where(pair_kept, buffer_index, 0)
    pair_out = jnp.where(pair_kept[:, None], returned[pair_place], bf_zero).reshape(
        block_rows, TOP, width
    )
    expert_part = jnp.sum(gate_weights[:, :, None] * pair_out, axis=1)
    cot_full = cot_rows.astype(jnp.float32)
    own_start = tensor_index * own_rows
    gate_part = jnp.sum(cot_full[:, None, :] * pair_out, axis=-1)
    expert_own = lax.dynamic_slice_in_dim(expert_part, own_start, own_rows, 0)
    residual_own = lax.dynamic_slice_in_dim(residual, own_start, own_rows, 0)
    layer_output = (residual_own + expert_own).astype(jnp.bfloat16)
    slot_gate = jnp.where(slot_used, gate_weights.reshape(-1)[slot_safe], 0.0)
    send_cot = (slot_gate[:, None] * cot_full[slot_token]).astype(jnp.bfloat16)
    expert_cot = to_owners(send_cot.reshape(layout)).reshape(
        EXP_DEV, dp_count * most_rows, features
    )
    hidden_cot = jnp.einsum(
        "end,efd->enf", expert_cot, expert_down, preferred_element_type=jnp.float32
    )
    gating_cot = (
        hidden_cot * up_pre * sigmoid_gate * (1.0 + gate_pre * (1.0 - sigmoid_gate))
    ).astype(jnp.bfloat16)
    upward_cot = (hidden_cot * gate_act).astype(jnp.bfloat16)
    down_gradient = jnp.einsum(
        "enf,end->efd", hidden, expert_cot, preferred_element_type=jnp.float32
    )
    gate_gradient = jnp.einsum(
        "end,enf->edf", received, gating_cot, preferred_element_type=jnp.float32
    )
    up_gradient = jnp.einsum(
        "end,enf->edf", received, upward_cot, preferred_element_type=jnp.float32
    )
    row_partial = jnp.einsum(
        "enf,edf->end", gating_cot, expert_gate, preferred_element_type=jnp.float32
    )
    row_partial = row_partial + jnp.einsum(
        "enf,edf->end", upward_cot, expert_up, preferred_element_type=jnp.float32
    )
    row_cot = owner_reduce(row_partial)
    row_back = lax.all_to_all(
        row_cot.reshape(EXP_DEV, dp_count, most_rows, width),
        "dp",
        split_axis=1,
        concat_axis=1,
        tiled=True,
    ).reshape(slot_total, width)
    pair_cot = jnp.where(pair_kept[:, None], row_back[pair_place], bf_zero).reshape(
        block_rows, TOP, width
    )
    normed_part = jnp.sum(pair_cot.astype(jnp.float32), axis=1)
    normed_cot = normed_part
    route_cot = gate_weights * (
        gate_part - jnp.sum(gate_weights * gate_part, axis=-1, keepdims=True)
    )
    logit_cot = jnp.sum(jnp.where(route_hot, route_cot[:, :, None], 0.0), axis=1).astype(
        jnp.bfloat16
    )
    router_gradient = contract(normed_second, logit_cot)
    normed_cot = normed_cot + transposed(logit_cot, router_all)
    midnorm_gradient = jnp.sum(normed_cot * unit_second, axis=0)
    residual_cot = cot_full + norm_back(normed_cot * gain_two, unit_second, scale_second)
    attention_cot = residual_cot.astype(jnp.bfloat16)
    context_gradient = contract(context, attention_cot)
    context_cot = (
        transposed(attention_cot, context_all)
        .astype(jnp.bfloat16)
        .reshape(block_rows, heads_key, group_width, HEAD_SIZE)
    )
    scores = score_block()
    soft_probs = jnp.exp(scores - log_total)
    prob_cot = jnp.einsum(
        "ikrd,jkd->krij", context_cot, value_rows, preferred_element_type=jnp.float32
    )
    score_cot = (
        soft_probs * (prob_cot - jnp.sum(soft_probs * prob_cot, axis=-1, keepdims=True))
    ).astype(jnp.bfloat16)
    value_cot = jnp.einsum(
        "krij,ikrd->jkd",
        soft_probs.astype(jnp.bfloat16),
        context_cot,
        preferred_element_type=jnp.float32,
    )
    value_cot = value_cot.astype(jnp.bfloat16).reshape(block_rows, heads_key * HEAD_SIZE)
    query_turned = (
        jnp.einsum(
            "krij,jkd->ikrd", score_cot, keys_rot, preferred_element_type=jnp.float32
        ).reshape(block_rows, heads_query, HEAD_SIZE)
        * score_scale
    )
    key_turned = (
        jnp.einsum("krij,ikrd->jkd", score_cot, query_rows, preferred_element_type=jnp.float32)
        * score_scale
    )
    query_back = rotary_apply(query_turned, cosine_table, -sine_values)
    key_back = rotary_apply(key_turned, cosine_table, -sine_values)
    querynorm_part = jnp.sum(query_back * query_unit, axis=(0, 1))
    keynorm_part = jnp.sum(key_back * key_unit, axis=(0, 1))
    query_raw_cot = (
        norm_back(query_back * query_factor, query_unit, query_scale)
        .astype(jnp.bfloat16)
        .reshape(block_rows, heads_query * HEAD_SIZE)
    )
    key_raw_cot = (
        norm_back(key_back * key_factor, key_unit, key_scale)
        .astype(jnp.bfloat16)
        .reshape(block_rows, heads_key * HEAD_SIZE)
    )
    query_gradient = contract(first_layer_normed, query_raw_cot)
    key_gradient = contract(first_layer_normed, key_raw_cot)
    value_gradient = contract(first_layer_normed, value_cot)
    first_part = (
        transposed(query_raw_cot, query_all)
        + transposed(key_raw_cot, key_all)
        + transposed(value_cot, value_all)
    )
    first_cot, querynorm_gradient, keynorm_gradient = (
        lax.psum(first_part.astype(jnp.bfloat16), "tensor").astype(jnp.float32),
        lax.psum(querynorm_part.astype(jnp.bfloat16), "tensor").astype(jnp.float32),
        lax.psum(keynorm_part.astype(jnp.bfloat16), "tensor").astype(jnp.float32),
    )
    prenorm_gradient = jnp.sum(first_cot * unit_first, axis=0)
    input_cot = residual_cot + norm_back(first_cot * gain_one, unit_first, scale_first)
    input_gradient = lax.dynamic_slice_in_dim(input_cot, own_start, own_rows, 0).astype(
        jnp.bfloat16
    )
    summed = (
        lax.psum_scatter(query_gradient, "dp", scatter_dimension=0, tiled=True),
        lax.psum_scatter(key_gradient, "dp", scatter_dimension=0, tiled=True),
        lax.psum_scatter(value_gradient, "dp", scatter_dimension=0, tiled=True),
        lax.psum_scatter(context_gradient, "dp", scatter_dimension=1, tiled=True),
        lax.psum_scatter(router_gradient, "dp", scatter_dimension=0, tiled=True),
        lax.psum_scatter(prenorm_gradient, "dp", scatter_dimension=0, tiled=True),
        lax.psum_scatter(midnorm_gradient, "dp", scatter_dimension=0, tiled=True),
        lax.psum_scatter(querynorm_gradient, "dp", scatter_dimension=0, tiled=True),
        lax.psum_scatter(keynorm_gradient, "dp", scatter_dimension=0, tiled=True),
    )
    return (
        layer_output,
        input_gradient,
        summed[0],
        summed[1],
        summed[2],
        summed[3],
        summed[4],
        gate_gradient,
        up_gradient,
        down_gradient,
        summed[5],
        summed[6],
        summed[7],
        summed[8],
    )


AUX = 128


GRID_Z = 4
VMEM_LIMIT = 56 * 1024 * 1024


def remote(src, dst, send_sem, recv_sem, device):
    return pltpu.make_async_remote_copy(
        src_ref=src,
        dst_ref=dst,
        send_sem=send_sem,
        recv_sem=recv_sem,
        device_id=device,
        device_id_type=pl.DeviceIdType.MESH,
    )


class Place:
    def __init__(self):
        self.dp = lax.axis_index("dp")
        self.y = lax.axis_index("tensor")
        self.z = self.dp // 4
        self.x = (self.dp // 2) % 2
        self.core = self.dp % 2
        self.sibling = (self.dp + 1 - 2 * self.core, self.y)
        self.x_mate = (self.dp + 2 - 4 * self.x, self.y)
        self.y_mate = (self.dp, 1 - self.y)
        self.above = (self.dp + 4, self.y)
        self.below = (self.dp - 4, self.y)
        self.has_above = self.z < GRID_Z - 1
        self.has_below = self.z > 0

    def farthest(self, k):
        return (3 - 3 * (self.z // 2), (2 + 3 * self.z) % 5, 1 + self.z % 2, self.z)[k]

    def dp_at(self, z, flip_x, flip_core):
        x = self.x + flip_x * (1 - 2 * self.x)
        core = self.core + flip_core * (1 - 2 * self.core)
        return z * 4 + x * 2 + core

    def y_at(self, flip_y):
        return self.y + flip_y * (1 - 2 * self.y)

    def greet(self):
        barrier = pltpu.get_barrier_semaphore()
        for mate in (self.sibling, self.x_mate, self.y_mate):
            pl.semaphore_signal(barrier, 1, device_id=mate, device_id_type=pl.DeviceIdType.MESH)

        @pl.when(self.has_above)
        def _():
            pl.semaphore_signal(
                barrier, 1, device_id=self.above, device_id_type=pl.DeviceIdType.MESH
            )

        @pl.when(self.has_below)
        def _():
            pl.semaphore_signal(
                barrier, 1, device_id=self.below, device_id_type=pl.DeviceIdType.MESH
            )

        pl.semaphore_wait(barrier, 4 + self.z * (GRID_Z - 1 - self.z) // 2)


def add_rows(target, sources, rows, step=16):
    start, count = rows

    def one(i, carry):
        at = pl.ds(pl.multiple_of(start + i * step, step), step)
        total = target[at, :].astype(jnp.float32)
        for source, shift in sources:
            there = pl.ds(pl.multiple_of(start - shift + i * step, step), step)
            total = total + source[there, :].astype(jnp.float32)
        target[at, :] = total.astype(target.dtype)
        return carry

    lax.fori_loop(0, count // step, one, 0)


def line_onward(me, source, buffer, sem, to, side, mate):
    ends = 1 - (me.z - 1 - to + GRID_Z - 1) // GRID_Z
    slot = to if side == 0 else to + (GRID_Z - to) * ends
    return remote(source, buffer.at[slot], sem.at[0, to], sem.at[1, slot], mate)


def line_sum(me, k, block, source, rows, buffer, sem, shift):
    to = me.farthest(k)
    for side, ahead, mate, more in (
        (0, to > me.z, me.above, me.has_below),
        (1, to < me.z, me.below, me.has_above),
    ):
        slot = to if k < GRID_Z - 1 or side == 0 else GRID_Z
        came = remote(source, buffer.at[slot], sem.at[0, slot], sem.at[1, slot], mate)

        def gather(came=came, slot=slot):
            came.wait_recv()
            add_rows(block, [(buffer.at[slot], shift)], rows)

        if k < GRID_Z - 1:

            @pl.when(ahead)
            def _():
                pl.when(more)(gather)
                line_onward(me, source, buffer, sem, to, side, mate).start()
        else:
            pl.when(more)(gather)


def line_sent(me, k, source, buffer, sem):
    to = me.farthest(k)
    for side, ahead, mate in ((0, to > me.z, me.above), (1, to < me.z, me.below)):

        @pl.when(ahead)
        def _():
            line_onward(me, source, buffer, sem, to, side, mate).wait_send()


ROW_PLAN = (
    ("eda", 0), ("cz", 0, 1, 1), ("edb", 0), ("ey", 0), ("cz", 0, 0, 1), ("ex", 0), ("eda", 1),
    ("cz", 0, 0, 0), ("cz", 1, 0, 1), ("edb", 1), ("lx", 0), ("cz", 1, 1, 1), ("eda", 2),
    ("cz", 2, 1, 1), ("ly", 0), ("ly", 1), ("cz", 2, 0, 1), ("lx", 2), ("ex", 1), ("eda", 3),
    ("cz", 0, 1, 0), ("cz", 1, 1, 0), ("edb", 2), ("lx", 1), ("ey", 1), ("ey", 2), ("col", 0),
    ("edb", 3), ("cz", 2, 1, 0), ("cz", 1, 0, 0), ("cz", 3, 0, 1), ("cy", 0), ("cz", 3, 1, 1),
    ("ly", 2), ("ex", 2), ("col", 1), ("ly", 3), ("cz", 2, 0, 0), ("lx", 3), ("ex", 3),
    ("col", 2), ("cy", 1), ("ey", 3), ("cz", 3, 0, 0), ("cz", 3, 1, 0), ("cx",), ("cend",),
    ("col", 3),
)


def row_scatter_kernel(
    part, out, own, core, diag_a, diag_b, from_x, from_y, from_z, c_z, c_y, c_x,
    load_s, core_s, diag_s, x_s, y_s, z_s, cz_s, cy_s, cx_s, out_s,
):
    me = Place()
    rows, third = own.shape[3], diag_a.shape[1]
    last = GRID_Z - 1
    spans = ((0, third), (third, third), (2 * third, rows - 2 * third))
    a_at, b_at, c_at = (pl.ds(*span) for span in spans)
    most, most_at = (0, 2 * third), pl.ds(0, 2 * third)
    loads, cores, here = {}, {}, set()

    def chunk(k, flip_x, flip_y, flip_core):
        return part.at[me.dp_at(me.farthest(k), flip_x, flip_core) * 2 + me.y_at(flip_y)]

    order = ((1, 1), (1, 0), (0, 1), (0, 0))
    for k in range(GRID_Z):
        for fx, fy in order:
            copy = pltpu.make_async_copy(
                chunk(k, fx, fy, 0), own.at[k, fx, fy], load_s.at[k, fx, fy]
            )
            copy.start()
            loads[k, fx, fy] = copy
    me.greet()
    for k in range(GRID_Z):
        for fx, fy in order:
            copy = remote(
                chunk(k, fx, fy, 1), core.at[k, fx, fy],
                core_s.at[0, k, fx, fy], core_s.at[1, k, fx, fy], me.sibling,
            )
            copy.start()
            cores[k, fx, fy] = copy

    def pieces(make):
        return [make(k) for k in range(GRID_Z)]

    da = pieces(lambda k: remote(own.at[k, 1, 1, a_at], diag_a.at[k], diag_s.at[0, k], diag_s.at[1, k], me.y_mate))
    db = pieces(lambda k: remote(own.at[k, 1, 1, b_at], diag_b.at[k], diag_s.at[2, k], diag_s.at[3, k], me.x_mate))
    xs = pieces(
        lambda k: [
            remote(own.at[k, 1, 0, at], from_x.at[k, at], x_s.at[0, k, h], x_s.at[1, k, h], me.x_mate)
            for h, at in enumerate((a_at, b_at))
        ]
    )
    ys = pieces(
        lambda k: [
            remote(own.at[k, 0, 1, at], from_y.at[k, at], y_s.at[0, k, h], y_s.at[1, k, h], me.y_mate)
            for h, at in enumerate((a_at, b_at))
        ]
    )
    cy = [
        remote(own.at[last, fx, 1, c_at], c_y.at[fx], cy_s.at[0, fx], cy_s.at[1, fx], me.y_mate)
        for fx in range(2)
    ]
    cx = remote(own.at[last, 1, 0, c_at], c_x, cx_s.at[0], cx_s.at[1], me.x_mate)

    def add(k, fx, fy, h, *more):
        if (k, fx, fy) not in here:
            here.add((k, fx, fy))
            loads[k, fx, fy].wait()
            cores[k, fx, fy].wait_recv()
        span = most if h is None else spans[h]
        add_rows(own.at[k, fx, fy], [(core.at[k, fx, fy], 0), *more], span)

    def diagonal_a(k):
        add(k, 1, 1, 0)
        da[k].start()

    def diagonal_b(k):
        add(k, 1, 1, 1)
        db[k].start()

    def early_x(k):
        add(k, 1, 0, 1)
        xs[k][1].start()

    def early_y(k):
        add(k, 0, 1, 0)
        ys[k][0].start()

    def late_x(k):
        da[k].wait_recv()
        add(k, 1, 0, 0, (diag_a.at[k], 0))
        xs[k][0].start()

    def late_y(k):
        db[k].wait_recv()
        add(k, 0, 1, 1, (diag_b.at[k], third))
        ys[k][1].start()

    def column(k):
        for h in range(2):
            xs[k][h].wait_recv()
            ys[k][h].wait_recv()
        add(k, 0, 0, None, (from_x.at[k], 0), (from_y.at[k], 0))
        block = own.at[k, 0, 0]
        line_sum(me, k, block, block.at[most_at], most, from_z, z_s, 0)

    def c_line(k, fx, fy):
        add(k, fx, fy, 2)
        block = own.at[k, fx, fy]
        line_sum(
            me, k, block, block.at[c_at], spans[2], c_z.at[fx, fy], cz_s.at[fx, fy], 2 * third
        )

    def c_over_x():
        cy[1].wait_recv()
        add_rows(own.at[last, 1, 0], [(c_y.at[1], 2 * third)], spans[2])
        cx.start()

    def c_end():
        cy[0].wait_recv()
        cx.wait_recv()
        add_rows(own.at[last, 0, 0], [(c_y.at[0], 2 * third), (c_x, 2 * third)], spans[2])

    actions = {
        "eda": diagonal_a, "edb": diagonal_b, "ex": early_x, "ey": early_y, "lx": late_x,
        "ly": late_y, "col": column, "cz": c_line, "cy": lambda fx: cy[fx].start(),
        "cx": c_over_x, "cend": c_end,
    }
    for name, *which in ROW_PLAN:
        actions[name](*which)
    copy = pltpu.make_async_copy(own.at[last, 0, 0], out, out_s)
    copy.start()
    for k in range(GRID_Z):
        da[k].wait_send()
        db[k].wait_send()
        for h in range(2):
            xs[k][h].wait_send()
            ys[k][h].wait_send()
        if k < last:
            line_sent(me, k, own.at[k, 0, 0, most_at], from_z, z_s)
            for fx, fy in order:
                line_sent(me, k, own.at[k, fx, fy, c_at], c_z.at[fx, fy], cz_s.at[fx, fy])
    for sent in (*cores.values(), *cy, cx):
        sent.wait_send()
    copy.wait()


def scatter_all(value, collective_id):
    devices = lax.axis_size("dp") * lax.axis_size("tensor")
    rows, width = value.shape[0] // devices, value.shape[1]
    third = 3 * rows // 8
    dma = pltpu.SemaphoreType.DMA
    low = value.dtype
    shapes = (
        (4, 2, 2, rows), (4, 2, 2, rows), (4, third), (4, third), (4, 2 * third), (4, 2 * third),
        (5, 2 * third), (2, 2, 5, rows - 2 * third), (2, rows - 2 * third), (rows - 2 * third,),
    )
    return pl.pallas_call(
        row_scatter_kernel,
        out_shape=jax.ShapeDtypeStruct((rows, width), low),
        in_specs=[pl.BlockSpec(memory_space=pl.ANY)],
        out_specs=pl.BlockSpec(memory_space=pl.ANY),
        scratch_shapes=[
            *(pltpu.VMEM((*shape, width), low) for shape in shapes),
            dma((4, 2, 2)),
            dma((2, 4, 2, 2)),
            dma((4, 4)),
            dma((2, 4, 2)),
            dma((2, 4, 2)),
            dma((2, 5)),
            dma((2, 2, 2, 5)),
            dma((2, 2)),
            dma((2,)),
            dma(()),
        ],
        compiler_params=pltpu.CompilerParams(
            collective_id=collective_id, has_side_effects=True, vmem_limit_bytes=VMEM_LIMIT
        ),
    )(value.reshape(devices, rows, width))


WINDOW_ALIGN = 16
EXPERT_VMEM = 60 * 1024 * 1024


def dot(left, right, dims=((1,), (0,))):
    return lax.dot_general(left, right, (dims, ((), ())), preferred_element_type=jnp.float32)


def expert_kernel(
    info, pos, rows_in, cots_in, gate_w, up_w, down_w,
    out, back, gate_g, up_g, down_g,
    x, dy, wgu, wd, slot_out, slot_row, gu, hg, rows_b, cots_b, g_stage, d_stage,
    load_s, w_s, out_s, g_s, d_s,
):
    bf16, f32 = jnp.bfloat16, jnp.float32
    blocks, block_rows, wide = rows_in.shape
    features = cots_in.shape[2]
    experts, padded = x.shape[0], x.shape[1]
    part = hg.shape[2]
    cap = hg.shape[1]
    window = padded - cap
    tile = cap // 2
    chunk = d_stage.shape[2]

    def load(b):
        slot = b % 2
        return (
            pltpu.make_async_copy(rows_in.at[b], rows_b.at[slot], load_s.at[slot, 0]),
            pltpu.make_async_copy(cots_in.at[b], cots_b.at[slot], load_s.at[slot, 1]),
        )

    for copy in load(0):
        copy.start()
    weights = []
    for e in range(experts):
        weights.append(pltpu.make_async_copy(gate_w.at[e], wgu.at[e, :, pl.ds(0, part)], w_s.at[e, 0]))
        weights.append(pltpu.make_async_copy(up_w.at[e], wgu.at[e, :, pl.ds(part, part)], w_s.at[e, 1]))
        weights.append(pltpu.make_async_copy(down_w.at[e], wd.at[e], w_s.at[e, 2]))
    for copy in weights:
        copy.start()

    def clear(i, carry):
        at = pl.ds(pl.multiple_of(i * 16, 16), 16)
        for e in range(experts):
            x[e, at, :] = jnp.zeros((16, wide), bf16)
            dy[e, at, :] = jnp.zeros((16, features), bf16)
        return carry

    lax.fori_loop(0, padded // 16, clear, 0)
    for e in range(experts):
        slot_out[e, pl.ds(cap, window), :] = jnp.zeros((window, features), bf16)
        slot_row[e, pl.ds(cap, window), :] = jnp.zeros((window, wide), bf16)

    def starts(b):
        return [pl.multiple_of(info[1 + b * experts + e], WINDOW_ALIGN) for e in range(experts)]

    def picks(b, begin):
        slots = lax.broadcasted_iota(jnp.int32, (window, block_rows), 0)
        return jnp.concatenate(
            [(slots + begin[e] == pos[b, pl.ds(e, 1), :]).astype(f32) for e in range(experts)],
            axis=0,
        )

    def take(b, carry):
        slot = b % 2

        @pl.when(b + 1 < blocks)
        def _():
            for copy in load(b + 1):
                copy.start()

        begin = starts(b)
        picked = picks(b, begin).astype(bf16)
        for copy in load(b):
            copy.wait()
        for source, target, width in ((rows_b, x, wide), (cots_b, dy, features)):
            for first in range(0, width, chunk):
                cols = pl.ds(first, min(chunk, width - first))
                got = dot(picked, source[slot, :, cols]).astype(bf16)
                for e in range(experts):
                    first_at = pl.ds(begin[e], WINDOW_ALIGN)
                    rest_at = pl.ds(begin[e] + WINDOW_ALIGN, window - WINDOW_ALIGN)
                    split = e * window + WINDOW_ALIGN
                    target[e, first_at, cols] += got[e * window : split]
                    target[e, rest_at, cols] = got[split : (e + 1) * window]
        return carry

    lax.fori_loop(0, blocks, take, 0)
    for copy in weights:
        copy.wait()

    lanes = lax.broadcasted_iota(jnp.int32, (tile, AUX), 1)

    def mlp(step, carry):
        e = step // (cap // tile)
        at = pl.ds(pl.multiple_of((step % (cap // tile)) * tile, tile), tile)
        own = info[0] * experts + e
        total = blocks * experts
        aux = x[e, at, pl.ds(features, AUX)].astype(f32)
        gate = jnp.sum(
            jnp.where((lanes == own) | (lanes == own + total), aux, 0.0), axis=1, keepdims=True
        )
        pre = dot(x[e, at, pl.ds(0, features)], wgu[e])
        gate_pre, up_pre = pre[:, :part], pre[:, part:]
        sig = 1.0 / (1.0 + jnp.exp(-gate_pre))
        act = gate_pre * sig
        hidden = (act * up_pre).astype(bf16).astype(f32)
        gated = (hidden * gate).astype(bf16)
        hg[e, at, :] = gated
        down_cot = dot(dy[e, at, :], wd[e], ((1,), (1,)))
        slot_cot = jnp.sum(hidden * down_cot, axis=1, keepdims=True)
        hidden_cot = down_cot * gate
        gu[e, at, pl.ds(0, part)] = (
            hidden_cot * up_pre * sig * (1.0 + gate_pre * (1.0 - sig))
        ).astype(bf16)
        gu[e, at, pl.ds(part, part)] = (hidden_cot * act).astype(bf16)
        for first in range(0, features, chunk):
            cols = pl.ds(first, chunk)
            slot_out[e, at, cols] = dot(gated, wd[e, :, cols]).astype(bf16)
            slot_row[e, at, cols] = dot(
                gu[e, at, :], wgu[e, pl.ds(first, chunk), :], ((1,), (1,))
            ).astype(bf16)
        high = slot_cot.astype(bf16).astype(f32)
        place = info[1 + blocks * experts] * 2 * total + own * 2
        slot_row[e, at, pl.ds(features, AUX)] = jnp.where(
            lanes == place, high, jnp.where(lanes == place + 1, slot_cot - high, 0.0)
        ).astype(bf16)
        return carry

    lax.fori_loop(0, experts * (cap // tile), mlp, 0)

    def stored(b):
        slot = b % 2
        return (
            pltpu.make_async_copy(cots_b.at[slot], out.at[b], out_s.at[slot, 0]),
            pltpu.make_async_copy(rows_b.at[slot], back.at[b], out_s.at[slot, 1]),
        )

    def put(b, carry):
        slot = b % 2

        @pl.when(b >= 2)
        def _():
            for copy in stored(b - 2):
                copy.wait()

        begin = starts(b)
        spread = picks(b, begin).T.astype(bf16)
        for source, target, width in ((slot_out, cots_b, features), (slot_row, rows_b, wide)):
            for first in range(0, width, chunk):
                cols = pl.ds(first, min(chunk, width - first))
                held = jnp.concatenate(
                    [source[e, pl.ds(begin[e], window), cols] for e in range(experts)], axis=0
                )
                target[slot, :, cols] = dot(spread, held).astype(bf16)
        for copy in stored(b):
            copy.start()
        return carry

    lax.fori_loop(0, blocks, put, 0)

    tile = g_stage.shape[1]
    tiles = features // tile

    def g_copies(step):
        slot = step % 2
        e, at = step // tiles, pl.ds(pl.multiple_of((step % tiles) * tile, tile), tile)
        return (
            pltpu.make_async_copy(g_stage.at[slot, :, pl.ds(0, part)], gate_g.at[e, at], g_s.at[slot, 0]),
            pltpu.make_async_copy(g_stage.at[slot, :, pl.ds(part, part)], up_g.at[e, at], g_s.at[slot, 1]),
        )

    def wide_grad(step, carry):
        slot = step % 2
        e, at = step // tiles, pl.ds(pl.multiple_of((step % tiles) * tile, tile), tile)

        @pl.when(step >= 2)
        def _():
            for copy in g_copies(step - 2):
                copy.wait()

        g_stage[slot] = dot(x[e, pl.ds(0, cap), at], gu[e], ((0,), (0,)))
        for copy in g_copies(step):
            copy.start()
        return carry

    lax.fori_loop(0, experts * tiles, wide_grad, 0)
    parts = features // chunk

    def d_copy(step):
        slot = step % 2
        e, at = step // parts, pl.ds(pl.multiple_of((step % parts) * chunk, chunk), chunk)
        return pltpu.make_async_copy(d_stage.at[slot], down_g.at[e, :, at], d_s.at[slot])

    def down_grad(step, carry):
        slot = step % 2
        e, at = step // parts, pl.ds(pl.multiple_of((step % parts) * chunk, chunk), chunk)

        @pl.when(step >= 2)
        def _():
            d_copy(step - 2).wait()

        d_stage[slot] = dot(hg[e], dy[e, pl.ds(0, cap), at], ((0,), (0,)))
        d_copy(step).start()
        return carry

    lax.fori_loop(0, experts * parts, down_grad, 0)
    for last in (2, 1):
        for copy in stored(blocks - last):
            copy.wait()
        for copy in g_copies(experts * tiles - last):
            copy.wait()
        d_copy(experts * parts - last).wait()


def expert_layer(info, pos, rows_in, cots_in, gate_w, up_w, down_w, capacity, most):
    bf16, f32 = jnp.bfloat16, jnp.float32
    blocks, block_rows, wide = rows_in.shape
    features = cots_in.shape[2]
    experts, part = gate_w.shape[0], gate_w.shape[2]
    padded = capacity + -(-most // WINDOW_ALIGN) * WINDOW_ALIGN + WINDOW_ALIGN
    dma = pltpu.SemaphoreType.DMA
    shape = jax.ShapeDtypeStruct
    anywhere = pl.BlockSpec(memory_space=pl.ANY)
    return pl.pallas_call(
        expert_kernel,
        out_shape=(
            shape((blocks, block_rows, features), bf16),
            shape((blocks, block_rows, wide), bf16),
            shape(gate_w.shape, f32),
            shape(up_w.shape, f32),
            shape(down_w.shape, f32),
        ),
        in_specs=[
            pl.BlockSpec(memory_space=pltpu.SMEM),
            pl.BlockSpec(memory_space=pltpu.VMEM),
        ]
        + [anywhere] * 5,
        out_specs=(anywhere,) * 5,
        scratch_shapes=[
            pltpu.VMEM((experts, padded, wide), bf16),
            pltpu.VMEM((experts, padded, features), bf16),
            pltpu.VMEM((experts, features, 2 * part), bf16),
            pltpu.VMEM((experts, part, features), bf16),
            pltpu.VMEM((experts, padded, features), bf16),
            pltpu.VMEM((experts, padded, wide), bf16),
            pltpu.VMEM((experts, capacity, 2 * part), bf16),
            pltpu.VMEM((experts, capacity, part), bf16),
            pltpu.VMEM((2, block_rows, wide), bf16),
            pltpu.VMEM((2, block_rows, features), bf16),
            pltpu.VMEM((2, features // 2, 2 * part), f32),
            pltpu.VMEM((2, part, features // 2), f32),
            dma((2, 2)),
            dma((experts, 3)),
            dma((2, 2)),
            dma((2, 2)),
            dma((2,)),
        ],
        compiler_params=pltpu.CompilerParams(vmem_limit_bytes=EXPERT_VMEM),
    )(info, pos, rows_in, cots_in, gate_w, up_w, down_w)


ATTENTION_VMEM = 60 * 1024 * 1024
SCORE_SCALE = HEAD_SIZE ** (-0.5)
def turn_tables(rows):
    frequency = np.exp(
        -math.log(rope_base) * np.arange(HEAD_SIZE // 2, dtype=np.float32) * (2.0 / HEAD_SIZE)
    ).astype(np.float32)
    angles = np.arange(rows, dtype=np.float32)[:, None] * frequency[None, :]
    cosine, sine = np.cos(angles), np.sin(angles)
    return (
        np.concatenate([cosine, cosine], axis=1).astype(np.float32),
        np.concatenate([-sine, sine], axis=1).astype(np.float32),
    )


def turn(value, cosine, sine):
    return value * cosine + pltpu.roll(value, HEAD_SIZE // 2, 1) * sine


def inverse_norm(value):
    return lax.rsqrt(jnp.mean(value * value, axis=-1, keepdims=True) + epsilon)


def split_pair(me, both):
    half = both.shape[0] // 2
    first = me.y == 0
    lower, upper = both[:half], both[half:]
    return jnp.where(first, upper, lower), jnp.where(first, lower, upper)


def meet_y(me):
    barrier = pltpu.get_barrier_semaphore()
    pl.semaphore_signal(barrier, 1, device_id=me.y_mate, device_id_type=pl.DeviceIdType.MESH)
    pl.semaphore_wait(barrier, 1)


def gain_rows(aux_t, experts, chunks):
    head = [aux_t[experts + 2 + i : experts + 3 + i, :] for i in range(2)]
    width = HEAD_SIZE
    heads = [sum(row[:, c * width : (c + 1) * width] for c in range(chunks)) for row in head]
    return aux_t[experts : experts + 1, :], aux_t[experts + 1 : experts + 2, :], *heads


def probabilities(query, key, allowed):
    scores = jnp.where(allowed, dot(query, key, ((1,), (1,))) * SCORE_SCALE, masked_score)
    spread = jnp.exp(scores - jnp.max(scores, axis=-1, keepdims=True))
    return spread / jnp.sum(spread, axis=-1, keepdims=True)


def allowed_pairs(length, rows):
    later = lax.broadcasted_iota(jnp.int32, (rows, rows), 0)
    sooner = lax.broadcasted_iota(jnp.int32, (rows, rows), 1)
    return (sooner <= later) & (sooner < length)


def placed(count, offset):
    row = lax.broadcasted_iota(jnp.int32, (count, AUX), 0)
    return (row + offset == lax.broadcasted_iota(jnp.int32, (count, AUX), 1)).astype(jnp.bfloat16)


OPENING_PLAN = (
    ("w", 0, 0), ("a", 0), ("w", 1, 0), ("pair",), ("a", 1), ("b", 0, 0), ("w", 2, 0), ("a", 2),
    ("ax", 0), ("bx",), ("w", 3, 0), ("w", 0, 1), ("y1", 1, 0, 0), ("ax", 2), ("b", 0, 1),
    ("ax", 1), ("wx", 1, 0), ("b", 1, 1), ("ay0",), ("w", 1, 1), ("wx", 0, 0), ("b", 1, 0),
    ("wx", 2, 0), ("b", 2, 1), ("w", 2, 1), ("wx", 3, 0), ("y1", 1, 1, 0), ("prep",), ("qkv",),
    ("h", 0), ("y1", 1, 0, 1), ("b", 2, 0), ("w", 3, 1), ("y1", 0, 0, 1), ("h", 1), ("b", 3, 0),
    ("wx", 1, 1), ("h", 2), ("wx", 2, 1), ("a", 3), ("h", 3), ("wx", 0, 1), ("b", 3, 1),
    ("wx", 3, 1), ("ctx",), ("ax", 3), ("fin",), ("n", 0), ("y1", 0, 1, 0),
    ("y1", 1, 1, 1), ("c0",), ("n", 1), ("n", 2), ("c1",), ("n", 3), ("nx", 1), ("c2", 0),
    ("cz", 1, 1, 0), ("nx", 0), ("c2", 1), ("cz", 1, 1, 1), ("ny", 1), ("ny", 2),
    ("cz", 2, 1, 0), ("cz", 1, 0, 0), ("y1", 2, 0, 1), ("ny", 3), ("y1", 0, 1, 1),
    ("y1", 3, 1, 0), ("y1", 2, 1, 0), ("ny", 0), ("nx", 3), ("cz", 2, 1, 1), ("y1", 3, 0, 1),
    ("nx", 2), ("y1", 0, 0, 0), ("cz", 3, 1, 0), ("y1", 2, 0, 0), ("cz", 3, 1, 1),
    ("y1", 3, 0, 0), ("y1", 3, 1, 1), ("y1", 2, 1, 1), ("cz", 2, 0, 0), ("cz", 1, 0, 1),
    ("nca", 1), ("cz", 2, 0, 1), ("cz", 3, 0, 1), ("nca", 0), ("ncb", 2), ("ncb", 0),
    ("nca", 3), ("ncb", 1), ("ncb", 3), ("cz", 3, 0, 0), ("nca", 2),
)


def opening_kernel(
    experts, qkv,
    lengths, sequence_order, query_w, key_w, value_w, context_w, router_t, prenorm, midnorm,
    querynorm, keynorm, routes_t, d_src, x_src, cosine_in, sine_in,
    w_out, d_out, x_out,
    rows_o, sent_o, residual_o, normed_o, raw_o, query_o, key_o, value_o, context_o,
    x, w, ctx, aux_w, normed, raw, query, key, value, context, att, got, residual, sent,
    local_s, pair_s, wz_s, wx_s, wc_s, az_s, ax_s, ay_s, bz_s, bx_s, by_s, dc_s,
    in_s, w_s, out_s, y_s,
    w_src, flat_ctx, flat_router, flat_gains, head_gains, flat_routes, cosine, sine, load_s,
    nl_s, nz_s, nx_s, ny_s, ndx_s, ndy_s, nc_s, cx_s, cy_s, cz_s, cc_s,
):
    bf16, f32 = jnp.bfloat16, jnp.float32
    me = Place()
    half = d_src.shape[0] // 2
    low, high = pl.ds(0, half), pl.ds(half, half)
    width = w_src.shape[1]
    first_cols = qkv + AUX
    columns = (pl.ds(0, first_cols), pl.ds(first_cols, width - first_cols))
    waits, sent_on = [], []

    def near(k):
        return me.farthest(GRID_Z - 1 - k)

    def w_at(k, fx, p):
        return w_out.at[me.dp_at(near(k), fx, 0), :, columns[p]]

    def d_at(k, fx, fy, rows):
        return d_out.at[me.dp_at(near(k), fx, 0) * 2 + me.y_at(fy), rows]

    wide, narrow = query_w.shape[1], key_w.shape[1]
    loads = [
        pltpu.make_async_copy(source, target, load_s.at[i])
        for i, (source, target) in enumerate(
            (
                (context_w, flat_ctx),
                (router_t, flat_router),
                (prenorm, flat_gains.at[0]),
                (midnorm, flat_gains.at[1]),
                (querynorm, head_gains.at[0]),
                (keynorm, head_gains.at[1]),
                (routes_t, flat_routes),
                (query_w, w_src.at[:, pl.ds(0, wide)]),
                (key_w, w_src.at[:, pl.ds(wide, narrow)]),
                (value_w, w_src.at[:, pl.ds(wide + narrow, narrow)]),
                (cosine_in, cosine),
                (sine_in, sine),
            )
        )
    ]
    for copy in loads:
        copy.start()
    for copy in loads[:7]:
        copy.wait()
    count = head_gains.shape[2]
    top, block_rows = flat_routes.shape
    w_src[:, pl.ds(first_cols, width - first_cols)] = flat_ctx[...].astype(f32).T.astype(bf16)
    gains = jnp.concatenate(
        [
            flat_gains[0].astype(f32),
            flat_gains[1].astype(f32),
            dot(head_gains[0], placed(count, me.dp * count)),
            dot(head_gains[1], placed(count, me.dp * count)),
            jnp.zeros((4, AUX), f32),
        ],
        axis=0,
    ).T.astype(bf16)
    aux = dot(flat_router[...].astype(f32).T.astype(bf16), placed(experts, 0))
    aux = aux + dot(gains, placed(8, experts))
    for part in range(block_rows // AUX):
        some = flat_routes[:, part * AUX : (part + 1) * AUX].astype(f32).T.astype(bf16)
        aux = aux + dot(some, placed(top, experts + 4 + part * top))
    w_src[:, pl.ds(qkv, AUX)] = aux.astype(bf16)
    for copy in loads[7:]:
        copy.wait()
    for i, (source, target) in enumerate(
        (
            (w_src, w_out.at[me.dp]),
            (d_src, d_out.at[me.dp * 2 + me.y]),
            (x_src, x_out.at[me.y]),
        )
    ):
        copy = pltpu.make_async_copy(source, target, local_s.at[i])
        copy.start()
        waits.append(copy)
    me.greet()

    def line(k, source, target, sem, start_only):
        zn = near(k)
        for side, came, more, mate in (
            (0, zn < me.z, me.has_above, me.above),
            (1, zn > me.z, me.has_below, me.below),
        ):
            copy = remote(source, target, sem.at[0, side, zn], sem.at[1, side, zn], mate)
            if start_only:

                @pl.when(more)
                def _():
                    copy.start()
            else:

                @pl.when(came)
                def _():
                    copy.wait_recv()

                    @pl.when(more)
                    def _():
                        copy.start()

    def line_done(k, source, target, sem):
        zn = near(k)
        for side, came, more, mate in (
            (0, zn <= me.z, me.has_above, me.above),
            (1, zn >= me.z, me.has_below, me.below),
        ):
            copy = remote(source, target, sem.at[0, side, zn], sem.at[1, side, zn], mate)

            @pl.when(came)
            def _():
                @pl.when(more)
                def _():
                    copy.wait_send()

    def w_source(k, p):
        return w_src.at[:, columns[p]] if k == 0 else w_at(k, 0, p)

    def d_source(k, rows):
        return d_src.at[rows] if k == 0 else d_at(k, 0, 0, rows)

    def go(source, target, sem, index, mate):
        copy = remote(source, target, sem.at[(0, *index)], sem.at[(1, *index)], mate)
        copy.start()
        sent_on.append(copy)
        return copy

    def to_core(source, target, sem, index):
        go(source, target, sem, index, me.sibling)

    wx, ax, ay, by = {}, {}, {}, {}

    def w_own(k, p):
        line(k, w_source(k, p), w_at(k, 0, p), wz_s.at[p], k == 0)
        wx[k, p] = go(w_source(k, p), w_at(k, 0, p), wx_s, (k, p), me.x_mate)
        to_core(w_source(k, p), w_at(k, 0, p), wc_s, (k, 0, p))

    def w_across(k, p):
        wx[k, p].wait_recv()
        to_core(w_at(k, 1, p), w_at(k, 1, p), wc_s, (k, 1, p))

    def w_from_core(k, p):
        for fx in range(2):
            block = w_at(k, fx, p)
            remote(block, block, wc_s.at[0, k, fx, p], wc_s.at[1, k, fx, p], me.sibling).wait_recv()

    def a_over_y(k):
        ay[k, 0] = go(d_source(k, low), d_at(k, 0, 0, low), ay_s, (k, 0), me.y_mate)

    def a_own(k):
        line(k, d_source(k, low), d_at(k, 0, 0, low), az_s, k == 0)
        if k:
            a_over_y(k)
        ax[k] = go(d_source(k, low), d_at(k, 0, 0, low), ax_s, (k,), me.x_mate)
        to_core(d_source(k, low), d_at(k, 0, 0, low), dc_s, (k, 0, 0, 0))

    def a_across(k):
        ax[k].wait_recv()
        block = d_at(k, 1, 0, low)
        ay[k, 1] = go(block, block, ay_s, (k, 1), me.y_mate)
        to_core(block, block, dc_s, (k, 1, 0, 0))

    def b_own(k, fx):
        source = d_source(k, high) if fx == 0 else d_at(k, 1, 0, high)
        block = d_at(k, fx, 0, high)
        line(k, source, block, bz_s.at[fx], k == 0)
        by[k, fx] = go(source, block, by_s, (k, fx), me.y_mate)
        to_core(source, block, dc_s, (k, fx, 0, 1))

    def y_done(k, fx, h):
        (ay, by)[h][k, fx].wait_recv()
        block = d_at(k, fx, 1, (low, high)[h])
        to_core(block, block, dc_s, (k, fx, 1, h))

    rows, features = x.shape[0] * x.shape[1], x.shape[2]
    own_rows = rows // 2
    heads, key_heads = query.shape[0], key.shape[0]
    chunk = 512
    turn_c, turn_s = cosine[...], sine[...]
    held, outs, copies = {}, [], []

    def pair_rows():
        held["pair"] = go(x_src, x_out.at[me.y], pair_s, (0,), me.y_mate)

    def b_over_x():
        held["bx"] = go(d_src.at[high], d_at(0, 0, 0, high), bx_s, (0,), me.x_mate)

    def b_step(k, fx):
        if (k, fx) == (0, 1):
            held["bx"].wait_recv()
        b_own(k, fx)

    def prepare():
        held["pair"].wait_recv()
        waits[2].wait()
        for k in range(GRID_Z):
            w_from_core(k, 0)
        waits[0].wait()
        loads = [
            pltpu.make_async_copy(w_out.at[:, :, pl.ds(qkv, AUX)], aux_w, in_s.at[1]),
            pltpu.make_async_copy(x_out, x, in_s.at[0]),
        ]
        held["parts"] = [
            pltpu.make_async_copy(
                w_out.at[:, :, pl.ds(c * chunk, chunk)],
                w.at[:, :, pl.ds(c * chunk, chunk)],
                w_s.at[c],
            )
            for c in range(qkv // chunk)
        ]
        for copy in loads + held["parts"]:
            copy.start()
        loads[0].wait()
        aux_t = aux_w[...].reshape(features, AUX).astype(f32).T
        held["gains"] = gain_rows(aux_t, experts, features // HEAD_SIZE)
        gain_one = held["gains"][0]
        loads[1].wait()

        def one(i, carry):
            at = pl.ds(pl.multiple_of(i * 32, 32), 32)
            for part in range(2):
                stream = x[part, at, :].astype(f32)
                there = pl.ds(pl.multiple_of(part * own_rows + i * 32, 32), 32)
                normed[there, :] = (stream * inverse_norm(stream) * gain_one).astype(bf16)
            return carry

        lax.fori_loop(0, own_rows // 32, one, 0)

    def project():
        for c, copy in enumerate(held["parts"]):
            copy.wait()
            cols = slice(c * chunk, (c + 1) * chunk)
            got_raw = dot(normed[...], w[:, :, cols].reshape(features, chunk))
            for h in range(chunk // HEAD_SIZE):
                raw[c * (chunk // HEAD_SIZE) + h] = got_raw[:, h * HEAD_SIZE : (h + 1) * HEAD_SIZE]
        for g in range(key_heads):
            unnormed = raw[heads + g]
            gained = unnormed * inverse_norm(unnormed) * held["gains"][3]
            key[g] = turn(gained, turn_c, turn_s).astype(bf16)
            value[g] = raw[heads + key_heads + g].astype(bf16)

    def attend(part):
        allowed = allowed_pairs(lengths[sequence_order[me.dp]], rows)
        query_gain = held["gains"][2]

        def head(h, carry):
            g = h // (heads // key_heads)
            unnormed = raw[h]
            gained = unnormed * inverse_norm(unnormed) * query_gain
            turned = turn(gained, turn_c, turn_s).astype(bf16)
            query[h] = turned
            probs = probabilities(turned, key[g], allowed).astype(bf16)
            at = pl.ds(pl.multiple_of(h * HEAD_SIZE, HEAD_SIZE), HEAD_SIZE)
            context[:, at] = dot(probs, value[g]).astype(bf16)
            return carry

        share = heads // 4
        lax.fori_loop(part * share, (part + 1) * share, head, 0)

    def save(pairs):
        for source, target in pairs:
            copy = pltpu.make_async_copy(source, target, out_s.at[len(outs)])
            copy.start()
            outs.append(copy)

    def ctx_part(c):
        span = chunk // ctx.shape[1]
        return ctx[c * span : (c + 1) * span].reshape(chunk, ctx.shape[2])

    def output_over_y():
        save(
            (
                (normed, normed_o), (raw, raw_o), (query, query_o), (key, key_o),
                (value, value_o), (context, context_o),
            )
        )
        for k in range(GRID_Z):
            w_from_core(k, 1)
        load = pltpu.make_async_copy(w_out.at[:, :, columns[1]], ctx, in_s.at[2])
        load.start()
        load.wait()
        for c in range(features // chunk):
            cols = pl.ds(c * chunk, chunk)
            their_part, residual[:, cols] = split_pair(
                me, dot(context[...], ctx_part(c), ((1,), (1,)))
            )
            att[:, cols] = their_part.astype(bf16)
            copy = remote(att.at[:, cols], got.at[:, cols], y_s.at[0, c], y_s.at[1, c], me.y_mate)
            copy.start()
            copies.append(copy)

    def finish():
        for copy in copies:
            copy.wait_recv()
        gain_two = held["gains"][1]

        def second_norm(i, carry):
            at = pl.ds(pl.multiple_of(i * 16, 16), 16)
            total = x[me.y, at, :].astype(f32) + (residual[at, :] + got[at, :].astype(f32))
            residual[at, :] = total
            sent[at, pl.ds(0, features)] = (total * inverse_norm(total) * gain_two).astype(bf16)
            return carry

        lax.fori_loop(0, own_rows // 16, second_norm, 0)
        logits = dot(sent[:, :features], aux_w[...].reshape(features, AUX))
        own = flat_routes[:, pl.ds(pl.multiple_of(me.y * own_rows, own_rows), own_rows)]
        own = own.astype(f32).T
        lane = lax.broadcasted_iota(jnp.int32, (own_rows, AUX), 1).astype(f32)
        hits = [lane == own[:, j : j + 1] for j in range(top)]
        picked = functools.reduce(jnp.logical_or, hits)
        logits = jnp.where(picked, logits, masked_score)
        spread = jnp.where(picked, jnp.exp(logits - jnp.max(logits, axis=-1, keepdims=True)), 0.0)
        gates = spread / jnp.sum(spread, axis=-1, keepdims=True)
        coarse = gates.astype(bf16).astype(f32)
        sent[:, pl.ds(features, AUX)] = (coarse + pltpu.roll(gates - coarse, experts, 1)).astype(bf16)
        save(((sent, sent_o), (residual, residual_o)))

    third = 3 * own_rows // 8
    n_low, n_high = pl.ds(0, third), pl.ds(third, third)
    n_most, n_rest = pl.ds(0, 2 * third), pl.ds(2 * third, own_rows - 2 * third)
    nx, ny, ndx, ndy, cy = {}, {}, {}, {}, {}

    def n_at(k, fx, fy, rows):
        return rows_o.at[me.dp_at(near(k), fx, 0) * 2 + me.y_at(fy), rows]

    def n_source(k, rows):
        return sent.at[rows] if k == 0 else n_at(k, 0, 0, rows)

    def n_own(k):
        source, block = n_source(k, n_most), n_at(k, 0, 0, n_most)
        line(k, source, block, nz_s, k == 0)
        nx[k] = go(source, block, nx_s, (k,), me.x_mate)
        ny[k] = go(source, block, ny_s, (k,), me.y_mate)
        to_core(source, block, nc_s, (k, 0))
        if k == 0:
            copy = pltpu.make_async_copy(sent, rows_o.at[me.dp * 2 + me.y], nl_s.at[0])
            copy.start()
            outs.append(copy)

    def n_over_y(k):
        nx[k].wait_recv()
        block = n_at(k, 1, 0, n_low)
        ndy[k] = go(block, block, ndy_s, (k,), me.y_mate)
        block = n_at(k, 1, 0, n_most)
        to_core(block, block, nc_s, (k, 1))

    def n_over_x(k):
        ny[k].wait_recv()
        block = n_at(k, 0, 1, n_high)
        ndx[k] = go(block, block, ndx_s, (k,), me.x_mate)
        block = n_at(k, 0, 1, n_most)
        to_core(block, block, nc_s, (k, 2))

    def n_corner(k, copies, rows, index):
        copies[k].wait_recv()
        block = n_at(k, 1, 1, rows)
        to_core(block, block, nc_s, (k, index))

    def c_line(k, fx, fy, source=None):
        block = n_at(k, fx, fy, n_rest)
        source = block if source is None else source
        line(k, source, block, cz_s.at[fx, fy], k == 0)
        to_core(source, block, cc_s, (k, fx, fy))

    def c_own():
        source, block = sent.at[n_rest], n_at(0, 0, 0, n_rest)
        held["cx"] = go(source, block, cx_s, (0,), me.x_mate)
        cy[0] = go(source, block, cy_s, (0,), me.y_mate)
        c_line(0, 0, 0, source)

    def c_from_x():
        held["cx"].wait_recv()
        block = n_at(0, 1, 0, n_rest)
        cy[1] = go(block, block, cy_s, (1,), me.y_mate)
        c_line(0, 1, 0)

    def c_from_y(fx):
        cy[fx].wait_recv()
        c_line(0, fx, 1)

    actions = {
        "n": n_own, "nx": n_over_y, "ny": n_over_x,
        "nca": lambda k: n_corner(k, ndy, n_low, 3), "ncb": lambda k: n_corner(k, ndx, n_high, 4),
        "c0": c_own, "c1": c_from_x, "c2": c_from_y, "cz": c_line,
        "pair": pair_rows, "bx": b_over_x, "ay0": lambda: a_over_y(0), "w": w_own, "wx": w_across,
        "a": a_own, "ax": a_across, "b": b_step, "y1": y_done, "prep": prepare, "qkv": project,
        "h": attend, "ctx": output_over_y, "fin": finish,
    }
    for name, *which in OPENING_PLAN:
        actions[name](*which)
    for k in range(GRID_Z):
        for p in range(2):
            line_done(k, w_source(k, p), w_at(k, 0, p), wz_s.at[p])
        line_done(k, d_source(k, low), d_at(k, 0, 0, low), az_s)
        line_done(k, d_source(k, high), d_at(k, 0, 0, high), bz_s.at[0])
        line_done(k, d_at(k, 1, 0, high), d_at(k, 1, 0, high), bz_s.at[1])
        line_done(k, n_source(k, n_most), n_at(k, 0, 0, n_most), nz_s)
        for fx in range(2):
            for fy in range(2):
                source = n_source(k, n_rest) if (fx, fy) == (0, 0) else n_at(k, fx, fy, n_rest)
                line_done(k, source, n_at(k, fx, fy, n_rest), cz_s.at[fx, fy])
    for copy in sent_on + copies:
        copy.wait_send()
    for k in range(GRID_Z):
        for fx in range(2):
            for fy in range(2):
                for h, at in enumerate((low, high)):
                    block = d_at(k, fx, fy, at)
                    remote(
                        block, block, dc_s.at[0, k, fx, fy, h], dc_s.at[1, k, fx, fy, h], me.sibling
                    ).wait_recv()
            for fy in range(2):
                block = n_at(k, fx, fy, n_rest)
                remote(
                    block, block, cc_s.at[0, k, fx, fy], cc_s.at[1, k, fx, fy], me.sibling
                ).wait_recv()
        for i, (fx, fy, at) in enumerate(
            ((0, 0, n_most), (1, 0, n_most), (0, 1, n_most), (1, 1, n_low), (1, 1, n_high))
        ):
            block = n_at(k, fx, fy, at)
            remote(block, block, nc_s.at[0, k, i], nc_s.at[1, k, i], me.sibling).wait_recv()
    waits[1].wait()
    for copy in outs:
        copy.wait()


def opening(
    lengths, sequence_order, weights, gains, routes, cotangents, inputs, experts, collective_id
):
    bf16, f32 = jnp.bfloat16, jnp.float32
    chips, pair = lax.axis_size("dp"), lax.axis_size("tensor")
    own_rows, features = inputs.shape
    rows = pair * own_rows
    query, key, value, context, router = weights
    shard, wide = query.shape
    heads, key_heads = wide // HEAD_SIZE, key.shape[1] // HEAD_SIZE
    width = 2 * wide + 2 * key.shape[1] + AUX
    count, top = gains[2].shape[0], routes.shape[1]
    qkv = (heads + 2 * key_heads) * HEAD_SIZE
    cosine, sine = turn_tables(rows)
    dma = pltpu.SemaphoreType.DMA
    shapes = (
        ((chips, shard, width), bf16),
        ((chips * pair, *cotangents.shape), bf16),
        ((pair, *inputs.shape), bf16),
        ((chips * pair, own_rows, features + AUX), bf16),
        ((own_rows, features + AUX), bf16),
        ((own_rows, features), f32),
        ((rows, features), bf16),
        ((heads + 2 * key_heads, rows, HEAD_SIZE), f32),
        ((heads, rows, HEAD_SIZE), bf16),
        ((key_heads, rows, HEAD_SIZE), bf16),
        ((key_heads, rows, HEAD_SIZE), bf16),
        ((rows, wide), bf16),
    )
    anywhere, smem = pl.BlockSpec(memory_space=pl.ANY), pl.BlockSpec(memory_space=pltpu.SMEM)
    w, d, x, gathered, *rest = pl.pallas_call(
        functools.partial(opening_kernel, experts, qkv),
        out_shape=tuple(jax.ShapeDtypeStruct(*shape) for shape in shapes),
        in_specs=[smem] * 2 + [anywhere] * 14,
        out_specs=(anywhere,) * len(shapes),
        scratch_shapes=[
            pltpu.VMEM((pair, own_rows, features), bf16),
            pltpu.VMEM((chips, shard, qkv), bf16),
            pltpu.VMEM((chips, shard, wide), bf16),
            pltpu.VMEM((chips, shard, AUX), bf16),
            pltpu.VMEM((rows, features), bf16),
            pltpu.VMEM((heads + 2 * key_heads, rows, HEAD_SIZE), f32),
            pltpu.VMEM((heads, rows, HEAD_SIZE), bf16),
            pltpu.VMEM((key_heads, rows, HEAD_SIZE), bf16),
            pltpu.VMEM((key_heads, rows, HEAD_SIZE), bf16),
            pltpu.VMEM((rows, wide), bf16),
            pltpu.VMEM((own_rows, features), bf16),
            pltpu.VMEM((own_rows, features), bf16),
            pltpu.VMEM((own_rows, features), f32),
            pltpu.VMEM((own_rows, features + AUX), bf16),
            dma((3,)),
            dma((2, 1)),
            dma((2, 2, 2, 4)),
            dma((2, 4, 2)),
            dma((2, 4, 2, 2)),
            dma((2, 2, 4)),
            dma((2, 4)),
            dma((2, 4, 2)),
            dma((2, 2, 2, 4)),
            dma((2, 1)),
            dma((2, 4, 2)),
            dma((2, 4, 2, 2, 2)),
            dma((3,)),
            dma((qkv // 512,)),
            dma((8,)),
            dma((2, features // 512)),
            pltpu.VMEM((shard, width), bf16),
            pltpu.VMEM(context.shape, bf16),
            pltpu.VMEM((experts, shard), bf16),
            pltpu.VMEM((2, 1, shard), bf16),
            pltpu.VMEM((2, 1, count), bf16),
            pltpu.VMEM((top, rows), jnp.int32),
            pltpu.VMEM((rows, HEAD_SIZE), f32),
            pltpu.VMEM((rows, HEAD_SIZE), f32),
            dma((12,)),
            dma((1,)),
            dma((2, 2, 4)),
            dma((2, 4)),
            dma((2, 4)),
            dma((2, 4)),
            dma((2, 4)),
            dma((2, 4, 5)),
            dma((2, 1)),
            dma((2, 2)),
            dma((2, 2, 2, 2, 4)),
            dma((2, 4, 2, 2)),
        ],
        compiler_params=pltpu.CompilerParams(
            collective_id=collective_id, has_side_effects=True, vmem_limit_bytes=ATTENTION_VMEM
        ),
    )(
        lengths, sequence_order, query, key, value, context, router.T,
        *(gain[None] for gain in gains), routes.T, cotangents, inputs, cosine, sine,
    )
    return (
        w.reshape(-1, w.shape[2]),
        d.reshape(chips, -1, d.shape[2]),
        x.reshape(-1, x.shape[2]),
        gathered.reshape(chips, -1, gathered.shape[2]),
        *rest,
    )


def unturn(value, cosine, sine):
    return value * cosine - pltpu.roll(value, HEAD_SIZE // 2, 1) * sine


def backward_kernel(
    experts, lengths, sequence_order, back_in, residual_in, sent_in, dy_in, x_in, packed,
    cosine_in, sine_in, normed_in,
    raw_in, query_in, key_in, value_in, context_in,
    grads, input_gradient,
    back, residual, sent, dy, x, w, ctx, aux_w, normed, raw, query, key, value, context,
    cot, context_cot, raw_cot, key_sum, value_sum, small, first, first_got, stage, result,
    cosine, sine, probs, own_first, in_s, out_s, y_s, g_s,
):
    bf16, f32 = jnp.bfloat16, jnp.float32
    me = Place()
    own_rows, features = residual.shape
    rows = 2 * own_rows
    heads, key_heads = query.shape[0], key.shape[0]
    group = heads // key_heads
    qkv, wide = w.shape[1], heads * HEAD_SIZE
    chunk = 512
    loads = [
        pltpu.make_async_copy(source, target, in_s.at[i])
        for i, (source, target) in enumerate(
            (
                (packed.at[:, pl.ds(qkv, AUX)], aux_w),
                (back_in, back),
                (sent_in, sent),
                (residual_in, residual),
                (dy_in, dy),
                (packed.at[:, pl.ds(qkv + AUX, wide)], ctx),
                (context_in, context),
                (value_in, value),
                (key_in, key),
                (query_in, query),
                (raw_in, raw),
                (packed.at[:, pl.ds(0, qkv)], w),
                (normed_in, normed),
                (x_in, x),
                (cosine_in, cosine),
                (sine_in, sine),
            )
        )
    ]
    for copy in loads:
        copy.start()
    meet_y(me)
    for copy in loads[:5]:
        copy.wait()
    aux_t = aux_w[...].astype(f32).T
    gain_one, gain_two, query_gain, key_gain = gain_rows(aux_t, experts, features // HEAD_SIZE)

    lane = lax.broadcasted_iota(jnp.int32, (own_rows, AUX), 1)
    coded = sent[:, features:].astype(f32)
    gates = coded + pltpu.roll(coded, AUX - experts, 1)
    gates = jnp.where(lane < experts, gates, 0.0)
    column = lax.broadcasted_iota(jnp.int32, (AUX, AUX), 0)
    target = lax.broadcasted_iota(jnp.int32, (AUX, AUX), 1)
    fold = ((column % (2 * experts)) // 2 == target).astype(bf16)
    gate_cot = dot(back[:, features:], fold)
    logit_cot = gates * (gate_cot - jnp.sum(gates * gate_cot, axis=-1, keepdims=True))
    logit_cot = logit_cot.astype(bf16)
    small[...] = dot(sent[:, :features], logit_cot, ((0,), (0,)))
    midnorm = jnp.zeros((1, features), f32)
    step, swaps = 32, []
    for i in range(own_rows // step):
        at = slice(i * step, (i + 1) * step)
        total = residual[at, :]
        scale = inverse_norm(total)
        unit = total * scale
        normed_cot = back[at, :features].astype(f32) + dot(
            logit_cot[at, :], aux_w[...], ((1,), (1,))
        )
        midnorm = midnorm + jnp.sum(normed_cot * unit, axis=0, keepdims=True)
        gained = normed_cot * gain_two
        total_cot = dy[at, :].astype(f32) + scale * (
            gained - unit * jnp.mean(gained * unit, axis=-1, keepdims=True)
        )
        residual[at, :] = total_cot
        there = pl.ds(pl.multiple_of(me.y * own_rows + i * step, step), step)
        cot[there, :] = total_cot.astype(bf16)
        swap = remote(cot.at[there], cot.at[there], y_s.at[0, i], y_s.at[1, i], me.y_mate)
        swap.start()
        swaps.append(swap)
    for copy in loads[5:10]:
        copy.wait()

    allowed = allowed_pairs(lengths[sequence_order[me.dp]], rows)

    def recall(h, carry):
        probs[h] = probabilities(query[h], key[h // group], allowed)
        return carry

    lax.fori_loop(0, heads, recall, 0, unroll=2)
    for swap in swaps:
        swap.wait_recv()
    for c in range(wide // chunk):
        cols = pl.ds(c * chunk, chunk)
        context_cot[:, cols] = dot(cot[...], ctx[:, cols]).astype(bf16)
    for copy in loads[10:]:
        copy.wait()

    turn_c, turn_s = cosine[...], sine[...]
    key_sum[...] = jnp.zeros_like(key_sum)
    value_sum[...] = jnp.zeros_like(value_sum)

    def raw_back(back_rows, unnormed, gain):
        scale = inverse_norm(unnormed)
        unit = unnormed * scale
        part = jnp.sum(back_rows * unit, axis=0, keepdims=True)
        gained = back_rows * gain
        raw_rows = scale * (gained - unit * jnp.mean(gained * unit, axis=-1, keepdims=True))
        return raw_rows.astype(bf16), part

    def head(h, query_part):
        g = h // group
        at = pl.ds(pl.multiple_of(h * HEAD_SIZE, HEAD_SIZE), HEAD_SIZE)
        soft = probs[h]
        cots = context_cot[:, at]
        prob_cot = dot(cots, value[g], ((1,), (1,)))
        score_cot = soft * (prob_cot - jnp.sum(soft * prob_cot, axis=-1, keepdims=True))
        score_cot = score_cot.astype(bf16)
        value_sum[g] += dot(soft.astype(bf16), cots, ((0,), (0,)))
        key_sum[g] += dot(score_cot, query[h], ((0,), (0,)))
        turned = dot(score_cot, key[g]) * SCORE_SCALE
        raw_cot[:, at], part = raw_back(unturn(turned, turn_c, turn_s), raw[h], query_gain)
        return query_part + part

    query_part = lax.fori_loop(0, heads, head, jnp.zeros((1, HEAD_SIZE), f32), unroll=2)
    key_part = jnp.zeros((1, HEAD_SIZE), f32)
    for g in range(key_heads):
        turned = key_sum[g] * SCORE_SCALE
        at = wide + g * HEAD_SIZE
        raw_cot[:, at : at + HEAD_SIZE], part = raw_back(
            unturn(turned, turn_c, turn_s), raw[heads + g], key_gain
        )
        key_part = key_part + part
        at = at + key_heads * HEAD_SIZE
        raw_cot[:, at : at + HEAD_SIZE] = value_sum[g].astype(bf16)

    copies = []
    for c in range(features // chunk):
        cols = pl.ds(c * chunk, chunk)
        their_part, own_first[:, cols] = split_pair(
            me, dot(raw_cot[...], w[cols, :], ((1,), (1,)))
        )
        first[:, cols] = their_part.astype(bf16)
        copy = remote(
            first.at[:, cols], first_got.at[:, cols], y_s.at[0, len(swaps) + c], y_s.at[1, len(swaps) + c], me.y_mate
        )
        copy.start()
        copies.append(copy)
    block = stage.shape[1]

    def store(i):
        slot = i % 2
        return pltpu.make_async_copy(
            stage.at[slot],
            grads.at[pl.ds(pl.multiple_of(i * block, block), block), pl.ds(0, qkv + wide)],
            g_s.at[slot],
        )

    def weight_grads(i, carry):
        slot = i % 2
        at = pl.ds(pl.multiple_of(i * block, block), block)

        @pl.when(i >= 2)
        def _():
            store(i - 2).wait()

        normed_t = normed[:, at].astype(f32).T.astype(bf16)
        cot_t = cot[:, at].astype(f32).T.astype(bf16)
        for c in range(qkv // chunk):
            cols = pl.ds(c * chunk, chunk)
            stage[slot, :, cols] = dot(normed_t, raw_cot[:, cols]).astype(bf16)
        for c in range(wide // chunk):
            cols = pl.ds(c * chunk, chunk)
            stage[slot, :, pl.ds(qkv + c * chunk, chunk)] = dot(cot_t, context[:, cols]).astype(bf16)
        store(i).start()
        return carry

    lax.fori_loop(0, features // block, weight_grads, 0)
    prenorm = jnp.zeros((1, features), f32)
    for copy in copies:
        copy.wait_recv()
    for c in range(features // chunk):
        cols = pl.ds(c * chunk, chunk)
        result_part = own_first[:, cols] + first_got[:, cols].astype(f32)
        back[:, cols] = result_part.astype(bf16)
    step = 32
    for i in range(own_rows // step):
        at = slice(i * step, (i + 1) * step)
        stream = x[pl.ds(pl.multiple_of(me.y * own_rows + i * step, step), step), :].astype(f32)
        scale = inverse_norm(stream)
        unit = stream * scale
        first_cot = back[at, :features].astype(f32)
        prenorm = prenorm + jnp.sum(first_cot * unit, axis=0, keepdims=True)
        gained = first_cot * gain_one
        result[at, :] = (
            residual[at, :]
            + scale * (gained - unit * jnp.mean(gained * unit, axis=-1, keepdims=True))
        ).astype(bf16)
    done = pltpu.make_async_copy(result, input_gradient, out_s.at[0])
    done.start()
    chunks = features // HEAD_SIZE
    extra = jnp.concatenate(
        [
            jnp.zeros((experts, features), f32),
            prenorm,
            midnorm,
            jnp.concatenate([query_part] * chunks, axis=1),
            jnp.concatenate([key_part] * chunks, axis=1),
            jnp.zeros((AUX - experts - 4, features), f32),
        ],
        axis=0,
    )
    aux_w[...] = (small[...] + extra.T).astype(bf16)
    last = pltpu.make_async_copy(aux_w, grads.at[:, pl.ds(qkv + wide, AUX)], out_s.at[1])
    last.start()
    for swap in swaps:
        swap.wait_send()
    for copy in copies:
        copy.wait_send()
    for i in (2, 1):
        store(features // block - i).wait()
    done.wait()
    last.wait()


def attention_backward(
    lengths, sequence_order, back, residual, sent, dy, x_pair, packed, saved, experts, collective_id
):
    bf16, f32 = jnp.bfloat16, jnp.float32
    normed, raw, query, key, value, context = saved
    own_rows, features = residual.shape
    rows = 2 * own_rows
    heads, key_heads = query.shape[0], key.shape[0]
    wide = heads * HEAD_SIZE
    qkv = wide + 2 * key_heads * HEAD_SIZE
    cosine, sine = turn_tables(rows)
    dma = pltpu.SemaphoreType.DMA
    anywhere, smem = pl.BlockSpec(memory_space=pl.ANY), pl.BlockSpec(memory_space=pltpu.SMEM)
    return pl.pallas_call(
        functools.partial(backward_kernel, experts),
        out_shape=(
            jax.ShapeDtypeStruct((features, qkv + wide + AUX), bf16),
            jax.ShapeDtypeStruct((own_rows, features), bf16),
        ),
        in_specs=[smem] * 2 + [anywhere] * 14,
        out_specs=(anywhere,) * 2,
        scratch_shapes=[
            pltpu.VMEM((own_rows, features + AUX), bf16),
            pltpu.VMEM((own_rows, features), f32),
            pltpu.VMEM((own_rows, features + AUX), bf16),
            pltpu.VMEM((own_rows, features), bf16),
            pltpu.VMEM((rows, features), bf16),
            pltpu.VMEM((features, qkv), bf16),
            pltpu.VMEM((features, wide), bf16),
            pltpu.VMEM((features, AUX), bf16),
            pltpu.VMEM((rows, features), bf16),
            pltpu.VMEM((heads + 2 * key_heads, rows, HEAD_SIZE), f32),
            pltpu.VMEM((heads, rows, HEAD_SIZE), bf16),
            pltpu.VMEM((key_heads, rows, HEAD_SIZE), bf16),
            pltpu.VMEM((key_heads, rows, HEAD_SIZE), bf16),
            pltpu.VMEM((rows, wide), bf16),
            pltpu.VMEM((rows, features), bf16),
            pltpu.VMEM((rows, wide), bf16),
            pltpu.VMEM((rows, qkv), bf16),
            pltpu.VMEM((key_heads, rows, HEAD_SIZE), f32),
            pltpu.VMEM((key_heads, rows, HEAD_SIZE), f32),
            pltpu.VMEM((features, AUX), f32),
            pltpu.VMEM((own_rows, features), bf16),
            pltpu.VMEM((own_rows, features), bf16),
            pltpu.VMEM((2, 512, qkv + wide), bf16),
            pltpu.VMEM((own_rows, features), bf16),
            pltpu.VMEM((rows, HEAD_SIZE), f32),
            pltpu.VMEM((rows, HEAD_SIZE), f32),
            pltpu.VMEM((heads, rows, rows), f32),
            pltpu.VMEM((own_rows, features), f32),
            dma((16,)),
            dma((2,)),
            dma((2, own_rows // 32 + features // 512)),
            dma((2,)),
        ],
        compiler_params=pltpu.CompilerParams(
            collective_id=collective_id, has_side_effects=True, vmem_limit_bytes=ATTENTION_VMEM
        ),
    )(
        lengths, sequence_order, back, residual, sent, dy, x_pair, packed, cosine, sine,
        normed, raw, query, key, value, context,
    )


LAST_CUT = 6
LAST_PLAN = (
    ("gx", 0, 1), ("dy", 0, 1, 1), ("hz", 0, 1), ("dy", 0, 0, 1), ("hz", 0, 0), ("gx", 0, 0),
    ("dy", 0, 1, 0), ("hz", 1, 1), ("db", 0, 0), ("db", 0, 1), ("hz", 2, 1), ("hz", 1, 0),
    ("gx", 1, 0), ("dy", 1, 1, 1), ("dy", 1, 1, 0), ("dy", 0, 0, 0), ("db", 1, 1),
    ("dy", 2, 1, 0), ("dax", 0), ("gx", 1, 1), ("gx", 2, 1), ("dy", 1, 0, 1), ("hz", 2, 0),
    ("gc", 0), ("dax", 1), ("dy", 2, 0, 1), ("dy", 2, 0, 0), ("da", 0), ("gx", 2, 0),
    ("dy", 3, 1, 0), ("dy", 3, 0, 0), ("db", 1, 0), ("dy", 2, 1, 1), ("gc", 1), ("dy", 1, 0, 0),
    ("gx", 3, 1), ("dy", 3, 1, 1), ("gx", 3, 0), ("hz", 3, 1), ("hz", 3, 0), ("db", 2, 1),
    ("hx",), ("dax", 2), ("dy", 3, 0, 1), ("gc", 2), ("da", 1), ("gc", 3), ("db", 2, 0),
    ("dax", 3), ("da", 2), ("hend",), ("sm",), ("db", 3, 1), ("db", 3, 0), ("sm2",), ("da", 3),
    ("bx",),
)


def last_scatter_kernel(
    g_part, d_part, g_out, d_out,
    g_own, g_core, g_x, g_z, d_own, d_core, d_y, a_x, b_x, a_z, b_z, small_got, h_z, h_x,
    gl_s, gc_s, gx_s, gz_s, dl_s, dc_s, dy_s, ax_s, bx_s, az_s, bz_s, small_s, hz_s, hx_s, out_s,
):
    me = Place()
    g_rows, d_rows = g_own.shape[2], d_own.shape[3]
    cut, g_most = a_x.shape[1], g_x.shape[1]
    g_half = g_rows // 2
    g_spans = ((0, g_half), (g_half, g_most - g_half))
    g_all, g_rest = (0, g_most), (g_most, g_rows - g_most)
    g_all_at, g_rest_at = pl.ds(*g_all), pl.ds(*g_rest)
    low, high = (0, cut), (cut, d_rows - cut)
    low_at, high_at = pl.ds(0, cut), pl.ds(cut, d_rows - cut)
    last = GRID_Z - 1
    loads, cores, sends = {}, {}, []

    def g_chunk(k, fx, fc):
        return g_part.at[me.dp_at(me.farthest(k), fx, fc)]

    def d_chunk(k, fx, fy, fc):
        return d_part.at[me.dp_at(me.farthest(k), fx, fc) * 2 + me.y_at(fy)]

    pairs = ((1, 1), (0, 1), (1, 0), (0, 0))
    for k in range(GRID_Z):
        for fx in (1, 0):
            loads[k, fx] = pltpu.make_async_copy(g_chunk(k, fx, 0), g_own.at[k, fx], gl_s.at[k, fx])
            loads[k, fx].start()
        for fx, fy in pairs:
            loads[k, fx, fy] = pltpu.make_async_copy(
                d_chunk(k, fx, fy, 0), d_own.at[k, fx, fy], dl_s.at[k, fx, fy]
            )
            loads[k, fx, fy].start()
    me.greet()
    for k in range(GRID_Z):
        for fx in (1, 0):
            cores[k, fx] = remote(
                g_chunk(k, fx, 1), g_core.at[k, fx],
                gc_s.at[0, k, fx], gc_s.at[1, k, fx], me.sibling,
            )
        for fx, fy in pairs:
            cores[k, fx, fy] = remote(
                d_chunk(k, fx, fy, 1), d_core.at[k, fx, fy],
                dc_s.at[0, k, fx, fy], dc_s.at[1, k, fx, fy], me.sibling,
            )
        for index in ((1,), (1, 1), (0, 1), (0,), (1, 0), (0, 0)):
            cores[(k, *index)].start()

    gx = [
        [
            remote(
                g_own.at[k, 1, pl.ds(*g_spans[h])], g_x.at[k, pl.ds(*g_spans[h])],
                gx_s.at[0, k, h], gx_s.at[1, k, h], me.x_mate,
            )
            for h in range(2)
        ]
        for k in range(GRID_Z)
    ]
    dy = {
        (k, fx, h): remote(
            d_own.at[k, fx, 1, at], d_y.at[k, fx, at],
            dy_s.at[0, k, fx, h], dy_s.at[1, k, fx, h], me.y_mate,
        )
        for k in range(GRID_Z)
        for fx in range(2)
        for h, at in enumerate((low_at, high_at))
    }
    ax = [
        remote(d_own.at[k, 1, 0, low_at], a_x.at[k], ax_s.at[0, k], ax_s.at[1, k], me.x_mate)
        for k in range(GRID_Z)
    ]
    bx = remote(d_own.at[last, 1, 0, high_at], b_x, bx_s.at[0], bx_s.at[1], me.x_mate)

    here = set()

    def arrive(*index):
        if index not in here:
            here.add(index)
            loads[index].wait()
            cores[index].wait_recv()

    def onward(source, buffer, sem, to, side, mate):
        ends = 1 - (me.z - 1 - to + GRID_Z - 1) // GRID_Z
        slot = to if side == 0 else to + (GRID_Z - to) * ends
        return remote(source, buffer.at[slot], sem.at[0, to], sem.at[1, slot], mate)

    def line(k, block, source, rows, buffer, sem, shift):
        to = me.farthest(k)
        for side, ahead, mate, more in (
            (0, to > me.z, me.above, me.has_below),
            (1, to < me.z, me.below, me.has_above),
        ):
            slot = to if k < last or side == 0 else GRID_Z
            came = remote(source, buffer.at[slot], sem.at[0, slot], sem.at[1, slot], mate)

            def gather(came=came, slot=slot):
                came.wait_recv()
                add_rows(block, [(buffer.at[slot], shift)], rows)

            if k < last:

                @pl.when(ahead)
                def _():
                    pl.when(more)(gather)
                    onward(source, buffer, sem, to, side, mate).start()
            else:
                pl.when(more)(gather)

    def line_done(k, source, buffer, sem):
        to = me.farthest(k)
        for side, ahead, mate in ((0, to > me.z, me.above), (1, to < me.z, me.below)):

            @pl.when(ahead)
            def _():
                onward(source, buffer, sem, to, side, mate).wait_send()

    width = g_own.shape[3]
    small_block = g_own.at[last, 0, :, pl.ds(width - AUX, AUX)]
    small = remote(small_block, small_got, small_s.at[0], small_s.at[1], me.y_mate)

    def g_across(k, h):
        arrive(k, 1)
        add_rows(g_own.at[k, 1], [(g_core.at[k, 1], 0)], g_spans[h])
        gx[k][h].start()

    def g_column(k):
        arrive(k, 0)
        for h in range(2):
            gx[k][h].wait_recv()
        add_rows(g_own.at[k, 0], [(g_core.at[k, 0], 0), (g_x.at[k], 0)], g_all)
        block = g_own.at[k, 0]
        line(k, block, block.at[g_all_at], g_all, g_z, gz_s, 0)

    def rest_line(k, fx):
        arrive(k, fx)
        block = g_own.at[k, fx]
        add_rows(block, [(g_core.at[k, fx], 0)], g_rest)
        line(k, block, block.at[g_rest_at], g_rest, h_z.at[fx], hz_s.at[fx], g_most)

    rest_x = remote(g_own.at[last, 1, g_rest_at], h_x, hx_s.at[0], hx_s.at[1], me.x_mate)

    def rest_end():
        rest_x.wait_recv()
        add_rows(g_own.at[last, 0], [(h_x, g_most)], g_rest)

    def over_y(k, fx, h):
        arrive(k, fx, 1)
        add_rows(d_own.at[k, fx, 1], [(d_core.at[k, fx, 1], 0)], (low, high)[h])
        dy[k, fx, h].start()

    def from_y(k, fx, h, *more):
        arrive(k, fx, 0)
        dy[k, fx, h].wait_recv()
        rest = [(d_core.at[k, fx, 0], 0), (d_y.at[k, fx], 0), *more]
        add_rows(d_own.at[k, fx, 0], rest, (low, high)[h])

    def b_line(k, fx):
        from_y(k, fx, 1)
        block = d_own.at[k, fx, 0]
        line(k, block, block.at[high_at], high, b_z.at[fx], bz_s.at[fx], cut)
        if fx and k == last:
            bx.start()

    def a_over_x(k):
        from_y(k, 1, 0)
        ax[k].start()

    def a_line(k):
        ax[k].wait_recv()
        from_y(k, 0, 0, (a_x.at[k], 0))
        block = d_own.at[k, 0, 0]
        line(k, block, block.at[low_at], low, a_z, az_s, 0)

    def b_from_x():
        bx.wait_recv()
        add_rows(d_own.at[last, 0, 0], [(b_x, cut)], high)

    def small_sum():
        small.wait()
        total = small_block[...].astype(jnp.float32) + small_got[...].astype(jnp.float32)
        small_block[...] = total.astype(small_got.dtype)

    actions = {
        "gx": g_across, "gc": g_column, "dy": over_y, "db": b_line, "dax": a_over_x, "da": a_line,
        "bx": b_from_x, "hz": rest_line, "hx": rest_x.start, "hend": rest_end, "sm": small.start, "sm2": small_sum,
    }
    for name, *which in LAST_PLAN:
        actions[name](*which)
    outs = [
        pltpu.make_async_copy(d_own.at[last, 0, 0], d_out, out_s.at[0]),
        pltpu.make_async_copy(g_own.at[last, 0], g_out, out_s.at[1]),
    ]
    for copy in outs:
        copy.start()
    for k in range(GRID_Z):
        for h in range(2):
            gx[k][h].wait_send()
        for fx in range(2):
            for h in range(2):
                dy[k, fx, h].wait_send()
        ax[k].wait_send()
        if k < last:
            line_done(k, g_own.at[k, 0, g_all_at], g_z, gz_s)
            for fx in range(2):
                line_done(k, g_own.at[k, fx, g_rest_at], h_z.at[fx], hz_s.at[fx])
                line_done(k, d_own.at[k, fx, 0, high_at], b_z.at[fx], bz_s.at[fx])
            line_done(k, d_own.at[k, 0, 0, low_at], a_z, az_s)
    bx.wait_send()
    rest_x.wait_send()
    for sent in cores.values():
        sent.wait_send()
    for copy in outs:
        copy.wait()


def last_scatter(grads, sums, collective_id):
    chips, pair = lax.axis_size("dp"), lax.axis_size("tensor")
    g_rows, g_wide = grads.shape[0] // chips, grads.shape[1]
    d_rows, d_wide = sums.shape[0] // (chips * pair), sums.shape[1]
    cut, most = d_rows * LAST_CUT // 8, 7 * g_rows // 8
    dma = pltpu.SemaphoreType.DMA
    low = grads.dtype
    anywhere = pl.BlockSpec(memory_space=pl.ANY)
    return pl.pallas_call(
        last_scatter_kernel,
        out_shape=(
            jax.ShapeDtypeStruct((g_rows, g_wide), low),
            jax.ShapeDtypeStruct((d_rows, d_wide), low),
        ),
        in_specs=[anywhere] * 2,
        out_specs=(anywhere,) * 2,
        scratch_shapes=[
            pltpu.VMEM((4, 2, g_rows, g_wide), low),
            pltpu.VMEM((4, 2, g_rows, g_wide), low),
            pltpu.VMEM((4, most, g_wide), low),
            pltpu.VMEM((5, most, g_wide), low),
            pltpu.VMEM((4, 2, 2, d_rows, d_wide), low),
            pltpu.VMEM((4, 2, 2, d_rows, d_wide), low),
            pltpu.VMEM((4, 2, d_rows, d_wide), low),
            pltpu.VMEM((4, cut, d_wide), low),
            pltpu.VMEM((d_rows - cut, d_wide), low),
            pltpu.VMEM((5, cut, d_wide), low),
            pltpu.VMEM((2, 5, d_rows - cut, d_wide), low),
            pltpu.VMEM((g_rows, AUX), low),
            pltpu.VMEM((2, 5, g_rows - most, g_wide), low),
            pltpu.VMEM((g_rows - most, g_wide), low),
            dma((4, 2)),
            dma((2, 4, 2)),
            dma((2, 4, 2)),
            dma((2, 5)),
            dma((4, 2, 2)),
            dma((2, 4, 2, 2)),
            dma((2, 4, 2, 2)),
            dma((2, 4)),
            dma((2,)),
            dma((2, 5)),
            dma((2, 2, 5)),
            dma((2,)),
            dma((2, 2, 5)),
            dma((2,)),
            dma((2,)),
        ],
        compiler_params=pltpu.CompilerParams(
            collective_id=collective_id, has_side_effects=True, vmem_limit_bytes=60 * 1024 * 1024
        ),
    )(grads.reshape(chips, g_rows, g_wide), sums.reshape(chips * pair, d_rows, d_wide))


def unpack_kernel(
    experts, summed, added, residual,
    layer_output, query, key, value, context, router, prenorm, midnorm, querynorm, keynorm,
):
    f32 = jnp.float32
    wide, narrow = query.shape[1], key.shape[1]
    layer_output[...] = (residual[...] + added[...].astype(f32)).astype(layer_output.dtype)
    query[...] = summed[:, pl.ds(0, wide)].astype(f32)
    key[...] = summed[:, pl.ds(wide, narrow)].astype(f32)
    value[...] = summed[:, pl.ds(wide + narrow, narrow)].astype(f32)
    start = wide + 2 * narrow
    context[...] = summed[:, pl.ds(start, wide)].astype(f32).T
    small = summed[:, pl.ds(start + wide, AUX)].astype(f32)
    router[...] = small[:, :experts]
    rows = small.T
    prenorm[...] = rows[experts : experts + 1, :]
    midnorm[...] = rows[experts + 1 : experts + 2, :]
    count = querynorm.shape[1]
    lane = lax.broadcasted_iota(jnp.int32, (count, AUX), 1)
    row = lax.broadcasted_iota(jnp.int32, (count, AUX), 0)
    pick = row + lax.axis_index("dp") * count == lane
    for target, at in ((querynorm, experts + 2), (keynorm, experts + 3)):
        part = jnp.where(pick, rows[at : at + 1, :], 0.0)
        target[...] = jnp.sum(part, axis=1, keepdims=True).T


def unpack(summed, added, residual, query_width, key_width, experts, norm_part):
    bf16, f32 = jnp.bfloat16, jnp.float32
    shard = summed.shape[0]
    own_rows, features = residual.shape
    shapes = (
        ((own_rows, features), bf16),
        ((shard, query_width), f32),
        ((shard, key_width), f32),
        ((shard, key_width), f32),
        ((query_width, shard), f32),
        ((shard, experts), f32),
        ((1, shard), f32),
        ((1, shard), f32),
        ((1, norm_part), f32),
        ((1, norm_part), f32),
    )
    vmem = pl.BlockSpec(memory_space=pltpu.VMEM)
    *large, first, second, third, fourth = pl.pallas_call(
        functools.partial(unpack_kernel, experts),
        out_shape=tuple(jax.ShapeDtypeStruct(*shape) for shape in shapes),
        in_specs=[vmem] * 3,
        out_specs=(vmem,) * len(shapes),
        compiler_params=pltpu.CompilerParams(vmem_limit_bytes=32 * 1024 * 1024),
    )(summed, added, residual)
    return (*large, first[0], second[0], third[0], fourth[0])


def gathered_body(
    layer_input,
    query_weight,
    key_projection,
    value_projection,
    context_weight,
    router_weight,
    expert_gate,
    expert_up,
    expert_down,
    prenorm_gain,
    midnorm_gain,
    querynorm_gain,
    keynorm_gain,
    routes,
    lengths,
    sequence_order,
    output_cotangent,
):
    bf16, f32 = jnp.bfloat16, jnp.float32
    tensor_count = lax.axis_size("tensor")
    tensor_index = lax.axis_index("tensor")
    dp_count = lax.axis_size("dp")
    dp_index = lax.axis_index("dp")
    own_rows, features = layer_input.shape
    block_rows = own_rows * tensor_count
    tokens = block_rows * dp_count
    expert_count = EXP_DEV * dp_count
    capacity = 3 * block_rows * TOP // (4 * EXP_DEV)
    most_rows = (5 * block_rows * TOP + 4 * expert_count - 1) // (4 * expert_count)
    shard = features // dp_count
    query_width = query_weight.shape[1]
    key_width = key_projection.shape[1]
    norm_part = HEAD_SIZE // dp_count

    packed, cot_all, input_rows, normed_all, sent, residual, *saved = opening(
        lengths,
        sequence_order,
        (query_weight, key_projection, value_projection, context_weight, router_weight),
        (prenorm_gain, midnorm_gain, querynorm_gain, keynorm_gain),
        routes,
        output_cotangent,
        layer_input,
        expert_count,
        0,
    )
    route_from = query_width + 2 * key_width + expert_count + 4
    routes_all = packed[:, route_from : route_from + 2 * TOP].astype(jnp.int32)
    routes_all = routes_all.reshape(dp_count, shard, 2, TOP).transpose(0, 3, 2, 1)
    routes_all = routes_all.reshape(dp_count, TOP, block_rows)
    position = jnp.arange(block_rows, dtype=jnp.int32)
    live = position[None, :] < lengths[sequence_order][:, None]

    expert_own = dp_index * EXP_DEV + jnp.arange(EXP_DEV, dtype=jnp.int32)
    hot = jnp.any(routes_all[:, None, :, :] == expert_own[None, :, None, None], axis=2)
    hot = hot & live[:, None, :]
    before = (position[:, None] < position[None, :]).astype(bf16)
    rank = jnp.einsum("bes,st->bet", hot.astype(bf16), before, preferred_element_type=f32)
    rank = rank.astype(jnp.int32)
    counts = rank[:, :, -1] + hot[:, :, -1]
    earlier = jnp.cumsum(counts, axis=0) - counts
    slot = earlier[:, :, None] + rank
    slot = jnp.where(hot & (slot < capacity), slot, -capacity)
    begin = jnp.minimum(earlier, capacity) // WINDOW_ALIGN * WINDOW_ALIGN
    info = jnp.concatenate([dp_index[None], begin.reshape(-1), tensor_index[None]])
    out_part, back_part, gate_gradient, up_gradient, down_gradient = expert_layer(
        info.astype(jnp.int32),
        slot,
        normed_all,
        cot_all,
        expert_gate,
        expert_up,
        expert_down,
        capacity,
        most_rows,
    )
    returned = scatter_all(back_part.reshape(tokens, features + AUX), 3)
    grads, input_gradient = attention_backward(
        lengths,
        sequence_order,
        returned,
        residual,
        sent,
        output_cotangent,
        input_rows,
        packed,
        saved,
        expert_count,
        6,
    )
    summed, expert_sum = last_scatter(grads, out_part.reshape(tokens, features), 4)
    (
        layer_output,
        query_gradient,
        key_gradient,
        value_gradient,
        context_gradient,
        router_gradient,
        prenorm_gradient,
        midnorm_gradient,
        querynorm_gradient,
        keynorm_gradient,
    ) = unpack(summed, expert_sum, residual, query_width, key_width, expert_count, norm_part)
    return (
        layer_output,
        input_gradient,
        query_gradient,
        key_gradient,
        value_gradient,
        context_gradient,
        router_gradient,
        gate_gradient,
        up_gradient,
        down_gradient,
        prenorm_gradient,
        midnorm_gradient,
        querynorm_gradient,
        keynorm_gradient,
    )


def solution(mesh):
    return jax.shard_map(
        gathered_body if mesh.shape["dp"] <= 16 else body,
        mesh=mesh,
        in_specs=(
            P(("dp", "tensor"), None),
            P("dp", "tensor"),
            P("dp", "tensor"),
            P("dp", "tensor"),
            P("tensor", "dp"),
            P("dp", None),
            P("dp", None, "tensor"),
            P("dp", None, "tensor"),
            P("dp", "tensor", None),
            P("dp"),
            P("dp"),
            P("dp"),
            P("dp"),
            P("dp", None),
            P(),
            P(),
            P(("dp", "tensor"), None),
        ),
        out_specs=(
            P(("dp", "tensor"), None),
            P(("dp", "tensor"), None),
            P("dp", "tensor"),
            P("dp", "tensor"),
            P("dp", "tensor"),
            P("tensor", "dp"),
            P("dp", None),
            P("dp", None, "tensor"),
            P("dp", None, "tensor"),
            P("dp", "tensor", None),
            P("dp"),
            P("dp"),
            P("dp"),
            P("dp"),
        ),
        check_vma=False,
    )
```
